32 devices in a mesh: dp: 8 (over z, y), head: 4 (over x, core).
Axes of the slice: x: 2, y: 2, z: 4, core: 2. Of those that a mesh axis runs over, the one named last changes fastest.
Arguments:
- images: bfloat16 [256, 8, 8, 768], P(('dp', 'head')), may hold values from -6 to 6
- cotangent: bfloat16 [256, 8, 8, 768], P(('dp', 'head')), may hold values from -6 to 6
- counts: int32 [32, 2], replicated, may hold values from 0 to 4, as said below
- labels: int32 [256], P(('dp', 'head')), may hold values from 0 to 999
- levels: int32 [256], P(('dp', 'head')), may hold values from 0 to 63
- noise_table: bfloat16 [64, 768], replicated, may hold values from -6 to 6
- class_table: bfloat16 [1000, 768], P(None, 'dp'), may hold values from -6 to 6
- gain_a: bfloat16 [768], P('head'), may hold values from 0.099609375 to 1.8984375
- shift_a: bfloat16 [768], P('head'), may hold values from -3 to 3
- conv_a: bfloat16 [768, 9, 768], P('dp', None, 'head'), may hold values from -0.078125 to 0.078125
- bias_a: bfloat16 [768], P('head'), may hold values from -3 to 3
- mod_weight: bfloat16 [768, 2, 768], P('dp'), may hold values from -0.109375 to 0.109375
- mod_bias: bfloat16 [2, 768], replicated, may hold values from -3 to 3
- gain_b: bfloat16 [768], P('head'), may hold values from 0.099609375 to 1.8984375
- shift_b: bfloat16 [768], P('head'), may hold values from -3 to 3
- conv_b: bfloat16 [768, 9, 768], P('dp', None, 'head'), may hold values from -0.078125 to 0.078125
- bias_b: bfloat16 [768], P('head'), may hold values from -3 to 3
- gain_c: bfloat16 [768], P('head'), may hold values from 0.099609375 to 1.8984375
- shift_c: bfloat16 [768], P('head'), may hold values from -3 to 3
- qkv_weight: bfloat16 [768, 3, 768], P('dp', None, 'head'), may hold values from -0.3125 to 0.3125
- proj_weight: bfloat16 [768, 768], P('dp', 'head'), may hold values from -0.625 to 0.625
- proj_bias: bfloat16 [768], P('head'), may hold values from -3 to 3
Outputs:
- block_out: bfloat16 [256, 8, 8, 768], P(('dp', 'head'))
- image_grad: float32 [256, 8, 8, 768], P(('dp', 'head'))
- class_grad: float32 [1000, 768], P(None, ('dp', 'head'))
- gaina_grad: float32 [768], P('head')
- shifta_grad: float32 [768], P('head')
- conva_grad: float32 [768, 9, 768], P('dp', None, 'head')
- biasa_grad: float32 [768], P('head')
- modw_grad: float32 [768, 2, 768], P(('dp', 'head'))
- modb_grad: float32 [2, 768], P(None, ('dp', 'head'))
- gainb_grad: float32 [768], P('head')
- shiftb_grad: float32 [768], P('head')
- convb_grad: float32 [768, 9, 768], P('dp', None, 'head')
- biasb_grad: float32 [768], P('head')
- gainc_grad: float32 [768], P('head')
- shiftc_grad: float32 [768], P('head')
- qkvw_grad: float32 [768, 3, 768], P('dp', None, 'head')
- projw_grad: float32 [768, 768], P('dp', 'head')
- projb_grad: float32 [768], P('head')
The draws below stay inside these ranges and needn't reach their ends.
Inputs may be any that keep to these rules, and one draw needn't show every extreme that they name: Each entry lies from 0 to 4; on some device both entries equal 4. A device's live image slots are its first counts[d, 0] + counts[d, 1] ones.
All inputs are finite; a program needn't handle non-finite values.
Results may differ from the reference program's by a relative error of at most 0.038.
Values may be sent and summed in bfloat16 or wider, within the bound.
A program may use at most 256 MiB of HBM per device.

```python
import math
import jax
import jax.numpy as jnp
from jax import lax

C = 768
E = 768
CLASSES = 1000
RES = 8
DH = 64
GROUPS = 32
LEVELS = 64
IMG_DEV = 8
IMAGES = 256


def draw_counts(key, part):
    key = jax.random.fold_in(key, 17)
    half = IMG_DEV // 2
    devices_all = IMAGES // IMG_DEV
    values = jax.random.randint(key, (devices_all, 2), 0, half + 1)
    chosen_one = jax.random.randint(jax.random.fold_in(key, 5), (), 0, devices_all)
    chosen = lax.iota(jnp.int32, devices_all)[:, None] == chosen_one
    return jnp.where(chosen, half, values).astype(jnp.int32)


def set_ends(entries, stream_key, least, top_value):
    longest = entries.shape.index(max(entries.shape))
    spots = []
    for shift in (0, 1):
        where = [jax.random.randint(jax.random.fold_in(stream_key, axis), (), 0, length) for axis, length in enumerate(entries.shape)]
        where[longest] = (where[longest] + shift) % entries.shape[longest]
        spots.append(tuple(where))
    return entries.at[spots[0]].set(least).at[spots[1]].set(top_value)


def level_of(stream_key, extent, pieces, low, top_value):
    level, own = 1.0, jax.random.fold_in(stream_key, 6)
    for dim, blocks in pieces:
        draws = jnp.exp(jax.random.uniform(jax.random.fold_in(own, dim), (blocks,), jnp.float32, low / len(pieces), top_value / len(pieces)))
        level = level * jnp.repeat(draws, extent[dim] // blocks).reshape([-1 if axis == dim else 1 for axis in range(len(extent))])
    return level


def noise(key, dims, width, bound, cuts=(), kind=jnp.bfloat16):
    values = jax.random.normal(key, dims, jnp.float32) * width
    if len(cuts) > 0:
        values = level_of(key, dims, cuts, -0.22, 0.18) * values
    return jnp.clip(values, min=-bound, max=bound).astype(kind)


def setup_inputs(seed: int = 0) -> dict:
    seeds = jax.random.split(jax.random.key(seed), 23)
    images = noise(seeds[0], (IMAGES, RES, RES, C), 1.0, 6.0, ((0, 32),))
    cotangent = noise(seeds[1], (IMAGES, RES, RES, C), 1.0, 6.0, ((0, 32),))
    counts = draw_counts(jax.random.fold_in(seeds[22], 71), 0)
    labels = set_ends(jax.random.randint(seeds[3], (IMAGES,), 0, CLASSES), jax.random.fold_in(seeds[3], 1), 0, CLASSES - 1).astype(jnp.int32)
    levels = set_ends(jax.random.randint(seeds[4], (IMAGES,), 0, LEVELS), jax.random.fold_in(seeds[4], 1), 0, LEVELS - 1).astype(jnp.int32)
    noise_table = noise(seeds[5], (LEVELS, E), 1.0, 6.0)
    class_table = noise(seeds[6], (CLASSES, E), 1.0, 6.0, ((1, 8),))
    gain_a = jnp.clip(1.0 + 0.18 * jax.random.normal(seeds[7], (C,), jnp.float32), 0.099609375, 1.8984375).astype(jnp.bfloat16)
    shift_a = noise(seeds[8], (C,), 0.5, 3.0, ((0, 4),))
    conv_a = noise(seeds[9], (C, 9, C), (9 * C) ** -0.5, 0.078125, ((0, 8), (2, 4)))
    bias_a = noise(seeds[10], (C,), 0.3, 3.0, ((0, 4),))
    mod_weight = noise(seeds[11], (E, 2, C), (4 * E) ** -0.5, 0.109375, ((0, 8),))
    mod_bias = noise(seeds[12], (2, C), 0.3, 3.0)
    gain_b = jnp.clip(1.0 + 0.18 * jax.random.normal(seeds[13], (C,), jnp.float32), 0.099609375, 1.8984375).astype(jnp.bfloat16)
    shift_b = noise(seeds[14], (C,), 0.5, 3.0, ((0, 4),))
    conv_b = noise(seeds[15], (C, 9, C), (9 * C) ** -0.5, 0.078125, ((0, 8), (2, 4)))
    bias_b = noise(seeds[16], (C,), 0.3, 3.0, ((0, 4),))
    gain_c = jnp.clip(1.0 + 0.18 * jax.random.normal(seeds[17], (C,), jnp.float32), 0.099609375, 1.8984375).astype(jnp.bfloat16)
    shift_c = noise(seeds[18], (C,), 0.5, 3.0, ((0, 4),))
    qkv_weight = noise(seeds[19], (C, 3, C), (C // 2) ** -0.5, 0.3125, ((0, 8), (2, 4)))
    proj_weight = noise(seeds[20], (C, C), (C // 8) ** -0.5, 0.625, ((0, 8), (1, 4)))
    proj_bias = noise(seeds[21], (C,), 0.3, 3.0, ((0, 4),))
    return {"images": images, "cotangent": cotangent, "counts": counts, "labels": labels, "levels": levels, "noise_table": noise_table, "class_table": class_table, "gain_a": gain_a, "shift_a": shift_a, "conv_a": conv_a, "bias_a": bias_a, "mod_weight": mod_weight, "mod_bias": mod_bias, "gain_b": gain_b, "shift_b": shift_b, "conv_b": conv_b, "bias_b": bias_b, "gain_c": gain_c, "shift_c": shift_c, "qkv_weight": qkv_weight, "proj_weight": proj_weight, "proj_bias": proj_bias}


@jax.custom_vjp
def low(v):
    return lax.optimization_barrier(v.astype(jnp.bfloat16)).astype(jnp.float32)

@jax.custom_vjp
def low_back(v):
    return v

def low_keep(v):
    return (low(v), None)

def low_pass(kept, grad):
    return (grad,)

def back_keep(v):
    return (v, None)

def back_low(kept, grad):
    return (low(grad),)
low.defvjp(low_keep, low_pass)
low_back.defvjp(back_keep, back_low)
HIGHEST = lax.Precision.HIGHEST

def group_norm(values, gain, shift):
    count = values.shape[0]
    grouped = values.reshape(count, -1, GROUPS, values.shape[-1] // GROUPS)
    mean = lax.optimization_barrier(jnp.mean(grouped, axis=(1, 3), keepdims=True))
    centred = grouped - mean
    variance = lax.optimization_barrier(jnp.mean(centred * centred, axis=(1, 3), keepdims=True))
    normed = (centred * lax.rsqrt(variance + 1e-05)).reshape(values.shape)
    return normed * gain + shift

def patches_of(act):
    count, rows, cols, chans = act.shape
    padded = jnp.pad(act, ((0, 0), (1, 1), (1, 1), (0, 0)))
    taps = [padded[:, i:i + rows, j:j + cols, :] for i in range(3) for j in range(3)]
    return jnp.stack(taps, axis=3).reshape(count * rows * cols, 9, chans)

def convolve(act, weight, bias):
    return jnp.einsum('ptc,cto->po', patches_of(act), weight, precision=HIGHEST) + bias

def forward(params, source, labels, levels, noise_table, live):
    class_table, gain_a, shift_a, conv_a, bias_a, mod_weight, mod_bias, gain_b, shift_b, conv_b, bias_b, gain_c, shift_c, qkv_weight, proj_weight, proj_bias = params
    count, rows, cols, chans = source.shape
    pixels = rows * cols
    act_a = low(jax.nn.silu(group_norm(source, gain_a, shift_a)))
    conv_out_a = low_back(convolve(act_a, conv_a, bias_a)).reshape(source.shape)
    embed = low(jax.nn.silu(noise_table[levels] + class_table[labels]))
    modulation = low(jnp.einsum('ne,etc->ntc', embed, mod_weight, precision=HIGHEST) + mod_bias)
    scale = modulation[:, 0][:, None, None, :]
    offset = modulation[:, 1][:, None, None, :]
    act_b = low(jax.nn.silu(offset + group_norm(conv_out_a, gain_b, shift_b) * (scale + 1.0)))
    conv_out_b = low_back(convolve(act_b, conv_b, bias_b)).reshape(source.shape)
    resid = source + conv_out_b
    attn_in = low(group_norm(resid, gain_c, shift_c)).reshape(count * pixels, chans)
    qkv = low_back(low(jnp.dot(attn_in, qkv_weight.reshape(chans, 3 * chans), precision=HIGHEST)))
    qkv = qkv.reshape(count, pixels, 3, chans // DH, DH)
    query, key, value = (qkv[:, :, 0], qkv[:, :, 1], qkv[:, :, 2])
    scores = low_back(jnp.einsum('nqhd,nkhd->nhqk', query, key, precision=HIGHEST) * DH ** (-0.5))
    probs = low(jax.nn.softmax(scores, axis=-1))
    mixed = jnp.einsum('nhqk,nkhd->nqhd', probs, value, precision=HIGHEST)
    mixed = low_back(low(mixed)).reshape(count * pixels, chans)
    result = resid.reshape(count * pixels, chans) + jnp.dot(mixed, proj_weight, precision=HIGHEST) + proj_bias
    return result.reshape(source.shape) * live[:, None, None, None]

def reference(images, cotangent, counts, labels, levels, noise_table, class_table, gain_a, shift_a, conv_a, bias_a, mod_weight, mod_bias, gain_b, shift_b, conv_b, bias_b, gain_c, shift_c, qkv_weight, proj_weight, proj_bias):
    params = tuple((p.astype(jnp.float32) for p in (class_table, gain_a, shift_a, conv_a, bias_a, mod_weight, mod_bias, gain_b, shift_b, conv_b, bias_b, gain_c, shift_c, qkv_weight, proj_weight, proj_bias)))
    noise_float = noise_table.astype(jnp.float32)
    slots = jnp.arange(IMAGES, dtype=jnp.int32)
    per_device = lax.optimization_barrier(jnp.sum(counts, axis=1)).astype(jnp.int32)
    live = (slots % IMG_DEV < per_device[slots // IMG_DEV]).astype(jnp.float32)
    block = math.gcd(IMAGES, 64)
    blocks = IMAGES // block
    shape = (blocks, block) + images.shape[1:]

    def step(totals, inputs):
        source, grad_in, label_block, level_block, live_block = inputs

        def run(weights, values):
            return forward(weights, values, label_block, level_block, noise_float, live_block)
        result, pull = jax.vjp(run, params, source.astype(jnp.float32))
        grad_params, grad_source = pull(grad_in.astype(jnp.float32))
        totals = jax.tree.map(lambda a, b: a + b, totals, grad_params)
        return (totals, (result.astype(jnp.bfloat16), grad_source))
    start = jax.tree.map(jnp.zeros_like, params)
    totals, (outputs, grads) = lax.scan(step, start, (images.reshape(shape), cotangent.reshape(shape), labels.reshape(blocks, block), levels.reshape(blocks, block), live.reshape(blocks, block)))
    return (outputs.reshape(images.shape), grads.reshape(images.shape), totals[0], totals[1], totals[2], totals[3], totals[4], totals[5], totals[6], totals[7], totals[8], totals[9], totals[10], totals[11], totals[12], totals[13], totals[14], totals[15])
```

```python
import functools

import jax
import jax.numpy as jnp
from jax import lax
from jax.experimental import pallas as pl
from jax.experimental.pallas import tpu as pltpu
from jax.sharding import PartitionSpec as P

C = 768
DH = 64
GROUPS = 32


EPSILON = 1e-05
HIGHEST = lax.Precision.HIGHEST


def norm_forward(values, gain, shift):
    count, chans = (values.shape[0], values.shape[-1])
    span = C // GROUPS
    grouped = values.reshape(count, -1, chans // span, span)
    mean = jnp.mean(grouped, axis=(1, 3), keepdims=True)
    centred = grouped - mean
    inverse = lax.rsqrt(jnp.mean(centred * centred, axis=(1, 3), keepdims=True) + EPSILON)
    normed = (centred * inverse).reshape(values.shape)
    return (normed * gain + shift, normed, inverse)


def norm_backward(grad_out, normed, inverse, gain):
    grad_gain = jnp.sum(grad_out * normed, axis=(0, 1, 2))
    grad_shift = jnp.sum(grad_out, axis=(0, 1, 2))
    count, chans = (grad_out.shape[0], grad_out.shape[-1])
    span = C // GROUPS
    layout = (count, -1, chans // span, span)
    grad_normed = (grad_out * gain).reshape(layout)
    normed_groups = normed.reshape(layout)
    mean_one = jnp.mean(grad_normed, axis=(1, 3), keepdims=True)
    mean_two = jnp.mean(grad_normed * normed_groups, axis=(1, 3), keepdims=True)
    grad_in = inverse * (grad_normed - mean_one - normed_groups * mean_two)
    return (grad_in.reshape(grad_out.shape), grad_gain, grad_shift)


def silu_slope(values):
    sigma = jax.nn.sigmoid(values)
    return sigma * (1.0 + values * (1.0 - sigma))


def patches_of(act):
    count, rows, cols, chans = act.shape
    padded = jnp.pad(act, ((0, 0), (1, 1), (1, 1), (0, 0)))
    taps = [padded[:, i : i + rows, j : j + cols, :] for i in range(3) for j in range(3)]
    return jnp.stack(taps, axis=3).reshape(count * rows * cols, 9, chans)


def contract_rows(left, right):
    return lax.dot_general(
        left, right, (((0,), (0,)), ((), ())), preferred_element_type=jnp.float32
    )


def contract_cols(left, right):
    return lax.dot_general(
        left, right, (((1,), (1,)), ((), ())), preferred_element_type=jnp.float32
    )


def conv_back(grad_low, weight, count, rows, cols):
    chans = weight.shape[1]
    padded = jnp.zeros((count, rows + 2, cols + 2, chans), jnp.float32)
    for tap in range(9):
        i, j = divmod(tap, 3)
        part = contract_cols(grad_low, weight[tap]).reshape(count, rows, cols, chans)
        padded = padded.at[:, i : i + rows, j : j + cols, :].add(part)
    return padded[:, 1 : rows + 1, 1 : cols + 1, :]


def keep_same(values):
    return values


def live_rows(counts, first, number, count):
    sums = jnp.sum(counts, axis=1)
    chosen = lax.dynamic_slice_in_dim(sums, first, number)
    slots = lax.iota(jnp.int32, count)
    return (slots[None, :] < chosen[:, None]).astype(jnp.float32).reshape(number * count)


def residual_forward(source, mod_pair, weights, spread):
    (
        conv_one,
        conv_two,
        gain_one,
        shift_one,
        bias_one,
        gain_two,
        shift_two,
        bias_two,
        gain_three,
        shift_three,
    ) = weights
    out_a, normed_a, inverse_a = norm_forward(source, gain_one, shift_one)
    wide_a = spread(jax.nn.silu(out_a).astype(jnp.bfloat16))
    conv_out_a = (
        jnp.einsum("ptc,tco->po", patches_of(wide_a), conv_one, preferred_element_type=jnp.float32)
        + bias_one
    ).reshape(source.shape)
    scale = mod_pair[:, :, 0:1, :]
    offset = mod_pair[:, :, 1:2, :]
    out_b, normed_b, inverse_b = norm_forward(conv_out_a, gain_two, shift_two)
    inner_b = offset + out_b * (scale + 1.0)
    wide_b = spread(jax.nn.silu(inner_b).astype(jnp.bfloat16))
    conv_out_b = (
        jnp.einsum("ptc,tco->po", patches_of(wide_b), conv_two, preferred_element_type=jnp.float32)
        + bias_two
    ).reshape(source.shape)
    resid = source + conv_out_b
    out_c, normed_c, inverse_c = norm_forward(resid, gain_three, shift_three)
    attn_in = out_c.astype(jnp.bfloat16)
    saved = (
        out_a,
        normed_a,
        inverse_a,
        wide_a,
        out_b,
        normed_b,
        inverse_b,
        inner_b,
        wide_b,
        normed_c,
        inverse_c,
        scale,
    )
    return (resid, attn_in, saved)


def residual_backward(grad_attn, grad_out, saved, weights, reduce_value):
    conv_one, conv_two, gain_one, gain_two, gain_three = (
        weights[0],
        weights[1],
        weights[2],
        weights[5],
        weights[8],
    )
    (
        out_a,
        normed_a,
        inverse_a,
        wide_a,
        out_b,
        normed_b,
        inverse_b,
        inner_b,
        wide_b,
        normed_c,
        inverse_c,
        scale,
    ) = saved
    count, rows, cols, local = grad_out.shape
    grad_resid_c, gainc_term, shiftc_term = norm_backward(
        grad_attn, normed_c, inverse_c, gain_three
    )
    grad_resid = grad_out + grad_resid_c
    grad_conv_b = grad_resid.reshape(-1, local).astype(jnp.bfloat16)
    biasb_term = jnp.sum(grad_conv_b.astype(jnp.float32), axis=0)
    convb_term = jnp.einsum(
        "ptc,po->tco", patches_of(wide_b), grad_conv_b, preferred_element_type=jnp.float32
    )
    grad_act_b = reduce_value(conv_back(grad_conv_b, conv_two, count, rows, cols))
    grad_inner = grad_act_b * silu_slope(inner_b)
    grad_offset = jnp.sum(grad_inner, axis=(1, 2))
    grad_scale = jnp.sum(grad_inner * out_b, axis=(1, 2))
    grad_mod = jnp.stack([grad_scale, grad_offset], axis=1)[:, None]
    grad_conv_full, gainb_term, shiftb_term = norm_backward(
        grad_inner * (scale + 1.0), normed_b, inverse_b, gain_two
    )
    grad_conv_a = grad_conv_full.reshape(-1, local).astype(jnp.bfloat16)
    biasa_term = jnp.sum(grad_conv_a.astype(jnp.float32), axis=0)
    conva_term = jnp.einsum(
        "ptc,po->tco", patches_of(wide_a), grad_conv_a, preferred_element_type=jnp.float32
    )
    grad_act_a = reduce_value(conv_back(grad_conv_a, conv_one, count, rows, cols))
    grad_source, gaina_term, shifta_term = norm_backward(
        grad_act_a * silu_slope(out_a), normed_a, inverse_a, gain_one
    )
    image_grad = grad_resid + grad_source
    vectors = (
        gaina_term,
        shifta_term,
        biasa_term,
        gainb_term,
        shiftb_term,
        biasb_term,
        gainc_term,
        shiftc_term,
    )
    return (image_grad, grad_mod, (conva_term, convb_term), vectors)


def attend_forward(block):
    query, key, value = (block[:, :, 0], block[:, :, 1], block[:, :, 2])
    batch, pixels, heads_here, depth = query.shape
    scores = jnp.einsum("bqhd,bkhd->bhqk", query, key, preferred_element_type=jnp.float32) * DH ** (
        -0.5
    )
    top = jnp.max(scores, axis=-1, keepdims=True)
    weights = jnp.exp(scores - top)
    sums = jnp.sum(weights, axis=-1, keepdims=True)
    probs = (weights / sums).astype(jnp.bfloat16)
    logsum = (top + jnp.log(sums))[..., 0]
    mixed = jnp.einsum("bhqk,bkhd->bqhd", probs, value, preferred_element_type=jnp.float32).astype(
        jnp.bfloat16
    )
    return (mixed.reshape(batch, pixels, heads_here * depth), logsum)


def attend_backward(block, logsum, grad_head):
    query, key, value = (block[:, :, 0], block[:, :, 1], block[:, :, 2])
    batch, pixels, heads_here, depth = query.shape
    factor = DH ** (-0.5)
    scores = jnp.einsum("bqhd,bkhd->bhqk", query, key, preferred_element_type=jnp.float32) * factor
    probs = jnp.exp(scores - logsum[..., None])
    grad_value = jnp.einsum(
        "bhqk,bqhd->bkhd", probs.astype(jnp.bfloat16), grad_head, preferred_element_type=jnp.float32
    )
    grad_probs = jnp.einsum("bqhd,bkhd->bhqk", grad_head, value, preferred_element_type=jnp.float32)
    inner = jnp.sum(grad_probs * probs, axis=-1, keepdims=True)
    grad_scores = (probs * (grad_probs - inner)).astype(jnp.bfloat16)
    grad_query = (
        jnp.einsum("bhqk,bkhd->bqhd", grad_scores, key, preferred_element_type=jnp.float32) * factor
    )
    grad_key = (
        jnp.einsum("bhqk,bqhd->bkhd", grad_scores, query, preferred_element_type=jnp.float32)
        * factor
    )
    stacked = jnp.stack([grad_query, grad_key, grad_value], axis=2).astype(jnp.bfloat16)
    return stacked.reshape(batch, pixels, 3, heads_here * depth)


MESH = pl.DeviceIdType.MESH
UNITS = 22
PAIRS = UNITS // 2
F32 = jnp.float32
BF16 = jnp.bfloat16
ANY = pl.BlockSpec(memory_space=pl.ANY)


def pack_units(conv_a, conv_b, qkv_weight, proj_weight):
    return jnp.concatenate(
        [
            jnp.swapaxes(conv_a, 0, 1),
            jnp.swapaxes(conv_b[:, 8:9], 0, 1),
            jnp.swapaxes(conv_b[:, 0:8], 0, 1),
            jnp.swapaxes(qkv_weight, 0, 1),
            proj_weight[None],
        ],
        axis=0,
    )


def chip_grid():
    return lax.axis_size("dp") // 2, lax.axis_size("head") // 2


def direct(rows):
    lines, across = chip_grid()
    return across == 2 and lax.axis_size("dp") % 4 == 0 and rows % 16 == 0


def place():
    d, h = lax.axis_index("dp"), lax.axis_index("head")
    return d // 2, lax.rem(d, 2), h // 2, lax.rem(h, 2)


def at_chip(z, y, x, c):
    return (z * 2 + y, x * 2 + c)


def greet(devices):
    barrier = pltpu.get_barrier_semaphore()
    for device in devices:
        pl.semaphore_signal(barrier, inc=1, device_id=device, device_id_type=MESH)
    pl.semaphore_wait(barrier, len(devices))


def remote(src, dst, send, recv, device):
    return pltpu.make_async_remote_copy(
        src_ref=src, dst_ref=dst, send_sem=send, recv_sem=recv, device_id=device, device_id_type=MESH
    )


def stages(length, steps):
    lag = len(steps) - 1
    for turn in range(lag):
        for k, step in enumerate(steps):
            if 0 <= turn - k:
                step(turn - k)

    def body(turn, carry):
        for k, step in enumerate(steps):
            step(turn - k)
        return carry

    lax.fori_loop(lag, length, body, 0)
    for turn in range(length, length + lag):
        for k, step in enumerate(steps):
            if turn - k < length:
                step(turn - k)


def gather_kernel(
    lines,
    wide,
    units_ref,
    whole_ref,
    halves,
    block,
    pair_send,
    pair_recv,
    pair_local,
    own_sem,
    z_send,
    z_recv,
    x_send,
    x_recv,
    y_send,
    y_recv,
    s_send,
    s_recv,
):
    z, y, x, c = place()
    half = lines // 2
    sibling = at_chip(z, y, x, 1 - c)
    along_x = at_chip(z, y, 1 - x, c)
    along_y = at_chip(z, 1 - y, x, c)
    line = [at_chip(lax.rem(z + k, lines), y, x, c) for k in range(1, lines)]
    greet([sibling, along_x, along_y] + line)

    def cols(xx):
        return pl.ds(pl.multiple_of(xx * wide, 128), wide)

    def spot(i, cc, zz, yy, xx):
        return whole_ref.at[i, cc, zz, yy, :, cols(xx)]

    swap = remote(units_ref.at[:, 1 - c], halves.at[c], pair_send, pair_recv, sibling)
    keep = pltpu.make_async_copy(units_ref.at[:, c], halves.at[c], pair_local)
    swap.start()
    keep.start()
    keep.wait()
    swap.wait()

    def own_copy(i):
        return pltpu.make_async_copy(block.at[i], spot(i, c, z, y, x), own_sem.at[i])

    def z_copy(i, k):
        return remote(
            block.at[i], spot(i, c, z, y, x), z_send.at[i, k], z_recv.at[i, k], line[k]
        )

    def x_copy(i, part):
        if part == 0:
            ref = spot(i, c, slice(None), y, x)
        else:
            ref = spot(i, c, pl.ds(half, half), 1 - y, x)
        return remote(ref, ref, x_send.at[i, part], x_recv.at[i, part], along_x)

    def y_copy(i, part):
        if part == 0:
            ref = spot(i, c, slice(None), y, x)
        else:
            ref = spot(i, c, pl.ds(0, half), y, 1 - x)
        return remote(ref, ref, y_send.at[i, part], y_recv.at[i, part], along_y)

    def s_copy(i, part):
        yy, xx = ((y, x), (y, 1 - x), (1 - y, x), (1 - y, 1 - x))[part]
        ref = spot(i, c, slice(None), yy, xx)
        return remote(ref, ref, s_send.at[i, part], s_recv.at[i, part], sibling)

    def begin(i):
        block[i] = jnp.concatenate([halves[0, i], halves[1, i]], axis=-1)
        own_copy(i).start()
        for k in range(lines - 1):
            z_copy(i, k).start()

    def spread_line(i):
        own_copy(i).wait()
        for k in range(lines - 1):
            z_copy(i, k).wait_recv()
        x_copy(i, 0).start()
        y_copy(i, 0).start()
        s_copy(i, 0).start()

    def pass_on(i):
        x_copy(i, 0).wait_recv()
        y_copy(i, 1).start()
        s_copy(i, 1).start()
        y_copy(i, 0).wait_recv()
        x_copy(i, 1).start()
        s_copy(i, 2).start()

    def finish(i):
        x_copy(i, 1).wait_recv()
        y_copy(i, 1).wait_recv()
        s_copy(i, 3).start()

    lax.fori_loop(0, PAIRS, lambda i, carry: (begin(i), carry)[1], 0)
    stages(PAIRS, [spread_line, pass_on, finish])

    def drain(i, carry):
        for k in range(lines - 1):
            z_copy(i, k).wait_send()
        for part in range(2):
            x_copy(i, part).wait_send()
            y_copy(i, part).wait_send()
        for part in range(4):
            s_copy(i, part).wait()
        return carry

    lax.fori_loop(0, PAIRS, drain, 0)


def gather_units(taps):
    units, rows, cols = taps.shape
    if not direct(rows):
        taps = lax.all_gather(taps, "dp", axis=1, tiled=True)
        return lax.all_gather(taps, "head", axis=2, tiled=True)
    lines, across = chip_grid()
    wide = 2 * cols
    dma = pltpu.SemaphoreType.DMA
    whole = pl.pallas_call(
        functools.partial(gather_kernel, lines, wide),
        out_shape=jax.ShapeDtypeStruct((PAIRS, 2, lines, 2, rows, across * wide), BF16),
        in_specs=[ANY],
        out_specs=ANY,
        scratch_shapes=[
            pltpu.VMEM((2, PAIRS, rows, cols), BF16),
            pltpu.VMEM((PAIRS, rows, wide), BF16),
            dma,
            dma,
            dma,
            dma((PAIRS,)),
            dma((PAIRS, lines - 1)),
            dma((PAIRS, lines - 1)),
            dma((PAIRS, 2)),
            dma((PAIRS, 2)),
            dma((PAIRS, 2)),
            dma((PAIRS, 2)),
            dma((PAIRS, 4)),
            dma((PAIRS, 4)),
        ],
        compiler_params=pltpu.CompilerParams(
            collective_id=0, has_side_effects=True, vmem_limit_bytes=32 * 2**20
        ),
        name="gather_weights",
    )(taps.reshape(PAIRS, 2, rows, cols))
    return whole.reshape(units, lines * 2 * rows, across * wide)


def scatter_kernel(
    lines,
    wide,
    terms_ref,
    out_ref,
    mine,
    other,
    from_x,
    from_y,
    from_z,
    block,
    ends,
    load_sem,
    s_send,
    s_recv,
    z_send,
    z_recv,
    x_send,
    x_recv,
    y_send,
    y_recv,
    end_send,
    end_recv,
):
    z, y, x, c = place()
    half = lines // 2
    cols = wide // 2
    sibling = at_chip(z, y, x, 1 - c)
    along_x = at_chip(z, y, 1 - x, c)
    along_y = at_chip(z, 1 - y, x, c)
    line = [at_chip(lax.rem(z + k, lines), y, x, c) for k in range(1, lines)]
    greet([sibling, along_x, along_y] + line)

    def lanes(xx):
        return pl.ds(pl.multiple_of(xx * wide, 128), wide)

    def load(i):
        return pltpu.make_async_copy(terms_ref.at[i, c], mine.at[i], load_sem.at[i])

    def s_copy(i):
        return remote(terms_ref.at[i, 1 - c], other.at[i], s_send.at[i], s_recv.at[i], sibling)

    def x_copy(i, part):
        if part == 0:
            src, dst = mine.at[i, pl.ds(half, half), 1 - y, :, lanes(1 - x)], from_x.at[i, pl.ds(lines, half)]
        else:
            src, dst = mine.at[i, :, y, :, lanes(1 - x)], from_x.at[i, pl.ds(0, lines)]
        return remote(src, dst, x_send.at[i, part], x_recv.at[i, part], along_x)

    def y_copy(i, part):
        if part == 0:
            src, dst = mine.at[i, pl.ds(0, half), 1 - y, :, lanes(1 - x)], from_y.at[i, pl.ds(lines, half)]
        else:
            src, dst = mine.at[i, :, 1 - y, :, lanes(x)], from_y.at[i, pl.ds(0, lines)]
        return remote(src, dst, y_send.at[i, part], y_recv.at[i, part], along_y)

    def z_copy(i, k):
        return remote(
            block.at[i, lax.rem(z + k + 1, lines)],
            from_z.at[i, k],
            z_send.at[i, k],
            z_recv.at[i, k],
            line[k],
        )

    def begin(i):
        load(i).start()
        s_copy(i).start()

    def pair_sum(i):
        load(i).wait()
        s_copy(i).wait_recv()

        def add(j, carry):
            for yy in range(2):
                mine[i, j, yy] = (mine[i, j, yy].astype(F32) + other[i, j, yy].astype(F32)).astype(BF16)
            return carry

        lax.fori_loop(0, lines, add, 0)
        x_copy(i, 0).start()
        y_copy(i, 0).start()

    def relay(i):
        x_copy(i, 0).wait_recv()
        y_copy(i, 0).wait_recv()
        for j in range(half):
            a = mine[i, j, y, :, lanes(1 - x)].astype(F32)
            mine[i, j, y, :, lanes(1 - x)] = (a + from_y[i, lines + j].astype(F32)).astype(BF16)
            b = mine[i, half + j, 1 - y, :, lanes(x)].astype(F32)
            mine[i, half + j, 1 - y, :, lanes(x)] = (b + from_x[i, lines + j].astype(F32)).astype(BF16)
        x_copy(i, 1).start()
        y_copy(i, 1).start()

    def total(i):
        x_copy(i, 1).wait_recv()
        y_copy(i, 1).wait_recv()

        def add(j, carry):
            block[i, j] = (
                mine[i, j, y, :, lanes(x)].astype(F32)
                + from_x[i, j].astype(F32)
                + from_y[i, j].astype(F32)
            ).astype(BF16)
            return carry

        lax.fori_loop(0, lines, add, 0)
        for k in range(lines - 1):
            z_copy(i, k).start()

    def last(i):
        value = block[i, z].astype(F32)
        for k in range(lines - 1):
            z_copy(i, k).wait_recv()
            value += from_z[i, k].astype(F32)
        for cc in range(2):
            ends[cc, i] = value[:, cc * cols : (cc + 1) * cols]

    lax.fori_loop(0, PAIRS, lambda i, carry: (begin(i), carry)[1], 0)
    stages(PAIRS, [pair_sum, relay, total, last])

    give = remote(ends.at[1 - c], out_ref.at[:, c], end_send, end_recv, sibling)
    keep = pltpu.make_async_copy(ends.at[c], out_ref.at[:, c], load_sem.at[0])
    give.start()
    keep.start()

    def drain(i, carry):
        s_copy(i).wait_send()
        for part in range(2):
            x_copy(i, part).wait_send()
            y_copy(i, part).wait_send()
        for k in range(lines - 1):
            z_copy(i, k).wait_send()
        return carry

    lax.fori_loop(0, PAIRS, drain, 0)
    keep.wait()
    give.wait()


def scatter_units(terms):
    units, depth, width = terms.shape
    n_dp, n_head = lax.axis_size("dp"), lax.axis_size("head")
    rows, cols = depth // n_dp, width // n_head
    if not direct(rows):
        out = lax.psum_scatter(terms, "head", scatter_dimension=2, tiled=True)
        return lax.psum_scatter(out.astype(F32), "dp", scatter_dimension=1, tiled=True)
    lines, across = chip_grid()
    wide = 2 * cols
    dma = pltpu.SemaphoreType.DMA
    out = pl.pallas_call(
        functools.partial(scatter_kernel, lines, wide),
        out_shape=jax.ShapeDtypeStruct((PAIRS, 2, rows, cols), F32),
        in_specs=[ANY],
        out_specs=ANY,
        scratch_shapes=[
            pltpu.VMEM((PAIRS, lines, 2, rows, across * wide), BF16),
            pltpu.VMEM((PAIRS, lines, 2, rows, across * wide), BF16),
            pltpu.VMEM((PAIRS, lines + lines // 2, rows, wide), BF16),
            pltpu.VMEM((PAIRS, lines + lines // 2, rows, wide), BF16),
            pltpu.VMEM((PAIRS, lines - 1, rows, wide), BF16),
            pltpu.VMEM((PAIRS, lines, rows, wide), BF16),
            pltpu.VMEM((2, PAIRS, rows, cols), F32),
            dma((PAIRS,)),
            dma((PAIRS,)),
            dma((PAIRS,)),
            dma((PAIRS, lines - 1)),
            dma((PAIRS, lines - 1)),
            dma((PAIRS, 2)),
            dma((PAIRS, 2)),
            dma((PAIRS, 2)),
            dma((PAIRS, 2)),
            dma,
            dma,
        ],
        compiler_params=pltpu.CompilerParams(
            collective_id=1, has_side_effects=True, vmem_limit_bytes=60 * 2**20
        ),
        name="scatter_grads",
    )(terms.reshape(PAIRS, 2, lines, 2, rows, across * wide))
    return out.reshape(units, rows, cols)


def shards(
    images,
    cotangent,
    counts,
    labels,
    levels,
    noise_table,
    class_table,
    gain_a,
    shift_a,
    conv_a,
    bias_a,
    mod_weight,
    mod_bias,
    gain_b,
    shift_b,
    conv_b,
    bias_b,
    gain_c,
    shift_c,
    qkv_weight,
    proj_weight,
    proj_bias,
):
    taps = pack_units(conv_a, conv_b, qkv_weight, proj_weight)
    whole = gather_units(taps)
    mod_full, class_full = (
        lax.all_gather(mod_weight, "dp", axis=0, tiled=True),
        lax.all_gather(class_table, "dp", axis=1, tiled=True),
    )
    count, rows, cols, channels = images.shape
    pixels = rows * cols
    groups_n = lax.axis_size("head")
    first_dp = lax.axis_index("dp") * groups_n
    class_hot = (labels[:, None] == lax.iota(jnp.int32, class_full.shape[0])[None, :]).astype(
        jnp.bfloat16
    )
    level_hot = (levels[:, None] == lax.iota(jnp.int32, noise_table.shape[0])[None, :]).astype(
        jnp.bfloat16
    )
    embed_pre = jnp.dot(class_hot, class_full, preferred_element_type=jnp.float32) + jnp.dot(
        level_hot, noise_table, preferred_element_type=jnp.float32
    )
    embed = jax.nn.silu(embed_pre).astype(jnp.bfloat16)
    modulation = (
        jnp.einsum("ne,etc->ntc", embed, mod_full, preferred_element_type=jnp.float32)
        + mod_bias.astype(jnp.float32)
    ).astype(jnp.bfloat16)
    mod_pair = modulation.reshape(count, 1, 2, channels)
    (
        conv_one,
        conv_two,
        qkv_full,
        proj_full,
        gain_one,
        shift_one,
        bias_one,
        gain_two,
        shift_two,
        bias_two,
        gain_three,
        shift_three,
        bias_three,
    ) = (
        whole[0:9],
        jnp.concatenate([whole[10:18], whole[9:10]], axis=0),
        jnp.swapaxes(whole[18:21], 0, 1),
        whole[21],
        lax.all_gather(gain_a, "head", axis=0, tiled=True),
        lax.all_gather(shift_a, "head", axis=0, tiled=True),
        lax.all_gather(bias_a, "head", axis=0, tiled=True),
        lax.all_gather(gain_b, "head", axis=0, tiled=True),
        lax.all_gather(shift_b, "head", axis=0, tiled=True),
        lax.all_gather(bias_b, "head", axis=0, tiled=True),
        lax.all_gather(gain_c, "head", axis=0, tiled=True),
        lax.all_gather(shift_c, "head", axis=0, tiled=True),
        lax.all_gather(proj_bias, "head", axis=0, tiled=True),
    )
    weights = (
        conv_one,
        conv_two,
        gain_one,
        shift_one,
        bias_one,
        gain_two,
        shift_two,
        bias_two,
        gain_three,
        shift_three,
    )
    live = live_rows(counts, first_dp + lax.axis_index("head"), 1, count)
    total = count * pixels
    source = images.astype(jnp.float32)
    resid, attn_in, saved = residual_forward(
        source, mod_pair.astype(jnp.float32), weights, keep_same
    )
    attn_flat = attn_in.reshape(total, channels)
    qkv_flat = qkv_full.reshape(channels, 3 * channels)
    qkv = jnp.dot(attn_flat, qkv_flat, preferred_element_type=jnp.float32).astype(jnp.bfloat16)
    heads = channels // DH
    block = qkv.reshape(count, pixels, 3, heads, DH)
    mixed, logsum = attend_forward(block)
    mixed_image = mixed.reshape(total, channels)
    result = (
        resid.reshape(total, channels)
        + jnp.dot(mixed_image, proj_full, preferred_element_type=jnp.float32)
        + bias_three
    )
    block_out = (result.reshape(images.shape) * live[:, None, None, None]).astype(jnp.bfloat16)
    grad_out = cotangent.astype(jnp.float32) * live[:, None, None, None]
    grad_flat = grad_out.reshape(total, channels)
    grad_low = grad_flat.astype(jnp.bfloat16)
    projw_full = contract_rows(mixed_image, grad_low)
    projb_full = jnp.sum(grad_flat, axis=0)
    grad_mixed = contract_cols(grad_low, proj_full).astype(jnp.bfloat16)
    stacked = attend_backward(block, logsum, grad_mixed.reshape(count, pixels, heads, DH))
    grad_qkv = stacked.reshape(total, 3 * channels)
    qkvw_full = contract_rows(attn_flat, grad_qkv).reshape(channels, 3, channels)
    grad_attn = contract_cols(grad_qkv, qkv_flat).reshape(images.shape)
    image_grad, grad_mod_part, conv_terms, vectors = residual_backward(
        grad_attn, grad_out, saved, weights, keep_same
    )
    (
        gaina_full,
        shifta_full,
        biasa_full,
        gainb_full,
        shiftb_full,
        biasb_full,
        gainc_full,
        shiftc_full,
    ) = vectors
    (
        gaina_term,
        shifta_term,
        biasa_term,
        gainb_term,
        shiftb_term,
        biasb_term,
        gainc_term,
        shiftc_term,
        projb_term,
    ) = (
        lax.psum_scatter(
            gaina_full.astype(jnp.bfloat16), "head", scatter_dimension=0, tiled=True
        ).astype(jnp.float32),
        lax.psum_scatter(
            shifta_full.astype(jnp.bfloat16), "head", scatter_dimension=0, tiled=True
        ).astype(jnp.float32),
        lax.psum_scatter(
            biasa_full.astype(jnp.bfloat16), "head", scatter_dimension=0, tiled=True
        ).astype(jnp.float32),
        lax.psum_scatter(
            gainb_full.astype(jnp.bfloat16), "head", scatter_dimension=0, tiled=True
        ).astype(jnp.float32),
        lax.psum_scatter(
            shiftb_full.astype(jnp.bfloat16), "head", scatter_dimension=0, tiled=True
        ).astype(jnp.float32),
        lax.psum_scatter(
            biasb_full.astype(jnp.bfloat16), "head", scatter_dimension=0, tiled=True
        ).astype(jnp.float32),
        lax.psum_scatter(
            gainc_full.astype(jnp.bfloat16), "head", scatter_dimension=0, tiled=True
        ).astype(jnp.float32),
        lax.psum_scatter(
            shiftc_full.astype(jnp.bfloat16), "head", scatter_dimension=0, tiled=True
        ).astype(jnp.float32),
        lax.psum_scatter(
            projb_full.astype(jnp.bfloat16), "head", scatter_dimension=0, tiled=True
        ).astype(jnp.float32),
    )
    grad_mod = grad_mod_part.reshape(count, 2, channels)
    modw_term = jnp.einsum("ne,ntc->etc", embed.astype(jnp.float32), grad_mod, precision=HIGHEST)
    modb_term = jnp.sum(grad_mod, axis=0)
    grad_embed = jnp.einsum(
        "ntc,etc->ne", grad_mod, mod_full.astype(jnp.float32), precision=HIGHEST
    ) * silu_slope(embed_pre)
    class_term = lax.dot_general(
        class_hot.astype(jnp.float32), grad_embed, (((0,), (0,)), ((), ())), precision=HIGHEST
    )
    modw_grad, class_grad, modb_grad = (
        lax.psum_scatter(modw_term, ("dp", "head"), scatter_dimension=0, tiled=True),
        lax.psum_scatter(class_term, ("dp", "head"), scatter_dimension=1, tiled=True),
        lax.psum_scatter(modb_term, ("dp", "head"), scatter_dimension=1, tiled=True),
    )
    terms = jnp.concatenate(
        [
            conv_terms[0].astype(jnp.bfloat16),
            conv_terms[1][8:9].astype(jnp.bfloat16),
            conv_terms[1][0:8].astype(jnp.bfloat16),
            jnp.swapaxes(qkvw_full, 0, 1).astype(jnp.bfloat16),
            projw_full[None].astype(jnp.bfloat16),
        ],
        axis=0,
    )
    summed = scatter_units(terms)
    conva_grad = jnp.swapaxes(summed[0:9], 0, 1)
    convb_grad = jnp.swapaxes(jnp.concatenate([summed[10:18], summed[9:10]], axis=0), 0, 1)
    qkvw_grad = jnp.swapaxes(summed[18:21], 0, 1)
    projw_grad = summed[21]
    (
        gaina_grad,
        shifta_grad,
        biasa_grad,
        gainb_grad,
        shiftb_grad,
        biasb_grad,
        gainc_grad,
        shiftc_grad,
        projb_grad,
    ) = lax.psum(
        (
            gaina_term,
            shifta_term,
            biasa_term,
            gainb_term,
            shiftb_term,
            biasb_term,
            gainc_term,
            shiftc_term,
            projb_term,
        ),
        "dp",
    )
    return (
        block_out,
        image_grad,
        class_grad,
        gaina_grad,
        shifta_grad,
        conva_grad,
        biasa_grad,
        modw_grad,
        modb_grad,
        gainb_grad,
        shiftb_grad,
        convb_grad,
        biasb_grad,
        gainc_grad,
        shiftc_grad,
        qkvw_grad,
        projw_grad,
        projb_grad,
    )


def solution(mesh):
    placed = (
        P(("dp", "head"), None, None, None),
        P(("dp", "head"), None, None, None),
        P(),
        P(("dp", "head")),
        P(("dp", "head")),
        P(),
        P(None, "dp"),
        P("head"),
        P("head"),
        P("dp", None, "head"),
        P("head"),
        P("dp", None, None),
        P(),
        P("head"),
        P("head"),
        P("dp", None, "head"),
        P("head"),
        P("head"),
        P("head"),
        P("dp", None, "head"),
        P("dp", "head"),
        P("head"),
    )
    return jax.shard_map(
        shards,
        mesh=mesh,
        in_specs=placed,
        out_specs=(
            P(("dp", "head"), None, None, None),
            P(("dp", "head"), None, None, None),
            P(None, ("dp", "head")),
            P("head"),
            P("head"),
            P("dp", None, "head"),
            P("head"),
            P(("dp", "head"), None, None),
            P(None, ("dp", "head")),
            P("head"),
            P("head"),
            P("dp", None, "head"),
            P("head"),
            P("head"),
            P("head"),
            P("dp", None, "head"),
            P("dp", "head"),
            P("head"),
        ),
        check_vma=False,
    )
```

```python
import functools

import jax
import jax.numpy as jnp
from jax import lax
from jax.experimental import pallas as pl
from jax.experimental.pallas import tpu as pltpu
from jax.sharding import PartitionSpec as P

C = 768
DH = 64
GROUPS = 32


EPSILON = 1e-05
HIGHEST = lax.Precision.HIGHEST


def norm_forward(values, gain, shift):
    count, chans = (values.shape[0], values.shape[-1])
    span = C // GROUPS
    grouped = values.reshape(count, -1, chans // span, span)
    mean = jnp.mean(grouped, axis=(1, 3), keepdims=True)
    centred = grouped - mean
    inverse = lax.rsqrt(jnp.mean(centred * centred, axis=(1, 3), keepdims=True) + EPSILON)
    normed = (centred * inverse).reshape(values.shape)
    return (normed * gain + shift, normed, inverse)


def norm_backward(grad_out, normed, inverse, gain):
    grad_gain = jnp.sum(grad_out * normed, axis=(0, 1, 2))
    grad_shift = jnp.sum(grad_out, axis=(0, 1, 2))
    count, chans = (grad_out.shape[0], grad_out.shape[-1])
    span = C // GROUPS
    layout = (count, -1, chans // span, span)
    grad_normed = (grad_out * gain).reshape(layout)
    normed_groups = normed.reshape(layout)
    mean_one = jnp.mean(grad_normed, axis=(1, 3), keepdims=True)
    mean_two = jnp.mean(grad_normed * normed_groups, axis=(1, 3), keepdims=True)
    grad_in = inverse * (grad_normed - mean_one - normed_groups * mean_two)
    return (grad_in.reshape(grad_out.shape), grad_gain, grad_shift)


def silu_slope(values):
    sigma = jax.nn.sigmoid(values)
    return sigma * (1.0 + values * (1.0 - sigma))


def patches_of(act):
    count, rows, cols, chans = act.shape
    padded = jnp.pad(act, ((0, 0), (1, 1), (1, 1), (0, 0)))
    taps = [padded[:, i : i + rows, j : j + cols, :] for i in range(3) for j in range(3)]
    return jnp.stack(taps, axis=3).reshape(count * rows * cols, 9, chans)


def contract_rows(left, right):
    return lax.dot_general(
        left, right, (((0,), (0,)), ((), ())), preferred_element_type=jnp.float32
    )


def contract_cols(left, right):
    return lax.dot_general(
        left, right, (((1,), (1,)), ((), ())), preferred_element_type=jnp.float32
    )


def conv_back(grad_low, weight, count, rows, cols):
    chans = weight.shape[0]
    padded = jnp.zeros((count, rows + 2, cols + 2, chans), jnp.float32)
    for tap in range(9):
        i, j = divmod(tap, 3)
        part = contract_cols(grad_low, weight[:, tap, :]).reshape(count, rows, cols, chans)
        padded = padded.at[:, i : i + rows, j : j + cols, :].add(part)
    return padded[:, 1 : rows + 1, 1 : cols + 1, :]


def keep_same(values):
    return values


def live_rows(counts, first, number, count):
    sums = jnp.sum(counts, axis=1)
    chosen = lax.dynamic_slice_in_dim(sums, first, number)
    slots = lax.iota(jnp.int32, count)
    return (slots[None, :] < chosen[:, None]).astype(jnp.float32).reshape(number * count)


def residual_forward(source, mod_pair, weights, spread):
    (
        conv_one,
        conv_two,
        gain_one,
        shift_one,
        bias_one,
        gain_two,
        shift_two,
        bias_two,
        gain_three,
        shift_three,
    ) = weights
    out_a, normed_a, inverse_a = norm_forward(source, gain_one, shift_one)
    wide_a = spread(jax.nn.silu(out_a).astype(jnp.bfloat16))
    conv_out_a = (
        jnp.einsum("ptc,cto->po", patches_of(wide_a), conv_one, preferred_element_type=jnp.float32)
        + bias_one
    ).reshape(source.shape)
    scale = mod_pair[:, :, 0:1, :]
    offset = mod_pair[:, :, 1:2, :]
    out_b, normed_b, inverse_b = norm_forward(conv_out_a, gain_two, shift_two)
    inner_b = offset + out_b * (scale + 1.0)
    wide_b = spread(jax.nn.silu(inner_b).astype(jnp.bfloat16))
    conv_out_b = (
        jnp.einsum("ptc,cto->po", patches_of(wide_b), conv_two, preferred_element_type=jnp.float32)
        + bias_two
    ).reshape(source.shape)
    resid = source + conv_out_b
    out_c, normed_c, inverse_c = norm_forward(resid, gain_three, shift_three)
    attn_in = out_c.astype(jnp.bfloat16)
    saved = (
        out_a,
        normed_a,
        inverse_a,
        wide_a,
        out_b,
        normed_b,
        inverse_b,
        inner_b,
        wide_b,
        normed_c,
        inverse_c,
        scale,
    )
    return (resid, attn_in, saved)


def residual_backward(grad_attn, grad_out, saved, weights, reduce_value):
    conv_one, conv_two, gain_one, gain_two, gain_three = (
        weights[0],
        weights[1],
        weights[2],
        weights[5],
        weights[8],
    )
    (
        out_a,
        normed_a,
        inverse_a,
        wide_a,
        out_b,
        normed_b,
        inverse_b,
        inner_b,
        wide_b,
        normed_c,
        inverse_c,
        scale,
    ) = saved
    count, rows, cols, local = grad_out.shape
    grad_resid_c, gainc_term, shiftc_term = norm_backward(
        grad_attn, normed_c, inverse_c, gain_three
    )
    grad_resid = grad_out + grad_resid_c
    grad_conv_b = grad_resid.reshape(-1, local).astype(jnp.bfloat16)
    biasb_term = jnp.sum(grad_conv_b.astype(jnp.float32), axis=0)
    convb_term = jnp.einsum(
        "ptc,po->cto", patches_of(wide_b), grad_conv_b, preferred_element_type=jnp.float32
    )
    grad_act_b = reduce_value(conv_back(grad_conv_b, conv_two, count, rows, cols))
    grad_inner = grad_act_b * silu_slope(inner_b)
    grad_offset = jnp.sum(grad_inner, axis=(1, 2))
    grad_scale = jnp.sum(grad_inner * out_b, axis=(1, 2))
    grad_mod = jnp.stack([grad_scale, grad_offset], axis=1)[:, None]
    grad_conv_full, gainb_term, shiftb_term = norm_backward(
        grad_inner * (scale + 1.0), normed_b, inverse_b, gain_two
    )
    grad_conv_a = grad_conv_full.reshape(-1, local).astype(jnp.bfloat16)
    biasa_term = jnp.sum(grad_conv_a.astype(jnp.float32), axis=0)
    conva_term = jnp.einsum(
        "ptc,po->cto", patches_of(wide_a), grad_conv_a, preferred_element_type=jnp.float32
    )
    grad_act_a = reduce_value(conv_back(grad_conv_a, conv_one, count, rows, cols))
    grad_source, gaina_term, shifta_term = norm_backward(
        grad_act_a * silu_slope(out_a), normed_a, inverse_a, gain_one
    )
    image_grad = grad_resid + grad_source
    vectors = (
        gaina_term,
        shifta_term,
        biasa_term,
        gainb_term,
        shiftb_term,
        biasb_term,
        gainc_term,
        shiftc_term,
    )
    return (image_grad, grad_mod, (conva_term, convb_term), vectors)


def attend_forward(block):
    query, key, value = (block[:, :, 0], block[:, :, 1], block[:, :, 2])
    batch, pixels, heads_here, depth = query.shape
    scores = jnp.einsum("bqhd,bkhd->bhqk", query, key, preferred_element_type=jnp.float32) * DH ** (
        -0.5
    )
    top = jnp.max(scores, axis=-1, keepdims=True)
    weights = jnp.exp(scores - top)
    sums = jnp.sum(weights, axis=-1, keepdims=True)
    probs = (weights / sums).astype(jnp.bfloat16)
    logsum = (top + jnp.log(sums))[..., 0]
    mixed = jnp.einsum("bhqk,bkhd->bqhd", probs, value, preferred_element_type=jnp.float32).astype(
        jnp.bfloat16
    )
    return (mixed.reshape(batch, pixels, heads_here * depth), logsum)


def attend_backward(block, logsum, grad_head):
    query, key, value = (block[:, :, 0], block[:, :, 1], block[:, :, 2])
    batch, pixels, heads_here, depth = query.shape
    factor = DH ** (-0.5)
    scores = jnp.einsum("bqhd,bkhd->bhqk", query, key, preferred_element_type=jnp.float32) * factor
    probs = jnp.exp(scores - logsum[..., None])
    grad_value = jnp.einsum(
        "bhqk,bqhd->bkhd", probs.astype(jnp.bfloat16), grad_head, preferred_element_type=jnp.float32
    )
    grad_probs = jnp.einsum("bqhd,bkhd->bhqk", grad_head, value, preferred_element_type=jnp.float32)
    inner = jnp.sum(grad_probs * probs, axis=-1, keepdims=True)
    grad_scores = (probs * (grad_probs - inner)).astype(jnp.bfloat16)
    grad_query = (
        jnp.einsum("bhqk,bkhd->bqhd", grad_scores, key, preferred_element_type=jnp.float32) * factor
    )
    grad_key = (
        jnp.einsum("bhqk,bqhd->bkhd", grad_scores, query, preferred_element_type=jnp.float32)
        * factor
    )
    stacked = jnp.stack([grad_query, grad_key, grad_value], axis=2).astype(jnp.bfloat16)
    return stacked.reshape(batch, pixels, 3, heads_here * depth)


def plain_shards(
    images,
    cotangent,
    counts,
    labels,
    levels,
    noise_table,
    class_table,
    gain_a,
    shift_a,
    conv_a,
    bias_a,
    mod_weight,
    mod_bias,
    gain_b,
    shift_b,
    conv_b,
    bias_b,
    gain_c,
    shift_c,
    qkv_weight,
    proj_weight,
    proj_bias,
):
    rows_a, rows_b, rows_qkv, rows_proj, mod_full, class_full = (
        lax.all_gather(conv_a, "dp", axis=0, tiled=True),
        lax.all_gather(conv_b, "dp", axis=0, tiled=True),
        lax.all_gather(qkv_weight, "dp", axis=0, tiled=True),
        lax.all_gather(proj_weight, "dp", axis=0, tiled=True),
        lax.all_gather(mod_weight, "dp", axis=0, tiled=True),
        lax.all_gather(class_table, "dp", axis=1, tiled=True),
    )
    count, rows, cols, channels = images.shape
    pixels = rows * cols
    groups_n = lax.axis_size("head")
    quarter = channels // groups_n
    heads_local = quarter // DH
    first_dp = lax.axis_index("dp") * groups_n
    class_hot = (labels[:, None] == lax.iota(jnp.int32, class_full.shape[0])[None, :]).astype(
        jnp.bfloat16
    )
    level_hot = (levels[:, None] == lax.iota(jnp.int32, noise_table.shape[0])[None, :]).astype(
        jnp.bfloat16
    )
    embed_pre = jnp.dot(class_hot, class_full, preferred_element_type=jnp.float32) + jnp.dot(
        level_hot, noise_table, preferred_element_type=jnp.float32
    )
    embed = jax.nn.silu(embed_pre).astype(jnp.bfloat16)
    modulation = (
        jnp.einsum("ne,etc->ntc", embed, mod_full, preferred_element_type=jnp.float32)
        + mod_bias.astype(jnp.float32)
    ).astype(jnp.bfloat16)
    mod_pair = modulation.reshape(count, 1, 2, channels)
    (
        conv_one,
        conv_two,
        qkv_full,
        proj_full,
        gain_one,
        shift_one,
        bias_one,
        gain_two,
        shift_two,
        bias_two,
        gain_three,
        shift_three,
        bias_three,
    ) = (
        lax.all_gather(rows_a, "head", axis=2, tiled=True),
        lax.all_gather(rows_b, "head", axis=2, tiled=True),
        lax.all_gather(rows_qkv, "head", axis=2, tiled=True),
        lax.all_gather(rows_proj, "head", axis=1, tiled=True),
        lax.all_gather(gain_a, "head", axis=0, tiled=True),
        lax.all_gather(shift_a, "head", axis=0, tiled=True),
        lax.all_gather(bias_a, "head", axis=0, tiled=True),
        lax.all_gather(gain_b, "head", axis=0, tiled=True),
        lax.all_gather(shift_b, "head", axis=0, tiled=True),
        lax.all_gather(bias_b, "head", axis=0, tiled=True),
        lax.all_gather(gain_c, "head", axis=0, tiled=True),
        lax.all_gather(shift_c, "head", axis=0, tiled=True),
        lax.all_gather(proj_bias, "head", axis=0, tiled=True),
    )
    weights = (
        conv_one,
        conv_two,
        gain_one,
        shift_one,
        bias_one,
        gain_two,
        shift_two,
        bias_two,
        gain_three,
        shift_three,
    )
    live = live_rows(counts, first_dp + lax.axis_index("head"), 1, count)
    total = count * pixels
    width = channels // groups_n
    source = images.astype(jnp.float32)
    resid, attn_in, saved = residual_forward(
        source, mod_pair.astype(jnp.float32), weights, keep_same
    )
    attn_flat = attn_in.reshape(total, channels)
    qkv_flat = qkv_full.reshape(channels, 3 * channels)
    qkv = jnp.dot(attn_flat, qkv_flat, preferred_element_type=jnp.float32).astype(jnp.bfloat16)
    packed = qkv.reshape(1, count, pixels, 3, groups_n, width)
    block = lax.all_to_all(packed, "head", split_axis=4, concat_axis=0, tiled=True)
    groups = block.shape[0]
    items = block.shape[1]
    flat = block.reshape(groups * items, pixels, 3, heads_local, DH)
    mixed, logsum = attend_forward(flat)
    mixed = mixed.reshape(groups, items, pixels, 1, width)
    returned = lax.all_to_all(mixed, "head", split_axis=0, concat_axis=3, tiled=True)
    returned, logsum, kept = (returned, logsum.reshape(groups, items, heads_local, pixels), block)
    mixed_image = returned.reshape(total, channels)
    result = (
        resid.reshape(total, channels)
        + jnp.dot(mixed_image, proj_full, preferred_element_type=jnp.float32)
        + bias_three
    )
    block_out = (result.reshape(images.shape) * live[:, None, None, None]).astype(jnp.bfloat16)
    grad_out = cotangent.astype(jnp.float32) * live[:, None, None, None]
    grad_flat = grad_out.reshape(total, channels)
    grad_low = grad_flat.astype(jnp.bfloat16)
    projw_full = contract_rows(mixed_image, grad_low)
    projb_full = jnp.sum(grad_flat, axis=0)
    grad_mixed = contract_cols(grad_low, proj_full).astype(jnp.bfloat16)
    arrived = lax.all_to_all(
        grad_mixed.reshape(1, count, pixels, groups_n, width),
        "head",
        split_axis=3,
        concat_axis=0,
        tiled=True,
    )
    flat_block = kept.reshape(groups_n * count, pixels, 3, heads_local, DH)
    grad_head = arrived.reshape(groups_n * count, pixels, heads_local, DH)
    stacked = attend_backward(
        flat_block, logsum.reshape(groups_n * count, heads_local, pixels), grad_head
    )
    stacked = stacked.reshape(groups_n, count, pixels, 3, 1, width)
    grad_qkv = lax.all_to_all(stacked, "head", split_axis=0, concat_axis=4, tiled=True).reshape(
        total, 3 * channels
    )
    qkvw_full = contract_rows(attn_flat, grad_qkv).reshape(channels, 3, channels)
    grad_attn = contract_cols(grad_qkv, qkv_flat).reshape(images.shape)
    image_grad, grad_mod_part, conv_terms, vectors = residual_backward(
        grad_attn, grad_out, saved, weights, keep_same
    )
    (
        gaina_full,
        shifta_full,
        biasa_full,
        gainb_full,
        shiftb_full,
        biasb_full,
        gainc_full,
        shiftc_full,
    ) = vectors
    (
        conva_term,
        convb_term,
        qkvw_term,
        projw_term,
        gaina_term,
        shifta_term,
        biasa_term,
        gainb_term,
        shiftb_term,
        biasb_term,
        gainc_term,
        shiftc_term,
        projb_term,
    ) = (
        lax.psum_scatter(
            conv_terms[0].astype(jnp.bfloat16), "head", scatter_dimension=2, tiled=True
        ).astype(jnp.float32),
        lax.psum_scatter(
            conv_terms[1].astype(jnp.bfloat16), "head", scatter_dimension=2, tiled=True
        ).astype(jnp.float32),
        lax.psum_scatter(
            qkvw_full.astype(jnp.bfloat16), "head", scatter_dimension=2, tiled=True
        ).astype(jnp.float32),
        lax.psum_scatter(
            projw_full.astype(jnp.bfloat16), "head", scatter_dimension=1, tiled=True
        ).astype(jnp.float32),
        lax.psum_scatter(
            gaina_full.astype(jnp.bfloat16), "head", scatter_dimension=0, tiled=True
        ).astype(jnp.float32),
        lax.psum_scatter(
            shifta_full.astype(jnp.bfloat16), "head", scatter_dimension=0, tiled=True
        ).astype(jnp.float32),
        lax.psum_scatter(
            biasa_full.astype(jnp.bfloat16), "head", scatter_dimension=0, tiled=True
        ).astype(jnp.float32),
        lax.psum_scatter(
            gainb_full.astype(jnp.bfloat16), "head", scatter_dimension=0, tiled=True
        ).astype(jnp.float32),
        lax.psum_scatter(
            shiftb_full.astype(jnp.bfloat16), "head", scatter_dimension=0, tiled=True
        ).astype(jnp.float32),
        lax.psum_scatter(
            biasb_full.astype(jnp.bfloat16), "head", scatter_dimension=0, tiled=True
        ).astype(jnp.float32),
        lax.psum_scatter(
            gainc_full.astype(jnp.bfloat16), "head", scatter_dimension=0, tiled=True
        ).astype(jnp.float32),
        lax.psum_scatter(
            shiftc_full.astype(jnp.bfloat16), "head", scatter_dimension=0, tiled=True
        ).astype(jnp.float32),
        lax.psum_scatter(
            projb_full.astype(jnp.bfloat16), "head", scatter_dimension=0, tiled=True
        ).astype(jnp.float32),
    )
    grad_mod = grad_mod_part.reshape(count, 2, channels)
    modw_term = jnp.einsum("ne,ntc->etc", embed.astype(jnp.float32), grad_mod, precision=HIGHEST)
    modb_term = jnp.sum(grad_mod, axis=0)
    grad_embed = jnp.einsum(
        "ntc,etc->ne", grad_mod, mod_full.astype(jnp.float32), precision=HIGHEST
    ) * silu_slope(embed_pre)
    class_term = lax.dot_general(
        class_hot.astype(jnp.float32), grad_embed, (((0,), (0,)), ((), ())), precision=HIGHEST
    )
    modw_grad, class_grad, modb_grad = (
        lax.psum_scatter(modw_term, ("dp", "head"), scatter_dimension=0, tiled=True),
        lax.psum_scatter(class_term, ("dp", "head"), scatter_dimension=1, tiled=True),
        lax.psum_scatter(modb_term, ("dp", "head"), scatter_dimension=1, tiled=True),
    )
    conva_grad, convb_grad, qkvw_grad, projw_grad = (
        lax.psum_scatter(conva_term, "dp", scatter_dimension=0, tiled=True),
        lax.psum_scatter(convb_term, "dp", scatter_dimension=0, tiled=True),
        lax.psum_scatter(qkvw_term, "dp", scatter_dimension=0, tiled=True),
        lax.psum_scatter(projw_term, "dp", scatter_dimension=0, tiled=True),
    )
    (
        gaina_grad,
        shifta_grad,
        biasa_grad,
        gainb_grad,
        shiftb_grad,
        biasb_grad,
        gainc_grad,
        shiftc_grad,
        projb_grad,
    ) = lax.psum(
        (
            gaina_term,
            shifta_term,
            biasa_term,
            gainb_term,
            shiftb_term,
            biasb_term,
            gainc_term,
            shiftc_term,
            projb_term,
        ),
        "dp",
    )
    return (
        block_out,
        image_grad,
        class_grad,
        gaina_grad,
        shifta_grad,
        conva_grad,
        biasa_grad,
        modw_grad,
        modb_grad,
        gainb_grad,
        shiftb_grad,
        convb_grad,
        biasb_grad,
        gainc_grad,
        shiftc_grad,
        qkvw_grad,
        projw_grad,
        projb_grad,
    )


MESH = pl.DeviceIdType.MESH
UNITS = 22
PAIRS = UNITS // 2
RES = 8
SLOTS = 8
PIX = RES * RES
LINE = SLOTS * RES
ALL = RES * LINE
WIDTH = 256
F32 = jnp.float32
BF16 = jnp.bfloat16
ANY = pl.BlockSpec(memory_space=pl.ANY)
VMEM = pl.BlockSpec(memory_space=pltpu.VMEM)
DMA = pltpu.SemaphoreType.DMA
DW_ORDER = (10, 9, 5, 6, 7, 8, 4, 0, 1, 2, 3)


def place():
    d, h = lax.axis_index("dp"), lax.axis_index("head")
    return d // 2, lax.rem(d, 2), h // 2, lax.rem(h, 2)


def at_chip(z, y, x, c):
    return (z * 2 + y, x * 2 + c)


def column_peers(n_dp):
    d, h = lax.axis_index("dp"), lax.axis_index("head")
    return [(lax.rem(d + k, n_dp), h) for k in range(1, n_dp)]


def head_peers(n_head):
    d, h = lax.axis_index("dp"), lax.axis_index("head")
    return [(d, lax.rem(h + k, n_head)) for k in range(1, n_head)]


def greet(devices):
    barrier = pltpu.get_barrier_semaphore()
    for device in devices:
        pl.semaphore_signal(barrier, inc=1, device_id=device, device_id_type=MESH)
    pl.semaphore_wait(barrier, len(devices))


def remote(src, dst, send, recv, device):
    return pltpu.make_async_remote_copy(
        src_ref=src, dst_ref=dst, send_sem=send, recv_sem=recv, device_id=device, device_id_type=MESH
    )


def each(count, body):
    def step(n, carry):
        body(n)
        return carry

    lax.fori_loop(0, count, step, 0)


def span(index, size):
    return pl.ds(pl.multiple_of(index * size, size), size)


def row(n):
    return pl.ds(n, 1)


def lines_from(i):
    return pl.ds(i * LINE if isinstance(i, int) else pl.multiple_of(i * LINE, LINE), ALL)


def dot(left, right):
    return jnp.dot(left, right, preferred_element_type=F32)


def dot_nt(left, right):
    return lax.dot_general(left, right, (((1,), (1,)), ((), ())), preferred_element_type=F32)


def dot_tn(left, right):
    return lax.dot_general(left, right, (((0,), (0,)), ((), ())), preferred_element_type=F32)


def in_group(first, second, axis):
    chan = lax.broadcasted_iota(jnp.int32, (first, second), axis)
    group = lax.broadcasted_iota(jnp.int32, (first, second), 1 - axis) * (C // GROUPS)
    inside = jnp.logical_and(chan >= group, chan < group + C // GROUPS)
    return jnp.where(inside, 1.0, 0.0).astype(BF16)


def pieces(values):
    high = values.astype(BF16).astype(F32)
    rest = values - high
    mid = rest.astype(BF16).astype(F32)
    return jnp.concatenate([high, mid, rest - mid], axis=0).astype(BF16)


def group_mean(sums):
    count = sums.shape[0]
    part = dot(pieces(sums), in_group(C, 128, 0))
    part = (part[:count] + part[count : 2 * count] + part[2 * count :]) * (1.0 / (PIX * (C // GROUPS)))
    back = dot(pieces(part), in_group(128, C, 1))
    return back[:count] + back[count : 2 * count] + back[2 * count :]


def sum_rows(values):
    return jnp.sum(values, axis=0, keepdims=True)


def norm_stats(get, mean_ref, inverse_ref, sums_ref):
    def first(n):
        sums_ref[row(n)] = sum_rows(get(n))

    each(SLOTS, first)
    mean_ref[...] = group_mean(sums_ref[...])

    def second(n):
        centred = get(n) - mean_ref[row(n)]
        sums_ref[row(n)] = sum_rows(centred * centred)

    each(SLOTS, second)
    inverse_ref[...] = lax.rsqrt(group_mean(sums_ref[...]) + EPSILON)


def silu(values):
    return values * jax.nn.sigmoid(values)


def shifted(values):
    spot = lax.rem(lax.broadcasted_iota(jnp.int32, values.shape, 0), RES)
    left = jnp.where(spot == 0, 0.0, pltpu.roll(values, 1, 0))
    right = jnp.where(spot == RES - 1, 0.0, pltpu.roll(values, values.shape[0] - 1, 0))
    return left, right


def chunk(n):
    return slice(n * WIDTH, (n + 1) * WIDTH)


CHUNKS = C // WIDTH


def weight_cols(ref, n):
    return ref[:, :, :, chunk(n)].reshape(C, WIDTH)


def weight_rows(ref, n):
    return ref[...].reshape(C, C)[chunk(n)]


def forward_kernel(
    lines,
    units_ref,
    vec_ref,
    images_ref,
    ids_ref,
    class_ref,
    noise_ref,
    modw_ref,
    modb_ref,
    whole_ref,
    vecs_ref,
    mod_ref,
    conv_ref,
    resid_ref,
    turned_a,
    turned_b,
    stats_ref,
    pre_ref,
    all_ids,
    halves,
    block,
    vec_all,
    mod_part,
    mod_got,
    act,
    act_f32,
    weights,
    sums_ref,
    pair_send,
    pair_recv,
    pair_local,
    own_sem,
    z_send,
    z_recv,
    x_send,
    x_recv,
    y_send,
    y_recv,
    s_send,
    s_recv,
    vec_send,
    vec_recv,
    ids_send,
    ids_recv,
    mod_send,
    mod_recv,
    load_sem,
):
    z, y, x, c = place()
    d, h = lax.axis_index("dp"), lax.axis_index("head")
    n_dp, n_head = lines * 2, 4
    half = lines // 2
    rows = block.shape[1]
    wide = block.shape[2]
    sibling = at_chip(z, y, x, 1 - c)
    along_x = at_chip(z, y, 1 - x, c)
    along_y = at_chip(z, 1 - y, x, c)
    line = [at_chip(lax.rem(z + k, lines), y, x, c) for k in range(1, lines)]
    column, heads = column_peers(n_dp), head_peers(n_head)
    greet(column + heads)

    def spot(i, cc, zz, yy, xx):
        return whole_ref.at[i, cc, zz, yy, :, span(xx, wide)]

    swap = remote(units_ref.at[:, 1 - c], halves.at[c], pair_send, pair_recv, sibling)
    keep = pltpu.make_async_copy(units_ref.at[:, c], halves.at[c], pair_local)

    def vec_copy(k):
        return remote(vec_ref, vec_all.at[h], vec_send.at[k], vec_recv.at[k], heads[k])

    def ids_copy(k):
        return remote(ids_ref, all_ids.at[d], ids_send.at[k], ids_recv.at[k], column[k])

    def mod_copy(k):
        return remote(
            mod_part.at[lax.rem(d + k + 1, n_dp)], mod_got.at[d], mod_send.at[k], mod_recv.at[k], column[k]
        )

    def own_copy(i):
        return pltpu.make_async_copy(block.at[i], spot(i, c, z, y, x), own_sem.at[i])

    def z_copy(i, k):
        return remote(block.at[i], spot(i, c, z, y, x), z_send.at[i, k], z_recv.at[i, k], line[k])

    def x_copy(i, part):
        if part == 0:
            ref = spot(i, c, slice(None), y, x)
        else:
            ref = spot(i, c, pl.ds(half, half), 1 - y, x)
        return remote(ref, ref, x_send.at[i, part], x_recv.at[i, part], along_x)

    def y_copy(i, part):
        if part == 0:
            ref = spot(i, c, slice(None), y, x)
        else:
            ref = spot(i, c, pl.ds(0, half), y, 1 - x)
        return remote(ref, ref, y_send.at[i, part], y_recv.at[i, part], along_y)

    def s_copy(i, part):
        yy, xx = ((y, x), (y, 1 - x), (1 - y, x), (1 - y, 1 - x))[part]
        ref = spot(i, c, slice(None), yy, xx)
        return remote(ref, ref, s_send.at[i, part], s_recv.at[i, part], sibling)

    def begin(i):
        block[i] = jnp.concatenate([halves[0, i], halves[1, i]], axis=-1)
        own_copy(i).start()
        for k in range(lines - 1):
            z_copy(i, k).start()

    def spread_line(i):
        own_copy(i).wait()
        for k in range(lines - 1):
            z_copy(i, k).wait_recv()
        x_copy(i, 0).start()
        y_copy(i, 0).start()
        s_copy(i, 0).start()

    def pass_on(i):
        x_copy(i, 0).wait_recv()
        y_copy(i, 1).start()
        s_copy(i, 1).start()
        y_copy(i, 0).wait_recv()
        x_copy(i, 1).start()
        s_copy(i, 2).start()

    def finish(i):
        x_copy(i, 1).wait_recv()
        y_copy(i, 1).wait_recv()
        s_copy(i, 3).start()

    def arrived(i):
        for part in range(4):
            s_copy(i, part).wait_recv()

    def load(i, k):
        slot = lax.rem(i, 2)
        return pltpu.make_async_copy(whole_ref.at[i, k], weights.at[slot, k], load_sem.at[slot, k])

    def fetch(i):
        arrived(i)
        load(i, 0).start()
        load(i, 1).start()

    def product(total, tap, slot, k):
        for n in range(CHUNKS):
            value = dot(act[tap % 3, lines_from(tap // 3)], weight_cols(weights.at[slot, k], n))
            total[:, :, :, chunk(n)] += value.reshape(RES, SLOTS, RES, WIDTH)

    def use_pair(total, i, first):
        slot = lax.rem(i, 2)
        load(i, 0).wait()
        load(i, 1).wait()
        for k in range(2):
            product(total, 2 * (i - first) + k, slot, k)

    def set_act(turned):
        def by_line(yy):
            value = act_f32[yy].reshape(LINE, C)
            left, right = shifted(value)
            spot_rows = pl.ds(pl.multiple_of((yy + 1) * LINE, LINE), LINE)
            act[0, spot_rows] = left.astype(BF16)
            act[1, spot_rows] = value.astype(BF16)
            act[2, spot_rows] = right.astype(BF16)

        each(RES, by_line)

        def turn(yy):
            value = act_f32[pl.ds(2 * yy, 2)].reshape(2 * LINE, C)
            turned[:, span(yy, 2 * LINE)] = value.T.astype(BF16)

        each(RES // 2, turn)

    def norm_a():
        for k in range(n_head - 1):
            vec_copy(k).wait()
        vecs_ref[...] = jnp.concatenate([vec_all[k].astype(F32) for k in range(n_head)], axis=-1)

        def get(n):
            return images_ref[span(n, PIX)].astype(F32)

        mean, inverse = stats_ref.at[0], stats_ref.at[1]
        norm_stats(get, mean, inverse, sums_ref)

        def to_act(n):
            value = (get(n) - mean[row(n)]) * inverse[row(n)]
            act_f32[:, n] = silu(value * vecs_ref[0:1] + vecs_ref[1:2]).reshape(RES, RES, C)
            conv_ref[:, n] = jnp.broadcast_to(vecs_ref[2:3].reshape(1, 1, C), (RES, RES, C))
            resid_ref[:, n] = (get(n) + vecs_ref[5:6]).reshape(RES, RES, C)

        each(SLOTS, to_act)
        set_act(turned_a)

    def embed():
        for k in range(n_dp - 1):
            ids_copy(k).wait()
        ids = all_ids[...].reshape(n_dp * SLOTS, 128)
        table = class_ref.shape[0]
        label_hot = lax.broadcasted_iota(jnp.int32, (n_dp * SLOTS, table), 1) == ids[:, 0:1]
        level_hot = lax.broadcasted_iota(jnp.int32, (n_dp * SLOTS, 128), 1) == ids[:, 1:2]
        pre = dot(jnp.where(label_hot, 1.0, 0.0).astype(BF16), class_ref[...])
        pre += dot(jnp.where(level_hot, 1.0, 0.0).astype(BF16), noise_ref[...])
        pre_ref[...] = pre
        part = dot(silu(pre).astype(BF16), modw_ref[...])
        for k in range(n_dp):
            mine = part[k * SLOTS : (k + 1) * SLOTS]
            mod_part[k] = jnp.concatenate([mine[:, :C], mine[:, C:]], axis=0).astype(BF16)
        mod_got[d] = mod_part[d]
        for k in range(n_dp - 1):
            mod_copy(k).start()

    def norm_b():
        for k in range(n_dp - 1):
            mod_copy(k).wait()
        total = modb_ref[...]
        for k in range(n_dp):
            total += mod_got[k].astype(F32)
        mod_ref[...] = total.astype(BF16).astype(F32)

        def get(n):
            return conv_ref[:, n].reshape(PIX, C)

        mean, inverse = stats_ref.at[2], stats_ref.at[3]
        norm_stats(get, mean, inverse, sums_ref)

        def to_act(n):
            value = (get(n) - mean[row(n)]) * inverse[row(n)]
            value = value * vecs_ref[3:4] + vecs_ref[4:5]
            value = mod_ref[row(SLOTS + n)] + value * (mod_ref[row(n)] + 1.0)
            act_f32[:, n] = silu(value).reshape(RES, RES, C)

        each(SLOTS, to_act)
        set_act(turned_b)

    swap.start()
    keep.start()
    for k in range(n_head - 1):
        vec_copy(k).start()
    for k in range(n_dp - 1):
        ids_copy(k).start()
    vec_all[h] = vec_ref[...]
    all_ids[d] = ids_ref[...]
    edge = jnp.zeros((LINE, C), BF16)
    for j in range(3):
        act[j, 0:LINE] = edge
        act[j, ALL + LINE : ALL + 2 * LINE] = edge
    keep.wait()
    swap.wait()
    each(PAIRS, begin)

    spread_line(0)
    spread_line(1)
    pass_on(0)
    norm_a()
    spread_line(2)
    pass_on(1)
    finish(0)
    embed()
    spread_line(3)
    pass_on(2)
    finish(1)
    fetch(0)

    def turns(first, last, total, start):
        def body(turn, carry):
            spread_line(turn)
            pass_on(turn - 1)
            finish(turn - 2)
            fetch(turn - 3)
            use_pair(total, turn - 4, start)
            return carry

        lax.fori_loop(first, last, body, 0)

    turns(4, 8, conv_ref, 0)
    spread_line(8)
    pass_on(7)
    finish(6)
    fetch(5)
    load(4, 0).wait()
    load(4, 1).wait()
    product(conv_ref, 8, 0, 0)
    norm_b()
    product(resid_ref, 8, 0, 1)
    turns(9, 11, resid_ref, 5)
    pass_on(10)
    finish(9)
    fetch(8)
    use_pair(resid_ref, 7, 5)
    finish(10)
    use_pair(resid_ref, 8, 5)
    arrived(9)
    arrived(10)

    def drain(i):
        for k in range(lines - 1):
            z_copy(i, k).wait_send()
        for part in range(2):
            x_copy(i, part).wait_send()
            y_copy(i, part).wait_send()
        for part in range(4):
            s_copy(i, part).wait_send()

    each(PAIRS, drain)


def run_forward(taps, vec, images, ids, class_rows, noise_rows, mod_rows, mod_bias):
    n_dp, n_head = lax.axis_size("dp"), lax.axis_size("head")
    units, rows, cols = taps.shape
    lines, across, wide = n_dp // 2, n_head // 2, 2 * cols
    board = (RES, SLOTS, RES, C)
    shape = jax.ShapeDtypeStruct
    return pl.pallas_call(
        functools.partial(forward_kernel, lines),
        out_shape=(
            shape((PAIRS, 2, lines, 2, rows, across * wide), BF16),
            shape((16, C), F32),
            shape((2 * SLOTS, C), F32),
            shape(board, F32),
            shape(board, F32),
            shape((C, ALL), BF16),
            shape((C, ALL), BF16),
            shape((4, SLOTS, C), F32),
            shape((n_dp * SLOTS, 128), F32),
            shape((n_dp, SLOTS, 128), jnp.int32),
        ),
        in_specs=[ANY] + [VMEM] * 7,
        out_specs=(ANY,) + (VMEM,) * 9,
        scratch_shapes=[
            pltpu.VMEM((2, PAIRS, rows, cols), BF16),
            pltpu.VMEM((PAIRS, rows, wide), BF16),
            pltpu.VMEM((n_head, 16, cols), BF16),
            pltpu.VMEM((n_dp, 2 * SLOTS, C), BF16),
            pltpu.VMEM((n_dp, 2 * SLOTS, C), BF16),
            pltpu.VMEM((3, ALL + 2 * LINE, C), BF16),
            pltpu.VMEM(board, F32),
            pltpu.VMEM((2, 2, lines, 2, rows, across * wide), BF16),
            pltpu.VMEM((SLOTS, C), F32),
            DMA,
            DMA,
            DMA,
            DMA((PAIRS,)),
            DMA((PAIRS, lines - 1)),
            DMA((PAIRS, lines - 1)),
            DMA((PAIRS, 2)),
            DMA((PAIRS, 2)),
            DMA((PAIRS, 2)),
            DMA((PAIRS, 2)),
            DMA((PAIRS, 4)),
            DMA((PAIRS, 4)),
            DMA((n_head - 1,)),
            DMA((n_head - 1,)),
            DMA((n_dp - 1,)),
            DMA((n_dp - 1,)),
            DMA((n_dp - 1,)),
            DMA((n_dp - 1,)),
            DMA((2, 2)),
        ],
        compiler_params=pltpu.CompilerParams(
            collective_id=0, has_side_effects=True, vmem_limit_bytes=48 * 2**20
        ),
        name="gather_forward",
    )(taps.reshape(PAIRS, 2, rows, cols), vec, images, ids, class_rows, noise_rows, mod_rows, mod_bias)


def attend_kernel(
    whole_ref,
    resid_ref,
    cot_ref,
    live_ref,
    vecs_ref,
    out_ref,
    grad_ref,
    grad_low,
    turned,
    right,
    sums_out,
    attn_in,
    qkv,
    weights,
    grad_attn,
    mixed,
    mean,
    inverse,
    sums_ref,
    pair_ref,
    load_sem,
):
    first = whole_ref.shape[0] - 2

    def load(k):
        return pltpu.make_async_copy(whole_ref.at[first + k // 2, k % 2], weights.at[k], load_sem.at[k])

    for k in range(4):
        load(k).start()

    def get(n):
        return resid_ref[:, n].reshape(PIX, C)

    norm_stats(get, mean, inverse, sums_ref)
    sums_out[...] = jnp.zeros_like(sums_out)

    def normed(n):
        return (get(n) - mean[row(n)]) * inverse[row(n)]

    def prepare(n):
        attn_in[span(n, PIX)] = (normed(n) * vecs_ref[6:7] + vecs_ref[7:8]).astype(BF16)
        grad = cot_ref[span(n, PIX)].astype(F32) * live_ref[row(n)]
        right[3, span(n, PIX)] = grad.astype(BF16)
        sums_out[8:9] += sum_rows(grad)

    each(SLOTS, prepare)
    for k in range(4):
        load(k).wait()
    for t in range(3):
        for n in range(CHUNKS):
            qkv[t, :, chunk(n)] = dot(attn_in[...], weight_cols(weights.at[t], n)).astype(BF16)
    for n in range(CHUNKS):
        qkv[3, :, chunk(n)] = dot_nt(right[3], weight_rows(weights.at[3], n)).astype(BF16)

    factor = DH ** (-0.5)
    lane = lax.broadcasted_iota(jnp.int32, (PIX, 2 * DH), 1)
    low = lane < DH

    def stack(value):
        zero = jnp.zeros_like(value)
        return jnp.concatenate([jnp.where(low, value, zero), jnp.where(low, zero, value)], axis=0)

    def pick(value):
        return jnp.where(low, value[:PIX], value[PIX:])

    def attend(n):
        for pair in range(C // (2 * DH)):
            lanes = slice(pair * 2 * DH, (pair + 1) * 2 * DH)
            query, key, value, grad = (qkv[t, span(n, PIX), lanes] for t in range(4))
            query2, grad2 = stack(query), stack(grad)
            scores = dot_nt(query2, key) * factor
            weight = jnp.exp(scores - jnp.max(scores, axis=-1, keepdims=True))
            probs = weight / jnp.sum(weight, axis=-1, keepdims=True)
            probs_low = probs.astype(BF16)
            mixed[span(n, PIX), lanes] = pick(dot(probs_low, value)).astype(BF16)
            grad_probs = dot_nt(grad2, value)
            inner = jnp.sum(grad_probs * probs, axis=-1, keepdims=True)
            grad_scores = (probs * (grad_probs - inner)).astype(BF16)
            right[0, span(n, PIX), lanes] = (pick(dot(grad_scores, key)) * factor).astype(BF16)
            right[1, span(n, PIX), lanes] = (dot_tn(grad_scores, query2) * factor).astype(BF16)
            right[2, span(n, PIX), lanes] = dot_tn(probs_low, grad2).astype(BF16)

    each(SLOTS, attend)

    for n in range(CHUNKS):
        grad_attn[:, chunk(n)] = dot(mixed[...], weight_cols(weights.at[3], n))

    def finish(n):
        value = get(n) + grad_attn[span(n, PIX)] + vecs_ref[8:9]
        out_ref[span(n, PIX)] = (value * live_ref[row(n)]).astype(BF16)

    each(SLOTS, finish)

    def turn(k):
        for slot, source in ((0, attn_in), (1, mixed)):
            value = source[span(k, 128)].astype(F32)
            turned[slot, :, span(k, 128)] = value.T.astype(BF16)

    each(ALL // 128, turn)

    for n in range(CHUNKS):
        total = None
        for t in range(3):
            value = dot_nt(right[t], weight_rows(weights.at[t], n))
            total = value if total is None else total + value
        grad_attn[:, chunk(n)] = total

    def back(n):
        grad, gn = grad_attn[span(n, PIX)], normed(n)
        sums_out[6:7] += sum_rows(grad * gn)
        sums_out[7:8] += sum_rows(grad)
        head = grad * vecs_ref[6:7]
        pair_ref[row(n)] = sum_rows(head)
        pair_ref[row(SLOTS + n)] = sum_rows(head * gn)

    each(SLOTS, back)
    pair_ref[...] = group_mean(pair_ref[...])

    def back_second(n):
        gn = normed(n)
        head = grad_attn[span(n, PIX)] * vecs_ref[6:7]
        value = inverse[row(n)] * (head - pair_ref[row(n)] - gn * pair_ref[row(SLOTS + n)])
        value += right[3, span(n, PIX)].astype(F32)
        grad_ref[:, n] = value.reshape(RES, RES, C)
        sums_out[5:6] += sum_rows(value.astype(BF16).astype(F32))

    each(SLOTS, back_second)

    def lower(yy):
        grad_low[span(yy, LINE)] = grad_ref[yy].reshape(LINE, C).astype(BF16)

    each(RES, lower)


def run_attention(whole, resid, cotangent, live, vecs):
    board = (RES, SLOTS, RES, C)
    shape = jax.ShapeDtypeStruct
    return pl.pallas_call(
        attend_kernel,
        out_shape=(
            shape((ALL, C), BF16),
            shape(board, F32),
            shape((ALL, C), BF16),
            shape((2, C, ALL), BF16),
            shape((4, ALL, C), BF16),
            shape((16, C), F32),
        ),
        in_specs=[ANY] + [VMEM] * 4,
        out_specs=(VMEM,) * 6,
        scratch_shapes=[
            pltpu.VMEM((ALL, C), BF16),
            pltpu.VMEM((4, ALL, C), BF16),
            pltpu.VMEM((4,) + whole.shape[2:], BF16),
            pltpu.VMEM((ALL, C), F32),
            pltpu.VMEM((ALL, C), BF16),
            pltpu.VMEM((SLOTS, C), F32),
            pltpu.VMEM((SLOTS, C), F32),
            pltpu.VMEM((SLOTS, C), F32),
            pltpu.VMEM((2 * SLOTS, C), F32),
            DMA((4,)),
        ],
        compiler_params=pltpu.CompilerParams(vmem_limit_bytes=56 * 2**20),
        name="attention",
    )(whole, resid, cotangent, live, vecs)


def backward_kernel(
    lines,
    whole_ref,
    turned_a,
    turned_b,
    turned_ref,
    right_ref,
    grad_low_ref,
    grad_resid_ref,
    conv_ref,
    images_ref,
    stats_ref,
    vecs_ref,
    mod_ref,
    sums_in,
    pre_ref,
    ids_ref,
    modw_ref,
    out_ref,
    image_ref,
    class_ref,
    modw_out,
    vec_out,
    mine,
    from_x,
    from_y,
    from_z,
    ends,
    lefts,
    rights,
    grads,
    stage,
    weights,
    total,
    sums_ref,
    pair_ref,
    gm_mine,
    gm_all,
    mw_mine,
    mw_got,
    ge_all,
    vs_mine,
    vs_got,
    vt_mine,
    vt_all,
    x_send,
    x_recv,
    y_send,
    y_recv,
    z_send,
    z_recv,
    e_send,
    e_recv,
    e_local,
    op_send,
    op_recv,
    op_local,
    load_sem,
    gm_send,
    gm_recv,
    mw_send,
    mw_recv,
    ge_send,
    ge_recv,
    vs_send,
    vs_recv,
    vt_send,
    vt_recv,
):
    z, y, x, c = place()
    d, h = lax.axis_index("dp"), lax.axis_index("head")
    n_dp, n_head = lines * 2, 4
    half = lines // 2
    rows, wide = from_z.shape[2], from_z.shape[3]
    cols = wide // 2
    sibling = at_chip(z, y, x, 1 - c)
    along_x = at_chip(z, y, 1 - x, c)
    along_y = at_chip(z, 1 - y, x, c)
    line = [at_chip(lax.rem(z + k, lines), y, x, c) for k in range(1, lines)]
    column, heads = column_peers(n_dp), head_peers(n_head)

    own_rows = pl.ds(LINE, ALL)

    def operand(k):
        if k == 0:
            return right_ref.at[2 + c], right_ref.at[3 - c], rights.at[0, c]
        if k == 1:
            return turned_ref.at[c], turned_ref.at[1 - c], lefts.at[1, c]
        if k == 2:
            return right_ref.at[c], right_ref.at[1 - c], rights.at[1, c]
        if k == 3:
            return turned_ref.at[0], turned_ref.at[0], lefts.at[0, c]
        if k == 4:
            return grad_low_ref, grad_low_ref, grads.at[1, c, own_rows]
        if k == 5:
            return turned_b, turned_b, lefts.at[2, c]
        return turned_a, turned_a, lefts.at[3, c]

    def op_own(k):
        source, _, target = operand(k)
        return pltpu.make_async_copy(source, target, op_local.at[k])

    def op_copy(k):
        _, source, target = operand(k)
        return remote(source, target, op_send.at[k], op_recv.at[k], sibling)

    def stage_copy():
        return remote(grads.at[1, c, own_rows], stage, op_send.at[7], op_recv.at[7], sibling)

    def op_wait(k):
        op_own(k).wait()
        op_copy(k).wait_recv()

    def lanes(xx):
        return span(xx, wide)

    def x_copy(i, part):
        if part == 0:
            src, dst = mine.at[i, pl.ds(half, half), 1 - y, :, lanes(1 - x)], from_x.at[i, pl.ds(lines, half)]
        else:
            src, dst = mine.at[i, :, y, :, lanes(1 - x)], from_x.at[i, pl.ds(0, lines)]
        return remote(src, dst, x_send.at[i, part], x_recv.at[i, part], along_x)

    def y_copy(i, part):
        if part == 0:
            src, dst = mine.at[i, pl.ds(0, half), 1 - y, :, lanes(1 - x)], from_y.at[i, pl.ds(lines, half)]
        else:
            src, dst = mine.at[i, :, 1 - y, :, lanes(x)], from_y.at[i, pl.ds(0, lines)]
        return remote(src, dst, y_send.at[i, part], y_recv.at[i, part], along_y)

    def z_copy(i, k):
        return remote(
            mine.at[i, lax.rem(z + k + 1, lines), y, :, lanes(x)],
            from_z.at[i, k],
            z_send.at[i, k],
            z_recv.at[i, k],
            line[k],
        )

    def e_copy(i):
        return remote(ends.at[1 - c, i], out_ref.at[i, c], e_send.at[i], e_recv.at[i], sibling)

    def e_own(i):
        return pltpu.make_async_copy(ends.at[c, i], out_ref.at[i, c], e_local.at[i])

    def offer(i):
        x_copy(i, 0).start()
        y_copy(i, 0).start()

    def relay(i):
        x_copy(i, 0).wait_recv()
        y_copy(i, 0).wait_recv()
        for j in range(half):
            a = mine[i, j, y, :, lanes(1 - x)].astype(F32)
            mine[i, j, y, :, lanes(1 - x)] = (a + from_y[i, lines + j].astype(F32)).astype(BF16)
            b = mine[i, half + j, 1 - y, :, lanes(x)].astype(F32)
            mine[i, half + j, 1 - y, :, lanes(x)] = (b + from_x[i, lines + j].astype(F32)).astype(BF16)
        x_copy(i, 1).start()
        y_copy(i, 1).start()

    def collect(i):
        x_copy(i, 1).wait_recv()
        y_copy(i, 1).wait_recv()

        def add(j):
            value = mine[i, j, y, :, lanes(x)].astype(F32)
            value += from_x[i, j].astype(F32) + from_y[i, j].astype(F32)
            mine[i, j, y, :, lanes(x)] = value.astype(BF16)

        each(lines, add)
        for k in range(lines - 1):
            z_copy(i, k).start()

    def last(i):
        value = mine[i, z, y, :, lanes(x)].astype(F32)
        for k in range(lines - 1):
            z_copy(i, k).wait_recv()
            value += from_z[i, k].astype(F32)
        for cc in range(2):
            ends[cc, i] = value[:, cc * cols : (cc + 1) * cols]
        e_copy(i).start()
        e_own(i).start()

    def put(i, n, value):
        mine[i, :, :, :, chunk(n)] = value.astype(BF16).reshape(mine.shape[1:4] + (WIDTH,))

    def plain_unit(i, left, right):
        for n in range(CHUNKS):
            value = dot(lefts[left, 0], rights[right, 0, :, chunk(n)])
            value += dot(lefts[left, 1], rights[right, 1, :, chunk(n)])
            put(i, n, value)

    def conv_product(left, tap, n):
        where, side = lines_from(2 - tap // 3), 2 - tap % 3
        value = dot(lefts[left, 0], grads[side, 0, where, chunk(n)])
        return value + dot(lefts[left, 1], grads[side, 1, where, chunk(n)])

    def conv_unit(i, left, k):
        for n in range(CHUNKS):
            put(i, n, conv_product(left, 2 * k + c, n))

    def extra_b():
        for n in range(CHUNKS):
            put(4, n, conv_product(2, 8, n))

    def extra_a():
        for n in range(CHUNKS):
            old = mine[4, :, :, :, chunk(n)].astype(F32).reshape(C, WIDTH)
            put(4, n, jnp.where(c == 0, conv_product(3, 8, n), old))

    def spread_sides(core):
        def by_line(yy):
            value = grads[1, core, pl.ds(pl.multiple_of((yy + 1) * LINE, LINE), LINE)].astype(F32)
            left, right = shifted(value)
            spot_rows = pl.ds(pl.multiple_of((yy + 1) * LINE, LINE), LINE)
            grads[0, core, spot_rows] = left.astype(BF16)
            grads[2, core, spot_rows] = right.astype(BF16)

        each(RES, by_line)

    def load(tap, base):
        unit = base + tap - 9 * (tap // 8) * (base // 10)
        return pltpu.make_async_copy(
            whole_ref.at[unit // 2, unit % 2], weights.at[tap % 2], load_sem.at[tap % 2]
        )

    def conv_back(tap, base):
        load(tap, base).wait()

        @pl.when(tap < 8)
        def _():
            load(tap + 1, base).start()

        part = grads[2 - tap % 3, c, lines_from(2 - tap // 3)]
        for n in range(CHUNKS):
            value = dot_nt(part, weight_rows(weights.at[tap % 2], n))
            total[:, :, :, chunk(n)] += value.reshape(RES, SLOTS, RES, WIDTH)

    def conv_back_range(first, stop, base):
        def body(tap, carry):
            conv_back(tap, base)
            return carry

        lax.fori_loop(first, stop, body, 0)

    def slope(values):
        sigma = jax.nn.sigmoid(values)
        return sigma * (1.0 + values * (1.0 - sigma))

    greet(column + heads)
    for k in range(7):
        op_own(k).start()
        op_copy(k).start()
    load(0, 10).start()
    vs_mine[...] = jnp.zeros_like(vs_mine)
    edge = jnp.zeros((LINE, C), BF16)
    for j in range(3):
        for core in range(2):
            grads[j, core, 0:LINE] = edge
            grads[j, core, ALL + LINE : ALL + 2 * LINE] = edge
    total[...] = jnp.zeros_like(total)
    sums_ref[...] = sums_in[...]

    op_wait(0)
    op_wait(1)
    plain_unit(10, 1, 0)
    offer(10)
    op_wait(2)
    op_wait(3)
    plain_unit(9, 0, 1)
    offer(9)
    op_wait(4)
    op_wait(5)
    spread_sides(0)
    spread_sides(1)

    def units_b(k, carry):
        conv_unit(5 + k, 2, k)
        offer(5 + k)
        return carry

    lax.fori_loop(0, 4, units_b, 0)
    extra_b()
    relay(10)
    conv_back_range(0, 3, 10)
    relay(9)
    conv_back_range(3, 6, 10)
    relay(5)
    conv_back_range(6, 9, 10)
    relay(6)
    load(0, 0).start()

    def norm_b_value(n):
        value = (conv_ref[:, n].reshape(PIX, C) - stats_ref[2, row(n)]) * stats_ref[3, row(n)]
        return value

    def back_b(n):
        normed = norm_b_value(n)
        out = normed * vecs_ref[3:4] + vecs_ref[4:5]
        scale = mod_ref[row(n)] + 1.0
        grad = total[:, n].reshape(PIX, C) * slope(mod_ref[row(SLOTS + n)] + out * scale)
        pair_ref[row(n)] = sum_rows(grad * out)
        pair_ref[row(SLOTS + n)] = sum_rows(grad)
        grad = grad * scale
        sums_ref[3:4] += sum_rows(grad * normed)
        sums_ref[4:5] += sum_rows(grad)
        total[:, n] = (grad * vecs_ref[3:4]).reshape(RES, RES, C)

    each(SLOTS, back_b)
    gm_mine[...] = pair_ref[...].astype(BF16)
    gm_all[d] = gm_mine[...]

    def gm_copy(k):
        return remote(gm_mine, gm_all.at[d], gm_send.at[k], gm_recv.at[k], column[k])

    for k in range(n_dp - 1):
        gm_copy(k).start()

    def group_pairs(get):
        def gather(n):
            head = total[:, n].reshape(PIX, C)
            pair_ref[row(n)] = sum_rows(head)
            pair_ref[row(SLOTS + n)] = sum_rows(head * get(n))

        each(SLOTS, gather)
        pair_ref[...] = group_mean(pair_ref[...])

    group_pairs(norm_b_value)

    def back_b_second(n):
        head = total[:, n].reshape(PIX, C)
        value = head - pair_ref[row(n)] - norm_b_value(n) * pair_ref[row(SLOTS + n)]
        value = (stats_ref[3, row(n)] * value).astype(BF16).astype(F32)
        sums_ref[2:3] += sum_rows(value)
        total[:, n] = value.reshape(RES, RES, C)

    each(SLOTS, back_b_second)

    def lower(yy):
        spot_rows = pl.ds(pl.multiple_of((yy + 1) * LINE, LINE), LINE)
        grads[1, c, spot_rows] = total[yy].reshape(LINE, C).astype(BF16)

    op_copy(4).wait_send()
    each(RES, lower)
    stage_copy().start()
    spread_sides(c)
    total[...] = jnp.zeros_like(total)
    relay(7)
    relay(8)
    collect(10)
    conv_back_range(0, 3, 0)
    stage_copy().wait_recv()

    def take(yy):
        spot_rows = pl.ds(pl.multiple_of((yy + 1) * LINE, LINE), LINE)
        grads[1, 1 - c, spot_rows] = stage[span(yy, LINE)]

    each(RES, take)
    spread_sides(1 - c)
    op_wait(6)
    extra_a()
    offer(4)

    def units_a(k, carry):
        conv_unit(k, 3, k)
        offer(k)
        return carry

    lax.fori_loop(0, 4, units_a, 0)
    collect(9)
    conv_back_range(3, 6, 0)
    collect(5)
    last(10)

    for k in range(n_dp - 1):
        gm_copy(k).wait()
    parts = gm_all[...].astype(F32)
    count = n_dp * SLOTS
    gm_scale = parts[:, :SLOTS].reshape(count, C)
    gm_offset = parts[:, SLOTS:].reshape(count, C)
    pre = pre_ref[...]
    emb = silu(pre).astype(BF16)
    part_rows = rows // n_head
    for k, value in ((0, gm_scale), (1, gm_offset)):
        low_value = value.astype(BF16)
        grad_w = dot_tn(emb, low_value)
        place_lanes = slice(k * C, (k + 1) * C)
        for hh in range(n_head):
            mw_mine[hh, 0:part_rows, place_lanes] = grad_w[hh * part_rows : (hh + 1) * part_rows]
            mw_mine[hh, part_rows : part_rows + 8, place_lanes] = jnp.broadcast_to(sum_rows(value), (8, C))
    grad_e = dot_nt(gm_scale.astype(BF16), modw_ref[:, :C]) + dot_nt(gm_offset.astype(BF16), modw_ref[:, C:])
    grad_e = grad_e * slope(pre)
    label = ids_ref[...].reshape(count, 128)[:, 0:1].astype(F32)
    lane = lax.broadcasted_iota(jnp.int32, grad_e.shape, 1)
    ge_all[h] = jnp.where(lane < rows, grad_e, label)

    def mw_copy(k):
        return remote(
            mw_mine.at[lax.rem(h + k + 1, n_head)], mw_got.at[k], mw_send.at[k], mw_recv.at[k], heads[k]
        )

    def ge_copy(k):
        return remote(ge_all.at[h], ge_all.at[h], ge_send.at[k], ge_recv.at[k], heads[k])

    for k in range(n_head - 1):
        mw_copy(k).start()
        ge_copy(k).start()

    conv_back_range(6, 9, 0)

    def norm_a_value(n):
        return (images_ref[span(n, PIX)].astype(F32) - stats_ref[0, row(n)]) * stats_ref[1, row(n)]

    def back_a(n):
        normed = norm_a_value(n)
        grad = total[:, n].reshape(PIX, C) * slope(normed * vecs_ref[0:1] + vecs_ref[1:2])
        sums_ref[0:1] += sum_rows(grad * normed)
        sums_ref[1:2] += sum_rows(grad)
        total[:, n] = (grad * vecs_ref[0:1]).reshape(RES, RES, C)

    each(SLOTS, back_a)

    for hh in range(n_head):
        vs_mine[hh] = sums_ref[:, hh * cols : (hh + 1) * cols]

    def vs_copy(k):
        return remote(
            vs_mine.at[lax.rem(h + k + 1, n_head)], vs_got.at[k], vs_send.at[k], vs_recv.at[k], heads[k]
        )

    def vt_copy(k):
        return remote(vt_mine, vt_all.at[d], vt_send.at[k], vt_recv.at[k], column[k])

    for k in range(n_head - 1):
        vs_copy(k).start()
    relay(4)
    collect(6)
    last(9)
    group_pairs(norm_a_value)

    def back_a_second(n):
        head = total[:, n].reshape(PIX, C)
        value = head - pair_ref[row(n)] - norm_a_value(n) * pair_ref[row(SLOTS + n)]
        image_ref[span(n, PIX)] = stats_ref[1, row(n)] * value + grad_resid_ref[:, n].reshape(PIX, C)

    each(SLOTS, back_a_second)
    relay(0)
    collect(7)
    last(5)
    value = vs_mine[h]
    for k in range(n_head - 1):
        vs_copy(k).wait()
        value += vs_got[k]
    vt_mine[...] = value
    vt_all[d] = value
    for k in range(n_dp - 1):
        vt_copy(k).start()
    relay(1)
    collect(8)
    last(6)
    value = mw_mine[h]
    for k in range(n_head - 1):
        mw_copy(k).wait()
        value += mw_got[k]
    modw_out[...] = value
    relay(2)
    collect(4)
    last(7)
    table = class_ref.shape[0]
    classes = None
    for k in range(n_head - 1):
        ge_copy(k).wait()
    for k in range(n_head):
        value = ge_all[k]
        hot = lax.broadcasted_iota(jnp.int32, (count, table), 1) == value[:, rows : rows + 1].astype(jnp.int32)
        value = dot_tn(jnp.where(hot, 1.0, 0.0).astype(BF16), value.astype(BF16))
        classes = value if classes is None else classes + value
    class_ref[...] = classes
    relay(3)
    collect(0)
    last(8)
    for k in range(n_dp - 1):
        vt_copy(k).wait()
    value = vt_all[0]
    for k in range(1, n_dp):
        value += vt_all[k]
    vec_out[...] = value
    collect(1)
    last(4)
    collect(2)
    last(0)
    collect(3)
    last(1)
    last(2)
    last(3)

    for k in range(7):
        if k != 4:
            op_copy(k).wait_send()
    stage_copy().wait_send()

    def drain(i):
        for part in range(2):
            x_copy(i, part).wait_send()
            y_copy(i, part).wait_send()
        for k in range(lines - 1):
            z_copy(i, k).wait_send()
        e_own(i).wait()
        e_copy(i).wait()

    each(PAIRS, drain)


def run_backward(whole, turned_a, turned_b, turned, right, grad_low, grad_resid, conv_out, images, stats, vecs, mod, sums, pre, ids, modw):
    n_dp, n_head = lax.axis_size("dp"), lax.axis_size("head")
    _, _, lines, _, rows, depth = whole.shape
    cols = depth // n_head
    wide = 2 * cols
    board = (RES, SLOTS, RES, C)
    shape = jax.ShapeDtypeStruct
    return pl.pallas_call(
        functools.partial(backward_kernel, lines),
        out_shape=(
            shape((PAIRS, 2, rows, cols), F32),
            shape((ALL, C), F32),
            shape((1024, 128), F32),
            shape((rows // n_head + 8, 2 * C), F32),
            shape((16, cols), F32),
        ),
        in_specs=[ANY] * 6 + [VMEM] * 10,
        out_specs=(ANY,) + (VMEM,) * 4,
        scratch_shapes=[
            pltpu.VMEM((PAIRS, lines, 2, rows, depth), BF16),
            pltpu.VMEM((PAIRS, lines + lines // 2, rows, wide), BF16),
            pltpu.VMEM((PAIRS, lines + lines // 2, rows, wide), BF16),
            pltpu.VMEM((PAIRS, lines - 1, rows, wide), BF16),
            pltpu.VMEM((2, PAIRS, rows, cols), F32),
            pltpu.VMEM((4, 2, C, ALL), BF16),
            pltpu.VMEM((2, 2, ALL, C), BF16),
            pltpu.VMEM((3, 2, ALL + 2 * LINE, C), BF16),
            pltpu.VMEM((ALL, C), BF16),
            pltpu.VMEM((2, lines, 2, rows, depth), BF16),
            pltpu.VMEM(board, F32),
            pltpu.VMEM((16, C), F32),
            pltpu.VMEM((2 * SLOTS, C), F32),
            pltpu.VMEM((2 * SLOTS, C), BF16),
            pltpu.VMEM((n_dp, 2 * SLOTS, C), BF16),
            pltpu.VMEM((n_head, rows // n_head + 8, 2 * C), F32),
            pltpu.VMEM((n_head - 1, rows // n_head + 8, 2 * C), F32),
            pltpu.VMEM((n_head, n_dp * SLOTS, 128), F32),
            pltpu.VMEM((n_head, 16, cols), F32),
            pltpu.VMEM((n_head - 1, 16, cols), F32),
            pltpu.VMEM((16, cols), F32),
            pltpu.VMEM((n_dp, 16, cols), F32),
            DMA((PAIRS, 2)),
            DMA((PAIRS, 2)),
            DMA((PAIRS, 2)),
            DMA((PAIRS, 2)),
            DMA((PAIRS, lines - 1)),
            DMA((PAIRS, lines - 1)),
            DMA((PAIRS,)),
            DMA((PAIRS,)),
            DMA((PAIRS,)),
            DMA((8,)),
            DMA((8,)),
            DMA((7,)),
            DMA((2,)),
            DMA((n_dp - 1,)),
            DMA((n_dp - 1,)),
            DMA((n_head - 1,)),
            DMA((n_head - 1,)),
            DMA((n_head - 1,)),
            DMA((n_head - 1,)),
            DMA((n_head - 1,)),
            DMA((n_head - 1,)),
            DMA((n_dp - 1,)),
            DMA((n_dp - 1,)),
        ],
        compiler_params=pltpu.CompilerParams(
            collective_id=1, has_side_effects=True, vmem_limit_bytes=64 * 2**20 - 2**18
        ),
        name="backward_scatter",
    )(whole, turned_a, turned_b, turned, right, grad_low, grad_resid, conv_out, images, stats, vecs, mod, sums, pre, ids, modw)


def direct(rows, cols):
    n_dp, n_head = lax.axis_size("dp"), lax.axis_size("head")
    return n_head == 4 and n_dp % 4 == 0 and n_dp <= 8 and rows % 32 == 0 and cols % 64 == 0


def fast_shards(
    images,
    cotangent,
    counts,
    labels,
    levels,
    noise_table,
    class_table,
    gain_a,
    shift_a,
    conv_a,
    bias_a,
    mod_weight,
    mod_bias,
    gain_b,
    shift_b,
    conv_b,
    bias_b,
    gain_c,
    shift_c,
    qkv_weight,
    proj_weight,
    proj_bias,
):
    n_head = lax.axis_size("head")
    d, h = lax.axis_index("dp"), lax.axis_index("head")
    rows = class_table.shape[1]
    taps = jnp.concatenate(
        [
            jnp.swapaxes(conv_a, 0, 1),
            jnp.swapaxes(conv_b[:, 8:9], 0, 1),
            jnp.swapaxes(conv_b[:, 0:8], 0, 1),
            jnp.swapaxes(qkv_weight, 0, 1),
            proj_weight[None],
        ],
        axis=0,
    )
    vec = jnp.stack([gain_a, shift_a, bias_a, gain_b, shift_b, bias_b, gain_c, shift_c, proj_bias])
    vec = jnp.pad(vec, ((0, 7), (0, 0)))
    ids = jnp.pad(jnp.stack([labels, levels], axis=1), ((0, 0), (0, 126)))
    class_rows = jnp.pad(class_table, ((0, 1024 - class_table.shape[0]), (0, 128 - rows)))
    noise_rows = lax.dynamic_slice_in_dim(noise_table, d * rows, rows, axis=1)
    noise_rows = jnp.pad(noise_rows, ((0, 128 - noise_rows.shape[0]), (0, 128 - rows)))
    mod_rows = jnp.pad(mod_weight.reshape(rows, 2 * C), ((0, 128 - rows), (0, 0)))
    bias_rows = jnp.repeat(mod_bias.astype(F32), SLOTS, axis=0)
    live = live_rows(counts, d * n_head + h, 1, SLOTS)
    live = jnp.broadcast_to(live[:, None], (SLOTS, C))
    flat = images.reshape(ALL, C)
    whole, vecs, mod, conv_out, resid, turned_a, turned_b, stats, pre, all_ids = run_forward(
        taps, vec, flat, ids, class_rows, noise_rows, mod_rows, bias_rows
    )
    block_out, grad_resid, grad_low, turned, right, sums = run_attention(
        whole, resid, cotangent.reshape(ALL, C), live, vecs
    )
    out, image_grad, classes, modw, vectors = run_backward(
        whole,
        turned_a,
        turned_b,
        turned,
        right,
        grad_low,
        grad_resid,
        conv_out,
        flat,
        stats,
        vecs,
        mod,
        sums,
        pre,
        all_ids,
        mod_rows,
    )
    out = out.reshape((UNITS,) + out.shape[2:])
    part = rows // n_head
    class_grad = lax.dynamic_slice(classes, (0, h * part), (class_table.shape[0], part))
    modb = modw[part].reshape(2, C)
    modb_grad = lax.dynamic_slice_in_dim(modb, (d * n_head + h) * part, part, axis=1)
    return (
        block_out.reshape(images.shape),
        image_grad.reshape(images.shape),
        class_grad,
        vectors[0],
        vectors[1],
        jnp.swapaxes(out[0:9], 0, 1),
        vectors[2],
        modw[:part].reshape(part, 2, C),
        modb_grad,
        vectors[3],
        vectors[4],
        jnp.swapaxes(jnp.concatenate([out[10:18], out[9:10]], axis=0), 0, 1),
        vectors[5],
        vectors[6],
        vectors[7],
        jnp.swapaxes(out[18:21], 0, 1),
        out[21],
        vectors[8],
    )


def shards(*args):
    rows, _, cols = args[9].shape
    if direct(rows, cols):
        return fast_shards(*args)
    return plain_shards(*args)


def solution(mesh):
    placed = (
        P(("dp", "head"), None, None, None),
        P(("dp", "head"), None, None, None),
        P(),
        P(("dp", "head")),
        P(("dp", "head")),
        P(),
        P(None, "dp"),
        P("head"),
        P("head"),
        P("dp", None, "head"),
        P("head"),
        P("dp", None, None),
        P(),
        P("head"),
        P("head"),
        P("dp", None, "head"),
        P("head"),
        P("head"),
        P("head"),
        P("dp", None, "head"),
        P("dp", "head"),
        P("head"),
    )
    return jax.shard_map(
        shards,
        mesh=mesh,
        in_specs=placed,
        out_specs=(
            P(("dp", "head"), None, None, None),
            P(("dp", "head"), None, None, None),
            P(None, ("dp", "head")),
            P("head"),
            P("head"),
            P("dp", None, "head"),
            P("head"),
            P(("dp", "head"), None, None),
            P(None, ("dp", "head")),
            P("head"),
            P("head"),
            P("dp", None, "head"),
            P("head"),
            P("head"),
            P("head"),
            P("dp", None, "head"),
            P("dp", "head"),
            P("head"),
        ),
        check_vma=False,
    )
```

```python
import functools

import jax
import jax.numpy as jnp
from jax import lax
from jax.experimental import pallas as pl
from jax.experimental.pallas import tpu as pltpu
from jax.sharding import PartitionSpec as P

C = 768
DH = 64
GROUPS = 32


EPSILON = 1e-05
HIGHEST = lax.Precision.HIGHEST


def norm_forward(values, gain, shift):
    count, chans = (values.shape[0], values.shape[-1])
    span = C // GROUPS
    grouped = values.reshape(count, -1, chans // span, span)
    mean = jnp.mean(grouped, axis=(1, 3), keepdims=True)
    centred = grouped - mean
    inverse = lax.rsqrt(jnp.mean(centred * centred, axis=(1, 3), keepdims=True) + EPSILON)
    normed = (centred * inverse).reshape(values.shape)
    return (normed * gain + shift, normed, inverse)


def norm_backward(grad_out, normed, inverse, gain):
    grad_gain = jnp.sum(grad_out * normed, axis=(0, 1, 2))
    grad_shift = jnp.sum(grad_out, axis=(0, 1, 2))
    count, chans = (grad_out.shape[0], grad_out.shape[-1])
    span = C // GROUPS
    layout = (count, -1, chans // span, span)
    grad_normed = (grad_out * gain).reshape(layout)
    normed_groups = normed.reshape(layout)
    mean_one = jnp.mean(grad_normed, axis=(1, 3), keepdims=True)
    mean_two = jnp.mean(grad_normed * normed_groups, axis=(1, 3), keepdims=True)
    grad_in = inverse * (grad_normed - mean_one - normed_groups * mean_two)
    return (grad_in.reshape(grad_out.shape), grad_gain, grad_shift)


def silu_slope(values):
    sigma = jax.nn.sigmoid(values)
    return sigma * (1.0 + values * (1.0 - sigma))


def patches_of(act):
    count, rows, cols, chans = act.shape
    padded = jnp.pad(act, ((0, 0), (1, 1), (1, 1), (0, 0)))
    taps = [padded[:, i : i + rows, j : j + cols, :] for i in range(3) for j in range(3)]
    return jnp.stack(taps, axis=3).reshape(count * rows * cols, 9, chans)


def contract_rows(left, right):
    return lax.dot_general(
        left, right, (((0,), (0,)), ((), ())), preferred_element_type=jnp.float32
    )


def contract_cols(left, right):
    return lax.dot_general(
        left, right, (((1,), (1,)), ((), ())), preferred_element_type=jnp.float32
    )


def conv_back(grad_low, weight, count, rows, cols):
    chans = weight.shape[0]
    padded = jnp.zeros((count, rows + 2, cols + 2, chans), jnp.float32)
    for tap in range(9):
        i, j = divmod(tap, 3)
        part = contract_cols(grad_low, weight[:, tap, :]).reshape(count, rows, cols, chans)
        padded = padded.at[:, i : i + rows, j : j + cols, :].add(part)
    return padded[:, 1 : rows + 1, 1 : cols + 1, :]


def keep_same(values):
    return values


def live_rows(counts, first, number, count):
    sums = jnp.sum(counts, axis=1)
    chosen = lax.dynamic_slice_in_dim(sums, first, number)
    slots = lax.iota(jnp.int32, count)
    return (slots[None, :] < chosen[:, None]).astype(jnp.float32).reshape(number * count)


def residual_forward(source, mod_pair, weights, spread):
    (
        conv_one,
        conv_two,
        gain_one,
        shift_one,
        bias_one,
        gain_two,
        shift_two,
        bias_two,
        gain_three,
        shift_three,
    ) = weights
    out_a, normed_a, inverse_a = norm_forward(source, gain_one, shift_one)
    wide_a = spread(jax.nn.silu(out_a).astype(jnp.bfloat16))
    conv_out_a = (
        jnp.einsum("ptc,cto->po", patches_of(wide_a), conv_one, preferred_element_type=jnp.float32)
        + bias_one
    ).reshape(source.shape)
    scale = mod_pair[:, :, 0:1, :]
    offset = mod_pair[:, :, 1:2, :]
    out_b, normed_b, inverse_b = norm_forward(conv_out_a, gain_two, shift_two)
    inner_b = offset + out_b * (scale + 1.0)
    wide_b = spread(jax.nn.silu(inner_b).astype(jnp.bfloat16))
    conv_out_b = (
        jnp.einsum("ptc,cto->po", patches_of(wide_b), conv_two, preferred_element_type=jnp.float32)
        + bias_two
    ).reshape(source.shape)
    resid = source + conv_out_b
    out_c, normed_c, inverse_c = norm_forward(resid, gain_three, shift_three)
    attn_in = out_c.astype(jnp.bfloat16)
    saved = (
        out_a,
        normed_a,
        inverse_a,
        wide_a,
        out_b,
        normed_b,
        inverse_b,
        inner_b,
        wide_b,
        normed_c,
        inverse_c,
        scale,
    )
    return (resid, attn_in, saved)


def residual_backward(grad_attn, grad_out, saved, weights, reduce_value):
    conv_one, conv_two, gain_one, gain_two, gain_three = (
        weights[0],
        weights[1],
        weights[2],
        weights[5],
        weights[8],
    )
    (
        out_a,
        normed_a,
        inverse_a,
        wide_a,
        out_b,
        normed_b,
        inverse_b,
        inner_b,
        wide_b,
        normed_c,
        inverse_c,
        scale,
    ) = saved
    count, rows, cols, local = grad_out.shape
    grad_resid_c, gainc_term, shiftc_term = norm_backward(
        grad_attn, normed_c, inverse_c, gain_three
    )
    grad_resid = grad_out + grad_resid_c
    grad_conv_b = grad_resid.reshape(-1, local).astype(jnp.bfloat16)
    biasb_term = jnp.sum(grad_conv_b.astype(jnp.float32), axis=0)
    convb_term = jnp.einsum(
        "ptc,po->cto", patches_of(wide_b), grad_conv_b, preferred_element_type=jnp.float32
    )
    grad_act_b = reduce_value(conv_back(grad_conv_b, conv_two, count, rows, cols))
    grad_inner = grad_act_b * silu_slope(inner_b)
    grad_offset = jnp.sum(grad_inner, axis=(1, 2))
    grad_scale = jnp.sum(grad_inner * out_b, axis=(1, 2))
    grad_mod = jnp.stack([grad_scale, grad_offset], axis=1)[:, None]
    grad_conv_full, gainb_term, shiftb_term = norm_backward(
        grad_inner * (scale + 1.0), normed_b, inverse_b, gain_two
    )
    grad_conv_a = grad_conv_full.reshape(-1, local).astype(jnp.bfloat16)
    biasa_term = jnp.sum(grad_conv_a.astype(jnp.float32), axis=0)
    conva_term = jnp.einsum(
        "ptc,po->cto", patches_of(wide_a), grad_conv_a, preferred_element_type=jnp.float32
    )
    grad_act_a = reduce_value(conv_back(grad_conv_a, conv_one, count, rows, cols))
    grad_source, gaina_term, shifta_term = norm_backward(
        grad_act_a * silu_slope(out_a), normed_a, inverse_a, gain_one
    )
    image_grad = grad_resid + grad_source
    vectors = (
        gaina_term,
        shifta_term,
        biasa_term,
        gainb_term,
        shiftb_term,
        biasb_term,
        gainc_term,
        shiftc_term,
    )
    return (image_grad, grad_mod, (conva_term, convb_term), vectors)


def attend_forward(block):
    query, key, value = (block[:, :, 0], block[:, :, 1], block[:, :, 2])
    batch, pixels, heads_here, depth = query.shape
    scores = jnp.einsum("bqhd,bkhd->bhqk", query, key, preferred_element_type=jnp.float32) * DH ** (
        -0.5
    )
    top = jnp.max(scores, axis=-1, keepdims=True)
    weights = jnp.exp(scores - top)
    sums = jnp.sum(weights, axis=-1, keepdims=True)
    probs = (weights / sums).astype(jnp.bfloat16)
    logsum = (top + jnp.log(sums))[..., 0]
    mixed = jnp.einsum("bhqk,bkhd->bqhd", probs, value, preferred_element_type=jnp.float32).astype(
        jnp.bfloat16
    )
    return (mixed.reshape(batch, pixels, heads_here * depth), logsum)


def attend_backward(block, logsum, grad_head):
    query, key, value = (block[:, :, 0], block[:, :, 1], block[:, :, 2])
    batch, pixels, heads_here, depth = query.shape
    factor = DH ** (-0.5)
    scores = jnp.einsum("bqhd,bkhd->bhqk", query, key, preferred_element_type=jnp.float32) * factor
    probs = jnp.exp(scores - logsum[..., None])
    grad_value = jnp.einsum(
        "bhqk,bqhd->bkhd", probs.astype(jnp.bfloat16), grad_head, preferred_element_type=jnp.float32
    )
    grad_probs = jnp.einsum("bqhd,bkhd->bhqk", grad_head, value, preferred_element_type=jnp.float32)
    inner = jnp.sum(grad_probs * probs, axis=-1, keepdims=True)
    grad_scores = (probs * (grad_probs - inner)).astype(jnp.bfloat16)
    grad_query = (
        jnp.einsum("bhqk,bkhd->bqhd", grad_scores, key, preferred_element_type=jnp.float32) * factor
    )
    grad_key = (
        jnp.einsum("bhqk,bqhd->bkhd", grad_scores, query, preferred_element_type=jnp.float32)
        * factor
    )
    stacked = jnp.stack([grad_query, grad_key, grad_value], axis=2).astype(jnp.bfloat16)
    return stacked.reshape(batch, pixels, 3, heads_here * depth)


def plain_shards(
    images,
    cotangent,
    counts,
    labels,
    levels,
    noise_table,
    class_table,
    gain_a,
    shift_a,
    conv_a,
    bias_a,
    mod_weight,
    mod_bias,
    gain_b,
    shift_b,
    conv_b,
    bias_b,
    gain_c,
    shift_c,
    qkv_weight,
    proj_weight,
    proj_bias,
):
    rows_a, rows_b, rows_qkv, rows_proj, mod_full, class_full = (
        lax.all_gather(conv_a, "dp", axis=0, tiled=True),
        lax.all_gather(conv_b, "dp", axis=0, tiled=True),
        lax.all_gather(qkv_weight, "dp", axis=0, tiled=True),
        lax.all_gather(proj_weight, "dp", axis=0, tiled=True),
        lax.all_gather(mod_weight, "dp", axis=0, tiled=True),
        lax.all_gather(class_table, "dp", axis=1, tiled=True),
    )
    count, rows, cols, channels = images.shape
    pixels = rows * cols
    groups_n = lax.axis_size("head")
    quarter = channels // groups_n
    heads_local = quarter // DH
    first_dp = lax.axis_index("dp") * groups_n
    class_hot = (labels[:, None] == lax.iota(jnp.int32, class_full.shape[0])[None, :]).astype(
        jnp.bfloat16
    )
    level_hot = (levels[:, None] == lax.iota(jnp.int32, noise_table.shape[0])[None, :]).astype(
        jnp.bfloat16
    )
    embed_pre = jnp.dot(class_hot, class_full, preferred_element_type=jnp.float32) + jnp.dot(
        level_hot, noise_table, preferred_element_type=jnp.float32
    )
    embed = jax.nn.silu(embed_pre).astype(jnp.bfloat16)
    modulation = (
        jnp.einsum("ne,etc->ntc", embed, mod_full, preferred_element_type=jnp.float32)
        + mod_bias.astype(jnp.float32)
    ).astype(jnp.bfloat16)
    mod_pair = modulation.reshape(count, 1, 2, channels)
    (
        conv_one,
        conv_two,
        qkv_full,
        proj_full,
        gain_one,
        shift_one,
        bias_one,
        gain_two,
        shift_two,
        bias_two,
        gain_three,
        shift_three,
        bias_three,
    ) = (
        lax.all_gather(rows_a, "head", axis=2, tiled=True),
        lax.all_gather(rows_b, "head", axis=2, tiled=True),
        lax.all_gather(rows_qkv, "head", axis=2, tiled=True),
        lax.all_gather(rows_proj, "head", axis=1, tiled=True),
        lax.all_gather(gain_a, "head", axis=0, tiled=True),
        lax.all_gather(shift_a, "head", axis=0, tiled=True),
        lax.all_gather(bias_a, "head", axis=0, tiled=True),
        lax.all_gather(gain_b, "head", axis=0, tiled=True),
        lax.all_gather(shift_b, "head", axis=0, tiled=True),
        lax.all_gather(bias_b, "head", axis=0, tiled=True),
        lax.all_gather(gain_c, "head", axis=0, tiled=True),
        lax.all_gather(shift_c, "head", axis=0, tiled=True),
        lax.all_gather(proj_bias, "head", axis=0, tiled=True),
    )
    weights = (
        conv_one,
        conv_two,
        gain_one,
        shift_one,
        bias_one,
        gain_two,
        shift_two,
        bias_two,
        gain_three,
        shift_three,
    )
    live = live_rows(counts, first_dp + lax.axis_index("head"), 1, count)
    total = count * pixels
    width = channels // groups_n
    source = images.astype(jnp.float32)
    resid, attn_in, saved = residual_forward(
        source, mod_pair.astype(jnp.float32), weights, keep_same
    )
    attn_flat = attn_in.reshape(total, channels)
    qkv_flat = qkv_full.reshape(channels, 3 * channels)
    qkv = jnp.dot(attn_flat, qkv_flat, preferred_element_type=jnp.float32).astype(jnp.bfloat16)
    packed = qkv.reshape(1, count, pixels, 3, groups_n, width)
    block = lax.all_to_all(packed, "head", split_axis=4, concat_axis=0, tiled=True)
    groups = block.shape[0]
    items = block.shape[1]
    flat = block.reshape(groups * items, pixels, 3, heads_local, DH)
    mixed, logsum = attend_forward(flat)
    mixed = mixed.reshape(groups, items, pixels, 1, width)
    returned = lax.all_to_all(mixed, "head", split_axis=0, concat_axis=3, tiled=True)
    returned, logsum, kept = (returned, logsum.reshape(groups, items, heads_local, pixels), block)
    mixed_image = returned.reshape(total, channels)
    result = (
        resid.reshape(total, channels)
        + jnp.dot(mixed_image, proj_full, preferred_element_type=jnp.float32)
        + bias_three
    )
    block_out = (result.reshape(images.shape) * live[:, None, None, None]).astype(jnp.bfloat16)
    grad_out = cotangent.astype(jnp.float32) * live[:, None, None, None]
    grad_flat = grad_out.reshape(total, channels)
    grad_low = grad_flat.astype(jnp.bfloat16)
    projw_full = contract_rows(mixed_image, grad_low)
    projb_full = jnp.sum(grad_flat, axis=0)
    grad_mixed = contract_cols(grad_low, proj_full).astype(jnp.bfloat16)
    arrived = lax.all_to_all(
        grad_mixed.reshape(1, count, pixels, groups_n, width),
        "head",
        split_axis=3,
        concat_axis=0,
        tiled=True,
    )
    flat_block = kept.reshape(groups_n * count, pixels, 3, heads_local, DH)
    grad_head = arrived.reshape(groups_n * count, pixels, heads_local, DH)
    stacked = attend_backward(
        flat_block, logsum.reshape(groups_n * count, heads_local, pixels), grad_head
    )
    stacked = stacked.reshape(groups_n, count, pixels, 3, 1, width)
    grad_qkv = lax.all_to_all(stacked, "head", split_axis=0, concat_axis=4, tiled=True).reshape(
        total, 3 * channels
    )
    qkvw_full = contract_rows(attn_flat, grad_qkv).reshape(channels, 3, channels)
    grad_attn = contract_cols(grad_qkv, qkv_flat).reshape(images.shape)
    image_grad, grad_mod_part, conv_terms, vectors = residual_backward(
        grad_attn, grad_out, saved, weights, keep_same
    )
    (
        gaina_full,
        shifta_full,
        biasa_full,
        gainb_full,
        shiftb_full,
        biasb_full,
        gainc_full,
        shiftc_full,
    ) = vectors
    (
        conva_term,
        convb_term,
        qkvw_term,
        projw_term,
        gaina_term,
        shifta_term,
        biasa_term,
        gainb_term,
        shiftb_term,
        biasb_term,
        gainc_term,
        shiftc_term,
        projb_term,
    ) = (
        lax.psum_scatter(
            conv_terms[0].astype(jnp.bfloat16), "head", scatter_dimension=2, tiled=True
        ).astype(jnp.float32),
        lax.psum_scatter(
            conv_terms[1].astype(jnp.bfloat16), "head", scatter_dimension=2, tiled=True
        ).astype(jnp.float32),
        lax.psum_scatter(
            qkvw_full.astype(jnp.bfloat16), "head", scatter_dimension=2, tiled=True
        ).astype(jnp.float32),
        lax.psum_scatter(
            projw_full.astype(jnp.bfloat16), "head", scatter_dimension=1, tiled=True
        ).astype(jnp.float32),
        lax.psum_scatter(
            gaina_full.astype(jnp.bfloat16), "head", scatter_dimension=0, tiled=True
        ).astype(jnp.float32),
        lax.psum_scatter(
            shifta_full.astype(jnp.bfloat16), "head", scatter_dimension=0, tiled=True
        ).astype(jnp.float32),
        lax.psum_scatter(
            biasa_full.astype(jnp.bfloat16), "head", scatter_dimension=0, tiled=True
        ).astype(jnp.float32),
        lax.psum_scatter(
            gainb_full.astype(jnp.bfloat16), "head", scatter_dimension=0, tiled=True
        ).astype(jnp.float32),
        lax.psum_scatter(
            shiftb_full.astype(jnp.bfloat16), "head", scatter_dimension=0, tiled=True
        ).astype(jnp.float32),
        lax.psum_scatter(
            biasb_full.astype(jnp.bfloat16), "head", scatter_dimension=0, tiled=True
        ).astype(jnp.float32),
        lax.psum_scatter(
            gainc_full.astype(jnp.bfloat16), "head", scatter_dimension=0, tiled=True
        ).astype(jnp.float32),
        lax.psum_scatter(
            shiftc_full.astype(jnp.bfloat16), "head", scatter_dimension=0, tiled=True
        ).astype(jnp.float32),
        lax.psum_scatter(
            projb_full.astype(jnp.bfloat16), "head", scatter_dimension=0, tiled=True
        ).astype(jnp.float32),
    )
    grad_mod = grad_mod_part.reshape(count, 2, channels)
    modw_term = jnp.einsum("ne,ntc->etc", embed.astype(jnp.float32), grad_mod, precision=HIGHEST)
    modb_term = jnp.sum(grad_mod, axis=0)
    grad_embed = jnp.einsum(
        "ntc,etc->ne", grad_mod, mod_full.astype(jnp.float32), precision=HIGHEST
    ) * silu_slope(embed_pre)
    class_term = lax.dot_general(
        class_hot.astype(jnp.float32), grad_embed, (((0,), (0,)), ((), ())), precision=HIGHEST
    )
    modw_grad, class_grad, modb_grad = (
        lax.psum_scatter(modw_term, ("dp", "head"), scatter_dimension=0, tiled=True),
        lax.psum_scatter(class_term, ("dp", "head"), scatter_dimension=1, tiled=True),
        lax.psum_scatter(modb_term, ("dp", "head"), scatter_dimension=1, tiled=True),
    )
    conva_grad, convb_grad, qkvw_grad, projw_grad = (
        lax.psum_scatter(conva_term, "dp", scatter_dimension=0, tiled=True),
        lax.psum_scatter(convb_term, "dp", scatter_dimension=0, tiled=True),
        lax.psum_scatter(qkvw_term, "dp", scatter_dimension=0, tiled=True),
        lax.psum_scatter(projw_term, "dp", scatter_dimension=0, tiled=True),
    )
    (
        gaina_grad,
        shifta_grad,
        biasa_grad,
        gainb_grad,
        shiftb_grad,
        biasb_grad,
        gainc_grad,
        shiftc_grad,
        projb_grad,
    ) = lax.psum(
        (
            gaina_term,
            shifta_term,
            biasa_term,
            gainb_term,
            shiftb_term,
            biasb_term,
            gainc_term,
            shiftc_term,
            projb_term,
        ),
        "dp",
    )
    return (
        block_out,
        image_grad,
        class_grad,
        gaina_grad,
        shifta_grad,
        conva_grad,
        biasa_grad,
        modw_grad,
        modb_grad,
        gainb_grad,
        shiftb_grad,
        convb_grad,
        biasb_grad,
        gainc_grad,
        shiftc_grad,
        qkvw_grad,
        projw_grad,
        projb_grad,
    )


MESH = pl.DeviceIdType.MESH
UNITS = 22
PAIRS = UNITS // 2
FAR = 9
RES = 8
SLOTS = 8
PIX = RES * RES
LINE = SLOTS * RES
ALL = RES * LINE
WIDTH = 256
F32 = jnp.float32
BF16 = jnp.bfloat16
ANY = pl.BlockSpec(memory_space=pl.ANY)
VMEM = pl.BlockSpec(memory_space=pltpu.VMEM)
DMA = pltpu.SemaphoreType.DMA


def place():
    d, h = lax.axis_index("dp"), lax.axis_index("head")
    return d // 2, lax.rem(d, 2), h // 2, lax.rem(h, 2)


def at_chip(z, y, x, c):
    return (z * 2 + y, x * 2 + c)


def column_peers(n_dp):
    d, h = lax.axis_index("dp"), lax.axis_index("head")
    return [(lax.rem(d + k, n_dp), h) for k in range(1, n_dp)]


def head_peers(n_head):
    d, h = lax.axis_index("dp"), lax.axis_index("head")
    return [(d, lax.rem(h + k, n_head)) for k in range(1, n_head)]


def greet(devices):
    barrier = pltpu.get_barrier_semaphore()
    for device in devices:
        pl.semaphore_signal(barrier, inc=1, device_id=device, device_id_type=MESH)
    pl.semaphore_wait(barrier, len(devices))


def remote(src, dst, send, recv, device):
    return pltpu.make_async_remote_copy(
        src_ref=src, dst_ref=dst, send_sem=send, recv_sem=recv, device_id=device, device_id_type=MESH
    )


def each(count, body):
    def step(n, carry):
        body(n)
        return carry

    lax.fori_loop(0, count, step, 0)


def span(index, size):
    return pl.ds(pl.multiple_of(index * size, size), size)


def row(n):
    return pl.ds(n, 1)


def lines_from(i):
    return pl.ds(i * LINE if isinstance(i, int) else pl.multiple_of(i * LINE, LINE), ALL)


def dot(left, right):
    return jnp.dot(left, right, preferred_element_type=F32)


def dot_nt(left, right):
    return lax.dot_general(left, right, (((1,), (1,)), ((), ())), preferred_element_type=F32)


def dot_tn(left, right):
    return lax.dot_general(left, right, (((0,), (0,)), ((), ())), preferred_element_type=F32)


def in_group(first, second, axis):
    chan = lax.broadcasted_iota(jnp.int32, (first, second), axis)
    group = lax.broadcasted_iota(jnp.int32, (first, second), 1 - axis) * (C // GROUPS)
    inside = jnp.logical_and(chan >= group, chan < group + C // GROUPS)
    return jnp.where(inside, 1.0, 0.0).astype(BF16)


def pieces(values):
    high = values.astype(BF16).astype(F32)
    rest = values - high
    mid = rest.astype(BF16).astype(F32)
    return jnp.concatenate([high, mid, rest - mid], axis=0).astype(BF16)


def group_mean(sums):
    count = sums.shape[0]
    part = dot(pieces(sums), in_group(C, 128, 0))
    part = (part[:count] + part[count : 2 * count] + part[2 * count :]) * (1.0 / (PIX * (C // GROUPS)))
    back = dot(pieces(part), in_group(128, C, 1))
    return back[:count] + back[count : 2 * count] + back[2 * count :]


def sum_rows(values):
    return jnp.sum(values, axis=0, keepdims=True)


def norm_stats(get, mean_ref, inverse_ref, sums_ref):
    def first(n):
        sums_ref[row(n)] = sum_rows(get(n))

    each(SLOTS, first)
    mean_ref[...] = group_mean(sums_ref[...])

    def second(n):
        centred = get(n) - mean_ref[row(n)]
        sums_ref[row(n)] = sum_rows(centred * centred)

    each(SLOTS, second)
    inverse_ref[...] = lax.rsqrt(group_mean(sums_ref[...]) + EPSILON)


def silu(values):
    return values * jax.nn.sigmoid(values)


def shifted(values):
    spot = lax.rem(lax.broadcasted_iota(jnp.int32, values.shape, 0), RES)
    left = jnp.where(spot == 0, 0.0, pltpu.roll(values, 1, 0))
    right = jnp.where(spot == RES - 1, 0.0, pltpu.roll(values, values.shape[0] - 1, 0))
    return left, right


def chunk(n):
    return slice(n * WIDTH, (n + 1) * WIDTH)


CHUNKS = C // WIDTH


def weight_cols(ref, n):
    return ref[:, :, :, chunk(n)].reshape(C, WIDTH)


def weight_rows(ref, n):
    return ref[...].reshape(C, C)[chunk(n)]


def forward_kernel(
    lines,
    units_ref,
    vec_ref,
    images_ref,
    ids_ref,
    class_ref,
    noise_ref,
    modw_ref,
    modb_ref,
    whole_ref,
    vecs_ref,
    mod_ref,
    conv_ref,
    resid_ref,
    turned_a,
    turned_b,
    stats_ref,
    pre_ref,
    all_ids,
    halves,
    block,
    vec_all,
    mod_part,
    mod_got,
    act,
    act_f32,
    weights,
    sums_ref,
    pair_send,
    pair_recv,
    pair_local,
    own_sem,
    z_send,
    z_recv,
    p_send,
    x_send,
    x_recv,
    y_send,
    y_recv,
    s_send,
    s_recv,
    vec_send,
    vec_recv,
    ids_send,
    ids_recv,
    mod_send,
    mod_recv,
    load_sem,
):
    z, y, x, c = place()
    d, h = lax.axis_index("dp"), lax.axis_index("head")
    n_dp, n_head = lines * 2, 4
    half = lines // 2
    inner = jnp.logical_and(z > 0, z < lines - 1)
    far = at_chip(lax.rem(3 * z + 1, lines), y, x, c)
    rows = block.shape[1]
    wide = block.shape[2]
    sibling = at_chip(z, y, x, 1 - c)
    along_x = at_chip(z, y, 1 - x, c)
    along_y = at_chip(z, 1 - y, x, c)
    line = [at_chip(lax.rem(z + k, lines), y, x, c) for k in range(1, lines)]
    column, heads = column_peers(n_dp), head_peers(n_head)
    greet(column + heads)

    def spot(i, cc, zz, yy, xx):
        return whole_ref.at[i, cc, zz, yy, :, span(xx, wide)]

    swap = remote(units_ref.at[:, 1 - c], halves.at[c], pair_send, pair_recv, sibling)
    keep = pltpu.make_async_copy(units_ref.at[:, c], halves.at[c], pair_local)

    def vec_copy(k):
        return remote(vec_ref, vec_all.at[h], vec_send.at[k], vec_recv.at[k], heads[k])

    def ids_copy(k):
        return remote(ids_ref, all_ids.at[d], ids_send.at[k], ids_recv.at[k], column[k])

    def mod_copy(k):
        return remote(
            mod_part.at[lax.rem(d + k + 1, n_dp)], mod_got.at[d], mod_send.at[k], mod_recv.at[k], column[k]
        )

    def own_copy(i):
        return pltpu.make_async_copy(block.at[i], spot(i, c, z, y, x), own_sem.at[i])

    def z_part(i, zz):
        if isinstance(i, int) and i >= FAR:
            return whole_ref.at[i, c, zz]
        return spot(i, c, zz, y, x)

    def z_copy(i, k):
        ref = z_part(i, z)
        source = ref if isinstance(i, int) and i >= FAR else block.at[i]
        return remote(source, ref, z_send.at[i, k], z_recv.at[i, k], line[k])

    def z_pass(i):
        ref = z_part(i, lax.rem(z + 2, lines))
        return remote(ref, ref, p_send.at[i], z_recv.at[i, lax.rem(2 * z + 2, lines)], far)

    def z_start(i):
        z_copy(i, 1).start()

        @pl.when(z != lines - 1)
        def _():
            z_copy(i, 0).start()

        @pl.when(z != 0)
        def _():
            z_copy(i, 2).start()

    def z_relay(i):
        z_copy(i, 1).wait_recv()

        @pl.when(inner)
        def _():
            z_pass(i).start()

    def z_finish(i):
        z_copy(i, 0).wait_recv()
        z_copy(i, 2).wait_recv()

    def z_drain(i):
        z_copy(i, 1).wait_send()

        @pl.when(z != lines - 1)
        def _():
            z_copy(i, 0).wait_send()

        @pl.when(z != 0)
        def _():
            z_copy(i, 2).wait_send()

        @pl.when(inner)
        def _():
            z_pass(i).wait_send()

    def x_copy(i, part):
        if isinstance(i, int) and i >= FAR:
            ref = spot(i, c, z, y, x) if part == 0 else spot(i, c, z, 1 - y, x).at[pl.ds(rows // 2, rows // 2)]
        elif part == 0:
            ref = spot(i, c, slice(None), y, x)
        else:
            ref = spot(i, c, pl.ds(half, half), 1 - y, x)
        return remote(ref, ref, x_send.at[i, part], x_recv.at[i, part], along_x)

    def y_copy(i, part):
        if isinstance(i, int) and i >= FAR:
            ref = spot(i, c, z, y, x) if part == 0 else spot(i, c, z, y, 1 - x).at[pl.ds(0, rows // 2)]
        elif part == 0:
            ref = spot(i, c, slice(None), y, x)
        else:
            ref = spot(i, c, pl.ds(0, half), y, 1 - x)
        return remote(ref, ref, y_send.at[i, part], y_recv.at[i, part], along_y)

    def s_copy(i, part):
        if isinstance(i, int) and i >= FAR:
            ref = whole_ref.at[i, c, part]
        else:
            yy, xx = ((y, x), (y, 1 - x), (1 - y, x), (1 - y, 1 - x))[part]
            ref = spot(i, c, slice(None), yy, xx)
        return remote(ref, ref, s_send.at[i, part], s_recv.at[i, part], sibling)

    def join(i):
        block[i] = jnp.concatenate([halves[0, i], halves[1, i]], axis=-1)
        own_copy(i).start()

    def begin(i):
        join(i)
        z_start(i)

    def far_begin(i):
        own_copy(i).wait()
        x_copy(i, 0).start()
        y_copy(i, 0).start()

    def far_pass(i):
        x_copy(i, 0).wait_recv()
        y_copy(i, 1).start()
        y_copy(i, 0).wait_recv()
        x_copy(i, 1).start()

    def far_line(i):
        x_copy(i, 1).wait_recv()
        y_copy(i, 1).wait_recv()
        z_start(i)

    def far_finish(i):
        z_finish(i)
        for part in range(lines):
            s_copy(i, part).start()

    def spread_line(i):
        own_copy(i).wait()
        z_finish(i)
        x_copy(i, 0).start()
        y_copy(i, 0).start()
        s_copy(i, 0).start()

    def pass_on(i):
        x_copy(i, 0).wait_recv()
        y_copy(i, 1).start()
        s_copy(i, 1).start()
        y_copy(i, 0).wait_recv()
        x_copy(i, 1).start()
        s_copy(i, 2).start()

    def finish(i):
        x_copy(i, 1).wait_recv()
        y_copy(i, 1).wait_recv()
        s_copy(i, 3).start()

    def arrived(i):
        for part in range(4):
            s_copy(i, part).wait_recv()

    def load(i, k):
        slot = i % 2
        return pltpu.make_async_copy(whole_ref.at[i, k], weights.at[slot, k], load_sem.at[slot, k])

    def fetch(i):
        arrived(i)
        load(i, 0).start()
        load(i, 1).start()

    def product(total, tap, slot, k):
        for n in range(CHUNKS):
            value = dot(act[tap % 3, lines_from(tap // 3)], weight_cols(weights.at[slot, k], n))
            total[:, :, :, chunk(n)] += value.reshape(RES, SLOTS, RES, WIDTH)

    def use_pair(total, i, first):
        slot = i % 2
        load(i, 0).wait()
        load(i, 1).wait()
        each(2, lambda k: product(total, 2 * (i - first) + k, slot, k))

    def set_act(turned):
        def by_line(yy):
            value = act_f32[yy].reshape(LINE, C)
            left, right = shifted(value)
            spot_rows = pl.ds(pl.multiple_of((yy + 1) * LINE, LINE), LINE)
            act[0, spot_rows] = left.astype(BF16)
            act[1, spot_rows] = value.astype(BF16)
            act[2, spot_rows] = right.astype(BF16)

        each(RES, by_line)

        def turn(yy):
            value = act_f32[pl.ds(2 * yy, 2)].reshape(2 * LINE, C)
            turned[:, span(yy, 2 * LINE)] = value.T.astype(BF16)

        each(RES // 2, turn)

    def norm_a():
        for k in range(n_head - 1):
            vec_copy(k).wait()
        vecs_ref[...] = jnp.concatenate([vec_all[k].astype(F32) for k in range(n_head)], axis=-1)

        def get(n):
            return images_ref[span(n, PIX)].astype(F32)

        mean, inverse = stats_ref.at[0], stats_ref.at[1]
        norm_stats(get, mean, inverse, sums_ref)

        def to_act(n):
            value = (get(n) - mean[row(n)]) * inverse[row(n)]
            act_f32[:, n] = silu(value * vecs_ref[0:1] + vecs_ref[1:2]).reshape(RES, RES, C)
            conv_ref[:, n] = jnp.broadcast_to(vecs_ref[2:3].reshape(1, 1, C), (RES, RES, C))
            resid_ref[:, n] = (get(n) + vecs_ref[5:6]).reshape(RES, RES, C)

        each(SLOTS, to_act)
        set_act(turned_a)

    def embed():
        for k in range(n_dp - 1):
            ids_copy(k).wait()
        ids = all_ids[...].reshape(n_dp * SLOTS, 128)
        table = class_ref.shape[0]
        label_hot = lax.broadcasted_iota(jnp.int32, (n_dp * SLOTS, table), 1) == ids[:, 0:1]
        level_hot = lax.broadcasted_iota(jnp.int32, (n_dp * SLOTS, 128), 1) == ids[:, 1:2]
        pre = dot(jnp.where(label_hot, 1.0, 0.0).astype(BF16), class_ref[...])
        pre += dot(jnp.where(level_hot, 1.0, 0.0).astype(BF16), noise_ref[...])
        pre_ref[...] = pre
        part = dot(silu(pre).astype(BF16), modw_ref[...])
        for k in range(n_dp):
            mine = part[k * SLOTS : (k + 1) * SLOTS]
            mod_part[k] = jnp.concatenate([mine[:, :C], mine[:, C:]], axis=0).astype(BF16)
        mod_got[d] = mod_part[d]
        for k in range(n_dp - 1):
            mod_copy(k).start()

    def norm_b():
        for k in range(n_dp - 1):
            mod_copy(k).wait()
        total = modb_ref[...]
        for k in range(n_dp):
            total += mod_got[k].astype(F32)
        mod_ref[...] = total.astype(BF16).astype(F32)

        def get(n):
            return conv_ref[:, n].reshape(PIX, C)

        mean, inverse = stats_ref.at[2], stats_ref.at[3]
        norm_stats(get, mean, inverse, sums_ref)

        def to_act(n):
            value = (get(n) - mean[row(n)]) * inverse[row(n)]
            value = value * vecs_ref[3:4] + vecs_ref[4:5]
            value = mod_ref[row(SLOTS + n)] + value * (mod_ref[row(n)] + 1.0)
            act_f32[:, n] = silu(value).reshape(RES, RES, C)

        each(SLOTS, to_act)
        set_act(turned_b)

    swap.start()
    keep.start()
    for k in range(n_head - 1):
        vec_copy(k).start()
    for k in range(n_dp - 1):
        ids_copy(k).start()
    vec_all[h] = vec_ref[...]
    all_ids[d] = ids_ref[...]
    edge = jnp.zeros((LINE, C), BF16)
    for j in range(3):
        act[j, 0:LINE] = edge
        act[j, ALL + LINE : ALL + 2 * LINE] = edge
    keep.wait()
    swap.wait()
    for i in (10, 9):
        join(i)
    begin(0)
    for i in (10, 9):
        far_begin(i)
    begin(1)
    z_relay(0)
    begin(2)
    spread_line(0)
    for i in (10, 9):
        far_pass(i)
    begin(3)
    z_relay(1)
    norm_a()
    spread_line(1)
    pass_on(0)
    begin(4)
    z_relay(2)
    embed()
    spread_line(2)
    pass_on(1)
    finish(0)
    begin(5)
    z_relay(3)
    begin(6)
    z_relay(4)
    far_line(10)
    spread_line(3)
    pass_on(2)
    finish(1)
    fetch(0)

    def body(turn, carry):
        @pl.when(turn < 6)
        def _():
            begin(turn + 3)

        @pl.when(turn == 6)
        def _():
            far_line(9)
            z_relay(10)

        z_relay(turn + 1)
        spread_line(turn)
        pass_on(turn - 1)
        finish(turn - 2)
        fetch(turn - 3)
        use_pair(conv_ref, turn - 4, 0)
        return carry

    lax.fori_loop(4, 8, body, 0)
    spread_line(8)
    pass_on(7)
    finish(6)
    fetch(5)
    load(4, 0).wait()
    load(4, 1).wait()
    product(conv_ref, 8, 0, 0)
    norm_b()
    product(resid_ref, 8, 0, 1)
    pass_on(8)
    finish(7)
    z_relay(9)
    fetch(6)
    far_finish(10)
    use_pair(resid_ref, 5, 5)
    finish(8)
    fetch(7)
    use_pair(resid_ref, 6, 5)
    fetch(8)
    use_pair(resid_ref, 7, 5)
    far_finish(9)
    use_pair(resid_ref, 8, 5)
    arrived(10)
    arrived(9)

    def drain(i):
        z_drain(i)
        for part in range(2):
            x_copy(i, part).wait_send()
            y_copy(i, part).wait_send()
        for part in range(4):
            s_copy(i, part).wait_send()

    each(FAR, drain)
    drain(9)
    drain(10)


def run_forward(taps, vec, images, ids, class_rows, noise_rows, mod_rows, mod_bias):
    n_dp, n_head = lax.axis_size("dp"), lax.axis_size("head")
    units, rows, cols = taps.shape
    lines, across, wide = n_dp // 2, n_head // 2, 2 * cols
    board = (RES, SLOTS, RES, C)
    shape = jax.ShapeDtypeStruct
    return pl.pallas_call(
        functools.partial(forward_kernel, lines),
        out_shape=(
            shape((PAIRS, 2, lines, 2, rows, across * wide), BF16),
            shape((16, C), F32),
            shape((2 * SLOTS, C), F32),
            shape(board, F32),
            shape(board, F32),
            shape((C, ALL), BF16),
            shape((C, ALL), BF16),
            shape((4, SLOTS, C), F32),
            shape((n_dp * SLOTS, 128), F32),
            shape((n_dp, SLOTS, 128), jnp.int32),
        ),
        in_specs=[ANY] + [VMEM] * 7,
        out_specs=(ANY,) + (VMEM,) * 9,
        scratch_shapes=[
            pltpu.VMEM((2, PAIRS, rows, cols), BF16),
            pltpu.VMEM((PAIRS, rows, wide), BF16),
            pltpu.VMEM((n_head, 16, cols), BF16),
            pltpu.VMEM((n_dp, 2 * SLOTS, C), BF16),
            pltpu.VMEM((n_dp, 2 * SLOTS, C), BF16),
            pltpu.VMEM((3, ALL + 2 * LINE, C), BF16),
            pltpu.VMEM(board, F32),
            pltpu.VMEM((2, 2, lines, 2, rows, across * wide), BF16),
            pltpu.VMEM((SLOTS, C), F32),
            DMA,
            DMA,
            DMA,
            DMA((PAIRS,)),
            DMA((PAIRS, lines - 1)),
            DMA((PAIRS, lines - 1)),
            DMA((PAIRS,)),
            DMA((PAIRS, 2)),
            DMA((PAIRS, 2)),
            DMA((PAIRS, 2)),
            DMA((PAIRS, 2)),
            DMA((PAIRS, 4)),
            DMA((PAIRS, 4)),
            DMA((n_head - 1,)),
            DMA((n_head - 1,)),
            DMA((n_dp - 1,)),
            DMA((n_dp - 1,)),
            DMA((n_dp - 1,)),
            DMA((n_dp - 1,)),
            DMA((2, 2)),
        ],
        compiler_params=pltpu.CompilerParams(
            collective_id=0, has_side_effects=True, vmem_limit_bytes=48 * 2**20
        ),
        name="gather_forward",
    )(taps.reshape(PAIRS, 2, rows, cols), vec, images, ids, class_rows, noise_rows, mod_rows, mod_bias)


def attend_kernel(
    whole_ref,
    resid_ref,
    cot_ref,
    live_ref,
    vecs_ref,
    out_ref,
    grad_ref,
    grad_low,
    turned,
    right,
    sums_out,
    attn_in,
    qkv,
    weights,
    grad_attn,
    mixed,
    mean,
    inverse,
    sums_ref,
    pair_ref,
    load_sem,
):
    first = whole_ref.shape[0] - 2

    def load(k):
        return pltpu.make_async_copy(whole_ref.at[first + k // 2, k % 2], weights.at[k], load_sem.at[k])

    for k in range(4):
        load(k).start()

    def get(n):
        return resid_ref[:, n].reshape(PIX, C)

    norm_stats(get, mean, inverse, sums_ref)
    sums_out[...] = jnp.zeros_like(sums_out)

    def normed(n):
        return (get(n) - mean[row(n)]) * inverse[row(n)]

    def prepare(n):
        attn_in[span(n, PIX)] = (normed(n) * vecs_ref[6:7] + vecs_ref[7:8]).astype(BF16)
        grad = cot_ref[span(n, PIX)].astype(F32) * live_ref[row(n)]
        right[3, span(n, PIX)] = grad.astype(BF16)
        sums_out[8:9] += sum_rows(grad)

    each(SLOTS, prepare)
    for k in range(4):
        load(k).wait()
    for t in range(3):
        for n in range(CHUNKS):
            qkv[t, :, chunk(n)] = dot(attn_in[...], weight_cols(weights.at[t], n)).astype(BF16)
    for n in range(CHUNKS):
        qkv[3, :, chunk(n)] = dot_nt(right[3], weight_rows(weights.at[3], n)).astype(BF16)

    factor = DH ** (-0.5)
    lane = lax.broadcasted_iota(jnp.int32, (PIX, 2 * DH), 1)
    low = lane < DH

    def stack(value):
        zero = jnp.zeros_like(value)
        return jnp.concatenate([jnp.where(low, value, zero), jnp.where(low, zero, value)], axis=0)

    def pick(value):
        return jnp.where(low, value[:PIX], value[PIX:])

    def attend(n):
        for pair in range(C // (2 * DH)):
            lanes = slice(pair * 2 * DH, (pair + 1) * 2 * DH)
            query, key, value, grad = (qkv[t, span(n, PIX), lanes] for t in range(4))
            query2, grad2 = stack(query), stack(grad)
            scores = dot_nt(query2, key) * factor
            weight = jnp.exp(scores - jnp.max(scores, axis=-1, keepdims=True))
            probs = weight / jnp.sum(weight, axis=-1, keepdims=True)
            probs_low = probs.astype(BF16)
            mixed[span(n, PIX), lanes] = pick(dot(probs_low, value)).astype(BF16)
            grad_probs = dot_nt(grad2, value)
            inner = jnp.sum(grad_probs * probs, axis=-1, keepdims=True)
            grad_scores = (probs * (grad_probs - inner)).astype(BF16)
            right[0, span(n, PIX), lanes] = (pick(dot(grad_scores, key)) * factor).astype(BF16)
            right[1, span(n, PIX), lanes] = (dot_tn(grad_scores, query2) * factor).astype(BF16)
            right[2, span(n, PIX), lanes] = dot_tn(probs_low, grad2).astype(BF16)

    each(SLOTS, attend)

    for n in range(CHUNKS):
        grad_attn[:, chunk(n)] = dot(mixed[...], weight_cols(weights.at[3], n))

    def finish(n):
        value = get(n) + grad_attn[span(n, PIX)] + vecs_ref[8:9]
        out_ref[span(n, PIX)] = (value * live_ref[row(n)]).astype(BF16)

    each(SLOTS, finish)

    def turn(k):
        for slot, source in ((0, attn_in), (1, mixed)):
            value = source[span(k, 128)].astype(F32)
            turned[slot, :, span(k, 128)] = value.T.astype(BF16)

    each(ALL // 128, turn)

    for n in range(CHUNKS):
        total = None
        for t in range(3):
            value = dot_nt(right[t], weight_rows(weights.at[t], n))
            total = value if total is None else total + value
        grad_attn[:, chunk(n)] = total

    def back(n):
        grad, gn = grad_attn[span(n, PIX)], normed(n)
        sums_out[6:7] += sum_rows(grad * gn)
        sums_out[7:8] += sum_rows(grad)
        head = grad * vecs_ref[6:7]
        pair_ref[row(n)] = sum_rows(head)
        pair_ref[row(SLOTS + n)] = sum_rows(head * gn)

    each(SLOTS, back)
    pair_ref[...] = group_mean(pair_ref[...])

    def back_second(n):
        gn = normed(n)
        head = grad_attn[span(n, PIX)] * vecs_ref[6:7]
        value = inverse[row(n)] * (head - pair_ref[row(n)] - gn * pair_ref[row(SLOTS + n)])
        value += right[3, span(n, PIX)].astype(F32)
        grad_ref[:, n] = value.reshape(RES, RES, C)
        sums_out[5:6] += sum_rows(value.astype(BF16).astype(F32))

    each(SLOTS, back_second)

    def lower(yy):
        grad_low[span(yy, LINE)] = grad_ref[yy].reshape(LINE, C).astype(BF16)

    each(RES, lower)


def run_attention(whole, resid, cotangent, live, vecs):
    board = (RES, SLOTS, RES, C)
    shape = jax.ShapeDtypeStruct
    return pl.pallas_call(
        attend_kernel,
        out_shape=(
            shape((ALL, C), BF16),
            shape(board, F32),
            shape((ALL, C), BF16),
            shape((2, C, ALL), BF16),
            shape((4, ALL, C), BF16),
            shape((16, C), F32),
        ),
        in_specs=[ANY] + [VMEM] * 4,
        out_specs=(VMEM,) * 6,
        scratch_shapes=[
            pltpu.VMEM((ALL, C), BF16),
            pltpu.VMEM((4, ALL, C), BF16),
            pltpu.VMEM((4,) + whole.shape[2:], BF16),
            pltpu.VMEM((ALL, C), F32),
            pltpu.VMEM((ALL, C), BF16),
            pltpu.VMEM((SLOTS, C), F32),
            pltpu.VMEM((SLOTS, C), F32),
            pltpu.VMEM((SLOTS, C), F32),
            pltpu.VMEM((2 * SLOTS, C), F32),
            DMA((4,)),
        ],
        compiler_params=pltpu.CompilerParams(vmem_limit_bytes=56 * 2**20),
        name="attention",
    )(whole, resid, cotangent, live, vecs)


def backward_kernel(
    lines,
    whole_ref,
    turned_a,
    turned_b,
    turned_ref,
    right_ref,
    grad_low_ref,
    grad_resid_ref,
    conv_ref,
    images_ref,
    stats_ref,
    vecs_ref,
    mod_ref,
    sums_in,
    pre_ref,
    ids_ref,
    modw_ref,
    out_ref,
    image_ref,
    class_ref,
    modw_out,
    vec_out,
    mine,
    from_x,
    from_y,
    from_z,
    far_x,
    far_y,
    far_z,
    ends,
    lefts,
    rights,
    grads,
    stage,
    weights,
    total,
    sums_ref,
    pair_ref,
    gm_mine,
    gm_all,
    mw_mine,
    mw_got,
    ge_all,
    vs_mine,
    vs_got,
    vt_mine,
    vt_all,
    x_send,
    x_recv,
    y_send,
    y_recv,
    z_send,
    z_recv,
    p_send,
    p_recv,
    e_send,
    e_recv,
    e_local,
    op_send,
    op_recv,
    op_local,
    load_sem,
    gm_send,
    gm_recv,
    mw_send,
    mw_recv,
    ge_send,
    ge_recv,
    vs_send,
    vs_recv,
    vt_send,
    vt_recv,
):
    z, y, x, c = place()
    d, h = lax.axis_index("dp"), lax.axis_index("head")
    n_dp, n_head = lines * 2, 4
    half = lines // 2
    inner = jnp.logical_and(z > 0, z < lines - 1)
    rows, wide = from_z.shape[2], from_z.shape[3]
    cols = wide // 2
    sibling = at_chip(z, y, x, 1 - c)
    along_x = at_chip(z, y, 1 - x, c)
    along_y = at_chip(z, 1 - y, x, c)
    line = [at_chip(lax.rem(z + k, lines), y, x, c) for k in range(1, lines)]
    column, heads = column_peers(n_dp), head_peers(n_head)

    own_rows = pl.ds(LINE, ALL)

    def operand(k):
        if k == 0:
            return right_ref.at[2 + c], right_ref.at[3 - c], rights.at[0, c]
        if k == 1:
            return turned_ref.at[c], turned_ref.at[1 - c], lefts.at[1, c]
        if k == 2:
            return right_ref.at[c], right_ref.at[1 - c], rights.at[1, c]
        if k == 3:
            return turned_ref.at[0], turned_ref.at[0], lefts.at[0, c]
        if k == 4:
            return grad_low_ref, grad_low_ref, grads.at[1, c, own_rows]
        if k == 5:
            return turned_b, turned_b, lefts.at[2, c]
        return turned_a, turned_a, lefts.at[3, c]

    def op_own(k):
        source, _, target = operand(k)
        return pltpu.make_async_copy(source, target, op_local.at[k])

    def op_copy(k):
        _, source, target = operand(k)
        return remote(source, target, op_send.at[k], op_recv.at[k], sibling)

    def stage_copy():
        return remote(grads.at[1, c, own_rows], stage, op_send.at[7], op_recv.at[7], sibling)

    def op_wait(k):
        op_own(k).wait()
        op_copy(k).wait_recv()

    def lanes(xx):
        return span(xx, wide)

    first, second = pl.ds(0, rows // 2), pl.ds(rows // 2, rows // 2)

    def is_far(i):
        return isinstance(i, int) and i >= FAR

    def x_copy(i, part):
        if is_far(i):
            into = far_x.at[i - FAR]
            if part == 0:
                src, dst = mine.at[i, z, 1 - y, second, lanes(1 - x)], into.at[pl.ds(rows, rows // 2)]
            else:
                src, dst = mine.at[i, z, y, :, lanes(1 - x)], into.at[pl.ds(0, rows)]
        elif part == 0:
            src, dst = mine.at[i, pl.ds(half, half), 1 - y, :, lanes(1 - x)], from_x.at[i, pl.ds(lines, half)]
        else:
            src, dst = mine.at[i, :, y, :, lanes(1 - x)], from_x.at[i, pl.ds(0, lines)]
        return remote(src, dst, x_send.at[i, part], x_recv.at[i, part], along_x)

    def y_copy(i, part):
        if is_far(i):
            into = far_y.at[i - FAR]
            if part == 0:
                src, dst = mine.at[i, z, 1 - y, first, lanes(1 - x)], into.at[pl.ds(rows, rows // 2)]
            else:
                src, dst = mine.at[i, z, 1 - y, :, lanes(x)], into.at[pl.ds(0, rows)]
        elif part == 0:
            src, dst = mine.at[i, pl.ds(0, half), 1 - y, :, lanes(1 - x)], from_y.at[i, pl.ds(lines, half)]
        else:
            src, dst = mine.at[i, :, 1 - y, :, lanes(x)], from_y.at[i, pl.ds(0, lines)]
        return remote(src, dst, y_send.at[i, part], y_recv.at[i, part], along_y)

    beyond = lax.rem(z + 2, lines)
    opposite = lines - 1 - z
    near_end = at_chip(1 + z // (lines - 1), y, x, c)

    def z_block(i, zz):
        return mine.at[i, zz] if is_far(i) else mine.at[i, zz, y, :, lanes(x)]

    def z_slot(i, k):
        return far_z.at[i - FAR, k] if is_far(i) else from_z.at[i, k]

    def z_copy(i, k):
        return remote(
            z_block(i, lax.rem(z + k + 1, lines)), z_slot(i, k), z_send.at[i, k], z_recv.at[i, k], line[k]
        )

    def z_give(i):
        return remote(z_block(i, opposite), z_slot(i, 3), p_send.at[i], p_recv.at[i], near_end)

    def z_start(i):
        @pl.when(z < lines - 1)
        def _():
            z_copy(i, 0).start()

        @pl.when(z > 0)
        def _():
            z_copy(i, 2).start()

        @pl.when(jnp.logical_not(inner))
        def _():
            z_copy(i, 1).start()
            z_give(i).start()

    def z_mix(i):
        @pl.when(inner)
        def _():
            z_give(i).wait_recv()
            if is_far(i):
                mine[i, beyond] += far_z[i - FAR, 3]
            else:
                mine[i, beyond, y, :, lanes(x)] += from_z[i, 3]
            z_copy(i, 1).start()

    def z_wait(i):
        z_copy(i, 1).wait_recv()

        @pl.when(z > 0)
        def _():
            z_copy(i, 0).wait_recv()

        @pl.when(z < lines - 1)
        def _():
            z_copy(i, 2).wait_recv()

    def z_drain(i):
        z_copy(i, 1).wait_send()

        @pl.when(z < lines - 1)
        def _():
            z_copy(i, 0).wait_send()

        @pl.when(z > 0)
        def _():
            z_copy(i, 2).wait_send()

        @pl.when(jnp.logical_not(inner))
        def _():
            z_give(i).wait_send()

    def e_copy(i):
        return remote(ends.at[1 - c, i], out_ref.at[i, c], e_send.at[i], e_recv.at[i], sibling)

    def e_own(i):
        return pltpu.make_async_copy(ends.at[c, i], out_ref.at[i, c], e_local.at[i])

    def finish(i, value):
        for cc in range(2):
            ends[cc, i] = value[:, cc * cols : (cc + 1) * cols]
        e_copy(i).start()
        e_own(i).start()

    def offer(i):
        x_copy(i, 0).start()
        y_copy(i, 0).start()

    def relay(i):
        x_copy(i, 0).wait_recv()
        y_copy(i, 0).wait_recv()
        if is_far(i):
            rest = pl.ds(rows, rows // 2)
            mine[i, z, y, first, lanes(1 - x)] += far_y[i - FAR, rest]
            mine[i, z, 1 - y, second, lanes(x)] += far_x[i - FAR, rest]
        else:
            for j in range(half):
                mine[i, j, y, :, lanes(1 - x)] += from_y[i, lines + j]
                mine[i, half + j, 1 - y, :, lanes(x)] += from_x[i, lines + j]
        x_copy(i, 1).start()
        y_copy(i, 1).start()

    def collect(i):
        x_copy(i, 1).wait_recv()
        y_copy(i, 1).wait_recv()
        if is_far(i):
            whole_rows = pl.ds(0, rows)
            value = mine[i, z, y, :, lanes(x)].astype(F32)
            value += far_x[i - FAR, whole_rows].astype(F32) + far_y[i - FAR, whole_rows].astype(F32)
            finish(i, value)
            return

        def add(j):
            value = mine[i, j, y, :, lanes(x)].astype(F32)
            value += from_x[i, j].astype(F32) + from_y[i, j].astype(F32)
            mine[i, j, y, :, lanes(x)] = value.astype(BF16)

        each(lines, add)
        z_start(i)

    def last(i):
        z_wait(i)
        if is_far(i):
            for yy in range(2):
                value = mine[i, z, yy].astype(F32)
                for k in range(lines - 1):
                    value += far_z[i - FAR, k, yy].astype(F32)
                mine[i, z, yy] = value.astype(BF16)
            offer(i)
            return
        value = mine[i, z, y, :, lanes(x)].astype(F32)
        for k in range(lines - 1):
            value += from_z[i, k].astype(F32)
        finish(i, value)

    def put(i, n, value):
        mine[i, :, :, :, chunk(n)] = value.astype(BF16).reshape(mine.shape[1:4] + (WIDTH,))

    def plain_unit(i, left, right):
        for n in range(CHUNKS):
            value = dot(lefts[left, 0], rights[right, 0, :, chunk(n)])
            value += dot(lefts[left, 1], rights[right, 1, :, chunk(n)])
            put(i, n, value)

    def conv_product(left, tap, n):
        where, side = lines_from(2 - tap // 3), 2 - tap % 3
        value = dot(lefts[left, 0], grads[side, 0, where, chunk(n)])
        return value + dot(lefts[left, 1], grads[side, 1, where, chunk(n)])

    def conv_unit(i, left, k):
        for n in range(CHUNKS):
            put(i, n, conv_product(left, 2 * k + c, n))

    def extra_b():
        for n in range(CHUNKS):
            put(4, n, conv_product(2, 8, n))

    def extra_a():
        for n in range(CHUNKS):
            old = mine[4, :, :, :, chunk(n)].astype(F32).reshape(C, WIDTH)
            put(4, n, jnp.where(c == 0, conv_product(3, 8, n), old))

    def spread_sides(core):
        def by_line(yy):
            value = grads[1, core, pl.ds(pl.multiple_of((yy + 1) * LINE, LINE), LINE)].astype(F32)
            left, right = shifted(value)
            spot_rows = pl.ds(pl.multiple_of((yy + 1) * LINE, LINE), LINE)
            grads[0, core, spot_rows] = left.astype(BF16)
            grads[2, core, spot_rows] = right.astype(BF16)

        each(RES, by_line)

    def load(tap, base):
        unit = base + tap - 9 * (tap // 8) * (base // 10)
        return pltpu.make_async_copy(
            whole_ref.at[unit // 2, unit % 2], weights.at[tap % 2], load_sem.at[tap % 2]
        )

    def conv_back(tap, base):
        load(tap, base).wait()

        @pl.when(tap < 8)
        def _():
            load(tap + 1, base).start()

        part = grads[2 - tap % 3, c, lines_from(2 - tap // 3)]
        for n in range(CHUNKS):
            value = dot_nt(part, weight_rows(weights.at[tap % 2], n))
            total[:, :, :, chunk(n)] += value.reshape(RES, SLOTS, RES, WIDTH)

    def conv_back_range(first, stop, base):
        def body(tap, carry):
            conv_back(tap, base)
            return carry

        lax.fori_loop(first, stop, body, 0)

    def slope(values):
        sigma = jax.nn.sigmoid(values)
        return sigma * (1.0 + values * (1.0 - sigma))

    for k in (0, 2):
        from_z[:, k] = jnp.zeros_like(from_z[:, k])
        far_z[:, k] = jnp.zeros_like(far_z[:, k])
    greet(column + heads)
    for k in range(7):
        op_own(k).start()
        op_copy(k).start()
    load(0, 10).start()
    vs_mine[...] = jnp.zeros_like(vs_mine)
    edge = jnp.zeros((LINE, C), BF16)
    for j in range(3):
        for core in range(2):
            grads[j, core, 0:LINE] = edge
            grads[j, core, ALL + LINE : ALL + 2 * LINE] = edge
    total[...] = jnp.zeros_like(total)
    sums_ref[...] = sums_in[...]

    op_wait(0)
    op_wait(1)
    plain_unit(10, 1, 0)
    z_start(10)
    op_wait(2)
    op_wait(3)
    plain_unit(9, 0, 1)
    z_start(9)
    op_wait(4)
    op_wait(5)
    spread_sides(0)
    spread_sides(1)

    def units_b(k, carry):
        conv_unit(5 + k, 2, k)
        offer(5 + k)
        return carry

    lax.fori_loop(0, 4, units_b, 0)
    z_mix(10)
    z_mix(9)
    extra_b()
    conv_back_range(0, 3, 10)
    relay(5)
    relay(6)
    conv_back_range(3, 6, 10)
    relay(7)
    relay(8)
    conv_back_range(6, 9, 10)
    last(10)
    load(0, 0).start()

    def norm_b_value(n):
        value = (conv_ref[:, n].reshape(PIX, C) - stats_ref[2, row(n)]) * stats_ref[3, row(n)]
        return value

    def back_b(n):
        normed = norm_b_value(n)
        out = normed * vecs_ref[3:4] + vecs_ref[4:5]
        scale = mod_ref[row(n)] + 1.0
        grad = total[:, n].reshape(PIX, C) * slope(mod_ref[row(SLOTS + n)] + out * scale)
        pair_ref[row(n)] = sum_rows(grad * out)
        pair_ref[row(SLOTS + n)] = sum_rows(grad)
        grad = grad * scale
        sums_ref[3:4] += sum_rows(grad * normed)
        sums_ref[4:5] += sum_rows(grad)
        total[:, n] = (grad * vecs_ref[3:4]).reshape(RES, RES, C)

    each(SLOTS, back_b)
    gm_mine[...] = pair_ref[...].astype(BF16)
    gm_all[d] = gm_mine[...]

    def gm_copy(k):
        return remote(gm_mine, gm_all.at[d], gm_send.at[k], gm_recv.at[k], column[k])

    for k in range(n_dp - 1):
        gm_copy(k).start()
    collect(5)

    def group_pairs(get):
        def gather(n):
            head = total[:, n].reshape(PIX, C)
            pair_ref[row(n)] = sum_rows(head)
            pair_ref[row(SLOTS + n)] = sum_rows(head * get(n))

        each(SLOTS, gather)
        pair_ref[...] = group_mean(pair_ref[...])

    group_pairs(norm_b_value)

    def back_b_second(n):
        head = total[:, n].reshape(PIX, C)
        value = head - pair_ref[row(n)] - norm_b_value(n) * pair_ref[row(SLOTS + n)]
        value = (stats_ref[3, row(n)] * value).astype(BF16).astype(F32)
        sums_ref[2:3] += sum_rows(value)
        total[:, n] = value.reshape(RES, RES, C)

    each(SLOTS, back_b_second)

    def lower(yy):
        spot_rows = pl.ds(pl.multiple_of((yy + 1) * LINE, LINE), LINE)
        grads[1, c, spot_rows] = total[yy].reshape(LINE, C).astype(BF16)

    op_copy(4).wait_send()
    each(RES, lower)
    stage_copy().start()
    spread_sides(c)
    total[...] = jnp.zeros_like(total)
    collect(6)
    last(9)
    conv_back_range(0, 3, 0)
    stage_copy().wait_recv()

    def take(yy):
        spot_rows = pl.ds(pl.multiple_of((yy + 1) * LINE, LINE), LINE)
        grads[1, 1 - c, spot_rows] = stage[span(yy, LINE)]

    each(RES, take)
    spread_sides(1 - c)
    op_wait(6)
    extra_a()
    offer(4)

    def units_a(k, carry):
        conv_unit(k, 3, k)
        offer(k)
        return carry

    lax.fori_loop(0, 4, units_a, 0)
    relay(10)
    z_mix(5)
    z_mix(6)
    collect(7)
    collect(8)
    relay(4)
    conv_back_range(3, 6, 0)
    relay(9)
    relay(0)
    z_mix(7)
    z_mix(8)
    last(5)

    for k in range(n_dp - 1):
        gm_copy(k).wait()
    parts = gm_all[...].astype(F32)
    count = n_dp * SLOTS
    gm_scale = parts[:, :SLOTS].reshape(count, C)
    gm_offset = parts[:, SLOTS:].reshape(count, C)
    pre = pre_ref[...]
    emb = silu(pre).astype(BF16)
    part_rows = rows // n_head
    for k, value in ((0, gm_scale), (1, gm_offset)):
        low_value = value.astype(BF16)
        grad_w = dot_tn(emb, low_value)
        place_lanes = slice(k * C, (k + 1) * C)
        for hh in range(n_head):
            mw_mine[hh, 0:part_rows, place_lanes] = grad_w[hh * part_rows : (hh + 1) * part_rows]
            mw_mine[hh, part_rows : part_rows + 8, place_lanes] = jnp.broadcast_to(sum_rows(value), (8, C))
    grad_e = dot_nt(gm_scale.astype(BF16), modw_ref[:, :C]) + dot_nt(gm_offset.astype(BF16), modw_ref[:, C:])
    grad_e = grad_e * slope(pre)
    label = ids_ref[...].reshape(count, 128)[:, 0:1].astype(F32)
    lane = lax.broadcasted_iota(jnp.int32, grad_e.shape, 1)
    ge_all[h] = jnp.where(lane < rows, grad_e, label)

    def mw_copy(k):
        return remote(
            mw_mine.at[lax.rem(h + k + 1, n_head)], mw_got.at[k], mw_send.at[k], mw_recv.at[k], heads[k]
        )

    def ge_copy(k):
        return remote(ge_all.at[h], ge_all.at[h], ge_send.at[k], ge_recv.at[k], heads[k])

    for k in range(n_head - 1):
        mw_copy(k).start()
        ge_copy(k).start()

    relay(1)
    conv_back_range(6, 9, 0)
    relay(2)
    collect(10)
    last(6)
    relay(3)

    def norm_a_value(n):
        return (images_ref[span(n, PIX)].astype(F32) - stats_ref[0, row(n)]) * stats_ref[1, row(n)]

    def back_a(n):
        normed = norm_a_value(n)
        grad = total[:, n].reshape(PIX, C) * slope(normed * vecs_ref[0:1] + vecs_ref[1:2])
        sums_ref[0:1] += sum_rows(grad * normed)
        sums_ref[1:2] += sum_rows(grad)
        total[:, n] = (grad * vecs_ref[0:1]).reshape(RES, RES, C)

    each(SLOTS, back_a)

    for hh in range(n_head):
        vs_mine[hh] = sums_ref[:, hh * cols : (hh + 1) * cols]

    def vs_copy(k):
        return remote(
            vs_mine.at[lax.rem(h + k + 1, n_head)], vs_got.at[k], vs_send.at[k], vs_recv.at[k], heads[k]
        )

    def vt_copy(k):
        return remote(vt_mine, vt_all.at[d], vt_send.at[k], vt_recv.at[k], column[k])

    for k in range(n_head - 1):
        vs_copy(k).start()
    collect(4)
    collect(9)
    last(7)
    group_pairs(norm_a_value)

    def back_a_second(n):
        head = total[:, n].reshape(PIX, C)
        value = head - pair_ref[row(n)] - norm_a_value(n) * pair_ref[row(SLOTS + n)]
        image_ref[span(n, PIX)] = stats_ref[1, row(n)] * value + grad_resid_ref[:, n].reshape(PIX, C)

    each(SLOTS, back_a_second)
    collect(0)
    z_mix(4)
    last(8)
    value = vs_mine[h]
    for k in range(n_head - 1):
        vs_copy(k).wait()
        value += vs_got[k]
    vt_mine[...] = value
    vt_all[d] = value
    for k in range(n_dp - 1):
        vt_copy(k).start()
    value = mw_mine[h]
    for k in range(n_head - 1):
        mw_copy(k).wait()
        value += mw_got[k]
    modw_out[...] = value
    collect(1)
    z_mix(0)
    last(4)
    table = class_ref.shape[0]
    classes = None
    for k in range(n_head - 1):
        ge_copy(k).wait()
    for k in range(n_head):
        value = ge_all[k]
        hot = lax.broadcasted_iota(jnp.int32, (count, table), 1) == value[:, rows : rows + 1].astype(jnp.int32)
        value = dot_tn(jnp.where(hot, 1.0, 0.0).astype(BF16), value.astype(BF16))
        classes = value if classes is None else classes + value
    class_ref[...] = classes
    collect(2)
    z_mix(1)
    last(0)
    for k in range(n_dp - 1):
        vt_copy(k).wait()
    value = vt_all[0]
    for k in range(1, n_dp):
        value += vt_all[k]
    vec_out[...] = value
    collect(3)
    z_mix(2)
    last(1)
    z_mix(3)
    last(2)
    last(3)

    for k in range(7):
        if k != 4:
            op_copy(k).wait_send()
    stage_copy().wait_send()

    def drain(i):
        for part in range(2):
            x_copy(i, part).wait_send()
            y_copy(i, part).wait_send()
        z_drain(i)
        e_own(i).wait()
        e_copy(i).wait()

    each(FAR, drain)
    drain(9)
    drain(10)


def run_backward(whole, turned_a, turned_b, turned, right, grad_low, grad_resid, conv_out, images, stats, vecs, mod, sums, pre, ids, modw):
    n_dp, n_head = lax.axis_size("dp"), lax.axis_size("head")
    _, _, lines, _, rows, depth = whole.shape
    cols = depth // n_head
    wide = 2 * cols
    board = (RES, SLOTS, RES, C)
    shape = jax.ShapeDtypeStruct
    return pl.pallas_call(
        functools.partial(backward_kernel, lines),
        out_shape=(
            shape((PAIRS, 2, rows, cols), F32),
            shape((ALL, C), F32),
            shape((1024, 128), F32),
            shape((rows // n_head + 8, 2 * C), F32),
            shape((16, cols), F32),
        ),
        in_specs=[ANY] * 6 + [VMEM] * 10,
        out_specs=(ANY,) + (VMEM,) * 4,
        scratch_shapes=[
            pltpu.VMEM((PAIRS, lines, 2, rows, depth), BF16),
            pltpu.VMEM((FAR, lines + lines // 2, rows, wide), BF16),
            pltpu.VMEM((FAR, lines + lines // 2, rows, wide), BF16),
            pltpu.VMEM((FAR, 4, rows, wide), BF16),
            pltpu.VMEM((PAIRS - FAR, rows + rows // 2, wide), BF16),
            pltpu.VMEM((PAIRS - FAR, rows + rows // 2, wide), BF16),
            pltpu.VMEM((PAIRS - FAR, 4, 2, rows, depth), BF16),
            pltpu.VMEM((2, PAIRS, rows, cols), F32),
            pltpu.VMEM((4, 2, C, ALL), BF16),
            pltpu.VMEM((2, 2, ALL, C), BF16),
            pltpu.VMEM((3, 2, ALL + 2 * LINE, C), BF16),
            pltpu.VMEM((ALL, C), BF16),
            pltpu.VMEM((2, lines, 2, rows, depth), BF16),
            pltpu.VMEM(board, F32),
            pltpu.VMEM((16, C), F32),
            pltpu.VMEM((2 * SLOTS, C), F32),
            pltpu.VMEM((2 * SLOTS, C), BF16),
            pltpu.VMEM((n_dp, 2 * SLOTS, C), BF16),
            pltpu.VMEM((n_head, rows // n_head + 8, 2 * C), F32),
            pltpu.VMEM((n_head - 1, rows // n_head + 8, 2 * C), F32),
            pltpu.VMEM((n_head, n_dp * SLOTS, 128), F32),
            pltpu.VMEM((n_head, 16, cols), F32),
            pltpu.VMEM((n_head - 1, 16, cols), F32),
            pltpu.VMEM((16, cols), F32),
            pltpu.VMEM((n_dp, 16, cols), F32),
            DMA((PAIRS, 2)),
            DMA((PAIRS, 2)),
            DMA((PAIRS, 2)),
            DMA((PAIRS, 2)),
            DMA((PAIRS, lines - 1)),
            DMA((PAIRS, lines - 1)),
            DMA((PAIRS,)),
            DMA((PAIRS,)),
            DMA((PAIRS,)),
            DMA((PAIRS,)),
            DMA((PAIRS,)),
            DMA((8,)),
            DMA((8,)),
            DMA((7,)),
            DMA((2,)),
            DMA((n_dp - 1,)),
            DMA((n_dp - 1,)),
            DMA((n_head - 1,)),
            DMA((n_head - 1,)),
            DMA((n_head - 1,)),
            DMA((n_head - 1,)),
            DMA((n_head - 1,)),
            DMA((n_head - 1,)),
            DMA((n_dp - 1,)),
            DMA((n_dp - 1,)),
        ],
        compiler_params=pltpu.CompilerParams(
            collective_id=1, has_side_effects=True, vmem_limit_bytes=64 * 2**20 - 2**18
        ),
        name="backward_scatter",
    )(whole, turned_a, turned_b, turned, right, grad_low, grad_resid, conv_out, images, stats, vecs, mod, sums, pre, ids, modw)


def direct(rows, cols):
    n_dp, n_head = lax.axis_size("dp"), lax.axis_size("head")
    return n_head == 4 and n_dp == 8 and rows % 32 == 0 and cols % 64 == 0


def fast_shards(
    images,
    cotangent,
    counts,
    labels,
    levels,
    noise_table,
    class_table,
    gain_a,
    shift_a,
    conv_a,
    bias_a,
    mod_weight,
    mod_bias,
    gain_b,
    shift_b,
    conv_b,
    bias_b,
    gain_c,
    shift_c,
    qkv_weight,
    proj_weight,
    proj_bias,
):
    n_head = lax.axis_size("head")
    d, h = lax.axis_index("dp"), lax.axis_index("head")
    rows = class_table.shape[1]
    taps = jnp.concatenate(
        [
            jnp.swapaxes(conv_a, 0, 1),
            jnp.swapaxes(conv_b[:, 8:9], 0, 1),
            jnp.swapaxes(conv_b[:, 0:8], 0, 1),
            jnp.swapaxes(qkv_weight, 0, 1),
            proj_weight[None],
        ],
        axis=0,
    )
    vec = jnp.stack([gain_a, shift_a, bias_a, gain_b, shift_b, bias_b, gain_c, shift_c, proj_bias])
    vec = jnp.pad(vec, ((0, 7), (0, 0)))
    ids = jnp.pad(jnp.stack([labels, levels], axis=1), ((0, 0), (0, 126)))
    class_rows = jnp.pad(class_table, ((0, 1024 - class_table.shape[0]), (0, 128 - rows)))
    noise_rows = lax.dynamic_slice_in_dim(noise_table, d * rows, rows, axis=1)
    noise_rows = jnp.pad(noise_rows, ((0, 128 - noise_rows.shape[0]), (0, 128 - rows)))
    mod_rows = jnp.pad(mod_weight.reshape(rows, 2 * C), ((0, 128 - rows), (0, 0)))
    bias_rows = jnp.repeat(mod_bias.astype(F32), SLOTS, axis=0)
    live = live_rows(counts, d * n_head + h, 1, SLOTS)
    live = jnp.broadcast_to(live[:, None], (SLOTS, C))
    flat = images.reshape(ALL, C)
    whole, vecs, mod, conv_out, resid, turned_a, turned_b, stats, pre, all_ids = run_forward(
        taps, vec, flat, ids, class_rows, noise_rows, mod_rows, bias_rows
    )
    block_out, grad_resid, grad_low, turned, right, sums = run_attention(
        whole, resid, cotangent.reshape(ALL, C), live, vecs
    )
    out, image_grad, classes, modw, vectors = run_backward(
        whole,
        turned_a,
        turned_b,
        turned,
        right,
        grad_low,
        grad_resid,
        conv_out,
        flat,
        stats,
        vecs,
        mod,
        sums,
        pre,
        all_ids,
        mod_rows,
    )
    out = out.reshape((UNITS,) + out.shape[2:])
    part = rows // n_head
    class_grad = lax.dynamic_slice(classes, (0, h * part), (class_table.shape[0], part))
    modb = modw[part].reshape(2, C)
    modb_grad = lax.dynamic_slice_in_dim(modb, (d * n_head + h) * part, part, axis=1)
    return (
        block_out.reshape(images.shape),
        image_grad.reshape(images.shape),
        class_grad,
        vectors[0],
        vectors[1],
        jnp.swapaxes(out[0:9], 0, 1),
        vectors[2],
        modw[:part].reshape(part, 2, C),
        modb_grad,
        vectors[3],
        vectors[4],
        jnp.swapaxes(jnp.concatenate([out[10:18], out[9:10]], axis=0), 0, 1),
        vectors[5],
        vectors[6],
        vectors[7],
        jnp.swapaxes(out[18:21], 0, 1),
        out[21],
        vectors[8],
    )


def shards(*args):
    rows, _, cols = args[9].shape
    if direct(rows, cols):
        return fast_shards(*args)
    return plain_shards(*args)


def solution(mesh):
    placed = (
        P(("dp", "head"), None, None, None),
        P(("dp", "head"), None, None, None),
        P(),
        P(("dp", "head")),
        P(("dp", "head")),
        P(),
        P(None, "dp"),
        P("head"),
        P("head"),
        P("dp", None, "head"),
        P("head"),
        P("dp", None, None),
        P(),
        P("head"),
        P("head"),
        P("dp", None, "head"),
        P("head"),
        P("head"),
        P("head"),
        P("dp", None, "head"),
        P("dp", "head"),
        P("head"),
    )
    return jax.shard_map(
        shards,
        mesh=mesh,
        in_specs=placed,
        out_specs=(
            P(("dp", "head"), None, None, None),
            P(("dp", "head"), None, None, None),
            P(None, ("dp", "head")),
            P("head"),
            P("head"),
            P("dp", None, "head"),
            P("head"),
            P(("dp", "head"), None, None),
            P(None, ("dp", "head")),
            P("head"),
            P("head"),
            P("dp", None, "head"),
            P("head"),
            P("head"),
            P("head"),
            P("dp", None, "head"),
            P("dp", "head"),
            P("head"),
        ),
        check_vma=False,
    )
```

```python
import functools

import jax
import jax.numpy as jnp
from jax import lax
from jax.experimental import pallas as pl
from jax.experimental.pallas import tpu as pltpu
from jax.sharding import PartitionSpec as P

C = 768
DH = 64
GROUPS = 32


EPSILON = 1e-05
HIGHEST = lax.Precision.HIGHEST


def norm_forward(values, gain, shift):
    count, chans = (values.shape[0], values.shape[-1])
    span = C // GROUPS
    grouped = values.reshape(count, -1, chans // span, span)
    mean = jnp.mean(grouped, axis=(1, 3), keepdims=True)
    centred = grouped - mean
    inverse = lax.rsqrt(jnp.mean(centred * centred, axis=(1, 3), keepdims=True) + EPSILON)
    normed = (centred * inverse).reshape(values.shape)
    return (normed * gain + shift, normed, inverse)


def norm_backward(grad_out, normed, inverse, gain):
    grad_gain = jnp.sum(grad_out * normed, axis=(0, 1, 2))
    grad_shift = jnp.sum(grad_out, axis=(0, 1, 2))
    count, chans = (grad_out.shape[0], grad_out.shape[-1])
    span = C // GROUPS
    layout = (count, -1, chans // span, span)
    grad_normed = (grad_out * gain).reshape(layout)
    normed_groups = normed.reshape(layout)
    mean_one = jnp.mean(grad_normed, axis=(1, 3), keepdims=True)
    mean_two = jnp.mean(grad_normed * normed_groups, axis=(1, 3), keepdims=True)
    grad_in = inverse * (grad_normed - mean_one - normed_groups * mean_two)
    return (grad_in.reshape(grad_out.shape), grad_gain, grad_shift)


def silu_slope(values):
    sigma = jax.nn.sigmoid(values)
    return sigma * (1.0 + values * (1.0 - sigma))


def patches_of(act):
    count, rows, cols, chans = act.shape
    padded = jnp.pad(act, ((0, 0), (1, 1), (1, 1), (0, 0)))
    taps = [padded[:, i : i + rows, j : j + cols, :] for i in range(3) for j in range(3)]
    return jnp.stack(taps, axis=3).reshape(count * rows * cols, 9, chans)


def contract_rows(left, right):
    return lax.dot_general(
        left, right, (((0,), (0,)), ((), ())), preferred_element_type=jnp.float32
    )


def contract_cols(left, right):
    return lax.dot_general(
        left, right, (((1,), (1,)), ((), ())), preferred_element_type=jnp.float32
    )


def conv_back(grad_low, weight, count, rows, cols):
    chans = weight.shape[0]
    padded = jnp.zeros((count, rows + 2, cols + 2, chans), jnp.float32)
    for tap in range(9):
        i, j = divmod(tap, 3)
        part = contract_cols(grad_low, weight[:, tap, :]).reshape(count, rows, cols, chans)
        padded = padded.at[:, i : i + rows, j : j + cols, :].add(part)
    return padded[:, 1 : rows + 1, 1 : cols + 1, :]


def keep_same(values):
    return values


def live_rows(counts, first, number, count):
    sums = jnp.sum(counts, axis=1)
    chosen = lax.dynamic_slice_in_dim(sums, first, number)
    slots = lax.iota(jnp.int32, count)
    return (slots[None, :] < chosen[:, None]).astype(jnp.float32).reshape(number * count)


def residual_forward(source, mod_pair, weights, spread):
    (
        conv_one,
        conv_two,
        gain_one,
        shift_one,
        bias_one,
        gain_two,
        shift_two,
        bias_two,
        gain_three,
        shift_three,
    ) = weights
    out_a, normed_a, inverse_a = norm_forward(source, gain_one, shift_one)
    wide_a = spread(jax.nn.silu(out_a).astype(jnp.bfloat16))
    conv_out_a = (
        jnp.einsum("ptc,cto->po", patches_of(wide_a), conv_one, preferred_element_type=jnp.float32)
        + bias_one
    ).reshape(source.shape)
    scale = mod_pair[:, :, 0:1, :]
    offset = mod_pair[:, :, 1:2, :]
    out_b, normed_b, inverse_b = norm_forward(conv_out_a, gain_two, shift_two)
    inner_b = offset + out_b * (scale + 1.0)
    wide_b = spread(jax.nn.silu(inner_b).astype(jnp.bfloat16))
    conv_out_b = (
        jnp.einsum("ptc,cto->po", patches_of(wide_b), conv_two, preferred_element_type=jnp.float32)
        + bias_two
    ).reshape(source.shape)
    resid = source + conv_out_b
    out_c, normed_c, inverse_c = norm_forward(resid, gain_three, shift_three)
    attn_in = out_c.astype(jnp.bfloat16)
    saved = (
        out_a,
        normed_a,
        inverse_a,
        wide_a,
        out_b,
        normed_b,
        inverse_b,
        inner_b,
        wide_b,
        normed_c,
        inverse_c,
        scale,
    )
    return (resid, attn_in, saved)


def residual_backward(grad_attn, grad_out, saved, weights, reduce_value):
    conv_one, conv_two, gain_one, gain_two, gain_three = (
        weights[0],
        weights[1],
        weights[2],
        weights[5],
        weights[8],
    )
    (
        out_a,
        normed_a,
        inverse_a,
        wide_a,
        out_b,
        normed_b,
        inverse_b,
        inner_b,
        wide_b,
        normed_c,
        inverse_c,
        scale,
    ) = saved
    count, rows, cols, local = grad_out.shape
    grad_resid_c, gainc_term, shiftc_term = norm_backward(
        grad_attn, normed_c, inverse_c, gain_three
    )
    grad_resid = grad_out + grad_resid_c
    grad_conv_b = grad_resid.reshape(-1, local).astype(jnp.bfloat16)
    biasb_term = jnp.sum(grad_conv_b.astype(jnp.float32), axis=0)
    convb_term = jnp.einsum(
        "ptc,po->cto", patches_of(wide_b), grad_conv_b, preferred_element_type=jnp.float32
    )
    grad_act_b = reduce_value(conv_back(grad_conv_b, conv_two, count, rows, cols))
    grad_inner = grad_act_b * silu_slope(inner_b)
    grad_offset = jnp.sum(grad_inner, axis=(1, 2))
    grad_scale = jnp.sum(grad_inner * out_b, axis=(1, 2))
    grad_mod = jnp.stack([grad_scale, grad_offset], axis=1)[:, None]
    grad_conv_full, gainb_term, shiftb_term = norm_backward(
        grad_inner * (scale + 1.0), normed_b, inverse_b, gain_two
    )
    grad_conv_a = grad_conv_full.reshape(-1, local).astype(jnp.bfloat16)
    biasa_term = jnp.sum(grad_conv_a.astype(jnp.float32), axis=0)
    conva_term = jnp.einsum(
        "ptc,po->cto", patches_of(wide_a), grad_conv_a, preferred_element_type=jnp.float32
    )
    grad_act_a = reduce_value(conv_back(grad_conv_a, conv_one, count, rows, cols))
    grad_source, gaina_term, shifta_term = norm_backward(
        grad_act_a * silu_slope(out_a), normed_a, inverse_a, gain_one
    )
    image_grad = grad_resid + grad_source
    vectors = (
        gaina_term,
        shifta_term,
        biasa_term,
        gainb_term,
        shiftb_term,
        biasb_term,
        gainc_term,
        shiftc_term,
    )
    return (image_grad, grad_mod, (conva_term, convb_term), vectors)


def attend_forward(block):
    query, key, value = (block[:, :, 0], block[:, :, 1], block[:, :, 2])
    batch, pixels, heads_here, depth = query.shape
    scores = jnp.einsum("bqhd,bkhd->bhqk", query, key, preferred_element_type=jnp.float32) * DH ** (
        -0.5
    )
    top = jnp.max(scores, axis=-1, keepdims=True)
    weights = jnp.exp(scores - top)
    sums = jnp.sum(weights, axis=-1, keepdims=True)
    probs = (weights / sums).astype(jnp.bfloat16)
    logsum = (top + jnp.log(sums))[..., 0]
    mixed = jnp.einsum("bhqk,bkhd->bqhd", probs, value, preferred_element_type=jnp.float32).astype(
        jnp.bfloat16
    )
    return (mixed.reshape(batch, pixels, heads_here * depth), logsum)


def attend_backward(block, logsum, grad_head):
    query, key, value = (block[:, :, 0], block[:, :, 1], block[:, :, 2])
    batch, pixels, heads_here, depth = query.shape
    factor = DH ** (-0.5)
    scores = jnp.einsum("bqhd,bkhd->bhqk", query, key, preferred_element_type=jnp.float32) * factor
    probs = jnp.exp(scores - logsum[..., None])
    grad_value = jnp.einsum(
        "bhqk,bqhd->bkhd", probs.astype(jnp.bfloat16), grad_head, preferred_element_type=jnp.float32
    )
    grad_probs = jnp.einsum("bqhd,bkhd->bhqk", grad_head, value, preferred_element_type=jnp.float32)
    inner = jnp.sum(grad_probs * probs, axis=-1, keepdims=True)
    grad_scores = (probs * (grad_probs - inner)).astype(jnp.bfloat16)
    grad_query = (
        jnp.einsum("bhqk,bkhd->bqhd", grad_scores, key, preferred_element_type=jnp.float32) * factor
    )
    grad_key = (
        jnp.einsum("bhqk,bqhd->bkhd", grad_scores, query, preferred_element_type=jnp.float32)
        * factor
    )
    stacked = jnp.stack([grad_query, grad_key, grad_value], axis=2).astype(jnp.bfloat16)
    return stacked.reshape(batch, pixels, 3, heads_here * depth)


def plain_shards(
    images,
    cotangent,
    counts,
    labels,
    levels,
    noise_table,
    class_table,
    gain_a,
    shift_a,
    conv_a,
    bias_a,
    mod_weight,
    mod_bias,
    gain_b,
    shift_b,
    conv_b,
    bias_b,
    gain_c,
    shift_c,
    qkv_weight,
    proj_weight,
    proj_bias,
):
    rows_a, rows_b, rows_qkv, rows_proj, mod_full, class_full = (
        lax.all_gather(conv_a, "dp", axis=0, tiled=True),
        lax.all_gather(conv_b, "dp", axis=0, tiled=True),
        lax.all_gather(qkv_weight, "dp", axis=0, tiled=True),
        lax.all_gather(proj_weight, "dp", axis=0, tiled=True),
        lax.all_gather(mod_weight, "dp", axis=0, tiled=True),
        lax.all_gather(class_table, "dp", axis=1, tiled=True),
    )
    count, rows, cols, channels = images.shape
    pixels = rows * cols
    groups_n = lax.axis_size("head")
    quarter = channels // groups_n
    heads_local = quarter // DH
    first_dp = lax.axis_index("dp") * groups_n
    class_hot = (labels[:, None] == lax.iota(jnp.int32, class_full.shape[0])[None, :]).astype(
        jnp.bfloat16
    )
    level_hot = (levels[:, None] == lax.iota(jnp.int32, noise_table.shape[0])[None, :]).astype(
        jnp.bfloat16
    )
    embed_pre = jnp.dot(class_hot, class_full, preferred_element_type=jnp.float32) + jnp.dot(
        level_hot, noise_table, preferred_element_type=jnp.float32
    )
    embed = jax.nn.silu(embed_pre).astype(jnp.bfloat16)
    modulation = (
        jnp.einsum("ne,etc->ntc", embed, mod_full, preferred_element_type=jnp.float32)
        + mod_bias.astype(jnp.float32)
    ).astype(jnp.bfloat16)
    mod_pair = modulation.reshape(count, 1, 2, channels)
    (
        conv_one,
        conv_two,
        qkv_full,
        proj_full,
        gain_one,
        shift_one,
        bias_one,
        gain_two,
        shift_two,
        bias_two,
        gain_three,
        shift_three,
        bias_three,
    ) = (
        lax.all_gather(rows_a, "head", axis=2, tiled=True),
        lax.all_gather(rows_b, "head", axis=2, tiled=True),
        lax.all_gather(rows_qkv, "head", axis=2, tiled=True),
        lax.all_gather(rows_proj, "head", axis=1, tiled=True),
        lax.all_gather(gain_a, "head", axis=0, tiled=True),
        lax.all_gather(shift_a, "head", axis=0, tiled=True),
        lax.all_gather(bias_a, "head", axis=0, tiled=True),
        lax.all_gather(gain_b, "head", axis=0, tiled=True),
        lax.all_gather(shift_b, "head", axis=0, tiled=True),
        lax.all_gather(bias_b, "head", axis=0, tiled=True),
        lax.all_gather(gain_c, "head", axis=0, tiled=True),
        lax.all_gather(shift_c, "head", axis=0, tiled=True),
        lax.all_gather(proj_bias, "head", axis=0, tiled=True),
    )
    weights = (
        conv_one,
        conv_two,
        gain_one,
        shift_one,
        bias_one,
        gain_two,
        shift_two,
        bias_two,
        gain_three,
        shift_three,
    )
    live = live_rows(counts, first_dp + lax.axis_index("head"), 1, count)
    total = count * pixels
    width = channels // groups_n
    source = images.astype(jnp.float32)
    resid, attn_in, saved = residual_forward(
        source, mod_pair.astype(jnp.float32), weights, keep_same
    )
    attn_flat = attn_in.reshape(total, channels)
    qkv_flat = qkv_full.reshape(channels, 3 * channels)
    qkv = jnp.dot(attn_flat, qkv_flat, preferred_element_type=jnp.float32).astype(jnp.bfloat16)
    packed = qkv.reshape(1, count, pixels, 3, groups_n, width)
    block = lax.all_to_all(packed, "head", split_axis=4, concat_axis=0, tiled=True)
    groups = block.shape[0]
    items = block.shape[1]
    flat = block.reshape(groups * items, pixels, 3, heads_local, DH)
    mixed, logsum = attend_forward(flat)
    mixed = mixed.reshape(groups, items, pixels, 1, width)
    returned = lax.all_to_all(mixed, "head", split_axis=0, concat_axis=3, tiled=True)
    returned, logsum, kept = (returned, logsum.reshape(groups, items, heads_local, pixels), block)
    mixed_image = returned.reshape(total, channels)
    result = (
        resid.reshape(total, channels)
        + jnp.dot(mixed_image, proj_full, preferred_element_type=jnp.float32)
        + bias_three
    )
    block_out = (result.reshape(images.shape) * live[:, None, None, None]).astype(jnp.bfloat16)
    grad_out = cotangent.astype(jnp.float32) * live[:, None, None, None]
    grad_flat = grad_out.reshape(total, channels)
    grad_low = grad_flat.astype(jnp.bfloat16)
    projw_full = contract_rows(mixed_image, grad_low)
    projb_full = jnp.sum(grad_flat, axis=0)
    grad_mixed = contract_cols(grad_low, proj_full).astype(jnp.bfloat16)
    arrived = lax.all_to_all(
        grad_mixed.reshape(1, count, pixels, groups_n, width),
        "head",
        split_axis=3,
        concat_axis=0,
        tiled=True,
    )
    flat_block = kept.reshape(groups_n * count, pixels, 3, heads_local, DH)
    grad_head = arrived.reshape(groups_n * count, pixels, heads_local, DH)
    stacked = attend_backward(
        flat_block, logsum.reshape(groups_n * count, heads_local, pixels), grad_head
    )
    stacked = stacked.reshape(groups_n, count, pixels, 3, 1, width)
    grad_qkv = lax.all_to_all(stacked, "head", split_axis=0, concat_axis=4, tiled=True).reshape(
        total, 3 * channels
    )
    qkvw_full = contract_rows(attn_flat, grad_qkv).reshape(channels, 3, channels)
    grad_attn = contract_cols(grad_qkv, qkv_flat).reshape(images.shape)
    image_grad, grad_mod_part, conv_terms, vectors = residual_backward(
        grad_attn, grad_out, saved, weights, keep_same
    )
    (
        gaina_full,
        shifta_full,
        biasa_full,
        gainb_full,
        shiftb_full,
        biasb_full,
        gainc_full,
        shiftc_full,
    ) = vectors
    (
        conva_term,
        convb_term,
        qkvw_term,
        projw_term,
        gaina_term,
        shifta_term,
        biasa_term,
        gainb_term,
        shiftb_term,
        biasb_term,
        gainc_term,
        shiftc_term,
        projb_term,
    ) = (
        lax.psum_scatter(
            conv_terms[0].astype(jnp.bfloat16), "head", scatter_dimension=2, tiled=True
        ).astype(jnp.float32),
        lax.psum_scatter(
            conv_terms[1].astype(jnp.bfloat16), "head", scatter_dimension=2, tiled=True
        ).astype(jnp.float32),
        lax.psum_scatter(
            qkvw_full.astype(jnp.bfloat16), "head", scatter_dimension=2, tiled=True
        ).astype(jnp.float32),
        lax.psum_scatter(
            projw_full.astype(jnp.bfloat16), "head", scatter_dimension=1, tiled=True
        ).astype(jnp.float32),
        lax.psum_scatter(
            gaina_full.astype(jnp.bfloat16), "head", scatter_dimension=0, tiled=True
        ).astype(jnp.float32),
        lax.psum_scatter(
            shifta_full.astype(jnp.bfloat16), "head", scatter_dimension=0, tiled=True
        ).astype(jnp.float32),
        lax.psum_scatter(
            biasa_full.astype(jnp.bfloat16), "head", scatter_dimension=0, tiled=True
        ).astype(jnp.float32),
        lax.psum_scatter(
            gainb_full.astype(jnp.bfloat16), "head", scatter_dimension=0, tiled=True
        ).astype(jnp.float32),
        lax.psum_scatter(
            shiftb_full.astype(jnp.bfloat16), "head", scatter_dimension=0, tiled=True
        ).astype(jnp.float32),
        lax.psum_scatter(
            biasb_full.astype(jnp.bfloat16), "head", scatter_dimension=0, tiled=True
        ).astype(jnp.float32),
        lax.psum_scatter(
            gainc_full.astype(jnp.bfloat16), "head", scatter_dimension=0, tiled=True
        ).astype(jnp.float32),
        lax.psum_scatter(
            shiftc_full.astype(jnp.bfloat16), "head", scatter_dimension=0, tiled=True
        ).astype(jnp.float32),
        lax.psum_scatter(
            projb_full.astype(jnp.bfloat16), "head", scatter_dimension=0, tiled=True
        ).astype(jnp.float32),
    )
    grad_mod = grad_mod_part.reshape(count, 2, channels)
    modw_term = jnp.einsum("ne,ntc->etc", embed.astype(jnp.float32), grad_mod, precision=HIGHEST)
    modb_term = jnp.sum(grad_mod, axis=0)
    grad_embed = jnp.einsum(
        "ntc,etc->ne", grad_mod, mod_full.astype(jnp.float32), precision=HIGHEST
    ) * silu_slope(embed_pre)
    class_term = lax.dot_general(
        class_hot.astype(jnp.float32), grad_embed, (((0,), (0,)), ((), ())), precision=HIGHEST
    )
    modw_grad, class_grad, modb_grad = (
        lax.psum_scatter(modw_term, ("dp", "head"), scatter_dimension=0, tiled=True),
        lax.psum_scatter(class_term, ("dp", "head"), scatter_dimension=1, tiled=True),
        lax.psum_scatter(modb_term, ("dp", "head"), scatter_dimension=1, tiled=True),
    )
    conva_grad, convb_grad, qkvw_grad, projw_grad = (
        lax.psum_scatter(conva_term, "dp", scatter_dimension=0, tiled=True),
        lax.psum_scatter(convb_term, "dp", scatter_dimension=0, tiled=True),
        lax.psum_scatter(qkvw_term, "dp", scatter_dimension=0, tiled=True),
        lax.psum_scatter(projw_term, "dp", scatter_dimension=0, tiled=True),
    )
    (
        gaina_grad,
        shifta_grad,
        biasa_grad,
        gainb_grad,
        shiftb_grad,
        biasb_grad,
        gainc_grad,
        shiftc_grad,
        projb_grad,
    ) = lax.psum(
        (
            gaina_term,
            shifta_term,
            biasa_term,
            gainb_term,
            shiftb_term,
            biasb_term,
            gainc_term,
            shiftc_term,
            projb_term,
        ),
        "dp",
    )
    return (
        block_out,
        image_grad,
        class_grad,
        gaina_grad,
        shifta_grad,
        conva_grad,
        biasa_grad,
        modw_grad,
        modb_grad,
        gainb_grad,
        shiftb_grad,
        convb_grad,
        biasb_grad,
        gainc_grad,
        shiftc_grad,
        qkvw_grad,
        projw_grad,
        projb_grad,
    )


MESH = pl.DeviceIdType.MESH
UNITS = 22
PAIRS = UNITS // 2
FAR = 9
RES = 8
SLOTS = 8
PIX = RES * RES
LINE = SLOTS * RES
ALL = RES * LINE
WIDTH = 256
F32 = jnp.float32
BF16 = jnp.bfloat16
ANY = pl.BlockSpec(memory_space=pl.ANY)
VMEM = pl.BlockSpec(memory_space=pltpu.VMEM)
DMA = pltpu.SemaphoreType.DMA


def place():
    d, h = lax.axis_index("dp"), lax.axis_index("head")
    return d // 2, lax.rem(d, 2), h // 2, lax.rem(h, 2)


def at_chip(z, y, x, c):
    return (z * 2 + y, x * 2 + c)


def column_peers(n_dp):
    d, h = lax.axis_index("dp"), lax.axis_index("head")
    return [(lax.rem(d + k, n_dp), h) for k in range(1, n_dp)]


def head_peers(n_head):
    d, h = lax.axis_index("dp"), lax.axis_index("head")
    return [(d, lax.rem(h + k, n_head)) for k in range(1, n_head)]


def greet(devices):
    barrier = pltpu.get_barrier_semaphore()
    for device in devices:
        pl.semaphore_signal(barrier, inc=1, device_id=device, device_id_type=MESH)
    pl.semaphore_wait(barrier, len(devices))


def remote(src, dst, send, recv, device):
    return pltpu.make_async_remote_copy(
        src_ref=src, dst_ref=dst, send_sem=send, recv_sem=recv, device_id=device, device_id_type=MESH
    )


def each(count, body):
    def step(n, carry):
        body(n)
        return carry

    lax.fori_loop(0, count, step, 0)


def span(index, size):
    return pl.ds(pl.multiple_of(index * size, size), size)


def row(n):
    return pl.ds(n, 1)


def lines_from(i):
    return pl.ds(i * LINE if isinstance(i, int) else pl.multiple_of(i * LINE, LINE), ALL)


def dot(left, right):
    return jnp.dot(left, right, preferred_element_type=F32)


def dot_nt(left, right):
    return lax.dot_general(left, right, (((1,), (1,)), ((), ())), preferred_element_type=F32)


def dot_tn(left, right):
    return lax.dot_general(left, right, (((0,), (0,)), ((), ())), preferred_element_type=F32)


def in_group(first, second, axis):
    chan = lax.broadcasted_iota(jnp.int32, (first, second), axis)
    group = lax.broadcasted_iota(jnp.int32, (first, second), 1 - axis) * (C // GROUPS)
    inside = jnp.logical_and(chan >= group, chan < group + C // GROUPS)
    return jnp.where(inside, 1.0, 0.0).astype(BF16)


def pieces(values):
    high = values.astype(BF16).astype(F32)
    rest = values - high
    mid = rest.astype(BF16).astype(F32)
    return jnp.concatenate([high, mid, rest - mid], axis=0).astype(BF16)


def group_mean(sums):
    count = sums.shape[0]
    part = dot(pieces(sums), in_group(C, 128, 0))
    part = (part[:count] + part[count : 2 * count] + part[2 * count :]) * (1.0 / (PIX * (C // GROUPS)))
    back = dot(pieces(part), in_group(128, C, 1))
    return back[:count] + back[count : 2 * count] + back[2 * count :]


def sum_rows(values):
    return jnp.sum(values, axis=0, keepdims=True)


def norm_stats(get, mean_ref, inverse_ref, sums_ref):
    def first(n):
        sums_ref[row(n)] = sum_rows(get(n))

    each(SLOTS, first)
    mean_ref[...] = group_mean(sums_ref[...])

    def second(n):
        centred = get(n) - mean_ref[row(n)]
        sums_ref[row(n)] = sum_rows(centred * centred)

    each(SLOTS, second)
    inverse_ref[...] = lax.rsqrt(group_mean(sums_ref[...]) + EPSILON)


def silu(values):
    return values * jax.nn.sigmoid(values)


def shifted(values):
    spot = lax.rem(lax.broadcasted_iota(jnp.int32, values.shape, 0), RES)
    left = jnp.where(spot == 0, 0.0, pltpu.roll(values, 1, 0))
    right = jnp.where(spot == RES - 1, 0.0, pltpu.roll(values, values.shape[0] - 1, 0))
    return left, right


def chunk(n):
    return slice(n * WIDTH, (n + 1) * WIDTH)


CHUNKS = C // WIDTH


def weight_cols(ref, n):
    return ref[:, :, :, chunk(n)].reshape(C, WIDTH)


def weight_rows(ref, n):
    return ref[...].reshape(C, C)[chunk(n)]


def forward_kernel(
    lines,
    units_ref,
    vec_ref,
    images_ref,
    cot_ref,
    live_ref,
    ids_ref,
    class_ref,
    noise_ref,
    modw_ref,
    modb_ref,
    whole_ref,
    conv_out,
    slopes_out,
    turned_out,
    block_out,
    grad_out,
    low_out,
    right_out,
    vecs_ref,
    mod_ref,
    stats_ref,
    pre_ref,
    all_ids,
    sums_out,
    halves,
    block,
    vec_all,
    mod_part,
    mod_got,
    act,
    act_f32,
    weights,
    sums_ref,
    conv_ref,
    resid_ref,
    slopes,
    turned,
    attn_in,
    qkv,
    right,
    low,
    pair_ref,
    pair_send,
    pair_recv,
    pair_local,
    own_sem,
    z_send,
    z_recv,
    p_send,
    x_send,
    x_recv,
    y_send,
    y_recv,
    s_send,
    s_recv,
    vec_send,
    vec_recv,
    ids_send,
    ids_recv,
    mod_send,
    mod_recv,
    load_sem,
    flush_sem,
):
    z, y, x, c = place()
    d, h = lax.axis_index("dp"), lax.axis_index("head")
    n_dp, n_head = lines * 2, 4
    half = lines // 2
    inner = jnp.logical_and(z > 0, z < lines - 1)
    far = at_chip(lax.rem(3 * z + 1, lines), y, x, c)
    rows = block.shape[1]
    wide = block.shape[2]
    sibling = at_chip(z, y, x, 1 - c)
    along_x = at_chip(z, y, 1 - x, c)
    along_y = at_chip(z, 1 - y, x, c)
    line = [at_chip(lax.rem(z + k, lines), y, x, c) for k in range(1, lines)]
    column, heads = column_peers(n_dp), head_peers(n_head)
    greet(column + heads)

    def spot(i, cc, zz, yy, xx):
        return whole_ref.at[i, cc, zz, yy, :, span(xx, wide)]

    swap = remote(units_ref.at[:, 1 - c], halves.at[c], pair_send, pair_recv, sibling)
    keep = pltpu.make_async_copy(units_ref.at[:, c], halves.at[c], pair_local)

    def vec_copy(k):
        return remote(vec_ref, vec_all.at[h], vec_send.at[k], vec_recv.at[k], heads[k])

    def ids_copy(k):
        return remote(ids_ref, all_ids.at[d], ids_send.at[k], ids_recv.at[k], column[k])

    def mod_copy(k):
        return remote(
            mod_part.at[lax.rem(d + k + 1, n_dp)], mod_got.at[d], mod_send.at[k], mod_recv.at[k], column[k]
        )

    def own_copy(i):
        return pltpu.make_async_copy(block.at[i], spot(i, c, z, y, x), own_sem.at[i])

    def z_part(i, zz):
        if isinstance(i, int) and i >= FAR:
            return whole_ref.at[i, c, zz]
        return spot(i, c, zz, y, x)

    def z_copy(i, k):
        ref = z_part(i, z)
        source = ref if isinstance(i, int) and i >= FAR else block.at[i]
        return remote(source, ref, z_send.at[i, k], z_recv.at[i, k], line[k])

    def z_pass(i):
        ref = z_part(i, lax.rem(z + 2, lines))
        return remote(ref, ref, p_send.at[i], z_recv.at[i, lax.rem(2 * z + 2, lines)], far)

    def z_start(i):
        z_copy(i, 1).start()

        @pl.when(z != lines - 1)
        def _():
            z_copy(i, 0).start()

        @pl.when(z != 0)
        def _():
            z_copy(i, 2).start()

    def z_relay(i):
        z_copy(i, 1).wait_recv()

        @pl.when(inner)
        def _():
            z_pass(i).start()

    def z_finish(i):
        z_copy(i, 0).wait_recv()
        z_copy(i, 2).wait_recv()

    def z_drain(i):
        z_copy(i, 1).wait_send()

        @pl.when(z != lines - 1)
        def _():
            z_copy(i, 0).wait_send()

        @pl.when(z != 0)
        def _():
            z_copy(i, 2).wait_send()

        @pl.when(inner)
        def _():
            z_pass(i).wait_send()

    def x_copy(i, part):
        if isinstance(i, int) and i >= FAR:
            ref = spot(i, c, z, y, x) if part == 0 else spot(i, c, z, 1 - y, x).at[pl.ds(rows // 2, rows // 2)]
        elif part == 0:
            ref = spot(i, c, slice(None), y, x)
        else:
            ref = spot(i, c, pl.ds(half, half), 1 - y, x)
        return remote(ref, ref, x_send.at[i, part], x_recv.at[i, part], along_x)

    def y_copy(i, part):
        if isinstance(i, int) and i >= FAR:
            ref = spot(i, c, z, y, x) if part == 0 else spot(i, c, z, y, 1 - x).at[pl.ds(0, rows // 2)]
        elif part == 0:
            ref = spot(i, c, slice(None), y, x)
        else:
            ref = spot(i, c, pl.ds(0, half), y, 1 - x)
        return remote(ref, ref, y_send.at[i, part], y_recv.at[i, part], along_y)

    def s_copy(i, part):
        if isinstance(i, int) and i >= FAR:
            ref = whole_ref.at[i, c, part]
        else:
            yy, xx = ((y, x), (y, 1 - x), (1 - y, x), (1 - y, 1 - x))[part]
            ref = spot(i, c, slice(None), yy, xx)
        return remote(ref, ref, s_send.at[i, part], s_recv.at[i, part], sibling)

    def join(i):
        block[i] = jnp.concatenate([halves[0, i], halves[1, i]], axis=-1)
        own_copy(i).start()

    def begin(i):
        join(i)
        z_start(i)

    def far_begin(i):
        own_copy(i).wait()
        x_copy(i, 0).start()
        y_copy(i, 0).start()

    def far_pass(i):
        x_copy(i, 0).wait_recv()
        y_copy(i, 1).start()
        y_copy(i, 0).wait_recv()
        x_copy(i, 1).start()

    def far_line(i):
        x_copy(i, 1).wait_recv()
        y_copy(i, 1).wait_recv()
        z_start(i)

    def far_finish(i):
        z_finish(i)
        for part in range(lines):
            s_copy(i, part).start()

    def spread_line(i):
        own_copy(i).wait()
        z_finish(i)
        x_copy(i, 0).start()
        y_copy(i, 0).start()
        s_copy(i, 0).start()

    def pass_on(i):
        x_copy(i, 0).wait_recv()
        y_copy(i, 1).start()
        s_copy(i, 1).start()
        y_copy(i, 0).wait_recv()
        x_copy(i, 1).start()
        s_copy(i, 2).start()

    def finish(i):
        x_copy(i, 1).wait_recv()
        y_copy(i, 1).wait_recv()
        s_copy(i, 3).start()

    def arrived(i):
        for part in range(4):
            s_copy(i, part).wait_recv()

    def load(i, k):
        slot = i % 2
        return pltpu.make_async_copy(whole_ref.at[i, k], weights.at[slot, k], load_sem.at[slot, k])

    def fetch(i):
        arrived(i)
        load(i, 0).start()
        load(i, 1).start()

    def product(total, tap, slot, k):
        for n in range(CHUNKS):
            value = dot(act[tap % 3, lines_from(tap // 3)], weight_cols(weights.at[slot, k], n))
            total[:, :, :, chunk(n)] += value.reshape(RES, SLOTS, RES, WIDTH)

    def use_pair(total, i, first):
        slot = i % 2
        load(i, 0).wait()
        load(i, 1).wait()
        each(2, lambda k: product(total, 2 * (i - first) + k, slot, k))

    flushed = (
        (conv_ref, conv_out),
        (slopes.at[0], slopes_out.at[0]),
        (slopes.at[1], slopes_out.at[1]),
        (turned.at[3], turned_out.at[3]),
        (turned.at[2], turned_out.at[2]),
        (turned.at[0], turned_out.at[0]),
        (turned.at[1], turned_out.at[1]),
        (low, block_out),
        (resid_ref, grad_out),
        (attn_in, low_out),
        (right, right_out),
    )

    def flush(k):
        return pltpu.make_async_copy(*flushed[k], flush_sem.at[k])

    def set_act(place_t):
        def by_line(yy):
            value = act_f32[yy].reshape(LINE, C)
            left, right = shifted(value)
            spot_rows = pl.ds(pl.multiple_of((yy + 1) * LINE, LINE), LINE)
            act[0, spot_rows] = left.astype(BF16)
            act[1, spot_rows] = value.astype(BF16)
            act[2, spot_rows] = right.astype(BF16)

        each(RES, by_line)

        def turn(yy):
            value = act_f32[pl.ds(2 * yy, 2)].reshape(2 * LINE, C)
            turned[place_t, :, span(yy, 2 * LINE)] = value.T.astype(BF16)

        each(RES // 2, turn)

    def activate(which, n, value):
        sigma = jax.nn.sigmoid(value)
        act_f32[:, n] = (value * sigma).reshape(RES, RES, C)
        slopes[which, :, n] = (sigma * (1.0 + value * (1.0 - sigma))).reshape(RES, RES, C)

    def norm_a():
        for k in range(n_head - 1):
            vec_copy(k).wait()
        vecs_ref[...] = jnp.concatenate([vec_all[k].astype(F32) for k in range(n_head)], axis=-1)

        def get(n):
            return images_ref[span(n, PIX)].astype(F32)

        mean, inverse = stats_ref.at[0], stats_ref.at[1]
        norm_stats(get, mean, inverse, sums_ref)

        def to_act(n):
            value = (get(n) - mean[row(n)]) * inverse[row(n)]
            activate(0, n, value * vecs_ref[0:1] + vecs_ref[1:2])
            conv_ref[:, n] = jnp.broadcast_to(vecs_ref[2:3].reshape(1, 1, C), (RES, RES, C))
            resid_ref[:, n] = (get(n) + vecs_ref[5:6]).reshape(RES, RES, C)

        each(SLOTS, to_act)
        set_act(3)
        flush(1).start()
        flush(3).start()

    def embed():
        for k in range(n_dp - 1):
            ids_copy(k).wait()
        ids = all_ids[...].reshape(n_dp * SLOTS, 128)
        table = class_ref.shape[0]
        label_hot = lax.broadcasted_iota(jnp.int32, (n_dp * SLOTS, table), 1) == ids[:, 0:1]
        level_hot = lax.broadcasted_iota(jnp.int32, (n_dp * SLOTS, 128), 1) == ids[:, 1:2]
        pre = dot(jnp.where(label_hot, 1.0, 0.0).astype(BF16), class_ref[...])
        pre += dot(jnp.where(level_hot, 1.0, 0.0).astype(BF16), noise_ref[...])
        pre_ref[...] = pre
        part = dot(silu(pre).astype(BF16), modw_ref[...])
        for k in range(n_dp):
            mine = part[k * SLOTS : (k + 1) * SLOTS]
            mod_part[k] = jnp.concatenate([mine[:, :C], mine[:, C:]], axis=0).astype(BF16)
        mod_got[d] = mod_part[d]
        for k in range(n_dp - 1):
            mod_copy(k).start()

    def norm_b():
        for k in range(n_dp - 1):
            mod_copy(k).wait()
        total = modb_ref[...]
        for k in range(n_dp):
            total += mod_got[k].astype(F32)
        mod_ref[...] = total.astype(BF16).astype(F32)

        def get(n):
            return conv_ref[:, n].reshape(PIX, C)

        mean, inverse = stats_ref.at[2], stats_ref.at[3]
        norm_stats(get, mean, inverse, sums_ref)

        def to_act(n):
            value = (get(n) - mean[row(n)]) * inverse[row(n)]
            value = value * vecs_ref[3:4] + vecs_ref[4:5]
            value = mod_ref[row(SLOTS + n)] + value * (mod_ref[row(n)] + 1.0)
            activate(1, n, value)

        each(SLOTS, to_act)
        set_act(2)
        flush(0).start()
        flush(2).start()
        flush(4).start()

    def residual(n):
        return resid_ref[:, n].reshape(PIX, C)

    def normed(n):
        return (residual(n) - stats_ref[4, row(n)]) * stats_ref[5, row(n)]

    def transpose_out(source, place_t):
        def turn(k):
            value = source[span(k, 2 * LINE)].astype(F32)
            turned[place_t, :, span(k, 2 * LINE)] = value.T.astype(BF16)

        each(ALL // (2 * LINE), turn)

    def norm_c():
        norm_stats(residual, stats_ref.at[4], stats_ref.at[5], sums_ref)
        sums_out[...] = jnp.zeros_like(sums_out)

        def prepare(n):
            attn_in[span(n, PIX)] = (normed(n) * vecs_ref[6:7] + vecs_ref[7:8]).astype(BF16)
            grad = cot_ref[span(n, PIX)].astype(F32) * live_ref[row(n)]
            right[3, span(n, PIX)] = grad.astype(BF16)
            sums_out[8:9] += sum_rows(grad)

        each(SLOTS, prepare)
        transpose_out(attn_in, 0)
        flush(5).start()

    def attention():
        unit = (weights.at[1, 0], weights.at[1, 1], weights.at[0, 0], weights.at[0, 1])
        for t in range(4):
            load(9 + t // 2, t % 2).wait()
            for n in range(CHUNKS):
                if t < 3:
                    value = dot(attn_in[...], weight_cols(unit[t], n))
                else:
                    value = dot_nt(right[3], weight_rows(unit[3], n))
                qkv[t, :, chunk(n)] = value.astype(BF16)
        factor = DH ** (-0.5)
        band = lax.broadcasted_iota(jnp.int32, (PIX, WIDTH), 1) // DH
        heads_at_once = WIDTH // DH

        def stack(value):
            zero = jnp.zeros_like(value)
            return jnp.concatenate([jnp.where(band == k, value, zero) for k in range(heads_at_once)], axis=0)

        def pick(value):
            out = value[:PIX]
            for k in range(1, heads_at_once):
                out = jnp.where(band == k, value[k * PIX : (k + 1) * PIX], out)
            return out

        def attend(n):
            for b in range(CHUNKS):
                query, key, value, grad = (qkv[t, span(n, PIX), chunk(b)] for t in range(4))
                query4, grad4 = stack(query), stack(grad)
                scores = dot_nt(key, query4) * factor
                weight = jnp.exp(scores - jnp.max(scores, axis=0, keepdims=True))
                probs = weight / jnp.sum(weight, axis=0, keepdims=True)
                probs_low = probs.astype(BF16)
                low[span(n, PIX), chunk(b)] = pick(dot_tn(probs_low, value)).astype(BF16)
                grad_probs = dot_nt(value, grad4)
                inner_sum = jnp.sum(grad_probs * probs, axis=0, keepdims=True)
                grad_scores = (probs * (grad_probs - inner_sum)).astype(BF16)
                right[0, span(n, PIX), chunk(b)] = (pick(dot_tn(grad_scores, key)) * factor).astype(BF16)
                right[1, span(n, PIX), chunk(b)] = (dot(grad_scores, query4) * factor).astype(BF16)
                right[2, span(n, PIX), chunk(b)] = dot(probs_low, grad4).astype(BF16)

        each(SLOTS, attend)
        flush(10).start()
        transpose_out(low, 1)
        flush(6).start()
        for n in range(CHUNKS):
            value = dot(low[...], weight_cols(unit[3], n))
            act_f32[:, :, :, chunk(n)] = value.reshape(SLOTS, RES, RES, WIDTH)

        def finish_out(n):
            value = residual(n) + act_f32[n].reshape(PIX, C) + vecs_ref[8:9]
            low[span(n, PIX)] = (value * live_ref[row(n)]).astype(BF16)

        each(SLOTS, finish_out)
        flush(7).start()
        for n in range(CHUNKS):
            value = dot_nt(right[0], weight_rows(unit[0], n))
            value += dot_nt(right[1], weight_rows(unit[1], n))
            value += dot_nt(right[2], weight_rows(unit[2], n))
            act_f32[:, :, :, chunk(n)] = value.reshape(SLOTS, RES, RES, WIDTH)

        def back(n):
            grad = act_f32[n].reshape(PIX, C)
            pair_ref[row(n)] = sum_rows(grad * normed(n))
            pair_ref[row(SLOTS + n)] = sum_rows(grad)

        each(SLOTS, back)
        sums_out[6:7] = sum_rows(pair_ref[0:SLOTS])
        sums_out[7:8] = sum_rows(pair_ref[SLOTS:])
        pair_ref[...] = group_mean(pair_ref[...] * vecs_ref[6:7])

        def back_second(n):
            inverse = stats_ref[5, row(n)]
            value = act_f32[n].reshape(PIX, C) * (vecs_ref[6:7] * inverse)
            value -= normed(n) * (pair_ref[row(n)] * inverse) + pair_ref[row(SLOTS + n)] * inverse
            value += right[3, span(n, PIX)].astype(F32)
            resid_ref[:, n] = value.reshape(RES, RES, C)
            sums_out[5:6] += sum_rows(value.astype(BF16).astype(F32))

        each(SLOTS, back_second)
        flush(8).start()

        def lower(yy):
            attn_in[span(yy, LINE)] = resid_ref[yy].reshape(LINE, C).astype(BF16)

        each(RES, lower)
        flush(9).start()

    swap.start()
    keep.start()
    for k in range(n_head - 1):
        vec_copy(k).start()
    for k in range(n_dp - 1):
        ids_copy(k).start()
    vec_all[h] = vec_ref[...]
    all_ids[d] = ids_ref[...]
    edge = jnp.zeros((LINE, C), BF16)
    for j in range(3):
        act[j, 0:LINE] = edge
        act[j, ALL + LINE : ALL + 2 * LINE] = edge
    keep.wait()
    swap.wait()
    for i in (10, 9):
        join(i)
    begin(0)
    for i in (10, 9):
        far_begin(i)
    begin(1)
    z_relay(0)
    begin(2)
    spread_line(0)
    for i in (10, 9):
        far_pass(i)
    begin(3)
    z_relay(1)
    norm_a()
    spread_line(1)
    pass_on(0)
    begin(4)
    z_relay(2)
    embed()
    spread_line(2)
    pass_on(1)
    finish(0)
    begin(5)
    z_relay(3)
    begin(6)
    z_relay(4)
    far_line(10)
    spread_line(3)
    pass_on(2)
    finish(1)
    fetch(0)

    def body(turn, carry):
        @pl.when(turn < 6)
        def _():
            begin(turn + 3)

        @pl.when(turn == 6)
        def _():
            far_line(9)
            z_relay(10)

        z_relay(turn + 1)
        spread_line(turn)
        pass_on(turn - 1)
        finish(turn - 2)
        fetch(turn - 3)
        use_pair(conv_ref, turn - 4, 0)
        return carry

    lax.fori_loop(4, 8, body, 0)
    spread_line(8)
    pass_on(7)
    finish(6)
    fetch(5)
    load(4, 0).wait()
    load(4, 1).wait()
    product(conv_ref, 8, 0, 0)
    norm_b()
    product(resid_ref, 8, 0, 1)
    pass_on(8)
    finish(7)
    z_relay(9)
    fetch(6)
    far_finish(10)
    use_pair(resid_ref, 5, 5)
    finish(8)
    fetch(7)
    use_pair(resid_ref, 6, 5)
    fetch(8)
    use_pair(resid_ref, 7, 5)
    far_finish(9)
    use_pair(resid_ref, 8, 5)
    norm_c()
    fetch(9)
    fetch(10)
    attention()

    def drain(i):
        z_drain(i)
        for part in range(2):
            x_copy(i, part).wait_send()
            y_copy(i, part).wait_send()
        for part in range(4):
            s_copy(i, part).wait_send()

    each(FAR, drain)
    drain(9)
    drain(10)
    for k in range(len(flushed)):
        flush(k).wait()


def run_forward(taps, vec, images, cotangent, live, ids, class_rows, noise_rows, mod_rows, mod_bias):
    n_dp, n_head = lax.axis_size("dp"), lax.axis_size("head")
    units, rows, cols = taps.shape
    lines, across, wide = n_dp // 2, n_head // 2, 2 * cols
    board = (RES, SLOTS, RES, C)
    shape = jax.ShapeDtypeStruct
    return pl.pallas_call(
        functools.partial(forward_kernel, lines),
        out_shape=(
            shape((PAIRS, 2, lines, 2, rows, across * wide), BF16),
            shape(board, F32),
            shape((2,) + board, F32),
            shape((4, C, ALL), BF16),
            shape((ALL, C), BF16),
            shape(board, F32),
            shape((ALL, C), BF16),
            shape((4, ALL, C), BF16),
            shape((16, C), F32),
            shape((2 * SLOTS, C), F32),
            shape((6, SLOTS, C), F32),
            shape((n_dp * SLOTS, 128), F32),
            shape((n_dp, SLOTS, 128), jnp.int32),
            shape((16, C), F32),
        ),
        in_specs=[ANY] + [VMEM] * 9,
        out_specs=(ANY,) * 8 + (VMEM,) * 6,
        scratch_shapes=[
            pltpu.VMEM((2, PAIRS, rows, cols), BF16),
            pltpu.VMEM((PAIRS, rows, wide), BF16),
            pltpu.VMEM((n_head, 16, cols), BF16),
            pltpu.VMEM((n_dp, 2 * SLOTS, C), BF16),
            pltpu.VMEM((n_dp, 2 * SLOTS, C), BF16),
            pltpu.VMEM((3, ALL + 2 * LINE, C), BF16),
            pltpu.VMEM(board, F32),
            pltpu.VMEM((2, 2, lines, 2, rows, across * wide), BF16),
            pltpu.VMEM((SLOTS, C), F32),
            pltpu.VMEM(board, F32),
            pltpu.VMEM(board, F32),
            pltpu.VMEM((2,) + board, F32),
            pltpu.VMEM((4, C, ALL), BF16),
            pltpu.VMEM((ALL, C), BF16),
            pltpu.VMEM((4, ALL, C), BF16),
            pltpu.VMEM((4, ALL, C), BF16),
            pltpu.VMEM((ALL, C), BF16),
            pltpu.VMEM((2 * SLOTS, C), F32),
            DMA,
            DMA,
            DMA,
            DMA((PAIRS,)),
            DMA((PAIRS, lines - 1)),
            DMA((PAIRS, lines - 1)),
            DMA((PAIRS,)),
            DMA((PAIRS, 2)),
            DMA((PAIRS, 2)),
            DMA((PAIRS, 2)),
            DMA((PAIRS, 2)),
            DMA((PAIRS, 4)),
            DMA((PAIRS, 4)),
            DMA((n_head - 1,)),
            DMA((n_head - 1,)),
            DMA((n_dp - 1,)),
            DMA((n_dp - 1,)),
            DMA((n_dp - 1,)),
            DMA((n_dp - 1,)),
            DMA((2, 2)),
            DMA((11,)),
        ],
        compiler_params=pltpu.CompilerParams(
            collective_id=0, has_side_effects=True, vmem_limit_bytes=56 * 2**20
        ),
        name="gather_forward",
    )(
        taps.reshape(PAIRS, 2, rows, cols),
        vec,
        images,
        cotangent,
        live,
        ids,
        class_rows,
        noise_rows,
        mod_rows,
        mod_bias,
    )


def backward_kernel(
    lines,
    whole_ref,
    turned_ref,
    right_ref,
    grad_low_ref,
    grad_resid_ref,
    conv_ref,
    slopes_ref,
    images_ref,
    stats_ref,
    vecs_ref,
    mod_ref,
    sums_in,
    pre_ref,
    ids_ref,
    modw_ref,
    out_ref,
    image_ref,
    class_ref,
    modw_out,
    vec_out,
    mine,
    from_x,
    from_y,
    from_z,
    far_x,
    far_y,
    far_z,
    ends,
    lefts,
    rights,
    grads,
    stage,
    weights,
    total,
    board,
    slopes,
    image_mine,
    sums_ref,
    pair_ref,
    coef_ref,
    gm_mine,
    gm_all,
    mw_mine,
    mw_got,
    ge_all,
    vs_mine,
    vs_got,
    vt_mine,
    vt_all,
    x_send,
    x_recv,
    y_send,
    y_recv,
    z_send,
    z_recv,
    p_send,
    p_recv,
    e_send,
    e_recv,
    e_local,
    op_send,
    op_recv,
    op_local,
    load_sem,
    in_sem,
    out_sem,
    gm_send,
    gm_recv,
    mw_send,
    mw_recv,
    ge_send,
    ge_recv,
    vs_send,
    vs_recv,
    vt_send,
    vt_recv,
):
    z, y, x, c = place()
    d, h = lax.axis_index("dp"), lax.axis_index("head")
    n_dp, n_head = lines * 2, 4
    half = lines // 2
    inner = jnp.logical_and(z > 0, z < lines - 1)
    rows, wide = from_z.shape[2], from_z.shape[3]
    cols = wide // 2
    sibling = at_chip(z, y, x, 1 - c)
    along_x = at_chip(z, y, 1 - x, c)
    along_y = at_chip(z, 1 - y, x, c)
    line = [at_chip(lax.rem(z + k, lines), y, x, c) for k in range(1, lines)]
    column, heads = column_peers(n_dp), head_peers(n_head)

    own_rows = pl.ds(LINE, ALL)

    def operand(k):
        if k == 0:
            return right_ref.at[2 + c], right_ref.at[3 - c], rights.at[0, span(c, ALL)]
        if k == 1:
            return turned_ref.at[c], turned_ref.at[1 - c], lefts.at[1, :, span(c, ALL)]
        if k == 2:
            return right_ref.at[c], right_ref.at[1 - c], rights.at[1, span(c, ALL)]
        if k == 3:
            return turned_ref.at[0], turned_ref.at[0], lefts.at[0, :, span(c, ALL)]
        if k == 4:
            return grad_low_ref, grad_low_ref, grads.at[1, c, own_rows]
        return turned_ref.at[k - 3], turned_ref.at[k - 3], lefts.at[k - 3, :, span(c, ALL)]

    def op_own(k):
        source, _, target = operand(k)
        return pltpu.make_async_copy(source, target, op_local.at[k])

    def op_copy(k):
        _, source, target = operand(k)
        return remote(source, target, op_send.at[k], op_recv.at[k], sibling)

    def stage_copy():
        return remote(grads.at[1, c, own_rows], stage, op_send.at[7], op_recv.at[7], sibling)

    def op_wait(k):
        op_own(k).wait()
        op_copy(k).wait_recv()

    def lanes(xx):
        return span(xx, wide)

    first, second = pl.ds(0, rows // 2), pl.ds(rows // 2, rows // 2)

    def is_far(i):
        return isinstance(i, int) and i >= FAR

    def x_copy(i, part):
        if is_far(i):
            into = far_x.at[i - FAR]
            if part == 0:
                src, dst = mine.at[i, z, 1 - y, second, lanes(1 - x)], into.at[pl.ds(rows, rows // 2)]
            else:
                src, dst = mine.at[i, z, y, :, lanes(1 - x)], into.at[pl.ds(0, rows)]
        elif part == 0:
            src, dst = mine.at[i, pl.ds(half, half), 1 - y, :, lanes(1 - x)], from_x.at[i, pl.ds(lines, half)]
        else:
            src, dst = mine.at[i, :, y, :, lanes(1 - x)], from_x.at[i, pl.ds(0, lines)]
        return remote(src, dst, x_send.at[i, part], x_recv.at[i, part], along_x)

    def y_copy(i, part):
        if is_far(i):
            into = far_y.at[i - FAR]
            if part == 0:
                src, dst = mine.at[i, z, 1 - y, first, lanes(1 - x)], into.at[pl.ds(rows, rows // 2)]
            else:
                src, dst = mine.at[i, z, 1 - y, :, lanes(x)], into.at[pl.ds(0, rows)]
        elif part == 0:
            src, dst = mine.at[i, pl.ds(0, half), 1 - y, :, lanes(1 - x)], from_y.at[i, pl.ds(lines, half)]
        else:
            src, dst = mine.at[i, :, 1 - y, :, lanes(x)], from_y.at[i, pl.ds(0, lines)]
        return remote(src, dst, y_send.at[i, part], y_recv.at[i, part], along_y)

    beyond = lax.rem(z + 2, lines)
    opposite = lines - 1 - z
    near_end = at_chip(1 + z // (lines - 1), y, x, c)

    def z_block(i, zz):
        return mine.at[i, zz] if is_far(i) else mine.at[i, zz, y, :, lanes(x)]

    def z_slot(i, k):
        return far_z.at[i - FAR, k] if is_far(i) else from_z.at[i, k]

    def z_copy(i, k):
        return remote(
            z_block(i, lax.rem(z + k + 1, lines)), z_slot(i, k), z_send.at[i, k], z_recv.at[i, k], line[k]
        )

    def z_give(i):
        return remote(z_block(i, opposite), z_slot(i, 3), p_send.at[i], p_recv.at[i], near_end)

    def z_start(i):
        @pl.when(jnp.logical_not(inner))
        def _():
            z_give(i).start()

        @pl.when(z < lines - 1)
        def _():
            z_copy(i, 0).start()

        @pl.when(z > 0)
        def _():
            z_copy(i, 2).start()

        @pl.when(jnp.logical_not(inner))
        def _():
            z_copy(i, 1).start()

    def z_mix(i):
        @pl.when(inner)
        def _():
            z_give(i).wait_recv()
            if is_far(i):
                mine[i, beyond] += far_z[i - FAR, 3]
            else:
                mine[i, beyond, y, :, lanes(x)] += from_z[i, 3]
            z_copy(i, 1).start()

    def z_wait(i):
        z_copy(i, 1).wait_recv()

        @pl.when(z > 0)
        def _():
            z_copy(i, 0).wait_recv()

        @pl.when(z < lines - 1)
        def _():
            z_copy(i, 2).wait_recv()

    def z_drain(i):
        z_copy(i, 1).wait_send()

        @pl.when(z < lines - 1)
        def _():
            z_copy(i, 0).wait_send()

        @pl.when(z > 0)
        def _():
            z_copy(i, 2).wait_send()

        @pl.when(jnp.logical_not(inner))
        def _():
            z_give(i).wait_send()

    def e_copy(i):
        return remote(ends.at[1 - c, i], out_ref.at[i, c], e_send.at[i], e_recv.at[i], sibling)

    def e_own(i):
        return pltpu.make_async_copy(ends.at[c, i], out_ref.at[i, c], e_local.at[i])

    def finish(i, value):
        for cc in range(2):
            ends[cc, i] = value[:, cc * cols : (cc + 1) * cols]
        e_copy(i).start()
        e_own(i).start()

    def offer(i):
        x_copy(i, 0).start()
        y_copy(i, 0).start()

    def relay(i):
        x_copy(i, 0).wait_recv()
        y_copy(i, 0).wait_recv()
        if is_far(i):
            rest = pl.ds(rows, rows // 2)
            mine[i, z, y, first, lanes(1 - x)] += far_y[i - FAR, rest]
            mine[i, z, 1 - y, second, lanes(x)] += far_x[i - FAR, rest]
        else:
            for j in range(half):
                mine[i, j, y, :, lanes(1 - x)] += from_y[i, lines + j]
                mine[i, half + j, 1 - y, :, lanes(x)] += from_x[i, lines + j]
        x_copy(i, 1).start()
        y_copy(i, 1).start()

    def collect(i):
        x_copy(i, 1).wait_recv()
        y_copy(i, 1).wait_recv()
        if is_far(i):
            whole_rows = pl.ds(0, rows)
            value = mine[i, z, y, :, lanes(x)].astype(F32)
            value += far_x[i - FAR, whole_rows].astype(F32) + far_y[i - FAR, whole_rows].astype(F32)
            finish(i, value)
            return

        def add(j):
            value = mine[i, j, y, :, lanes(x)].astype(F32)
            value += from_x[i, j].astype(F32) + from_y[i, j].astype(F32)
            mine[i, j, y, :, lanes(x)] = value.astype(BF16)

        each(lines, add)
        z_start(i)

    def last(i):
        z_wait(i)
        if is_far(i):
            for yy in range(2):
                value = mine[i, z, yy].astype(F32)
                for k in range(lines - 1):
                    value += far_z[i - FAR, k, yy].astype(F32)
                mine[i, z, yy] = value.astype(BF16)
            offer(i)
            return
        value = mine[i, z, y, :, lanes(x)].astype(F32)
        for k in range(lines - 1):
            value += from_z[i, k].astype(F32)
        finish(i, value)

    def put(i, n, value):
        mine[i, :, :, :, chunk(n)] = value.astype(BF16).reshape(mine.shape[1:4] + (WIDTH,))

    def plain_unit(i, left, right):
        for n in range(CHUNKS):
            put(i, n, dot(lefts[left], rights[right, :, chunk(n)]))

    def conv_unit(i, left, tap):
        where, side = lines_from(2 - tap // 3), 2 - tap % 3
        for n in range(CHUNKS):
            both = jnp.concatenate([grads[side, core, where, chunk(n)] for core in range(2)], axis=0)
            put(i, n, dot(lefts[left], both))

    def extra_b():
        @pl.when(c == 1)
        def _():
            conv_unit(4, 2, 8)

    def extra_a():
        @pl.when(c == 0)
        def _():
            conv_unit(4, 3, 8)

    def spread_sides(core):
        def by_line(yy):
            value = grads[1, core, pl.ds(pl.multiple_of((yy + 1) * LINE, LINE), LINE)].astype(F32)
            left, right = shifted(value)
            spot_rows = pl.ds(pl.multiple_of((yy + 1) * LINE, LINE), LINE)
            grads[0, core, spot_rows] = left.astype(BF16)
            grads[2, core, spot_rows] = right.astype(BF16)

        each(RES, by_line)

    def load(tap, base):
        unit = base + tap - 9 * (tap // 8) * (base // 10)
        return pltpu.make_async_copy(
            whole_ref.at[unit // 2, unit % 2], weights.at[tap % 2], load_sem.at[tap % 2]
        )

    def conv_back(tap, base):
        load(tap, base).wait()

        @pl.when(tap < 8)
        def _():
            load(tap + 1, base).start()

        part = grads[2 - tap % 3, c, lines_from(2 - tap // 3)]
        for n in range(CHUNKS):
            value = dot_nt(part, weight_rows(weights.at[tap % 2], n))
            total[:, :, :, chunk(n)] += value.reshape(RES, SLOTS, RES, WIDTH)

    def conv_back_range(first, stop, base):
        def body(tap, carry):
            conv_back(tap, base)
            return carry

        lax.fori_loop(first, stop, body, 0)

    def slope(values):
        sigma = jax.nn.sigmoid(values)
        return sigma * (1.0 + values * (1.0 - sigma))

    for k in (0, 2):
        from_z[:, k] = jnp.zeros_like(from_z[:, k])
        far_z[:, k] = jnp.zeros_like(far_z[:, k])
    greet(column + heads)
    for k in range(7):
        op_own(k).start()
        op_copy(k).start()
    load(0, 10).start()

    def fetch(k):
        source, target = (
            (conv_ref, board),
            (slopes_ref.at[1], slopes),
            (slopes_ref.at[0], slopes),
            (grad_resid_ref, board),
        )[k]
        return pltpu.make_async_copy(source, target, in_sem.at[k])

    fetch(0).start()
    fetch(1).start()
    vs_mine[...] = jnp.zeros_like(vs_mine)
    edge = jnp.zeros((LINE, C), BF16)
    for j in range(3):
        for core in range(2):
            grads[j, core, 0:LINE] = edge
            grads[j, core, ALL + LINE : ALL + 2 * LINE] = edge
    total[...] = jnp.zeros_like(total)
    sums_ref[...] = sums_in[...]

    def norm_b_value(n):
        return (board[:, n].reshape(PIX, C) - stats_ref[2, row(n)]) * stats_ref[3, row(n)]

    def norm_a_value(n):
        return (images_ref[span(n, PIX)].astype(F32) - stats_ref[0, row(n)]) * stats_ref[1, row(n)]

    def back_sums(get):
        def body(n):
            grad = (total[:, n] * slopes[:, n]).reshape(PIX, C)
            total[:, n] = grad.reshape(RES, RES, C)
            pair_ref[row(n)] = sum_rows(grad * get(n))
            pair_ref[row(SLOTS + n)] = sum_rows(grad)

        each(SLOTS, body)

    def back_factors(factor, inverse):
        coef_ref[0:SLOTS] = factor * inverse
        means = group_mean(pair_ref[...] * jnp.concatenate([factor, factor], axis=0))
        coef_ref[SLOTS : 2 * SLOTS] = means[:SLOTS] * inverse
        coef_ref[2 * SLOTS :] = means[SLOTS:] * inverse

    def back_value(n, get):
        value = total[:, n].reshape(PIX, C) * coef_ref[row(n)]
        return value - get(n) * coef_ref[row(SLOTS + n)] - coef_ref[row(2 * SLOTS + n)]

    def gm_copy(k):
        return remote(gm_mine, gm_all.at[d], gm_send.at[k], gm_recv.at[k], column[k])

    def mw_copy(k):
        return remote(
            mw_mine.at[lax.rem(h + k + 1, n_head)], mw_got.at[k], mw_send.at[k], mw_recv.at[k], heads[k]
        )

    def ge_copy(k):
        return remote(ge_all.at[h], ge_all.at[h], ge_send.at[k], ge_recv.at[k], heads[k])

    def vs_copy(k):
        return remote(
            vs_mine.at[lax.rem(h + k + 1, n_head)], vs_got.at[k], vs_send.at[k], vs_recv.at[k], heads[k]
        )

    def vt_copy(k):
        return remote(vt_mine, vt_all.at[d], vt_send.at[k], vt_recv.at[k], column[k])

    def image_copy():
        return pltpu.make_async_copy(image_mine, image_ref, out_sem)

    count = n_dp * SLOTS

    def start():
        op_wait(0)
        op_wait(1)

    def dw(i):
        if i == 10:
            plain_unit(10, 1, 0)
        elif i == 9:
            op_wait(2)
            op_wait(3)
            plain_unit(9, 0, 1)
        elif i > 4:
            conv_unit(i, 2, 2 * (i - 5) + c)
        else:
            conv_unit(i, 3, 2 * i + c)

    def sides():
        op_wait(4)
        op_wait(5)
        spread_sides(0)
        spread_sides(1)

    def back_b_first():
        load(0, 0).start()
        fetch(0).wait()
        fetch(1).wait()
        back_sums(norm_b_value)
        alone, with_norm = pair_ref[SLOTS:], pair_ref[:SLOTS]
        scale = mod_ref[0:SLOTS] + 1.0
        gm_mine[...] = jnp.concatenate([vecs_ref[3:4] * with_norm + vecs_ref[4:5] * alone, alone], axis=0).astype(BF16)
        gm_all[d] = gm_mine[...]
        for k in range(n_dp - 1):
            gm_copy(k).start()
        sums_ref[3:4] = sum_rows(with_norm * scale)
        sums_ref[4:5] = sum_rows(alone * scale)
        back_factors(scale * vecs_ref[3:4], stats_ref[3])

    def back_b_second():
        fetch(2).start()

        def body(n):
            value = back_value(n, norm_b_value).astype(BF16).astype(F32)
            sums_ref[2:3] += sum_rows(value)
            total[:, n] = value.reshape(RES, RES, C)

        each(SLOTS, body)
        fetch(3).start()

    def lower():
        def by_line(yy):
            spot_rows = pl.ds(pl.multiple_of((yy + 1) * LINE, LINE), LINE)
            grads[1, c, spot_rows] = total[yy].reshape(LINE, C).astype(BF16)

        each(RES, by_line)
        stage_copy().start()
        spread_sides(c)
        total[...] = jnp.zeros_like(total)

    def take():
        stage_copy().wait_recv()

        def by_line(yy):
            spot_rows = pl.ds(pl.multiple_of((yy + 1) * LINE, LINE), LINE)
            grads[1, 1 - c, spot_rows] = stage[span(yy, LINE)]

        each(RES, by_line)
        spread_sides(1 - c)
        op_wait(6)

    def modulation():
        for k in range(n_dp - 1):
            gm_copy(k).wait()
        parts = gm_all[...].astype(F32)
        gm_scale = parts[:, :SLOTS].reshape(count, C)
        gm_offset = parts[:, SLOTS:].reshape(count, C)
        pre = pre_ref[...]
        emb = silu(pre).astype(BF16)
        part_rows = rows // n_head
        for k, value in ((0, gm_scale), (1, gm_offset)):
            low_value = value.astype(BF16)
            grad_w = dot_tn(emb, low_value)
            place_lanes = slice(k * C, (k + 1) * C)
            for hh in range(n_head):
                mw_mine[hh, 0:part_rows, place_lanes] = grad_w[hh * part_rows : (hh + 1) * part_rows]
                mw_mine[hh, part_rows : part_rows + 8, place_lanes] = jnp.broadcast_to(sum_rows(value), (8, C))
        grad_e = dot_nt(gm_scale.astype(BF16), modw_ref[:, :C]) + dot_nt(gm_offset.astype(BF16), modw_ref[:, C:])
        grad_e = grad_e * slope(pre)
        label = ids_ref[...].reshape(count, 128)[:, 0:1].astype(F32)
        lane = lax.broadcasted_iota(jnp.int32, grad_e.shape, 1)
        ge_all[h] = jnp.where(lane < rows, grad_e, label)
        for k in range(n_head - 1):
            mw_copy(k).start()
            ge_copy(k).start()

    def back_a_first():
        fetch(2).wait()
        back_sums(norm_a_value)
        sums_ref[0:1] = sum_rows(pair_ref[:SLOTS])
        sums_ref[1:2] = sum_rows(pair_ref[SLOTS:])
        for hh in range(n_head):
            vs_mine[hh] = sums_ref[:, hh * cols : (hh + 1) * cols]
        for k in range(n_head - 1):
            vs_copy(k).start()
        back_factors(jnp.broadcast_to(vecs_ref[0:1], (SLOTS, C)), stats_ref[1])

    def back_a_second():
        fetch(3).wait()

        def body(n):
            image_mine[span(n, PIX)] = back_value(n, norm_a_value) + board[:, n].reshape(PIX, C)

        each(SLOTS, body)
        image_copy().start()

    def vec_first():
        value = vs_mine[h]
        for k in range(n_head - 1):
            vs_copy(k).wait()
            value += vs_got[k]
        vt_mine[...] = value
        vt_all[d] = value
        for k in range(n_dp - 1):
            vt_copy(k).start()

    def mod_out():
        value = mw_mine[h]
        for k in range(n_head - 1):
            mw_copy(k).wait()
            value += mw_got[k]
        modw_out[...] = value

    def class_out():
        for k in range(n_head - 1):
            ge_copy(k).wait()
        table = class_ref.shape[0]
        value = ge_all[...].reshape(n_head * count, 128)
        label = value.T[rows : rows + 1].astype(jnp.int32)
        hot = lax.broadcasted_iota(jnp.int32, (table, n_head * count), 0) == label
        class_ref[...] = dot(jnp.where(hot, 1.0, 0.0).astype(BF16), value.astype(BF16))

    def vec_second():
        for k in range(n_dp - 1):
            vt_copy(k).wait()
        value = vt_all[0]
        for k in range(1, n_dp):
            value += vt_all[k]
        vec_out[...] = value

    start()
    dw(10)
    z_start(10)
    dw(9)
    z_start(9)
    sides()
    dw(5)
    offer(5)
    dw(6)
    offer(6)
    dw(7)
    z_mix(10)
    offer(7)
    dw(8)
    relay(5)
    offer(8)
    extra_b()
    conv_back_range(0, 3, 10)
    relay(6)
    conv_back_range(3, 6, 10)
    relay(7)
    conv_back_range(6, 9, 10)
    collect(5)
    back_b_first()
    relay(8)
    z_mix(9)
    back_b_second()
    lower()
    conv_back_range(0, 3, 0)
    collect(6)
    take()
    extra_a()
    offer(4)
    collect(7)
    dw(0)
    z_mix(5)
    offer(0)
    dw(1)
    offer(1)
    dw(2)
    offer(2)
    dw(3)
    z_mix(6)
    collect(8)
    offer(3)
    conv_back_range(3, 6, 0)
    last(10)
    relay(4)
    relay(0)
    z_mix(7)
    conv_back_range(6, 9, 0)
    last(9)
    relay(1)
    relay(2)
    z_mix(8)
    back_a_first()
    relay(3)
    relay(10)
    modulation()
    last(5)
    back_a_second()
    collect(4)
    last(6)
    vec_first()
    z_mix(4)
    mod_out()
    last(7)
    class_out()
    last(8)
    vec_second()
    collect(0)
    relay(9)
    z_mix(0)
    last(4)
    collect(1)
    z_mix(1)
    last(0)
    collect(2)
    last(1)
    z_mix(2)
    collect(3)
    collect(10)
    last(2)
    collect(9)
    z_mix(3)
    last(3)

    for k in range(7):
        op_copy(k).wait_send()
    stage_copy().wait_send()
    image_copy().wait()

    def drain(i):
        for part in range(2):
            x_copy(i, part).wait_send()
            y_copy(i, part).wait_send()
        z_drain(i)
        e_own(i).wait()
        e_copy(i).wait()

    each(FAR, drain)
    drain(9)
    drain(10)


def run_backward(whole, turned, right, grad_low, grad_resid, conv_out, slopes, images, stats, vecs, mod, sums, pre, ids, modw):
    n_dp, n_head = lax.axis_size("dp"), lax.axis_size("head")
    _, _, lines, _, rows, depth = whole.shape
    cols = depth // n_head
    wide = 2 * cols
    board = (RES, SLOTS, RES, C)
    shape = jax.ShapeDtypeStruct
    return pl.pallas_call(
        functools.partial(backward_kernel, lines),
        out_shape=(
            shape((PAIRS, 2, rows, cols), F32),
            shape((ALL, C), F32),
            shape((1024, 128), F32),
            shape((rows // n_head + 8, 2 * C), F32),
            shape((16, cols), F32),
        ),
        in_specs=[ANY] * 7 + [VMEM] * 8,
        out_specs=(ANY, ANY) + (VMEM,) * 3,
        scratch_shapes=[
            pltpu.VMEM((PAIRS, lines, 2, rows, depth), BF16),
            pltpu.VMEM((FAR, lines + lines // 2, rows, wide), BF16),
            pltpu.VMEM((FAR, lines + lines // 2, rows, wide), BF16),
            pltpu.VMEM((FAR, 4, rows, wide), BF16),
            pltpu.VMEM((PAIRS - FAR, rows + rows // 2, wide), BF16),
            pltpu.VMEM((PAIRS - FAR, rows + rows // 2, wide), BF16),
            pltpu.VMEM((PAIRS - FAR, 4, 2, rows, depth), BF16),
            pltpu.VMEM((2, PAIRS, rows, cols), F32),
            pltpu.VMEM((4, C, 2 * ALL), BF16),
            pltpu.VMEM((2, 2 * ALL, C), BF16),
            pltpu.VMEM((3, 2, ALL + 2 * LINE, C), BF16),
            pltpu.VMEM((ALL, C), BF16),
            pltpu.VMEM((2, lines, 2, rows, depth), BF16),
            pltpu.VMEM(board, F32),
            pltpu.VMEM(board, F32),
            pltpu.VMEM(board, F32),
            pltpu.VMEM((ALL, C), F32),
            pltpu.VMEM((16, C), F32),
            pltpu.VMEM((2 * SLOTS, C), F32),
            pltpu.VMEM((3 * SLOTS, C), F32),
            pltpu.VMEM((2 * SLOTS, C), BF16),
            pltpu.VMEM((n_dp, 2 * SLOTS, C), BF16),
            pltpu.VMEM((n_head, rows // n_head + 8, 2 * C), F32),
            pltpu.VMEM((n_head - 1, rows // n_head + 8, 2 * C), F32),
            pltpu.VMEM((n_head, n_dp * SLOTS, 128), F32),
            pltpu.VMEM((n_head, 16, cols), F32),
            pltpu.VMEM((n_head - 1, 16, cols), F32),
            pltpu.VMEM((16, cols), F32),
            pltpu.VMEM((n_dp, 16, cols), F32),
            DMA((PAIRS, 2)),
            DMA((PAIRS, 2)),
            DMA((PAIRS, 2)),
            DMA((PAIRS, 2)),
            DMA((PAIRS, lines - 1)),
            DMA((PAIRS, lines - 1)),
            DMA((PAIRS,)),
            DMA((PAIRS,)),
            DMA((PAIRS,)),
            DMA((PAIRS,)),
            DMA((PAIRS,)),
            DMA((8,)),
            DMA((8,)),
            DMA((7,)),
            DMA((2,)),
            DMA((4,)),
            DMA,
            DMA((n_dp - 1,)),
            DMA((n_dp - 1,)),
            DMA((n_head - 1,)),
            DMA((n_head - 1,)),
            DMA((n_head - 1,)),
            DMA((n_head - 1,)),
            DMA((n_head - 1,)),
            DMA((n_head - 1,)),
            DMA((n_dp - 1,)),
            DMA((n_dp - 1,)),
        ],
        compiler_params=pltpu.CompilerParams(
            collective_id=1, has_side_effects=True, vmem_limit_bytes=64 * 2**20 - 2**18
        ),
        name="backward_scatter",
    )(whole, turned, right, grad_low, grad_resid, conv_out, slopes, images, stats, vecs, mod, sums, pre, ids, modw)


def direct(rows, cols):
    n_dp, n_head = lax.axis_size("dp"), lax.axis_size("head")
    return n_head == 4 and n_dp == 8 and rows % 32 == 0 and cols % 64 == 0


def fast_shards(
    images,
    cotangent,
    counts,
    labels,
    levels,
    noise_table,
    class_table,
    gain_a,
    shift_a,
    conv_a,
    bias_a,
    mod_weight,
    mod_bias,
    gain_b,
    shift_b,
    conv_b,
    bias_b,
    gain_c,
    shift_c,
    qkv_weight,
    proj_weight,
    proj_bias,
):
    n_head = lax.axis_size("head")
    d, h = lax.axis_index("dp"), lax.axis_index("head")
    rows = class_table.shape[1]
    taps = jnp.concatenate(
        [
            jnp.swapaxes(conv_a, 0, 1),
            jnp.swapaxes(conv_b[:, 8:9], 0, 1),
            jnp.swapaxes(conv_b[:, 0:8], 0, 1),
            jnp.swapaxes(qkv_weight, 0, 1),
            proj_weight[None],
        ],
        axis=0,
    )
    vec = jnp.stack([gain_a, shift_a, bias_a, gain_b, shift_b, bias_b, gain_c, shift_c, proj_bias])
    vec = jnp.pad(vec, ((0, 7), (0, 0)))
    ids = jnp.pad(jnp.stack([labels, levels], axis=1), ((0, 0), (0, 126)))
    class_rows = jnp.pad(class_table, ((0, 1024 - class_table.shape[0]), (0, 128 - rows)))
    noise_rows = lax.dynamic_slice_in_dim(noise_table, d * rows, rows, axis=1)
    noise_rows = jnp.pad(noise_rows, ((0, 128 - noise_rows.shape[0]), (0, 128 - rows)))
    mod_rows = jnp.pad(mod_weight.reshape(rows, 2 * C), ((0, 128 - rows), (0, 0)))
    bias_rows = jnp.repeat(mod_bias.astype(F32), SLOTS, axis=0)
    live = live_rows(counts, d * n_head + h, 1, SLOTS)
    live = jnp.broadcast_to(live[:, None], (SLOTS, C))
    flat = images.reshape(ALL, C)
    (
        whole,
        conv_out,
        slopes,
        turned,
        block_out,
        grad_resid,
        grad_low,
        right,
        vecs,
        mod,
        stats,
        pre,
        all_ids,
        sums,
    ) = run_forward(
        taps, vec, flat, cotangent.reshape(ALL, C), live, ids, class_rows, noise_rows, mod_rows, bias_rows
    )
    out, image_grad, classes, modw, vectors = run_backward(
        whole,
        turned,
        right,
        grad_low,
        grad_resid,
        conv_out,
        slopes,
        flat,
        stats,
        vecs,
        mod,
        sums,
        pre,
        all_ids,
        mod_rows,
    )
    out = out.reshape((UNITS,) + out.shape[2:])
    part = rows // n_head
    class_grad = lax.dynamic_slice(classes, (0, h * part), (class_table.shape[0], part))
    modb = modw[part].reshape(2, C)
    modb_grad = lax.dynamic_slice_in_dim(modb, (d * n_head + h) * part, part, axis=1)
    return (
        block_out.reshape(images.shape),
        image_grad.reshape(images.shape),
        class_grad,
        vectors[0],
        vectors[1],
        jnp.swapaxes(out[0:9], 0, 1),
        vectors[2],
        modw[:part].reshape(part, 2, C),
        modb_grad,
        vectors[3],
        vectors[4],
        jnp.swapaxes(jnp.concatenate([out[10:18], out[9:10]], axis=0), 0, 1),
        vectors[5],
        vectors[6],
        vectors[7],
        jnp.swapaxes(out[18:21], 0, 1),
        out[21],
        vectors[8],
    )


def shards(*args):
    rows, _, cols = args[9].shape
    if direct(rows, cols):
        return fast_shards(*args)
    return plain_shards(*args)


def solution(mesh):
    placed = (
        P(("dp", "head"), None, None, None),
        P(("dp", "head"), None, None, None),
        P(),
        P(("dp", "head")),
        P(("dp", "head")),
        P(),
        P(None, "dp"),
        P("head"),
        P("head"),
        P("dp", None, "head"),
        P("head"),
        P("dp", None, None),
        P(),
        P("head"),
        P("head"),
        P("dp", None, "head"),
        P("head"),
        P("head"),
        P("head"),
        P("dp", None, "head"),
        P("dp", "head"),
        P("head"),
    )
    return jax.shard_map(
        shards,
        mesh=mesh,
        in_specs=placed,
        out_specs=(
            P(("dp", "head"), None, None, None),
            P(("dp", "head"), None, None, None),
            P(None, ("dp", "head")),
            P("head"),
            P("head"),
            P("dp", None, "head"),
            P("head"),
            P(("dp", "head"), None, None),
            P(None, ("dp", "head")),
            P("head"),
            P("head"),
            P("dp", None, "head"),
            P("head"),
            P("head"),
            P("head"),
            P("dp", None, "head"),
            P("dp", "head"),
            P("head"),
        ),
        check_vma=False,
    )
```

```python
import functools

import jax
import jax.numpy as jnp
from jax import lax
from jax.experimental import pallas as pl
from jax.experimental.pallas import tpu as pltpu
from jax.sharding import PartitionSpec as P

C = 768
DH = 64
GROUPS = 32


EPSILON = 1e-05
HIGHEST = lax.Precision.HIGHEST


def norm_forward(values, gain, shift):
    count, chans = (values.shape[0], values.shape[-1])
    span = C // GROUPS
    grouped = values.reshape(count, -1, chans // span, span)
    mean = jnp.mean(grouped, axis=(1, 3), keepdims=True)
    centred = grouped - mean
    inverse = lax.rsqrt(jnp.mean(centred * centred, axis=(1, 3), keepdims=True) + EPSILON)
    normed = (centred * inverse).reshape(values.shape)
    return (normed * gain + shift, normed, inverse)


def norm_backward(grad_out, normed, inverse, gain):
    grad_gain = jnp.sum(grad_out * normed, axis=(0, 1, 2))
    grad_shift = jnp.sum(grad_out, axis=(0, 1, 2))
    count, chans = (grad_out.shape[0], grad_out.shape[-1])
    span = C // GROUPS
    layout = (count, -1, chans // span, span)
    grad_normed = (grad_out * gain).reshape(layout)
    normed_groups = normed.reshape(layout)
    mean_one = jnp.mean(grad_normed, axis=(1, 3), keepdims=True)
    mean_two = jnp.mean(grad_normed * normed_groups, axis=(1, 3), keepdims=True)
    grad_in = inverse * (grad_normed - mean_one - normed_groups * mean_two)
    return (grad_in.reshape(grad_out.shape), grad_gain, grad_shift)


def silu_slope(values):
    sigma = jax.nn.sigmoid(values)
    return sigma * (1.0 + values * (1.0 - sigma))


def patches_of(act):
    count, rows, cols, chans = act.shape
    padded = jnp.pad(act, ((0, 0), (1, 1), (1, 1), (0, 0)))
    taps = [padded[:, i : i + rows, j : j + cols, :] for i in range(3) for j in range(3)]
    return jnp.stack(taps, axis=3).reshape(count * rows * cols, 9, chans)


def contract_rows(left, right):
    return lax.dot_general(
        left, right, (((0,), (0,)), ((), ())), preferred_element_type=jnp.float32
    )


def contract_cols(left, right):
    return lax.dot_general(
        left, right, (((1,), (1,)), ((), ())), preferred_element_type=jnp.float32
    )


def conv_back(grad_low, weight, count, rows, cols):
    chans = weight.shape[0]
    padded = jnp.zeros((count, rows + 2, cols + 2, chans), jnp.float32)
    for tap in range(9):
        i, j = divmod(tap, 3)
        part = contract_cols(grad_low, weight[:, tap, :]).reshape(count, rows, cols, chans)
        padded = padded.at[:, i : i + rows, j : j + cols, :].add(part)
    return padded[:, 1 : rows + 1, 1 : cols + 1, :]


def keep_same(values):
    return values


def live_rows(counts, first, number, count):
    sums = jnp.sum(counts, axis=1)
    chosen = lax.dynamic_slice_in_dim(sums, first, number)
    slots = lax.iota(jnp.int32, count)
    return (slots[None, :] < chosen[:, None]).astype(jnp.float32).reshape(number * count)


def residual_forward(source, mod_pair, weights, spread):
    (
        conv_one,
        conv_two,
        gain_one,
        shift_one,
        bias_one,
        gain_two,
        shift_two,
        bias_two,
        gain_three,
        shift_three,
    ) = weights
    out_a, normed_a, inverse_a = norm_forward(source, gain_one, shift_one)
    wide_a = spread(jax.nn.silu(out_a).astype(jnp.bfloat16))
    conv_out_a = (
        jnp.einsum("ptc,cto->po", patches_of(wide_a), conv_one, preferred_element_type=jnp.float32)
        + bias_one
    ).reshape(source.shape)
    scale = mod_pair[:, :, 0:1, :]
    offset = mod_pair[:, :, 1:2, :]
    out_b, normed_b, inverse_b = norm_forward(conv_out_a, gain_two, shift_two)
    inner_b = offset + out_b * (scale + 1.0)
    wide_b = spread(jax.nn.silu(inner_b).astype(jnp.bfloat16))
    conv_out_b = (
        jnp.einsum("ptc,cto->po", patches_of(wide_b), conv_two, preferred_element_type=jnp.float32)
        + bias_two
    ).reshape(source.shape)
    resid = source + conv_out_b
    out_c, normed_c, inverse_c = norm_forward(resid, gain_three, shift_three)
    attn_in = out_c.astype(jnp.bfloat16)
    saved = (
        out_a,
        normed_a,
        inverse_a,
        wide_a,
        out_b,
        normed_b,
        inverse_b,
        inner_b,
        wide_b,
        normed_c,
        inverse_c,
        scale,
    )
    return (resid, attn_in, saved)


def residual_backward(grad_attn, grad_out, saved, weights, reduce_value):
    conv_one, conv_two, gain_one, gain_two, gain_three = (
        weights[0],
        weights[1],
        weights[2],
        weights[5],
        weights[8],
    )
    (
        out_a,
        normed_a,
        inverse_a,
        wide_a,
        out_b,
        normed_b,
        inverse_b,
        inner_b,
        wide_b,
        normed_c,
        inverse_c,
        scale,
    ) = saved
    count, rows, cols, local = grad_out.shape
    grad_resid_c, gainc_term, shiftc_term = norm_backward(
        grad_attn, normed_c, inverse_c, gain_three
    )
    grad_resid = grad_out + grad_resid_c
    grad_conv_b = grad_resid.reshape(-1, local).astype(jnp.bfloat16)
    biasb_term = jnp.sum(grad_conv_b.astype(jnp.float32), axis=0)
    convb_term = jnp.einsum(
        "ptc,po->cto", patches_of(wide_b), grad_conv_b, preferred_element_type=jnp.float32
    )
    grad_act_b = reduce_value(conv_back(grad_conv_b, conv_two, count, rows, cols))
    grad_inner = grad_act_b * silu_slope(inner_b)
    grad_offset = jnp.sum(grad_inner, axis=(1, 2))
    grad_scale = jnp.sum(grad_inner * out_b, axis=(1, 2))
    grad_mod = jnp.stack([grad_scale, grad_offset], axis=1)[:, None]
    grad_conv_full, gainb_term, shiftb_term = norm_backward(
        grad_inner * (scale + 1.0), normed_b, inverse_b, gain_two
    )
    grad_conv_a = grad_conv_full.reshape(-1, local).astype(jnp.bfloat16)
    biasa_term = jnp.sum(grad_conv_a.astype(jnp.float32), axis=0)
    conva_term = jnp.einsum(
        "ptc,po->cto", patches_of(wide_a), grad_conv_a, preferred_element_type=jnp.float32
    )
    grad_act_a = reduce_value(conv_back(grad_conv_a, conv_one, count, rows, cols))
    grad_source, gaina_term, shifta_term = norm_backward(
        grad_act_a * silu_slope(out_a), normed_a, inverse_a, gain_one
    )
    image_grad = grad_resid + grad_source
    vectors = (
        gaina_term,
        shifta_term,
        biasa_term,
        gainb_term,
        shiftb_term,
        biasb_term,
        gainc_term,
        shiftc_term,
    )
    return (image_grad, grad_mod, (conva_term, convb_term), vectors)


def attend_forward(block):
    query, key, value = (block[:, :, 0], block[:, :, 1], block[:, :, 2])
    batch, pixels, heads_here, depth = query.shape
    scores = jnp.einsum("bqhd,bkhd->bhqk", query, key, preferred_element_type=jnp.float32) * DH ** (
        -0.5
    )
    top = jnp.max(scores, axis=-1, keepdims=True)
    weights = jnp.exp(scores - top)
    sums = jnp.sum(weights, axis=-1, keepdims=True)
    probs = (weights / sums).astype(jnp.bfloat16)
    logsum = (top + jnp.log(sums))[..., 0]
    mixed = jnp.einsum("bhqk,bkhd->bqhd", probs, value, preferred_element_type=jnp.float32).astype(
        jnp.bfloat16
    )
    return (mixed.reshape(batch, pixels, heads_here * depth), logsum)


def attend_backward(block, logsum, grad_head):
    query, key, value = (block[:, :, 0], block[:, :, 1], block[:, :, 2])
    batch, pixels, heads_here, depth = query.shape
    factor = DH ** (-0.5)
    scores = jnp.einsum("bqhd,bkhd->bhqk", query, key, preferred_element_type=jnp.float32) * factor
    probs = jnp.exp(scores - logsum[..., None])
    grad_value = jnp.einsum(
        "bhqk,bqhd->bkhd", probs.astype(jnp.bfloat16), grad_head, preferred_element_type=jnp.float32
    )
    grad_probs = jnp.einsum("bqhd,bkhd->bhqk", grad_head, value, preferred_element_type=jnp.float32)
    inner = jnp.sum(grad_probs * probs, axis=-1, keepdims=True)
    grad_scores = (probs * (grad_probs - inner)).astype(jnp.bfloat16)
    grad_query = (
        jnp.einsum("bhqk,bkhd->bqhd", grad_scores, key, preferred_element_type=jnp.float32) * factor
    )
    grad_key = (
        jnp.einsum("bhqk,bqhd->bkhd", grad_scores, query, preferred_element_type=jnp.float32)
        * factor
    )
    stacked = jnp.stack([grad_query, grad_key, grad_value], axis=2).astype(jnp.bfloat16)
    return stacked.reshape(batch, pixels, 3, heads_here * depth)


def plain_shards(
    images,
    cotangent,
    counts,
    labels,
    levels,
    noise_table,
    class_table,
    gain_a,
    shift_a,
    conv_a,
    bias_a,
    mod_weight,
    mod_bias,
    gain_b,
    shift_b,
    conv_b,
    bias_b,
    gain_c,
    shift_c,
    qkv_weight,
    proj_weight,
    proj_bias,
):
    rows_a, rows_b, rows_qkv, rows_proj, mod_full, class_full = (
        lax.all_gather(conv_a, "dp", axis=0, tiled=True),
        lax.all_gather(conv_b, "dp", axis=0, tiled=True),
        lax.all_gather(qkv_weight, "dp", axis=0, tiled=True),
        lax.all_gather(proj_weight, "dp", axis=0, tiled=True),
        lax.all_gather(mod_weight, "dp", axis=0, tiled=True),
        lax.all_gather(class_table, "dp", axis=1, tiled=True),
    )
    count, rows, cols, channels = images.shape
    pixels = rows * cols
    groups_n = lax.axis_size("head")
    quarter = channels // groups_n
    heads_local = quarter // DH
    first_dp = lax.axis_index("dp") * groups_n
    class_hot = (labels[:, None] == lax.iota(jnp.int32, class_full.shape[0])[None, :]).astype(
        jnp.bfloat16
    )
    level_hot = (levels[:, None] == lax.iota(jnp.int32, noise_table.shape[0])[None, :]).astype(
        jnp.bfloat16
    )
    embed_pre = jnp.dot(class_hot, class_full, preferred_element_type=jnp.float32) + jnp.dot(
        level_hot, noise_table, preferred_element_type=jnp.float32
    )
    embed = jax.nn.silu(embed_pre).astype(jnp.bfloat16)
    modulation = (
        jnp.einsum("ne,etc->ntc", embed, mod_full, preferred_element_type=jnp.float32)
        + mod_bias.astype(jnp.float32)
    ).astype(jnp.bfloat16)
    mod_pair = modulation.reshape(count, 1, 2, channels)
    (
        conv_one,
        conv_two,
        qkv_full,
        proj_full,
        gain_one,
        shift_one,
        bias_one,
        gain_two,
        shift_two,
        bias_two,
        gain_three,
        shift_three,
        bias_three,
    ) = (
        lax.all_gather(rows_a, "head", axis=2, tiled=True),
        lax.all_gather(rows_b, "head", axis=2, tiled=True),
        lax.all_gather(rows_qkv, "head", axis=2, tiled=True),
        lax.all_gather(rows_proj, "head", axis=1, tiled=True),
        lax.all_gather(gain_a, "head", axis=0, tiled=True),
        lax.all_gather(shift_a, "head", axis=0, tiled=True),
        lax.all_gather(bias_a, "head", axis=0, tiled=True),
        lax.all_gather(gain_b, "head", axis=0, tiled=True),
        lax.all_gather(shift_b, "head", axis=0, tiled=True),
        lax.all_gather(bias_b, "head", axis=0, tiled=True),
        lax.all_gather(gain_c, "head", axis=0, tiled=True),
        lax.all_gather(shift_c, "head", axis=0, tiled=True),
        lax.all_gather(proj_bias, "head", axis=0, tiled=True),
    )
    weights = (
        conv_one,
        conv_two,
        gain_one,
        shift_one,
        bias_one,
        gain_two,
        shift_two,
        bias_two,
        gain_three,
        shift_three,
    )
    live = live_rows(counts, first_dp + lax.axis_index("head"), 1, count)
    total = count * pixels
    width = channels // groups_n
    source = images.astype(jnp.float32)
    resid, attn_in, saved = residual_forward(
        source, mod_pair.astype(jnp.float32), weights, keep_same
    )
    attn_flat = attn_in.reshape(total, channels)
    qkv_flat = qkv_full.reshape(channels, 3 * channels)
    qkv = jnp.dot(attn_flat, qkv_flat, preferred_element_type=jnp.float32).astype(jnp.bfloat16)
    packed = qkv.reshape(1, count, pixels, 3, groups_n, width)
    block = lax.all_to_all(packed, "head", split_axis=4, concat_axis=0, tiled=True)
    groups = block.shape[0]
    items = block.shape[1]
    flat = block.reshape(groups * items, pixels, 3, heads_local, DH)
    mixed, logsum = attend_forward(flat)
    mixed = mixed.reshape(groups, items, pixels, 1, width)
    returned = lax.all_to_all(mixed, "head", split_axis=0, concat_axis=3, tiled=True)
    returned, logsum, kept = (returned, logsum.reshape(groups, items, heads_local, pixels), block)
    mixed_image = returned.reshape(total, channels)
    result = (
        resid.reshape(total, channels)
        + jnp.dot(mixed_image, proj_full, preferred_element_type=jnp.float32)
        + bias_three
    )
    block_out = (result.reshape(images.shape) * live[:, None, None, None]).astype(jnp.bfloat16)
    grad_out = cotangent.astype(jnp.float32) * live[:, None, None, None]
    grad_flat = grad_out.reshape(total, channels)
    grad_low = grad_flat.astype(jnp.bfloat16)
    projw_full = contract_rows(mixed_image, grad_low)
    projb_full = jnp.sum(grad_flat, axis=0)
    grad_mixed = contract_cols(grad_low, proj_full).astype(jnp.bfloat16)
    arrived = lax.all_to_all(
        grad_mixed.reshape(1, count, pixels, groups_n, width),
        "head",
        split_axis=3,
        concat_axis=0,
        tiled=True,
    )
    flat_block = kept.reshape(groups_n * count, pixels, 3, heads_local, DH)
    grad_head = arrived.reshape(groups_n * count, pixels, heads_local, DH)
    stacked = attend_backward(
        flat_block, logsum.reshape(groups_n * count, heads_local, pixels), grad_head
    )
    stacked = stacked.reshape(groups_n, count, pixels, 3, 1, width)
    grad_qkv = lax.all_to_all(stacked, "head", split_axis=0, concat_axis=4, tiled=True).reshape(
        total, 3 * channels
    )
    qkvw_full = contract_rows(attn_flat, grad_qkv).reshape(channels, 3, channels)
    grad_attn = contract_cols(grad_qkv, qkv_flat).reshape(images.shape)
    image_grad, grad_mod_part, conv_terms, vectors = residual_backward(
        grad_attn, grad_out, saved, weights, keep_same
    )
    (
        gaina_full,
        shifta_full,
        biasa_full,
        gainb_full,
        shiftb_full,
        biasb_full,
        gainc_full,
        shiftc_full,
    ) = vectors
    (
        conva_term,
        convb_term,
        qkvw_term,
        projw_term,
        gaina_term,
        shifta_term,
        biasa_term,
        gainb_term,
        shiftb_term,
        biasb_term,
        gainc_term,
        shiftc_term,
        projb_term,
    ) = (
        lax.psum_scatter(
            conv_terms[0].astype(jnp.bfloat16), "head", scatter_dimension=2, tiled=True
        ).astype(jnp.float32),
        lax.psum_scatter(
            conv_terms[1].astype(jnp.bfloat16), "head", scatter_dimension=2, tiled=True
        ).astype(jnp.float32),
        lax.psum_scatter(
            qkvw_full.astype(jnp.bfloat16), "head", scatter_dimension=2, tiled=True
        ).astype(jnp.float32),
        lax.psum_scatter(
            projw_full.astype(jnp.bfloat16), "head", scatter_dimension=1, tiled=True
        ).astype(jnp.float32),
        lax.psum_scatter(
            gaina_full.astype(jnp.bfloat16), "head", scatter_dimension=0, tiled=True
        ).astype(jnp.float32),
        lax.psum_scatter(
            shifta_full.astype(jnp.bfloat16), "head", scatter_dimension=0, tiled=True
        ).astype(jnp.float32),
        lax.psum_scatter(
            biasa_full.astype(jnp.bfloat16), "head", scatter_dimension=0, tiled=True
        ).astype(jnp.float32),
        lax.psum_scatter(
            gainb_full.astype(jnp.bfloat16), "head", scatter_dimension=0, tiled=True
        ).astype(jnp.float32),
        lax.psum_scatter(
            shiftb_full.astype(jnp.bfloat16), "head", scatter_dimension=0, tiled=True
        ).astype(jnp.float32),
        lax.psum_scatter(
            biasb_full.astype(jnp.bfloat16), "head", scatter_dimension=0, tiled=True
        ).astype(jnp.float32),
        lax.psum_scatter(
            gainc_full.astype(jnp.bfloat16), "head", scatter_dimension=0, tiled=True
        ).astype(jnp.float32),
        lax.psum_scatter(
            shiftc_full.astype(jnp.bfloat16), "head", scatter_dimension=0, tiled=True
        ).astype(jnp.float32),
        lax.psum_scatter(
            projb_full.astype(jnp.bfloat16), "head", scatter_dimension=0, tiled=True
        ).astype(jnp.float32),
    )
    grad_mod = grad_mod_part.reshape(count, 2, channels)
    modw_term = jnp.einsum("ne,ntc->etc", embed.astype(jnp.float32), grad_mod, precision=HIGHEST)
    modb_term = jnp.sum(grad_mod, axis=0)
    grad_embed = jnp.einsum(
        "ntc,etc->ne", grad_mod, mod_full.astype(jnp.float32), precision=HIGHEST
    ) * silu_slope(embed_pre)
    class_term = lax.dot_general(
        class_hot.astype(jnp.float32), grad_embed, (((0,), (0,)), ((), ())), precision=HIGHEST
    )
    modw_grad, class_grad, modb_grad = (
        lax.psum_scatter(modw_term, ("dp", "head"), scatter_dimension=0, tiled=True),
        lax.psum_scatter(class_term, ("dp", "head"), scatter_dimension=1, tiled=True),
        lax.psum_scatter(modb_term, ("dp", "head"), scatter_dimension=1, tiled=True),
    )
    conva_grad, convb_grad, qkvw_grad, projw_grad = (
        lax.psum_scatter(conva_term, "dp", scatter_dimension=0, tiled=True),
        lax.psum_scatter(convb_term, "dp", scatter_dimension=0, tiled=True),
        lax.psum_scatter(qkvw_term, "dp", scatter_dimension=0, tiled=True),
        lax.psum_scatter(projw_term, "dp", scatter_dimension=0, tiled=True),
    )
    (
        gaina_grad,
        shifta_grad,
        biasa_grad,
        gainb_grad,
        shiftb_grad,
        biasb_grad,
        gainc_grad,
        shiftc_grad,
        projb_grad,
    ) = lax.psum(
        (
            gaina_term,
            shifta_term,
            biasa_term,
            gainb_term,
            shiftb_term,
            biasb_term,
            gainc_term,
            shiftc_term,
            projb_term,
        ),
        "dp",
    )
    return (
        block_out,
        image_grad,
        class_grad,
        gaina_grad,
        shifta_grad,
        conva_grad,
        biasa_grad,
        modw_grad,
        modb_grad,
        gainb_grad,
        shiftb_grad,
        convb_grad,
        biasb_grad,
        gainc_grad,
        shiftc_grad,
        qkvw_grad,
        projw_grad,
        projb_grad,
    )


MESH = pl.DeviceIdType.MESH
UNITS = 22
PAIRS = UNITS // 2
FAR = 9
VECTORS = 9
RES = 8
SLOTS = 8
PIX = RES * RES
LINE = SLOTS * RES
ALL = RES * LINE
WIDTH = 256
F32 = jnp.float32
BF16 = jnp.bfloat16
ANY = pl.BlockSpec(memory_space=pl.ANY)
VMEM = pl.BlockSpec(memory_space=pltpu.VMEM)
SMEM = pl.BlockSpec(memory_space=pltpu.SMEM)
DMA = pltpu.SemaphoreType.DMA


def place():
    d, h = lax.axis_index("dp"), lax.axis_index("head")
    return d // 2, lax.rem(d, 2), h // 2, lax.rem(h, 2)


def at_chip(z, y, x, c):
    return (z * 2 + y, x * 2 + c)


def column_peers(n_dp):
    d, h = lax.axis_index("dp"), lax.axis_index("head")
    return [(lax.rem(d + k, n_dp), h) for k in range(1, n_dp)]


def head_peers(n_head):
    d, h = lax.axis_index("dp"), lax.axis_index("head")
    return [(d, lax.rem(h + k, n_head)) for k in range(1, n_head)]


def greet(devices):
    barrier = pltpu.get_barrier_semaphore()
    for device in devices:
        pl.semaphore_signal(barrier, inc=1, device_id=device, device_id_type=MESH)
    pl.semaphore_wait(barrier, len(devices))


def remote(src, dst, send, recv, device):
    return pltpu.make_async_remote_copy(
        src_ref=src, dst_ref=dst, send_sem=send, recv_sem=recv, device_id=device, device_id_type=MESH
    )


def each(count, body):
    def step(n, carry):
        body(n)
        return carry

    lax.fori_loop(0, count, step, 0)


def span(index, size):
    return pl.ds(pl.multiple_of(index * size, size), size)


def row(n):
    return pl.ds(n, 1)


def lines_from(i):
    return pl.ds(i * LINE if isinstance(i, int) else pl.multiple_of(i * LINE, LINE), ALL)


def dot(left, right):
    return jnp.dot(left, right, preferred_element_type=F32)


def dot_nt(left, right):
    return lax.dot_general(left, right, (((1,), (1,)), ((), ())), preferred_element_type=F32)


def dot_tn(left, right):
    return lax.dot_general(left, right, (((0,), (0,)), ((), ())), preferred_element_type=F32)


def in_group(first, second, axis):
    chan = lax.broadcasted_iota(jnp.int32, (first, second), axis)
    group = lax.broadcasted_iota(jnp.int32, (first, second), 1 - axis) * (C // GROUPS)
    inside = jnp.logical_and(chan >= group, chan < group + C // GROUPS)
    return jnp.where(inside, 1.0, 0.0).astype(BF16)


def pieces(values):
    high = values.astype(BF16).astype(F32)
    rest = values - high
    mid = rest.astype(BF16).astype(F32)
    return jnp.concatenate([high, mid, rest - mid], axis=0).astype(BF16)


def group_mean(sums):
    count = sums.shape[0]
    part = dot(pieces(sums), in_group(C, 128, 0))
    part = (part[:count] + part[count : 2 * count] + part[2 * count :]) * (1.0 / (PIX * (C // GROUPS)))
    back = dot(pieces(part), in_group(128, C, 1))
    return back[:count] + back[count : 2 * count] + back[2 * count :]


def sum_rows(values):
    return jnp.sum(values, axis=0, keepdims=True)


def norm_stats(get, mean_ref, inverse_ref, sums_ref):
    def first(n):
        sums_ref[row(n)] = sum_rows(get(n))

    each(SLOTS, first)
    mean_ref[...] = group_mean(sums_ref[...])

    def second(n):
        centred = get(n) - mean_ref[row(n)]
        sums_ref[row(n)] = sum_rows(centred * centred)

    each(SLOTS, second)
    inverse_ref[...] = lax.rsqrt(group_mean(sums_ref[...]) + EPSILON)


def silu(values):
    return values * jax.nn.sigmoid(values)


def shifted(values):
    spot = lax.rem(lax.broadcasted_iota(jnp.int32, values.shape, 0), RES)
    left = jnp.where(spot == 0, 0.0, pltpu.roll(values, 1, 0))
    right = jnp.where(spot == RES - 1, 0.0, pltpu.roll(values, values.shape[0] - 1, 0))
    return left, right


def chunk(n):
    return slice(n * WIDTH, (n + 1) * WIDTH)


CHUNKS = C // WIDTH


def weight_cols(ref, n):
    return ref[:, :, :, chunk(n)].reshape(C, WIDTH)


def weight_rows(ref, n):
    return ref[...].reshape(C, C)[chunk(n)]


def forward_kernel(
    lines,
    weights_a,
    weights_b,
    weights_qkv,
    weights_proj,
    images_hbm,
    cot_hbm,
    counts_ref,
    labels_ref,
    levels_ref,
    class_table,
    noise_table,
    modw_table,
    modb_ref,
    *refs,
):
    vectors, refs = refs[:VECTORS], refs[VECTORS:]
    forward_steps(
        lines,
        vectors,
        weights_a,
        weights_b,
        weights_qkv,
        weights_proj,
        images_hbm,
        cot_hbm,
        counts_ref,
        labels_ref,
        levels_ref,
        class_table,
        noise_table,
        modw_table,
        modb_ref,
        *refs,
    )


def forward_steps(
    lines,
    vectors,
    weights_a,
    weights_b,
    weights_qkv,
    weights_proj,
    images_hbm,
    cot_hbm,
    counts_ref,
    labels_ref,
    levels_ref,
    class_table,
    noise_table,
    modw_table,
    modb_ref,
    whole_ref,
    conv_out,
    slopes_out,
    turned_out,
    block_out,
    grad_out,
    low_out,
    right_out,
    vecs_ref,
    mod_ref,
    stats_ref,
    pre_ref,
    all_ids,
    sums_out,
    halves,
    block,
    vec_ref,
    ids_ref,
    class_ref,
    modw_ref,
    vec_all,
    mod_part,
    mod_got,
    act,
    act_f32,
    weights,
    sums_ref,
    conv_ref,
    resid_ref,
    slopes,
    turned,
    attn_in,
    qkv,
    right,
    low,
    pair_ref,
    pair_send,
    pair_recv,
    pair_local,
    own_sem,
    z_send,
    z_recv,
    p_send,
    x_send,
    x_recv,
    y_send,
    y_recv,
    s_send,
    s_recv,
    vec_send,
    vec_recv,
    ids_send,
    ids_recv,
    mod_send,
    mod_recv,
    load_sem,
    flush_sem,
    in_sem,
):
    z, y, x, c = place()
    d, h = lax.axis_index("dp"), lax.axis_index("head")
    n_dp, n_head = lines * 2, 4
    half = lines // 2
    inner = jnp.logical_and(z > 0, z < lines - 1)
    far = at_chip(lax.rem(3 * z + 1, lines), y, x, c)
    rows = block.shape[1]
    wide = block.shape[2]
    cols_own = wide // 2
    sibling = at_chip(z, y, x, 1 - c)
    along_x = at_chip(z, y, 1 - x, c)
    along_y = at_chip(z, 1 - y, x, c)
    line = [at_chip(lax.rem(z + k, lines), y, x, c) for k in range(1, lines)]
    column, heads = column_peers(n_dp), head_peers(n_head)
    greet(column + heads)

    def spot(i, cc, zz, yy, xx):
        return whole_ref.at[i, cc, zz, yy, :, span(xx, wide)]

    def parts_of(core):
        return (
            (weights_a.at[pl.ds(4 * core, 4)], pl.ds(0, 4)),
            (weights_b.at[pl.ds(4 * core, 4)], pl.ds(5, 4)),
            (weights_qkv.at[pl.ds(core, 1)], pl.ds(9, 1)),
        )

    last_parts = (
        ((weights_a.at[8], 4), (weights_qkv.at[2], 10)),
        ((weights_b.at[8], 4), (weights_proj, 10)),
    )

    def keep_copy(k):
        source, where = parts_of(c)[k]
        return pltpu.make_async_copy(source, halves.at[c, where], pair_local.at[k])

    def swap_copy(k):
        source, where = parts_of(1 - c)[k]
        return remote(source, halves.at[c, where], pair_send.at[k], pair_recv.at[k], sibling)

    def last_keep(core, k):
        source, where = last_parts[core][k]
        return pltpu.make_async_copy(source, halves.at[c, where], pair_local.at[3 + k])

    def last_swap(core, k):
        source, where = last_parts[core][k]
        return remote(source, halves.at[c, where], pair_send.at[3 + k], pair_recv.at[3 + k], sibling)

    def swap_start():
        for k in range(3):
            swap_copy(k).start()
            keep_copy(k).start()
        for core in range(2):

            @pl.when(c == core)
            def _():
                for k in range(2):
                    last_swap(1 - core, k).start()
                    last_keep(core, k).start()

    def swap_wait(k):
        if k < 3:
            keep_copy(k).wait()
            swap_copy(k).wait()
        else:
            last_keep(0, k - 3).wait()
            last_swap(0, k - 3).wait()

    def images_copy():
        return pltpu.make_async_copy(images_hbm, images_ref, in_sem.at[0])

    def cot_copy():
        return pltpu.make_async_copy(cot_hbm, cot_ref, in_sem.at[1])

    images_ref, cot_ref = attn_in, low

    def vec_copy(k):
        return remote(vec_ref, vec_all.at[h], vec_send.at[k], vec_recv.at[k], heads[k])

    def ids_copy(k):
        return remote(ids_ref, all_ids.at[d], ids_send.at[k], ids_recv.at[k], column[k])

    def mod_copy(k):
        return remote(
            mod_part.at[lax.rem(d + k + 1, n_dp)], mod_got.at[d], mod_send.at[k], mod_recv.at[k], column[k]
        )

    def own_copy(i):
        return pltpu.make_async_copy(block.at[i], spot(i, c, z, y, x), own_sem.at[i])

    def z_part(i, zz):
        if isinstance(i, int) and i >= FAR:
            return whole_ref.at[i, c, zz]
        return spot(i, c, zz, y, x)

    def z_copy(i, k):
        ref = z_part(i, z)
        source = ref if isinstance(i, int) and i >= FAR else block.at[i]
        return remote(source, ref, z_send.at[i, k], z_recv.at[i, k], line[k])

    def z_pass(i):
        ref = z_part(i, lax.rem(z + 2, lines))
        return remote(ref, ref, p_send.at[i], z_recv.at[i, lax.rem(2 * z + 2, lines)], far)

    def z_start(i):
        z_copy(i, 1).start()

        @pl.when(z != lines - 1)
        def _():
            z_copy(i, 0).start()

        @pl.when(z != 0)
        def _():
            z_copy(i, 2).start()

    def z_relay(i):
        z_copy(i, 1).wait_recv()

        @pl.when(inner)
        def _():
            z_pass(i).start()

    def z_finish(i):
        z_copy(i, 0).wait_recv()
        z_copy(i, 2).wait_recv()

    def z_drain(i):
        z_copy(i, 1).wait_send()

        @pl.when(z != lines - 1)
        def _():
            z_copy(i, 0).wait_send()

        @pl.when(z != 0)
        def _():
            z_copy(i, 2).wait_send()

        @pl.when(inner)
        def _():
            z_pass(i).wait_send()

    def x_copy(i, part):
        if isinstance(i, int) and i >= FAR:
            ref = spot(i, c, z, y, x) if part == 0 else spot(i, c, z, 1 - y, x).at[pl.ds(rows // 2, rows // 2)]
        elif part == 0:
            ref = spot(i, c, slice(None), y, x)
        else:
            ref = spot(i, c, pl.ds(half, half), 1 - y, x)
        return remote(ref, ref, x_send.at[i, part], x_recv.at[i, part], along_x)

    def y_copy(i, part):
        if isinstance(i, int) and i >= FAR:
            ref = spot(i, c, z, y, x) if part == 0 else spot(i, c, z, y, 1 - x).at[pl.ds(0, rows // 2)]
        elif part == 0:
            ref = spot(i, c, slice(None), y, x)
        else:
            ref = spot(i, c, pl.ds(0, half), y, 1 - x)
        return remote(ref, ref, y_send.at[i, part], y_recv.at[i, part], along_y)

    def s_copy(i, part):
        if isinstance(i, int) and i >= FAR:
            ref = whole_ref.at[i, c, part]
        else:
            yy, xx = ((y, x), (y, 1 - x), (1 - y, x), (1 - y, 1 - x))[part]
            ref = spot(i, c, slice(None), yy, xx)
        return remote(ref, ref, s_send.at[i, part], s_recv.at[i, part], sibling)

    def join(i):
        block[i] = jnp.concatenate([halves[0, i], halves[1, i]], axis=-1)
        own_copy(i).start()

    def begin(i):
        join(i)
        z_start(i)

    def far_begin(i):
        own_copy(i).wait()
        x_copy(i, 0).start()
        y_copy(i, 0).start()

    def far_pass(i):
        x_copy(i, 0).wait_recv()
        y_copy(i, 1).start()
        y_copy(i, 0).wait_recv()
        x_copy(i, 1).start()

    def far_line(i):
        x_copy(i, 1).wait_recv()
        y_copy(i, 1).wait_recv()
        z_start(i)

    def far_finish(i):
        z_finish(i)
        for part in range(lines):
            s_copy(i, part).start()

    def spread_line(i):
        own_copy(i).wait()
        z_finish(i)
        x_copy(i, 0).start()
        y_copy(i, 0).start()
        s_copy(i, 0).start()

    def pass_on(i):
        x_copy(i, 0).wait_recv()
        y_copy(i, 1).start()
        s_copy(i, 1).start()
        y_copy(i, 0).wait_recv()
        x_copy(i, 1).start()
        s_copy(i, 2).start()

    def finish(i):
        x_copy(i, 1).wait_recv()
        y_copy(i, 1).wait_recv()
        s_copy(i, 3).start()

    def arrived(i):
        for part in range(4):
            s_copy(i, part).wait_recv()

    def load(i, k):
        slot = i % 2
        return pltpu.make_async_copy(whole_ref.at[i, k], weights.at[slot, k], load_sem.at[slot, k])

    def fetch(i):
        arrived(i)
        load(i, 0).start()
        load(i, 1).start()

    def product(total, tap, slot, k):
        for n in range(CHUNKS):
            value = dot(act[tap % 3, lines_from(tap // 3)], weight_cols(weights.at[slot, k], n))
            total[:, :, :, chunk(n)] += value.reshape(RES, SLOTS, RES, WIDTH)

    def use_pair(total, i, first):
        slot = i % 2
        load(i, 0).wait()
        load(i, 1).wait()
        each(2, lambda k: product(total, i - first + 4 * k, slot, k))

    flushed = (
        (conv_ref, conv_out),
        (slopes.at[0], slopes_out.at[0]),
        (slopes.at[1], slopes_out.at[1]),
        (turned.at[3], turned_out.at[3]),
        (turned.at[2], turned_out.at[2]),
        (turned.at[0], turned_out.at[0]),
        (turned.at[1], turned_out.at[1]),
        (low, block_out),
        (resid_ref, grad_out),
        (attn_in, low_out),
        (right, right_out),
    )

    def flush(k):
        return pltpu.make_async_copy(*flushed[k], flush_sem.at[k])

    def set_act(place_t):
        def by_line(yy):
            value = act_f32[yy].reshape(LINE, C)
            left, right = shifted(value)
            spot_rows = pl.ds(pl.multiple_of((yy + 1) * LINE, LINE), LINE)
            act[0, spot_rows] = left.astype(BF16)
            act[1, spot_rows] = value.astype(BF16)
            act[2, spot_rows] = right.astype(BF16)

        each(RES, by_line)

        def turn(yy):
            value = act_f32[pl.ds(2 * yy, 2)].reshape(2 * LINE, C)
            turned[place_t, :, span(yy, 2 * LINE)] = value.T.astype(BF16)

        each(RES // 2, turn)

    def activate(which, n, value):
        sigma = jax.nn.sigmoid(value)
        act_f32[:, n] = (value * sigma).reshape(RES, RES, C)
        slopes[which, :, n] = (sigma * (1.0 + value * (1.0 - sigma))).reshape(RES, RES, C)

    def norm_a():
        for k in range(n_head - 1):
            vec_copy(k).wait()
        vecs_ref[...] = jnp.concatenate([vec_all[k].astype(F32) for k in range(n_head)], axis=-1)

        images_copy().wait()

        def get(n):
            return images_ref[span(n, PIX)].astype(F32)

        mean, inverse = stats_ref.at[0], stats_ref.at[1]
        norm_stats(get, mean, inverse, sums_ref)

        def to_act(n):
            value = (get(n) - mean[row(n)]) * inverse[row(n)]
            activate(0, n, value * vecs_ref[0:1] + vecs_ref[1:2])
            conv_ref[:, n] = jnp.broadcast_to(vecs_ref[2:3].reshape(1, 1, C), (RES, RES, C))
            resid_ref[:, n] = (get(n) + vecs_ref[5:6]).reshape(RES, RES, C)

        each(SLOTS, to_act)
        set_act(3)
        flush(1).start()
        flush(3).start()

    def embed():
        for k in range(n_dp - 1):
            ids_copy(k).wait()
        ids = all_ids[...].reshape(n_dp * SLOTS, 128)
        table = class_ref.shape[1]
        label_hot = lax.broadcasted_iota(jnp.int32, (n_dp * SLOTS, table), 1) == ids[:, 0:1]
        levels = noise_table.shape[0]
        level_hot = lax.broadcasted_iota(jnp.int32, (n_dp * SLOTS, levels), 1) == ids[:, 1:2]
        pre = dot_nt(jnp.where(label_hot, 1.0, 0.0).astype(BF16), class_ref[...])
        width = class_table.shape[0]
        place_of = lax.broadcasted_iota(jnp.int32, (C, 128), 0) - d * width
        lane = lax.broadcasted_iota(jnp.int32, (C, 128), 1)
        chosen = jnp.logical_and(place_of == lane, lane < width)
        noise = dot(noise_table[...], jnp.where(chosen, 1.0, 0.0).astype(BF16)).astype(BF16)
        pre += dot(jnp.where(level_hot, 1.0, 0.0).astype(BF16), noise)
        pre_ref[...] = pre
        part = dot(silu(pre).astype(BF16), modw_ref[...])
        for k in range(n_dp):
            mine = part[k * SLOTS : (k + 1) * SLOTS]
            mod_part[k] = jnp.concatenate([mine[:, :C], mine[:, C:]], axis=0).astype(BF16)
        mod_got[d] = mod_part[d]
        for k in range(n_dp - 1):
            mod_copy(k).start()

    def norm_b():
        for k in range(n_dp - 1):
            mod_copy(k).wait()
        bias = modb_ref[...].astype(F32)
        total = jnp.concatenate([jnp.broadcast_to(bias[k : k + 1], (SLOTS, C)) for k in range(2)], axis=0)
        for k in range(n_dp):
            total += mod_got[k].astype(F32)
        mod_ref[...] = total.astype(BF16).astype(F32)

        def get(n):
            return conv_ref[:, n].reshape(PIX, C)

        mean, inverse = stats_ref.at[2], stats_ref.at[3]
        norm_stats(get, mean, inverse, sums_ref)

        def to_act(n):
            value = (get(n) - mean[row(n)]) * inverse[row(n)]
            value = value * vecs_ref[3:4] + vecs_ref[4:5]
            value = mod_ref[row(SLOTS + n)] + value * (mod_ref[row(n)] + 1.0)
            activate(1, n, value)

        each(SLOTS, to_act)
        set_act(2)
        flush(0).start()
        flush(2).start()
        flush(4).start()

    def residual(n):
        return resid_ref[:, n].reshape(PIX, C)

    def normed(n):
        return (residual(n) - stats_ref[4, row(n)]) * stats_ref[5, row(n)]

    def transpose_out(source, place_t):
        def turn(k):
            value = source[span(k, 2 * LINE)].astype(F32)
            turned[place_t, :, span(k, 2 * LINE)] = value.T.astype(BF16)

        each(ALL // (2 * LINE), turn)

    def live(n):
        slots = counts_ref[d * n_head + h, 0] + counts_ref[d * n_head + h, 1]
        return jnp.where(n < slots, 1.0, 0.0)

    def norm_c():
        cot_copy().wait()
        norm_stats(residual, stats_ref.at[4], stats_ref.at[5], sums_ref)
        sums_out[...] = jnp.zeros_like(sums_out)

        def prepare(n):
            attn_in[span(n, PIX)] = (normed(n) * vecs_ref[6:7] + vecs_ref[7:8]).astype(BF16)
            grad = cot_ref[span(n, PIX)].astype(F32) * live(n)
            right[3, span(n, PIX)] = grad.astype(BF16)
            sums_out[8:9] += sum_rows(grad)

        each(SLOTS, prepare)
        transpose_out(attn_in, 0)
        flush(5).start()

    def attention():
        unit = (weights.at[1, 0], weights.at[1, 1], weights.at[0, 0], weights.at[0, 1])
        for t in range(4):
            load(9 + t // 2, t % 2).wait()
            for n in range(CHUNKS):
                if t < 3:
                    value = dot(attn_in[...], weight_cols(unit[t], n))
                else:
                    value = dot_nt(right[3], weight_rows(unit[3], n))
                qkv[t, :, chunk(n)] = value.astype(BF16)
        factor = DH ** (-0.5)
        band = lax.broadcasted_iota(jnp.int32, (PIX, WIDTH), 1) // DH
        heads_at_once = WIDTH // DH

        def stack(value):
            zero = jnp.zeros_like(value)
            return jnp.concatenate([jnp.where(band == k, value, zero) for k in range(heads_at_once)], axis=0)

        def pick(value):
            out = value[:PIX]
            for k in range(1, heads_at_once):
                out = jnp.where(band == k, value[k * PIX : (k + 1) * PIX], out)
            return out

        def attend(n):
            for b in range(CHUNKS):
                query, key, value, grad = (qkv[t, span(n, PIX), chunk(b)] for t in range(4))
                query4, grad4 = stack(query), stack(grad)
                scores = dot_nt(key, query4) * factor
                weight = jnp.exp(scores - jnp.max(scores, axis=0, keepdims=True))
                probs = weight / jnp.sum(weight, axis=0, keepdims=True)
                probs_low = probs.astype(BF16)
                low[span(n, PIX), chunk(b)] = pick(dot_tn(probs_low, value)).astype(BF16)
                grad_probs = dot_nt(value, grad4)
                inner_sum = jnp.sum(grad_probs * probs, axis=0, keepdims=True)
                grad_scores = (probs * (grad_probs - inner_sum)).astype(BF16)
                right[0, span(n, PIX), chunk(b)] = (pick(dot_tn(grad_scores, key)) * factor).astype(BF16)
                right[1, span(n, PIX), chunk(b)] = (dot(grad_scores, query4) * factor).astype(BF16)
                right[2, span(n, PIX), chunk(b)] = dot(probs_low, grad4).astype(BF16)

        each(SLOTS, attend)
        flush(10).start()
        transpose_out(low, 1)
        flush(6).start()
        for n in range(CHUNKS):
            value = dot(low[...], weight_cols(unit[3], n))
            act_f32[:, :, :, chunk(n)] = value.reshape(SLOTS, RES, RES, WIDTH)

        def finish_out(n):
            value = residual(n) + act_f32[n].reshape(PIX, C) + vecs_ref[8:9]
            low[span(n, PIX)] = (value * live(n)).astype(BF16)

        each(SLOTS, finish_out)
        flush(7).start()
        for n in range(CHUNKS):
            value = dot_nt(right[0], weight_rows(unit[0], n))
            value += dot_nt(right[1], weight_rows(unit[1], n))
            value += dot_nt(right[2], weight_rows(unit[2], n))
            act_f32[:, :, :, chunk(n)] = value.reshape(SLOTS, RES, RES, WIDTH)

        def back(n):
            grad = act_f32[n].reshape(PIX, C)
            pair_ref[row(n)] = sum_rows(grad * normed(n))
            pair_ref[row(SLOTS + n)] = sum_rows(grad)

        each(SLOTS, back)
        sums_out[6:7] = sum_rows(pair_ref[0:SLOTS])
        sums_out[7:8] = sum_rows(pair_ref[SLOTS:])
        pair_ref[...] = group_mean(pair_ref[...] * vecs_ref[6:7])

        def back_second(n):
            inverse = stats_ref[5, row(n)]
            value = act_f32[n].reshape(PIX, C) * (vecs_ref[6:7] * inverse)
            value -= normed(n) * (pair_ref[row(n)] * inverse) + pair_ref[row(SLOTS + n)] * inverse
            value += right[3, span(n, PIX)].astype(F32)
            resid_ref[:, n] = value.reshape(RES, RES, C)
            sums_out[5:6] += sum_rows(value.astype(BF16).astype(F32))

        each(SLOTS, back_second)
        flush(8).start()

        def lower(yy):
            attn_in[span(yy, LINE)] = resid_ref[yy].reshape(LINE, C).astype(BF16)

        each(RES, lower)
        flush(9).start()

    swap_start()
    images_copy().start()
    cot_copy().start()
    one = [ref[...].astype(F32).reshape(1, cols_own) for ref in vectors]
    vec_ref[...] = jnp.concatenate(one + [jnp.zeros((16 - VECTORS, cols_own), F32)], axis=0).astype(BF16)
    lane = lax.broadcasted_iota(jnp.int32, (1, 128), 1)
    for n in range(SLOTS):
        ids_ref[n : n + 1] = jnp.where(lane == 0, labels_ref[n], levels_ref[n])
    for k in range(n_head - 1):
        vec_copy(k).start()
    for k in range(n_dp - 1):
        ids_copy(k).start()
    width = class_table.shape[0]
    class_ref[...] = jnp.zeros_like(class_ref)
    class_ref[0:width, 0 : class_table.shape[1]] = class_table[...]
    modw_ref[...] = jnp.zeros_like(modw_ref)
    modw_ref[0:width] = modw_table[...]
    vec_all[h] = vec_ref[...]
    all_ids[d] = ids_ref[...]
    edge = jnp.zeros((LINE, C), BF16)
    for j in range(3):
        act[j, 0:LINE] = edge
        act[j, ALL + LINE : ALL + 2 * LINE] = edge
    for k in range(5):
        swap_wait(k)
    for i in (10, 9):
        join(i)
    begin(0)
    for i in (10, 9):
        far_begin(i)
    begin(1)
    z_relay(0)
    begin(2)
    spread_line(0)
    for i in (10, 9):
        far_pass(i)
    begin(3)
    z_relay(1)
    norm_a()
    spread_line(1)
    pass_on(0)
    begin(4)
    z_relay(2)
    embed()
    spread_line(2)
    pass_on(1)
    finish(0)
    begin(5)
    z_relay(3)
    begin(6)
    z_relay(4)
    far_line(10)
    spread_line(3)
    pass_on(2)
    finish(1)
    fetch(0)

    def body(turn, carry):
        @pl.when(turn < 6)
        def _():
            begin(turn + 3)

        @pl.when(turn == 6)
        def _():
            far_line(9)
            z_relay(10)

        z_relay(turn + 1)
        spread_line(turn)
        pass_on(turn - 1)
        finish(turn - 2)
        fetch(turn - 3)
        use_pair(conv_ref, turn - 4, 0)
        return carry

    lax.fori_loop(4, 8, body, 0)
    spread_line(8)
    pass_on(7)
    finish(6)
    fetch(5)
    load(4, 0).wait()
    load(4, 1).wait()
    product(conv_ref, 8, 0, 0)
    norm_b()
    product(resid_ref, 8, 0, 1)
    pass_on(8)
    finish(7)
    z_relay(9)
    fetch(6)
    far_finish(10)
    use_pair(resid_ref, 5, 5)
    finish(8)
    fetch(7)
    use_pair(resid_ref, 6, 5)
    fetch(8)
    use_pair(resid_ref, 7, 5)
    far_finish(9)
    use_pair(resid_ref, 8, 5)
    norm_c()
    fetch(9)
    fetch(10)
    attention()

    def drain(i):
        z_drain(i)
        for part in range(2):
            x_copy(i, part).wait_send()
            y_copy(i, part).wait_send()
        for part in range(4):
            s_copy(i, part).wait_send()

    each(FAR, drain)
    drain(9)
    drain(10)
    for k in range(len(flushed)):
        flush(k).wait()


def run_forward(weights, images, cotangent, counts, labels, levels, class_table, noise_table, modw, modb, vectors):
    n_dp, n_head = lax.axis_size("dp"), lax.axis_size("head")
    rows, cols = weights[0].shape[1:]
    lines, across, wide = n_dp // 2, n_head // 2, 2 * cols
    board = (RES, SLOTS, RES, C)
    shape = jax.ShapeDtypeStruct
    return pl.pallas_call(
        functools.partial(forward_kernel, lines),
        out_shape=(
            shape((PAIRS, 2, lines, 2, rows, across * wide), BF16),
            shape(board, F32),
            shape((2,) + board, F32),
            shape((4, C, ALL), BF16),
            shape((ALL, C), BF16),
            shape(board, F32),
            shape((ALL, C), BF16),
            shape((4, ALL, C), BF16),
            shape((16, C), F32),
            shape((2 * SLOTS, C), F32),
            shape((6, SLOTS, C), F32),
            shape((n_dp * SLOTS, 128), F32),
            shape((n_dp, SLOTS, 128), jnp.int32),
            shape((16, C), F32),
        ),
        in_specs=[ANY] * 6 + [SMEM] * 3 + [VMEM] * (4 + VECTORS),
        out_specs=(ANY,) * 8 + (VMEM,) * 6,
        scratch_shapes=[
            pltpu.VMEM((2, PAIRS, rows, cols), BF16),
            pltpu.VMEM((PAIRS, rows, wide), BF16),
            pltpu.VMEM((16, cols), BF16),
            pltpu.VMEM((SLOTS, 128), jnp.int32),
            pltpu.VMEM((128, 1024), BF16),
            pltpu.VMEM((128, 2 * C), BF16),
            pltpu.VMEM((n_head, 16, cols), BF16),
            pltpu.VMEM((n_dp, 2 * SLOTS, C), BF16),
            pltpu.VMEM((n_dp, 2 * SLOTS, C), BF16),
            pltpu.VMEM((3, ALL + 2 * LINE, C), BF16),
            pltpu.VMEM(board, F32),
            pltpu.VMEM((2, 2, lines, 2, rows, across * wide), BF16),
            pltpu.VMEM((SLOTS, C), F32),
            pltpu.VMEM(board, F32),
            pltpu.VMEM(board, F32),
            pltpu.VMEM((2,) + board, F32),
            pltpu.VMEM((4, C, ALL), BF16),
            pltpu.VMEM((ALL, C), BF16),
            pltpu.VMEM((4, ALL, C), BF16),
            pltpu.VMEM((4, ALL, C), BF16),
            pltpu.VMEM((ALL, C), BF16),
            pltpu.VMEM((2 * SLOTS, C), F32),
            DMA((5,)),
            DMA((5,)),
            DMA((5,)),
            DMA((PAIRS,)),
            DMA((PAIRS, lines - 1)),
            DMA((PAIRS, lines - 1)),
            DMA((PAIRS,)),
            DMA((PAIRS, 2)),
            DMA((PAIRS, 2)),
            DMA((PAIRS, 2)),
            DMA((PAIRS, 2)),
            DMA((PAIRS, 4)),
            DMA((PAIRS, 4)),
            DMA((n_head - 1,)),
            DMA((n_head - 1,)),
            DMA((n_dp - 1,)),
            DMA((n_dp - 1,)),
            DMA((n_dp - 1,)),
            DMA((n_dp - 1,)),
            DMA((2, 2)),
            DMA((11,)),
            DMA((2,)),
        ],
        compiler_params=pltpu.CompilerParams(
            collective_id=0, has_side_effects=True, vmem_limit_bytes=56 * 2**20
        ),
        name="gather_forward",
    )(
        *weights,
        images,
        cotangent,
        counts,
        labels,
        levels,
        class_table,
        noise_table,
        modw,
        modb,
        *vectors,
    )


def backward_kernel(
    lines,
    whole_ref,
    turned_ref,
    right_ref,
    grad_low_ref,
    grad_resid_ref,
    conv_ref,
    slopes_ref,
    images_hbm,
    stats_ref,
    vecs_ref,
    mod_ref,
    sums_in,
    pre_ref,
    ids_ref,
    modw_table,
    out_a,
    out_b,
    out_qkv,
    out_proj,
    image_ref,
    class_ref,
    modw_out,
    modb_out,
    vec_out,
    mine,
    from_x,
    from_y,
    from_z,
    far_x,
    far_y,
    far_z,
    ends,
    modw_ref,
    lefts,
    rights,
    grads,
    stage,
    weights,
    total,
    board,
    slopes,
    image_mine,
    images_ref,
    sums_ref,
    pair_ref,
    coef_ref,
    gm_mine,
    gm_all,
    mw_mine,
    mw_got,
    ge_all,
    vs_mine,
    vs_got,
    vt_mine,
    vt_all,
    x_send,
    x_recv,
    y_send,
    y_recv,
    z_send,
    z_recv,
    p_send,
    p_recv,
    e_send,
    e_recv,
    e_local,
    op_send,
    op_recv,
    op_local,
    load_sem,
    in_sem,
    out_sem,
    gm_send,
    gm_recv,
    mw_send,
    mw_recv,
    ge_send,
    ge_recv,
    vs_send,
    vs_recv,
    vt_send,
    vt_recv,
):
    z, y, x, c = place()
    d, h = lax.axis_index("dp"), lax.axis_index("head")
    n_dp, n_head = lines * 2, 4
    half = lines // 2
    inner = jnp.logical_and(z > 0, z < lines - 1)
    rows, wide = from_z.shape[2], from_z.shape[3]
    cols = wide // 2
    sibling = at_chip(z, y, x, 1 - c)
    along_x = at_chip(z, y, 1 - x, c)
    along_y = at_chip(z, 1 - y, x, c)
    line = [at_chip(lax.rem(z + k, lines), y, x, c) for k in range(1, lines)]
    column, heads = column_peers(n_dp), head_peers(n_head)

    own_rows = pl.ds(LINE, ALL)

    def operand(k):
        if k == 0:
            return right_ref.at[2 + c], right_ref.at[3 - c], rights.at[0, span(c, ALL)]
        if k == 1:
            return turned_ref.at[c], turned_ref.at[1 - c], lefts.at[1, :, span(c, ALL)]
        if k == 2:
            return right_ref.at[c], right_ref.at[1 - c], rights.at[1, span(c, ALL)]
        if k == 3:
            return turned_ref.at[0], turned_ref.at[0], lefts.at[0, :, span(c, ALL)]
        if k == 4:
            return grad_low_ref, grad_low_ref, grads.at[1, c, own_rows]
        return turned_ref.at[k - 3], turned_ref.at[k - 3], lefts.at[k - 3, :, span(c, ALL)]

    def op_own(k):
        source, _, target = operand(k)
        return pltpu.make_async_copy(source, target, op_local.at[k])

    def op_copy(k):
        _, source, target = operand(k)
        return remote(source, target, op_send.at[k], op_recv.at[k], sibling)

    def stage_copy():
        return remote(grads.at[1, c, own_rows], stage, op_send.at[7], op_recv.at[7], sibling)

    def op_wait(k):
        op_own(k).wait()
        op_copy(k).wait_recv()

    def lanes(xx):
        return span(xx, wide)

    first, second = pl.ds(0, rows // 2), pl.ds(rows // 2, rows // 2)

    def is_far(i):
        return isinstance(i, int) and i >= FAR

    def x_copy(i, part):
        if is_far(i):
            into = far_x.at[i - FAR]
            if part == 0:
                src, dst = mine.at[i, z, 1 - y, second, lanes(1 - x)], into.at[pl.ds(rows, rows // 2)]
            else:
                src, dst = mine.at[i, z, y, :, lanes(1 - x)], into.at[pl.ds(0, rows)]
        elif part == 0:
            src, dst = mine.at[i, pl.ds(half, half), 1 - y, :, lanes(1 - x)], from_x.at[i, pl.ds(lines, half)]
        else:
            src, dst = mine.at[i, :, y, :, lanes(1 - x)], from_x.at[i, pl.ds(0, lines)]
        return remote(src, dst, x_send.at[i, part], x_recv.at[i, part], along_x)

    def y_copy(i, part):
        if is_far(i):
            into = far_y.at[i - FAR]
            if part == 0:
                src, dst = mine.at[i, z, 1 - y, first, lanes(1 - x)], into.at[pl.ds(rows, rows // 2)]
            else:
                src, dst = mine.at[i, z, 1 - y, :, lanes(x)], into.at[pl.ds(0, rows)]
        elif part == 0:
            src, dst = mine.at[i, pl.ds(0, half), 1 - y, :, lanes(1 - x)], from_y.at[i, pl.ds(lines, half)]
        else:
            src, dst = mine.at[i, :, 1 - y, :, lanes(x)], from_y.at[i, pl.ds(0, lines)]
        return remote(src, dst, y_send.at[i, part], y_recv.at[i, part], along_y)

    beyond = lax.rem(z + 2, lines)
    opposite = lines - 1 - z
    near_end = at_chip(1 + z // (lines - 1), y, x, c)

    def z_block(i, zz):
        return mine.at[i, zz] if is_far(i) else mine.at[i, zz, y, :, lanes(x)]

    def z_slot(i, k):
        return far_z.at[i - FAR, k] if is_far(i) else from_z.at[i, k]

    def z_copy(i, k):
        return remote(
            z_block(i, lax.rem(z + k + 1, lines)), z_slot(i, k), z_send.at[i, k], z_recv.at[i, k], line[k]
        )

    def z_give(i):
        return remote(z_block(i, opposite), z_slot(i, 3), p_send.at[i], p_recv.at[i], near_end)

    def z_start(i):
        @pl.when(jnp.logical_not(inner))
        def _():
            z_give(i).start()

        @pl.when(z < lines - 1)
        def _():
            z_copy(i, 0).start()

        @pl.when(z > 0)
        def _():
            z_copy(i, 2).start()

        @pl.when(jnp.logical_not(inner))
        def _():
            z_copy(i, 1).start()

    def z_mix(i):
        @pl.when(inner)
        def _():
            z_give(i).wait_recv()
            if is_far(i):
                mine[i, beyond] += far_z[i - FAR, 3]
            else:
                mine[i, beyond, y, :, lanes(x)] += from_z[i, 3]
            z_copy(i, 1).start()

    def z_wait(i):
        z_copy(i, 1).wait_recv()

        @pl.when(z > 0)
        def _():
            z_copy(i, 0).wait_recv()

        @pl.when(z < lines - 1)
        def _():
            z_copy(i, 2).wait_recv()

    def z_drain(i):
        z_copy(i, 1).wait_send()

        @pl.when(z < lines - 1)
        def _():
            z_copy(i, 0).wait_send()

        @pl.when(z > 0)
        def _():
            z_copy(i, 2).wait_send()

        @pl.when(jnp.logical_not(inner))
        def _():
            z_give(i).wait_send()

    def target(i, core):
        if isinstance(i, int) and i == 10:
            return out_proj if core == 1 else out_qkv.at[2]
        if isinstance(i, int) and i == 9:
            return out_qkv.at[core]
        if isinstance(i, int) and i == 4:
            return out_b.at[8] if core == 1 else out_a.at[8]
        if isinstance(i, int) and i > 4:
            return out_b.at[4 * core + i - 5]
        return out_a.at[4 * core + i]

    def e_copy(i, core):
        return remote(ends.at[1 - c, i], target(i, core), e_send.at[i], e_recv.at[i], sibling)

    def e_own(i, core):
        return pltpu.make_async_copy(ends.at[c, i], target(i, core), e_local.at[i])

    def finish(i, value):
        for cc in range(2):
            ends[cc, i] = value[:, cc * cols : (cc + 1) * cols]
        if i in (4, 10):
            for core in range(2):

                @pl.when(c == core)
                def _():
                    e_copy(i, core).start()
                    e_own(i, core).start()
        else:
            e_copy(i, c).start()
            e_own(i, c).start()

    def offer(i):
        x_copy(i, 0).start()
        y_copy(i, 0).start()

    def relay(i):
        x_copy(i, 0).wait_recv()
        y_copy(i, 0).wait_recv()
        if is_far(i):
            rest = pl.ds(rows, rows // 2)
            mine[i, z, y, first, lanes(1 - x)] += far_y[i - FAR, rest]
            mine[i, z, 1 - y, second, lanes(x)] += far_x[i - FAR, rest]
        else:
            for j in range(half):
                mine[i, j, y, :, lanes(1 - x)] += from_y[i, lines + j]
                mine[i, half + j, 1 - y, :, lanes(x)] += from_x[i, lines + j]
        x_copy(i, 1).start()
        y_copy(i, 1).start()

    def collect(i):
        x_copy(i, 1).wait_recv()
        y_copy(i, 1).wait_recv()
        if is_far(i):
            whole_rows = pl.ds(0, rows)
            value = mine[i, z, y, :, lanes(x)].astype(F32)
            value += far_x[i - FAR, whole_rows].astype(F32) + far_y[i - FAR, whole_rows].astype(F32)
            finish(i, value)
            return

        def add(j):
            value = mine[i, j, y, :, lanes(x)].astype(F32)
            value += from_x[i, j].astype(F32) + from_y[i, j].astype(F32)
            mine[i, j, y, :, lanes(x)] = value.astype(BF16)

        each(lines, add)
        z_start(i)

    def last(i):
        z_wait(i)
        if is_far(i):
            for yy in range(2):
                value = mine[i, z, yy].astype(F32)
                for k in range(lines - 1):
                    value += far_z[i - FAR, k, yy].astype(F32)
                mine[i, z, yy] = value.astype(BF16)
            offer(i)
            return
        value = mine[i, z, y, :, lanes(x)].astype(F32)
        for k in range(lines - 1):
            value += from_z[i, k].astype(F32)
        finish(i, value)

    def put(i, n, value):
        mine[i, :, :, :, chunk(n)] = value.astype(BF16).reshape(mine.shape[1:4] + (WIDTH,))

    def plain_unit(i, left, right):
        for n in range(CHUNKS):
            put(i, n, dot(lefts[left], rights[right, :, chunk(n)]))

    def conv_unit(i, left, tap):
        where, side = lines_from(2 - tap // 3), 2 - tap % 3
        for n in range(CHUNKS):
            both = jnp.concatenate([grads[side, core, where, chunk(n)] for core in range(2)], axis=0)
            put(i, n, dot(lefts[left], both))

    def extra_b():
        @pl.when(c == 1)
        def _():
            conv_unit(4, 2, 8)

    def extra_a():
        @pl.when(c == 0)
        def _():
            conv_unit(4, 3, 8)

    def spread_sides(core):
        def by_line(yy):
            value = grads[1, core, pl.ds(pl.multiple_of((yy + 1) * LINE, LINE), LINE)].astype(F32)
            left, right = shifted(value)
            spot_rows = pl.ds(pl.multiple_of((yy + 1) * LINE, LINE), LINE)
            grads[0, core, spot_rows] = left.astype(BF16)
            grads[2, core, spot_rows] = right.astype(BF16)

        each(RES, by_line)

    def load(tap, base):
        ninth = tap // 8
        i = (base // 2 + tap % 4) * (1 - ninth) + 4 * ninth
        k = (tap // 4) % 2 + (base // 10) * ninth
        return pltpu.make_async_copy(whole_ref.at[i, k], weights.at[tap % 2], load_sem.at[tap % 2])

    def conv_back(tap, base):
        load(tap, base).wait()

        @pl.when(tap < 8)
        def _():
            load(tap + 1, base).start()

        part = grads[2 - tap % 3, c, lines_from(2 - tap // 3)]
        for n in range(CHUNKS):
            value = dot_nt(part, weight_rows(weights.at[tap % 2], n))
            total[:, :, :, chunk(n)] += value.reshape(RES, SLOTS, RES, WIDTH)

    def conv_back_range(first, stop, base):
        def body(tap, carry):
            conv_back(tap, base)
            return carry

        lax.fori_loop(first, stop, body, 0)

    def slope(values):
        sigma = jax.nn.sigmoid(values)
        return sigma * (1.0 + values * (1.0 - sigma))

    for k in (0, 2):
        from_z[:, k] = jnp.zeros_like(from_z[:, k])
        far_z[:, k] = jnp.zeros_like(far_z[:, k])
    greet(column + heads)
    def op_start(k):
        op_own(k).start()
        op_copy(k).start()

    for k in range(6):
        op_start(k)
    load(0, 10).start()

    def fetch(k):
        source, target = (
            (conv_ref, board),
            (slopes_ref.at[1], slopes),
            (slopes_ref.at[0], slopes),
            (grad_resid_ref, board),
            (images_hbm, images_ref),
        )[k]
        return pltpu.make_async_copy(source, target, in_sem.at[k])

    fetch(0).start()
    fetch(1).start()
    vs_mine[...] = jnp.zeros_like(vs_mine)
    edge = jnp.zeros((LINE, C), BF16)
    for j in range(3):
        for core in range(2):
            grads[j, core, 0:LINE] = edge
            grads[j, core, ALL + LINE : ALL + 2 * LINE] = edge
    total[...] = jnp.zeros_like(total)
    sums_ref[...] = sums_in[...]
    modw_ref[...] = jnp.zeros_like(modw_ref)
    modw_ref[0:rows] = modw_table[...]

    def norm_b_value(n):
        return (board[:, n].reshape(PIX, C) - stats_ref[2, row(n)]) * stats_ref[3, row(n)]

    def norm_a_value(n):
        return (images_ref[span(n, PIX)].astype(F32) - stats_ref[0, row(n)]) * stats_ref[1, row(n)]

    def back_sums(get):
        def body(n):
            grad = (total[:, n] * slopes[:, n]).reshape(PIX, C)
            total[:, n] = grad.reshape(RES, RES, C)
            pair_ref[row(n)] = sum_rows(grad * get(n))
            pair_ref[row(SLOTS + n)] = sum_rows(grad)

        each(SLOTS, body)

    def back_factors(factor, inverse):
        coef_ref[0:SLOTS] = factor * inverse
        means = group_mean(pair_ref[...] * jnp.concatenate([factor, factor], axis=0))
        coef_ref[SLOTS : 2 * SLOTS] = means[:SLOTS] * inverse
        coef_ref[2 * SLOTS :] = means[SLOTS:] * inverse

    def back_value(n, get):
        value = total[:, n].reshape(PIX, C) * coef_ref[row(n)]
        return value - get(n) * coef_ref[row(SLOTS + n)] - coef_ref[row(2 * SLOTS + n)]

    def gm_copy(k):
        return remote(gm_mine, gm_all.at[d], gm_send.at[k], gm_recv.at[k], column[k])

    def mw_copy(k):
        return remote(
            mw_mine.at[lax.rem(h + k + 1, n_head)], mw_got.at[k], mw_send.at[k], mw_recv.at[k], heads[k]
        )

    def ge_copy(k):
        return remote(ge_all.at[h], ge_all.at[h], ge_send.at[k], ge_recv.at[k], heads[k])

    def vs_copy(k):
        return remote(
            vs_mine.at[lax.rem(h + k + 1, n_head)], vs_got.at[k], vs_send.at[k], vs_recv.at[k], heads[k]
        )

    def vt_copy(k):
        return remote(vt_mine, vt_all.at[d], vt_send.at[k], vt_recv.at[k], column[k])

    def image_copy():
        return pltpu.make_async_copy(image_mine, image_ref, out_sem)

    count = n_dp * SLOTS

    def start():
        op_wait(0)
        op_wait(1)

    def dw(i):
        if i == 10:
            plain_unit(10, 1, 0)
        elif i == 9:
            op_wait(2)
            op_wait(3)
            plain_unit(9, 0, 1)
        elif i > 4:
            conv_unit(i, 2, 4 * c + i - 5)
        else:
            conv_unit(i, 3, 4 * c + i)

    def sides():
        op_wait(4)
        op_wait(5)
        spread_sides(0)
        spread_sides(1)

    def back_b_first():
        load(0, 0).start()
        op_start(6)
        fetch(0).wait()
        fetch(1).wait()
        back_sums(norm_b_value)
        alone, with_norm = pair_ref[SLOTS:], pair_ref[:SLOTS]
        scale = mod_ref[0:SLOTS] + 1.0
        gm_mine[...] = jnp.concatenate([vecs_ref[3:4] * with_norm + vecs_ref[4:5] * alone, alone], axis=0).astype(BF16)
        gm_all[d] = gm_mine[...]
        for k in range(n_dp - 1):
            gm_copy(k).start()
        sums_ref[3:4] = sum_rows(with_norm * scale)
        sums_ref[4:5] = sum_rows(alone * scale)
        back_factors(scale * vecs_ref[3:4], stats_ref[3])

    def back_b_second():
        fetch(2).start()
        fetch(4).start()

        def body(n):
            value = back_value(n, norm_b_value).astype(BF16).astype(F32)
            sums_ref[2:3] += sum_rows(value)
            total[:, n] = value.reshape(RES, RES, C)

        each(SLOTS, body)
        fetch(3).start()

    def lower():
        def by_line(yy):
            spot_rows = pl.ds(pl.multiple_of((yy + 1) * LINE, LINE), LINE)
            grads[1, c, spot_rows] = total[yy].reshape(LINE, C).astype(BF16)

        each(RES, by_line)
        stage_copy().start()
        spread_sides(c)
        total[...] = jnp.zeros_like(total)

    def take():
        stage_copy().wait_recv()

        def by_line(yy):
            spot_rows = pl.ds(pl.multiple_of((yy + 1) * LINE, LINE), LINE)
            grads[1, 1 - c, spot_rows] = stage[span(yy, LINE)]

        each(RES, by_line)
        spread_sides(1 - c)
        op_wait(6)

    def modulation():
        for k in range(n_dp - 1):
            gm_copy(k).wait()
        parts = gm_all[...].astype(F32)
        gm_scale = parts[:, :SLOTS].reshape(count, C)
        gm_offset = parts[:, SLOTS:].reshape(count, C)
        pre = pre_ref[...]
        emb = silu(pre).astype(BF16)
        part_rows = rows // n_head
        for k, value in ((0, gm_scale), (1, gm_offset)):
            low_value = value.astype(BF16)
            grad_w = dot_tn(emb, low_value)
            place_lanes = slice(k * C, (k + 1) * C)
            for hh in range(n_head):
                mw_mine[hh, 0:part_rows, place_lanes] = grad_w[hh * part_rows : (hh + 1) * part_rows]
                mw_mine[hh, part_rows : part_rows + 8, place_lanes] = jnp.broadcast_to(sum_rows(value), (8, C))
        grad_e = dot_nt(gm_scale.astype(BF16), modw_ref[:, :C]) + dot_nt(gm_offset.astype(BF16), modw_ref[:, C:])
        grad_e = grad_e * slope(pre)
        label = ids_ref[...].reshape(count, 128)[:, 0:1].astype(F32)
        lane = lax.broadcasted_iota(jnp.int32, grad_e.shape, 1)
        ge_all[h] = jnp.where(lane < rows, grad_e, label)
        for k in range(n_head - 1):
            mw_copy(k).start()
            ge_copy(k).start()

    def back_a_first():
        fetch(2).wait()
        fetch(4).wait()
        back_sums(norm_a_value)
        sums_ref[0:1] = sum_rows(pair_ref[:SLOTS])
        sums_ref[1:2] = sum_rows(pair_ref[SLOTS:])
        for hh in range(n_head):
            vs_mine[hh] = sums_ref[:, hh * cols : (hh + 1) * cols]
        for k in range(n_head - 1):
            vs_copy(k).start()
        back_factors(jnp.broadcast_to(vecs_ref[0:1], (SLOTS, C)), stats_ref[1])

    def back_a_second():
        fetch(3).wait()

        def body(n):
            image_mine[span(n, PIX)] = back_value(n, norm_a_value) + board[:, n].reshape(PIX, C)

        each(SLOTS, body)
        image_copy().start()

    def vec_first():
        value = vs_mine[h]
        for k in range(n_head - 1):
            vs_copy(k).wait()
            value += vs_got[k]
        vt_mine[...] = value
        vt_all[d] = value
        for k in range(n_dp - 1):
            vt_copy(k).start()

    def mod_out():
        value = mw_mine[h]
        for k in range(n_head - 1):
            mw_copy(k).wait()
            value += mw_got[k]
        part_rows = rows // n_head
        first_lane = (d * n_head + h) * part_rows
        for k in range(2):
            lanes_of = slice(k * C, (k + 1) * C)
            modw_out[:, k] = value[:part_rows, lanes_of]
            turned_row = pltpu.roll(value[part_rows:, lanes_of], lax.rem(C - first_lane, C), 1)
            modb_out[k : k + 1] = turned_row[0:1, :part_rows]

    def class_out():
        for k in range(n_head - 1):
            ge_copy(k).wait()
        table = class_ref.shape[1]
        part = rows // n_head
        value = ge_all[...].reshape(n_head * count, 128)
        label = value[:, rows : rows + 1].astype(jnp.int32)
        hot = lax.broadcasted_iota(jnp.int32, (n_head * count, table), 1) == label
        own = pltpu.roll(value, lax.rem(128 - h * part, 128), 1).astype(BF16)
        value = dot_tn(own, jnp.where(hot, 1.0, 0.0).astype(BF16))
        class_ref[...] = value[:part]

    def vec_second():
        for k in range(n_dp - 1):
            vt_copy(k).wait()
        value = vt_all[0]
        for k in range(1, n_dp):
            value += vt_all[k]
        vec_out[...] = value

    start()
    dw(10)
    z_start(10)
    dw(9)
    z_start(9)
    sides()
    dw(5)
    offer(5)
    dw(6)
    offer(6)
    dw(7)
    z_mix(10)
    offer(7)
    dw(8)
    relay(5)
    offer(8)
    extra_b()
    conv_back_range(0, 3, 10)
    relay(6)
    conv_back_range(3, 6, 10)
    relay(7)
    conv_back_range(6, 9, 10)
    collect(5)
    back_b_first()
    relay(8)
    z_mix(9)
    back_b_second()
    lower()
    conv_back_range(0, 3, 0)
    collect(6)
    take()
    extra_a()
    offer(4)
    collect(7)
    dw(0)
    z_mix(5)
    offer(0)
    dw(1)
    offer(1)
    dw(2)
    offer(2)
    dw(3)
    z_mix(6)
    collect(8)
    offer(3)
    conv_back_range(3, 6, 0)
    last(10)
    relay(4)
    relay(0)
    z_mix(7)
    conv_back_range(6, 9, 0)
    last(9)
    relay(1)
    relay(2)
    z_mix(8)
    back_a_first()
    relay(3)
    relay(10)
    modulation()
    last(5)
    back_a_second()
    collect(4)
    last(6)
    vec_first()
    z_mix(4)
    mod_out()
    last(7)
    class_out()
    last(8)
    vec_second()
    collect(0)
    relay(9)
    z_mix(0)
    last(4)
    collect(1)
    z_mix(1)
    last(0)
    collect(2)
    last(1)
    z_mix(2)
    collect(3)
    collect(10)
    last(2)
    collect(9)
    z_mix(3)
    last(3)

    for k in range(7):
        op_copy(k).wait_send()
    stage_copy().wait_send()
    image_copy().wait()

    def drain(i):
        for part in range(2):
            x_copy(i, part).wait_send()
            y_copy(i, part).wait_send()
        z_drain(i)
        e_copy(i, 0).wait()
        e_own(i, 0).wait()

    each(FAR, drain)
    drain(9)
    drain(10)


def run_backward(whole, turned, right, grad_low, grad_resid, conv_out, slopes, images, stats, vecs, mod, sums, pre, ids, modw, classes):
    n_dp, n_head = lax.axis_size("dp"), lax.axis_size("head")
    _, _, lines, _, rows, depth = whole.shape
    cols = depth // n_head
    wide = 2 * cols
    board = (RES, SLOTS, RES, C)
    shape = jax.ShapeDtypeStruct
    return pl.pallas_call(
        functools.partial(backward_kernel, lines),
        out_shape=(
            shape((9, rows, cols), F32),
            shape((9, rows, cols), F32),
            shape((3, rows, cols), F32),
            shape((rows, cols), F32),
            shape((ALL, C), F32),
            shape((rows // n_head, classes), F32),
            shape((rows // n_head, 2, C), F32),
            shape((2, rows // n_head), F32),
            shape((16, cols), F32),
        ),
        in_specs=[ANY] * 8 + [VMEM] * 7,
        out_specs=(ANY,) * 5 + (VMEM,) * 4,
        scratch_shapes=[
            pltpu.VMEM((PAIRS, lines, 2, rows, depth), BF16),
            pltpu.VMEM((FAR, lines + lines // 2, rows, wide), BF16),
            pltpu.VMEM((FAR, lines + lines // 2, rows, wide), BF16),
            pltpu.VMEM((FAR, 4, rows, wide), BF16),
            pltpu.VMEM((PAIRS - FAR, rows + rows // 2, wide), BF16),
            pltpu.VMEM((PAIRS - FAR, rows + rows // 2, wide), BF16),
            pltpu.VMEM((PAIRS - FAR, 4, 2, rows, depth), BF16),
            pltpu.VMEM((2, PAIRS, rows, cols), F32),
            pltpu.VMEM((128, 2 * C), BF16),
            pltpu.VMEM((4, C, 2 * ALL), BF16),
            pltpu.VMEM((2, 2 * ALL, C), BF16),
            pltpu.VMEM((3, 2, ALL + 2 * LINE, C), BF16),
            pltpu.VMEM((ALL, C), BF16),
            pltpu.VMEM((2, lines, 2, rows, depth), BF16),
            pltpu.VMEM(board, F32),
            pltpu.VMEM(board, F32),
            pltpu.VMEM(board, F32),
            pltpu.VMEM((ALL, C), F32),
            pltpu.VMEM((ALL, C), BF16),
            pltpu.VMEM((16, C), F32),
            pltpu.VMEM((2 * SLOTS, C), F32),
            pltpu.VMEM((3 * SLOTS, C), F32),
            pltpu.VMEM((2 * SLOTS, C), BF16),
            pltpu.VMEM((n_dp, 2 * SLOTS, C), BF16),
            pltpu.VMEM((n_head, rows // n_head + 8, 2 * C), F32),
            pltpu.VMEM((n_head - 1, rows // n_head + 8, 2 * C), F32),
            pltpu.VMEM((n_head, n_dp * SLOTS, 128), F32),
            pltpu.VMEM((n_head, 16, cols), F32),
            pltpu.VMEM((n_head - 1, 16, cols), F32),
            pltpu.VMEM((16, cols), F32),
            pltpu.VMEM((n_dp, 16, cols), F32),
            DMA((PAIRS, 2)),
            DMA((PAIRS, 2)),
            DMA((PAIRS, 2)),
            DMA((PAIRS, 2)),
            DMA((PAIRS, lines - 1)),
            DMA((PAIRS, lines - 1)),
            DMA((PAIRS,)),
            DMA((PAIRS,)),
            DMA((PAIRS,)),
            DMA((PAIRS,)),
            DMA((PAIRS,)),
            DMA((8,)),
            DMA((8,)),
            DMA((7,)),
            DMA((2,)),
            DMA((5,)),
            DMA,
            DMA((n_dp - 1,)),
            DMA((n_dp - 1,)),
            DMA((n_head - 1,)),
            DMA((n_head - 1,)),
            DMA((n_head - 1,)),
            DMA((n_head - 1,)),
            DMA((n_head - 1,)),
            DMA((n_head - 1,)),
            DMA((n_dp - 1,)),
            DMA((n_dp - 1,)),
        ],
        compiler_params=pltpu.CompilerParams(
            collective_id=1, has_side_effects=True, vmem_limit_bytes=64 * 2**20 - 2**18
        ),
        name="backward_scatter",
    )(whole, turned, right, grad_low, grad_resid, conv_out, slopes, images, stats, vecs, mod, sums, pre, ids, modw)


def results_kernel(count, *refs):
    sources, vec_ref, refs = refs[:count], refs[count], refs[count + 1 :]
    targets, vectors, sems = refs[:count], refs[count:-1], refs[-1]
    copies = [
        pltpu.make_async_copy(source, target, sems.at[k])
        for k, (source, target) in enumerate(zip(sources, targets))
    ]
    for copy in copies:
        copy.start()
    for k, ref in enumerate(vectors):
        ref[...] = vec_ref[k].reshape(ref.shape)
    for copy in copies:
        copy.wait()


def run_results(arrays, vec):
    count = len(arrays)
    shape = jax.ShapeDtypeStruct
    return pl.pallas_call(
        functools.partial(results_kernel, count),
        out_shape=tuple(shape(one.shape, one.dtype) for one in arrays)
        + (shape(vec.shape[1:], F32),) * VECTORS,
        in_specs=[ANY] * count + [VMEM],
        out_specs=(ANY,) * count + (VMEM,) * VECTORS,
        scratch_shapes=[DMA((count,))],
        compiler_params=pltpu.CompilerParams(vmem_limit_bytes=60 * 2**20),
        name="results",
    )(*arrays, vec)


def direct(rows, cols):
    n_dp, n_head = lax.axis_size("dp"), lax.axis_size("head")
    return n_head == 4 and n_dp == 8 and rows % 32 == 0 and cols % 64 == 0


def fast_shards(
    images,
    cotangent,
    counts,
    labels,
    levels,
    noise_table,
    class_table,
    gain_a,
    shift_a,
    conv_a,
    bias_a,
    mod_weight,
    mod_bias,
    gain_b,
    shift_b,
    conv_b,
    bias_b,
    gain_c,
    shift_c,
    qkv_weight,
    proj_weight,
    proj_bias,
):
    weights = (
        jnp.swapaxes(conv_a, 0, 1),
        jnp.swapaxes(conv_b, 0, 1),
        jnp.swapaxes(qkv_weight, 0, 1),
        proj_weight,
    )
    vectors = (gain_a, shift_a, bias_a, gain_b, shift_b, bias_b, gain_c, shift_c, proj_bias)
    modw = mod_weight.reshape(mod_weight.shape[0], 2 * C)
    flat = images.reshape(ALL, C)
    (
        whole,
        conv_out,
        slopes,
        turned,
        block_out,
        grad_resid,
        grad_low,
        right,
        vecs,
        mod,
        stats,
        pre,
        all_ids,
        sums,
    ) = run_forward(
        weights,
        flat,
        cotangent.reshape(ALL, C),
        counts,
        labels,
        levels,
        class_table.T,
        noise_table,
        modw,
        mod_bias,
        vectors,
    )
    *arrays, vec = run_backward(
        whole,
        turned,
        right,
        grad_low,
        grad_resid,
        conv_out,
        slopes,
        flat,
        stats,
        vecs,
        mod,
        sums,
        pre,
        all_ids,
        modw,
        class_table.shape[0],
    )
    block_out, conva, convb, qkvw, projw, image_grad, class_grad, modw_grad, modb_grad, *rest = run_results(
        (block_out, *arrays), vec
    )
    gaina, shifta, biasa, gainb, shiftb, biasb, gainc, shiftc, projb = rest
    return (
        block_out.reshape(images.shape),
        image_grad.reshape(images.shape),
        class_grad.T,
        gaina,
        shifta,
        jnp.swapaxes(conva, 0, 1),
        biasa,
        modw_grad,
        modb_grad,
        gainb,
        shiftb,
        jnp.swapaxes(convb, 0, 1),
        biasb,
        gainc,
        shiftc,
        jnp.swapaxes(qkvw, 0, 1),
        projw,
        projb,
    )


def shards(*args):
    rows, _, cols = args[9].shape
    if direct(rows, cols):
        return fast_shards(*args)
    return plain_shards(*args)


def solution(mesh):
    placed = (
        P(("dp", "head"), None, None, None),
        P(("dp", "head"), None, None, None),
        P(),
        P(("dp", "head")),
        P(("dp", "head")),
        P(),
        P(None, "dp"),
        P("head"),
        P("head"),
        P("dp", None, "head"),
        P("head"),
        P("dp", None, None),
        P(),
        P("head"),
        P("head"),
        P("dp", None, "head"),
        P("head"),
        P("head"),
        P("head"),
        P("dp", None, "head"),
        P("dp", "head"),
        P("head"),
    )
    return jax.shard_map(
        shards,
        mesh=mesh,
        in_specs=placed,
        out_specs=(
            P(("dp", "head"), None, None, None),
            P(("dp", "head"), None, None, None),
            P(None, ("dp", "head")),
            P("head"),
            P("head"),
            P("dp", None, "head"),
            P("head"),
            P(("dp", "head"), None, None),
            P(None, ("dp", "head")),
            P("head"),
            P("head"),
            P("dp", None, "head"),
            P("head"),
            P("head"),
            P("head"),
            P("dp", None, "head"),
            P("dp", "head"),
            P("head"),
        ),
        check_vma=False,
    )
```

```python
import functools

import jax
import jax.numpy as jnp
from jax import lax
from jax.experimental import pallas as pl
from jax.experimental.pallas import tpu as pltpu
from jax.sharding import PartitionSpec as P

C = 768
DH = 64
GROUPS = 32


EPSILON = 1e-05
HIGHEST = lax.Precision.HIGHEST


def norm_forward(values, gain, shift):
    count, chans = (values.shape[0], values.shape[-1])
    span = C // GROUPS
    grouped = values.reshape(count, -1, chans // span, span)
    mean = jnp.mean(grouped, axis=(1, 3), keepdims=True)
    centred = grouped - mean
    inverse = lax.rsqrt(jnp.mean(centred * centred, axis=(1, 3), keepdims=True) + EPSILON)
    normed = (centred * inverse).reshape(values.shape)
    return (normed * gain + shift, normed, inverse)


def norm_backward(grad_out, normed, inverse, gain):
    grad_gain = jnp.sum(grad_out * normed, axis=(0, 1, 2))
    grad_shift = jnp.sum(grad_out, axis=(0, 1, 2))
    count, chans = (grad_out.shape[0], grad_out.shape[-1])
    span = C // GROUPS
    layout = (count, -1, chans // span, span)
    grad_normed = (grad_out * gain).reshape(layout)
    normed_groups = normed.reshape(layout)
    mean_one = jnp.mean(grad_normed, axis=(1, 3), keepdims=True)
    mean_two = jnp.mean(grad_normed * normed_groups, axis=(1, 3), keepdims=True)
    grad_in = inverse * (grad_normed - mean_one - normed_groups * mean_two)
    return (grad_in.reshape(grad_out.shape), grad_gain, grad_shift)


def silu_slope(values):
    sigma = jax.nn.sigmoid(values)
    return sigma * (1.0 + values * (1.0 - sigma))


def patches_of(act):
    count, rows, cols, chans = act.shape
    padded = jnp.pad(act, ((0, 0), (1, 1), (1, 1), (0, 0)))
    taps = [padded[:, i : i + rows, j : j + cols, :] for i in range(3) for j in range(3)]
    return jnp.stack(taps, axis=3).reshape(count * rows * cols, 9, chans)


def contract_rows(left, right):
    return lax.dot_general(
        left, right, (((0,), (0,)), ((), ())), preferred_element_type=jnp.float32
    )


def contract_cols(left, right):
    return lax.dot_general(
        left, right, (((1,), (1,)), ((), ())), preferred_element_type=jnp.float32
    )


def conv_back(grad_low, weight, count, rows, cols):
    chans = weight.shape[0]
    padded = jnp.zeros((count, rows + 2, cols + 2, chans), jnp.float32)
    for tap in range(9):
        i, j = divmod(tap, 3)
        part = contract_cols(grad_low, weight[:, tap, :]).reshape(count, rows, cols, chans)
        padded = padded.at[:, i : i + rows, j : j + cols, :].add(part)
    return padded[:, 1 : rows + 1, 1 : cols + 1, :]


def keep_same(values):
    return values


def live_rows(counts, first, number, count):
    sums = jnp.sum(counts, axis=1)
    chosen = lax.dynamic_slice_in_dim(sums, first, number)
    slots = lax.iota(jnp.int32, count)
    return (slots[None, :] < chosen[:, None]).astype(jnp.float32).reshape(number * count)


def residual_forward(source, mod_pair, weights, spread):
    (
        conv_one,
        conv_two,
        gain_one,
        shift_one,
        bias_one,
        gain_two,
        shift_two,
        bias_two,
        gain_three,
        shift_three,
    ) = weights
    out_a, normed_a, inverse_a = norm_forward(source, gain_one, shift_one)
    wide_a = spread(jax.nn.silu(out_a).astype(jnp.bfloat16))
    conv_out_a = (
        jnp.einsum("ptc,cto->po", patches_of(wide_a), conv_one, preferred_element_type=jnp.float32)
        + bias_one
    ).reshape(source.shape)
    scale = mod_pair[:, :, 0:1, :]
    offset = mod_pair[:, :, 1:2, :]
    out_b, normed_b, inverse_b = norm_forward(conv_out_a, gain_two, shift_two)
    inner_b = offset + out_b * (scale + 1.0)
    wide_b = spread(jax.nn.silu(inner_b).astype(jnp.bfloat16))
    conv_out_b = (
        jnp.einsum("ptc,cto->po", patches_of(wide_b), conv_two, preferred_element_type=jnp.float32)
        + bias_two
    ).reshape(source.shape)
    resid = source + conv_out_b
    out_c, normed_c, inverse_c = norm_forward(resid, gain_three, shift_three)
    attn_in = out_c.astype(jnp.bfloat16)
    saved = (
        out_a,
        normed_a,
        inverse_a,
        wide_a,
        out_b,
        normed_b,
        inverse_b,
        inner_b,
        wide_b,
        normed_c,
        inverse_c,
        scale,
    )
    return (resid, attn_in, saved)


def residual_backward(grad_attn, grad_out, saved, weights, reduce_value):
    conv_one, conv_two, gain_one, gain_two, gain_three = (
        weights[0],
        weights[1],
        weights[2],
        weights[5],
        weights[8],
    )
    (
        out_a,
        normed_a,
        inverse_a,
        wide_a,
        out_b,
        normed_b,
        inverse_b,
        inner_b,
        wide_b,
        normed_c,
        inverse_c,
        scale,
    ) = saved
    count, rows, cols, local = grad_out.shape
    grad_resid_c, gainc_term, shiftc_term = norm_backward(
        grad_attn, normed_c, inverse_c, gain_three
    )
    grad_resid = grad_out + grad_resid_c
    grad_conv_b = grad_resid.reshape(-1, local).astype(jnp.bfloat16)
    biasb_term = jnp.sum(grad_conv_b.astype(jnp.float32), axis=0)
    convb_term = jnp.einsum(
        "ptc,po->cto", patches_of(wide_b), grad_conv_b, preferred_element_type=jnp.float32
    )
    grad_act_b = reduce_value(conv_back(grad_conv_b, conv_two, count, rows, cols))
    grad_inner = grad_act_b * silu_slope(inner_b)
    grad_offset = jnp.sum(grad_inner, axis=(1, 2))
    grad_scale = jnp.sum(grad_inner * out_b, axis=(1, 2))
    grad_mod = jnp.stack([grad_scale, grad_offset], axis=1)[:, None]
    grad_conv_full, gainb_term, shiftb_term = norm_backward(
        grad_inner * (scale + 1.0), normed_b, inverse_b, gain_two
    )
    grad_conv_a = grad_conv_full.reshape(-1, local).astype(jnp.bfloat16)
    biasa_term = jnp.sum(grad_conv_a.astype(jnp.float32), axis=0)
    conva_term = jnp.einsum(
        "ptc,po->cto", patches_of(wide_a), grad_conv_a, preferred_element_type=jnp.float32
    )
    grad_act_a = reduce_value(conv_back(grad_conv_a, conv_one, count, rows, cols))
    grad_source, gaina_term, shifta_term = norm_backward(
        grad_act_a * silu_slope(out_a), normed_a, inverse_a, gain_one
    )
    image_grad = grad_resid + grad_source
    vectors = (
        gaina_term,
        shifta_term,
        biasa_term,
        gainb_term,
        shiftb_term,
        biasb_term,
        gainc_term,
        shiftc_term,
    )
    return (image_grad, grad_mod, (conva_term, convb_term), vectors)


def attend_forward(block):
    query, key, value = (block[:, :, 0], block[:, :, 1], block[:, :, 2])
    batch, pixels, heads_here, depth = query.shape
    scores = jnp.einsum("bqhd,bkhd->bhqk", query, key, preferred_element_type=jnp.float32) * DH ** (
        -0.5
    )
    top = jnp.max(scores, axis=-1, keepdims=True)
    weights = jnp.exp(scores - top)
    sums = jnp.sum(weights, axis=-1, keepdims=True)
    probs = (weights / sums).astype(jnp.bfloat16)
    logsum = (top + jnp.log(sums))[..., 0]
    mixed = jnp.einsum("bhqk,bkhd->bqhd", probs, value, preferred_element_type=jnp.float32).astype(
        jnp.bfloat16
    )
    return (mixed.reshape(batch, pixels, heads_here * depth), logsum)


def attend_backward(block, logsum, grad_head):
    query, key, value = (block[:, :, 0], block[:, :, 1], block[:, :, 2])
    batch, pixels, heads_here, depth = query.shape
    factor = DH ** (-0.5)
    scores = jnp.einsum("bqhd,bkhd->bhqk", query, key, preferred_element_type=jnp.float32) * factor
    probs = jnp.exp(scores - logsum[..., None])
    grad_value = jnp.einsum(
        "bhqk,bqhd->bkhd", probs.astype(jnp.bfloat16), grad_head, preferred_element_type=jnp.float32
    )
    grad_probs = jnp.einsum("bqhd,bkhd->bhqk", grad_head, value, preferred_element_type=jnp.float32)
    inner = jnp.sum(grad_probs * probs, axis=-1, keepdims=True)
    grad_scores = (probs * (grad_probs - inner)).astype(jnp.bfloat16)
    grad_query = (
        jnp.einsum("bhqk,bkhd->bqhd", grad_scores, key, preferred_element_type=jnp.float32) * factor
    )
    grad_key = (
        jnp.einsum("bhqk,bqhd->bkhd", grad_scores, query, preferred_element_type=jnp.float32)
        * factor
    )
    stacked = jnp.stack([grad_query, grad_key, grad_value], axis=2).astype(jnp.bfloat16)
    return stacked.reshape(batch, pixels, 3, heads_here * depth)


def plain_shards(
    images,
    cotangent,
    counts,
    labels,
    levels,
    noise_table,
    class_table,
    gain_a,
    shift_a,
    conv_a,
    bias_a,
    mod_weight,
    mod_bias,
    gain_b,
    shift_b,
    conv_b,
    bias_b,
    gain_c,
    shift_c,
    qkv_weight,
    proj_weight,
    proj_bias,
):
    rows_a, rows_b, rows_qkv, rows_proj, mod_full, class_full = (
        lax.all_gather(conv_a, "dp", axis=0, tiled=True),
        lax.all_gather(conv_b, "dp", axis=0, tiled=True),
        lax.all_gather(qkv_weight, "dp", axis=0, tiled=True),
        lax.all_gather(proj_weight, "dp", axis=0, tiled=True),
        lax.all_gather(mod_weight, "dp", axis=0, tiled=True),
        lax.all_gather(class_table, "dp", axis=1, tiled=True),
    )
    count, rows, cols, channels = images.shape
    pixels = rows * cols
    groups_n = lax.axis_size("head")
    quarter = channels // groups_n
    heads_local = quarter // DH
    first_dp = lax.axis_index("dp") * groups_n
    class_hot = (labels[:, None] == lax.iota(jnp.int32, class_full.shape[0])[None, :]).astype(
        jnp.bfloat16
    )
    level_hot = (levels[:, None] == lax.iota(jnp.int32, noise_table.shape[0])[None, :]).astype(
        jnp.bfloat16
    )
    embed_pre = jnp.dot(class_hot, class_full, preferred_element_type=jnp.float32) + jnp.dot(
        level_hot, noise_table, preferred_element_type=jnp.float32
    )
    embed = jax.nn.silu(embed_pre).astype(jnp.bfloat16)
    modulation = (
        jnp.einsum("ne,etc->ntc", embed, mod_full, preferred_element_type=jnp.float32)
        + mod_bias.astype(jnp.float32)
    ).astype(jnp.bfloat16)
    mod_pair = modulation.reshape(count, 1, 2, channels)
    (
        conv_one,
        conv_two,
        qkv_full,
        proj_full,
        gain_one,
        shift_one,
        bias_one,
        gain_two,
        shift_two,
        bias_two,
        gain_three,
        shift_three,
        bias_three,
    ) = (
        lax.all_gather(rows_a, "head", axis=2, tiled=True),
        lax.all_gather(rows_b, "head", axis=2, tiled=True),
        lax.all_gather(rows_qkv, "head", axis=2, tiled=True),
        lax.all_gather(rows_proj, "head", axis=1, tiled=True),
        lax.all_gather(gain_a, "head", axis=0, tiled=True),
        lax.all_gather(shift_a, "head", axis=0, tiled=True),
        lax.all_gather(bias_a, "head", axis=0, tiled=True),
        lax.all_gather(gain_b, "head", axis=0, tiled=True),
        lax.all_gather(shift_b, "head", axis=0, tiled=True),
        lax.all_gather(bias_b, "head", axis=0, tiled=True),
        lax.all_gather(gain_c, "head", axis=0, tiled=True),
        lax.all_gather(shift_c, "head", axis=0, tiled=True),
        lax.all_gather(proj_bias, "head", axis=0, tiled=True),
    )
    weights = (
        conv_one,
        conv_two,
        gain_one,
        shift_one,
        bias_one,
        gain_two,
        shift_two,
        bias_two,
        gain_three,
        shift_three,
    )
    live = live_rows(counts, first_dp + lax.axis_index("head"), 1, count)
    total = count * pixels
    width = channels // groups_n
    source = images.astype(jnp.float32)
    resid, attn_in, saved = residual_forward(
        source, mod_pair.astype(jnp.float32), weights, keep_same
    )
    attn_flat = attn_in.reshape(total, channels)
    qkv_flat = qkv_full.reshape(channels, 3 * channels)
    qkv = jnp.dot(attn_flat, qkv_flat, preferred_element_type=jnp.float32).astype(jnp.bfloat16)
    packed = qkv.reshape(1, count, pixels, 3, groups_n, width)
    block = lax.all_to_all(packed, "head", split_axis=4, concat_axis=0, tiled=True)
    groups = block.shape[0]
    items = block.shape[1]
    flat = block.reshape(groups * items, pixels, 3, heads_local, DH)
    mixed, logsum = attend_forward(flat)
    mixed = mixed.reshape(groups, items, pixels, 1, width)
    returned = lax.all_to_all(mixed, "head", split_axis=0, concat_axis=3, tiled=True)
    returned, logsum, kept = (returned, logsum.reshape(groups, items, heads_local, pixels), block)
    mixed_image = returned.reshape(total, channels)
    result = (
        resid.reshape(total, channels)
        + jnp.dot(mixed_image, proj_full, preferred_element_type=jnp.float32)
        + bias_three
    )
    block_out = (result.reshape(images.shape) * live[:, None, None, None]).astype(jnp.bfloat16)
    grad_out = cotangent.astype(jnp.float32) * live[:, None, None, None]
    grad_flat = grad_out.reshape(total, channels)
    grad_low = grad_flat.astype(jnp.bfloat16)
    projw_full = contract_rows(mixed_image, grad_low)
    projb_full = jnp.sum(grad_flat, axis=0)
    grad_mixed = contract_cols(grad_low, proj_full).astype(jnp.bfloat16)
    arrived = lax.all_to_all(
        grad_mixed.reshape(1, count, pixels, groups_n, width),
        "head",
        split_axis=3,
        concat_axis=0,
        tiled=True,
    )
    flat_block = kept.reshape(groups_n * count, pixels, 3, heads_local, DH)
    grad_head = arrived.reshape(groups_n * count, pixels, heads_local, DH)
    stacked = attend_backward(
        flat_block, logsum.reshape(groups_n * count, heads_local, pixels), grad_head
    )
    stacked = stacked.reshape(groups_n, count, pixels, 3, 1, width)
    grad_qkv = lax.all_to_all(stacked, "head", split_axis=0, concat_axis=4, tiled=True).reshape(
        total, 3 * channels
    )
    qkvw_full = contract_rows(attn_flat, grad_qkv).reshape(channels, 3, channels)
    grad_attn = contract_cols(grad_qkv, qkv_flat).reshape(images.shape)
    image_grad, grad_mod_part, conv_terms, vectors = residual_backward(
        grad_attn, grad_out, saved, weights, keep_same
    )
    (
        gaina_full,
        shifta_full,
        biasa_full,
        gainb_full,
        shiftb_full,
        biasb_full,
        gainc_full,
        shiftc_full,
    ) = vectors
    (
        conva_term,
        convb_term,
        qkvw_term,
        projw_term,
        gaina_term,
        shifta_term,
        biasa_term,
        gainb_term,
        shiftb_term,
        biasb_term,
        gainc_term,
        shiftc_term,
        projb_term,
    ) = (
        lax.psum_scatter(
            conv_terms[0].astype(jnp.bfloat16), "head", scatter_dimension=2, tiled=True
        ).astype(jnp.float32),
        lax.psum_scatter(
            conv_terms[1].astype(jnp.bfloat16), "head", scatter_dimension=2, tiled=True
        ).astype(jnp.float32),
        lax.psum_scatter(
            qkvw_full.astype(jnp.bfloat16), "head", scatter_dimension=2, tiled=True
        ).astype(jnp.float32),
        lax.psum_scatter(
            projw_full.astype(jnp.bfloat16), "head", scatter_dimension=1, tiled=True
        ).astype(jnp.float32),
        lax.psum_scatter(
            gaina_full.astype(jnp.bfloat16), "head", scatter_dimension=0, tiled=True
        ).astype(jnp.float32),
        lax.psum_scatter(
            shifta_full.astype(jnp.bfloat16), "head", scatter_dimension=0, tiled=True
        ).astype(jnp.float32),
        lax.psum_scatter(
            biasa_full.astype(jnp.bfloat16), "head", scatter_dimension=0, tiled=True
        ).astype(jnp.float32),
        lax.psum_scatter(
            gainb_full.astype(jnp.bfloat16), "head", scatter_dimension=0, tiled=True
        ).astype(jnp.float32),
        lax.psum_scatter(
            shiftb_full.astype(jnp.bfloat16), "head", scatter_dimension=0, tiled=True
        ).astype(jnp.float32),
        lax.psum_scatter(
            biasb_full.astype(jnp.bfloat16), "head", scatter_dimension=0, tiled=True
        ).astype(jnp.float32),
        lax.psum_scatter(
            gainc_full.astype(jnp.bfloat16), "head", scatter_dimension=0, tiled=True
        ).astype(jnp.float32),
        lax.psum_scatter(
            shiftc_full.astype(jnp.bfloat16), "head", scatter_dimension=0, tiled=True
        ).astype(jnp.float32),
        lax.psum_scatter(
            projb_full.astype(jnp.bfloat16), "head", scatter_dimension=0, tiled=True
        ).astype(jnp.float32),
    )
    grad_mod = grad_mod_part.reshape(count, 2, channels)
    modw_term = jnp.einsum("ne,ntc->etc", embed.astype(jnp.float32), grad_mod, precision=HIGHEST)
    modb_term = jnp.sum(grad_mod, axis=0)
    grad_embed = jnp.einsum(
        "ntc,etc->ne", grad_mod, mod_full.astype(jnp.float32), precision=HIGHEST
    ) * silu_slope(embed_pre)
    class_term = lax.dot_general(
        class_hot.astype(jnp.float32), grad_embed, (((0,), (0,)), ((), ())), precision=HIGHEST
    )
    modw_grad, class_grad, modb_grad = (
        lax.psum_scatter(modw_term, ("dp", "head"), scatter_dimension=0, tiled=True),
        lax.psum_scatter(class_term, ("dp", "head"), scatter_dimension=1, tiled=True),
        lax.psum_scatter(modb_term, ("dp", "head"), scatter_dimension=1, tiled=True),
    )
    conva_grad, convb_grad, qkvw_grad, projw_grad = (
        lax.psum_scatter(conva_term, "dp", scatter_dimension=0, tiled=True),
        lax.psum_scatter(convb_term, "dp", scatter_dimension=0, tiled=True),
        lax.psum_scatter(qkvw_term, "dp", scatter_dimension=0, tiled=True),
        lax.psum_scatter(projw_term, "dp", scatter_dimension=0, tiled=True),
    )
    (
        gaina_grad,
        shifta_grad,
        biasa_grad,
        gainb_grad,
        shiftb_grad,
        biasb_grad,
        gainc_grad,
        shiftc_grad,
        projb_grad,
    ) = lax.psum(
        (
            gaina_term,
            shifta_term,
            biasa_term,
            gainb_term,
            shiftb_term,
            biasb_term,
            gainc_term,
            shiftc_term,
            projb_term,
        ),
        "dp",
    )
    return (
        block_out,
        image_grad,
        class_grad,
        gaina_grad,
        shifta_grad,
        conva_grad,
        biasa_grad,
        modw_grad,
        modb_grad,
        gainb_grad,
        shiftb_grad,
        convb_grad,
        biasb_grad,
        gainc_grad,
        shiftc_grad,
        qkvw_grad,
        projw_grad,
        projb_grad,
    )


MESH = pl.DeviceIdType.MESH
UNITS = 22
PAIRS = UNITS // 2
FAR = 9
VECTORS = 9
RES = 8
SLOTS = 8
PIX = RES * RES
LINE = SLOTS * RES
ALL = RES * LINE
WIDTH = 256
F32 = jnp.float32
BF16 = jnp.bfloat16
ANY = pl.BlockSpec(memory_space=pl.ANY)
VMEM = pl.BlockSpec(memory_space=pltpu.VMEM)
SMEM = pl.BlockSpec(memory_space=pltpu.SMEM)
DMA = pltpu.SemaphoreType.DMA


def place():
    d, h = lax.axis_index("dp"), lax.axis_index("head")
    return d // 2, lax.rem(d, 2), h // 2, lax.rem(h, 2)


def at_chip(z, y, x, c):
    return (z * 2 + y, x * 2 + c)


def column_peers(n_dp):
    d, h = lax.axis_index("dp"), lax.axis_index("head")
    return [(lax.rem(d + k, n_dp), h) for k in range(1, n_dp)]


def head_peers(n_head):
    d, h = lax.axis_index("dp"), lax.axis_index("head")
    return [(d, lax.rem(h + k, n_head)) for k in range(1, n_head)]


def greet(devices):
    barrier = pltpu.get_barrier_semaphore()
    for device in devices:
        pl.semaphore_signal(barrier, inc=1, device_id=device, device_id_type=MESH)
    pl.semaphore_wait(barrier, len(devices))


def remote(src, dst, send, recv, device):
    return pltpu.make_async_remote_copy(
        src_ref=src, dst_ref=dst, send_sem=send, recv_sem=recv, device_id=device, device_id_type=MESH
    )


def each(count, body):
    def step(n, carry):
        body(n)
        return carry

    lax.fori_loop(0, count, step, 0)


def span(index, size):
    return pl.ds(pl.multiple_of(index * size, size), size)


def row(n):
    return pl.ds(n, 1)


def lines_from(i):
    return pl.ds(i * LINE if isinstance(i, int) else pl.multiple_of(i * LINE, LINE), ALL)


def dot(left, right):
    return jnp.dot(left, right, preferred_element_type=F32)


def dot_nt(left, right):
    return lax.dot_general(left, right, (((1,), (1,)), ((), ())), preferred_element_type=F32)


def dot_tn(left, right):
    return lax.dot_general(left, right, (((0,), (0,)), ((), ())), preferred_element_type=F32)


def in_group(first, second, axis):
    chan = lax.broadcasted_iota(jnp.int32, (first, second), axis)
    group = lax.broadcasted_iota(jnp.int32, (first, second), 1 - axis) * (C // GROUPS)
    inside = jnp.logical_and(chan >= group, chan < group + C // GROUPS)
    return jnp.where(inside, 1.0, 0.0).astype(BF16)


def pieces(values):
    high = values.astype(BF16).astype(F32)
    rest = values - high
    mid = rest.astype(BF16).astype(F32)
    return jnp.concatenate([high, mid, rest - mid], axis=0).astype(BF16)


def group_mean(sums):
    count = sums.shape[0]
    part = dot(pieces(sums), in_group(C, 128, 0))
    part = (part[:count] + part[count : 2 * count] + part[2 * count :]) * (1.0 / (PIX * (C // GROUPS)))
    back = dot(pieces(part), in_group(128, C, 1))
    return back[:count] + back[count : 2 * count] + back[2 * count :]


def sum_rows(values):
    return jnp.sum(values, axis=0, keepdims=True)


def norm_stats(get, mean_ref, inverse_ref, sums_ref):
    def first(n):
        sums_ref[row(n)] = sum_rows(get(n))

    each(SLOTS, first)
    mean_ref[...] = group_mean(sums_ref[...])

    def second(n):
        centred = get(n) - mean_ref[row(n)]
        sums_ref[row(n)] = sum_rows(centred * centred)

    each(SLOTS, second)
    inverse_ref[...] = lax.rsqrt(group_mean(sums_ref[...]) + EPSILON)


def silu(values):
    return values * jax.nn.sigmoid(values)


def shifted(values):
    spot = lax.rem(lax.broadcasted_iota(jnp.int32, values.shape, 0), RES)
    left = jnp.where(spot == 0, 0.0, pltpu.roll(values, 1, 0))
    right = jnp.where(spot == RES - 1, 0.0, pltpu.roll(values, values.shape[0] - 1, 0))
    return left, right


def chunk(n):
    return slice(n * WIDTH, (n + 1) * WIDTH)


CHUNKS = C // WIDTH


def weight_cols(ref, n):
    return ref[:, :, :, chunk(n)].reshape(C, WIDTH)


def weight_rows(ref, n):
    return ref[...].reshape(C, C)[chunk(n)]


def forward_kernel(
    lines,
    weights_a,
    weights_b,
    weights_qkv,
    weights_proj,
    images_hbm,
    cot_hbm,
    counts_ref,
    labels_ref,
    levels_ref,
    class_table,
    noise_table,
    modw_table,
    modb_ref,
    *refs,
):
    vectors, refs = refs[:VECTORS], refs[VECTORS:]
    forward_steps(
        lines,
        vectors,
        weights_a,
        weights_b,
        weights_qkv,
        weights_proj,
        images_hbm,
        cot_hbm,
        counts_ref,
        labels_ref,
        levels_ref,
        class_table,
        noise_table,
        modw_table,
        modb_ref,
        *refs,
    )


def forward_steps(
    lines,
    vectors,
    weights_a,
    weights_b,
    weights_qkv,
    weights_proj,
    images_hbm,
    cot_hbm,
    counts_ref,
    labels_ref,
    levels_ref,
    class_table,
    noise_table,
    modw_table,
    modb_ref,
    whole_out,
    conv_out,
    slopes_out,
    turned_out,
    block_out,
    grad_out,
    low_out,
    right_out,
    vecs_ref,
    mod_ref,
    stats_ref,
    pre_ref,
    all_ids,
    sums_out,
    halves,
    whole_ref,
    vec_ref,
    ids_ref,
    class_ref,
    modw_ref,
    vec_all,
    mod_part,
    mod_got,
    act,
    act_f32,
    sums_ref,
    conv_ref,
    resid_ref,
    slopes,
    turned,
    attn_in,
    qkv,
    right,
    low,
    pair_ref,
    pair_send,
    pair_recv,
    pair_local,
    z_send,
    z_recv,
    p_send,
    x_send,
    x_recv,
    y_send,
    y_recv,
    s_send,
    s_recv,
    vec_send,
    vec_recv,
    ids_send,
    ids_recv,
    mod_send,
    mod_recv,
    unit_sem,
    flush_sem,
    in_sem,
):
    z, y, x, c = place()
    d, h = lax.axis_index("dp"), lax.axis_index("head")
    n_dp, n_head = lines * 2, 4
    half = lines // 2
    inner = jnp.logical_and(z > 0, z < lines - 1)
    far = at_chip(lax.rem(3 * z + 1, lines), y, x, c)
    rows, cols_own = halves.shape[2:]
    wide = 2 * cols_own
    sibling = at_chip(z, y, x, 1 - c)
    along_x = at_chip(z, y, 1 - x, c)
    along_y = at_chip(z, 1 - y, x, c)
    line = [at_chip(lax.rem(z + k, lines), y, x, c) for k in range(1, lines)]
    column, heads = column_peers(n_dp), head_peers(n_head)
    greet(column + heads)

    def spot(i, cc, zz, yy, xx):
        return whole_ref.at[i, cc, zz, yy, :, span(xx, wide)]

    def parts_of(core):
        return (
            (weights_a.at[pl.ds(4 * core, 4)], pl.ds(0, 4)),
            (weights_b.at[pl.ds(4 * core, 4)], pl.ds(5, 4)),
            (weights_qkv.at[pl.ds(core, 1)], pl.ds(9, 1)),
        )

    last_parts = (
        ((weights_a.at[8], 4), (weights_qkv.at[2], 10)),
        ((weights_b.at[8], 4), (weights_proj, 10)),
    )

    def keep_copy(k):
        source, where = parts_of(c)[k]
        return pltpu.make_async_copy(source, halves.at[c, where], pair_local.at[k])

    def swap_copy(k):
        source, where = parts_of(1 - c)[k]
        return remote(source, halves.at[c, where], pair_send.at[k], pair_recv.at[k], sibling)

    def last_keep(core, k):
        source, where = last_parts[core][k]
        return pltpu.make_async_copy(source, halves.at[c, where], pair_local.at[3 + k])

    def last_swap(core, k):
        source, where = last_parts[core][k]
        return remote(source, halves.at[c, where], pair_send.at[3 + k], pair_recv.at[3 + k], sibling)

    def swap_start():
        for k in range(3):
            swap_copy(k).start()
            keep_copy(k).start()
        for core in range(2):

            @pl.when(c == core)
            def _():
                for k in range(2):
                    last_swap(1 - core, k).start()
                    last_keep(core, k).start()

    def swap_wait(k):
        if k < 3:
            keep_copy(k).wait()
            swap_copy(k).wait()
        else:
            last_keep(0, k - 3).wait()
            last_swap(0, k - 3).wait()

    def images_copy():
        return pltpu.make_async_copy(images_hbm, images_ref, in_sem.at[0])

    def cot_copy():
        return pltpu.make_async_copy(cot_hbm, cot_ref, in_sem.at[1])

    images_ref, cot_ref = attn_in, low

    def vec_copy(k):
        return remote(vec_ref, vec_all.at[h], vec_send.at[k], vec_recv.at[k], heads[k])

    def ids_copy(k):
        return remote(ids_ref, all_ids.at[d], ids_send.at[k], ids_recv.at[k], column[k])

    def mod_copy(k):
        return remote(
            mod_part.at[lax.rem(d + k + 1, n_dp)], mod_got.at[d], mod_send.at[k], mod_recv.at[k], column[k]
        )

    def z_part(i, zz):
        if isinstance(i, int) and i >= FAR:
            return whole_ref.at[i, c, zz]
        return spot(i, c, zz, y, x)

    def z_copy(i, k):
        ref = z_part(i, z)
        return remote(ref, ref, z_send.at[i, k], z_recv.at[i, k], line[k])

    def z_pass(i):
        ref = z_part(i, lax.rem(z + 2, lines))
        return remote(ref, ref, p_send.at[i], z_recv.at[i, lax.rem(2 * z + 2, lines)], far)

    def z_start(i):
        z_copy(i, 1).start()

        @pl.when(z != lines - 1)
        def _():
            z_copy(i, 0).start()

        @pl.when(z != 0)
        def _():
            z_copy(i, 2).start()

    def z_relay(i):
        z_copy(i, 1).wait_recv()

        @pl.when(inner)
        def _():
            z_pass(i).start()

    def z_finish(i):
        z_copy(i, 0).wait_recv()
        z_copy(i, 2).wait_recv()

    def z_drain(i):
        z_copy(i, 1).wait_send()

        @pl.when(z != lines - 1)
        def _():
            z_copy(i, 0).wait_send()

        @pl.when(z != 0)
        def _():
            z_copy(i, 2).wait_send()

        @pl.when(inner)
        def _():
            z_pass(i).wait_send()

    def x_copy(i, part):
        if isinstance(i, int) and i >= FAR:
            ref = spot(i, c, z, y, x) if part == 0 else spot(i, c, z, 1 - y, x).at[pl.ds(rows // 2, rows // 2)]
        elif part == 0:
            ref = spot(i, c, slice(None), y, x)
        else:
            ref = spot(i, c, pl.ds(half, half), 1 - y, x)
        return remote(ref, ref, x_send.at[i, part], x_recv.at[i, part], along_x)

    def y_copy(i, part):
        if isinstance(i, int) and i >= FAR:
            ref = spot(i, c, z, y, x) if part == 0 else spot(i, c, z, y, 1 - x).at[pl.ds(0, rows // 2)]
        elif part == 0:
            ref = spot(i, c, slice(None), y, x)
        else:
            ref = spot(i, c, pl.ds(0, half), y, 1 - x)
        return remote(ref, ref, y_send.at[i, part], y_recv.at[i, part], along_y)

    def s_copy(i, part):
        if isinstance(i, int) and i >= FAR:
            ref = whole_ref.at[i, c, part]
        else:
            yy, xx = ((y, x), (y, 1 - x), (1 - y, x), (1 - y, 1 - x))[part]
            ref = spot(i, c, slice(None), yy, xx)
        return remote(ref, ref, s_send.at[i, part], s_recv.at[i, part], sibling)

    def join(i):
        whole_ref[i, c, z, y, :, span(x, wide)] = jnp.concatenate([halves[0, i], halves[1, i]], axis=-1)

    def begin(i):
        join(i)
        z_start(i)

    def far_begin(i):
        x_copy(i, 0).start()
        y_copy(i, 0).start()

    def far_pass(i):
        x_copy(i, 0).wait_recv()
        y_copy(i, 1).start()
        y_copy(i, 0).wait_recv()
        x_copy(i, 1).start()

    def far_line(i):
        x_copy(i, 1).wait_recv()
        y_copy(i, 1).wait_recv()
        z_start(i)

    def far_finish(i):
        z_finish(i)
        for part in range(lines):
            s_copy(i, part).start()

    def spread_line(i):
        z_finish(i)
        x_copy(i, 0).start()
        y_copy(i, 0).start()
        s_copy(i, 0).start()

    def pass_on(i):
        x_copy(i, 0).wait_recv()
        y_copy(i, 1).start()
        s_copy(i, 1).start()
        y_copy(i, 0).wait_recv()
        x_copy(i, 1).start()
        s_copy(i, 2).start()

    def finish(i):
        x_copy(i, 1).wait_recv()
        y_copy(i, 1).wait_recv()
        s_copy(i, 3).start()

    def arrived(i):
        for part in range(4):
            s_copy(i, part).wait_recv()

    def unit_copy(i):
        return pltpu.make_async_copy(whole_ref.at[i], whole_out.at[i], unit_sem.at[i])

    def fetch(i):
        arrived(i)
        if not isinstance(i, int) or i < FAR:
            unit_copy(i).start()

    def product(total, tap, i, k):
        for n in range(CHUNKS):
            value = dot(act[tap % 3, lines_from(tap // 3)], weight_cols(whole_ref.at[i, k], n))
            total[:, :, :, chunk(n)] += value.reshape(RES, SLOTS, RES, WIDTH)

    def use_pair(total, i, first):
        each(2, lambda k: product(total, i - first + 4 * k, i, k))

    flushed = (
        (conv_ref, conv_out),
        (slopes.at[0], slopes_out.at[0]),
        (slopes.at[1], slopes_out.at[1]),
        (turned.at[3], turned_out.at[3]),
        (turned.at[2], turned_out.at[2]),
        (turned.at[0], turned_out.at[0]),
        (turned.at[1], turned_out.at[1]),
        (low, block_out),
        (resid_ref, grad_out),
        (attn_in, low_out),
        (right, right_out),
    )

    def flush(k):
        return pltpu.make_async_copy(*flushed[k], flush_sem.at[k])

    def set_act(place_t):
        def by_line(yy):
            value = act_f32[yy].reshape(LINE, C)
            left, right = shifted(value)
            spot_rows = pl.ds(pl.multiple_of((yy + 1) * LINE, LINE), LINE)
            act[0, spot_rows] = left.astype(BF16)
            act[1, spot_rows] = value.astype(BF16)
            act[2, spot_rows] = right.astype(BF16)

        each(RES, by_line)

        def turn(yy):
            value = act_f32[pl.ds(2 * yy, 2)].reshape(2 * LINE, C)
            turned[place_t, :, span(yy, 2 * LINE)] = value.T.astype(BF16)

        each(RES // 2, turn)

    def activate(which, n, value):
        sigma = jax.nn.sigmoid(value)
        act_f32[:, n] = (value * sigma).reshape(RES, RES, C)
        slopes[which, :, n] = (sigma * (1.0 + value * (1.0 - sigma))).reshape(RES, RES, C)

    def norm_a():
        for k in range(n_head - 1):
            vec_copy(k).wait()
        vecs_ref[...] = jnp.concatenate([vec_all[k].astype(F32) for k in range(n_head)], axis=-1)

        images_copy().wait()

        def get(n):
            return images_ref[span(n, PIX)].astype(F32)

        mean, inverse = stats_ref.at[0], stats_ref.at[1]
        norm_stats(get, mean, inverse, sums_ref)

        def to_act(n):
            value = (get(n) - mean[row(n)]) * inverse[row(n)]
            activate(0, n, value * vecs_ref[0:1] + vecs_ref[1:2])
            conv_ref[:, n] = jnp.broadcast_to(vecs_ref[2:3].reshape(1, 1, C), (RES, RES, C))
            resid_ref[:, n] = (get(n) + vecs_ref[5:6]).reshape(RES, RES, C)

        each(SLOTS, to_act)
        set_act(3)
        flush(1).start()
        flush(3).start()

    def embed():
        for k in range(n_dp - 1):
            ids_copy(k).wait()
        ids = all_ids[...].reshape(n_dp * SLOTS, 128)
        table = class_ref.shape[1]
        label_hot = lax.broadcasted_iota(jnp.int32, (n_dp * SLOTS, table), 1) == ids[:, 0:1]
        levels = noise_table.shape[0]
        level_hot = lax.broadcasted_iota(jnp.int32, (n_dp * SLOTS, levels), 1) == ids[:, 1:2]
        pre = dot_nt(jnp.where(label_hot, 1.0, 0.0).astype(BF16), class_ref[...])
        width = class_table.shape[0]
        place_of = lax.broadcasted_iota(jnp.int32, (C, 128), 0) - d * width
        lane = lax.broadcasted_iota(jnp.int32, (C, 128), 1)
        chosen = jnp.logical_and(place_of == lane, lane < width)
        noise = dot(noise_table[...], jnp.where(chosen, 1.0, 0.0).astype(BF16)).astype(BF16)
        pre += dot(jnp.where(level_hot, 1.0, 0.0).astype(BF16), noise)
        pre_ref[...] = pre
        part = dot(silu(pre).astype(BF16), modw_ref[...])
        for k in range(n_dp):
            mine = part[k * SLOTS : (k + 1) * SLOTS]
            mod_part[k] = jnp.concatenate([mine[:, :C], mine[:, C:]], axis=0).astype(BF16)
        mod_got[d] = mod_part[d]
        for k in range(n_dp - 1):
            mod_copy(k).start()

    def norm_b():
        for k in range(n_dp - 1):
            mod_copy(k).wait()
        bias = modb_ref[...].astype(F32)
        total = jnp.concatenate([jnp.broadcast_to(bias[k : k + 1], (SLOTS, C)) for k in range(2)], axis=0)
        for k in range(n_dp):
            total += mod_got[k].astype(F32)
        mod_ref[...] = total.astype(BF16).astype(F32)

        def get(n):
            return conv_ref[:, n].reshape(PIX, C)

        mean, inverse = stats_ref.at[2], stats_ref.at[3]
        norm_stats(get, mean, inverse, sums_ref)

        def to_act(n):
            value = (get(n) - mean[row(n)]) * inverse[row(n)]
            value = value * vecs_ref[3:4] + vecs_ref[4:5]
            value = mod_ref[row(SLOTS + n)] + value * (mod_ref[row(n)] + 1.0)
            activate(1, n, value)

        each(SLOTS, to_act)
        set_act(2)
        flush(0).start()
        flush(2).start()
        flush(4).start()

    def residual(n):
        return resid_ref[:, n].reshape(PIX, C)

    def normed(n):
        return (residual(n) - stats_ref[4, row(n)]) * stats_ref[5, row(n)]

    def transpose_out(source, place_t):
        def turn(k):
            value = source[span(k, 2 * LINE)].astype(F32)
            turned[place_t, :, span(k, 2 * LINE)] = value.T.astype(BF16)

        each(ALL // (2 * LINE), turn)

    def live(n):
        slots = counts_ref[d * n_head + h, 0] + counts_ref[d * n_head + h, 1]
        return jnp.where(n < slots, 1.0, 0.0)

    def norm_c():
        cot_copy().wait()
        norm_stats(residual, stats_ref.at[4], stats_ref.at[5], sums_ref)
        sums_out[...] = jnp.zeros_like(sums_out)

        def prepare(n):
            attn_in[span(n, PIX)] = (normed(n) * vecs_ref[6:7] + vecs_ref[7:8]).astype(BF16)
            grad = cot_ref[span(n, PIX)].astype(F32) * live(n)
            right[3, span(n, PIX)] = grad.astype(BF16)
            sums_out[8:9] += sum_rows(grad)

        each(SLOTS, prepare)
        transpose_out(attn_in, 0)
        flush(5).start()

    def attention():
        unit = tuple(whole_ref.at[9 + t // 2, t % 2] for t in range(4))
        for t in range(4):
            for n in range(CHUNKS):
                if t < 3:
                    value = dot(attn_in[...], weight_cols(unit[t], n))
                else:
                    value = dot_nt(right[3], weight_rows(unit[3], n))
                qkv[t, :, chunk(n)] = value.astype(BF16)
        factor = DH ** (-0.5)
        band = lax.broadcasted_iota(jnp.int32, (PIX, WIDTH), 1) // DH
        heads_at_once = WIDTH // DH

        def stack(value):
            zero = jnp.zeros_like(value)
            return jnp.concatenate([jnp.where(band == k, value, zero) for k in range(heads_at_once)], axis=0)

        def pick(value):
            out = value[:PIX]
            for k in range(1, heads_at_once):
                out = jnp.where(band == k, value[k * PIX : (k + 1) * PIX], out)
            return out

        def attend(n):
            for b in range(CHUNKS):
                query, key, value, grad = (qkv[t, span(n, PIX), chunk(b)] for t in range(4))
                query4, grad4 = stack(query), stack(grad)
                scores = dot_nt(key, query4) * factor
                weight = jnp.exp(scores - jnp.max(scores, axis=0, keepdims=True))
                probs = weight / jnp.sum(weight, axis=0, keepdims=True)
                probs_low = probs.astype(BF16)
                low[span(n, PIX), chunk(b)] = pick(dot_tn(probs_low, value)).astype(BF16)
                grad_probs = dot_nt(value, grad4)
                inner_sum = jnp.sum(grad_probs * probs, axis=0, keepdims=True)
                grad_scores = (probs * (grad_probs - inner_sum)).astype(BF16)
                right[0, span(n, PIX), chunk(b)] = (pick(dot_tn(grad_scores, key)) * factor).astype(BF16)
                right[1, span(n, PIX), chunk(b)] = (dot(grad_scores, query4) * factor).astype(BF16)
                right[2, span(n, PIX), chunk(b)] = dot(probs_low, grad4).astype(BF16)

        each(SLOTS, attend)
        flush(10).start()
        transpose_out(low, 1)
        flush(6).start()
        for n in range(CHUNKS):
            value = dot(low[...], weight_cols(unit[3], n))
            act_f32[:, :, :, chunk(n)] = value.reshape(SLOTS, RES, RES, WIDTH)

        def finish_out(n):
            value = residual(n) + act_f32[n].reshape(PIX, C) + vecs_ref[8:9]
            low[span(n, PIX)] = (value * live(n)).astype(BF16)

        each(SLOTS, finish_out)
        flush(7).start()
        for n in range(CHUNKS):
            value = dot_nt(right[0], weight_rows(unit[0], n))
            value += dot_nt(right[1], weight_rows(unit[1], n))
            value += dot_nt(right[2], weight_rows(unit[2], n))
            act_f32[:, :, :, chunk(n)] = value.reshape(SLOTS, RES, RES, WIDTH)

        def back(n):
            grad = act_f32[n].reshape(PIX, C)
            pair_ref[row(n)] = sum_rows(grad * normed(n))
            pair_ref[row(SLOTS + n)] = sum_rows(grad)

        each(SLOTS, back)
        sums_out[6:7] = sum_rows(pair_ref[0:SLOTS])
        sums_out[7:8] = sum_rows(pair_ref[SLOTS:])
        pair_ref[...] = group_mean(pair_ref[...] * vecs_ref[6:7])

        def back_second(n):
            inverse = stats_ref[5, row(n)]
            value = act_f32[n].reshape(PIX, C) * (vecs_ref[6:7] * inverse)
            value -= normed(n) * (pair_ref[row(n)] * inverse) + pair_ref[row(SLOTS + n)] * inverse
            value += right[3, span(n, PIX)].astype(F32)
            resid_ref[:, n] = value.reshape(RES, RES, C)
            sums_out[5:6] += sum_rows(value.astype(BF16).astype(F32))

        each(SLOTS, back_second)
        flush(8).start()

        def lower(yy):
            attn_in[span(yy, LINE)] = resid_ref[yy].reshape(LINE, C).astype(BF16)

        each(RES, lower)
        flush(9).start()

    swap_start()
    images_copy().start()
    cot_copy().start()
    one = [ref[...].astype(F32).reshape(1, cols_own) for ref in vectors]
    vec_ref[...] = jnp.concatenate(one + [jnp.zeros((16 - VECTORS, cols_own), F32)], axis=0).astype(BF16)
    lane = lax.broadcasted_iota(jnp.int32, (1, 128), 1)
    for n in range(SLOTS):
        ids_ref[n : n + 1] = jnp.where(lane == 0, labels_ref[n], levels_ref[n])
    for k in range(n_head - 1):
        vec_copy(k).start()
    for k in range(n_dp - 1):
        ids_copy(k).start()
    width = class_table.shape[0]
    class_ref[...] = jnp.zeros_like(class_ref)
    class_ref[0:width, 0 : class_table.shape[1]] = class_table[...]
    modw_ref[...] = jnp.zeros_like(modw_ref)
    modw_ref[0:width] = modw_table[...]
    vec_all[h] = vec_ref[...]
    all_ids[d] = ids_ref[...]
    edge = jnp.zeros((LINE, C), BF16)
    for j in range(3):
        act[j, 0:LINE] = edge
        act[j, ALL + LINE : ALL + 2 * LINE] = edge
    for k in range(5):
        swap_wait(k)
    for i in (10, 9):
        join(i)
    begin(0)
    for i in (10, 9):
        far_begin(i)
    begin(1)
    z_relay(0)
    begin(2)
    spread_line(0)
    for i in (10, 9):
        far_pass(i)
    begin(3)
    z_relay(1)
    norm_a()
    spread_line(1)
    pass_on(0)
    begin(4)
    z_relay(2)
    embed()
    spread_line(2)
    pass_on(1)
    finish(0)
    begin(5)
    z_relay(3)
    begin(6)
    z_relay(4)
    far_line(10)
    spread_line(3)
    pass_on(2)
    finish(1)
    fetch(0)

    def body(turn, carry):
        @pl.when(turn < 6)
        def _():
            begin(turn + 3)

        @pl.when(turn == 6)
        def _():
            far_line(9)
            z_relay(10)

        z_relay(turn + 1)
        spread_line(turn)
        pass_on(turn - 1)
        finish(turn - 2)
        fetch(turn - 3)
        use_pair(conv_ref, turn - 4, 0)
        return carry

    lax.fori_loop(4, 8, body, 0)
    spread_line(8)
    pass_on(7)
    finish(6)
    fetch(5)
    product(conv_ref, 8, 4, 0)
    norm_b()
    product(resid_ref, 8, 4, 1)
    pass_on(8)
    finish(7)
    z_relay(9)
    fetch(6)
    far_finish(10)
    use_pair(resid_ref, 5, 5)
    finish(8)
    fetch(7)
    use_pair(resid_ref, 6, 5)
    fetch(8)
    use_pair(resid_ref, 7, 5)
    far_finish(9)
    use_pair(resid_ref, 8, 5)
    norm_c()
    fetch(9)
    fetch(10)
    attention()

    def drain(i):
        z_drain(i)
        for part in range(2):
            x_copy(i, part).wait_send()
            y_copy(i, part).wait_send()
        for part in range(4):
            s_copy(i, part).wait_send()

    each(FAR, drain)
    drain(9)
    drain(10)
    for k in range(len(flushed)):
        flush(k).wait()
    each(FAR, lambda i: unit_copy(i).wait())


def run_forward(weights, images, cotangent, counts, labels, levels, class_table, noise_table, modw, modb, vectors):
    n_dp, n_head = lax.axis_size("dp"), lax.axis_size("head")
    rows, cols = weights[0].shape[1:]
    lines, across, wide = n_dp // 2, n_head // 2, 2 * cols
    board = (RES, SLOTS, RES, C)
    shape = jax.ShapeDtypeStruct
    return pl.pallas_call(
        functools.partial(forward_kernel, lines),
        out_shape=(
            shape((FAR, 2, lines, 2, rows, across * wide), BF16),
            shape(board, F32),
            shape((2,) + board, F32),
            shape((4, C, ALL), BF16),
            shape((ALL, C), BF16),
            shape(board, F32),
            shape((ALL, C), BF16),
            shape((4, ALL, C), BF16),
            shape((16, C), F32),
            shape((2 * SLOTS, C), F32),
            shape((6, SLOTS, C), F32),
            shape((n_dp * SLOTS, 128), F32),
            shape((n_dp, SLOTS, 128), jnp.int32),
            shape((16, C), F32),
        ),
        in_specs=[ANY] * 6 + [SMEM] * 3 + [VMEM] * (4 + VECTORS),
        out_specs=(ANY,) * 8 + (VMEM,) * 6,
        scratch_shapes=[
            pltpu.VMEM((2, PAIRS, rows, cols), BF16),
            pltpu.VMEM((PAIRS, 2, lines, 2, rows, across * wide), BF16),
            pltpu.VMEM((16, cols), BF16),
            pltpu.VMEM((SLOTS, 128), jnp.int32),
            pltpu.VMEM((128, 1024), BF16),
            pltpu.VMEM((128, 2 * C), BF16),
            pltpu.VMEM((n_head, 16, cols), BF16),
            pltpu.VMEM((n_dp, 2 * SLOTS, C), BF16),
            pltpu.VMEM((n_dp, 2 * SLOTS, C), BF16),
            pltpu.VMEM((3, ALL + 2 * LINE, C), BF16),
            pltpu.VMEM(board, F32),
            pltpu.VMEM((SLOTS, C), F32),
            pltpu.VMEM(board, F32),
            pltpu.VMEM(board, F32),
            pltpu.VMEM((2,) + board, F32),
            pltpu.VMEM((4, C, ALL), BF16),
            pltpu.VMEM((ALL, C), BF16),
            pltpu.VMEM((4, ALL, C), BF16),
            pltpu.VMEM((4, ALL, C), BF16),
            pltpu.VMEM((ALL, C), BF16),
            pltpu.VMEM((2 * SLOTS, C), F32),
            DMA((5,)),
            DMA((5,)),
            DMA((5,)),
            DMA((PAIRS, lines - 1)),
            DMA((PAIRS, lines - 1)),
            DMA((PAIRS,)),
            DMA((PAIRS, 2)),
            DMA((PAIRS, 2)),
            DMA((PAIRS, 2)),
            DMA((PAIRS, 2)),
            DMA((PAIRS, 4)),
            DMA((PAIRS, 4)),
            DMA((n_head - 1,)),
            DMA((n_head - 1,)),
            DMA((n_dp - 1,)),
            DMA((n_dp - 1,)),
            DMA((n_dp - 1,)),
            DMA((n_dp - 1,)),
            DMA((FAR,)),
            DMA((11,)),
            DMA((2,)),
        ],
        compiler_params=pltpu.CompilerParams(
            collective_id=0, has_side_effects=True, vmem_limit_bytes=62 * 2**20
        ),
        name="gather_forward",
    )(
        *weights,
        images,
        cotangent,
        counts,
        labels,
        levels,
        class_table,
        noise_table,
        modw,
        modb,
        *vectors,
    )


def backward_kernel(
    lines,
    whole_ref,
    turned_ref,
    right_ref,
    grad_low_ref,
    grad_resid_ref,
    conv_ref,
    slopes_ref,
    images_hbm,
    stats_ref,
    vecs_ref,
    mod_ref,
    sums_in,
    pre_ref,
    ids_ref,
    modw_table,
    out_a,
    out_b,
    out_qkv,
    out_proj,
    image_ref,
    class_ref,
    modw_out,
    modb_out,
    vec_out,
    mine,
    from_x,
    from_y,
    from_z,
    far_x,
    far_y,
    far_z,
    ends,
    modw_ref,
    lefts,
    rights,
    grads,
    stage,
    weights,
    total,
    board,
    slopes,
    image_mine,
    images_ref,
    sums_ref,
    pair_ref,
    coef_ref,
    gm_mine,
    gm_all,
    mw_mine,
    mw_got,
    ge_all,
    vs_mine,
    vs_got,
    vt_mine,
    vt_all,
    x_send,
    x_recv,
    y_send,
    y_recv,
    z_send,
    z_recv,
    p_send,
    p_recv,
    e_send,
    e_recv,
    e_local,
    op_send,
    op_recv,
    op_local,
    load_sem,
    in_sem,
    out_sem,
    gm_send,
    gm_recv,
    mw_send,
    mw_recv,
    ge_send,
    ge_recv,
    vs_send,
    vs_recv,
    vt_send,
    vt_recv,
):
    z, y, x, c = place()
    d, h = lax.axis_index("dp"), lax.axis_index("head")
    n_dp, n_head = lines * 2, 4
    half = lines // 2
    inner = jnp.logical_and(z > 0, z < lines - 1)
    rows, wide = from_z.shape[2], from_z.shape[3]
    cols = wide // 2
    sibling = at_chip(z, y, x, 1 - c)
    along_x = at_chip(z, y, 1 - x, c)
    along_y = at_chip(z, 1 - y, x, c)
    line = [at_chip(lax.rem(z + k, lines), y, x, c) for k in range(1, lines)]
    column, heads = column_peers(n_dp), head_peers(n_head)

    own_rows = pl.ds(LINE, ALL)

    def operand(k):
        if k == 0:
            return right_ref.at[2 + c], right_ref.at[3 - c], rights.at[0, span(c, ALL)]
        if k == 1:
            return turned_ref.at[c], turned_ref.at[1 - c], lefts.at[1, :, span(c, ALL)]
        if k == 2:
            return right_ref.at[c], right_ref.at[1 - c], rights.at[1, span(c, ALL)]
        if k == 3:
            return turned_ref.at[0], turned_ref.at[0], lefts.at[0, :, span(c, ALL)]
        if k == 4:
            return grad_low_ref, grad_low_ref, grads.at[1, c, own_rows]
        return turned_ref.at[k - 3], turned_ref.at[k - 3], lefts.at[k - 3, :, span(c, ALL)]

    def op_own(k):
        source, _, target = operand(k)
        return pltpu.make_async_copy(source, target, op_local.at[k])

    def op_copy(k):
        _, source, target = operand(k)
        return remote(source, target, op_send.at[k], op_recv.at[k], sibling)

    def stage_copy():
        return remote(grads.at[1, c, own_rows], stage, op_send.at[7], op_recv.at[7], sibling)

    def op_wait(k):
        op_own(k).wait()
        op_copy(k).wait_recv()

    def lanes(xx):
        return span(xx, wide)

    first, second = pl.ds(0, rows // 2), pl.ds(rows // 2, rows // 2)

    def is_far(i):
        return isinstance(i, int) and i >= FAR

    def x_copy(i, part):
        if is_far(i):
            into = far_x.at[i - FAR]
            if part == 0:
                src, dst = mine.at[i, z, 1 - y, second, lanes(1 - x)], into.at[pl.ds(rows, rows // 2)]
            else:
                src, dst = mine.at[i, z, y, :, lanes(1 - x)], into.at[pl.ds(0, rows)]
        elif part == 0:
            src, dst = mine.at[i, pl.ds(half, half), 1 - y, :, lanes(1 - x)], from_x.at[i, pl.ds(lines, half)]
        else:
            src, dst = mine.at[i, :, y, :, lanes(1 - x)], from_x.at[i, pl.ds(0, lines)]
        return remote(src, dst, x_send.at[i, part], x_recv.at[i, part], along_x)

    def y_copy(i, part):
        if is_far(i):
            into = far_y.at[i - FAR]
            if part == 0:
                src, dst = mine.at[i, z, 1 - y, first, lanes(1 - x)], into.at[pl.ds(rows, rows // 2)]
            else:
                src, dst = mine.at[i, z, 1 - y, :, lanes(x)], into.at[pl.ds(0, rows)]
        elif part == 0:
            src, dst = mine.at[i, pl.ds(0, half), 1 - y, :, lanes(1 - x)], from_y.at[i, pl.ds(lines, half)]
        else:
            src, dst = mine.at[i, :, 1 - y, :, lanes(x)], from_y.at[i, pl.ds(0, lines)]
        return remote(src, dst, y_send.at[i, part], y_recv.at[i, part], along_y)

    beyond = lax.rem(z + 2, lines)
    opposite = lines - 1 - z
    near_end = at_chip(1 + z // (lines - 1), y, x, c)

    def z_block(i, zz):
        return mine.at[i, zz] if is_far(i) else mine.at[i, zz, y, :, lanes(x)]

    def z_slot(i, k):
        return far_z.at[i - FAR, k] if is_far(i) else from_z.at[i, k]

    def z_copy(i, k):
        return remote(
            z_block(i, lax.rem(z + k + 1, lines)), z_slot(i, k), z_send.at[i, k], z_recv.at[i, k], line[k]
        )

    def z_give(i):
        return remote(z_block(i, opposite), z_slot(i, 3), p_send.at[i], p_recv.at[i], near_end)

    def z_start(i):
        @pl.when(jnp.logical_not(inner))
        def _():
            z_give(i).start()

        @pl.when(z < lines - 1)
        def _():
            z_copy(i, 0).start()

        @pl.when(z > 0)
        def _():
            z_copy(i, 2).start()

        @pl.when(jnp.logical_not(inner))
        def _():
            z_copy(i, 1).start()

    def z_mix(i):
        @pl.when(inner)
        def _():
            z_give(i).wait_recv()
            if is_far(i):
                mine[i, beyond] += far_z[i - FAR, 3]
            else:
                mine[i, beyond, y, :, lanes(x)] += from_z[i, 3]
            z_copy(i, 1).start()

    def z_wait(i):
        z_copy(i, 1).wait_recv()

        @pl.when(z > 0)
        def _():
            z_copy(i, 0).wait_recv()

        @pl.when(z < lines - 1)
        def _():
            z_copy(i, 2).wait_recv()

    def z_drain(i):
        z_copy(i, 1).wait_send()

        @pl.when(z < lines - 1)
        def _():
            z_copy(i, 0).wait_send()

        @pl.when(z > 0)
        def _():
            z_copy(i, 2).wait_send()

        @pl.when(jnp.logical_not(inner))
        def _():
            z_give(i).wait_send()

    def target(i, core):
        if isinstance(i, int) and i == 10:
            return out_proj if core == 1 else out_qkv.at[2]
        if isinstance(i, int) and i == 9:
            return out_qkv.at[core]
        if isinstance(i, int) and i == 4:
            return out_b.at[8] if core == 1 else out_a.at[8]
        if isinstance(i, int) and i > 4:
            return out_b.at[4 * core + i - 5]
        return out_a.at[4 * core + i]

    def e_copy(i, core):
        return remote(ends.at[1 - c, i], target(i, core), e_send.at[i], e_recv.at[i], sibling)

    def e_own(i, core):
        return pltpu.make_async_copy(ends.at[c, i], target(i, core), e_local.at[i])

    def finish(i, value):
        for cc in range(2):
            ends[cc, i] = value[:, cc * cols : (cc + 1) * cols]
        if i in (4, 10):
            for core in range(2):

                @pl.when(c == core)
                def _():
                    e_copy(i, core).start()
                    e_own(i, core).start()
        else:
            e_copy(i, c).start()
            e_own(i, c).start()

    def offer(i):
        x_copy(i, 0).start()
        y_copy(i, 0).start()

    def relay(i):
        x_copy(i, 0).wait_recv()
        y_copy(i, 0).wait_recv()
        if is_far(i):
            rest = pl.ds(rows, rows // 2)
            mine[i, z, y, first, lanes(1 - x)] += far_y[i - FAR, rest]
            mine[i, z, 1 - y, second, lanes(x)] += far_x[i - FAR, rest]
        else:
            for j in range(half):
                mine[i, j, y, :, lanes(1 - x)] += from_y[i, lines + j]
                mine[i, half + j, 1 - y, :, lanes(x)] += from_x[i, lines + j]
        x_copy(i, 1).start()
        y_copy(i, 1).start()

    def collect(i):
        x_copy(i, 1).wait_recv()
        y_copy(i, 1).wait_recv()
        if is_far(i):
            whole_rows = pl.ds(0, rows)
            value = mine[i, z, y, :, lanes(x)].astype(F32)
            value += far_x[i - FAR, whole_rows].astype(F32) + far_y[i - FAR, whole_rows].astype(F32)
            finish(i, value)
            return

        def add(j):
            value = mine[i, j, y, :, lanes(x)].astype(F32)
            value += from_x[i, j].astype(F32) + from_y[i, j].astype(F32)
            mine[i, j, y, :, lanes(x)] = value.astype(BF16)

        each(lines, add)
        z_start(i)

    def last(i):
        z_wait(i)
        if is_far(i):
            for yy in range(2):
                value = mine[i, z, yy].astype(F32)
                for k in range(lines - 1):
                    value += far_z[i - FAR, k, yy].astype(F32)
                mine[i, z, yy] = value.astype(BF16)
            offer(i)
            return
        value = mine[i, z, y, :, lanes(x)].astype(F32)
        for k in range(lines - 1):
            value += from_z[i, k].astype(F32)
        finish(i, value)

    def put(i, n, value):
        mine[i, :, :, :, chunk(n)] = value.astype(BF16).reshape(mine.shape[1:4] + (WIDTH,))

    def plain_unit(i, left, right):
        for n in range(CHUNKS):
            put(i, n, dot(lefts[left], rights[right, :, chunk(n)]))

    def conv_unit(i, left, tap):
        where, side = lines_from(2 - tap // 3), 2 - tap % 3
        for n in range(CHUNKS):
            both = jnp.concatenate([grads[side, core, where, chunk(n)] for core in range(2)], axis=0)
            put(i, n, dot(lefts[left], both))

    def extra_b():
        @pl.when(c == 1)
        def _():
            conv_unit(4, 2, 8)

    def extra_a():
        @pl.when(c == 0)
        def _():
            conv_unit(4, 3, 8)

    def spread_sides(core):
        def by_line(yy):
            value = grads[1, core, pl.ds(pl.multiple_of((yy + 1) * LINE, LINE), LINE)].astype(F32)
            left, right = shifted(value)
            spot_rows = pl.ds(pl.multiple_of((yy + 1) * LINE, LINE), LINE)
            grads[0, core, spot_rows] = left.astype(BF16)
            grads[2, core, spot_rows] = right.astype(BF16)

        each(RES, by_line)

    def load(tap, base):
        ninth = tap // 8
        i = (base // 2 + tap % 4) * (1 - ninth) + 4 * ninth
        k = (tap // 4) % 2 + (base // 10) * ninth
        return pltpu.make_async_copy(whole_ref.at[i, k], weights.at[tap % 2], load_sem.at[tap % 2])

    def conv_back(tap, base):
        load(tap, base).wait()

        @pl.when(tap < 8)
        def _():
            load(tap + 1, base).start()

        part = grads[2 - tap % 3, c, lines_from(2 - tap // 3)]
        for n in range(CHUNKS):
            value = dot_nt(part, weight_rows(weights.at[tap % 2], n))
            total[:, :, :, chunk(n)] += value.reshape(RES, SLOTS, RES, WIDTH)

    def conv_back_range(first, stop, base):
        def body(tap, carry):
            conv_back(tap, base)
            return carry

        lax.fori_loop(first, stop, body, 0)

    def slope(values):
        sigma = jax.nn.sigmoid(values)
        return sigma * (1.0 + values * (1.0 - sigma))

    for k in (0, 2):
        from_z[:, k] = jnp.zeros_like(from_z[:, k])
        far_z[:, k] = jnp.zeros_like(far_z[:, k])
    greet(column + heads)
    def op_start(k):
        op_own(k).start()
        op_copy(k).start()

    for k in range(6):
        op_start(k)
    load(0, 10).start()

    def fetch(k):
        source, target = (
            (conv_ref, board),
            (slopes_ref.at[1], slopes),
            (slopes_ref.at[0], slopes),
            (grad_resid_ref, board),
            (images_hbm, images_ref),
        )[k]
        return pltpu.make_async_copy(source, target, in_sem.at[k])

    fetch(0).start()
    fetch(1).start()
    vs_mine[...] = jnp.zeros_like(vs_mine)
    edge = jnp.zeros((LINE, C), BF16)
    for j in range(3):
        for core in range(2):
            grads[j, core, 0:LINE] = edge
            grads[j, core, ALL + LINE : ALL + 2 * LINE] = edge
    total[...] = jnp.zeros_like(total)
    sums_ref[...] = sums_in[...]
    modw_ref[...] = jnp.zeros_like(modw_ref)
    modw_ref[0:rows] = modw_table[...]

    def norm_b_value(n):
        return (board[:, n].reshape(PIX, C) - stats_ref[2, row(n)]) * stats_ref[3, row(n)]

    def norm_a_value(n):
        return (images_ref[span(n, PIX)].astype(F32) - stats_ref[0, row(n)]) * stats_ref[1, row(n)]

    def back_sums(get):
        def body(n):
            grad = (total[:, n] * slopes[:, n]).reshape(PIX, C)
            total[:, n] = grad.reshape(RES, RES, C)
            pair_ref[row(n)] = sum_rows(grad * get(n))
            pair_ref[row(SLOTS + n)] = sum_rows(grad)

        each(SLOTS, body)

    def back_factors(factor, inverse):
        coef_ref[0:SLOTS] = factor * inverse
        means = group_mean(pair_ref[...] * jnp.concatenate([factor, factor], axis=0))
        coef_ref[SLOTS : 2 * SLOTS] = means[:SLOTS] * inverse
        coef_ref[2 * SLOTS :] = means[SLOTS:] * inverse

    def back_value(n, get):
        value = total[:, n].reshape(PIX, C) * coef_ref[row(n)]
        return value - get(n) * coef_ref[row(SLOTS + n)] - coef_ref[row(2 * SLOTS + n)]

    def gm_copy(k):
        return remote(gm_mine, gm_all.at[d], gm_send.at[k], gm_recv.at[k], column[k])

    def mw_copy(k):
        return remote(
            mw_mine.at[lax.rem(h + k + 1, n_head)], mw_got.at[k], mw_send.at[k], mw_recv.at[k], heads[k]
        )

    def ge_copy(k):
        return remote(ge_all.at[h], ge_all.at[h], ge_send.at[k], ge_recv.at[k], heads[k])

    def vs_copy(k):
        return remote(
            vs_mine.at[lax.rem(h + k + 1, n_head)], vs_got.at[k], vs_send.at[k], vs_recv.at[k], heads[k]
        )

    def vt_copy(k):
        return remote(vt_mine, vt_all.at[d], vt_send.at[k], vt_recv.at[k], column[k])

    def image_copy():
        return pltpu.make_async_copy(image_mine, image_ref, out_sem)

    count = n_dp * SLOTS

    def start():
        op_wait(0)
        op_wait(1)

    def dw(i):
        if i == 10:
            plain_unit(10, 1, 0)
        elif i == 9:
            op_wait(2)
            op_wait(3)
            plain_unit(9, 0, 1)
        elif i > 4:
            conv_unit(i, 2, 4 * c + i - 5)
        else:
            conv_unit(i, 3, 4 * c + i)

    def sides():
        op_wait(4)
        op_wait(5)
        spread_sides(0)
        spread_sides(1)

    def back_b_first():
        load(0, 0).start()
        op_start(6)
        fetch(0).wait()
        fetch(1).wait()
        back_sums(norm_b_value)
        alone, with_norm = pair_ref[SLOTS:], pair_ref[:SLOTS]
        scale = mod_ref[0:SLOTS] + 1.0
        gm_mine[...] = jnp.concatenate([vecs_ref[3:4] * with_norm + vecs_ref[4:5] * alone, alone], axis=0).astype(BF16)
        gm_all[d] = gm_mine[...]
        for k in range(n_dp - 1):
            gm_copy(k).start()
        sums_ref[3:4] = sum_rows(with_norm * scale)
        sums_ref[4:5] = sum_rows(alone * scale)
        back_factors(scale * vecs_ref[3:4], stats_ref[3])

    def back_b_second():
        fetch(2).start()
        fetch(4).start()

        def body(n):
            value = back_value(n, norm_b_value).astype(BF16).astype(F32)
            sums_ref[2:3] += sum_rows(value)
            total[:, n] = value.reshape(RES, RES, C)

        each(SLOTS, body)
        fetch(3).start()

    def lower():
        def by_line(yy):
            spot_rows = pl.ds(pl.multiple_of((yy + 1) * LINE, LINE), LINE)
            grads[1, c, spot_rows] = total[yy].reshape(LINE, C).astype(BF16)

        each(RES, by_line)
        stage_copy().start()
        spread_sides(c)
        total[...] = jnp.zeros_like(total)

    def take():
        stage_copy().wait_recv()

        def by_line(yy):
            spot_rows = pl.ds(pl.multiple_of((yy + 1) * LINE, LINE), LINE)
            grads[1, 1 - c, spot_rows] = stage[span(yy, LINE)]

        each(RES, by_line)
        spread_sides(1 - c)
        op_wait(6)

    def modulation():
        for k in range(n_dp - 1):
            gm_copy(k).wait()
        parts = gm_all[...].astype(F32)
        gm_scale = parts[:, :SLOTS].reshape(count, C)
        gm_offset = parts[:, SLOTS:].reshape(count, C)
        pre = pre_ref[...]
        emb = silu(pre).astype(BF16)
        part_rows = rows // n_head
        for k, value in ((0, gm_scale), (1, gm_offset)):
            low_value = value.astype(BF16)
            grad_w = dot_tn(emb, low_value)
            place_lanes = slice(k * C, (k + 1) * C)
            for hh in range(n_head):
                mw_mine[hh, 0:part_rows, place_lanes] = grad_w[hh * part_rows : (hh + 1) * part_rows]
                mw_mine[hh, part_rows : part_rows + 8, place_lanes] = jnp.broadcast_to(sum_rows(value), (8, C))
        grad_e = dot_nt(gm_scale.astype(BF16), modw_ref[:, :C]) + dot_nt(gm_offset.astype(BF16), modw_ref[:, C:])
        grad_e = grad_e * slope(pre)
        label = ids_ref[...].reshape(count, 128)[:, 0:1].astype(F32)
        lane = lax.broadcasted_iota(jnp.int32, grad_e.shape, 1)
        ge_all[h] = jnp.where(lane < rows, grad_e, label)
        for k in range(n_head - 1):
            mw_copy(k).start()
            ge_copy(k).start()

    def back_a_first():
        fetch(2).wait()
        fetch(4).wait()
        back_sums(norm_a_value)
        sums_ref[0:1] = sum_rows(pair_ref[:SLOTS])
        sums_ref[1:2] = sum_rows(pair_ref[SLOTS:])
        for hh in range(n_head):
            vs_mine[hh] = sums_ref[:, hh * cols : (hh + 1) * cols]
        for k in range(n_head - 1):
            vs_copy(k).start()
        back_factors(jnp.broadcast_to(vecs_ref[0:1], (SLOTS, C)), stats_ref[1])

    def back_a_second():
        fetch(3).wait()

        def body(n):
            image_mine[span(n, PIX)] = back_value(n, norm_a_value) + board[:, n].reshape(PIX, C)

        each(SLOTS, body)
        image_copy().start()

    def vec_first():
        value = vs_mine[h]
        for k in range(n_head - 1):
            vs_copy(k).wait()
            value += vs_got[k]
        vt_mine[...] = value
        vt_all[d] = value
        for k in range(n_dp - 1):
            vt_copy(k).start()

    def mod_out():
        value = mw_mine[h]
        for k in range(n_head - 1):
            mw_copy(k).wait()
            value += mw_got[k]
        part_rows = rows // n_head
        first_lane = (d * n_head + h) * part_rows
        for k in range(2):
            lanes_of = slice(k * C, (k + 1) * C)
            modw_out[:, k] = value[:part_rows, lanes_of]
            turned_row = pltpu.roll(value[part_rows:, lanes_of], lax.rem(C - first_lane, C), 1)
            modb_out[k : k + 1] = turned_row[0:1, :part_rows]

    def class_out():
        for k in range(n_head - 1):
            ge_copy(k).wait()
        table = class_ref.shape[1]
        part = rows // n_head
        value = ge_all[...].reshape(n_head * count, 128)
        label = value[:, rows : rows + 1].astype(jnp.int32)
        hot = lax.broadcasted_iota(jnp.int32, (n_head * count, table), 1) == label
        own = pltpu.roll(value, lax.rem(128 - h * part, 128), 1).astype(BF16)
        value = dot_tn(own, jnp.where(hot, 1.0, 0.0).astype(BF16))
        class_ref[...] = value[:part]

    def vec_second():
        for k in range(n_dp - 1):
            vt_copy(k).wait()
        value = vt_all[0]
        for k in range(1, n_dp):
            value += vt_all[k]
        vec_out[...] = value

    start()
    dw(10)
    z_start(10)
    dw(9)
    z_start(9)
    sides()
    dw(5)
    offer(5)
    dw(6)
    offer(6)
    dw(7)
    z_mix(10)
    offer(7)
    dw(8)
    relay(5)
    offer(8)
    extra_b()
    conv_back_range(0, 3, 10)
    relay(6)
    conv_back_range(3, 6, 10)
    relay(7)
    conv_back_range(6, 9, 10)
    collect(5)
    back_b_first()
    relay(8)
    z_mix(9)
    back_b_second()
    lower()
    conv_back_range(0, 3, 0)
    collect(6)
    take()
    extra_a()
    offer(4)
    collect(7)
    dw(0)
    z_mix(5)
    offer(0)
    dw(1)
    offer(1)
    dw(2)
    offer(2)
    dw(3)
    z_mix(6)
    collect(8)
    offer(3)
    conv_back_range(3, 6, 0)
    last(10)
    relay(4)
    relay(0)
    z_mix(7)
    conv_back_range(6, 9, 0)
    last(9)
    relay(1)
    relay(2)
    z_mix(8)
    back_a_first()
    relay(3)
    relay(10)
    modulation()
    last(5)
    back_a_second()
    collect(4)
    last(6)
    vec_first()
    z_mix(4)
    mod_out()
    last(7)
    class_out()
    last(8)
    vec_second()
    collect(0)
    relay(9)
    z_mix(0)
    last(4)
    collect(1)
    z_mix(1)
    last(0)
    collect(2)
    last(1)
    z_mix(2)
    collect(3)
    collect(10)
    last(2)
    collect(9)
    z_mix(3)
    last(3)

    for k in range(7):
        op_copy(k).wait_send()
    stage_copy().wait_send()
    image_copy().wait()

    def drain(i):
        for part in range(2):
            x_copy(i, part).wait_send()
            y_copy(i, part).wait_send()
        z_drain(i)
        e_copy(i, 0).wait()
        e_own(i, 0).wait()

    each(FAR, drain)
    drain(9)
    drain(10)


def run_backward(whole, turned, right, grad_low, grad_resid, conv_out, slopes, images, stats, vecs, mod, sums, pre, ids, modw, classes):
    n_dp, n_head = lax.axis_size("dp"), lax.axis_size("head")
    _, _, lines, _, rows, depth = whole.shape
    cols = depth // n_head
    wide = 2 * cols
    board = (RES, SLOTS, RES, C)
    shape = jax.ShapeDtypeStruct
    return pl.pallas_call(
        functools.partial(backward_kernel, lines),
        out_shape=(
            shape((9, rows, cols), F32),
            shape((9, rows, cols), F32),
            shape((3, rows, cols), F32),
            shape((rows, cols), F32),
            shape((ALL, C), F32),
            shape((rows // n_head, classes), F32),
            shape((rows // n_head, 2, C), F32),
            shape((2, rows // n_head), F32),
            shape((16, cols), F32),
        ),
        in_specs=[ANY] * 8 + [VMEM] * 7,
        out_specs=(ANY,) * 5 + (VMEM,) * 4,
        scratch_shapes=[
            pltpu.VMEM((PAIRS, lines, 2, rows, depth), BF16),
            pltpu.VMEM((FAR, lines + lines // 2, rows, wide), BF16),
            pltpu.VMEM((FAR, lines + lines // 2, rows, wide), BF16),
            pltpu.VMEM((FAR, 4, rows, wide), BF16),
            pltpu.VMEM((PAIRS - FAR, rows + rows // 2, wide), BF16),
            pltpu.VMEM((PAIRS - FAR, rows + rows // 2, wide), BF16),
            pltpu.VMEM((PAIRS - FAR, 4, 2, rows, depth), BF16),
            pltpu.VMEM((2, PAIRS, rows, cols), F32),
            pltpu.VMEM((128, 2 * C), BF16),
            pltpu.VMEM((4, C, 2 * ALL), BF16),
            pltpu.VMEM((2, 2 * ALL, C), BF16),
            pltpu.VMEM((3, 2, ALL + 2 * LINE, C), BF16),
            pltpu.VMEM((ALL, C), BF16),
            pltpu.VMEM((2, lines, 2, rows, depth), BF16),
            pltpu.VMEM(board, F32),
            pltpu.VMEM(board, F32),
            pltpu.VMEM(board, F32),
            pltpu.VMEM((ALL, C), F32),
            pltpu.VMEM((ALL, C), BF16),
            pltpu.VMEM((16, C), F32),
            pltpu.VMEM((2 * SLOTS, C), F32),
            pltpu.VMEM((3 * SLOTS, C), F32),
            pltpu.VMEM((2 * SLOTS, C), BF16),
            pltpu.VMEM((n_dp, 2 * SLOTS, C), BF16),
            pltpu.VMEM((n_head, rows // n_head + 8, 2 * C), F32),
            pltpu.VMEM((n_head - 1, rows // n_head + 8, 2 * C), F32),
            pltpu.VMEM((n_head, n_dp * SLOTS, 128), F32),
            pltpu.VMEM((n_head, 16, cols), F32),
            pltpu.VMEM((n_head - 1, 16, cols), F32),
            pltpu.VMEM((16, cols), F32),
            pltpu.VMEM((n_dp, 16, cols), F32),
            DMA((PAIRS, 2)),
            DMA((PAIRS, 2)),
            DMA((PAIRS, 2)),
            DMA((PAIRS, 2)),
            DMA((PAIRS, lines - 1)),
            DMA((PAIRS, lines - 1)),
            DMA((PAIRS,)),
            DMA((PAIRS,)),
            DMA((PAIRS,)),
            DMA((PAIRS,)),
            DMA((PAIRS,)),
            DMA((8,)),
            DMA((8,)),
            DMA((7,)),
            DMA((2,)),
            DMA((5,)),
            DMA,
            DMA((n_dp - 1,)),
            DMA((n_dp - 1,)),
            DMA((n_head - 1,)),
            DMA((n_head - 1,)),
            DMA((n_head - 1,)),
            DMA((n_head - 1,)),
            DMA((n_head - 1,)),
            DMA((n_head - 1,)),
            DMA((n_dp - 1,)),
            DMA((n_dp - 1,)),
        ],
        compiler_params=pltpu.CompilerParams(
            collective_id=1, has_side_effects=True, vmem_limit_bytes=64 * 2**20 - 2**18
        ),
        name="backward_scatter",
    )(whole, turned, right, grad_low, grad_resid, conv_out, slopes, images, stats, vecs, mod, sums, pre, ids, modw)


def results_kernel(count, *refs):
    sources, vec_ref, refs = refs[:count], refs[count], refs[count + 1 :]
    targets, vectors, sems = refs[:count], refs[count:-1], refs[-1]
    copies = [
        pltpu.make_async_copy(source, target, sems.at[k])
        for k, (source, target) in enumerate(zip(sources, targets))
    ]
    for copy in copies:
        copy.start()
    for k, ref in enumerate(vectors):
        ref[...] = vec_ref[k].reshape(ref.shape)
    for copy in copies:
        copy.wait()


def run_results(arrays, vec):
    count = len(arrays)
    shape = jax.ShapeDtypeStruct
    return pl.pallas_call(
        functools.partial(results_kernel, count),
        out_shape=tuple(shape(one.shape, one.dtype) for one in arrays)
        + (shape(vec.shape[1:], F32),) * VECTORS,
        in_specs=[VMEM] * (count + 1),
        out_specs=(ANY,) * count + (VMEM,) * VECTORS,
        scratch_shapes=[DMA((count,))],
        compiler_params=pltpu.CompilerParams(vmem_limit_bytes=60 * 2**20),
        name="results",
    )(*arrays, vec)


def direct(rows, cols):
    n_dp, n_head = lax.axis_size("dp"), lax.axis_size("head")
    return n_head == 4 and n_dp == 8 and rows % 32 == 0 and cols % 64 == 0


def fast_shards(
    images,
    cotangent,
    counts,
    labels,
    levels,
    noise_table,
    class_table,
    gain_a,
    shift_a,
    conv_a,
    bias_a,
    mod_weight,
    mod_bias,
    gain_b,
    shift_b,
    conv_b,
    bias_b,
    gain_c,
    shift_c,
    qkv_weight,
    proj_weight,
    proj_bias,
):
    weights = (
        jnp.swapaxes(conv_a, 0, 1),
        jnp.swapaxes(conv_b, 0, 1),
        jnp.swapaxes(qkv_weight, 0, 1),
        proj_weight,
    )
    vectors = (gain_a, shift_a, bias_a, gain_b, shift_b, bias_b, gain_c, shift_c, proj_bias)
    modw = mod_weight.reshape(mod_weight.shape[0], 2 * C)
    flat = images.reshape(ALL, C)
    (
        whole,
        conv_out,
        slopes,
        turned,
        block_out,
        grad_resid,
        grad_low,
        right,
        vecs,
        mod,
        stats,
        pre,
        all_ids,
        sums,
    ) = run_forward(
        weights,
        flat,
        cotangent.reshape(ALL, C),
        counts,
        labels,
        levels,
        class_table.T,
        noise_table,
        modw,
        mod_bias,
        vectors,
    )
    *arrays, vec = run_backward(
        whole,
        turned,
        right,
        grad_low,
        grad_resid,
        conv_out,
        slopes,
        flat,
        stats,
        vecs,
        mod,
        sums,
        pre,
        all_ids,
        modw,
        class_table.shape[0],
    )
    block_out, conva, convb, qkvw, projw, image_grad, class_grad, modw_grad, modb_grad, *rest = run_results(
        (block_out, *arrays), vec
    )
    gaina, shifta, biasa, gainb, shiftb, biasb, gainc, shiftc, projb = rest
    return (
        block_out.reshape(images.shape),
        image_grad.reshape(images.shape),
        class_grad.T,
        gaina,
        shifta,
        jnp.swapaxes(conva, 0, 1),
        biasa,
        modw_grad,
        modb_grad,
        gainb,
        shiftb,
        jnp.swapaxes(convb, 0, 1),
        biasb,
        gainc,
        shiftc,
        jnp.swapaxes(qkvw, 0, 1),
        projw,
        projb,
    )


def shards(*args):
    rows, _, cols = args[9].shape
    if direct(rows, cols):
        return fast_shards(*args)
    return plain_shards(*args)


def solution(mesh):
    placed = (
        P(("dp", "head"), None, None, None),
        P(("dp", "head"), None, None, None),
        P(),
        P(("dp", "head")),
        P(("dp", "head")),
        P(),
        P(None, "dp"),
        P("head"),
        P("head"),
        P("dp", None, "head"),
        P("head"),
        P("dp", None, None),
        P(),
        P("head"),
        P("head"),
        P("dp", None, "head"),
        P("head"),
        P("head"),
        P("head"),
        P("dp", None, "head"),
        P("dp", "head"),
        P("head"),
    )
    return jax.shard_map(
        shards,
        mesh=mesh,
        in_specs=placed,
        out_specs=(
            P(("dp", "head"), None, None, None),
            P(("dp", "head"), None, None, None),
            P(None, ("dp", "head")),
            P("head"),
            P("head"),
            P("dp", None, "head"),
            P("head"),
            P(("dp", "head"), None, None),
            P(None, ("dp", "head")),
            P("head"),
            P("head"),
            P("dp", None, "head"),
            P("head"),
            P("head"),
            P("head"),
            P("dp", None, "head"),
            P("dp", "head"),
            P("head"),
        ),
        check_vma=False,
    )
```

```python
import functools

import jax
import jax.numpy as jnp
from jax import lax
from jax.experimental import pallas as pl
from jax.experimental.pallas import tpu as pltpu
from jax.sharding import PartitionSpec as P

C = 768
DH = 64
GROUPS = 32


EPSILON = 1e-05
HIGHEST = lax.Precision.HIGHEST


def norm_forward(values, gain, shift):
    count, chans = (values.shape[0], values.shape[-1])
    span = C // GROUPS
    grouped = values.reshape(count, -1, chans // span, span)
    mean = jnp.mean(grouped, axis=(1, 3), keepdims=True)
    centred = grouped - mean
    inverse = lax.rsqrt(jnp.mean(centred * centred, axis=(1, 3), keepdims=True) + EPSILON)
    normed = (centred * inverse).reshape(values.shape)
    return (normed * gain + shift, normed, inverse)


def norm_backward(grad_out, normed, inverse, gain):
    grad_gain = jnp.sum(grad_out * normed, axis=(0, 1, 2))
    grad_shift = jnp.sum(grad_out, axis=(0, 1, 2))
    count, chans = (grad_out.shape[0], grad_out.shape[-1])
    span = C // GROUPS
    layout = (count, -1, chans // span, span)
    grad_normed = (grad_out * gain).reshape(layout)
    normed_groups = normed.reshape(layout)
    mean_one = jnp.mean(grad_normed, axis=(1, 3), keepdims=True)
    mean_two = jnp.mean(grad_normed * normed_groups, axis=(1, 3), keepdims=True)
    grad_in = inverse * (grad_normed - mean_one - normed_groups * mean_two)
    return (grad_in.reshape(grad_out.shape), grad_gain, grad_shift)


def silu_slope(values):
    sigma = jax.nn.sigmoid(values)
    return sigma * (1.0 + values * (1.0 - sigma))


def patches_of(act):
    count, rows, cols, chans = act.shape
    padded = jnp.pad(act, ((0, 0), (1, 1), (1, 1), (0, 0)))
    taps = [padded[:, i : i + rows, j : j + cols, :] for i in range(3) for j in range(3)]
    return jnp.stack(taps, axis=3).reshape(count * rows * cols, 9, chans)


def contract_rows(left, right):
    return lax.dot_general(
        left, right, (((0,), (0,)), ((), ())), preferred_element_type=jnp.float32
    )


def contract_cols(left, right):
    return lax.dot_general(
        left, right, (((1,), (1,)), ((), ())), preferred_element_type=jnp.float32
    )


def conv_back(grad_low, weight, count, rows, cols):
    chans = weight.shape[0]
    padded = jnp.zeros((count, rows + 2, cols + 2, chans), jnp.float32)
    for tap in range(9):
        i, j = divmod(tap, 3)
        part = contract_cols(grad_low, weight[:, tap, :]).reshape(count, rows, cols, chans)
        padded = padded.at[:, i : i + rows, j : j + cols, :].add(part)
    return padded[:, 1 : rows + 1, 1 : cols + 1, :]


def keep_same(values):
    return values


def live_rows(counts, first, number, count):
    sums = jnp.sum(counts, axis=1)
    chosen = lax.dynamic_slice_in_dim(sums, first, number)
    slots = lax.iota(jnp.int32, count)
    return (slots[None, :] < chosen[:, None]).astype(jnp.float32).reshape(number * count)


def residual_forward(source, mod_pair, weights, spread):
    (
        conv_one,
        conv_two,
        gain_one,
        shift_one,
        bias_one,
        gain_two,
        shift_two,
        bias_two,
        gain_three,
        shift_three,
    ) = weights
    out_a, normed_a, inverse_a = norm_forward(source, gain_one, shift_one)
    wide_a = spread(jax.nn.silu(out_a).astype(jnp.bfloat16))
    conv_out_a = (
        jnp.einsum("ptc,cto->po", patches_of(wide_a), conv_one, preferred_element_type=jnp.float32)
        + bias_one
    ).reshape(source.shape)
    scale = mod_pair[:, :, 0:1, :]
    offset = mod_pair[:, :, 1:2, :]
    out_b, normed_b, inverse_b = norm_forward(conv_out_a, gain_two, shift_two)
    inner_b = offset + out_b * (scale + 1.0)
    wide_b = spread(jax.nn.silu(inner_b).astype(jnp.bfloat16))
    conv_out_b = (
        jnp.einsum("ptc,cto->po", patches_of(wide_b), conv_two, preferred_element_type=jnp.float32)
        + bias_two
    ).reshape(source.shape)
    resid = source + conv_out_b
    out_c, normed_c, inverse_c = norm_forward(resid, gain_three, shift_three)
    attn_in = out_c.astype(jnp.bfloat16)
    saved = (
        out_a,
        normed_a,
        inverse_a,
        wide_a,
        out_b,
        normed_b,
        inverse_b,
        inner_b,
        wide_b,
        normed_c,
        inverse_c,
        scale,
    )
    return (resid, attn_in, saved)


def residual_backward(grad_attn, grad_out, saved, weights, reduce_value):
    conv_one, conv_two, gain_one, gain_two, gain_three = (
        weights[0],
        weights[1],
        weights[2],
        weights[5],
        weights[8],
    )
    (
        out_a,
        normed_a,
        inverse_a,
        wide_a,
        out_b,
        normed_b,
        inverse_b,
        inner_b,
        wide_b,
        normed_c,
        inverse_c,
        scale,
    ) = saved
    count, rows, cols, local = grad_out.shape
    grad_resid_c, gainc_term, shiftc_term = norm_backward(
        grad_attn, normed_c, inverse_c, gain_three
    )
    grad_resid = grad_out + grad_resid_c
    grad_conv_b = grad_resid.reshape(-1, local).astype(jnp.bfloat16)
    biasb_term = jnp.sum(grad_conv_b.astype(jnp.float32), axis=0)
    convb_term = jnp.einsum(
        "ptc,po->cto", patches_of(wide_b), grad_conv_b, preferred_element_type=jnp.float32
    )
    grad_act_b = reduce_value(conv_back(grad_conv_b, conv_two, count, rows, cols))
    grad_inner = grad_act_b * silu_slope(inner_b)
    grad_offset = jnp.sum(grad_inner, axis=(1, 2))
    grad_scale = jnp.sum(grad_inner * out_b, axis=(1, 2))
    grad_mod = jnp.stack([grad_scale, grad_offset], axis=1)[:, None]
    grad_conv_full, gainb_term, shiftb_term = norm_backward(
        grad_inner * (scale + 1.0), normed_b, inverse_b, gain_two
    )
    grad_conv_a = grad_conv_full.reshape(-1, local).astype(jnp.bfloat16)
    biasa_term = jnp.sum(grad_conv_a.astype(jnp.float32), axis=0)
    conva_term = jnp.einsum(
        "ptc,po->cto", patches_of(wide_a), grad_conv_a, preferred_element_type=jnp.float32
    )
    grad_act_a = reduce_value(conv_back(grad_conv_a, conv_one, count, rows, cols))
    grad_source, gaina_term, shifta_term = norm_backward(
        grad_act_a * silu_slope(out_a), normed_a, inverse_a, gain_one
    )
    image_grad = grad_resid + grad_source
    vectors = (
        gaina_term,
        shifta_term,
        biasa_term,
        gainb_term,
        shiftb_term,
        biasb_term,
        gainc_term,
        shiftc_term,
    )
    return (image_grad, grad_mod, (conva_term, convb_term), vectors)


def attend_forward(block):
    query, key, value = (block[:, :, 0], block[:, :, 1], block[:, :, 2])
    batch, pixels, heads_here, depth = query.shape
    scores = jnp.einsum("bqhd,bkhd->bhqk", query, key, preferred_element_type=jnp.float32) * DH ** (
        -0.5
    )
    top = jnp.max(scores, axis=-1, keepdims=True)
    weights = jnp.exp(scores - top)
    sums = jnp.sum(weights, axis=-1, keepdims=True)
    probs = (weights / sums).astype(jnp.bfloat16)
    logsum = (top + jnp.log(sums))[..., 0]
    mixed = jnp.einsum("bhqk,bkhd->bqhd", probs, value, preferred_element_type=jnp.float32).astype(
        jnp.bfloat16
    )
    return (mixed.reshape(batch, pixels, heads_here * depth), logsum)


def attend_backward(block, logsum, grad_head):
    query, key, value = (block[:, :, 0], block[:, :, 1], block[:, :, 2])
    batch, pixels, heads_here, depth = query.shape
    factor = DH ** (-0.5)
    scores = jnp.einsum("bqhd,bkhd->bhqk", query, key, preferred_element_type=jnp.float32) * factor
    probs = jnp.exp(scores - logsum[..., None])
    grad_value = jnp.einsum(
        "bhqk,bqhd->bkhd", probs.astype(jnp.bfloat16), grad_head, preferred_element_type=jnp.float32
    )
    grad_probs = jnp.einsum("bqhd,bkhd->bhqk", grad_head, value, preferred_element_type=jnp.float32)
    inner = jnp.sum(grad_probs * probs, axis=-1, keepdims=True)
    grad_scores = (probs * (grad_probs - inner)).astype(jnp.bfloat16)
    grad_query = (
        jnp.einsum("bhqk,bkhd->bqhd", grad_scores, key, preferred_element_type=jnp.float32) * factor
    )
    grad_key = (
        jnp.einsum("bhqk,bqhd->bkhd", grad_scores, query, preferred_element_type=jnp.float32)
        * factor
    )
    stacked = jnp.stack([grad_query, grad_key, grad_value], axis=2).astype(jnp.bfloat16)
    return stacked.reshape(batch, pixels, 3, heads_here * depth)


def plain_shards(
    images,
    cotangent,
    counts,
    labels,
    levels,
    noise_table,
    class_table,
    gain_a,
    shift_a,
    conv_a,
    bias_a,
    mod_weight,
    mod_bias,
    gain_b,
    shift_b,
    conv_b,
    bias_b,
    gain_c,
    shift_c,
    qkv_weight,
    proj_weight,
    proj_bias,
):
    rows_a, rows_b, rows_qkv, rows_proj, mod_full, class_full = (
        lax.all_gather(conv_a, "dp", axis=0, tiled=True),
        lax.all_gather(conv_b, "dp", axis=0, tiled=True),
        lax.all_gather(qkv_weight, "dp", axis=0, tiled=True),
        lax.all_gather(proj_weight, "dp", axis=0, tiled=True),
        lax.all_gather(mod_weight, "dp", axis=0, tiled=True),
        lax.all_gather(class_table, "dp", axis=1, tiled=True),
    )
    count, rows, cols, channels = images.shape
    pixels = rows * cols
    groups_n = lax.axis_size("head")
    quarter = channels // groups_n
    heads_local = quarter // DH
    first_dp = lax.axis_index("dp") * groups_n
    class_hot = (labels[:, None] == lax.iota(jnp.int32, class_full.shape[0])[None, :]).astype(
        jnp.bfloat16
    )
    level_hot = (levels[:, None] == lax.iota(jnp.int32, noise_table.shape[0])[None, :]).astype(
        jnp.bfloat16
    )
    embed_pre = jnp.dot(class_hot, class_full, preferred_element_type=jnp.float32) + jnp.dot(
        level_hot, noise_table, preferred_element_type=jnp.float32
    )
    embed = jax.nn.silu(embed_pre).astype(jnp.bfloat16)
    modulation = (
        jnp.einsum("ne,etc->ntc", embed, mod_full, preferred_element_type=jnp.float32)
        + mod_bias.astype(jnp.float32)
    ).astype(jnp.bfloat16)
    mod_pair = modulation.reshape(count, 1, 2, channels)
    (
        conv_one,
        conv_two,
        qkv_full,
        proj_full,
        gain_one,
        shift_one,
        bias_one,
        gain_two,
        shift_two,
        bias_two,
        gain_three,
        shift_three,
        bias_three,
    ) = (
        lax.all_gather(rows_a, "head", axis=2, tiled=True),
        lax.all_gather(rows_b, "head", axis=2, tiled=True),
        lax.all_gather(rows_qkv, "head", axis=2, tiled=True),
        lax.all_gather(rows_proj, "head", axis=1, tiled=True),
        lax.all_gather(gain_a, "head", axis=0, tiled=True),
        lax.all_gather(shift_a, "head", axis=0, tiled=True),
        lax.all_gather(bias_a, "head", axis=0, tiled=True),
        lax.all_gather(gain_b, "head", axis=0, tiled=True),
        lax.all_gather(shift_b, "head", axis=0, tiled=True),
        lax.all_gather(bias_b, "head", axis=0, tiled=True),
        lax.all_gather(gain_c, "head", axis=0, tiled=True),
        lax.all_gather(shift_c, "head", axis=0, tiled=True),
        lax.all_gather(proj_bias, "head", axis=0, tiled=True),
    )
    weights = (
        conv_one,
        conv_two,
        gain_one,
        shift_one,
        bias_one,
        gain_two,
        shift_two,
        bias_two,
        gain_three,
        shift_three,
    )
    live = live_rows(counts, first_dp + lax.axis_index("head"), 1, count)
    total = count * pixels
    width = channels // groups_n
    source = images.astype(jnp.float32)
    resid, attn_in, saved = residual_forward(
        source, mod_pair.astype(jnp.float32), weights, keep_same
    )
    attn_flat = attn_in.reshape(total, channels)
    qkv_flat = qkv_full.reshape(channels, 3 * channels)
    qkv = jnp.dot(attn_flat, qkv_flat, preferred_element_type=jnp.float32).astype(jnp.bfloat16)
    packed = qkv.reshape(1, count, pixels, 3, groups_n, width)
    block = lax.all_to_all(packed, "head", split_axis=4, concat_axis=0, tiled=True)
    groups = block.shape[0]
    items = block.shape[1]
    flat = block.reshape(groups * items, pixels, 3, heads_local, DH)
    mixed, logsum = attend_forward(flat)
    mixed = mixed.reshape(groups, items, pixels, 1, width)
    returned = lax.all_to_all(mixed, "head", split_axis=0, concat_axis=3, tiled=True)
    returned, logsum, kept = (returned, logsum.reshape(groups, items, heads_local, pixels), block)
    mixed_image = returned.reshape(total, channels)
    result = (
        resid.reshape(total, channels)
        + jnp.dot(mixed_image, proj_full, preferred_element_type=jnp.float32)
        + bias_three
    )
    block_out = (result.reshape(images.shape) * live[:, None, None, None]).astype(jnp.bfloat16)
    grad_out = cotangent.astype(jnp.float32) * live[:, None, None, None]
    grad_flat = grad_out.reshape(total, channels)
    grad_low = grad_flat.astype(jnp.bfloat16)
    projw_full = contract_rows(mixed_image, grad_low)
    projb_full = jnp.sum(grad_flat, axis=0)
    grad_mixed = contract_cols(grad_low, proj_full).astype(jnp.bfloat16)
    arrived = lax.all_to_all(
        grad_mixed.reshape(1, count, pixels, groups_n, width),
        "head",
        split_axis=3,
        concat_axis=0,
        tiled=True,
    )
    flat_block = kept.reshape(groups_n * count, pixels, 3, heads_local, DH)
    grad_head = arrived.reshape(groups_n * count, pixels, heads_local, DH)
    stacked = attend_backward(
        flat_block, logsum.reshape(groups_n * count, heads_local, pixels), grad_head
    )
    stacked = stacked.reshape(groups_n, count, pixels, 3, 1, width)
    grad_qkv = lax.all_to_all(stacked, "head", split_axis=0, concat_axis=4, tiled=True).reshape(
        total, 3 * channels
    )
    qkvw_full = contract_rows(attn_flat, grad_qkv).reshape(channels, 3, channels)
    grad_attn = contract_cols(grad_qkv, qkv_flat).reshape(images.shape)
    image_grad, grad_mod_part, conv_terms, vectors = residual_backward(
        grad_attn, grad_out, saved, weights, keep_same
    )
    (
        gaina_full,
        shifta_full,
        biasa_full,
        gainb_full,
        shiftb_full,
        biasb_full,
        gainc_full,
        shiftc_full,
    ) = vectors
    (
        conva_term,
        convb_term,
        qkvw_term,
        projw_term,
        gaina_term,
        shifta_term,
        biasa_term,
        gainb_term,
        shiftb_term,
        biasb_term,
        gainc_term,
        shiftc_term,
        projb_term,
    ) = (
        lax.psum_scatter(
            conv_terms[0].astype(jnp.bfloat16), "head", scatter_dimension=2, tiled=True
        ).astype(jnp.float32),
        lax.psum_scatter(
            conv_terms[1].astype(jnp.bfloat16), "head", scatter_dimension=2, tiled=True
        ).astype(jnp.float32),
        lax.psum_scatter(
            qkvw_full.astype(jnp.bfloat16), "head", scatter_dimension=2, tiled=True
        ).astype(jnp.float32),
        lax.psum_scatter(
            projw_full.astype(jnp.bfloat16), "head", scatter_dimension=1, tiled=True
        ).astype(jnp.float32),
        lax.psum_scatter(
            gaina_full.astype(jnp.bfloat16), "head", scatter_dimension=0, tiled=True
        ).astype(jnp.float32),
        lax.psum_scatter(
            shifta_full.astype(jnp.bfloat16), "head", scatter_dimension=0, tiled=True
        ).astype(jnp.float32),
        lax.psum_scatter(
            biasa_full.astype(jnp.bfloat16), "head", scatter_dimension=0, tiled=True
        ).astype(jnp.float32),
        lax.psum_scatter(
            gainb_full.astype(jnp.bfloat16), "head", scatter_dimension=0, tiled=True
        ).astype(jnp.float32),
        lax.psum_scatter(
            shiftb_full.astype(jnp.bfloat16), "head", scatter_dimension=0, tiled=True
        ).astype(jnp.float32),
        lax.psum_scatter(
            biasb_full.astype(jnp.bfloat16), "head", scatter_dimension=0, tiled=True
        ).astype(jnp.float32),
        lax.psum_scatter(
            gainc_full.astype(jnp.bfloat16), "head", scatter_dimension=0, tiled=True
        ).astype(jnp.float32),
        lax.psum_scatter(
            shiftc_full.astype(jnp.bfloat16), "head", scatter_dimension=0, tiled=True
        ).astype(jnp.float32),
        lax.psum_scatter(
            projb_full.astype(jnp.bfloat16), "head", scatter_dimension=0, tiled=True
        ).astype(jnp.float32),
    )
    grad_mod = grad_mod_part.reshape(count, 2, channels)
    modw_term = jnp.einsum("ne,ntc->etc", embed.astype(jnp.float32), grad_mod, precision=HIGHEST)
    modb_term = jnp.sum(grad_mod, axis=0)
    grad_embed = jnp.einsum(
        "ntc,etc->ne", grad_mod, mod_full.astype(jnp.float32), precision=HIGHEST
    ) * silu_slope(embed_pre)
    class_term = lax.dot_general(
        class_hot.astype(jnp.float32), grad_embed, (((0,), (0,)), ((), ())), precision=HIGHEST
    )
    modw_grad, class_grad, modb_grad = (
        lax.psum_scatter(modw_term, ("dp", "head"), scatter_dimension=0, tiled=True),
        lax.psum_scatter(class_term, ("dp", "head"), scatter_dimension=1, tiled=True),
        lax.psum_scatter(modb_term, ("dp", "head"), scatter_dimension=1, tiled=True),
    )
    conva_grad, convb_grad, qkvw_grad, projw_grad = (
        lax.psum_scatter(conva_term, "dp", scatter_dimension=0, tiled=True),
        lax.psum_scatter(convb_term, "dp", scatter_dimension=0, tiled=True),
        lax.psum_scatter(qkvw_term, "dp", scatter_dimension=0, tiled=True),
        lax.psum_scatter(projw_term, "dp", scatter_dimension=0, tiled=True),
    )
    (
        gaina_grad,
        shifta_grad,
        biasa_grad,
        gainb_grad,
        shiftb_grad,
        biasb_grad,
        gainc_grad,
        shiftc_grad,
        projb_grad,
    ) = lax.psum(
        (
            gaina_term,
            shifta_term,
            biasa_term,
            gainb_term,
            shiftb_term,
            biasb_term,
            gainc_term,
            shiftc_term,
            projb_term,
        ),
        "dp",
    )
    return (
        block_out,
        image_grad,
        class_grad,
        gaina_grad,
        shifta_grad,
        conva_grad,
        biasa_grad,
        modw_grad,
        modb_grad,
        gainb_grad,
        shiftb_grad,
        convb_grad,
        biasb_grad,
        gainc_grad,
        shiftc_grad,
        qkvw_grad,
        projw_grad,
        projb_grad,
    )


MESH = pl.DeviceIdType.MESH
UNITS = 22
PAIRS = UNITS // 2
FAR = 9
VECTORS = 9
RES = 8
SLOTS = 8
PIX = RES * RES
LINE = SLOTS * RES
ALL = RES * LINE
WIDTH = 768
BAND = 256
F32 = jnp.float32
BF16 = jnp.bfloat16
ANY = pl.BlockSpec(memory_space=pl.ANY)
VMEM = pl.BlockSpec(memory_space=pltpu.VMEM)
SMEM = pl.BlockSpec(memory_space=pltpu.SMEM)
DMA = pltpu.SemaphoreType.DMA


def place():
    d, h = lax.axis_index("dp"), lax.axis_index("head")
    return d // 2, lax.rem(d, 2), h // 2, lax.rem(h, 2)


def at_chip(z, y, x, c):
    return (z * 2 + y, x * 2 + c)


def column_peers(n_dp):
    d, h = lax.axis_index("dp"), lax.axis_index("head")
    return [(lax.rem(d + k, n_dp), h) for k in range(1, n_dp)]


def head_peers(n_head):
    d, h = lax.axis_index("dp"), lax.axis_index("head")
    return [(d, lax.rem(h + k, n_head)) for k in range(1, n_head)]


def greet(devices):
    barrier = pltpu.get_barrier_semaphore()
    for device in devices:
        pl.semaphore_signal(barrier, inc=1, device_id=device, device_id_type=MESH)
    pl.semaphore_wait(barrier, len(devices))


def remote(src, dst, send, recv, device):
    return pltpu.make_async_remote_copy(
        src_ref=src, dst_ref=dst, send_sem=send, recv_sem=recv, device_id=device, device_id_type=MESH
    )


def each(count, body):
    def step(n, carry):
        body(n)
        return carry

    lax.fori_loop(0, count, step, 0)


def span(index, size):
    return pl.ds(pl.multiple_of(index * size, size), size)


def row(n):
    return pl.ds(n, 1)


def lines_from(i):
    return pl.ds(i * LINE if isinstance(i, int) else pl.multiple_of(i * LINE, LINE), ALL)


def dot(left, right):
    return jnp.dot(left, right, preferred_element_type=F32)


def dot_nt(left, right):
    return lax.dot_general(left, right, (((1,), (1,)), ((), ())), preferred_element_type=F32)


def dot_tn(left, right):
    return lax.dot_general(left, right, (((0,), (0,)), ((), ())), preferred_element_type=F32)


def in_group(first, second, axis):
    chan = lax.broadcasted_iota(jnp.int32, (first, second), axis)
    group = lax.broadcasted_iota(jnp.int32, (first, second), 1 - axis) * (C // GROUPS)
    inside = jnp.logical_and(chan >= group, chan < group + C // GROUPS)
    return jnp.where(inside, 1.0, 0.0).astype(BF16)


def pieces(values):
    high = values.astype(BF16).astype(F32)
    rest = values - high
    mid = rest.astype(BF16).astype(F32)
    return jnp.concatenate([high, mid, rest - mid], axis=0).astype(BF16)


def group_mean(sums):
    count = sums.shape[0]
    part = dot(pieces(sums), in_group(C, 128, 0))
    part = (part[:count] + part[count : 2 * count] + part[2 * count :]) * (1.0 / (PIX * (C // GROUPS)))
    back = dot(pieces(part), in_group(128, C, 1))
    return back[:count] + back[count : 2 * count] + back[2 * count :]


def sum_rows(values):
    return jnp.sum(values, axis=0, keepdims=True)


def norm_stats(get, mean_ref, inverse_ref, sums_ref):
    def first(n):
        sums_ref[row(n)] = sum_rows(get(n))

    each(SLOTS, first)
    mean_ref[...] = group_mean(sums_ref[...])

    def second(n):
        centred = get(n) - mean_ref[row(n)]
        sums_ref[row(n)] = sum_rows(centred * centred)

    each(SLOTS, second)
    inverse_ref[...] = lax.rsqrt(group_mean(sums_ref[...]) + EPSILON)


def silu(values):
    return values * jax.nn.sigmoid(values)


def shifted(values):
    spot = lax.rem(lax.broadcasted_iota(jnp.int32, values.shape, 0), RES)
    left = jnp.where(spot == 0, 0.0, pltpu.roll(values, 1, 0))
    right = jnp.where(spot == RES - 1, 0.0, pltpu.roll(values, values.shape[0] - 1, 0))
    return left, right


def chunk(n):
    return slice(n * WIDTH, (n + 1) * WIDTH)


CHUNKS = C // WIDTH


def weight_cols(ref, n):
    return ref[:, :, :, chunk(n)].reshape(C, WIDTH)


def weight_rows(ref, n):
    return ref[...].reshape(C, C)[chunk(n)]


def forward_kernel(
    lines,
    weights_a,
    weights_b,
    weights_qkv,
    weights_proj,
    images_hbm,
    cot_hbm,
    counts_ref,
    labels_ref,
    levels_ref,
    class_table,
    noise_table,
    modw_table,
    modb_ref,
    *refs,
):
    vectors, refs = refs[:VECTORS], refs[VECTORS:]
    forward_steps(
        lines,
        vectors,
        weights_a,
        weights_b,
        weights_qkv,
        weights_proj,
        images_hbm,
        cot_hbm,
        counts_ref,
        labels_ref,
        levels_ref,
        class_table,
        noise_table,
        modw_table,
        modb_ref,
        *refs,
    )


def forward_steps(
    lines,
    vectors,
    weights_a,
    weights_b,
    weights_qkv,
    weights_proj,
    images_hbm,
    cot_hbm,
    counts_ref,
    labels_ref,
    levels_ref,
    class_table,
    noise_table,
    modw_table,
    modb_ref,
    whole_out,
    conv_out,
    slopes_out,
    turned_out,
    block_out,
    grad_out,
    low_out,
    right_out,
    vecs_ref,
    mod_ref,
    stats_ref,
    pre_ref,
    all_ids,
    sums_out,
    halves,
    whole_ref,
    vec_ref,
    ids_ref,
    class_ref,
    modw_ref,
    vec_all,
    mod_part,
    mod_got,
    act,
    act_f32,
    sums_ref,
    conv_ref,
    resid_ref,
    slopes,
    turned,
    attn_in,
    qkv,
    right,
    low,
    pair_ref,
    pair_send,
    pair_recv,
    pair_local,
    z_send,
    z_recv,
    p_send,
    x_send,
    x_recv,
    y_send,
    y_recv,
    s_send,
    s_recv,
    vec_send,
    vec_recv,
    ids_send,
    ids_recv,
    mod_send,
    mod_recv,
    unit_sem,
    flush_sem,
    in_sem,
):
    z, y, x, c = place()
    d, h = lax.axis_index("dp"), lax.axis_index("head")
    n_dp, n_head = lines * 2, 4
    half = lines // 2
    inner = jnp.logical_and(z > 0, z < lines - 1)
    far = at_chip(lax.rem(3 * z + 1, lines), y, x, c)
    rows, cols_own = halves.shape[2:]
    wide = 2 * cols_own
    sibling = at_chip(z, y, x, 1 - c)
    along_x = at_chip(z, y, 1 - x, c)
    along_y = at_chip(z, 1 - y, x, c)
    line = [at_chip(lax.rem(z + k, lines), y, x, c) for k in range(1, lines)]
    column, heads = column_peers(n_dp), head_peers(n_head)
    greet(column + heads)

    def spot(i, cc, zz, yy, xx):
        return whole_ref.at[i, cc, zz, yy, :, span(xx, wide)]

    def parts_of(core):
        return (
            (weights_a.at[pl.ds(4 * core, 4)], pl.ds(0, 4)),
            (weights_b.at[pl.ds(4 * core, 4)], pl.ds(5, 4)),
            (weights_qkv.at[pl.ds(core, 1)], pl.ds(9, 1)),
        )

    last_parts = (
        ((weights_a.at[8], 4), (weights_qkv.at[2], 10)),
        ((weights_b.at[8], 4), (weights_proj, 10)),
    )

    def keep_copy(k):
        source, where = parts_of(c)[k]
        return pltpu.make_async_copy(source, halves.at[c, where], pair_local.at[k])

    def swap_copy(k):
        source, where = parts_of(1 - c)[k]
        return remote(source, halves.at[c, where], pair_send.at[k], pair_recv.at[k], sibling)

    def last_keep(core, k):
        source, where = last_parts[core][k]
        return pltpu.make_async_copy(source, halves.at[c, where], pair_local.at[3 + k])

    def last_swap(core, k):
        source, where = last_parts[core][k]
        return remote(source, halves.at[c, where], pair_send.at[3 + k], pair_recv.at[3 + k], sibling)

    def swap_start():
        for k in range(3):
            swap_copy(k).start()
            keep_copy(k).start()
        for core in range(2):

            @pl.when(c == core)
            def _():
                for k in range(2):
                    last_swap(1 - core, k).start()
                    last_keep(core, k).start()

    def swap_wait(k):
        if k < 3:
            keep_copy(k).wait()
            swap_copy(k).wait()
        else:
            last_keep(0, k - 3).wait()
            last_swap(0, k - 3).wait()

    def images_copy():
        return pltpu.make_async_copy(images_hbm, images_ref, in_sem.at[0])

    def cot_copy():
        return pltpu.make_async_copy(cot_hbm, cot_ref, in_sem.at[1])

    images_ref, cot_ref = attn_in, low

    def vec_copy(k):
        return remote(vec_ref, vec_all.at[h], vec_send.at[k], vec_recv.at[k], heads[k])

    def ids_copy(k):
        return remote(ids_ref, all_ids.at[d], ids_send.at[k], ids_recv.at[k], column[k])

    def mod_copy(k):
        return remote(
            mod_part.at[lax.rem(d + k + 1, n_dp)], mod_got.at[d], mod_send.at[k], mod_recv.at[k], column[k]
        )

    def z_part(i, zz):
        if isinstance(i, int) and i >= FAR:
            return whole_ref.at[i, c, zz]
        return spot(i, c, zz, y, x)

    def z_copy(i, k):
        ref = z_part(i, z)
        return remote(ref, ref, z_send.at[i, k], z_recv.at[i, k], line[k])

    def z_pass(i):
        ref = z_part(i, lax.rem(z + 2, lines))
        return remote(ref, ref, p_send.at[i], z_recv.at[i, lax.rem(2 * z + 2, lines)], far)

    def z_start(i):
        z_copy(i, 1).start()

        @pl.when(z != lines - 1)
        def _():
            z_copy(i, 0).start()

        @pl.when(z != 0)
        def _():
            z_copy(i, 2).start()

    def z_relay(i):
        z_copy(i, 1).wait_recv()

        @pl.when(inner)
        def _():
            z_pass(i).start()

    def z_finish(i):
        z_copy(i, 0).wait_recv()
        z_copy(i, 2).wait_recv()

    def z_drain(i):
        z_copy(i, 1).wait_send()

        @pl.when(z != lines - 1)
        def _():
            z_copy(i, 0).wait_send()

        @pl.when(z != 0)
        def _():
            z_copy(i, 2).wait_send()

        @pl.when(inner)
        def _():
            z_pass(i).wait_send()

    def x_copy(i, part):
        if isinstance(i, int) and i >= FAR:
            ref = spot(i, c, z, y, x) if part == 0 else spot(i, c, z, 1 - y, x).at[pl.ds(rows // 2, rows // 2)]
        elif part == 0:
            ref = spot(i, c, slice(None), y, x)
        else:
            ref = spot(i, c, pl.ds(half, half), 1 - y, x)
        return remote(ref, ref, x_send.at[i, part], x_recv.at[i, part], along_x)

    def y_copy(i, part):
        if isinstance(i, int) and i >= FAR:
            ref = spot(i, c, z, y, x) if part == 0 else spot(i, c, z, y, 1 - x).at[pl.ds(0, rows // 2)]
        elif part == 0:
            ref = spot(i, c, slice(None), y, x)
        else:
            ref = spot(i, c, pl.ds(0, half), y, 1 - x)
        return remote(ref, ref, y_send.at[i, part], y_recv.at[i, part], along_y)

    def s_copy(i, part):
        if isinstance(i, int) and i >= FAR:
            ref = whole_ref.at[i, c, part]
        else:
            yy, xx = ((y, x), (y, 1 - x), (1 - y, x), (1 - y, 1 - x))[part]
            ref = spot(i, c, slice(None), yy, xx)
        return remote(ref, ref, s_send.at[i, part], s_recv.at[i, part], sibling)

    def join(i):
        whole_ref[i, c, z, y, :, span(x, wide)] = jnp.concatenate([halves[0, i], halves[1, i]], axis=-1)

    def begin(i):
        join(i)
        z_start(i)

    def far_begin(i):
        x_copy(i, 0).start()
        y_copy(i, 0).start()

    def far_pass(i):
        x_copy(i, 0).wait_recv()
        y_copy(i, 1).start()
        y_copy(i, 0).wait_recv()
        x_copy(i, 1).start()

    def far_line(i):
        x_copy(i, 1).wait_recv()
        y_copy(i, 1).wait_recv()
        z_start(i)

    def far_finish(i):
        z_finish(i)
        for part in range(lines):
            s_copy(i, part).start()

    def spread_line(i):
        z_finish(i)
        x_copy(i, 0).start()
        y_copy(i, 0).start()
        s_copy(i, 0).start()

    def pass_on(i):
        x_copy(i, 0).wait_recv()
        y_copy(i, 1).start()
        s_copy(i, 1).start()
        y_copy(i, 0).wait_recv()
        x_copy(i, 1).start()
        s_copy(i, 2).start()

    def finish(i):
        x_copy(i, 1).wait_recv()
        y_copy(i, 1).wait_recv()
        s_copy(i, 3).start()

    def arrived(i):
        for part in range(4):
            s_copy(i, part).wait_recv()

    def unit_copy(i):
        return pltpu.make_async_copy(whole_ref.at[i], whole_out.at[i], unit_sem.at[i])

    def fetch(i):
        arrived(i)
        if not isinstance(i, int) or i < FAR:
            unit_copy(i).start()

    def product(total, tap, i, k):
        for n in range(CHUNKS):
            value = dot(act[tap % 3, lines_from(tap // 3)], weight_cols(whole_ref.at[i, k], n))
            total[:, :, :, chunk(n)] += value.reshape(RES, SLOTS, RES, WIDTH)

    def use_pair(total, i, first):
        each(2, lambda k: product(total, i - first + 4 * k, i, k))

    flushed = (
        (conv_ref, conv_out),
        (slopes.at[0], slopes_out.at[0]),
        (slopes.at[1], slopes_out.at[1]),
        (turned.at[3], turned_out.at[3]),
        (turned.at[2], turned_out.at[2]),
        (turned.at[0], turned_out.at[0]),
        (turned.at[1], turned_out.at[1]),
        (low, block_out),
        (resid_ref, grad_out),
        (attn_in, low_out),
        (right, right_out),
    )

    def flush(k):
        return pltpu.make_async_copy(*flushed[k], flush_sem.at[k])

    def set_act(place_t):
        def by_line(yy):
            value = act_f32[yy].reshape(LINE, C)
            left, right = shifted(value)
            spot_rows = pl.ds(pl.multiple_of((yy + 1) * LINE, LINE), LINE)
            act[0, spot_rows] = left.astype(BF16)
            act[1, spot_rows] = value.astype(BF16)
            act[2, spot_rows] = right.astype(BF16)

        each(RES, by_line)

        def turn(yy):
            value = act_f32[pl.ds(2 * yy, 2)].reshape(2 * LINE, C)
            turned[place_t, :, span(yy, 2 * LINE)] = value.T.astype(BF16)

        each(RES // 2, turn)

    def activate(which, n, value):
        sigma = jax.nn.sigmoid(value)
        act_f32[:, n] = (value * sigma).reshape(RES, RES, C)
        slopes[which, :, n] = (sigma * (1.0 + value * (1.0 - sigma))).reshape(RES, RES, C)

    def norm_a():
        for k in range(n_head - 1):
            vec_copy(k).wait()
        vecs_ref[...] = jnp.concatenate([vec_all[k].astype(F32) for k in range(n_head)], axis=-1)

        images_copy().wait()

        def get(n):
            return images_ref[span(n, PIX)].astype(F32)

        mean, inverse = stats_ref.at[0], stats_ref.at[1]
        norm_stats(get, mean, inverse, sums_ref)

        def to_act(n):
            value = (get(n) - mean[row(n)]) * inverse[row(n)]
            activate(0, n, value * vecs_ref[0:1] + vecs_ref[1:2])
            conv_ref[:, n] = jnp.broadcast_to(vecs_ref[2:3].reshape(1, 1, C), (RES, RES, C))
            resid_ref[:, n] = (get(n) + vecs_ref[5:6]).reshape(RES, RES, C)

        each(SLOTS, to_act)
        set_act(3)
        flush(1).start()
        flush(3).start()

    def embed():
        for k in range(n_dp - 1):
            ids_copy(k).wait()
        ids = all_ids[...].reshape(n_dp * SLOTS, 128)
        table = class_ref.shape[1]
        label_hot = lax.broadcasted_iota(jnp.int32, (n_dp * SLOTS, table), 1) == ids[:, 0:1]
        levels = noise_table.shape[0]
        level_hot = lax.broadcasted_iota(jnp.int32, (n_dp * SLOTS, levels), 1) == ids[:, 1:2]
        pre = dot_nt(jnp.where(label_hot, 1.0, 0.0).astype(BF16), class_ref[...])
        width = class_table.shape[0]
        place_of = lax.broadcasted_iota(jnp.int32, (C, 128), 0) - d * width
        lane = lax.broadcasted_iota(jnp.int32, (C, 128), 1)
        chosen = jnp.logical_and(place_of == lane, lane < width)
        noise = dot(noise_table[...], jnp.where(chosen, 1.0, 0.0).astype(BF16)).astype(BF16)
        pre += dot(jnp.where(level_hot, 1.0, 0.0).astype(BF16), noise)
        pre_ref[...] = pre
        part = dot(silu(pre).astype(BF16), modw_ref[...])
        for k in range(n_dp):
            mine = part[k * SLOTS : (k + 1) * SLOTS]
            mod_part[k] = jnp.concatenate([mine[:, :C], mine[:, C:]], axis=0).astype(BF16)
        mod_got[d] = mod_part[d]
        for k in range(n_dp - 1):
            mod_copy(k).start()

    def norm_b():
        for k in range(n_dp - 1):
            mod_copy(k).wait()
        bias = modb_ref[...].astype(F32)
        total = jnp.concatenate([jnp.broadcast_to(bias[k : k + 1], (SLOTS, C)) for k in range(2)], axis=0)
        for k in range(n_dp):
            total += mod_got[k].astype(F32)
        mod_ref[...] = total.astype(BF16).astype(F32)

        def get(n):
            return conv_ref[:, n].reshape(PIX, C)

        mean, inverse = stats_ref.at[2], stats_ref.at[3]
        norm_stats(get, mean, inverse, sums_ref)

        def to_act(n):
            value = (get(n) - mean[row(n)]) * inverse[row(n)]
            value = value * vecs_ref[3:4] + vecs_ref[4:5]
            value = mod_ref[row(SLOTS + n)] + value * (mod_ref[row(n)] + 1.0)
            activate(1, n, value)

        each(SLOTS, to_act)
        set_act(2)
        flush(0).start()
        flush(2).start()
        flush(4).start()

    def residual(n):
        return resid_ref[:, n].reshape(PIX, C)

    def normed(n):
        return (residual(n) - stats_ref[4, row(n)]) * stats_ref[5, row(n)]

    def transpose_out(source, place_t):
        def turn(k):
            value = source[span(k, 2 * LINE)].astype(F32)
            turned[place_t, :, span(k, 2 * LINE)] = value.T.astype(BF16)

        each(ALL // (2 * LINE), turn)

    def live(n):
        slots = counts_ref[d * n_head + h, 0] + counts_ref[d * n_head + h, 1]
        return jnp.where(n < slots, 1.0, 0.0)

    def norm_c():
        cot_copy().wait()
        norm_stats(residual, stats_ref.at[4], stats_ref.at[5], sums_ref)
        sums_out[...] = jnp.zeros_like(sums_out)

        def prepare(n):
            attn_in[span(n, PIX)] = (normed(n) * vecs_ref[6:7] + vecs_ref[7:8]).astype(BF16)
            grad = cot_ref[span(n, PIX)].astype(F32) * live(n)
            right[3, span(n, PIX)] = grad.astype(BF16)
            sums_out[8:9] += sum_rows(grad)

        each(SLOTS, prepare)
        transpose_out(attn_in, 0)
        flush(5).start()

    def attention():
        unit = tuple(whole_ref.at[9 + t // 2, t % 2] for t in range(4))
        for t in range(4):
            for n in range(CHUNKS):
                if t < 3:
                    value = dot(attn_in[...], weight_cols(unit[t], n))
                else:
                    value = dot_nt(right[3], weight_rows(unit[3], n))
                qkv[t, :, chunk(n)] = value.astype(BF16)
        factor = DH ** (-0.5)
        band = lax.broadcasted_iota(jnp.int32, (PIX, BAND), 1) // DH
        heads_at_once = BAND // DH

        def stack(value):
            zero = jnp.zeros_like(value)
            return jnp.concatenate([jnp.where(band == k, value, zero) for k in range(heads_at_once)], axis=0)

        def pick(value):
            out = value[:PIX]
            for k in range(1, heads_at_once):
                out = jnp.where(band == k, value[k * PIX : (k + 1) * PIX], out)
            return out

        def attend(n):
            for b in range(C // BAND):
                query, key, value, grad = (qkv[t, span(n, PIX), slice(b * BAND, (b + 1) * BAND)] for t in range(4))
                query4, grad4 = stack(query), stack(grad)
                scores = dot_nt(key, query4) * factor
                weight = jnp.exp(scores - jnp.max(scores, axis=0, keepdims=True))
                probs = weight / jnp.sum(weight, axis=0, keepdims=True)
                probs_low = probs.astype(BF16)
                low[span(n, PIX), slice(b * BAND, (b + 1) * BAND)] = pick(dot_tn(probs_low, value)).astype(BF16)
                grad_probs = dot_nt(value, grad4)
                inner_sum = jnp.sum(grad_probs * probs, axis=0, keepdims=True)
                grad_scores = (probs * (grad_probs - inner_sum)).astype(BF16)
                right[0, span(n, PIX), slice(b * BAND, (b + 1) * BAND)] = (pick(dot_tn(grad_scores, key)) * factor).astype(BF16)
                right[1, span(n, PIX), slice(b * BAND, (b + 1) * BAND)] = (dot(grad_scores, query4) * factor).astype(BF16)
                right[2, span(n, PIX), slice(b * BAND, (b + 1) * BAND)] = dot(probs_low, grad4).astype(BF16)

        each(SLOTS, attend)
        flush(10).start()
        transpose_out(low, 1)
        flush(6).start()
        for n in range(CHUNKS):
            value = dot(low[...], weight_cols(unit[3], n))
            act_f32[:, :, :, chunk(n)] = value.reshape(SLOTS, RES, RES, WIDTH)

        def finish_out(n):
            value = residual(n) + act_f32[n].reshape(PIX, C) + vecs_ref[8:9]
            low[span(n, PIX)] = (value * live(n)).astype(BF16)

        each(SLOTS, finish_out)
        flush(7).start()
        for n in range(CHUNKS):
            value = dot_nt(right[0], weight_rows(unit[0], n))
            value += dot_nt(right[1], weight_rows(unit[1], n))
            value += dot_nt(right[2], weight_rows(unit[2], n))
            act_f32[:, :, :, chunk(n)] = value.reshape(SLOTS, RES, RES, WIDTH)

        def back(n):
            grad = act_f32[n].reshape(PIX, C)
            pair_ref[row(n)] = sum_rows(grad * normed(n))
            pair_ref[row(SLOTS + n)] = sum_rows(grad)

        each(SLOTS, back)
        sums_out[6:7] = sum_rows(pair_ref[0:SLOTS])
        sums_out[7:8] = sum_rows(pair_ref[SLOTS:])
        pair_ref[...] = group_mean(pair_ref[...] * vecs_ref[6:7])

        def back_second(n):
            inverse = stats_ref[5, row(n)]
            value = act_f32[n].reshape(PIX, C) * (vecs_ref[6:7] * inverse)
            value -= normed(n) * (pair_ref[row(n)] * inverse) + pair_ref[row(SLOTS + n)] * inverse
            value += right[3, span(n, PIX)].astype(F32)
            resid_ref[:, n] = value.reshape(RES, RES, C)
            sums_out[5:6] += sum_rows(value.astype(BF16).astype(F32))

        each(SLOTS, back_second)
        flush(8).start()

        def lower(yy):
            attn_in[span(yy, LINE)] = resid_ref[yy].reshape(LINE, C).astype(BF16)

        each(RES, lower)
        flush(9).start()

    swap_start()
    images_copy().start()
    cot_copy().start()
    one = [ref[...].astype(F32).reshape(1, cols_own) for ref in vectors]
    vec_ref[...] = jnp.concatenate(one + [jnp.zeros((16 - VECTORS, cols_own), F32)], axis=0).astype(BF16)
    lane = lax.broadcasted_iota(jnp.int32, (1, 128), 1)
    for n in range(SLOTS):
        ids_ref[n : n + 1] = jnp.where(lane == 0, labels_ref[n], levels_ref[n])
    for k in range(n_head - 1):
        vec_copy(k).start()
    for k in range(n_dp - 1):
        ids_copy(k).start()
    width = class_table.shape[0]
    class_ref[...] = jnp.zeros_like(class_ref)
    class_ref[0:width, 0 : class_table.shape[1]] = class_table[...]
    modw_ref[...] = jnp.zeros_like(modw_ref)
    modw_ref[0:width] = modw_table[...]
    vec_all[h] = vec_ref[...]
    all_ids[d] = ids_ref[...]
    edge = jnp.zeros((LINE, C), BF16)
    for j in range(3):
        act[j, 0:LINE] = edge
        act[j, ALL + LINE : ALL + 2 * LINE] = edge
    for k in range(5):
        swap_wait(k)
    for i in (10, 9):
        join(i)
    begin(0)
    for i in (10, 9):
        far_begin(i)
    begin(1)
    z_relay(0)
    begin(2)
    spread_line(0)
    for i in (10, 9):
        far_pass(i)
    begin(3)
    z_relay(1)
    norm_a()
    spread_line(1)
    pass_on(0)
    begin(4)
    z_relay(2)
    embed()
    spread_line(2)
    pass_on(1)
    finish(0)
    begin(5)
    z_relay(3)
    begin(6)
    z_relay(4)
    far_line(10)
    spread_line(3)
    pass_on(2)
    finish(1)
    fetch(0)

    def body(turn, carry):
        @pl.when(turn < 6)
        def _():
            begin(turn + 3)

        @pl.when(turn == 6)
        def _():
            far_line(9)
            z_relay(10)

        z_relay(turn + 1)
        spread_line(turn)
        pass_on(turn - 1)
        finish(turn - 2)
        fetch(turn - 3)
        use_pair(conv_ref, turn - 4, 0)
        return carry

    lax.fori_loop(4, 8, body, 0)
    spread_line(8)
    pass_on(7)
    finish(6)
    fetch(5)
    product(conv_ref, 8, 4, 0)
    norm_b()
    product(resid_ref, 8, 4, 1)
    pass_on(8)
    finish(7)
    z_relay(9)
    fetch(6)
    far_finish(10)
    use_pair(resid_ref, 5, 5)
    finish(8)
    fetch(7)
    use_pair(resid_ref, 6, 5)
    fetch(8)
    use_pair(resid_ref, 7, 5)
    far_finish(9)
    use_pair(resid_ref, 8, 5)
    norm_c()
    fetch(9)
    fetch(10)
    attention()

    def drain(i):
        z_drain(i)
        for part in range(2):
            x_copy(i, part).wait_send()
            y_copy(i, part).wait_send()
        for part in range(4):
            s_copy(i, part).wait_send()

    each(FAR, drain)
    drain(9)
    drain(10)
    for k in range(len(flushed)):
        flush(k).wait()
    each(FAR, lambda i: unit_copy(i).wait())


def run_forward(weights, images, cotangent, counts, labels, levels, class_table, noise_table, modw, modb, vectors):
    n_dp, n_head = lax.axis_size("dp"), lax.axis_size("head")
    rows, cols = weights[0].shape[1:]
    lines, across, wide = n_dp // 2, n_head // 2, 2 * cols
    board = (RES, SLOTS, RES, C)
    shape = jax.ShapeDtypeStruct
    return pl.pallas_call(
        functools.partial(forward_kernel, lines),
        out_shape=(
            shape((FAR, 2, lines, 2, rows, across * wide), BF16),
            shape(board, F32),
            shape((2,) + board, F32),
            shape((4, C, ALL), BF16),
            shape((ALL, C), BF16),
            shape(board, F32),
            shape((ALL, C), BF16),
            shape((4, ALL, C), BF16),
            shape((16, C), F32),
            shape((2 * SLOTS, C), F32),
            shape((6, SLOTS, C), F32),
            shape((n_dp * SLOTS, 128), F32),
            shape((n_dp, SLOTS, 128), jnp.int32),
            shape((16, C), F32),
        ),
        in_specs=[ANY] * 6 + [SMEM] * 3 + [VMEM] * (4 + VECTORS),
        out_specs=(ANY,) * 8 + (VMEM,) * 6,
        scratch_shapes=[
            pltpu.VMEM((2, PAIRS, rows, cols), BF16),
            pltpu.VMEM((PAIRS, 2, lines, 2, rows, across * wide), BF16),
            pltpu.VMEM((16, cols), BF16),
            pltpu.VMEM((SLOTS, 128), jnp.int32),
            pltpu.VMEM((128, 1024), BF16),
            pltpu.VMEM((128, 2 * C), BF16),
            pltpu.VMEM((n_head, 16, cols), BF16),
            pltpu.VMEM((n_dp, 2 * SLOTS, C), BF16),
            pltpu.VMEM((n_dp, 2 * SLOTS, C), BF16),
            pltpu.VMEM((3, ALL + 2 * LINE, C), BF16),
            pltpu.VMEM(board, F32),
            pltpu.VMEM((SLOTS, C), F32),
            pltpu.VMEM(board, F32),
            pltpu.VMEM(board, F32),
            pltpu.VMEM((2,) + board, F32),
            pltpu.VMEM((4, C, ALL), BF16),
            pltpu.VMEM((ALL, C), BF16),
            pltpu.VMEM((4, ALL, C), BF16),
            pltpu.VMEM((4, ALL, C), BF16),
            pltpu.VMEM((ALL, C), BF16),
            pltpu.VMEM((2 * SLOTS, C), F32),
            DMA((5,)),
            DMA((5,)),
            DMA((5,)),
            DMA((PAIRS, lines - 1)),
            DMA((PAIRS, lines - 1)),
            DMA((PAIRS,)),
            DMA((PAIRS, 2)),
            DMA((PAIRS, 2)),
            DMA((PAIRS, 2)),
            DMA((PAIRS, 2)),
            DMA((PAIRS, 4)),
            DMA((PAIRS, 4)),
            DMA((n_head - 1,)),
            DMA((n_head - 1,)),
            DMA((n_dp - 1,)),
            DMA((n_dp - 1,)),
            DMA((n_dp - 1,)),
            DMA((n_dp - 1,)),
            DMA((FAR,)),
            DMA((11,)),
            DMA((2,)),
        ],
        compiler_params=pltpu.CompilerParams(
            collective_id=0, has_side_effects=True, vmem_limit_bytes=62 * 2**20
        ),
        name="gather_forward",
    )(
        *weights,
        images,
        cotangent,
        counts,
        labels,
        levels,
        class_table,
        noise_table,
        modw,
        modb,
        *vectors,
    )


def backward_kernel(
    lines,
    whole_ref,
    turned_ref,
    right_ref,
    grad_low_ref,
    grad_resid_ref,
    conv_ref,
    slopes_ref,
    images_hbm,
    stats_ref,
    vecs_ref,
    mod_ref,
    sums_in,
    pre_ref,
    ids_ref,
    modw_table,
    out_a,
    out_b,
    out_qkv,
    out_proj,
    image_ref,
    class_ref,
    modw_out,
    modb_out,
    vec_out,
    mine,
    from_x,
    from_y,
    from_z,
    far_x,
    far_y,
    far_z,
    ends,
    modw_ref,
    lefts,
    rights,
    grads,
    stage,
    weights,
    total,
    board,
    slopes,
    image_mine,
    images_ref,
    sums_ref,
    pair_ref,
    coef_ref,
    gm_mine,
    gm_all,
    mw_mine,
    mw_got,
    ge_all,
    vs_mine,
    vs_got,
    vt_mine,
    vt_all,
    x_send,
    x_recv,
    y_send,
    y_recv,
    z_send,
    z_recv,
    p_send,
    p_recv,
    e_send,
    e_recv,
    e_local,
    op_send,
    op_recv,
    op_local,
    load_sem,
    in_sem,
    out_sem,
    gm_send,
    gm_recv,
    mw_send,
    mw_recv,
    ge_send,
    ge_recv,
    vs_send,
    vs_recv,
    vt_send,
    vt_recv,
):
    z, y, x, c = place()
    d, h = lax.axis_index("dp"), lax.axis_index("head")
    n_dp, n_head = lines * 2, 4
    half = lines // 2
    inner = jnp.logical_and(z > 0, z < lines - 1)
    rows, wide = from_z.shape[2], from_z.shape[3]
    cols = wide // 2
    sibling = at_chip(z, y, x, 1 - c)
    along_x = at_chip(z, y, 1 - x, c)
    along_y = at_chip(z, 1 - y, x, c)
    line = [at_chip(lax.rem(z + k, lines), y, x, c) for k in range(1, lines)]
    column, heads = column_peers(n_dp), head_peers(n_head)

    own_rows = pl.ds(LINE, ALL)

    def operand(k):
        if k == 0:
            return right_ref.at[2 + c], right_ref.at[3 - c], rights.at[0, span(c, ALL)]
        if k == 1:
            return turned_ref.at[c], turned_ref.at[1 - c], lefts.at[1, :, span(c, ALL)]
        if k == 2:
            return right_ref.at[c], right_ref.at[1 - c], rights.at[1, span(c, ALL)]
        if k == 3:
            return turned_ref.at[0], turned_ref.at[0], lefts.at[0, :, span(c, ALL)]
        if k == 4:
            return grad_low_ref, grad_low_ref, grads.at[1, c, own_rows]
        return turned_ref.at[k - 3], turned_ref.at[k - 3], lefts.at[k - 3, :, span(c, ALL)]

    def op_own(k):
        source, _, target = operand(k)
        return pltpu.make_async_copy(source, target, op_local.at[k])

    def op_copy(k):
        _, source, target = operand(k)
        return remote(source, target, op_send.at[k], op_recv.at[k], sibling)

    def stage_copy():
        return remote(grads.at[1, c, own_rows], stage, op_send.at[7], op_recv.at[7], sibling)

    def op_wait(k):
        op_own(k).wait()
        op_copy(k).wait_recv()

    def lanes(xx):
        return span(xx, wide)

    first, second = pl.ds(0, rows // 2), pl.ds(rows // 2, rows // 2)

    def is_far(i):
        return isinstance(i, int) and i >= FAR

    def x_copy(i, part):
        if is_far(i):
            into = far_x.at[i - FAR]
            if part == 0:
                src, dst = mine.at[i, z, 1 - y, second, lanes(1 - x)], into.at[pl.ds(rows, rows // 2)]
            else:
                src, dst = mine.at[i, z, y, :, lanes(1 - x)], into.at[pl.ds(0, rows)]
        elif part == 0:
            src, dst = mine.at[i, pl.ds(half, half), 1 - y, :, lanes(1 - x)], from_x.at[i, pl.ds(lines, half)]
        else:
            src, dst = mine.at[i, :, y, :, lanes(1 - x)], from_x.at[i, pl.ds(0, lines)]
        return remote(src, dst, x_send.at[i, part], x_recv.at[i, part], along_x)

    def y_copy(i, part):
        if is_far(i):
            into = far_y.at[i - FAR]
            if part == 0:
                src, dst = mine.at[i, z, 1 - y, first, lanes(1 - x)], into.at[pl.ds(rows, rows // 2)]
            else:
                src, dst = mine.at[i, z, 1 - y, :, lanes(x)], into.at[pl.ds(0, rows)]
        elif part == 0:
            src, dst = mine.at[i, pl.ds(0, half), 1 - y, :, lanes(1 - x)], from_y.at[i, pl.ds(lines, half)]
        else:
            src, dst = mine.at[i, :, 1 - y, :, lanes(x)], from_y.at[i, pl.ds(0, lines)]
        return remote(src, dst, y_send.at[i, part], y_recv.at[i, part], along_y)

    beyond = lax.rem(z + 2, lines)
    opposite = lines - 1 - z
    near_end = at_chip(1 + z // (lines - 1), y, x, c)

    def z_block(i, zz):
        return mine.at[i, zz] if is_far(i) else mine.at[i, zz, y, :, lanes(x)]

    def z_slot(i, k):
        return far_z.at[i - FAR, k] if is_far(i) else from_z.at[i, k]

    def z_copy(i, k):
        return remote(
            z_block(i, lax.rem(z + k + 1, lines)), z_slot(i, k), z_send.at[i, k], z_recv.at[i, k], line[k]
        )

    def z_give(i):
        return remote(z_block(i, opposite), z_slot(i, 3), p_send.at[i], p_recv.at[i], near_end)

    def z_start(i):
        @pl.when(jnp.logical_not(inner))
        def _():
            z_give(i).start()

        @pl.when(z < lines - 1)
        def _():
            z_copy(i, 0).start()

        @pl.when(z > 0)
        def _():
            z_copy(i, 2).start()

        @pl.when(jnp.logical_not(inner))
        def _():
            z_copy(i, 1).start()

    def z_mix(i):
        @pl.when(inner)
        def _():
            z_give(i).wait_recv()
            if is_far(i):
                mine[i, beyond] += far_z[i - FAR, 3]
            else:
                mine[i, beyond, y, :, lanes(x)] += from_z[i, 3]
            z_copy(i, 1).start()

    def z_wait(i):
        z_copy(i, 1).wait_recv()

        @pl.when(z > 0)
        def _():
            z_copy(i, 0).wait_recv()

        @pl.when(z < lines - 1)
        def _():
            z_copy(i, 2).wait_recv()

    def z_drain(i):
        z_copy(i, 1).wait_send()

        @pl.when(z < lines - 1)
        def _():
            z_copy(i, 0).wait_send()

        @pl.when(z > 0)
        def _():
            z_copy(i, 2).wait_send()

        @pl.when(jnp.logical_not(inner))
        def _():
            z_give(i).wait_send()

    def target(i, core):
        if isinstance(i, int) and i == 10:
            return out_proj if core == 1 else out_qkv.at[2]
        if isinstance(i, int) and i == 9:
            return out_qkv.at[core]
        if isinstance(i, int) and i == 4:
            return out_b.at[8] if core == 1 else out_a.at[8]
        if isinstance(i, int) and i > 4:
            return out_b.at[4 * core + i - 5]
        return out_a.at[4 * core + i]

    def e_copy(i, core):
        return remote(ends.at[1 - c, i], target(i, core), e_send.at[i], e_recv.at[i], sibling)

    def e_own(i, core):
        return pltpu.make_async_copy(ends.at[c, i], target(i, core), e_local.at[i])

    def finish(i, value):
        for cc in range(2):
            ends[cc, i] = value[:, cc * cols : (cc + 1) * cols]
        if i in (4, 10):
            for core in range(2):

                @pl.when(c == core)
                def _():
                    e_copy(i, core).start()
                    e_own(i, core).start()
        else:
            e_copy(i, c).start()
            e_own(i, c).start()

    def offer(i):
        x_copy(i, 0).start()
        y_copy(i, 0).start()

    def relay(i):
        x_copy(i, 0).wait_recv()
        y_copy(i, 0).wait_recv()
        if is_far(i):
            rest = pl.ds(rows, rows // 2)
            mine[i, z, y, first, lanes(1 - x)] += far_y[i - FAR, rest]
            mine[i, z, 1 - y, second, lanes(x)] += far_x[i - FAR, rest]
        else:
            for j in range(half):
                mine[i, j, y, :, lanes(1 - x)] += from_y[i, lines + j]
                mine[i, half + j, 1 - y, :, lanes(x)] += from_x[i, lines + j]
        x_copy(i, 1).start()
        y_copy(i, 1).start()

    def collect(i):
        x_copy(i, 1).wait_recv()
        y_copy(i, 1).wait_recv()
        if is_far(i):
            whole_rows = pl.ds(0, rows)
            value = mine[i, z, y, :, lanes(x)].astype(F32)
            value += far_x[i - FAR, whole_rows].astype(F32) + far_y[i - FAR, whole_rows].astype(F32)
            finish(i, value)
            return

        def add(j):
            value = mine[i, j, y, :, lanes(x)].astype(F32)
            value += from_x[i, j].astype(F32) + from_y[i, j].astype(F32)
            mine[i, j, y, :, lanes(x)] = value.astype(BF16)

        each(lines, add)
        z_start(i)

    def last(i):
        z_wait(i)
        if is_far(i):
            for yy in range(2):
                value = mine[i, z, yy].astype(F32)
                for k in range(lines - 1):
                    value += far_z[i - FAR, k, yy].astype(F32)
                mine[i, z, yy] = value.astype(BF16)
            offer(i)
            return
        value = mine[i, z, y, :, lanes(x)].astype(F32)
        for k in range(lines - 1):
            value += from_z[i, k].astype(F32)
        finish(i, value)

    def put(i, n, value):
        mine[i, :, :, :, chunk(n)] = value.astype(BF16).reshape(mine.shape[1:4] + (WIDTH,))

    def plain_unit(i, left, right):
        for n in range(CHUNKS):
            put(i, n, dot(lefts[left], rights[right, :, chunk(n)]))

    def conv_unit(i, left, tap):
        where, side = lines_from(2 - tap // 3), 2 - tap % 3
        for n in range(CHUNKS):
            both = jnp.concatenate([grads[side, core, where, chunk(n)] for core in range(2)], axis=0)
            put(i, n, dot(lefts[left], both))

    def extra_b():
        @pl.when(c == 1)
        def _():
            conv_unit(4, 2, 8)

    def extra_a():
        @pl.when(c == 0)
        def _():
            conv_unit(4, 3, 8)

    def spread_sides(core):
        def by_line(yy):
            value = grads[1, core, pl.ds(pl.multiple_of((yy + 1) * LINE, LINE), LINE)].astype(F32)
            left, right = shifted(value)
            spot_rows = pl.ds(pl.multiple_of((yy + 1) * LINE, LINE), LINE)
            grads[0, core, spot_rows] = left.astype(BF16)
            grads[2, core, spot_rows] = right.astype(BF16)

        each(RES, by_line)

    def load(tap, base):
        ninth = tap // 8
        i = (base // 2 + tap % 4) * (1 - ninth) + 4 * ninth
        k = (tap // 4) % 2 + (base // 10) * ninth
        return pltpu.make_async_copy(whole_ref.at[i, k], weights.at[tap % 2], load_sem.at[tap % 2])

    def conv_back(tap, base):
        load(tap, base).wait()

        @pl.when(tap < 8)
        def _():
            load(tap + 1, base).start()

        part = grads[2 - tap % 3, c, lines_from(2 - tap // 3)]
        for n in range(CHUNKS):
            value = dot_nt(part, weight_rows(weights.at[tap % 2], n))
            total[:, :, :, chunk(n)] += value.reshape(RES, SLOTS, RES, WIDTH)

    def conv_back_range(first, stop, base):
        def body(tap, carry):
            conv_back(tap, base)
            return carry

        lax.fori_loop(first, stop, body, 0)

    def slope(values):
        sigma = jax.nn.sigmoid(values)
        return sigma * (1.0 + values * (1.0 - sigma))

    for k in (0, 2):
        from_z[:, k] = jnp.zeros_like(from_z[:, k])
        far_z[:, k] = jnp.zeros_like(far_z[:, k])
    greet(column + heads)
    def op_start(k):
        op_own(k).start()
        op_copy(k).start()

    for k in range(6):
        op_start(k)
    load(0, 10).start()

    def fetch(k):
        source, target = (
            (conv_ref, board),
            (slopes_ref.at[1], slopes),
            (slopes_ref.at[0], slopes),
            (grad_resid_ref, board),
            (images_hbm, images_ref),
        )[k]
        return pltpu.make_async_copy(source, target, in_sem.at[k])

    fetch(0).start()
    fetch(1).start()
    vs_mine[...] = jnp.zeros_like(vs_mine)
    edge = jnp.zeros((LINE, C), BF16)
    for j in range(3):
        for core in range(2):
            grads[j, core, 0:LINE] = edge
            grads[j, core, ALL + LINE : ALL + 2 * LINE] = edge
    total[...] = jnp.zeros_like(total)
    sums_ref[...] = sums_in[...]
    modw_ref[...] = jnp.zeros_like(modw_ref)
    modw_ref[0:rows] = modw_table[...]

    def norm_b_value(n):
        return (board[:, n].reshape(PIX, C) - stats_ref[2, row(n)]) * stats_ref[3, row(n)]

    def norm_a_value(n):
        return (images_ref[span(n, PIX)].astype(F32) - stats_ref[0, row(n)]) * stats_ref[1, row(n)]

    def back_sums(get):
        def body(n):
            grad = (total[:, n] * slopes[:, n]).reshape(PIX, C)
            total[:, n] = grad.reshape(RES, RES, C)
            pair_ref[row(n)] = sum_rows(grad * get(n))
            pair_ref[row(SLOTS + n)] = sum_rows(grad)

        each(SLOTS, body)

    def back_factors(factor, inverse):
        coef_ref[0:SLOTS] = factor * inverse
        means = group_mean(pair_ref[...] * jnp.concatenate([factor, factor], axis=0))
        coef_ref[SLOTS : 2 * SLOTS] = means[:SLOTS] * inverse
        coef_ref[2 * SLOTS :] = means[SLOTS:] * inverse

    def back_value(n, get):
        value = total[:, n].reshape(PIX, C) * coef_ref[row(n)]
        return value - get(n) * coef_ref[row(SLOTS + n)] - coef_ref[row(2 * SLOTS + n)]

    def gm_copy(k):
        return remote(gm_mine, gm_all.at[d], gm_send.at[k], gm_recv.at[k], column[k])

    def mw_copy(k):
        return remote(
            mw_mine.at[lax.rem(h + k + 1, n_head)], mw_got.at[k], mw_send.at[k], mw_recv.at[k], heads[k]
        )

    def ge_copy(k):
        return remote(ge_all.at[h], ge_all.at[h], ge_send.at[k], ge_recv.at[k], heads[k])

    def vs_copy(k):
        return remote(
            vs_mine.at[lax.rem(h + k + 1, n_head)], vs_got.at[k], vs_send.at[k], vs_recv.at[k], heads[k]
        )

    def vt_copy(k):
        return remote(vt_mine, vt_all.at[d], vt_send.at[k], vt_recv.at[k], column[k])

    def image_copy():
        return pltpu.make_async_copy(image_mine, image_ref, out_sem)

    count = n_dp * SLOTS

    def start():
        op_wait(0)
        op_wait(1)

    def dw(i):
        if i == 10:
            plain_unit(10, 1, 0)
        elif i == 9:
            op_wait(2)
            op_wait(3)
            plain_unit(9, 0, 1)
        elif i > 4:
            conv_unit(i, 2, 4 * c + i - 5)
        else:
            conv_unit(i, 3, 4 * c + i)

    def sides():
        op_wait(4)
        op_wait(5)
        spread_sides(0)
        spread_sides(1)

    def back_b_first():
        load(0, 0).start()
        op_start(6)
        fetch(0).wait()
        fetch(1).wait()
        back_sums(norm_b_value)
        alone, with_norm = pair_ref[SLOTS:], pair_ref[:SLOTS]
        scale = mod_ref[0:SLOTS] + 1.0
        gm_mine[...] = jnp.concatenate([vecs_ref[3:4] * with_norm + vecs_ref[4:5] * alone, alone], axis=0).astype(BF16)
        gm_all[d] = gm_mine[...]
        for k in range(n_dp - 1):
            gm_copy(k).start()
        sums_ref[3:4] = sum_rows(with_norm * scale)
        sums_ref[4:5] = sum_rows(alone * scale)
        back_factors(scale * vecs_ref[3:4], stats_ref[3])

    def back_b_second():
        fetch(2).start()
        fetch(4).start()

        def body(n):
            value = back_value(n, norm_b_value).astype(BF16).astype(F32)
            sums_ref[2:3] += sum_rows(value)
            total[:, n] = value.reshape(RES, RES, C)

        each(SLOTS, body)
        fetch(3).start()

    def lower():
        def by_line(yy):
            spot_rows = pl.ds(pl.multiple_of((yy + 1) * LINE, LINE), LINE)
            grads[1, c, spot_rows] = total[yy].reshape(LINE, C).astype(BF16)

        each(RES, by_line)
        stage_copy().start()
        spread_sides(c)
        total[...] = jnp.zeros_like(total)

    def take():
        stage_copy().wait_recv()

        def by_line(yy):
            spot_rows = pl.ds(pl.multiple_of((yy + 1) * LINE, LINE), LINE)
            grads[1, 1 - c, spot_rows] = stage[span(yy, LINE)]

        each(RES, by_line)
        spread_sides(1 - c)
        op_wait(6)

    def modulation():
        for k in range(n_dp - 1):
            gm_copy(k).wait()
        parts = gm_all[...].astype(F32)
        gm_scale = parts[:, :SLOTS].reshape(count, C)
        gm_offset = parts[:, SLOTS:].reshape(count, C)
        pre = pre_ref[...]
        emb = silu(pre).astype(BF16)
        part_rows = rows // n_head
        for k, value in ((0, gm_scale), (1, gm_offset)):
            low_value = value.astype(BF16)
            grad_w = dot_tn(emb, low_value)
            place_lanes = slice(k * C, (k + 1) * C)
            for hh in range(n_head):
                mw_mine[hh, 0:part_rows, place_lanes] = grad_w[hh * part_rows : (hh + 1) * part_rows]
                mw_mine[hh, part_rows : part_rows + 8, place_lanes] = jnp.broadcast_to(sum_rows(value), (8, C))
        grad_e = dot_nt(gm_scale.astype(BF16), modw_ref[:, :C]) + dot_nt(gm_offset.astype(BF16), modw_ref[:, C:])
        grad_e = grad_e * slope(pre)
        label = ids_ref[...].reshape(count, 128)[:, 0:1].astype(F32)
        lane = lax.broadcasted_iota(jnp.int32, grad_e.shape, 1)
        ge_all[h] = jnp.where(lane < rows, grad_e, label)
        for k in range(n_head - 1):
            mw_copy(k).start()
            ge_copy(k).start()

    def back_a_first():
        fetch(2).wait()
        fetch(4).wait()
        back_sums(norm_a_value)
        sums_ref[0:1] = sum_rows(pair_ref[:SLOTS])
        sums_ref[1:2] = sum_rows(pair_ref[SLOTS:])
        for hh in range(n_head):
            vs_mine[hh] = sums_ref[:, hh * cols : (hh + 1) * cols]
        for k in range(n_head - 1):
            vs_copy(k).start()
        back_factors(jnp.broadcast_to(vecs_ref[0:1], (SLOTS, C)), stats_ref[1])

    def back_a_second():
        fetch(3).wait()

        def body(n):
            image_mine[span(n, PIX)] = back_value(n, norm_a_value) + board[:, n].reshape(PIX, C)

        each(SLOTS, body)
        image_copy().start()

    def vec_first():
        value = vs_mine[h]
        for k in range(n_head - 1):
            vs_copy(k).wait()
            value += vs_got[k]
        vt_mine[...] = value
        vt_all[d] = value
        for k in range(n_dp - 1):
            vt_copy(k).start()

    def mod_out():
        value = mw_mine[h]
        for k in range(n_head - 1):
            mw_copy(k).wait()
            value += mw_got[k]
        part_rows = rows // n_head
        first_lane = (d * n_head + h) * part_rows
        for k in range(2):
            lanes_of = slice(k * C, (k + 1) * C)
            modw_out[:, k] = value[:part_rows, lanes_of]
            turned_row = pltpu.roll(value[part_rows:, lanes_of], lax.rem(C - first_lane, C), 1)
            modb_out[k : k + 1] = turned_row[0:1, :part_rows]

    def class_out():
        for k in range(n_head - 1):
            ge_copy(k).wait()
        table = class_ref.shape[1]
        part = rows // n_head
        value = ge_all[...].reshape(n_head * count, 128)
        label = value[:, rows : rows + 1].astype(jnp.int32)
        hot = lax.broadcasted_iota(jnp.int32, (n_head * count, table), 1) == label
        own = pltpu.roll(value, lax.rem(128 - h * part, 128), 1).astype(BF16)
        value = dot_tn(own, jnp.where(hot, 1.0, 0.0).astype(BF16))
        class_ref[...] = value[:part]

    def vec_second():
        for k in range(n_dp - 1):
            vt_copy(k).wait()
        value = vt_all[0]
        for k in range(1, n_dp):
            value += vt_all[k]
        vec_out[...] = value

    start()
    dw(10)
    z_start(10)
    dw(9)
    z_start(9)
    sides()
    dw(5)
    offer(5)
    dw(6)
    offer(6)
    dw(7)
    z_mix(10)
    offer(7)
    dw(8)
    relay(5)
    offer(8)
    extra_b()
    conv_back_range(0, 3, 10)
    relay(6)
    conv_back_range(3, 6, 10)
    relay(7)
    conv_back_range(6, 9, 10)
    collect(5)
    back_b_first()
    relay(8)
    z_mix(9)
    back_b_second()
    lower()
    conv_back_range(0, 3, 0)
    collect(6)
    take()
    extra_a()
    offer(4)
    collect(7)
    dw(0)
    z_mix(5)
    offer(0)
    dw(1)
    offer(1)
    dw(2)
    offer(2)
    dw(3)
    z_mix(6)
    collect(8)
    offer(3)
    conv_back_range(3, 6, 0)
    last(10)
    relay(4)
    relay(0)
    z_mix(7)
    conv_back_range(6, 9, 0)
    last(9)
    relay(1)
    relay(2)
    z_mix(8)
    back_a_first()
    relay(3)
    relay(10)
    modulation()
    last(5)
    back_a_second()
    collect(4)
    last(6)
    vec_first()
    z_mix(4)
    mod_out()
    last(7)
    class_out()
    last(8)
    vec_second()
    collect(0)
    relay(9)
    z_mix(0)
    last(4)
    collect(1)
    z_mix(1)
    last(0)
    collect(2)
    last(1)
    z_mix(2)
    collect(3)
    collect(10)
    last(2)
    collect(9)
    z_mix(3)
    last(3)

    for k in range(7):
        op_copy(k).wait_send()
    stage_copy().wait_send()
    image_copy().wait()

    def drain(i):
        for part in range(2):
            x_copy(i, part).wait_send()
            y_copy(i, part).wait_send()
        z_drain(i)
        e_copy(i, 0).wait()
        e_own(i, 0).wait()

    each(FAR, drain)
    drain(9)
    drain(10)


def run_backward(whole, turned, right, grad_low, grad_resid, conv_out, slopes, images, stats, vecs, mod, sums, pre, ids, modw, classes):
    n_dp, n_head = lax.axis_size("dp"), lax.axis_size("head")
    _, _, lines, _, rows, depth = whole.shape
    cols = depth // n_head
    wide = 2 * cols
    board = (RES, SLOTS, RES, C)
    shape = jax.ShapeDtypeStruct
    return pl.pallas_call(
        functools.partial(backward_kernel, lines),
        out_shape=(
            shape((9, rows, cols), F32),
            shape((9, rows, cols), F32),
            shape((3, rows, cols), F32),
            shape((rows, cols), F32),
            shape((ALL, C), F32),
            shape((rows // n_head, classes), F32),
            shape((rows // n_head, 2, C), F32),
            shape((2, rows // n_head), F32),
            shape((16, cols), F32),
        ),
        in_specs=[ANY] * 8 + [VMEM] * 7,
        out_specs=(ANY,) * 5 + (VMEM,) * 4,
        scratch_shapes=[
            pltpu.VMEM((PAIRS, lines, 2, rows, depth), BF16),
            pltpu.VMEM((FAR, lines + lines // 2, rows, wide), BF16),
            pltpu.VMEM((FAR, lines + lines // 2, rows, wide), BF16),
            pltpu.VMEM((FAR, 4, rows, wide), BF16),
            pltpu.VMEM((PAIRS - FAR, rows + rows // 2, wide), BF16),
            pltpu.VMEM((PAIRS - FAR, rows + rows // 2, wide), BF16),
            pltpu.VMEM((PAIRS - FAR, 4, 2, rows, depth), BF16),
            pltpu.VMEM((2, PAIRS, rows, cols), F32),
            pltpu.VMEM((128, 2 * C), BF16),
            pltpu.VMEM((4, C, 2 * ALL), BF16),
            pltpu.VMEM((2, 2 * ALL, C), BF16),
            pltpu.VMEM((3, 2, ALL + 2 * LINE, C), BF16),
            pltpu.VMEM((ALL, C), BF16),
            pltpu.VMEM((2, lines, 2, rows, depth), BF16),
            pltpu.VMEM(board, F32),
            pltpu.VMEM(board, F32),
            pltpu.VMEM(board, F32),
            pltpu.VMEM((ALL, C), F32),
            pltpu.VMEM((ALL, C), BF16),
            pltpu.VMEM((16, C), F32),
            pltpu.VMEM((2 * SLOTS, C), F32),
            pltpu.VMEM((3 * SLOTS, C), F32),
            pltpu.VMEM((2 * SLOTS, C), BF16),
            pltpu.VMEM((n_dp, 2 * SLOTS, C), BF16),
            pltpu.VMEM((n_head, rows // n_head + 8, 2 * C), F32),
            pltpu.VMEM((n_head - 1, rows // n_head + 8, 2 * C), F32),
            pltpu.VMEM((n_head, n_dp * SLOTS, 128), F32),
            pltpu.VMEM((n_head, 16, cols), F32),
            pltpu.VMEM((n_head - 1, 16, cols), F32),
            pltpu.VMEM((16, cols), F32),
            pltpu.VMEM((n_dp, 16, cols), F32),
            DMA((PAIRS, 2)),
            DMA((PAIRS, 2)),
            DMA((PAIRS, 2)),
            DMA((PAIRS, 2)),
            DMA((PAIRS, lines - 1)),
            DMA((PAIRS, lines - 1)),
            DMA((PAIRS,)),
            DMA((PAIRS,)),
            DMA((PAIRS,)),
            DMA((PAIRS,)),
            DMA((PAIRS,)),
            DMA((8,)),
            DMA((8,)),
            DMA((7,)),
            DMA((2,)),
            DMA((5,)),
            DMA,
            DMA((n_dp - 1,)),
            DMA((n_dp - 1,)),
            DMA((n_head - 1,)),
            DMA((n_head - 1,)),
            DMA((n_head - 1,)),
            DMA((n_head - 1,)),
            DMA((n_head - 1,)),
            DMA((n_head - 1,)),
            DMA((n_dp - 1,)),
            DMA((n_dp - 1,)),
        ],
        compiler_params=pltpu.CompilerParams(
            collective_id=1, has_side_effects=True, vmem_limit_bytes=64 * 2**20 - 2**18
        ),
        name="backward_scatter",
    )(whole, turned, right, grad_low, grad_resid, conv_out, slopes, images, stats, vecs, mod, sums, pre, ids, modw)


def results_kernel(count, *refs):
    sources, vec_ref, refs = refs[:count], refs[count], refs[count + 1 :]
    targets, vectors, sems = refs[:count], refs[count:-1], refs[-1]
    copies = [
        pltpu.make_async_copy(source, target, sems.at[k])
        for k, (source, target) in enumerate(zip(sources, targets))
    ]
    for copy in copies:
        copy.start()
    for k, ref in enumerate(vectors):
        ref[...] = vec_ref[k].reshape(ref.shape)
    for copy in copies:
        copy.wait()


def run_results(arrays, vec):
    count = len(arrays)
    shape = jax.ShapeDtypeStruct
    return pl.pallas_call(
        functools.partial(results_kernel, count),
        out_shape=tuple(shape(one.shape, one.dtype) for one in arrays)
        + (shape(vec.shape[1:], F32),) * VECTORS,
        in_specs=[VMEM] * (count + 1),
        out_specs=(ANY,) * count + (VMEM,) * VECTORS,
        scratch_shapes=[DMA((count,))],
        compiler_params=pltpu.CompilerParams(vmem_limit_bytes=60 * 2**20),
        name="results",
    )(*arrays, vec)


def direct(rows, cols):
    n_dp, n_head = lax.axis_size("dp"), lax.axis_size("head")
    return n_head == 4 and n_dp == 8 and rows % 32 == 0 and cols % 64 == 0


def fast_shards(
    images,
    cotangent,
    counts,
    labels,
    levels,
    noise_table,
    class_table,
    gain_a,
    shift_a,
    conv_a,
    bias_a,
    mod_weight,
    mod_bias,
    gain_b,
    shift_b,
    conv_b,
    bias_b,
    gain_c,
    shift_c,
    qkv_weight,
    proj_weight,
    proj_bias,
):
    weights = (
        jnp.swapaxes(conv_a, 0, 1),
        jnp.swapaxes(conv_b, 0, 1),
        jnp.swapaxes(qkv_weight, 0, 1),
        proj_weight,
    )
    vectors = (gain_a, shift_a, bias_a, gain_b, shift_b, bias_b, gain_c, shift_c, proj_bias)
    modw = mod_weight.reshape(mod_weight.shape[0], 2 * C)
    flat = images.reshape(ALL, C)
    (
        whole,
        conv_out,
        slopes,
        turned,
        block_out,
        grad_resid,
        grad_low,
        right,
        vecs,
        mod,
        stats,
        pre,
        all_ids,
        sums,
    ) = run_forward(
        weights,
        flat,
        cotangent.reshape(ALL, C),
        counts,
        labels,
        levels,
        class_table.T,
        noise_table,
        modw,
        mod_bias,
        vectors,
    )
    *arrays, vec = run_backward(
        whole,
        turned,
        right,
        grad_low,
        grad_resid,
        conv_out,
        slopes,
        flat,
        stats,
        vecs,
        mod,
        sums,
        pre,
        all_ids,
        modw,
        class_table.shape[0],
    )
    block_out, conva, convb, qkvw, projw, image_grad, class_grad, modw_grad, modb_grad, *rest = run_results(
        (block_out, *arrays), vec
    )
    gaina, shifta, biasa, gainb, shiftb, biasb, gainc, shiftc, projb = rest
    return (
        block_out.reshape(images.shape),
        image_grad.reshape(images.shape),
        class_grad.T,
        gaina,
        shifta,
        jnp.swapaxes(conva, 0, 1),
        biasa,
        modw_grad,
        modb_grad,
        gainb,
        shiftb,
        jnp.swapaxes(convb, 0, 1),
        biasb,
        gainc,
        shiftc,
        jnp.swapaxes(qkvw, 0, 1),
        projw,
        projb,
    )


def shards(*args):
    rows, _, cols = args[9].shape
    if direct(rows, cols):
        return fast_shards(*args)
    return plain_shards(*args)


def solution(mesh):
    placed = (
        P(("dp", "head"), None, None, None),
        P(("dp", "head"), None, None, None),
        P(),
        P(("dp", "head")),
        P(("dp", "head")),
        P(),
        P(None, "dp"),
        P("head"),
        P("head"),
        P("dp", None, "head"),
        P("head"),
        P("dp", None, None),
        P(),
        P("head"),
        P("head"),
        P("dp", None, "head"),
        P("head"),
        P("head"),
        P("head"),
        P("dp", None, "head"),
        P("dp", "head"),
        P("head"),
    )
    return jax.shard_map(
        shards,
        mesh=mesh,
        in_specs=placed,
        out_specs=(
            P(("dp", "head"), None, None, None),
            P(("dp", "head"), None, None, None),
            P(None, ("dp", "head")),
            P("head"),
            P("head"),
            P("dp", None, "head"),
            P("head"),
            P(("dp", "head"), None, None),
            P(None, ("dp", "head")),
            P("head"),
            P("head"),
            P("dp", None, "head"),
            P("head"),
            P("head"),
            P("head"),
            P("dp", None, "head"),
            P("dp", "head"),
            P("head"),
        ),
        check_vma=False,
    )
```

```python
import functools

import jax
import jax.numpy as jnp
from jax import lax
from jax.experimental import pallas as pl
from jax.experimental.pallas import tpu as pltpu
from jax.sharding import PartitionSpec as P

C = 768
DH = 64
GROUPS = 32


EPSILON = 1e-05
HIGHEST = lax.Precision.HIGHEST


def norm_forward(values, gain, shift):
    count, chans = (values.shape[0], values.shape[-1])
    span = C // GROUPS
    grouped = values.reshape(count, -1, chans // span, span)
    mean = jnp.mean(grouped, axis=(1, 3), keepdims=True)
    centred = grouped - mean
    inverse = lax.rsqrt(jnp.mean(centred * centred, axis=(1, 3), keepdims=True) + EPSILON)
    normed = (centred * inverse).reshape(values.shape)
    return (normed * gain + shift, normed, inverse)


def norm_backward(grad_out, normed, inverse, gain):
    grad_gain = jnp.sum(grad_out * normed, axis=(0, 1, 2))
    grad_shift = jnp.sum(grad_out, axis=(0, 1, 2))
    count, chans = (grad_out.shape[0], grad_out.shape[-1])
    span = C // GROUPS
    layout = (count, -1, chans // span, span)
    grad_normed = (grad_out * gain).reshape(layout)
    normed_groups = normed.reshape(layout)
    mean_one = jnp.mean(grad_normed, axis=(1, 3), keepdims=True)
    mean_two = jnp.mean(grad_normed * normed_groups, axis=(1, 3), keepdims=True)
    grad_in = inverse * (grad_normed - mean_one - normed_groups * mean_two)
    return (grad_in.reshape(grad_out.shape), grad_gain, grad_shift)


def silu_slope(values):
    sigma = jax.nn.sigmoid(values)
    return sigma * (1.0 + values * (1.0 - sigma))


def patches_of(act):
    count, rows, cols, chans = act.shape
    padded = jnp.pad(act, ((0, 0), (1, 1), (1, 1), (0, 0)))
    taps = [padded[:, i : i + rows, j : j + cols, :] for i in range(3) for j in range(3)]
    return jnp.stack(taps, axis=3).reshape(count * rows * cols, 9, chans)


def contract_rows(left, right):
    return lax.dot_general(
        left, right, (((0,), (0,)), ((), ())), preferred_element_type=jnp.float32
    )


def contract_cols(left, right):
    return lax.dot_general(
        left, right, (((1,), (1,)), ((), ())), preferred_element_type=jnp.float32
    )


def conv_back(grad_low, weight, count, rows, cols):
    chans = weight.shape[0]
    padded = jnp.zeros((count, rows + 2, cols + 2, chans), jnp.float32)
    for tap in range(9):
        i, j = divmod(tap, 3)
        part = contract_cols(grad_low, weight[:, tap, :]).reshape(count, rows, cols, chans)
        padded = padded.at[:, i : i + rows, j : j + cols, :].add(part)
    return padded[:, 1 : rows + 1, 1 : cols + 1, :]


def keep_same(values):
    return values


def live_rows(counts, first, number, count):
    sums = jnp.sum(counts, axis=1)
    chosen = lax.dynamic_slice_in_dim(sums, first, number)
    slots = lax.iota(jnp.int32, count)
    return (slots[None, :] < chosen[:, None]).astype(jnp.float32).reshape(number * count)


def residual_forward(source, mod_pair, weights, spread):
    (
        conv_one,
        conv_two,
        gain_one,
        shift_one,
        bias_one,
        gain_two,
        shift_two,
        bias_two,
        gain_three,
        shift_three,
    ) = weights
    out_a, normed_a, inverse_a = norm_forward(source, gain_one, shift_one)
    wide_a = spread(jax.nn.silu(out_a).astype(jnp.bfloat16))
    conv_out_a = (
        jnp.einsum("ptc,cto->po", patches_of(wide_a), conv_one, preferred_element_type=jnp.float32)
        + bias_one
    ).reshape(source.shape)
    scale = mod_pair[:, :, 0:1, :]
    offset = mod_pair[:, :, 1:2, :]
    out_b, normed_b, inverse_b = norm_forward(conv_out_a, gain_two, shift_two)
    inner_b = offset + out_b * (scale + 1.0)
    wide_b = spread(jax.nn.silu(inner_b).astype(jnp.bfloat16))
    conv_out_b = (
        jnp.einsum("ptc,cto->po", patches_of(wide_b), conv_two, preferred_element_type=jnp.float32)
        + bias_two
    ).reshape(source.shape)
    resid = source + conv_out_b
    out_c, normed_c, inverse_c = norm_forward(resid, gain_three, shift_three)
    attn_in = out_c.astype(jnp.bfloat16)
    saved = (
        out_a,
        normed_a,
        inverse_a,
        wide_a,
        out_b,
        normed_b,
        inverse_b,
        inner_b,
        wide_b,
        normed_c,
        inverse_c,
        scale,
    )
    return (resid, attn_in, saved)


def residual_backward(grad_attn, grad_out, saved, weights, reduce_value):
    conv_one, conv_two, gain_one, gain_two, gain_three = (
        weights[0],
        weights[1],
        weights[2],
        weights[5],
        weights[8],
    )
    (
        out_a,
        normed_a,
        inverse_a,
        wide_a,
        out_b,
        normed_b,
        inverse_b,
        inner_b,
        wide_b,
        normed_c,
        inverse_c,
        scale,
    ) = saved
    count, rows, cols, local = grad_out.shape
    grad_resid_c, gainc_term, shiftc_term = norm_backward(
        grad_attn, normed_c, inverse_c, gain_three
    )
    grad_resid = grad_out + grad_resid_c
    grad_conv_b = grad_resid.reshape(-1, local).astype(jnp.bfloat16)
    biasb_term = jnp.sum(grad_conv_b.astype(jnp.float32), axis=0)
    convb_term = jnp.einsum(
        "ptc,po->cto", patches_of(wide_b), grad_conv_b, preferred_element_type=jnp.float32
    )
    grad_act_b = reduce_value(conv_back(grad_conv_b, conv_two, count, rows, cols))
    grad_inner = grad_act_b * silu_slope(inner_b)
    grad_offset = jnp.sum(grad_inner, axis=(1, 2))
    grad_scale = jnp.sum(grad_inner * out_b, axis=(1, 2))
    grad_mod = jnp.stack([grad_scale, grad_offset], axis=1)[:, None]
    grad_conv_full, gainb_term, shiftb_term = norm_backward(
        grad_inner * (scale + 1.0), normed_b, inverse_b, gain_two
    )
    grad_conv_a = grad_conv_full.reshape(-1, local).astype(jnp.bfloat16)
    biasa_term = jnp.sum(grad_conv_a.astype(jnp.float32), axis=0)
    conva_term = jnp.einsum(
        "ptc,po->cto", patches_of(wide_a), grad_conv_a, preferred_element_type=jnp.float32
    )
    grad_act_a = reduce_value(conv_back(grad_conv_a, conv_one, count, rows, cols))
    grad_source, gaina_term, shifta_term = norm_backward(
        grad_act_a * silu_slope(out_a), normed_a, inverse_a, gain_one
    )
    image_grad = grad_resid + grad_source
    vectors = (
        gaina_term,
        shifta_term,
        biasa_term,
        gainb_term,
        shiftb_term,
        biasb_term,
        gainc_term,
        shiftc_term,
    )
    return (image_grad, grad_mod, (conva_term, convb_term), vectors)


def attend_forward(block):
    query, key, value = (block[:, :, 0], block[:, :, 1], block[:, :, 2])
    batch, pixels, heads_here, depth = query.shape
    scores = jnp.einsum("bqhd,bkhd->bhqk", query, key, preferred_element_type=jnp.float32) * DH ** (
        -0.5
    )
    top = jnp.max(scores, axis=-1, keepdims=True)
    weights = jnp.exp(scores - top)
    sums = jnp.sum(weights, axis=-1, keepdims=True)
    probs = (weights / sums).astype(jnp.bfloat16)
    logsum = (top + jnp.log(sums))[..., 0]
    mixed = jnp.einsum("bhqk,bkhd->bqhd", probs, value, preferred_element_type=jnp.float32).astype(
        jnp.bfloat16
    )
    return (mixed.reshape(batch, pixels, heads_here * depth), logsum)


def attend_backward(block, logsum, grad_head):
    query, key, value = (block[:, :, 0], block[:, :, 1], block[:, :, 2])
    batch, pixels, heads_here, depth = query.shape
    factor = DH ** (-0.5)
    scores = jnp.einsum("bqhd,bkhd->bhqk", query, key, preferred_element_type=jnp.float32) * factor
    probs = jnp.exp(scores - logsum[..., None])
    grad_value = jnp.einsum(
        "bhqk,bqhd->bkhd", probs.astype(jnp.bfloat16), grad_head, preferred_element_type=jnp.float32
    )
    grad_probs = jnp.einsum("bqhd,bkhd->bhqk", grad_head, value, preferred_element_type=jnp.float32)
    inner = jnp.sum(grad_probs * probs, axis=-1, keepdims=True)
    grad_scores = (probs * (grad_probs - inner)).astype(jnp.bfloat16)
    grad_query = (
        jnp.einsum("bhqk,bkhd->bqhd", grad_scores, key, preferred_element_type=jnp.float32) * factor
    )
    grad_key = (
        jnp.einsum("bhqk,bqhd->bkhd", grad_scores, query, preferred_element_type=jnp.float32)
        * factor
    )
    stacked = jnp.stack([grad_query, grad_key, grad_value], axis=2).astype(jnp.bfloat16)
    return stacked.reshape(batch, pixels, 3, heads_here * depth)


def plain_shards(
    images,
    cotangent,
    counts,
    labels,
    levels,
    noise_table,
    class_table,
    gain_a,
    shift_a,
    conv_a,
    bias_a,
    mod_weight,
    mod_bias,
    gain_b,
    shift_b,
    conv_b,
    bias_b,
    gain_c,
    shift_c,
    qkv_weight,
    proj_weight,
    proj_bias,
):
    rows_a, rows_b, rows_qkv, rows_proj, mod_full, class_full = (
        lax.all_gather(conv_a, "dp", axis=0, tiled=True),
        lax.all_gather(conv_b, "dp", axis=0, tiled=True),
        lax.all_gather(qkv_weight, "dp", axis=0, tiled=True),
        lax.all_gather(proj_weight, "dp", axis=0, tiled=True),
        lax.all_gather(mod_weight, "dp", axis=0, tiled=True),
        lax.all_gather(class_table, "dp", axis=1, tiled=True),
    )
    count, rows, cols, channels = images.shape
    pixels = rows * cols
    groups_n = lax.axis_size("head")
    quarter = channels // groups_n
    heads_local = quarter // DH
    first_dp = lax.axis_index("dp") * groups_n
    class_hot = (labels[:, None] == lax.iota(jnp.int32, class_full.shape[0])[None, :]).astype(
        jnp.bfloat16
    )
    level_hot = (levels[:, None] == lax.iota(jnp.int32, noise_table.shape[0])[None, :]).astype(
        jnp.bfloat16
    )
    embed_pre = jnp.dot(class_hot, class_full, preferred_element_type=jnp.float32) + jnp.dot(
        level_hot, noise_table, preferred_element_type=jnp.float32
    )
    embed = jax.nn.silu(embed_pre).astype(jnp.bfloat16)
    modulation = (
        jnp.einsum("ne,etc->ntc", embed, mod_full, preferred_element_type=jnp.float32)
        + mod_bias.astype(jnp.float32)
    ).astype(jnp.bfloat16)
    mod_pair = modulation.reshape(count, 1, 2, channels)
    (
        conv_one,
        conv_two,
        qkv_full,
        proj_full,
        gain_one,
        shift_one,
        bias_one,
        gain_two,
        shift_two,
        bias_two,
        gain_three,
        shift_three,
        bias_three,
    ) = (
        lax.all_gather(rows_a, "head", axis=2, tiled=True),
        lax.all_gather(rows_b, "head", axis=2, tiled=True),
        lax.all_gather(rows_qkv, "head", axis=2, tiled=True),
        lax.all_gather(rows_proj, "head", axis=1, tiled=True),
        lax.all_gather(gain_a, "head", axis=0, tiled=True),
        lax.all_gather(shift_a, "head", axis=0, tiled=True),
        lax.all_gather(bias_a, "head", axis=0, tiled=True),
        lax.all_gather(gain_b, "head", axis=0, tiled=True),
        lax.all_gather(shift_b, "head", axis=0, tiled=True),
        lax.all_gather(bias_b, "head", axis=0, tiled=True),
        lax.all_gather(gain_c, "head", axis=0, tiled=True),
        lax.all_gather(shift_c, "head", axis=0, tiled=True),
        lax.all_gather(proj_bias, "head", axis=0, tiled=True),
    )
    weights = (
        conv_one,
        conv_two,
        gain_one,
        shift_one,
        bias_one,
        gain_two,
        shift_two,
        bias_two,
        gain_three,
        shift_three,
    )
    live = live_rows(counts, first_dp + lax.axis_index("head"), 1, count)
    total = count * pixels
    width = channels // groups_n
    source = images.astype(jnp.float32)
    resid, attn_in, saved = residual_forward(
        source, mod_pair.astype(jnp.float32), weights, keep_same
    )
    attn_flat = attn_in.reshape(total, channels)
    qkv_flat = qkv_full.reshape(channels, 3 * channels)
    qkv = jnp.dot(attn_flat, qkv_flat, preferred_element_type=jnp.float32).astype(jnp.bfloat16)
    packed = qkv.reshape(1, count, pixels, 3, groups_n, width)
    block = lax.all_to_all(packed, "head", split_axis=4, concat_axis=0, tiled=True)
    groups = block.shape[0]
    items = block.shape[1]
    flat = block.reshape(groups * items, pixels, 3, heads_local, DH)
    mixed, logsum = attend_forward(flat)
    mixed = mixed.reshape(groups, items, pixels, 1, width)
    returned = lax.all_to_all(mixed, "head", split_axis=0, concat_axis=3, tiled=True)
    returned, logsum, kept = (returned, logsum.reshape(groups, items, heads_local, pixels), block)
    mixed_image = returned.reshape(total, channels)
    result = (
        resid.reshape(total, channels)
        + jnp.dot(mixed_image, proj_full, preferred_element_type=jnp.float32)
        + bias_three
    )
    block_out = (result.reshape(images.shape) * live[:, None, None, None]).astype(jnp.bfloat16)
    grad_out = cotangent.astype(jnp.float32) * live[:, None, None, None]
    grad_flat = grad_out.reshape(total, channels)
    grad_low = grad_flat.astype(jnp.bfloat16)
    projw_full = contract_rows(mixed_image, grad_low)
    projb_full = jnp.sum(grad_flat, axis=0)
    grad_mixed = contract_cols(grad_low, proj_full).astype(jnp.bfloat16)
    arrived = lax.all_to_all(
        grad_mixed.reshape(1, count, pixels, groups_n, width),
        "head",
        split_axis=3,
        concat_axis=0,
        tiled=True,
    )
    flat_block = kept.reshape(groups_n * count, pixels, 3, heads_local, DH)
    grad_head = arrived.reshape(groups_n * count, pixels, heads_local, DH)
    stacked = attend_backward(
        flat_block, logsum.reshape(groups_n * count, heads_local, pixels), grad_head
    )
    stacked = stacked.reshape(groups_n, count, pixels, 3, 1, width)
    grad_qkv = lax.all_to_all(stacked, "head", split_axis=0, concat_axis=4, tiled=True).reshape(
        total, 3 * channels
    )
    qkvw_full = contract_rows(attn_flat, grad_qkv).reshape(channels, 3, channels)
    grad_attn = contract_cols(grad_qkv, qkv_flat).reshape(images.shape)
    image_grad, grad_mod_part, conv_terms, vectors = residual_backward(
        grad_attn, grad_out, saved, weights, keep_same
    )
    (
        gaina_full,
        shifta_full,
        biasa_full,
        gainb_full,
        shiftb_full,
        biasb_full,
        gainc_full,
        shiftc_full,
    ) = vectors
    (
        conva_term,
        convb_term,
        qkvw_term,
        projw_term,
        gaina_term,
        shifta_term,
        biasa_term,
        gainb_term,
        shiftb_term,
        biasb_term,
        gainc_term,
        shiftc_term,
        projb_term,
    ) = (
        lax.psum_scatter(
            conv_terms[0].astype(jnp.bfloat16), "head", scatter_dimension=2, tiled=True
        ).astype(jnp.float32),
        lax.psum_scatter(
            conv_terms[1].astype(jnp.bfloat16), "head", scatter_dimension=2, tiled=True
        ).astype(jnp.float32),
        lax.psum_scatter(
            qkvw_full.astype(jnp.bfloat16), "head", scatter_dimension=2, tiled=True
        ).astype(jnp.float32),
        lax.psum_scatter(
            projw_full.astype(jnp.bfloat16), "head", scatter_dimension=1, tiled=True
        ).astype(jnp.float32),
        lax.psum_scatter(
            gaina_full.astype(jnp.bfloat16), "head", scatter_dimension=0, tiled=True
        ).astype(jnp.float32),
        lax.psum_scatter(
            shifta_full.astype(jnp.bfloat16), "head", scatter_dimension=0, tiled=True
        ).astype(jnp.float32),
        lax.psum_scatter(
            biasa_full.astype(jnp.bfloat16), "head", scatter_dimension=0, tiled=True
        ).astype(jnp.float32),
        lax.psum_scatter(
            gainb_full.astype(jnp.bfloat16), "head", scatter_dimension=0, tiled=True
        ).astype(jnp.float32),
        lax.psum_scatter(
            shiftb_full.astype(jnp.bfloat16), "head", scatter_dimension=0, tiled=True
        ).astype(jnp.float32),
        lax.psum_scatter(
            biasb_full.astype(jnp.bfloat16), "head", scatter_dimension=0, tiled=True
        ).astype(jnp.float32),
        lax.psum_scatter(
            gainc_full.astype(jnp.bfloat16), "head", scatter_dimension=0, tiled=True
        ).astype(jnp.float32),
        lax.psum_scatter(
            shiftc_full.astype(jnp.bfloat16), "head", scatter_dimension=0, tiled=True
        ).astype(jnp.float32),
        lax.psum_scatter(
            projb_full.astype(jnp.bfloat16), "head", scatter_dimension=0, tiled=True
        ).astype(jnp.float32),
    )
    grad_mod = grad_mod_part.reshape(count, 2, channels)
    modw_term = jnp.einsum("ne,ntc->etc", embed.astype(jnp.float32), grad_mod, precision=HIGHEST)
    modb_term = jnp.sum(grad_mod, axis=0)
    grad_embed = jnp.einsum(
        "ntc,etc->ne", grad_mod, mod_full.astype(jnp.float32), precision=HIGHEST
    ) * silu_slope(embed_pre)
    class_term = lax.dot_general(
        class_hot.astype(jnp.float32), grad_embed, (((0,), (0,)), ((), ())), precision=HIGHEST
    )
    modw_grad, class_grad, modb_grad = (
        lax.psum_scatter(modw_term, ("dp", "head"), scatter_dimension=0, tiled=True),
        lax.psum_scatter(class_term, ("dp", "head"), scatter_dimension=1, tiled=True),
        lax.psum_scatter(modb_term, ("dp", "head"), scatter_dimension=1, tiled=True),
    )
    conva_grad, convb_grad, qkvw_grad, projw_grad = (
        lax.psum_scatter(conva_term, "dp", scatter_dimension=0, tiled=True),
        lax.psum_scatter(convb_term, "dp", scatter_dimension=0, tiled=True),
        lax.psum_scatter(qkvw_term, "dp", scatter_dimension=0, tiled=True),
        lax.psum_scatter(projw_term, "dp", scatter_dimension=0, tiled=True),
    )
    (
        gaina_grad,
        shifta_grad,
        biasa_grad,
        gainb_grad,
        shiftb_grad,
        biasb_grad,
        gainc_grad,
        shiftc_grad,
        projb_grad,
    ) = lax.psum(
        (
            gaina_term,
            shifta_term,
            biasa_term,
            gainb_term,
            shiftb_term,
            biasb_term,
            gainc_term,
            shiftc_term,
            projb_term,
        ),
        "dp",
    )
    return (
        block_out,
        image_grad,
        class_grad,
        gaina_grad,
        shifta_grad,
        conva_grad,
        biasa_grad,
        modw_grad,
        modb_grad,
        gainb_grad,
        shiftb_grad,
        convb_grad,
        biasb_grad,
        gainc_grad,
        shiftc_grad,
        qkvw_grad,
        projw_grad,
        projb_grad,
    )


MESH = pl.DeviceIdType.MESH
UNITS = 22
PAIRS = UNITS // 2
FAR = 9
VECTORS = 9
RES = 8
SLOTS = 8
PIX = RES * RES
LINE = SLOTS * RES
ALL = RES * LINE
WIDTH = 768
BAND = 256
F32 = jnp.float32
BF16 = jnp.bfloat16
ANY = pl.BlockSpec(memory_space=pl.ANY)
VMEM = pl.BlockSpec(memory_space=pltpu.VMEM)
SMEM = pl.BlockSpec(memory_space=pltpu.SMEM)
DMA = pltpu.SemaphoreType.DMA


def place():
    d, h = lax.axis_index("dp"), lax.axis_index("head")
    return d // 2, lax.rem(d, 2), h // 2, lax.rem(h, 2)


def at_chip(z, y, x, c):
    return (z * 2 + y, x * 2 + c)


def column_peers(n_dp):
    d, h = lax.axis_index("dp"), lax.axis_index("head")
    return [(lax.rem(d + k, n_dp), h) for k in range(1, n_dp)]


def head_peers(n_head):
    d, h = lax.axis_index("dp"), lax.axis_index("head")
    return [(d, lax.rem(h + k, n_head)) for k in range(1, n_head)]


def greet(devices):
    barrier = pltpu.get_barrier_semaphore()
    for device in devices:
        pl.semaphore_signal(barrier, inc=1, device_id=device, device_id_type=MESH)
    pl.semaphore_wait(barrier, len(devices))


def remote(src, dst, send, recv, device):
    return pltpu.make_async_remote_copy(
        src_ref=src, dst_ref=dst, send_sem=send, recv_sem=recv, device_id=device, device_id_type=MESH
    )


def each(count, body):
    def step(n, carry):
        body(n)
        return carry

    lax.fori_loop(0, count, step, 0)


def span(index, size):
    return pl.ds(pl.multiple_of(index * size, size), size)


def row(n):
    return pl.ds(n, 1)


def lines_from(i):
    return pl.ds(i * LINE if isinstance(i, int) else pl.multiple_of(i * LINE, LINE), ALL)


def dot(left, right):
    return jnp.dot(left, right, preferred_element_type=F32)


def dot_nt(left, right):
    return lax.dot_general(left, right, (((1,), (1,)), ((), ())), preferred_element_type=F32)


def dot_tn(left, right):
    return lax.dot_general(left, right, (((0,), (0,)), ((), ())), preferred_element_type=F32)


def in_group(first, second, axis):
    chan = lax.broadcasted_iota(jnp.int32, (first, second), axis)
    group = lax.broadcasted_iota(jnp.int32, (first, second), 1 - axis) * (C // GROUPS)
    inside = jnp.logical_and(chan >= group, chan < group + C // GROUPS)
    return jnp.where(inside, 1.0, 0.0).astype(BF16)


def pieces(values):
    high = values.astype(BF16).astype(F32)
    rest = values - high
    mid = rest.astype(BF16).astype(F32)
    return jnp.concatenate([high, mid, rest - mid], axis=0).astype(BF16)


def group_mean(sums):
    count = sums.shape[0]
    part = dot(pieces(sums), in_group(C, 128, 0))
    part = (part[:count] + part[count : 2 * count] + part[2 * count :]) * (1.0 / (PIX * (C // GROUPS)))
    back = dot(pieces(part), in_group(128, C, 1))
    return back[:count] + back[count : 2 * count] + back[2 * count :]


def sum_rows(values):
    return jnp.sum(values, axis=0, keepdims=True)


def norm_stats(get, mean_ref, inverse_ref, sums_ref):
    def first(n):
        sums_ref[row(n)] = sum_rows(get(n))

    each(SLOTS, first)
    mean_ref[...] = group_mean(sums_ref[...])

    def second(n):
        centred = get(n) - mean_ref[row(n)]
        sums_ref[row(n)] = sum_rows(centred * centred)

    each(SLOTS, second)
    inverse_ref[...] = lax.rsqrt(group_mean(sums_ref[...]) + EPSILON)


def silu(values):
    return values * jax.nn.sigmoid(values)


def shifted(values):
    spot = lax.rem(lax.broadcasted_iota(jnp.int32, values.shape, 0), RES)
    left = jnp.where(spot == 0, 0.0, pltpu.roll(values, 1, 0))
    right = jnp.where(spot == RES - 1, 0.0, pltpu.roll(values, values.shape[0] - 1, 0))
    return left, right


def chunk(n):
    return slice(n * WIDTH, (n + 1) * WIDTH)


CHUNKS = C // WIDTH


def weight_cols(ref, n):
    return ref[:, :, :, chunk(n)].reshape(C, WIDTH)


def weight_rows(ref, n):
    return ref[...].reshape(C, C)[chunk(n)]


def forward_kernel(
    lines,
    weights_a,
    weights_b,
    weights_qkv,
    weights_proj,
    images_hbm,
    cot_hbm,
    counts_ref,
    labels_ref,
    levels_ref,
    class_table,
    noise_table,
    modw_table,
    modb_ref,
    *refs,
):
    vectors, refs = refs[:VECTORS], refs[VECTORS:]
    forward_steps(
        lines,
        vectors,
        weights_a,
        weights_b,
        weights_qkv,
        weights_proj,
        images_hbm,
        cot_hbm,
        counts_ref,
        labels_ref,
        levels_ref,
        class_table,
        noise_table,
        modw_table,
        modb_ref,
        *refs,
    )


def forward_steps(
    lines,
    vectors,
    weights_a,
    weights_b,
    weights_qkv,
    weights_proj,
    images_hbm,
    cot_hbm,
    counts_ref,
    labels_ref,
    levels_ref,
    class_table,
    noise_table,
    modw_table,
    modb_ref,
    whole_out,
    conv_out,
    slopes_out,
    turned_out,
    block_out,
    grad_out,
    low_out,
    right_out,
    vecs_ref,
    mod_ref,
    stats_ref,
    pre_ref,
    all_ids,
    sums_out,
    halves,
    whole_ref,
    vec_ref,
    ids_ref,
    class_ref,
    modw_ref,
    vec_all,
    mod_part,
    mod_got,
    act,
    act_f32,
    sums_ref,
    conv_ref,
    resid_ref,
    slopes,
    turned,
    attn_in,
    qkv,
    right,
    low,
    pair_ref,
    pair_send,
    pair_recv,
    pair_local,
    z_send,
    z_recv,
    p_send,
    x_send,
    x_recv,
    y_send,
    y_recv,
    s_send,
    s_recv,
    vec_send,
    vec_recv,
    ids_send,
    ids_recv,
    mod_send,
    mod_recv,
    unit_sem,
    flush_sem,
    in_sem,
    share_local,
    share_send,
    share_recv,
):
    z, y, x, c = place()
    d, h = lax.axis_index("dp"), lax.axis_index("head")
    n_dp, n_head = lines * 2, 4
    half = lines // 2
    inner = jnp.logical_and(z > 0, z < lines - 1)
    far = at_chip(lax.rem(3 * z + 1, lines), y, x, c)
    rows, cols_own = halves.shape[2:]
    wide = 2 * cols_own
    sibling = at_chip(z, y, x, 1 - c)
    along_x = at_chip(z, y, 1 - x, c)
    along_y = at_chip(z, 1 - y, x, c)
    line = [at_chip(lax.rem(z + k, lines), y, x, c) for k in range(1, lines)]
    column, heads = column_peers(n_dp), head_peers(n_head)
    greet(column + heads)

    def spot(i, cc, zz, yy, xx):
        return whole_ref.at[i, cc, zz, yy, :, span(xx, wide)]

    def parts_of(core):
        return (
            (weights_a.at[pl.ds(4 * core, 4)], pl.ds(0, 4)),
            (weights_b.at[pl.ds(4 * core, 4)], pl.ds(5, 4)),
            (weights_qkv.at[pl.ds(core, 1)], pl.ds(9, 1)),
        )

    last_parts = (
        ((weights_a.at[8], 4), (weights_qkv.at[2], 10)),
        ((weights_b.at[8], 4), (weights_proj, 10)),
    )

    def keep_copy(k):
        source, where = parts_of(c)[k]
        return pltpu.make_async_copy(source, halves.at[c, where], pair_local.at[k])

    def swap_copy(k):
        source, where = parts_of(1 - c)[k]
        return remote(source, halves.at[c, where], pair_send.at[k], pair_recv.at[k], sibling)

    def last_keep(core, k):
        source, where = last_parts[core][k]
        return pltpu.make_async_copy(source, halves.at[c, where], pair_local.at[3 + k])

    def last_swap(core, k):
        source, where = last_parts[core][k]
        return remote(source, halves.at[c, where], pair_send.at[3 + k], pair_recv.at[3 + k], sibling)

    def swap_start():
        for k in range(3):
            swap_copy(k).start()
            keep_copy(k).start()
        for core in range(2):

            @pl.when(c == core)
            def _():
                for k in range(2):
                    last_swap(1 - core, k).start()
                    last_keep(core, k).start()

    def swap_wait(k):
        if k < 3:
            keep_copy(k).wait()
            swap_copy(k).wait()
        else:
            last_keep(0, k - 3).wait()
            last_swap(0, k - 3).wait()

    def images_copy():
        return pltpu.make_async_copy(images_hbm, images_ref, in_sem.at[0])

    def cot_copy():
        return pltpu.make_async_copy(cot_hbm, cot_ref, in_sem.at[1])

    images_ref, cot_ref = attn_in, low

    def vec_copy(k):
        return remote(vec_ref, vec_all.at[h], vec_send.at[k], vec_recv.at[k], heads[k])

    def ids_copy(k):
        return remote(ids_ref, all_ids.at[d], ids_send.at[k], ids_recv.at[k], column[k])

    def mod_copy(k):
        return remote(
            mod_part.at[lax.rem(d + k + 1, n_dp)], mod_got.at[d], mod_send.at[k], mod_recv.at[k], column[k]
        )

    def z_part(i, zz):
        if isinstance(i, int) and i >= FAR:
            return whole_ref.at[i, c, zz]
        return spot(i, c, zz, y, x)

    def z_copy(i, k):
        ref = z_part(i, z)
        return remote(ref, ref, z_send.at[i, k], z_recv.at[i, k], line[k])

    def z_pass(i):
        ref = z_part(i, lax.rem(z + 2, lines))
        return remote(ref, ref, p_send.at[i], z_recv.at[i, lax.rem(2 * z + 2, lines)], far)

    def z_start(i):
        z_copy(i, 1).start()

        @pl.when(z != lines - 1)
        def _():
            z_copy(i, 0).start()

        @pl.when(z != 0)
        def _():
            z_copy(i, 2).start()

    def z_relay(i):
        z_copy(i, 1).wait_recv()

        @pl.when(inner)
        def _():
            z_pass(i).start()

    def z_finish(i):
        z_copy(i, 0).wait_recv()
        z_copy(i, 2).wait_recv()

    def z_drain(i):
        z_copy(i, 1).wait_send()

        @pl.when(z != lines - 1)
        def _():
            z_copy(i, 0).wait_send()

        @pl.when(z != 0)
        def _():
            z_copy(i, 2).wait_send()

        @pl.when(inner)
        def _():
            z_pass(i).wait_send()

    def x_copy(i, part):
        if isinstance(i, int) and i >= FAR:
            ref = spot(i, c, z, y, x) if part == 0 else spot(i, c, z, 1 - y, x).at[pl.ds(rows // 2, rows // 2)]
        elif part == 0:
            ref = spot(i, c, slice(None), y, x)
        else:
            ref = spot(i, c, pl.ds(half, half), 1 - y, x)
        return remote(ref, ref, x_send.at[i, part], x_recv.at[i, part], along_x)

    def y_copy(i, part):
        if isinstance(i, int) and i >= FAR:
            ref = spot(i, c, z, y, x) if part == 0 else spot(i, c, z, y, 1 - x).at[pl.ds(0, rows // 2)]
        elif part == 0:
            ref = spot(i, c, slice(None), y, x)
        else:
            ref = spot(i, c, pl.ds(0, half), y, 1 - x)
        return remote(ref, ref, y_send.at[i, part], y_recv.at[i, part], along_y)

    def s_copy(i, part):
        if isinstance(i, int) and i >= FAR:
            ref = whole_ref.at[i, c, part]
        else:
            yy, xx = ((y, x), (y, 1 - x), (1 - y, x), (1 - y, 1 - x))[part]
            ref = spot(i, c, slice(None), yy, xx)
        return remote(ref, ref, s_send.at[i, part], s_recv.at[i, part], sibling)

    def join(i):
        whole_ref[i, c, z, y, :, span(x, wide)] = jnp.concatenate([halves[0, i], halves[1, i]], axis=-1)

    def begin(i):
        join(i)
        z_start(i)

    def far_begin(i):
        x_copy(i, 0).start()
        y_copy(i, 0).start()

    def far_pass(i):
        x_copy(i, 0).wait_recv()
        y_copy(i, 1).start()
        y_copy(i, 0).wait_recv()
        x_copy(i, 1).start()

    def far_line(i):
        x_copy(i, 1).wait_recv()
        y_copy(i, 1).wait_recv()
        z_start(i)

    def far_finish(i):
        z_finish(i)
        for part in range(lines):
            s_copy(i, part).start()

    def spread_line(i):
        z_finish(i)
        x_copy(i, 0).start()
        y_copy(i, 0).start()
        s_copy(i, 0).start()

    def pass_on(i):
        x_copy(i, 0).wait_recv()
        y_copy(i, 1).start()
        s_copy(i, 1).start()
        y_copy(i, 0).wait_recv()
        x_copy(i, 1).start()
        s_copy(i, 2).start()

    def finish(i):
        x_copy(i, 1).wait_recv()
        y_copy(i, 1).wait_recv()
        s_copy(i, 3).start()

    def arrived(i):
        for part in range(4):
            s_copy(i, part).wait_recv()

    def unit_copy(i):
        return pltpu.make_async_copy(whole_ref.at[i], whole_out.at[i], unit_sem.at[i])

    def fetch(i):
        arrived(i)
        if not isinstance(i, int) or i < FAR:
            unit_copy(i).start()

    def product(total, tap, i, k):
        for n in range(CHUNKS):
            value = dot(act[tap % 3, lines_from(tap // 3)], weight_cols(whole_ref.at[i, k], n))
            total[:, :, :, chunk(n)] += value.reshape(RES, SLOTS, RES, WIDTH)

    def use_pair(total, i, first):
        each(2, lambda k: product(total, i - first + 4 * k, i, k))

    flushed = (
        (conv_ref, conv_out),
        (slopes.at[0], slopes_out.at[0]),
        (slopes.at[1], slopes_out.at[1]),
        (low, block_out),
        (resid_ref, grad_out),
        (attn_in, low_out),
    )

    def share_parts(k):
        if k < 4:
            return turned.at[k], turned_out.at[k, :, span(c, ALL)]
        if k == 4:
            return right.at[3], right_out.at[3, span(c, ALL)]
        return right.at[pl.ds(0, 3)], right_out.at[pl.ds(0, 3), span(c, ALL)]

    def share_keep(k):
        return pltpu.make_async_copy(*share_parts(k), share_local.at[k])

    def share_give(k):
        return remote(*share_parts(k), share_send.at[k], share_recv.at[k], sibling)

    def share(k):
        share_keep(k).start()
        share_give(k).start()

    def flush(k):
        return pltpu.make_async_copy(*flushed[k], flush_sem.at[k])

    def set_act(place_t):
        def by_line(yy):
            value = act_f32[yy].reshape(LINE, C)
            left, right = shifted(value)
            spot_rows = pl.ds(pl.multiple_of((yy + 1) * LINE, LINE), LINE)
            act[0, spot_rows] = left.astype(BF16)
            act[1, spot_rows] = value.astype(BF16)
            act[2, spot_rows] = right.astype(BF16)

        each(RES, by_line)

        def turn(yy):
            value = act_f32[pl.ds(2 * yy, 2)].reshape(2 * LINE, C)
            turned[place_t, :, span(yy, 2 * LINE)] = value.T.astype(BF16)

        each(RES // 2, turn)

    def activate(which, n, value):
        sigma = jax.nn.sigmoid(value)
        act_f32[:, n] = (value * sigma).reshape(RES, RES, C)
        slopes[which, :, n] = (sigma * (1.0 + value * (1.0 - sigma))).reshape(RES, RES, C)

    def norm_a():
        for k in range(n_head - 1):
            vec_copy(k).wait()
        vecs_ref[...] = jnp.concatenate([vec_all[k].astype(F32) for k in range(n_head)], axis=-1)

        images_copy().wait()

        def get(n):
            return images_ref[span(n, PIX)].astype(F32)

        mean, inverse = stats_ref.at[0], stats_ref.at[1]
        norm_stats(get, mean, inverse, sums_ref)

        def to_act(n):
            value = (get(n) - mean[row(n)]) * inverse[row(n)]
            activate(0, n, value * vecs_ref[0:1] + vecs_ref[1:2])
            conv_ref[:, n] = jnp.broadcast_to(vecs_ref[2:3].reshape(1, 1, C), (RES, RES, C))
            resid_ref[:, n] = (get(n) + vecs_ref[5:6]).reshape(RES, RES, C)

        each(SLOTS, to_act)
        set_act(3)
        flush(1).start()
        share(3)

    def embed():
        for k in range(n_dp - 1):
            ids_copy(k).wait()
        ids = all_ids[...].reshape(n_dp * SLOTS, 128)
        table = class_ref.shape[1]
        label_hot = lax.broadcasted_iota(jnp.int32, (n_dp * SLOTS, table), 1) == ids[:, 0:1]
        levels = noise_table.shape[0]
        level_hot = lax.broadcasted_iota(jnp.int32, (n_dp * SLOTS, levels), 1) == ids[:, 1:2]
        pre = dot_nt(jnp.where(label_hot, 1.0, 0.0).astype(BF16), class_ref[...])
        width = class_table.shape[0]
        place_of = lax.broadcasted_iota(jnp.int32, (C, 128), 0) - d * width
        lane = lax.broadcasted_iota(jnp.int32, (C, 128), 1)
        chosen = jnp.logical_and(place_of == lane, lane < width)
        noise = dot(noise_table[...], jnp.where(chosen, 1.0, 0.0).astype(BF16)).astype(BF16)
        pre += dot(jnp.where(level_hot, 1.0, 0.0).astype(BF16), noise)
        pre_ref[...] = pre
        part = dot(silu(pre).astype(BF16), modw_ref[...])
        for k in range(n_dp):
            mine = part[k * SLOTS : (k + 1) * SLOTS]
            mod_part[k] = jnp.concatenate([mine[:, :C], mine[:, C:]], axis=0).astype(BF16)
        mod_got[d] = mod_part[d]
        for k in range(n_dp - 1):
            mod_copy(k).start()

    def norm_b():
        for k in range(n_dp - 1):
            mod_copy(k).wait()
        bias = modb_ref[...].astype(F32)
        total = jnp.concatenate([jnp.broadcast_to(bias[k : k + 1], (SLOTS, C)) for k in range(2)], axis=0)
        for k in range(n_dp):
            total += mod_got[k].astype(F32)
        mod_ref[...] = total.astype(BF16).astype(F32)

        def get(n):
            return conv_ref[:, n].reshape(PIX, C)

        mean, inverse = stats_ref.at[2], stats_ref.at[3]
        norm_stats(get, mean, inverse, sums_ref)

        def to_act(n):
            value = (get(n) - mean[row(n)]) * inverse[row(n)]
            value = value * vecs_ref[3:4] + vecs_ref[4:5]
            value = mod_ref[row(SLOTS + n)] + value * (mod_ref[row(n)] + 1.0)
            activate(1, n, value)

        each(SLOTS, to_act)
        set_act(2)
        flush(0).start()
        flush(2).start()
        share(2)

    def residual(n):
        return resid_ref[:, n].reshape(PIX, C)

    def normed(n):
        return (residual(n) - stats_ref[4, row(n)]) * stats_ref[5, row(n)]

    def transpose_out(source, place_t):
        def turn(k):
            value = source[span(k, 2 * LINE)].astype(F32)
            turned[place_t, :, span(k, 2 * LINE)] = value.T.astype(BF16)

        each(ALL // (2 * LINE), turn)

    def live(n):
        slots = counts_ref[d * n_head + h, 0] + counts_ref[d * n_head + h, 1]
        return jnp.where(n < slots, 1.0, 0.0)

    def norm_c():
        cot_copy().wait()
        norm_stats(residual, stats_ref.at[4], stats_ref.at[5], sums_ref)
        sums_out[...] = jnp.zeros_like(sums_out)

        def prepare(n):
            attn_in[span(n, PIX)] = (normed(n) * vecs_ref[6:7] + vecs_ref[7:8]).astype(BF16)
            grad = cot_ref[span(n, PIX)].astype(F32) * live(n)
            right[3, span(n, PIX)] = grad.astype(BF16)
            sums_out[8:9] += sum_rows(grad)

        each(SLOTS, prepare)
        transpose_out(attn_in, 0)
        share(0)
        share(4)

    def attention():
        unit = tuple(whole_ref.at[9 + t // 2, t % 2] for t in range(4))
        for t in range(4):
            for n in range(CHUNKS):
                if t < 3:
                    value = dot(attn_in[...], weight_cols(unit[t], n))
                else:
                    value = dot_nt(right[3], weight_rows(unit[3], n))
                qkv[t, :, chunk(n)] = value.astype(BF16)
        factor = DH ** (-0.5)
        band = lax.broadcasted_iota(jnp.int32, (PIX, BAND), 1) // DH
        heads_at_once = BAND // DH

        def stack(value):
            zero = jnp.zeros_like(value)
            return jnp.concatenate([jnp.where(band == k, value, zero) for k in range(heads_at_once)], axis=0)

        def pick(value):
            out = value[:PIX]
            for k in range(1, heads_at_once):
                out = jnp.where(band == k, value[k * PIX : (k + 1) * PIX], out)
            return out

        def attend(n):
            for b in range(C // BAND):
                query, key, value, grad = (qkv[t, span(n, PIX), slice(b * BAND, (b + 1) * BAND)] for t in range(4))
                query4, grad4 = stack(query), stack(grad)
                scores = dot_nt(key, query4) * factor
                weight = jnp.exp(scores - jnp.max(scores, axis=0, keepdims=True))
                probs = weight / jnp.sum(weight, axis=0, keepdims=True)
                probs_low = probs.astype(BF16)
                low[span(n, PIX), slice(b * BAND, (b + 1) * BAND)] = pick(dot_tn(probs_low, value)).astype(BF16)
                grad_probs = dot_nt(value, grad4)
                inner_sum = jnp.sum(grad_probs * probs, axis=0, keepdims=True)
                grad_scores = (probs * (grad_probs - inner_sum)).astype(BF16)
                right[0, span(n, PIX), slice(b * BAND, (b + 1) * BAND)] = (pick(dot_tn(grad_scores, key)) * factor).astype(BF16)
                right[1, span(n, PIX), slice(b * BAND, (b + 1) * BAND)] = (dot(grad_scores, query4) * factor).astype(BF16)
                right[2, span(n, PIX), slice(b * BAND, (b + 1) * BAND)] = dot(probs_low, grad4).astype(BF16)

        each(SLOTS, attend)
        share(5)
        transpose_out(low, 1)
        share(1)
        for n in range(CHUNKS):
            value = dot(low[...], weight_cols(unit[3], n))
            act_f32[:, :, :, chunk(n)] = value.reshape(SLOTS, RES, RES, WIDTH)

        def finish_out(n):
            value = residual(n) + act_f32[n].reshape(PIX, C) + vecs_ref[8:9]
            low[span(n, PIX)] = (value * live(n)).astype(BF16)

        each(SLOTS, finish_out)
        flush(3).start()
        for n in range(CHUNKS):
            value = dot_nt(right[0], weight_rows(unit[0], n))
            value += dot_nt(right[1], weight_rows(unit[1], n))
            value += dot_nt(right[2], weight_rows(unit[2], n))
            act_f32[:, :, :, chunk(n)] = value.reshape(SLOTS, RES, RES, WIDTH)

        def back(n):
            grad = act_f32[n].reshape(PIX, C)
            pair_ref[row(n)] = sum_rows(grad * normed(n))
            pair_ref[row(SLOTS + n)] = sum_rows(grad)

        each(SLOTS, back)
        sums_out[6:7] = sum_rows(pair_ref[0:SLOTS])
        sums_out[7:8] = sum_rows(pair_ref[SLOTS:])
        pair_ref[...] = group_mean(pair_ref[...] * vecs_ref[6:7])

        def back_second(n):
            inverse = stats_ref[5, row(n)]
            value = act_f32[n].reshape(PIX, C) * (vecs_ref[6:7] * inverse)
            value -= normed(n) * (pair_ref[row(n)] * inverse) + pair_ref[row(SLOTS + n)] * inverse
            value += right[3, span(n, PIX)].astype(F32)
            resid_ref[:, n] = value.reshape(RES, RES, C)
            sums_out[5:6] += sum_rows(value.astype(BF16).astype(F32))

        each(SLOTS, back_second)
        flush(4).start()

        def lower(yy):
            attn_in[span(yy, LINE)] = resid_ref[yy].reshape(LINE, C).astype(BF16)

        each(RES, lower)
        flush(5).start()

    swap_start()
    images_copy().start()
    cot_copy().start()
    one = [ref[...].astype(F32).reshape(1, cols_own) for ref in vectors]
    vec_ref[...] = jnp.concatenate(one + [jnp.zeros((16 - VECTORS, cols_own), F32)], axis=0).astype(BF16)
    lane = lax.broadcasted_iota(jnp.int32, (1, 128), 1)
    for n in range(SLOTS):
        ids_ref[n : n + 1] = jnp.where(lane == 0, labels_ref[n], levels_ref[n])
    for k in range(n_head - 1):
        vec_copy(k).start()
    for k in range(n_dp - 1):
        ids_copy(k).start()
    width = class_table.shape[0]
    class_ref[...] = jnp.zeros_like(class_ref)
    class_ref[0:width, 0 : class_table.shape[1]] = class_table[...]
    modw_ref[...] = jnp.zeros_like(modw_ref)
    modw_ref[0:width] = modw_table[...]
    vec_all[h] = vec_ref[...]
    all_ids[d] = ids_ref[...]
    edge = jnp.zeros((LINE, C), BF16)
    for j in range(3):
        act[j, 0:LINE] = edge
        act[j, ALL + LINE : ALL + 2 * LINE] = edge
    for k in range(5):
        swap_wait(k)
    for i in (10, 9):
        join(i)
    begin(0)
    for i in (10, 9):
        far_begin(i)
    begin(1)
    z_relay(0)
    begin(2)
    spread_line(0)
    for i in (10, 9):
        far_pass(i)
    begin(3)
    z_relay(1)
    norm_a()
    spread_line(1)
    pass_on(0)
    begin(4)
    z_relay(2)
    embed()
    spread_line(2)
    pass_on(1)
    finish(0)
    begin(5)
    z_relay(3)
    begin(6)
    z_relay(4)
    far_line(10)
    spread_line(3)
    pass_on(2)
    finish(1)
    fetch(0)

    def body(turn, carry):
        @pl.when(turn < 6)
        def _():
            begin(turn + 3)

        @pl.when(turn == 6)
        def _():
            far_line(9)
            z_relay(10)

        z_relay(turn + 1)
        spread_line(turn)
        pass_on(turn - 1)
        finish(turn - 2)
        fetch(turn - 3)
        use_pair(conv_ref, turn - 4, 0)
        return carry

    lax.fori_loop(4, 8, body, 0)
    spread_line(8)
    pass_on(7)
    finish(6)
    fetch(5)
    product(conv_ref, 8, 4, 0)
    norm_b()
    product(resid_ref, 8, 4, 1)
    pass_on(8)
    finish(7)
    z_relay(9)
    fetch(6)
    far_finish(10)
    use_pair(resid_ref, 5, 5)
    finish(8)
    fetch(7)
    use_pair(resid_ref, 6, 5)
    fetch(8)
    use_pair(resid_ref, 7, 5)
    far_finish(9)
    use_pair(resid_ref, 8, 5)
    norm_c()
    fetch(9)
    fetch(10)
    attention()

    def drain(i):
        z_drain(i)
        for part in range(2):
            x_copy(i, part).wait_send()
            y_copy(i, part).wait_send()
        for part in range(4):
            s_copy(i, part).wait_send()

    each(FAR, drain)
    drain(9)
    drain(10)
    for k in range(len(flushed)):
        flush(k).wait()
    each(FAR, lambda i: unit_copy(i).wait())
    for k in range(6):
        share_keep(k).wait()
        share_give(k).wait()


def run_forward(weights, images, cotangent, counts, labels, levels, class_table, noise_table, modw, modb, vectors):
    n_dp, n_head = lax.axis_size("dp"), lax.axis_size("head")
    rows, cols = weights[0].shape[1:]
    lines, across, wide = n_dp // 2, n_head // 2, 2 * cols
    board = (RES, SLOTS, RES, C)
    shape = jax.ShapeDtypeStruct
    return pl.pallas_call(
        functools.partial(forward_kernel, lines),
        out_shape=(
            shape((FAR, 2, lines, 2, rows, across * wide), BF16),
            shape(board, F32),
            shape((2,) + board, F32),
            shape((4, C, 2 * ALL), BF16),
            shape((ALL, C), BF16),
            shape(board, F32),
            shape((ALL, C), BF16),
            shape((4, 2 * ALL, C), BF16),
            shape((16, C), F32),
            shape((2 * SLOTS, C), F32),
            shape((6, SLOTS, C), F32),
            shape((n_dp * SLOTS, 128), F32),
            shape((n_dp, SLOTS, 128), jnp.int32),
            shape((16, C), F32),
        ),
        in_specs=[ANY] * 6 + [SMEM] * 3 + [VMEM] * (4 + VECTORS),
        out_specs=(ANY,) * 8 + (VMEM,) * 6,
        scratch_shapes=[
            pltpu.VMEM((2, PAIRS, rows, cols), BF16),
            pltpu.VMEM((PAIRS, 2, lines, 2, rows, across * wide), BF16),
            pltpu.VMEM((16, cols), BF16),
            pltpu.VMEM((SLOTS, 128), jnp.int32),
            pltpu.VMEM((128, 1024), BF16),
            pltpu.VMEM((128, 2 * C), BF16),
            pltpu.VMEM((n_head, 16, cols), BF16),
            pltpu.VMEM((n_dp, 2 * SLOTS, C), BF16),
            pltpu.VMEM((n_dp, 2 * SLOTS, C), BF16),
            pltpu.VMEM((3, ALL + 2 * LINE, C), BF16),
            pltpu.VMEM(board, F32),
            pltpu.VMEM((SLOTS, C), F32),
            pltpu.VMEM(board, F32),
            pltpu.VMEM(board, F32),
            pltpu.VMEM((2,) + board, F32),
            pltpu.VMEM((4, C, ALL), BF16),
            pltpu.VMEM((ALL, C), BF16),
            pltpu.VMEM((4, ALL, C), BF16),
            pltpu.VMEM((4, ALL, C), BF16),
            pltpu.VMEM((ALL, C), BF16),
            pltpu.VMEM((2 * SLOTS, C), F32),
            DMA((5,)),
            DMA((5,)),
            DMA((5,)),
            DMA((PAIRS, lines - 1)),
            DMA((PAIRS, lines - 1)),
            DMA((PAIRS,)),
            DMA((PAIRS, 2)),
            DMA((PAIRS, 2)),
            DMA((PAIRS, 2)),
            DMA((PAIRS, 2)),
            DMA((PAIRS, 4)),
            DMA((PAIRS, 4)),
            DMA((n_head - 1,)),
            DMA((n_head - 1,)),
            DMA((n_dp - 1,)),
            DMA((n_dp - 1,)),
            DMA((n_dp - 1,)),
            DMA((n_dp - 1,)),
            DMA((FAR,)),
            DMA((6,)),
            DMA((2,)),
            DMA((6,)),
            DMA((6,)),
            DMA((6,)),
        ],
        compiler_params=pltpu.CompilerParams(
            collective_id=0, has_side_effects=True, vmem_limit_bytes=62 * 2**20
        ),
        name="gather_forward",
    )(
        *weights,
        images,
        cotangent,
        counts,
        labels,
        levels,
        class_table,
        noise_table,
        modw,
        modb,
        *vectors,
    )


BACK_FAR = (10, 8)
BACK_NEAR = tuple(i for i in range(PAIRS) if i not in BACK_FAR)
AHEAD = 3


def backward_kernel(
    lines,
    whole_ref,
    turned_ref,
    right_ref,
    grad_low_ref,
    grad_resid_ref,
    conv_ref,
    slopes_ref,
    images_hbm,
    stats_ref,
    vecs_ref,
    mod_ref,
    sums_in,
    pre_ref,
    ids_ref,
    modw_table,
    out_a,
    out_b,
    out_qkv,
    out_proj,
    image_ref,
    class_ref,
    modw_out,
    modb_out,
    vec_out,
    mine,
    from_x,
    from_y,
    from_z,
    far_x,
    far_y,
    far_z,
    ends,
    modw_ref,
    lefts,
    rights,
    grads,
    stage,
    stage_mine,
    weights,
    total,
    board,
    slopes,
    image_mine,
    images_ref,
    sums_ref,
    pair_ref,
    coef_ref,
    gm_mine,
    gm_all,
    mw_mine,
    mw_got,
    ge_all,
    vs_mine,
    vs_got,
    vt_mine,
    vt_all,
    x_send,
    x_recv,
    y_send,
    y_recv,
    z_send,
    z_recv,
    p_send,
    p_recv,
    e_send,
    e_recv,
    e_local,
    op_send,
    op_recv,
    op_local,
    load_sem,
    in_sem,
    out_sem,
    gm_send,
    gm_recv,
    mw_send,
    mw_recv,
    ge_send,
    ge_recv,
    vs_send,
    vs_recv,
    vt_send,
    vt_recv,
):
    z, y, x, c = place()
    d, h = lax.axis_index("dp"), lax.axis_index("head")
    n_dp, n_head = lines * 2, 4
    half = lines // 2
    inner = jnp.logical_and(z > 0, z < lines - 1)
    rows, wide = from_z.shape[2], from_z.shape[3]
    cols = wide // 2
    sibling = at_chip(z, y, x, 1 - c)
    along_x = at_chip(z, y, 1 - x, c)
    along_y = at_chip(z, 1 - y, x, c)
    line = [at_chip(lax.rem(z + k, lines), y, x, c) for k in range(1, lines)]
    column, heads = column_peers(n_dp), head_peers(n_head)

    own_rows = pl.ds(LINE, ALL)

    def op_own(k):
        source, place_of = (
            (right_ref.at[2 + c], rights.at[0]),
            (turned_ref.at[c], lefts.at[1]),
            (right_ref.at[c], rights.at[1]),
            (turned_ref.at[0], lefts.at[0]),
            (grad_low_ref, grads.at[1, c, own_rows]),
            (turned_ref.at[2], lefts.at[2]),
            (turned_ref.at[3], lefts.at[3]),
        )[k]
        return pltpu.make_async_copy(source, place_of, op_local.at[k])

    def low_copy():
        return remote(grad_low_ref, grads.at[1, c, own_rows], op_send.at[0], op_recv.at[0], sibling)

    def stage_copy():
        return remote(stage_mine, stage, op_send.at[1], op_recv.at[1], sibling)

    def lanes(xx):
        return span(xx, wide)

    first, second = pl.ds(0, rows // 2), pl.ds(rows // 2, rows // 2)

    def is_far(i):
        return i in BACK_FAR

    def x_copy(i, part):
        if is_far(i):
            into = far_x.at[BACK_FAR.index(i)]
            if part == 0:
                src, dst = mine.at[i, z, 1 - y, second, lanes(1 - x)], into.at[pl.ds(rows, rows // 2)]
            else:
                src, dst = mine.at[i, z, y, :, lanes(1 - x)], into.at[pl.ds(0, rows)]
        elif part == 0:
            src, dst = mine.at[i, pl.ds(half, half), 1 - y, :, lanes(1 - x)], from_x.at[BACK_NEAR.index(i), pl.ds(lines, half)]
        else:
            src, dst = mine.at[i, :, y, :, lanes(1 - x)], from_x.at[BACK_NEAR.index(i), pl.ds(0, lines)]
        return remote(src, dst, x_send.at[i, part], x_recv.at[i, part], along_x)

    def y_copy(i, part):
        if is_far(i):
            into = far_y.at[BACK_FAR.index(i)]
            if part == 0:
                src, dst = mine.at[i, z, 1 - y, first, lanes(1 - x)], into.at[pl.ds(rows, rows // 2)]
            else:
                src, dst = mine.at[i, z, 1 - y, :, lanes(x)], into.at[pl.ds(0, rows)]
        elif part == 0:
            src, dst = mine.at[i, pl.ds(0, half), 1 - y, :, lanes(1 - x)], from_y.at[BACK_NEAR.index(i), pl.ds(lines, half)]
        else:
            src, dst = mine.at[i, :, 1 - y, :, lanes(x)], from_y.at[BACK_NEAR.index(i), pl.ds(0, lines)]
        return remote(src, dst, y_send.at[i, part], y_recv.at[i, part], along_y)

    beyond = lax.rem(z + 2, lines)
    opposite = lines - 1 - z
    near_end = at_chip(1 + z // (lines - 1), y, x, c)

    def z_block(i, zz):
        return mine.at[i, zz] if is_far(i) else mine.at[i, zz, y, :, lanes(x)]

    def z_slot(i, k):
        return far_z.at[BACK_FAR.index(i), k] if is_far(i) else from_z.at[BACK_NEAR.index(i), k]

    def z_copy(i, k):
        return remote(
            z_block(i, lax.rem(z + k + 1, lines)), z_slot(i, k), z_send.at[i, k], z_recv.at[i, k], line[k]
        )

    def z_give(i):
        return remote(z_block(i, opposite), z_slot(i, 3), p_send.at[i], p_recv.at[i], near_end)

    def z_start(i):
        @pl.when(jnp.logical_not(inner))
        def _():
            z_give(i).start()

        @pl.when(z < lines - 1)
        def _():
            z_copy(i, 0).start()

        @pl.when(z > 0)
        def _():
            z_copy(i, 2).start()

        @pl.when(jnp.logical_not(inner))
        def _():
            z_copy(i, 1).start()

    def z_mix(i):
        @pl.when(inner)
        def _():
            z_give(i).wait_recv()
            if is_far(i):
                mine[i, beyond] += far_z[BACK_FAR.index(i), 3]
            else:
                mine[i, beyond, y, :, lanes(x)] += from_z[BACK_NEAR.index(i), 3]
            z_copy(i, 1).start()

    def z_wait(i):
        z_copy(i, 1).wait_recv()

        @pl.when(z > 0)
        def _():
            z_copy(i, 0).wait_recv()

        @pl.when(z < lines - 1)
        def _():
            z_copy(i, 2).wait_recv()

    def z_drain(i):
        z_copy(i, 1).wait_send()

        @pl.when(z < lines - 1)
        def _():
            z_copy(i, 0).wait_send()

        @pl.when(z > 0)
        def _():
            z_copy(i, 2).wait_send()

        @pl.when(jnp.logical_not(inner))
        def _():
            z_give(i).wait_send()

    def target(i, core):
        if isinstance(i, int) and i == 10:
            return out_proj if core == 1 else out_qkv.at[2]
        if isinstance(i, int) and i == 9:
            return out_qkv.at[core]
        if isinstance(i, int) and i == 4:
            return out_b.at[8] if core == 1 else out_a.at[8]
        if isinstance(i, int) and i > 4:
            return out_b.at[4 * core + i - 5]
        return out_a.at[4 * core + i]

    def e_copy(i, core):
        return remote(ends.at[1 - c, i], target(i, core), e_send.at[i], e_recv.at[i], sibling)

    def e_own(i, core):
        return pltpu.make_async_copy(ends.at[c, i], target(i, core), e_local.at[i])

    def finish(i, value):
        for cc in range(2):
            ends[cc, i] = value[:, cc * cols : (cc + 1) * cols]
        if i in (4, 10):
            for core in range(2):

                @pl.when(c == core)
                def _():
                    e_copy(i, core).start()
                    e_own(i, core).start()
        else:
            e_copy(i, c).start()
            e_own(i, c).start()

    def offer(i):
        x_copy(i, 0).start()
        y_copy(i, 0).start()

    def relay(i):
        x_copy(i, 0).wait_recv()
        y_copy(i, 0).wait_recv()
        if is_far(i):
            rest = pl.ds(rows, rows // 2)
            mine[i, z, y, first, lanes(1 - x)] += far_y[BACK_FAR.index(i), rest]
            mine[i, z, 1 - y, second, lanes(x)] += far_x[BACK_FAR.index(i), rest]
        else:
            for j in range(half):
                mine[i, j, y, :, lanes(1 - x)] += from_y[BACK_NEAR.index(i), lines + j]
                mine[i, half + j, 1 - y, :, lanes(x)] += from_x[BACK_NEAR.index(i), lines + j]
        x_copy(i, 1).start()
        y_copy(i, 1).start()

    def collect(i):
        x_copy(i, 1).wait_recv()
        y_copy(i, 1).wait_recv()
        if is_far(i):
            whole_rows = pl.ds(0, rows)
            value = mine[i, z, y, :, lanes(x)].astype(F32)
            value += far_x[BACK_FAR.index(i), whole_rows].astype(F32) + far_y[BACK_FAR.index(i), whole_rows].astype(F32)
            finish(i, value)
            return

        def add(j):
            value = mine[i, j, y, :, lanes(x)].astype(F32)
            value += from_x[BACK_NEAR.index(i), j].astype(F32) + from_y[BACK_NEAR.index(i), j].astype(F32)
            mine[i, j, y, :, lanes(x)] = value.astype(BF16)

        each(lines, add)
        z_start(i)

    def last(i):
        z_wait(i)
        if is_far(i):
            for yy in range(2):
                value = mine[i, z, yy].astype(F32)
                for k in range(lines - 1):
                    value += far_z[BACK_FAR.index(i), k, yy].astype(F32)
                mine[i, z, yy] = value.astype(BF16)
            offer(i)
            return
        value = mine[i, z, y, :, lanes(x)].astype(F32)
        for k in range(lines - 1):
            value += from_z[BACK_NEAR.index(i), k].astype(F32)
        finish(i, value)

    def put(i, n, value):
        mine[i, :, :, :, chunk(n)] = value.astype(BF16).reshape(mine.shape[1:4] + (WIDTH,))

    def plain_unit(i, left, right):
        for n in range(CHUNKS):
            put(i, n, dot(lefts[left], rights[right, :, chunk(n)]))

    def conv_unit(i, left, tap):
        where, side = lines_from(2 - tap // 3), 2 - tap % 3
        for n in range(CHUNKS):
            both = jnp.concatenate([grads[side, core, where, chunk(n)] for core in range(2)], axis=0)
            put(i, n, dot(lefts[left], both))

    def extra_b():
        @pl.when(c == 1)
        def _():
            conv_unit(4, 2, 8)

    def extra_a():
        @pl.when(c == 0)
        def _():
            conv_unit(4, 3, 8)

    def spread_sides(core):
        def by_line(yy):
            value = grads[1, core, pl.ds(pl.multiple_of((yy + 1) * LINE, LINE), LINE)].astype(F32)
            left, right = shifted(value)
            spot_rows = pl.ds(pl.multiple_of((yy + 1) * LINE, LINE), LINE)
            grads[0, core, spot_rows] = left.astype(BF16)
            grads[2, core, spot_rows] = right.astype(BF16)

        each(RES, by_line)

    def load(tap, base):
        ninth = tap // 8
        i = (base // 2 + tap % 4) * (1 - ninth) + 4 * ninth
        k = (tap // 4) % 2 + (base // 10) * ninth
        return pltpu.make_async_copy(whole_ref.at[i, k], weights.at[tap % (AHEAD + 1)], load_sem.at[tap % (AHEAD + 1)])

    def conv_back(tap, base):
        load(tap, base).wait()

        @pl.when(tap < 9 - AHEAD)
        def _():
            load(tap + AHEAD, base).start()

        part = grads[2 - tap % 3, c, lines_from(2 - tap // 3)]
        for n in range(CHUNKS):
            value = dot_nt(part, weight_rows(weights.at[tap % (AHEAD + 1)], n))
            total[:, :, :, chunk(n)] += value.reshape(RES, SLOTS, RES, WIDTH)

    def conv_back_range(first, stop, base):
        def body(tap, carry):
            conv_back(tap, base)
            return carry

        lax.fori_loop(first, stop, body, 0)

    def slope(values):
        sigma = jax.nn.sigmoid(values)
        return sigma * (1.0 + values * (1.0 - sigma))

    for k in (0, 2):
        from_z[:, k] = jnp.zeros_like(from_z[:, k])
        far_z[:, k] = jnp.zeros_like(far_z[:, k])
    greet(column + heads)
    low_copy().start()
    for k in (4, 0, 1, 2, 3, 5):
        op_own(k).start()
    for tap in range(AHEAD):
        load(tap, 10).start()

    def fetch(k):
        source, target = (
            (conv_ref, board),
            (slopes_ref.at[1], slopes),
            (slopes_ref.at[0], slopes),
            (grad_resid_ref, board),
            (images_hbm, images_ref),
        )[k]
        return pltpu.make_async_copy(source, target, in_sem.at[k])

    fetch(0).start()
    fetch(1).start()
    vs_mine[...] = jnp.zeros_like(vs_mine)
    edge = jnp.zeros((LINE, C), BF16)
    for j in range(3):
        for core in range(2):
            grads[j, core, 0:LINE] = edge
            grads[j, core, ALL + LINE : ALL + 2 * LINE] = edge
    total[...] = jnp.zeros_like(total)
    sums_ref[...] = sums_in[...]
    modw_ref[...] = jnp.zeros_like(modw_ref)
    modw_ref[0:rows] = modw_table[...]

    def norm_b_value(n):
        return (board[:, n].reshape(PIX, C) - stats_ref[2, row(n)]) * stats_ref[3, row(n)]

    def norm_a_value(n):
        return (images_ref[span(n, PIX)].astype(F32) - stats_ref[0, row(n)]) * stats_ref[1, row(n)]

    def back_sums(get):
        def body(n):
            grad = (total[:, n] * slopes[:, n]).reshape(PIX, C)
            total[:, n] = grad.reshape(RES, RES, C)
            pair_ref[row(n)] = sum_rows(grad * get(n))
            pair_ref[row(SLOTS + n)] = sum_rows(grad)

        each(SLOTS, body)

    def back_factors(factor, inverse):
        coef_ref[0:SLOTS] = factor * inverse
        means = group_mean(pair_ref[...] * jnp.concatenate([factor, factor], axis=0))
        coef_ref[SLOTS : 2 * SLOTS] = means[:SLOTS] * inverse
        coef_ref[2 * SLOTS :] = means[SLOTS:] * inverse

    def back_value(n, get):
        value = total[:, n].reshape(PIX, C) * coef_ref[row(n)]
        return value - get(n) * coef_ref[row(SLOTS + n)] - coef_ref[row(2 * SLOTS + n)]

    def gm_copy(k):
        return remote(gm_mine, gm_all.at[d], gm_send.at[k], gm_recv.at[k], column[k])

    def mw_copy(k):
        return remote(
            mw_mine.at[lax.rem(h + k + 1, n_head)], mw_got.at[k], mw_send.at[k], mw_recv.at[k], heads[k]
        )

    def ge_copy(k):
        return remote(ge_all.at[h], ge_all.at[h], ge_send.at[k], ge_recv.at[k], heads[k])

    def vs_copy(k):
        return remote(
            vs_mine.at[lax.rem(h + k + 1, n_head)], vs_got.at[k], vs_send.at[k], vs_recv.at[k], heads[k]
        )

    def vt_copy(k):
        return remote(vt_mine, vt_all.at[d], vt_send.at[k], vt_recv.at[k], column[k])

    def image_copy():
        return pltpu.make_async_copy(image_mine, image_ref, out_sem)

    count = n_dp * SLOTS

    def start():
        op_own(0).wait()
        op_own(1).wait()

    def dw(i):
        if i == 10:
            plain_unit(10, 1, 0)
        elif i == 9:
            op_own(2).wait()
            op_own(3).wait()
            plain_unit(9, 0, 1)
        elif i > 4:
            conv_unit(i, 2, 4 * c + i - 5)
        else:
            conv_unit(i, 3, 4 * c + i)

    def sides():
        op_own(4).wait()
        low_copy().wait_recv()
        op_own(5).wait()
        spread_sides(0)
        spread_sides(1)

    def back_b_first():
        for tap in range(AHEAD):
            load(tap, 0).start()
        op_own(6).start()
        fetch(0).wait()
        fetch(1).wait()
        back_sums(norm_b_value)
        alone, with_norm = pair_ref[SLOTS:], pair_ref[:SLOTS]
        scale = mod_ref[0:SLOTS] + 1.0
        gm_mine[...] = jnp.concatenate([vecs_ref[3:4] * with_norm + vecs_ref[4:5] * alone, alone], axis=0).astype(BF16)
        gm_all[d] = gm_mine[...]
        for k in range(n_dp - 1):
            gm_copy(k).start()
        sums_ref[3:4] = sum_rows(with_norm * scale)
        sums_ref[4:5] = sum_rows(alone * scale)
        back_factors(scale * vecs_ref[3:4], stats_ref[3])

    def back_b_second():
        fetch(2).start()
        fetch(4).start()

        def body(n):
            value = back_value(n, norm_b_value).astype(BF16).astype(F32)
            sums_ref[2:3] += sum_rows(value)
            total[:, n] = value.reshape(RES, RES, C)

        each(SLOTS, body)
        fetch(3).start()

    def lower():
        def by_line(yy):
            stage_mine[span(yy, LINE)] = total[yy].reshape(LINE, C).astype(BF16)

        each(RES, by_line)
        stage_copy().start()
        total[...] = jnp.zeros_like(total)

    def take():
        stage_copy().wait_recv()

        def by_line(yy):
            spot_rows = pl.ds(pl.multiple_of((yy + 1) * LINE, LINE), LINE)
            grads[1, c, spot_rows] = stage_mine[span(yy, LINE)]
            grads[1, 1 - c, spot_rows] = stage[span(yy, LINE)]

        each(RES, by_line)
        spread_sides(0)
        spread_sides(1)
        op_own(6).wait()

    def modulation():
        for k in range(n_dp - 1):
            gm_copy(k).wait()
        parts = gm_all[...].astype(F32)
        gm_scale = parts[:, :SLOTS].reshape(count, C)
        gm_offset = parts[:, SLOTS:].reshape(count, C)
        pre = pre_ref[...]
        emb = silu(pre).astype(BF16)
        part_rows = rows // n_head
        for k, value in ((0, gm_scale), (1, gm_offset)):
            low_value = value.astype(BF16)
            grad_w = dot_tn(emb, low_value)
            place_lanes = slice(k * C, (k + 1) * C)
            for hh in range(n_head):
                mw_mine[hh, 0:part_rows, place_lanes] = grad_w[hh * part_rows : (hh + 1) * part_rows]
                mw_mine[hh, part_rows : part_rows + 8, place_lanes] = jnp.broadcast_to(sum_rows(value), (8, C))
        grad_e = dot_nt(gm_scale.astype(BF16), modw_ref[:, :C]) + dot_nt(gm_offset.astype(BF16), modw_ref[:, C:])
        grad_e = grad_e * slope(pre)
        label = ids_ref[...].reshape(count, 128)[:, 0:1].astype(F32)
        lane = lax.broadcasted_iota(jnp.int32, grad_e.shape, 1)
        ge_all[h] = jnp.where(lane < rows, grad_e, label)
        for k in range(n_head - 1):
            mw_copy(k).start()
            ge_copy(k).start()

    def back_a_first():
        fetch(2).wait()
        fetch(4).wait()
        back_sums(norm_a_value)
        sums_ref[0:1] = sum_rows(pair_ref[:SLOTS])
        sums_ref[1:2] = sum_rows(pair_ref[SLOTS:])
        for hh in range(n_head):
            vs_mine[hh] = sums_ref[:, hh * cols : (hh + 1) * cols]
        for k in range(n_head - 1):
            vs_copy(k).start()
        back_factors(jnp.broadcast_to(vecs_ref[0:1], (SLOTS, C)), stats_ref[1])

    def back_a_second():
        fetch(3).wait()

        def body(n):
            image_mine[span(n, PIX)] = back_value(n, norm_a_value) + board[:, n].reshape(PIX, C)

        each(SLOTS, body)
        image_copy().start()

    def vec_first():
        value = vs_mine[h]
        for k in range(n_head - 1):
            vs_copy(k).wait()
            value += vs_got[k]
        vt_mine[...] = value
        vt_all[d] = value
        for k in range(n_dp - 1):
            vt_copy(k).start()

    def mod_out():
        value = mw_mine[h]
        for k in range(n_head - 1):
            mw_copy(k).wait()
            value += mw_got[k]
        part_rows = rows // n_head
        first_lane = (d * n_head + h) * part_rows
        for k in range(2):
            lanes_of = slice(k * C, (k + 1) * C)
            modw_out[:, k] = value[:part_rows, lanes_of]
            turned_row = pltpu.roll(value[part_rows:, lanes_of], lax.rem(C - first_lane, C), 1)
            modb_out[k : k + 1] = turned_row[0:1, :part_rows]

    def class_out():
        for k in range(n_head - 1):
            ge_copy(k).wait()
        table = class_ref.shape[1]
        part = rows // n_head
        value = ge_all[...].reshape(n_head * count, 128)
        label = value[:, rows : rows + 1].astype(jnp.int32)
        hot = lax.broadcasted_iota(jnp.int32, (n_head * count, table), 1) == label
        own = pltpu.roll(value, lax.rem(128 - h * part, 128), 1).astype(BF16)
        value = dot_tn(own, jnp.where(hot, 1.0, 0.0).astype(BF16))
        class_ref[...] = value[:part]

    def vec_second():
        for k in range(n_dp - 1):
            vt_copy(k).wait()
        value = vt_all[0]
        for k in range(1, n_dp):
            value += vt_all[k]
        vec_out[...] = value

    start()
    dw(10)
    z_start(10)
    dw(9)
    offer(9)
    sides()
    dw(5)
    offer(5)
    dw(6)
    z_mix(10)
    relay(9)
    offer(6)
    conv_back_range(0, 3, 10)
    relay(5)
    conv_back_range(3, 6, 10)
    collect(9)
    conv_back_range(6, 9, 10)
    relay(6)
    z_mix(9)
    back_b_first()
    back_b_second()
    collect(5)
    lower()
    z_mix(5)
    dw(7)
    collect(6)
    offer(7)
    dw(8)
    last(10)
    z_mix(6)
    z_start(8)
    extra_b()
    relay(7)
    relay(10)
    last(9)
    take()
    extra_a()
    offer(4)
    last(5)
    dw(0)
    z_mix(8)
    offer(0)
    dw(1)
    collect(7)
    collect(10)
    offer(1)
    dw(2)
    offer(2)
    dw(3)
    relay(4)
    offer(3)
    conv_back_range(0, 3, 0)
    relay(0)
    relay(1)
    z_mix(7)
    conv_back_range(3, 6, 0)
    relay(2)
    last(6)
    conv_back_range(6, 9, 0)
    back_a_first()
    collect(4)
    modulation()
    last(8)
    relay(3)
    z_mix(4)
    collect(0)
    last(7)
    z_mix(0)
    back_a_second()
    vec_first()
    mod_out()
    collect(1)
    class_out()
    z_mix(1)
    vec_second()
    last(4)
    collect(2)
    relay(8)
    last(0)
    z_mix(2)
    last(1)
    collect(3)
    collect(8)
    z_mix(3)
    last(2)
    last(3)

    low_copy().wait_send()
    stage_copy().wait_send()
    image_copy().wait()

    def drain(i):
        for part in range(2):
            x_copy(i, part).wait_send()
            y_copy(i, part).wait_send()
        z_drain(i)
        e_copy(i, 0).wait()
        e_own(i, 0).wait()

    for i in range(PAIRS):
        drain(i)


def run_backward(whole, turned, right, grad_low, grad_resid, conv_out, slopes, images, stats, vecs, mod, sums, pre, ids, modw, classes):
    n_dp, n_head = lax.axis_size("dp"), lax.axis_size("head")
    _, _, lines, _, rows, depth = whole.shape
    cols = depth // n_head
    wide = 2 * cols
    board = (RES, SLOTS, RES, C)
    shape = jax.ShapeDtypeStruct
    return pl.pallas_call(
        functools.partial(backward_kernel, lines),
        out_shape=(
            shape((9, rows, cols), F32),
            shape((9, rows, cols), F32),
            shape((3, rows, cols), F32),
            shape((rows, cols), F32),
            shape((ALL, C), F32),
            shape((rows // n_head, classes), F32),
            shape((rows // n_head, 2, C), F32),
            shape((2, rows // n_head), F32),
            shape((16, cols), F32),
        ),
        in_specs=[ANY] * 8 + [VMEM] * 7,
        out_specs=(ANY,) * 5 + (VMEM,) * 4,
        scratch_shapes=[
            pltpu.VMEM((PAIRS, lines, 2, rows, depth), BF16),
            pltpu.VMEM((len(BACK_NEAR), lines + lines // 2, rows, wide), BF16),
            pltpu.VMEM((len(BACK_NEAR), lines + lines // 2, rows, wide), BF16),
            pltpu.VMEM((len(BACK_NEAR), 4, rows, wide), BF16),
            pltpu.VMEM((len(BACK_FAR), rows + rows // 2, wide), BF16),
            pltpu.VMEM((len(BACK_FAR), rows + rows // 2, wide), BF16),
            pltpu.VMEM((len(BACK_FAR), 4, 2, rows, depth), BF16),
            pltpu.VMEM((2, PAIRS, rows, cols), F32),
            pltpu.VMEM((128, 2 * C), BF16),
            pltpu.VMEM((4, C, 2 * ALL), BF16),
            pltpu.VMEM((2, 2 * ALL, C), BF16),
            pltpu.VMEM((3, 2, ALL + 2 * LINE, C), BF16),
            pltpu.VMEM((ALL, C), BF16),
            pltpu.VMEM((ALL, C), BF16),
            pltpu.VMEM((AHEAD + 1, lines, 2, rows, depth), BF16),
            pltpu.VMEM(board, F32),
            pltpu.VMEM(board, F32),
            pltpu.VMEM(board, F32),
            pltpu.VMEM((ALL, C), F32),
            pltpu.VMEM((ALL, C), BF16),
            pltpu.VMEM((16, C), F32),
            pltpu.VMEM((2 * SLOTS, C), F32),
            pltpu.VMEM((3 * SLOTS, C), F32),
            pltpu.VMEM((2 * SLOTS, C), BF16),
            pltpu.VMEM((n_dp, 2 * SLOTS, C), BF16),
            pltpu.VMEM((n_head, rows // n_head + 8, 2 * C), F32),
            pltpu.VMEM((n_head - 1, rows // n_head + 8, 2 * C), F32),
            pltpu.VMEM((n_head, n_dp * SLOTS, 128), F32),
            pltpu.VMEM((n_head, 16, cols), F32),
            pltpu.VMEM((n_head - 1, 16, cols), F32),
            pltpu.VMEM((16, cols), F32),
            pltpu.VMEM((n_dp, 16, cols), F32),
            DMA((PAIRS, 2)),
            DMA((PAIRS, 2)),
            DMA((PAIRS, 2)),
            DMA((PAIRS, 2)),
            DMA((PAIRS, lines - 1)),
            DMA((PAIRS, lines - 1)),
            DMA((PAIRS,)),
            DMA((PAIRS,)),
            DMA((PAIRS,)),
            DMA((PAIRS,)),
            DMA((PAIRS,)),
            DMA((2,)),
            DMA((2,)),
            DMA((7,)),
            DMA((AHEAD + 1,)),
            DMA((5,)),
            DMA,
            DMA((n_dp - 1,)),
            DMA((n_dp - 1,)),
            DMA((n_head - 1,)),
            DMA((n_head - 1,)),
            DMA((n_head - 1,)),
            DMA((n_head - 1,)),
            DMA((n_head - 1,)),
            DMA((n_head - 1,)),
            DMA((n_dp - 1,)),
            DMA((n_dp - 1,)),
        ],
        compiler_params=pltpu.CompilerParams(
            collective_id=1, has_side_effects=True, vmem_limit_bytes=64 * 2**20 - 2**18
        ),
        name="backward_scatter",
    )(whole, turned, right, grad_low, grad_resid, conv_out, slopes, images, stats, vecs, mod, sums, pre, ids, modw)


def results_kernel(count, *refs):
    sources, vec_ref, refs = refs[:count], refs[count], refs[count + 1 :]
    targets, vectors, sems = refs[:count], refs[count:-1], refs[-1]
    copies = [
        pltpu.make_async_copy(source, target, sems.at[k])
        for k, (source, target) in enumerate(zip(sources, targets))
    ]
    for copy in copies:
        copy.start()
    for k, ref in enumerate(vectors):
        ref[...] = vec_ref[k].reshape(ref.shape)
    for copy in copies:
        copy.wait()


def run_results(arrays, vec):
    count = len(arrays)
    shape = jax.ShapeDtypeStruct
    return pl.pallas_call(
        functools.partial(results_kernel, count),
        out_shape=tuple(shape(one.shape, one.dtype) for one in arrays)
        + (shape(vec.shape[1:], F32),) * VECTORS,
        in_specs=[VMEM] * (count + 1),
        out_specs=(ANY,) * count + (VMEM,) * VECTORS,
        scratch_shapes=[DMA((count,))],
        compiler_params=pltpu.CompilerParams(vmem_limit_bytes=60 * 2**20),
        name="results",
    )(*arrays, vec)


def direct(rows, cols):
    n_dp, n_head = lax.axis_size("dp"), lax.axis_size("head")
    return n_head == 4 and n_dp == 8 and rows % 32 == 0 and cols % 64 == 0


def fast_shards(
    images,
    cotangent,
    counts,
    labels,
    levels,
    noise_table,
    class_table,
    gain_a,
    shift_a,
    conv_a,
    bias_a,
    mod_weight,
    mod_bias,
    gain_b,
    shift_b,
    conv_b,
    bias_b,
    gain_c,
    shift_c,
    qkv_weight,
    proj_weight,
    proj_bias,
):
    weights = (
        jnp.swapaxes(conv_a, 0, 1),
        jnp.swapaxes(conv_b, 0, 1),
        jnp.swapaxes(qkv_weight, 0, 1),
        proj_weight,
    )
    vectors = (gain_a, shift_a, bias_a, gain_b, shift_b, bias_b, gain_c, shift_c, proj_bias)
    modw = mod_weight.reshape(mod_weight.shape[0], 2 * C)
    flat = images.reshape(ALL, C)
    (
        whole,
        conv_out,
        slopes,
        turned,
        block_out,
        grad_resid,
        grad_low,
        right,
        vecs,
        mod,
        stats,
        pre,
        all_ids,
        sums,
    ) = run_forward(
        weights,
        flat,
        cotangent.reshape(ALL, C),
        counts,
        labels,
        levels,
        class_table.T,
        noise_table,
        modw,
        mod_bias,
        vectors,
    )
    *arrays, vec = run_backward(
        whole,
        turned,
        right,
        grad_low,
        grad_resid,
        conv_out,
        slopes,
        flat,
        stats,
        vecs,
        mod,
        sums,
        pre,
        all_ids,
        modw,
        class_table.shape[0],
    )
    block_out, conva, convb, qkvw, projw, image_grad, class_grad, modw_grad, modb_grad, *rest = run_results(
        (block_out, *arrays), vec
    )
    gaina, shifta, biasa, gainb, shiftb, biasb, gainc, shiftc, projb = rest
    return (
        block_out.reshape(images.shape),
        image_grad.reshape(images.shape),
        class_grad.T,
        gaina,
        shifta,
        jnp.swapaxes(conva, 0, 1),
        biasa,
        modw_grad,
        modb_grad,
        gainb,
        shiftb,
        jnp.swapaxes(convb, 0, 1),
        biasb,
        gainc,
        shiftc,
        jnp.swapaxes(qkvw, 0, 1),
        projw,
        projb,
    )


def shards(*args):
    rows, _, cols = args[9].shape
    if direct(rows, cols):
        return fast_shards(*args)
    return plain_shards(*args)


def solution(mesh):
    placed = (
        P(("dp", "head"), None, None, None),
        P(("dp", "head"), None, None, None),
        P(),
        P(("dp", "head")),
        P(("dp", "head")),
        P(),
        P(None, "dp"),
        P("head"),
        P("head"),
        P("dp", None, "head"),
        P("head"),
        P("dp", None, None),
        P(),
        P("head"),
        P("head"),
        P("dp", None, "head"),
        P("head"),
        P("head"),
        P("head"),
        P("dp", None, "head"),
        P("dp", "head"),
        P("head"),
    )
    return jax.shard_map(
        shards,
        mesh=mesh,
        in_specs=placed,
        out_specs=(
            P(("dp", "head"), None, None, None),
            P(("dp", "head"), None, None, None),
            P(None, ("dp", "head")),
            P("head"),
            P("head"),
            P("dp", None, "head"),
            P("head"),
            P(("dp", "head"), None, None),
            P(None, ("dp", "head")),
            P("head"),
            P("head"),
            P("dp", None, "head"),
            P("head"),
            P("head"),
            P("head"),
            P("dp", None, "head"),
            P("dp", "head"),
            P("head"),
        ),
        check_vma=False,
    )
```

```python
import functools

import jax
import jax.numpy as jnp
from jax import lax
from jax.experimental import pallas as pl
from jax.experimental.pallas import tpu as pltpu
from jax.sharding import PartitionSpec as P

C = 768
DH = 64
GROUPS = 32


EPSILON = 1e-05
HIGHEST = lax.Precision.HIGHEST


def norm_forward(values, gain, shift):
    count, chans = (values.shape[0], values.shape[-1])
    span = C // GROUPS
    grouped = values.reshape(count, -1, chans // span, span)
    mean = jnp.mean(grouped, axis=(1, 3), keepdims=True)
    centred = grouped - mean
    inverse = lax.rsqrt(jnp.mean(centred * centred, axis=(1, 3), keepdims=True) + EPSILON)
    normed = (centred * inverse).reshape(values.shape)
    return (normed * gain + shift, normed, inverse)


def norm_backward(grad_out, normed, inverse, gain):
    grad_gain = jnp.sum(grad_out * normed, axis=(0, 1, 2))
    grad_shift = jnp.sum(grad_out, axis=(0, 1, 2))
    count, chans = (grad_out.shape[0], grad_out.shape[-1])
    span = C // GROUPS
    layout = (count, -1, chans // span, span)
    grad_normed = (grad_out * gain).reshape(layout)
    normed_groups = normed.reshape(layout)
    mean_one = jnp.mean(grad_normed, axis=(1, 3), keepdims=True)
    mean_two = jnp.mean(grad_normed * normed_groups, axis=(1, 3), keepdims=True)
    grad_in = inverse * (grad_normed - mean_one - normed_groups * mean_two)
    return (grad_in.reshape(grad_out.shape), grad_gain, grad_shift)


def silu_slope(values):
    sigma = jax.nn.sigmoid(values)
    return sigma * (1.0 + values * (1.0 - sigma))


def patches_of(act):
    count, rows, cols, chans = act.shape
    padded = jnp.pad(act, ((0, 0), (1, 1), (1, 1), (0, 0)))
    taps = [padded[:, i : i + rows, j : j + cols, :] for i in range(3) for j in range(3)]
    return jnp.stack(taps, axis=3).reshape(count * rows * cols, 9, chans)


def contract_rows(left, right):
    return lax.dot_general(
        left, right, (((0,), (0,)), ((), ())), preferred_element_type=jnp.float32
    )


def contract_cols(left, right):
    return lax.dot_general(
        left, right, (((1,), (1,)), ((), ())), preferred_element_type=jnp.float32
    )


def conv_back(grad_low, weight, count, rows, cols):
    chans = weight.shape[0]
    padded = jnp.zeros((count, rows + 2, cols + 2, chans), jnp.float32)
    for tap in range(9):
        i, j = divmod(tap, 3)
        part = contract_cols(grad_low, weight[:, tap, :]).reshape(count, rows, cols, chans)
        padded = padded.at[:, i : i + rows, j : j + cols, :].add(part)
    return padded[:, 1 : rows + 1, 1 : cols + 1, :]


def keep_same(values):
    return values


def live_rows(counts, first, number, count):
    sums = jnp.sum(counts, axis=1)
    chosen = lax.dynamic_slice_in_dim(sums, first, number)
    slots = lax.iota(jnp.int32, count)
    return (slots[None, :] < chosen[:, None]).astype(jnp.float32).reshape(number * count)


def residual_forward(source, mod_pair, weights, spread):
    (
        conv_one,
        conv_two,
        gain_one,
        shift_one,
        bias_one,
        gain_two,
        shift_two,
        bias_two,
        gain_three,
        shift_three,
    ) = weights
    out_a, normed_a, inverse_a = norm_forward(source, gain_one, shift_one)
    wide_a = spread(jax.nn.silu(out_a).astype(jnp.bfloat16))
    conv_out_a = (
        jnp.einsum("ptc,cto->po", patches_of(wide_a), conv_one, preferred_element_type=jnp.float32)
        + bias_one
    ).reshape(source.shape)
    scale = mod_pair[:, :, 0:1, :]
    offset = mod_pair[:, :, 1:2, :]
    out_b, normed_b, inverse_b = norm_forward(conv_out_a, gain_two, shift_two)
    inner_b = offset + out_b * (scale + 1.0)
    wide_b = spread(jax.nn.silu(inner_b).astype(jnp.bfloat16))
    conv_out_b = (
        jnp.einsum("ptc,cto->po", patches_of(wide_b), conv_two, preferred_element_type=jnp.float32)
        + bias_two
    ).reshape(source.shape)
    resid = source + conv_out_b
    out_c, normed_c, inverse_c = norm_forward(resid, gain_three, shift_three)
    attn_in = out_c.astype(jnp.bfloat16)
    saved = (
        out_a,
        normed_a,
        inverse_a,
        wide_a,
        out_b,
        normed_b,
        inverse_b,
        inner_b,
        wide_b,
        normed_c,
        inverse_c,
        scale,
    )
    return (resid, attn_in, saved)


def residual_backward(grad_attn, grad_out, saved, weights, reduce_value):
    conv_one, conv_two, gain_one, gain_two, gain_three = (
        weights[0],
        weights[1],
        weights[2],
        weights[5],
        weights[8],
    )
    (
        out_a,
        normed_a,
        inverse_a,
        wide_a,
        out_b,
        normed_b,
        inverse_b,
        inner_b,
        wide_b,
        normed_c,
        inverse_c,
        scale,
    ) = saved
    count, rows, cols, local = grad_out.shape
    grad_resid_c, gainc_term, shiftc_term = norm_backward(
        grad_attn, normed_c, inverse_c, gain_three
    )
    grad_resid = grad_out + grad_resid_c
    grad_conv_b = grad_resid.reshape(-1, local).astype(jnp.bfloat16)
    biasb_term = jnp.sum(grad_conv_b.astype(jnp.float32), axis=0)
    convb_term = jnp.einsum(
        "ptc,po->cto", patches_of(wide_b), grad_conv_b, preferred_element_type=jnp.float32
    )
    grad_act_b = reduce_value(conv_back(grad_conv_b, conv_two, count, rows, cols))
    grad_inner = grad_act_b * silu_slope(inner_b)
    grad_offset = jnp.sum(grad_inner, axis=(1, 2))
    grad_scale = jnp.sum(grad_inner * out_b, axis=(1, 2))
    grad_mod = jnp.stack([grad_scale, grad_offset], axis=1)[:, None]
    grad_conv_full, gainb_term, shiftb_term = norm_backward(
        grad_inner * (scale + 1.0), normed_b, inverse_b, gain_two
    )
    grad_conv_a = grad_conv_full.reshape(-1, local).astype(jnp.bfloat16)
    biasa_term = jnp.sum(grad_conv_a.astype(jnp.float32), axis=0)
    conva_term = jnp.einsum(
        "ptc,po->cto", patches_of(wide_a), grad_conv_a, preferred_element_type=jnp.float32
    )
    grad_act_a = reduce_value(conv_back(grad_conv_a, conv_one, count, rows, cols))
    grad_source, gaina_term, shifta_term = norm_backward(
        grad_act_a * silu_slope(out_a), normed_a, inverse_a, gain_one
    )
    image_grad = grad_resid + grad_source
    vectors = (
        gaina_term,
        shifta_term,
        biasa_term,
        gainb_term,
        shiftb_term,
        biasb_term,
        gainc_term,
        shiftc_term,
    )
    return (image_grad, grad_mod, (conva_term, convb_term), vectors)


def attend_forward(block):
    query, key, value = (block[:, :, 0], block[:, :, 1], block[:, :, 2])
    batch, pixels, heads_here, depth = query.shape
    scores = jnp.einsum("bqhd,bkhd->bhqk", query, key, preferred_element_type=jnp.float32) * DH ** (
        -0.5
    )
    top = jnp.max(scores, axis=-1, keepdims=True)
    weights = jnp.exp(scores - top)
    sums = jnp.sum(weights, axis=-1, keepdims=True)
    probs = (weights / sums).astype(jnp.bfloat16)
    logsum = (top + jnp.log(sums))[..., 0]
    mixed = jnp.einsum("bhqk,bkhd->bqhd", probs, value, preferred_element_type=jnp.float32).astype(
        jnp.bfloat16
    )
    return (mixed.reshape(batch, pixels, heads_here * depth), logsum)


def attend_backward(block, logsum, grad_head):
    query, key, value = (block[:, :, 0], block[:, :, 1], block[:, :, 2])
    batch, pixels, heads_here, depth = query.shape
    factor = DH ** (-0.5)
    scores = jnp.einsum("bqhd,bkhd->bhqk", query, key, preferred_element_type=jnp.float32) * factor
    probs = jnp.exp(scores - logsum[..., None])
    grad_value = jnp.einsum(
        "bhqk,bqhd->bkhd", probs.astype(jnp.bfloat16), grad_head, preferred_element_type=jnp.float32
    )
    grad_probs = jnp.einsum("bqhd,bkhd->bhqk", grad_head, value, preferred_element_type=jnp.float32)
    inner = jnp.sum(grad_probs * probs, axis=-1, keepdims=True)
    grad_scores = (probs * (grad_probs - inner)).astype(jnp.bfloat16)
    grad_query = (
        jnp.einsum("bhqk,bkhd->bqhd", grad_scores, key, preferred_element_type=jnp.float32) * factor
    )
    grad_key = (
        jnp.einsum("bhqk,bqhd->bkhd", grad_scores, query, preferred_element_type=jnp.float32)
        * factor
    )
    stacked = jnp.stack([grad_query, grad_key, grad_value], axis=2).astype(jnp.bfloat16)
    return stacked.reshape(batch, pixels, 3, heads_here * depth)


def plain_shards(
    images,
    cotangent,
    counts,
    labels,
    levels,
    noise_table,
    class_table,
    gain_a,
    shift_a,
    conv_a,
    bias_a,
    mod_weight,
    mod_bias,
    gain_b,
    shift_b,
    conv_b,
    bias_b,
    gain_c,
    shift_c,
    qkv_weight,
    proj_weight,
    proj_bias,
):
    rows_a, rows_b, rows_qkv, rows_proj, mod_full, class_full = (
        lax.all_gather(conv_a, "dp", axis=0, tiled=True),
        lax.all_gather(conv_b, "dp", axis=0, tiled=True),
        lax.all_gather(qkv_weight, "dp", axis=0, tiled=True),
        lax.all_gather(proj_weight, "dp", axis=0, tiled=True),
        lax.all_gather(mod_weight, "dp", axis=0, tiled=True),
        lax.all_gather(class_table, "dp", axis=1, tiled=True),
    )
    count, rows, cols, channels = images.shape
    pixels = rows * cols
    groups_n = lax.axis_size("head")
    quarter = channels // groups_n
    heads_local = quarter // DH
    first_dp = lax.axis_index("dp") * groups_n
    class_hot = (labels[:, None] == lax.iota(jnp.int32, class_full.shape[0])[None, :]).astype(
        jnp.bfloat16
    )
    level_hot = (levels[:, None] == lax.iota(jnp.int32, noise_table.shape[0])[None, :]).astype(
        jnp.bfloat16
    )
    embed_pre = jnp.dot(class_hot, class_full, preferred_element_type=jnp.float32) + jnp.dot(
        level_hot, noise_table, preferred_element_type=jnp.float32
    )
    embed = jax.nn.silu(embed_pre).astype(jnp.bfloat16)
    modulation = (
        jnp.einsum("ne,etc->ntc", embed, mod_full, preferred_element_type=jnp.float32)
        + mod_bias.astype(jnp.float32)
    ).astype(jnp.bfloat16)
    mod_pair = modulation.reshape(count, 1, 2, channels)
    (
        conv_one,
        conv_two,
        qkv_full,
        proj_full,
        gain_one,
        shift_one,
        bias_one,
        gain_two,
        shift_two,
        bias_two,
        gain_three,
        shift_three,
        bias_three,
    ) = (
        lax.all_gather(rows_a, "head", axis=2, tiled=True),
        lax.all_gather(rows_b, "head", axis=2, tiled=True),
        lax.all_gather(rows_qkv, "head", axis=2, tiled=True),
        lax.all_gather(rows_proj, "head", axis=1, tiled=True),
        lax.all_gather(gain_a, "head", axis=0, tiled=True),
        lax.all_gather(shift_a, "head", axis=0, tiled=True),
        lax.all_gather(bias_a, "head", axis=0, tiled=True),
        lax.all_gather(gain_b, "head", axis=0, tiled=True),
        lax.all_gather(shift_b, "head", axis=0, tiled=True),
        lax.all_gather(bias_b, "head", axis=0, tiled=True),
        lax.all_gather(gain_c, "head", axis=0, tiled=True),
        lax.all_gather(shift_c, "head", axis=0, tiled=True),
        lax.all_gather(proj_bias, "head", axis=0, tiled=True),
    )
    weights = (
        conv_one,
        conv_two,
        gain_one,
        shift_one,
        bias_one,
        gain_two,
        shift_two,
        bias_two,
        gain_three,
        shift_three,
    )
    live = live_rows(counts, first_dp + lax.axis_index("head"), 1, count)
    total = count * pixels
    width = channels // groups_n
    source = images.astype(jnp.float32)
    resid, attn_in, saved = residual_forward(
        source, mod_pair.astype(jnp.float32), weights, keep_same
    )
    attn_flat = attn_in.reshape(total, channels)
    qkv_flat = qkv_full.reshape(channels, 3 * channels)
    qkv = jnp.dot(attn_flat, qkv_flat, preferred_element_type=jnp.float32).astype(jnp.bfloat16)
    packed = qkv.reshape(1, count, pixels, 3, groups_n, width)
    block = lax.all_to_all(packed, "head", split_axis=4, concat_axis=0, tiled=True)
    groups = block.shape[0]
    items = block.shape[1]
    flat = block.reshape(groups * items, pixels, 3, heads_local, DH)
    mixed, logsum = attend_forward(flat)
    mixed = mixed.reshape(groups, items, pixels, 1, width)
    returned = lax.all_to_all(mixed, "head", split_axis=0, concat_axis=3, tiled=True)
    returned, logsum, kept = (returned, logsum.reshape(groups, items, heads_local, pixels), block)
    mixed_image = returned.reshape(total, channels)
    result = (
        resid.reshape(total, channels)
        + jnp.dot(mixed_image, proj_full, preferred_element_type=jnp.float32)
        + bias_three
    )
    block_out = (result.reshape(images.shape) * live[:, None, None, None]).astype(jnp.bfloat16)
    grad_out = cotangent.astype(jnp.float32) * live[:, None, None, None]
    grad_flat = grad_out.reshape(total, channels)
    grad_low = grad_flat.astype(jnp.bfloat16)
    projw_full = contract_rows(mixed_image, grad_low)
    projb_full = jnp.sum(grad_flat, axis=0)
    grad_mixed = contract_cols(grad_low, proj_full).astype(jnp.bfloat16)
    arrived = lax.all_to_all(
        grad_mixed.reshape(1, count, pixels, groups_n, width),
        "head",
        split_axis=3,
        concat_axis=0,
        tiled=True,
    )
    flat_block = kept.reshape(groups_n * count, pixels, 3, heads_local, DH)
    grad_head = arrived.reshape(groups_n * count, pixels, heads_local, DH)
    stacked = attend_backward(
        flat_block, logsum.reshape(groups_n * count, heads_local, pixels), grad_head
    )
    stacked = stacked.reshape(groups_n, count, pixels, 3, 1, width)
    grad_qkv = lax.all_to_all(stacked, "head", split_axis=0, concat_axis=4, tiled=True).reshape(
        total, 3 * channels
    )
    qkvw_full = contract_rows(attn_flat, grad_qkv).reshape(channels, 3, channels)
    grad_attn = contract_cols(grad_qkv, qkv_flat).reshape(images.shape)
    image_grad, grad_mod_part, conv_terms, vectors = residual_backward(
        grad_attn, grad_out, saved, weights, keep_same
    )
    (
        gaina_full,
        shifta_full,
        biasa_full,
        gainb_full,
        shiftb_full,
        biasb_full,
        gainc_full,
        shiftc_full,
    ) = vectors
    (
        conva_term,
        convb_term,
        qkvw_term,
        projw_term,
        gaina_term,
        shifta_term,
        biasa_term,
        gainb_term,
        shiftb_term,
        biasb_term,
        gainc_term,
        shiftc_term,
        projb_term,
    ) = (
        lax.psum_scatter(
            conv_terms[0].astype(jnp.bfloat16), "head", scatter_dimension=2, tiled=True
        ).astype(jnp.float32),
        lax.psum_scatter(
            conv_terms[1].astype(jnp.bfloat16), "head", scatter_dimension=2, tiled=True
        ).astype(jnp.float32),
        lax.psum_scatter(
            qkvw_full.astype(jnp.bfloat16), "head", scatter_dimension=2, tiled=True
        ).astype(jnp.float32),
        lax.psum_scatter(
            projw_full.astype(jnp.bfloat16), "head", scatter_dimension=1, tiled=True
        ).astype(jnp.float32),
        lax.psum_scatter(
            gaina_full.astype(jnp.bfloat16), "head", scatter_dimension=0, tiled=True
        ).astype(jnp.float32),
        lax.psum_scatter(
            shifta_full.astype(jnp.bfloat16), "head", scatter_dimension=0, tiled=True
        ).astype(jnp.float32),
        lax.psum_scatter(
            biasa_full.astype(jnp.bfloat16), "head", scatter_dimension=0, tiled=True
        ).astype(jnp.float32),
        lax.psum_scatter(
            gainb_full.astype(jnp.bfloat16), "head", scatter_dimension=0, tiled=True
        ).astype(jnp.float32),
        lax.psum_scatter(
            shiftb_full.astype(jnp.bfloat16), "head", scatter_dimension=0, tiled=True
        ).astype(jnp.float32),
        lax.psum_scatter(
            biasb_full.astype(jnp.bfloat16), "head", scatter_dimension=0, tiled=True
        ).astype(jnp.float32),
        lax.psum_scatter(
            gainc_full.astype(jnp.bfloat16), "head", scatter_dimension=0, tiled=True
        ).astype(jnp.float32),
        lax.psum_scatter(
            shiftc_full.astype(jnp.bfloat16), "head", scatter_dimension=0, tiled=True
        ).astype(jnp.float32),
        lax.psum_scatter(
            projb_full.astype(jnp.bfloat16), "head", scatter_dimension=0, tiled=True
        ).astype(jnp.float32),
    )
    grad_mod = grad_mod_part.reshape(count, 2, channels)
    modw_term = jnp.einsum("ne,ntc->etc", embed.astype(jnp.float32), grad_mod, precision=HIGHEST)
    modb_term = jnp.sum(grad_mod, axis=0)
    grad_embed = jnp.einsum(
        "ntc,etc->ne", grad_mod, mod_full.astype(jnp.float32), precision=HIGHEST
    ) * silu_slope(embed_pre)
    class_term = lax.dot_general(
        class_hot.astype(jnp.float32), grad_embed, (((0,), (0,)), ((), ())), precision=HIGHEST
    )
    modw_grad, class_grad, modb_grad = (
        lax.psum_scatter(modw_term, ("dp", "head"), scatter_dimension=0, tiled=True),
        lax.psum_scatter(class_term, ("dp", "head"), scatter_dimension=1, tiled=True),
        lax.psum_scatter(modb_term, ("dp", "head"), scatter_dimension=1, tiled=True),
    )
    conva_grad, convb_grad, qkvw_grad, projw_grad = (
        lax.psum_scatter(conva_term, "dp", scatter_dimension=0, tiled=True),
        lax.psum_scatter(convb_term, "dp", scatter_dimension=0, tiled=True),
        lax.psum_scatter(qkvw_term, "dp", scatter_dimension=0, tiled=True),
        lax.psum_scatter(projw_term, "dp", scatter_dimension=0, tiled=True),
    )
    (
        gaina_grad,
        shifta_grad,
        biasa_grad,
        gainb_grad,
        shiftb_grad,
        biasb_grad,
        gainc_grad,
        shiftc_grad,
        projb_grad,
    ) = lax.psum(
        (
            gaina_term,
            shifta_term,
            biasa_term,
            gainb_term,
            shiftb_term,
            biasb_term,
            gainc_term,
            shiftc_term,
            projb_term,
        ),
        "dp",
    )
    return (
        block_out,
        image_grad,
        class_grad,
        gaina_grad,
        shifta_grad,
        conva_grad,
        biasa_grad,
        modw_grad,
        modb_grad,
        gainb_grad,
        shiftb_grad,
        convb_grad,
        biasb_grad,
        gainc_grad,
        shiftc_grad,
        qkvw_grad,
        projw_grad,
        projb_grad,
    )


MESH = pl.DeviceIdType.MESH
UNITS = 22
PAIRS = UNITS // 2
FAR = 9
VECTORS = 9
RES = 8
SLOTS = 8
PIX = RES * RES
LINE = SLOTS * RES
ALL = RES * LINE
WIDTH = 768
BAND = 256
F32 = jnp.float32
BF16 = jnp.bfloat16
ANY = pl.BlockSpec(memory_space=pl.ANY)
VMEM = pl.BlockSpec(memory_space=pltpu.VMEM)
SMEM = pl.BlockSpec(memory_space=pltpu.SMEM)
DMA = pltpu.SemaphoreType.DMA


def place():
    d, h = lax.axis_index("dp"), lax.axis_index("head")
    return d // 2, lax.rem(d, 2), h // 2, lax.rem(h, 2)


def at_chip(z, y, x, c):
    return (z * 2 + y, x * 2 + c)


def column_peers(n_dp):
    d, h = lax.axis_index("dp"), lax.axis_index("head")
    return [(lax.rem(d + k, n_dp), h) for k in range(1, n_dp)]


def head_peers(n_head):
    d, h = lax.axis_index("dp"), lax.axis_index("head")
    return [(d, lax.rem(h + k, n_head)) for k in range(1, n_head)]


def greet(devices):
    barrier = pltpu.get_barrier_semaphore()
    for device in devices:
        pl.semaphore_signal(barrier, inc=1, device_id=device, device_id_type=MESH)
    pl.semaphore_wait(barrier, len(devices))


def remote(src, dst, send, recv, device):
    return pltpu.make_async_remote_copy(
        src_ref=src, dst_ref=dst, send_sem=send, recv_sem=recv, device_id=device, device_id_type=MESH
    )


def each(count, body):
    def step(n, carry):
        body(n)
        return carry

    lax.fori_loop(0, count, step, 0)


def span(index, size):
    return pl.ds(pl.multiple_of(index * size, size), size)


def row(n):
    return pl.ds(n, 1)


def lines_from(i):
    return pl.ds(i * LINE if isinstance(i, int) else pl.multiple_of(i * LINE, LINE), ALL)


def dot(left, right):
    return jnp.dot(left, right, preferred_element_type=F32)


def dot_nt(left, right):
    return lax.dot_general(left, right, (((1,), (1,)), ((), ())), preferred_element_type=F32)


def dot_tn(left, right):
    return lax.dot_general(left, right, (((0,), (0,)), ((), ())), preferred_element_type=F32)


def in_group(first, second, axis):
    chan = lax.broadcasted_iota(jnp.int32, (first, second), axis)
    group = lax.broadcasted_iota(jnp.int32, (first, second), 1 - axis) * (C // GROUPS)
    inside = jnp.logical_and(chan >= group, chan < group + C // GROUPS)
    return jnp.where(inside, 1.0, 0.0).astype(BF16)


def pieces(values):
    high = values.astype(BF16).astype(F32)
    rest = values - high
    mid = rest.astype(BF16).astype(F32)
    return jnp.concatenate([high, mid, rest - mid], axis=0).astype(BF16)


def group_mean(sums):
    count = sums.shape[0]
    part = dot(pieces(sums), in_group(C, 128, 0))
    part = (part[:count] + part[count : 2 * count] + part[2 * count :]) * (1.0 / (PIX * (C // GROUPS)))
    back = dot(pieces(part), in_group(128, C, 1))
    return back[:count] + back[count : 2 * count] + back[2 * count :]


def sum_rows(values):
    return jnp.sum(values, axis=0, keepdims=True)


def norm_stats(get, mean_ref, inverse_ref, sums_ref):
    def first(n):
        sums_ref[row(n)] = sum_rows(get(n))

    each(SLOTS, first)
    mean_ref[...] = group_mean(sums_ref[...])

    def second(n):
        centred = get(n) - mean_ref[row(n)]
        sums_ref[row(n)] = sum_rows(centred * centred)

    each(SLOTS, second)
    inverse_ref[...] = lax.rsqrt(group_mean(sums_ref[...]) + EPSILON)


def silu(values):
    return values * jax.nn.sigmoid(values)


def shifted(values):
    spot = lax.rem(lax.broadcasted_iota(jnp.int32, values.shape, 0), RES)
    left = jnp.where(spot == 0, 0.0, pltpu.roll(values, 1, 0))
    right = jnp.where(spot == RES - 1, 0.0, pltpu.roll(values, values.shape[0] - 1, 0))
    return left, right


def chunk(n):
    return slice(n * WIDTH, (n + 1) * WIDTH)


CHUNKS = C // WIDTH


def weight_cols(ref, n):
    return ref[:, :, :, chunk(n)].reshape(C, WIDTH)


def weight_rows(ref, n):
    return ref[...].reshape(C, C)[chunk(n)]


def forward_kernel(
    lines,
    weights_a,
    weights_b,
    weights_qkv,
    weights_proj,
    images_hbm,
    cot_hbm,
    counts_ref,
    labels_ref,
    levels_ref,
    class_table,
    noise_table,
    modw_table,
    modb_ref,
    *refs,
):
    vectors, refs = refs[:VECTORS], refs[VECTORS:]
    forward_steps(
        lines,
        vectors,
        weights_a,
        weights_b,
        weights_qkv,
        weights_proj,
        images_hbm,
        cot_hbm,
        counts_ref,
        labels_ref,
        levels_ref,
        class_table,
        noise_table,
        modw_table,
        modb_ref,
        *refs,
    )


def forward_steps(
    lines,
    vectors,
    weights_a,
    weights_b,
    weights_qkv,
    weights_proj,
    images_hbm,
    cot_hbm,
    counts_ref,
    labels_ref,
    levels_ref,
    class_table,
    noise_table,
    modw_table,
    modb_ref,
    whole_out,
    conv_out,
    slopes_out,
    turned_out,
    block_out,
    grad_out,
    low_out,
    right_out,
    vecs_ref,
    mod_ref,
    stats_ref,
    pre_ref,
    all_ids,
    sums_out,
    halves,
    whole_ref,
    vec_ref,
    ids_ref,
    class_ref,
    modw_ref,
    vec_all,
    mod_part,
    mod_got,
    act,
    act_f32,
    sums_ref,
    conv_ref,
    resid_ref,
    slopes,
    turned,
    attn_in,
    qkv,
    right,
    low,
    pair_ref,
    pair_send,
    pair_recv,
    pair_local,
    z_send,
    z_recv,
    p_send,
    x_send,
    x_recv,
    y_send,
    y_recv,
    s_send,
    s_recv,
    vec_send,
    vec_recv,
    ids_send,
    ids_recv,
    mod_send,
    mod_recv,
    unit_sem,
    flush_sem,
    in_sem,
    share_local,
    share_send,
    share_recv,
):
    z, y, x, c = place()
    d, h = lax.axis_index("dp"), lax.axis_index("head")
    n_dp, n_head = lines * 2, 4
    half = lines // 2
    inner = jnp.logical_and(z > 0, z < lines - 1)
    far = at_chip(lax.rem(3 * z + 1, lines), y, x, c)
    rows, cols_own = halves.shape[2:]
    wide = 2 * cols_own
    sibling = at_chip(z, y, x, 1 - c)
    along_x = at_chip(z, y, 1 - x, c)
    along_y = at_chip(z, 1 - y, x, c)
    line = [at_chip(lax.rem(z + k, lines), y, x, c) for k in range(1, lines)]
    column, heads = column_peers(n_dp), head_peers(n_head)
    greet(column + heads)

    def spot(i, cc, zz, yy, xx):
        return whole_ref.at[i, cc, zz, yy, :, span(xx, wide)]

    def parts_of(core):
        return (
            (weights_a.at[pl.ds(4 * core, 4)], pl.ds(0, 4)),
            (weights_b.at[pl.ds(4 * core, 4)], pl.ds(5, 4)),
            (weights_qkv.at[pl.ds(core, 1)], pl.ds(9, 1)),
        )

    last_parts = (
        ((weights_a.at[8], 4), (weights_qkv.at[2], 10)),
        ((weights_b.at[8], 4), (weights_proj, 10)),
    )

    def keep_copy(k):
        source, where = parts_of(c)[k]
        return pltpu.make_async_copy(source, halves.at[c, where], pair_local.at[k])

    def swap_copy(k):
        source, where = parts_of(1 - c)[k]
        return remote(source, halves.at[c, where], pair_send.at[k], pair_recv.at[k], sibling)

    def last_keep(core, k):
        source, where = last_parts[core][k]
        return pltpu.make_async_copy(source, halves.at[c, where], pair_local.at[3 + k])

    def last_swap(core, k):
        source, where = last_parts[core][k]
        return remote(source, halves.at[c, where], pair_send.at[3 + k], pair_recv.at[3 + k], sibling)

    def swap_start():
        for k in range(3):
            swap_copy(k).start()
            keep_copy(k).start()
        for core in range(2):

            @pl.when(c == core)
            def _():
                for k in range(2):
                    last_swap(1 - core, k).start()
                    last_keep(core, k).start()

    def swap_wait(k):
        if k < 3:
            keep_copy(k).wait()
            swap_copy(k).wait()
        else:
            last_keep(0, k - 3).wait()
            last_swap(0, k - 3).wait()

    def images_copy():
        return pltpu.make_async_copy(images_hbm, images_ref, in_sem.at[0])

    def cot_copy():
        return pltpu.make_async_copy(cot_hbm, cot_ref, in_sem.at[1])

    images_ref, cot_ref = attn_in, low

    def vec_copy(k):
        return remote(vec_ref, vec_all.at[h], vec_send.at[k], vec_recv.at[k], heads[k])

    def ids_copy(k):
        return remote(ids_ref, all_ids.at[d], ids_send.at[k], ids_recv.at[k], column[k])

    def mod_copy(k):
        return remote(
            mod_part.at[lax.rem(d + k + 1, n_dp)], mod_got.at[d], mod_send.at[k], mod_recv.at[k], column[k]
        )

    def z_part(i, zz):
        if isinstance(i, int) and i >= FAR:
            return whole_ref.at[i, c, zz]
        return spot(i, c, zz, y, x)

    def z_copy(i, k):
        ref = z_part(i, z)
        return remote(ref, ref, z_send.at[i, k], z_recv.at[i, k], line[k])

    def z_pass(i):
        ref = z_part(i, lax.rem(z + 2, lines))
        return remote(ref, ref, p_send.at[i], z_recv.at[i, lax.rem(2 * z + 2, lines)], far)

    def z_start(i):
        z_copy(i, 1).start()

        @pl.when(z != lines - 1)
        def _():
            z_copy(i, 0).start()

        @pl.when(z != 0)
        def _():
            z_copy(i, 2).start()

    def z_relay(i):
        z_copy(i, 1).wait_recv()

        @pl.when(inner)
        def _():
            z_pass(i).start()

    def z_finish(i):
        z_copy(i, 0).wait_recv()
        z_copy(i, 2).wait_recv()

    def z_drain(i):
        z_copy(i, 1).wait_send()

        @pl.when(z != lines - 1)
        def _():
            z_copy(i, 0).wait_send()

        @pl.when(z != 0)
        def _():
            z_copy(i, 2).wait_send()

        @pl.when(inner)
        def _():
            z_pass(i).wait_send()

    def x_copy(i, part):
        if isinstance(i, int) and i >= FAR:
            ref = spot(i, c, z, y, x) if part == 0 else spot(i, c, z, 1 - y, x).at[pl.ds(rows // 2, rows // 2)]
        elif part == 0:
            ref = spot(i, c, slice(None), y, x)
        else:
            ref = spot(i, c, pl.ds(half, half), 1 - y, x)
        return remote(ref, ref, x_send.at[i, part], x_recv.at[i, part], along_x)

    def y_copy(i, part):
        if isinstance(i, int) and i >= FAR:
            ref = spot(i, c, z, y, x) if part == 0 else spot(i, c, z, y, 1 - x).at[pl.ds(0, rows // 2)]
        elif part == 0:
            ref = spot(i, c, slice(None), y, x)
        else:
            ref = spot(i, c, pl.ds(0, half), y, 1 - x)
        return remote(ref, ref, y_send.at[i, part], y_recv.at[i, part], along_y)

    def s_copy(i, part):
        if isinstance(i, int) and i >= FAR:
            ref = whole_ref.at[i, c, part]
        else:
            yy, xx = ((y, x), (y, 1 - x), (1 - y, x), (1 - y, 1 - x))[part]
            ref = spot(i, c, slice(None), yy, xx)
        return remote(ref, ref, s_send.at[i, part], s_recv.at[i, part], sibling)

    def join(i):
        whole_ref[i, c, z, y, :, span(x, wide)] = jnp.concatenate([halves[0, i], halves[1, i]], axis=-1)

    def begin(i):
        join(i)
        z_start(i)

    def far_begin(i):
        x_copy(i, 0).start()
        y_copy(i, 0).start()

    def far_pass(i):
        x_copy(i, 0).wait_recv()
        y_copy(i, 1).start()
        y_copy(i, 0).wait_recv()
        x_copy(i, 1).start()

    def far_line(i):
        x_copy(i, 1).wait_recv()
        y_copy(i, 1).wait_recv()
        z_start(i)

    def far_finish(i):
        z_finish(i)
        for part in range(lines):
            s_copy(i, part).start()

    def spread_line(i):
        z_finish(i)
        x_copy(i, 0).start()
        y_copy(i, 0).start()
        s_copy(i, 0).start()

    def pass_on(i):
        x_copy(i, 0).wait_recv()
        y_copy(i, 1).start()
        s_copy(i, 1).start()
        y_copy(i, 0).wait_recv()
        x_copy(i, 1).start()
        s_copy(i, 2).start()

    def finish(i):
        x_copy(i, 1).wait_recv()
        y_copy(i, 1).wait_recv()
        s_copy(i, 3).start()

    def arrived(i):
        for part in range(4):
            s_copy(i, part).wait_recv()

    def unit_copy(i):
        return pltpu.make_async_copy(whole_ref.at[i], whole_out.at[i], unit_sem.at[i])

    def fetch(i):
        arrived(i)
        if not isinstance(i, int) or i < FAR:
            unit_copy(i).start()

    def product(total, tap, i, k):
        for n in range(CHUNKS):
            value = dot(act[tap % 3, lines_from(tap // 3)], weight_cols(whole_ref.at[i, k], n))
            total[:, :, :, chunk(n)] += value.reshape(RES, SLOTS, RES, WIDTH)

    def use_pair(total, i, first):
        each(2, lambda k: product(total, i - first + 4 * k, i, k))

    flushed = (
        (conv_ref, conv_out),
        (slopes.at[0], slopes_out.at[0]),
        (slopes.at[1], slopes_out.at[1]),
        (low, block_out),
        (resid_ref, grad_out),
        (attn_in, low_out),
    )

    def share_parts(k):
        if k < 4:
            return turned.at[k], turned_out.at[k, :, span(c, ALL)]
        part = (3, 1 - c, 2)[k - 4]
        return right.at[part], right_out.at[part, span(c, ALL)]

    def share_give(k):
        return remote(*share_parts(k), share_send.at[k], share_recv.at[k], sibling)

    def right_keep(k):
        return pltpu.make_async_copy(right.at[k], right_out.at[k, span(c, ALL)], share_local.at[4 + k])

    def turned_keep(k):
        return pltpu.make_async_copy(*share_parts(k), share_local.at[k])

    def share_if(k, giving, run):
        if k in (1, 4, 6):
            taker = 0 if k == 6 else 1
            pl.when(c == (1 - taker if giving else taker))(run)
        else:
            run()

    def share(k):
        share_if(k, True, lambda: share_give(k).start())

    def share_wait():
        for k in range(7):
            share_if(k, True, lambda k=k: share_give(k).wait_send())
            share_if(k, False, lambda k=k: share_give(k).wait_recv())
        for k in range(4):
            turned_keep(k).wait()
            right_keep(k).wait()

    def flush(k):
        return pltpu.make_async_copy(*flushed[k], flush_sem.at[k])

    def set_act(place_t):
        def by_line(yy):
            value = act_f32[yy].reshape(LINE, C)
            left, right = shifted(value)
            spot_rows = pl.ds(pl.multiple_of((yy + 1) * LINE, LINE), LINE)
            act[0, spot_rows] = left.astype(BF16)
            act[1, spot_rows] = value.astype(BF16)
            act[2, spot_rows] = right.astype(BF16)

        each(RES, by_line)

        def turn(yy):
            value = act_f32[pl.ds(2 * yy, 2)].reshape(2 * LINE, C)
            turned[place_t, :, span(yy, 2 * LINE)] = value.T.astype(BF16)

        each(RES // 2, turn)

    def activate(which, n, value):
        sigma = jax.nn.sigmoid(value)
        act_f32[:, n] = (value * sigma).reshape(RES, RES, C)
        slopes[which, :, n] = (sigma * (1.0 + value * (1.0 - sigma))).reshape(RES, RES, C)

    def norm_a():
        for k in range(n_head - 1):
            vec_copy(k).wait()
        vecs_ref[...] = jnp.concatenate([vec_all[k].astype(F32) for k in range(n_head)], axis=-1)

        images_copy().wait()

        def get(n):
            return images_ref[span(n, PIX)].astype(F32)

        mean, inverse = stats_ref.at[0], stats_ref.at[1]
        norm_stats(get, mean, inverse, sums_ref)

        def to_act(n):
            value = (get(n) - mean[row(n)]) * inverse[row(n)]
            activate(0, n, value * vecs_ref[0:1] + vecs_ref[1:2])
            conv_ref[:, n] = jnp.broadcast_to(vecs_ref[2:3].reshape(1, 1, C), (RES, RES, C))
            resid_ref[:, n] = (get(n) + vecs_ref[5:6]).reshape(RES, RES, C)

        each(SLOTS, to_act)
        set_act(3)
        flush(1).start()
        turned_keep(3).start()
        share(3)

    def embed():
        for k in range(n_dp - 1):
            ids_copy(k).wait()
        ids = all_ids[...].reshape(n_dp * SLOTS, 128)
        table = class_ref.shape[1]
        label_hot = lax.broadcasted_iota(jnp.int32, (n_dp * SLOTS, table), 1) == ids[:, 0:1]
        levels = noise_table.shape[0]
        level_hot = lax.broadcasted_iota(jnp.int32, (n_dp * SLOTS, levels), 1) == ids[:, 1:2]
        pre = dot_nt(jnp.where(label_hot, 1.0, 0.0).astype(BF16), class_ref[...])
        width = class_table.shape[0]
        place_of = lax.broadcasted_iota(jnp.int32, (C, 128), 0) - d * width
        lane = lax.broadcasted_iota(jnp.int32, (C, 128), 1)
        chosen = jnp.logical_and(place_of == lane, lane < width)
        noise = dot(noise_table[...], jnp.where(chosen, 1.0, 0.0).astype(BF16)).astype(BF16)
        pre += dot(jnp.where(level_hot, 1.0, 0.0).astype(BF16), noise)
        pre_ref[...] = pre
        part = dot(silu(pre).astype(BF16), modw_ref[...])
        for k in range(n_dp):
            mine = part[k * SLOTS : (k + 1) * SLOTS]
            mod_part[k] = jnp.concatenate([mine[:, :C], mine[:, C:]], axis=0).astype(BF16)
        mod_got[d] = mod_part[d]
        for k in range(n_dp - 1):
            mod_copy(k).start()

    def norm_b():
        for k in range(n_dp - 1):
            mod_copy(k).wait()
        bias = modb_ref[...].astype(F32)
        total = jnp.concatenate([jnp.broadcast_to(bias[k : k + 1], (SLOTS, C)) for k in range(2)], axis=0)
        for k in range(n_dp):
            total += mod_got[k].astype(F32)
        mod_ref[...] = total.astype(BF16).astype(F32)

        def get(n):
            return conv_ref[:, n].reshape(PIX, C)

        mean, inverse = stats_ref.at[2], stats_ref.at[3]
        norm_stats(get, mean, inverse, sums_ref)

        def to_act(n):
            value = (get(n) - mean[row(n)]) * inverse[row(n)]
            value = value * vecs_ref[3:4] + vecs_ref[4:5]
            value = mod_ref[row(SLOTS + n)] + value * (mod_ref[row(n)] + 1.0)
            activate(1, n, value)

        each(SLOTS, to_act)
        set_act(2)
        flush(0).start()
        flush(2).start()
        turned_keep(2).start()
        share(2)

    def residual(n):
        return resid_ref[:, n].reshape(PIX, C)

    def normed(n):
        return (residual(n) - stats_ref[4, row(n)]) * stats_ref[5, row(n)]

    def transpose_out(source, place_t):
        def turn(k):
            value = source[span(k, 2 * LINE)].astype(F32)
            turned[place_t, :, span(k, 2 * LINE)] = value.T.astype(BF16)

        each(ALL // (2 * LINE), turn)

    def live(n):
        slots = counts_ref[0, d * n_head + h] + counts_ref[1, d * n_head + h]
        return jnp.where(n < slots, 1.0, 0.0)

    def norm_c():
        cot_copy().wait()
        norm_stats(residual, stats_ref.at[4], stats_ref.at[5], sums_ref)
        sums_out[...] = jnp.zeros_like(sums_out)

        def prepare(n):
            attn_in[span(n, PIX)] = (normed(n) * vecs_ref[6:7] + vecs_ref[7:8]).astype(BF16)
            grad = cot_ref[span(n, PIX)].astype(F32) * live(n)
            right[3, span(n, PIX)] = grad.astype(BF16)
            sums_out[8:9] += sum_rows(grad)

        each(SLOTS, prepare)
        transpose_out(attn_in, 0)
        turned_keep(0).start()
        right_keep(3).start()
        share(0)
        share(4)

    def attention():
        unit = tuple(whole_ref.at[9 + t // 2, t % 2] for t in range(4))
        for t in range(4):
            for n in range(CHUNKS):
                if t < 3:
                    value = dot(attn_in[...], weight_cols(unit[t], n))
                else:
                    value = dot_nt(right[3], weight_rows(unit[3], n))
                qkv[t, :, chunk(n)] = value.astype(BF16)
        factor = DH ** (-0.5)
        band = lax.broadcasted_iota(jnp.int32, (PIX, BAND), 1) // DH
        heads_at_once = BAND // DH

        def stack(value):
            zero = jnp.zeros_like(value)
            return jnp.concatenate([jnp.where(band == k, value, zero) for k in range(heads_at_once)], axis=0)

        def pick(value):
            out = value[:PIX]
            for k in range(1, heads_at_once):
                out = jnp.where(band == k, value[k * PIX : (k + 1) * PIX], out)
            return out

        def attend(n):
            for b in range(C // BAND):
                query, key, value, grad = (qkv[t, span(n, PIX), slice(b * BAND, (b + 1) * BAND)] for t in range(4))
                query4, grad4 = stack(query), stack(grad)
                scores = dot_nt(key, query4) * factor
                weight = jnp.exp(scores - jnp.max(scores, axis=0, keepdims=True))
                probs = weight / jnp.sum(weight, axis=0, keepdims=True)
                probs_low = probs.astype(BF16)
                low[span(n, PIX), slice(b * BAND, (b + 1) * BAND)] = pick(dot_tn(probs_low, value)).astype(BF16)
                grad_probs = dot_nt(value, grad4)
                inner_sum = jnp.sum(grad_probs * probs, axis=0, keepdims=True)
                grad_scores = (probs * (grad_probs - inner_sum)).astype(BF16)
                right[0, span(n, PIX), slice(b * BAND, (b + 1) * BAND)] = (pick(dot_tn(grad_scores, key)) * factor).astype(BF16)
                right[1, span(n, PIX), slice(b * BAND, (b + 1) * BAND)] = (dot(grad_scores, query4) * factor).astype(BF16)
                right[2, span(n, PIX), slice(b * BAND, (b + 1) * BAND)] = dot(probs_low, grad4).astype(BF16)

        each(SLOTS, attend)
        share(5)
        share(6)
        for k in range(3):
            right_keep(k).start()
        transpose_out(low, 1)
        turned_keep(1).start()
        share(1)
        for n in range(CHUNKS):
            value = dot(low[...], weight_cols(unit[3], n))
            act_f32[:, :, :, chunk(n)] = value.reshape(SLOTS, RES, RES, WIDTH)

        def finish_out(n):
            value = residual(n) + act_f32[n].reshape(PIX, C) + vecs_ref[8:9]
            low[span(n, PIX)] = (value * live(n)).astype(BF16)

        each(SLOTS, finish_out)
        flush(3).start()
        for n in range(CHUNKS):
            value = dot_nt(right[0], weight_rows(unit[0], n))
            value += dot_nt(right[1], weight_rows(unit[1], n))
            value += dot_nt(right[2], weight_rows(unit[2], n))
            act_f32[:, :, :, chunk(n)] = value.reshape(SLOTS, RES, RES, WIDTH)

        def back(n):
            grad = act_f32[n].reshape(PIX, C)
            pair_ref[row(n)] = sum_rows(grad * normed(n))
            pair_ref[row(SLOTS + n)] = sum_rows(grad)

        each(SLOTS, back)
        sums_out[6:7] = sum_rows(pair_ref[0:SLOTS])
        sums_out[7:8] = sum_rows(pair_ref[SLOTS:])
        pair_ref[...] = group_mean(pair_ref[...] * vecs_ref[6:7])

        def back_second(n):
            inverse = stats_ref[5, row(n)]
            value = act_f32[n].reshape(PIX, C) * (vecs_ref[6:7] * inverse)
            value -= normed(n) * (pair_ref[row(n)] * inverse) + pair_ref[row(SLOTS + n)] * inverse
            value += right[3, span(n, PIX)].astype(F32)
            resid_ref[:, n] = value.reshape(RES, RES, C)
            sums_out[5:6] += sum_rows(value.astype(BF16).astype(F32))

        each(SLOTS, back_second)
        flush(4).start()

        def lower(yy):
            attn_in[span(yy, LINE)] = resid_ref[yy].reshape(LINE, C).astype(BF16)

        each(RES, lower)
        flush(5).start()

    swap_start()
    images_copy().start()
    cot_copy().start()
    one = [ref[...].astype(F32).reshape(1, cols_own) for ref in vectors]
    vec_ref[...] = jnp.concatenate(one + [jnp.zeros((16 - VECTORS, cols_own), F32)], axis=0).astype(BF16)
    lane = lax.broadcasted_iota(jnp.int32, (1, 128), 1)
    for n in range(SLOTS):
        ids_ref[n : n + 1] = jnp.where(lane == 0, labels_ref[n], levels_ref[n])
    for k in range(n_head - 1):
        vec_copy(k).start()
    for k in range(n_dp - 1):
        ids_copy(k).start()
    width = class_table.shape[0]
    class_ref[...] = jnp.zeros_like(class_ref)
    class_ref[0:width, 0 : class_table.shape[1]] = class_table[...]
    modw_ref[...] = jnp.zeros_like(modw_ref)
    table = modw_table[...].astype(F32)
    for k in range(2):
        modw_ref[0:width, k * C : (k + 1) * C] = table[:, k].astype(BF16)
    vec_all[h] = vec_ref[...]
    all_ids[d] = ids_ref[...]
    edge = jnp.zeros((LINE, C), BF16)
    for j in range(3):
        act[j, 0:LINE] = edge
        act[j, ALL + LINE : ALL + 2 * LINE] = edge
    for k in range(5):
        swap_wait(k)
    for i in (10, 9):
        join(i)
    begin(0)
    for i in (10, 9):
        far_begin(i)
    begin(1)
    z_relay(0)
    begin(2)
    spread_line(0)
    for i in (10, 9):
        far_pass(i)
    begin(3)
    z_relay(1)
    norm_a()
    spread_line(1)
    pass_on(0)
    begin(4)
    z_relay(2)
    embed()
    spread_line(2)
    pass_on(1)
    finish(0)
    begin(5)
    z_relay(3)
    begin(6)
    z_relay(4)
    far_line(10)
    spread_line(3)
    pass_on(2)
    finish(1)
    fetch(0)

    def body(turn, carry):
        @pl.when(turn < 6)
        def _():
            begin(turn + 3)

        @pl.when(turn == 6)
        def _():
            far_line(9)
            z_relay(10)

        z_relay(turn + 1)
        spread_line(turn)
        pass_on(turn - 1)
        finish(turn - 2)
        fetch(turn - 3)
        use_pair(conv_ref, turn - 4, 0)
        return carry

    lax.fori_loop(4, 8, body, 0)
    spread_line(8)
    pass_on(7)
    finish(6)
    fetch(5)
    product(conv_ref, 8, 4, 0)
    norm_b()
    product(resid_ref, 8, 4, 1)
    pass_on(8)
    finish(7)
    z_relay(9)
    fetch(6)
    far_finish(10)
    use_pair(resid_ref, 5, 5)
    finish(8)
    fetch(7)
    use_pair(resid_ref, 6, 5)
    fetch(8)
    use_pair(resid_ref, 7, 5)
    far_finish(9)
    use_pair(resid_ref, 8, 5)
    norm_c()
    fetch(9)
    fetch(10)
    attention()

    def drain(i):
        z_drain(i)
        for part in range(2):
            x_copy(i, part).wait_send()
            y_copy(i, part).wait_send()
        for part in range(4):
            s_copy(i, part).wait_send()

    each(FAR, drain)
    drain(9)
    drain(10)
    for k in range(len(flushed)):
        flush(k).wait()
    each(FAR, lambda i: unit_copy(i).wait())
    share_wait()


def run_forward(weights, images, cotangent, counts, labels, levels, class_table, noise_table, modw, modb, vectors):
    n_dp, n_head = lax.axis_size("dp"), lax.axis_size("head")
    rows, cols = weights[0].shape[1:]
    lines, across, wide = n_dp // 2, n_head // 2, 2 * cols
    board = (RES, SLOTS, RES, C)
    shape = jax.ShapeDtypeStruct
    return pl.pallas_call(
        functools.partial(forward_kernel, lines),
        out_shape=(
            shape((FAR, 2, lines, 2, rows, across * wide), BF16),
            shape(board, F32),
            shape((2,) + board, F32),
            shape((4, C, 2 * ALL), BF16),
            shape((ALL, C), BF16),
            shape(board, F32),
            shape((ALL, C), BF16),
            shape((4, 2 * ALL, C), BF16),
            shape((16, C), F32),
            shape((2 * SLOTS, C), F32),
            shape((6, SLOTS, C), F32),
            shape((n_dp * SLOTS, 128), F32),
            shape((n_dp, SLOTS, 128), jnp.int32),
            shape((16, C), F32),
        ),
        in_specs=[ANY] * 6 + [SMEM] * 3 + [VMEM] * (4 + VECTORS),
        out_specs=(ANY,) * 8 + (VMEM,) * 6,
        scratch_shapes=[
            pltpu.VMEM((2, PAIRS, rows, cols), BF16),
            pltpu.VMEM((PAIRS, 2, lines, 2, rows, across * wide), BF16),
            pltpu.VMEM((16, cols), BF16),
            pltpu.VMEM((SLOTS, 128), jnp.int32),
            pltpu.VMEM((128, 1024), BF16),
            pltpu.VMEM((128, 2 * C), BF16),
            pltpu.VMEM((n_head, 16, cols), BF16),
            pltpu.VMEM((n_dp, 2 * SLOTS, C), BF16),
            pltpu.VMEM((n_dp, 2 * SLOTS, C), BF16),
            pltpu.VMEM((3, ALL + 2 * LINE, C), BF16),
            pltpu.VMEM(board, F32),
            pltpu.VMEM((SLOTS, C), F32),
            pltpu.VMEM(board, F32),
            pltpu.VMEM(board, F32),
            pltpu.VMEM((2,) + board, F32),
            pltpu.VMEM((4, C, ALL), BF16),
            pltpu.VMEM((ALL, C), BF16),
            pltpu.VMEM((4, ALL, C), BF16),
            pltpu.VMEM((4, ALL, C), BF16),
            pltpu.VMEM((ALL, C), BF16),
            pltpu.VMEM((2 * SLOTS, C), F32),
            DMA((5,)),
            DMA((5,)),
            DMA((5,)),
            DMA((PAIRS, lines - 1)),
            DMA((PAIRS, lines - 1)),
            DMA((PAIRS,)),
            DMA((PAIRS, 2)),
            DMA((PAIRS, 2)),
            DMA((PAIRS, 2)),
            DMA((PAIRS, 2)),
            DMA((PAIRS, 4)),
            DMA((PAIRS, 4)),
            DMA((n_head - 1,)),
            DMA((n_head - 1,)),
            DMA((n_dp - 1,)),
            DMA((n_dp - 1,)),
            DMA((n_dp - 1,)),
            DMA((n_dp - 1,)),
            DMA((FAR,)),
            DMA((6,)),
            DMA((2,)),
            DMA((8,)),
            DMA((7,)),
            DMA((7,)),
        ],
        compiler_params=pltpu.CompilerParams(
            collective_id=0, has_side_effects=True, vmem_limit_bytes=62 * 2**20
        ),
        name="gather_forward",
    )(
        *weights,
        images,
        cotangent,
        counts,
        labels,
        levels,
        class_table,
        noise_table,
        modw,
        modb,
        *vectors,
    )


BACK_FAR = (10, 8)
BACK_NEAR = tuple(i for i in range(PAIRS) if i not in BACK_FAR)
AHEAD = 3


def backward_kernel(
    lines,
    whole_ref,
    turned_ref,
    right_ref,
    grad_low_ref,
    grad_resid_ref,
    conv_ref,
    slopes_ref,
    images_hbm,
    stats_ref,
    vecs_ref,
    mod_ref,
    sums_in,
    pre_ref,
    ids_ref,
    modw_table,
    out_a,
    out_b,
    out_qkv,
    out_proj,
    image_ref,
    class_ref,
    modw_out,
    modb_out,
    vec_out,
    mine,
    from_x,
    from_y,
    from_z,
    far_x,
    far_y,
    far_z,
    ends,
    modw_ref,
    lefts,
    rights,
    grads,
    stage,
    stage_mine,
    weights,
    total,
    board,
    slopes,
    image_mine,
    images_ref,
    sums_ref,
    pair_ref,
    coef_ref,
    gm_mine,
    gm_all,
    mw_mine,
    mw_got,
    ge_all,
    vs_mine,
    vs_got,
    vt_mine,
    vt_all,
    x_send,
    x_recv,
    y_send,
    y_recv,
    z_send,
    z_recv,
    p_send,
    p_recv,
    e_send,
    e_recv,
    e_local,
    op_send,
    op_recv,
    op_local,
    load_sem,
    in_sem,
    out_sem,
    gm_send,
    gm_recv,
    mw_send,
    mw_recv,
    ge_send,
    ge_recv,
    vs_send,
    vs_recv,
    vt_send,
    vt_recv,
):
    z, y, x, c = place()
    d, h = lax.axis_index("dp"), lax.axis_index("head")
    n_dp, n_head = lines * 2, 4
    half = lines // 2
    inner = jnp.logical_and(z > 0, z < lines - 1)
    rows, wide = from_z.shape[2], from_z.shape[3]
    cols = wide // 2
    sibling = at_chip(z, y, x, 1 - c)
    along_x = at_chip(z, y, 1 - x, c)
    along_y = at_chip(z, 1 - y, x, c)
    line = [at_chip(lax.rem(z + k, lines), y, x, c) for k in range(1, lines)]
    column, heads = column_peers(n_dp), head_peers(n_head)

    own_rows = pl.ds(LINE, ALL)

    def op_own(k):
        source, place_of = (
            (right_ref.at[2 + c], rights.at[0]),
            (turned_ref.at[c], lefts.at[1]),
            (right_ref.at[c], rights.at[1]),
            (turned_ref.at[0], lefts.at[0]),
            (grad_low_ref, grads.at[1, c, own_rows]),
            (turned_ref.at[2], lefts.at[2]),
            (turned_ref.at[3], lefts.at[3]),
        )[k]
        return pltpu.make_async_copy(source, place_of, op_local.at[k])

    def low_copy():
        return remote(grad_low_ref, grads.at[1, c, own_rows], op_send.at[0], op_recv.at[0], sibling)

    def stage_copy():
        return remote(stage_mine, stage, op_send.at[1], op_recv.at[1], sibling)

    def lanes(xx):
        return span(xx, wide)

    first, second = pl.ds(0, rows // 2), pl.ds(rows // 2, rows // 2)

    def is_far(i):
        return i in BACK_FAR

    def x_copy(i, part):
        if is_far(i):
            into = far_x.at[BACK_FAR.index(i)]
            if part == 0:
                src, dst = mine.at[i, z, 1 - y, second, lanes(1 - x)], into.at[pl.ds(rows, rows // 2)]
            else:
                src, dst = mine.at[i, z, y, :, lanes(1 - x)], into.at[pl.ds(0, rows)]
        elif part == 0:
            src, dst = mine.at[i, pl.ds(half, half), 1 - y, :, lanes(1 - x)], from_x.at[BACK_NEAR.index(i), pl.ds(lines, half)]
        else:
            src, dst = mine.at[i, :, y, :, lanes(1 - x)], from_x.at[BACK_NEAR.index(i), pl.ds(0, lines)]
        return remote(src, dst, x_send.at[i, part], x_recv.at[i, part], along_x)

    def y_copy(i, part):
        if is_far(i):
            into = far_y.at[BACK_FAR.index(i)]
            if part == 0:
                src, dst = mine.at[i, z, 1 - y, first, lanes(1 - x)], into.at[pl.ds(rows, rows // 2)]
            else:
                src, dst = mine.at[i, z, 1 - y, :, lanes(x)], into.at[pl.ds(0, rows)]
        elif part == 0:
            src, dst = mine.at[i, pl.ds(0, half), 1 - y, :, lanes(1 - x)], from_y.at[BACK_NEAR.index(i), pl.ds(lines, half)]
        else:
            src, dst = mine.at[i, :, 1 - y, :, lanes(x)], from_y.at[BACK_NEAR.index(i), pl.ds(0, lines)]
        return remote(src, dst, y_send.at[i, part], y_recv.at[i, part], along_y)

    beyond = lax.rem(z + 2, lines)
    opposite = lines - 1 - z
    near_end = at_chip(1 + z // (lines - 1), y, x, c)

    def z_block(i, zz):
        return mine.at[i, zz] if is_far(i) else mine.at[i, zz, y, :, lanes(x)]

    def z_slot(i, k):
        return far_z.at[BACK_FAR.index(i), k] if is_far(i) else from_z.at[BACK_NEAR.index(i), k]

    def z_copy(i, k):
        return remote(
            z_block(i, lax.rem(z + k + 1, lines)), z_slot(i, k), z_send.at[i, k], z_recv.at[i, k], line[k]
        )

    def z_give(i):
        return remote(z_block(i, opposite), z_slot(i, 3), p_send.at[i], p_recv.at[i], near_end)

    def z_start(i):
        @pl.when(jnp.logical_not(inner))
        def _():
            z_give(i).start()

        @pl.when(z < lines - 1)
        def _():
            z_copy(i, 0).start()

        @pl.when(z > 0)
        def _():
            z_copy(i, 2).start()

        @pl.when(jnp.logical_not(inner))
        def _():
            z_copy(i, 1).start()

    def z_mix(i):
        @pl.when(inner)
        def _():
            z_give(i).wait_recv()
            if is_far(i):
                mine[i, beyond] += far_z[BACK_FAR.index(i), 3]
            else:
                mine[i, beyond, y, :, lanes(x)] += from_z[BACK_NEAR.index(i), 3]
            z_copy(i, 1).start()

    def z_wait(i):
        z_copy(i, 1).wait_recv()

        @pl.when(z > 0)
        def _():
            z_copy(i, 0).wait_recv()

        @pl.when(z < lines - 1)
        def _():
            z_copy(i, 2).wait_recv()

    def z_drain(i):
        z_copy(i, 1).wait_send()

        @pl.when(z < lines - 1)
        def _():
            z_copy(i, 0).wait_send()

        @pl.when(z > 0)
        def _():
            z_copy(i, 2).wait_send()

        @pl.when(jnp.logical_not(inner))
        def _():
            z_give(i).wait_send()

    def target(i, core):
        if isinstance(i, int) and i == 10:
            return out_proj if core == 1 else out_qkv.at[2]
        if isinstance(i, int) and i == 9:
            return out_qkv.at[core]
        if isinstance(i, int) and i == 4:
            return out_b.at[8] if core == 1 else out_a.at[8]
        if isinstance(i, int) and i > 4:
            return out_b.at[4 * core + i - 5]
        return out_a.at[4 * core + i]

    def e_copy(i, core):
        return remote(ends.at[1 - c, i], target(i, core), e_send.at[i], e_recv.at[i], sibling)

    def e_own(i, core):
        return pltpu.make_async_copy(ends.at[c, i], target(i, core), e_local.at[i])

    def finish(i, value):
        for cc in range(2):
            ends[cc, i] = value[:, cc * cols : (cc + 1) * cols]
        if i in (4, 10):
            for core in range(2):

                @pl.when(c == core)
                def _():
                    e_copy(i, core).start()
                    e_own(i, core).start()
        else:
            e_copy(i, c).start()
            e_own(i, c).start()

    def offer(i):
        x_copy(i, 0).start()
        y_copy(i, 0).start()

    def relay(i):
        x_copy(i, 0).wait_recv()
        y_copy(i, 0).wait_recv()
        if is_far(i):
            rest = pl.ds(rows, rows // 2)
            mine[i, z, y, first, lanes(1 - x)] += far_y[BACK_FAR.index(i), rest]
            mine[i, z, 1 - y, second, lanes(x)] += far_x[BACK_FAR.index(i), rest]
        else:
            for j in range(half):
                mine[i, j, y, :, lanes(1 - x)] += from_y[BACK_NEAR.index(i), lines + j]
                mine[i, half + j, 1 - y, :, lanes(x)] += from_x[BACK_NEAR.index(i), lines + j]
        x_copy(i, 1).start()
        y_copy(i, 1).start()

    def collect(i):
        x_copy(i, 1).wait_recv()
        y_copy(i, 1).wait_recv()
        if is_far(i):
            whole_rows = pl.ds(0, rows)
            value = mine[i, z, y, :, lanes(x)].astype(F32)
            value += far_x[BACK_FAR.index(i), whole_rows].astype(F32) + far_y[BACK_FAR.index(i), whole_rows].astype(F32)
            finish(i, value)
            return

        def add(j):
            value = mine[i, j, y, :, lanes(x)].astype(F32)
            value += from_x[BACK_NEAR.index(i), j].astype(F32) + from_y[BACK_NEAR.index(i), j].astype(F32)
            mine[i, j, y, :, lanes(x)] = value.astype(BF16)

        each(lines, add)
        z_start(i)

    def last(i):
        z_wait(i)
        if is_far(i):
            for yy in range(2):
                value = mine[i, z, yy].astype(F32)
                for k in range(lines - 1):
                    value += far_z[BACK_FAR.index(i), k, yy].astype(F32)
                mine[i, z, yy] = value.astype(BF16)
            offer(i)
            return
        value = mine[i, z, y, :, lanes(x)].astype(F32)
        for k in range(lines - 1):
            value += from_z[BACK_NEAR.index(i), k].astype(F32)
        finish(i, value)

    def put(i, n, value):
        mine[i, :, :, :, chunk(n)] = value.astype(BF16).reshape(mine.shape[1:4] + (WIDTH,))

    def plain_unit(i, left, right):
        for n in range(CHUNKS):
            put(i, n, dot(lefts[left], rights[right, :, chunk(n)]))

    def conv_unit(i, left, tap):
        where, side = lines_from(2 - tap // 3), 2 - tap % 3
        for n in range(CHUNKS):
            both = jnp.concatenate([grads[side, core, where, chunk(n)] for core in range(2)], axis=0)
            put(i, n, dot(lefts[left], both))

    def extra_b():
        @pl.when(c == 1)
        def _():
            conv_unit(4, 2, 8)

    def extra_a():
        @pl.when(c == 0)
        def _():
            conv_unit(4, 3, 8)

    def spread_sides(core):
        def by_line(yy):
            value = grads[1, core, pl.ds(pl.multiple_of((yy + 1) * LINE, LINE), LINE)].astype(F32)
            left, right = shifted(value)
            spot_rows = pl.ds(pl.multiple_of((yy + 1) * LINE, LINE), LINE)
            grads[0, core, spot_rows] = left.astype(BF16)
            grads[2, core, spot_rows] = right.astype(BF16)

        each(RES, by_line)

    def load(tap, base):
        ninth = tap // 8
        i = (base // 2 + tap % 4) * (1 - ninth) + 4 * ninth
        k = (tap // 4) % 2 + (base // 10) * ninth
        return pltpu.make_async_copy(whole_ref.at[i, k], weights.at[tap % (AHEAD + 1)], load_sem.at[tap % (AHEAD + 1)])

    def conv_back(tap, base):
        load(tap, base).wait()

        @pl.when(tap < 9 - AHEAD)
        def _():
            load(tap + AHEAD, base).start()

        part = grads[2 - tap % 3, c, lines_from(2 - tap // 3)]
        for n in range(CHUNKS):
            value = dot_nt(part, weight_rows(weights.at[tap % (AHEAD + 1)], n))
            total[:, :, :, chunk(n)] += value.reshape(RES, SLOTS, RES, WIDTH)

    def conv_back_range(first, stop, base):
        def body(tap, carry):
            conv_back(tap, base)
            return carry

        lax.fori_loop(first, stop, body, 0)

    def slope(values):
        sigma = jax.nn.sigmoid(values)
        return sigma * (1.0 + values * (1.0 - sigma))

    for k in (0, 2):
        from_z[:, k] = jnp.zeros_like(from_z[:, k])
        far_z[:, k] = jnp.zeros_like(far_z[:, k])
    greet(column + heads)
    low_copy().start()
    for k in (4, 0, 1, 2, 3, 5):
        op_own(k).start()
    for tap in range(AHEAD):
        load(tap, 10).start()

    def fetch(k):
        source, target = (
            (conv_ref, board),
            (slopes_ref.at[1], slopes),
            (slopes_ref.at[0], slopes),
            (grad_resid_ref, board),
            (images_hbm, images_ref),
        )[k]
        return pltpu.make_async_copy(source, target, in_sem.at[k])

    fetch(0).start()
    fetch(1).start()
    vs_mine[...] = jnp.zeros_like(vs_mine)
    edge = jnp.zeros((LINE, C), BF16)
    for j in range(3):
        for core in range(2):
            grads[j, core, 0:LINE] = edge
            grads[j, core, ALL + LINE : ALL + 2 * LINE] = edge
    total[...] = jnp.zeros_like(total)
    sums_ref[...] = sums_in[...]
    modw_ref[...] = jnp.zeros_like(modw_ref)
    table = modw_table[...].astype(F32)
    for k in range(2):
        modw_ref[0:rows, k * C : (k + 1) * C] = table[:, k].astype(BF16)

    def norm_b_value(n):
        return (board[:, n].reshape(PIX, C) - stats_ref[2, row(n)]) * stats_ref[3, row(n)]

    def norm_a_value(n):
        return (images_ref[span(n, PIX)].astype(F32) - stats_ref[0, row(n)]) * stats_ref[1, row(n)]

    def back_sums(get):
        def body(n):
            grad = (total[:, n] * slopes[:, n]).reshape(PIX, C)
            total[:, n] = grad.reshape(RES, RES, C)
            pair_ref[row(n)] = sum_rows(grad * get(n))
            pair_ref[row(SLOTS + n)] = sum_rows(grad)

        each(SLOTS, body)

    def back_factors(factor, inverse):
        coef_ref[0:SLOTS] = factor * inverse
        means = group_mean(pair_ref[...] * jnp.concatenate([factor, factor], axis=0))
        coef_ref[SLOTS : 2 * SLOTS] = means[:SLOTS] * inverse
        coef_ref[2 * SLOTS :] = means[SLOTS:] * inverse

    def back_value(n, get):
        value = total[:, n].reshape(PIX, C) * coef_ref[row(n)]
        return value - get(n) * coef_ref[row(SLOTS + n)] - coef_ref[row(2 * SLOTS + n)]

    def gm_copy(k):
        return remote(gm_mine, gm_all.at[d], gm_send.at[k], gm_recv.at[k], column[k])

    def mw_copy(k):
        return remote(
            mw_mine.at[lax.rem(h + k + 1, n_head)], mw_got.at[k], mw_send.at[k], mw_recv.at[k], heads[k]
        )

    def ge_copy(k):
        return remote(ge_all.at[h], ge_all.at[h], ge_send.at[k], ge_recv.at[k], heads[k])

    def vs_copy(k):
        return remote(
            vs_mine.at[lax.rem(h + k + 1, n_head)], vs_got.at[k], vs_send.at[k], vs_recv.at[k], heads[k]
        )

    def vt_copy(k):
        return remote(vt_mine, vt_all.at[d], vt_send.at[k], vt_recv.at[k], column[k])

    def image_copy():
        return pltpu.make_async_copy(image_mine, image_ref, out_sem)

    count = n_dp * SLOTS

    def start():
        op_own(0).wait()
        op_own(1).wait()

    def dw(i):
        if i == 10:
            plain_unit(10, 1, 0)
        elif i == 9:
            op_own(2).wait()
            op_own(3).wait()
            plain_unit(9, 0, 1)
        elif i > 4:
            conv_unit(i, 2, 4 * c + i - 5)
        else:
            conv_unit(i, 3, 4 * c + i)

    def sides():
        op_own(4).wait()
        low_copy().wait_recv()
        op_own(5).wait()
        spread_sides(0)
        spread_sides(1)

    def back_b_first():
        for tap in range(AHEAD):
            load(tap, 0).start()
        op_own(6).start()
        fetch(0).wait()
        fetch(1).wait()
        back_sums(norm_b_value)
        alone, with_norm = pair_ref[SLOTS:], pair_ref[:SLOTS]
        scale = mod_ref[0:SLOTS] + 1.0
        gm_mine[...] = jnp.concatenate([vecs_ref[3:4] * with_norm + vecs_ref[4:5] * alone, alone], axis=0).astype(BF16)
        gm_all[d] = gm_mine[...]
        for k in range(n_dp - 1):
            gm_copy(k).start()
        sums_ref[3:4] = sum_rows(with_norm * scale)
        sums_ref[4:5] = sum_rows(alone * scale)
        back_factors(scale * vecs_ref[3:4], stats_ref[3])

    def back_b_second():
        fetch(2).start()
        fetch(4).start()

        def body(n):
            value = back_value(n, norm_b_value).astype(BF16).astype(F32)
            sums_ref[2:3] += sum_rows(value)
            total[:, n] = value.reshape(RES, RES, C)

        each(SLOTS, body)
        fetch(3).start()

    def lower():
        def by_line(yy):
            stage_mine[span(yy, LINE)] = total[yy].reshape(LINE, C).astype(BF16)

        each(RES, by_line)
        stage_copy().start()
        total[...] = jnp.zeros_like(total)

    def take():
        stage_copy().wait_recv()

        def by_line(yy):
            spot_rows = pl.ds(pl.multiple_of((yy + 1) * LINE, LINE), LINE)
            grads[1, c, spot_rows] = stage_mine[span(yy, LINE)]
            grads[1, 1 - c, spot_rows] = stage[span(yy, LINE)]

        each(RES, by_line)
        spread_sides(0)
        spread_sides(1)
        op_own(6).wait()

    def modulation():
        for k in range(n_dp - 1):
            gm_copy(k).wait()
        parts = gm_all[...].astype(F32)
        gm_scale = parts[:, :SLOTS].reshape(count, C)
        gm_offset = parts[:, SLOTS:].reshape(count, C)
        pre = pre_ref[...]
        emb = silu(pre).astype(BF16)
        part_rows = rows // n_head
        for k, value in ((0, gm_scale), (1, gm_offset)):
            low_value = value.astype(BF16)
            grad_w = dot_tn(emb, low_value)
            place_lanes = slice(k * C, (k + 1) * C)
            for hh in range(n_head):
                mw_mine[hh, 0:part_rows, place_lanes] = grad_w[hh * part_rows : (hh + 1) * part_rows]
                mw_mine[hh, part_rows : part_rows + 8, place_lanes] = jnp.broadcast_to(sum_rows(value), (8, C))
        grad_e = dot_nt(gm_scale.astype(BF16), modw_ref[:, :C]) + dot_nt(gm_offset.astype(BF16), modw_ref[:, C:])
        grad_e = grad_e * slope(pre)
        label = ids_ref[...].reshape(count, 128)[:, 0:1].astype(F32)
        lane = lax.broadcasted_iota(jnp.int32, grad_e.shape, 1)
        ge_all[h] = jnp.where(lane < rows, grad_e, label)
        for k in range(n_head - 1):
            mw_copy(k).start()
            ge_copy(k).start()

    def back_a_first():
        fetch(2).wait()
        fetch(4).wait()
        back_sums(norm_a_value)
        sums_ref[0:1] = sum_rows(pair_ref[:SLOTS])
        sums_ref[1:2] = sum_rows(pair_ref[SLOTS:])
        for hh in range(n_head):
            vs_mine[hh] = sums_ref[:, hh * cols : (hh + 1) * cols]
        for k in range(n_head - 1):
            vs_copy(k).start()
        back_factors(jnp.broadcast_to(vecs_ref[0:1], (SLOTS, C)), stats_ref[1])

    def back_a_second():
        fetch(3).wait()

        def body(n):
            image_mine[span(n, PIX)] = back_value(n, norm_a_value) + board[:, n].reshape(PIX, C)

        each(SLOTS, body)
        image_copy().start()

    def vec_first():
        value = vs_mine[h]
        for k in range(n_head - 1):
            vs_copy(k).wait()
            value += vs_got[k]
        vt_mine[...] = value
        vt_all[d] = value
        for k in range(n_dp - 1):
            vt_copy(k).start()

    def mod_out():
        value = mw_mine[h]
        for k in range(n_head - 1):
            mw_copy(k).wait()
            value += mw_got[k]
        part_rows = rows // n_head
        first_lane = (d * n_head + h) * part_rows
        for k in range(2):
            lanes_of = slice(k * C, (k + 1) * C)
            modw_out[:, k] = value[:part_rows, lanes_of]
            turned_row = pltpu.roll(value[part_rows:, lanes_of], lax.rem(C - first_lane, C), 1)
            modb_out[k : k + 1] = turned_row[0:1, :part_rows]

    def class_out():
        for k in range(n_head - 1):
            ge_copy(k).wait()
        table = class_ref.shape[1]
        part = rows // n_head
        value = ge_all[...].reshape(n_head * count, 128)
        label = value[:, rows : rows + 1].astype(jnp.int32)
        hot = lax.broadcasted_iota(jnp.int32, (n_head * count, table), 1) == label
        own = pltpu.roll(value, lax.rem(128 - h * part, 128), 1).astype(BF16)
        value = dot_tn(own, jnp.where(hot, 1.0, 0.0).astype(BF16))
        class_ref[...] = value[:part]

    def vec_second():
        for k in range(n_dp - 1):
            vt_copy(k).wait()
        value = vt_all[0]
        for k in range(1, n_dp):
            value += vt_all[k]
        vec_out[...] = value

    start()
    dw(10)
    z_start(10)
    dw(9)
    offer(9)
    sides()
    dw(5)
    offer(5)
    dw(6)
    z_mix(10)
    relay(9)
    offer(6)
    conv_back_range(0, 3, 10)
    relay(5)
    conv_back_range(3, 6, 10)
    collect(9)
    conv_back_range(6, 9, 10)
    relay(6)
    z_mix(9)
    back_b_first()
    back_b_second()
    collect(5)
    lower()
    z_mix(5)
    dw(7)
    collect(6)
    offer(7)
    dw(8)
    last(10)
    z_mix(6)
    z_start(8)
    extra_b()
    relay(7)
    relay(10)
    last(9)
    take()
    extra_a()
    offer(4)
    last(5)
    dw(0)
    z_mix(8)
    offer(0)
    dw(1)
    collect(7)
    collect(10)
    offer(1)
    dw(2)
    offer(2)
    dw(3)
    relay(4)
    offer(3)
    conv_back_range(0, 3, 0)
    relay(0)
    relay(1)
    z_mix(7)
    conv_back_range(3, 6, 0)
    relay(2)
    last(6)
    conv_back_range(6, 9, 0)
    back_a_first()
    collect(4)
    modulation()
    last(8)
    relay(3)
    z_mix(4)
    collect(0)
    last(7)
    z_mix(0)
    back_a_second()
    vec_first()
    mod_out()
    collect(1)
    class_out()
    z_mix(1)
    vec_second()
    last(4)
    collect(2)
    relay(8)
    last(0)
    z_mix(2)
    last(1)
    collect(3)
    collect(8)
    z_mix(3)
    last(2)
    last(3)

    low_copy().wait_send()
    stage_copy().wait_send()
    image_copy().wait()

    def drain(i):
        for part in range(2):
            x_copy(i, part).wait_send()
            y_copy(i, part).wait_send()
        z_drain(i)
        e_copy(i, 0).wait()
        e_own(i, 0).wait()

    for i in range(PAIRS):
        drain(i)


def run_backward(whole, turned, right, grad_low, grad_resid, conv_out, slopes, images, stats, vecs, mod, sums, pre, ids, modw, classes):
    n_dp, n_head = lax.axis_size("dp"), lax.axis_size("head")
    _, _, lines, _, rows, depth = whole.shape
    cols = depth // n_head
    wide = 2 * cols
    board = (RES, SLOTS, RES, C)
    shape = jax.ShapeDtypeStruct
    return pl.pallas_call(
        functools.partial(backward_kernel, lines),
        out_shape=(
            shape((9, rows, cols), F32),
            shape((9, rows, cols), F32),
            shape((3, rows, cols), F32),
            shape((rows, cols), F32),
            shape((ALL, C), F32),
            shape((rows // n_head, classes), F32),
            shape((rows // n_head, 2, C), F32),
            shape((2, rows // n_head), F32),
            shape((16, cols), F32),
        ),
        in_specs=[ANY] * 8 + [VMEM] * 7,
        out_specs=(ANY,) * 5 + (VMEM,) * 4,
        scratch_shapes=[
            pltpu.VMEM((PAIRS, lines, 2, rows, depth), BF16),
            pltpu.VMEM((len(BACK_NEAR), lines + lines // 2, rows, wide), BF16),
            pltpu.VMEM((len(BACK_NEAR), lines + lines // 2, rows, wide), BF16),
            pltpu.VMEM((len(BACK_NEAR), 4, rows, wide), BF16),
            pltpu.VMEM((len(BACK_FAR), rows + rows // 2, wide), BF16),
            pltpu.VMEM((len(BACK_FAR), rows + rows // 2, wide), BF16),
            pltpu.VMEM((len(BACK_FAR), 4, 2, rows, depth), BF16),
            pltpu.VMEM((2, PAIRS, rows, cols), F32),
            pltpu.VMEM((128, 2 * C), BF16),
            pltpu.VMEM((4, C, 2 * ALL), BF16),
            pltpu.VMEM((2, 2 * ALL, C), BF16),
            pltpu.VMEM((3, 2, ALL + 2 * LINE, C), BF16),
            pltpu.VMEM((ALL, C), BF16),
            pltpu.VMEM((ALL, C), BF16),
            pltpu.VMEM((AHEAD + 1, lines, 2, rows, depth), BF16),
            pltpu.VMEM(board, F32),
            pltpu.VMEM(board, F32),
            pltpu.VMEM(board, F32),
            pltpu.VMEM((ALL, C), F32),
            pltpu.VMEM((ALL, C), BF16),
            pltpu.VMEM((16, C), F32),
            pltpu.VMEM((2 * SLOTS, C), F32),
            pltpu.VMEM((3 * SLOTS, C), F32),
            pltpu.VMEM((2 * SLOTS, C), BF16),
            pltpu.VMEM((n_dp, 2 * SLOTS, C), BF16),
            pltpu.VMEM((n_head, rows // n_head + 8, 2 * C), F32),
            pltpu.VMEM((n_head - 1, rows // n_head + 8, 2 * C), F32),
            pltpu.VMEM((n_head, n_dp * SLOTS, 128), F32),
            pltpu.VMEM((n_head, 16, cols), F32),
            pltpu.VMEM((n_head - 1, 16, cols), F32),
            pltpu.VMEM((16, cols), F32),
            pltpu.VMEM((n_dp, 16, cols), F32),
            DMA((PAIRS, 2)),
            DMA((PAIRS, 2)),
            DMA((PAIRS, 2)),
            DMA((PAIRS, 2)),
            DMA((PAIRS, lines - 1)),
            DMA((PAIRS, lines - 1)),
            DMA((PAIRS,)),
            DMA((PAIRS,)),
            DMA((PAIRS,)),
            DMA((PAIRS,)),
            DMA((PAIRS,)),
            DMA((2,)),
            DMA((2,)),
            DMA((7,)),
            DMA((AHEAD + 1,)),
            DMA((5,)),
            DMA,
            DMA((n_dp - 1,)),
            DMA((n_dp - 1,)),
            DMA((n_head - 1,)),
            DMA((n_head - 1,)),
            DMA((n_head - 1,)),
            DMA((n_head - 1,)),
            DMA((n_head - 1,)),
            DMA((n_head - 1,)),
            DMA((n_dp - 1,)),
            DMA((n_dp - 1,)),
        ],
        compiler_params=pltpu.CompilerParams(
            collective_id=1, has_side_effects=True, vmem_limit_bytes=64 * 2**20 - 2**18
        ),
        name="backward_scatter",
    )(whole, turned, right, grad_low, grad_resid, conv_out, slopes, images, stats, vecs, mod, sums, pre, ids, modw)


def results_kernel(count, *refs):
    sources, vec_ref, refs = refs[:count], refs[count], refs[count + 1 :]
    targets, vectors = refs[:count], refs[count : count + VECTORS]
    held, in_sems, out_sems = refs[count + VECTORS : -2], refs[-2], refs[-1]
    arrive = [pltpu.make_async_copy(sources[k], held[k], in_sems.at[k]) for k in range(count)]
    leave = [pltpu.make_async_copy(held[k], targets[k], out_sems.at[k]) for k in range(count)]
    for copy in arrive:
        copy.start()
    for k, ref in enumerate(vectors):
        ref[...] = vec_ref[k].reshape(ref.shape)
    for k in range(count):
        arrive[k].wait()
        leave[k].start()
    for copy in leave:
        copy.wait()


def run_results(arrays, vec):
    count = len(arrays)
    shape = jax.ShapeDtypeStruct
    return pl.pallas_call(
        functools.partial(results_kernel, count),
        out_shape=tuple(shape(one.shape, one.dtype) for one in arrays)
        + (shape(vec.shape[1:], F32),) * VECTORS,
        in_specs=[ANY] * count + [VMEM],
        out_specs=(ANY,) * count + (VMEM,) * VECTORS,
        scratch_shapes=[pltpu.VMEM(one.shape, one.dtype) for one in arrays] + [DMA((count,)), DMA((count,))],
        compiler_params=pltpu.CompilerParams(vmem_limit_bytes=60 * 2**20),
        name="results",
    )(*arrays, vec)


def direct(rows, cols):
    n_dp, n_head = lax.axis_size("dp"), lax.axis_size("head")
    return n_head == 4 and n_dp == 8 and rows % 32 == 0 and cols % 64 == 0


def fast_shards(
    images,
    cotangent,
    counts,
    labels,
    levels,
    noise_table,
    class_table,
    gain_a,
    shift_a,
    conv_a,
    bias_a,
    mod_weight,
    mod_bias,
    gain_b,
    shift_b,
    conv_b,
    bias_b,
    gain_c,
    shift_c,
    qkv_weight,
    proj_weight,
    proj_bias,
):
    weights = (
        jnp.swapaxes(conv_a, 0, 1),
        jnp.swapaxes(conv_b, 0, 1),
        jnp.swapaxes(qkv_weight, 0, 1),
        proj_weight,
    )
    vectors = (gain_a, shift_a, bias_a, gain_b, shift_b, bias_b, gain_c, shift_c, proj_bias)
    flat = images.reshape(ALL, C)
    (
        whole,
        conv_out,
        slopes,
        turned,
        block_out,
        grad_resid,
        grad_low,
        right,
        vecs,
        mod,
        stats,
        pre,
        all_ids,
        sums,
    ) = run_forward(
        weights,
        flat,
        cotangent.reshape(ALL, C),
        counts.T,
        labels,
        levels,
        class_table.T,
        noise_table,
        mod_weight,
        mod_bias,
        vectors,
    )
    *arrays, vec = run_backward(
        whole,
        turned,
        right,
        grad_low,
        grad_resid,
        conv_out,
        slopes,
        flat,
        stats,
        vecs,
        mod,
        sums,
        pre,
        all_ids,
        mod_weight,
        class_table.shape[0],
    )
    block_out, conva, convb, qkvw, projw, image_grad, class_grad, modw_grad, modb_grad, *rest = run_results(
        (block_out, *arrays), vec
    )
    gaina, shifta, biasa, gainb, shiftb, biasb, gainc, shiftc, projb = rest
    return (
        block_out.reshape(images.shape),
        image_grad.reshape(images.shape),
        class_grad.T,
        gaina,
        shifta,
        jnp.swapaxes(conva, 0, 1),
        biasa,
        modw_grad,
        modb_grad,
        gainb,
        shiftb,
        jnp.swapaxes(convb, 0, 1),
        biasb,
        gainc,
        shiftc,
        jnp.swapaxes(qkvw, 0, 1),
        projw,
        projb,
    )


def shards(*args):
    rows, _, cols = args[9].shape
    if direct(rows, cols):
        return fast_shards(*args)
    return plain_shards(*args)


def solution(mesh):
    placed = (
        P(("dp", "head"), None, None, None),
        P(("dp", "head"), None, None, None),
        P(),
        P(("dp", "head")),
        P(("dp", "head")),
        P(),
        P(None, "dp"),
        P("head"),
        P("head"),
        P("dp", None, "head"),
        P("head"),
        P("dp", None, None),
        P(),
        P("head"),
        P("head"),
        P("dp", None, "head"),
        P("head"),
        P("head"),
        P("head"),
        P("dp", None, "head"),
        P("dp", "head"),
        P("head"),
    )
    return jax.shard_map(
        shards,
        mesh=mesh,
        in_specs=placed,
        out_specs=(
            P(("dp", "head"), None, None, None),
            P(("dp", "head"), None, None, None),
            P(None, ("dp", "head")),
            P("head"),
            P("head"),
            P("dp", None, "head"),
            P("head"),
            P(("dp", "head"), None, None),
            P(None, ("dp", "head")),
            P("head"),
            P("head"),
            P("dp", None, "head"),
            P("head"),
            P("head"),
            P("head"),
            P("dp", None, "head"),
            P("dp", "head"),
            P("head"),
        ),
        check_vma=False,
    )
```

```python
import functools

import jax
import jax.numpy as jnp
from jax import lax
from jax.experimental import pallas as pl
from jax.experimental.pallas import tpu as pltpu
from jax.sharding import PartitionSpec as P

C = 768
DH = 64
GROUPS = 32


EPSILON = 1e-05
HIGHEST = lax.Precision.HIGHEST


def norm_forward(values, gain, shift):
    count, chans = (values.shape[0], values.shape[-1])
    span = C // GROUPS
    grouped = values.reshape(count, -1, chans // span, span)
    mean = jnp.mean(grouped, axis=(1, 3), keepdims=True)
    centred = grouped - mean
    inverse = lax.rsqrt(jnp.mean(centred * centred, axis=(1, 3), keepdims=True) + EPSILON)
    normed = (centred * inverse).reshape(values.shape)
    return (normed * gain + shift, normed, inverse)


def norm_backward(grad_out, normed, inverse, gain):
    grad_gain = jnp.sum(grad_out * normed, axis=(0, 1, 2))
    grad_shift = jnp.sum(grad_out, axis=(0, 1, 2))
    count, chans = (grad_out.shape[0], grad_out.shape[-1])
    span = C // GROUPS
    layout = (count, -1, chans // span, span)
    grad_normed = (grad_out * gain).reshape(layout)
    normed_groups = normed.reshape(layout)
    mean_one = jnp.mean(grad_normed, axis=(1, 3), keepdims=True)
    mean_two = jnp.mean(grad_normed * normed_groups, axis=(1, 3), keepdims=True)
    grad_in = inverse * (grad_normed - mean_one - normed_groups * mean_two)
    return (grad_in.reshape(grad_out.shape), grad_gain, grad_shift)


def silu_slope(values):
    sigma = jax.nn.sigmoid(values)
    return sigma * (1.0 + values * (1.0 - sigma))


def patches_of(act):
    count, rows, cols, chans = act.shape
    padded = jnp.pad(act, ((0, 0), (1, 1), (1, 1), (0, 0)))
    taps = [padded[:, i : i + rows, j : j + cols, :] for i in range(3) for j in range(3)]
    return jnp.stack(taps, axis=3).reshape(count * rows * cols, 9, chans)


def contract_rows(left, right):
    return lax.dot_general(
        left, right, (((0,), (0,)), ((), ())), preferred_element_type=jnp.float32
    )


def contract_cols(left, right):
    return lax.dot_general(
        left, right, (((1,), (1,)), ((), ())), preferred_element_type=jnp.float32
    )


def conv_back(grad_low, weight, count, rows, cols):
    chans = weight.shape[0]
    padded = jnp.zeros((count, rows + 2, cols + 2, chans), jnp.float32)
    for tap in range(9):
        i, j = divmod(tap, 3)
        part = contract_cols(grad_low, weight[:, tap, :]).reshape(count, rows, cols, chans)
        padded = padded.at[:, i : i + rows, j : j + cols, :].add(part)
    return padded[:, 1 : rows + 1, 1 : cols + 1, :]


def keep_same(values):
    return values


def live_rows(counts, first, number, count):
    sums = jnp.sum(counts, axis=1)
    chosen = lax.dynamic_slice_in_dim(sums, first, number)
    slots = lax.iota(jnp.int32, count)
    return (slots[None, :] < chosen[:, None]).astype(jnp.float32).reshape(number * count)


def residual_forward(source, mod_pair, weights, spread):
    (
        conv_one,
        conv_two,
        gain_one,
        shift_one,
        bias_one,
        gain_two,
        shift_two,
        bias_two,
        gain_three,
        shift_three,
    ) = weights
    out_a, normed_a, inverse_a = norm_forward(source, gain_one, shift_one)
    wide_a = spread(jax.nn.silu(out_a).astype(jnp.bfloat16))
    conv_out_a = (
        jnp.einsum("ptc,cto->po", patches_of(wide_a), conv_one, preferred_element_type=jnp.float32)
        + bias_one
    ).reshape(source.shape)
    scale = mod_pair[:, :, 0:1, :]
    offset = mod_pair[:, :, 1:2, :]
    out_b, normed_b, inverse_b = norm_forward(conv_out_a, gain_two, shift_two)
    inner_b = offset + out_b * (scale + 1.0)
    wide_b = spread(jax.nn.silu(inner_b).astype(jnp.bfloat16))
    conv_out_b = (
        jnp.einsum("ptc,cto->po", patches_of(wide_b), conv_two, preferred_element_type=jnp.float32)
        + bias_two
    ).reshape(source.shape)
    resid = source + conv_out_b
    out_c, normed_c, inverse_c = norm_forward(resid, gain_three, shift_three)
    attn_in = out_c.astype(jnp.bfloat16)
    saved = (
        out_a,
        normed_a,
        inverse_a,
        wide_a,
        out_b,
        normed_b,
        inverse_b,
        inner_b,
        wide_b,
        normed_c,
        inverse_c,
        scale,
    )
    return (resid, attn_in, saved)


def residual_backward(grad_attn, grad_out, saved, weights, reduce_value):
    conv_one, conv_two, gain_one, gain_two, gain_three = (
        weights[0],
        weights[1],
        weights[2],
        weights[5],
        weights[8],
    )
    (
        out_a,
        normed_a,
        inverse_a,
        wide_a,
        out_b,
        normed_b,
        inverse_b,
        inner_b,
        wide_b,
        normed_c,
        inverse_c,
        scale,
    ) = saved
    count, rows, cols, local = grad_out.shape
    grad_resid_c, gainc_term, shiftc_term = norm_backward(
        grad_attn, normed_c, inverse_c, gain_three
    )
    grad_resid = grad_out + grad_resid_c
    grad_conv_b = grad_resid.reshape(-1, local).astype(jnp.bfloat16)
    biasb_term = jnp.sum(grad_conv_b.astype(jnp.float32), axis=0)
    convb_term = jnp.einsum(
        "ptc,po->cto", patches_of(wide_b), grad_conv_b, preferred_element_type=jnp.float32
    )
    grad_act_b = reduce_value(conv_back(grad_conv_b, conv_two, count, rows, cols))
    grad_inner = grad_act_b * silu_slope(inner_b)
    grad_offset = jnp.sum(grad_inner, axis=(1, 2))
    grad_scale = jnp.sum(grad_inner * out_b, axis=(1, 2))
    grad_mod = jnp.stack([grad_scale, grad_offset], axis=1)[:, None]
    grad_conv_full, gainb_term, shiftb_term = norm_backward(
        grad_inner * (scale + 1.0), normed_b, inverse_b, gain_two
    )
    grad_conv_a = grad_conv_full.reshape(-1, local).astype(jnp.bfloat16)
    biasa_term = jnp.sum(grad_conv_a.astype(jnp.float32), axis=0)
    conva_term = jnp.einsum(
        "ptc,po->cto", patches_of(wide_a), grad_conv_a, preferred_element_type=jnp.float32
    )
    grad_act_a = reduce_value(conv_back(grad_conv_a, conv_one, count, rows, cols))
    grad_source, gaina_term, shifta_term = norm_backward(
        grad_act_a * silu_slope(out_a), normed_a, inverse_a, gain_one
    )
    image_grad = grad_resid + grad_source
    vectors = (
        gaina_term,
        shifta_term,
        biasa_term,
        gainb_term,
        shiftb_term,
        biasb_term,
        gainc_term,
        shiftc_term,
    )
    return (image_grad, grad_mod, (conva_term, convb_term), vectors)


def attend_forward(block):
    query, key, value = (block[:, :, 0], block[:, :, 1], block[:, :, 2])
    batch, pixels, heads_here, depth = query.shape
    scores = jnp.einsum("bqhd,bkhd->bhqk", query, key, preferred_element_type=jnp.float32) * DH ** (
        -0.5
    )
    top = jnp.max(scores, axis=-1, keepdims=True)
    weights = jnp.exp(scores - top)
    sums = jnp.sum(weights, axis=-1, keepdims=True)
    probs = (weights / sums).astype(jnp.bfloat16)
    logsum = (top + jnp.log(sums))[..., 0]
    mixed = jnp.einsum("bhqk,bkhd->bqhd", probs, value, preferred_element_type=jnp.float32).astype(
        jnp.bfloat16
    )
    return (mixed.reshape(batch, pixels, heads_here * depth), logsum)


def attend_backward(block, logsum, grad_head):
    query, key, value = (block[:, :, 0], block[:, :, 1], block[:, :, 2])
    batch, pixels, heads_here, depth = query.shape
    factor = DH ** (-0.5)
    scores = jnp.einsum("bqhd,bkhd->bhqk", query, key, preferred_element_type=jnp.float32) * factor
    probs = jnp.exp(scores - logsum[..., None])
    grad_value = jnp.einsum(
        "bhqk,bqhd->bkhd", probs.astype(jnp.bfloat16), grad_head, preferred_element_type=jnp.float32
    )
    grad_probs = jnp.einsum("bqhd,bkhd->bhqk", grad_head, value, preferred_element_type=jnp.float32)
    inner = jnp.sum(grad_probs * probs, axis=-1, keepdims=True)
    grad_scores = (probs * (grad_probs - inner)).astype(jnp.bfloat16)
    grad_query = (
        jnp.einsum("bhqk,bkhd->bqhd", grad_scores, key, preferred_element_type=jnp.float32) * factor
    )
    grad_key = (
        jnp.einsum("bhqk,bqhd->bkhd", grad_scores, query, preferred_element_type=jnp.float32)
        * factor
    )
    stacked = jnp.stack([grad_query, grad_key, grad_value], axis=2).astype(jnp.bfloat16)
    return stacked.reshape(batch, pixels, 3, heads_here * depth)


def plain_shards(
    images,
    cotangent,
    counts,
    labels,
    levels,
    noise_table,
    class_table,
    gain_a,
    shift_a,
    conv_a,
    bias_a,
    mod_weight,
    mod_bias,
    gain_b,
    shift_b,
    conv_b,
    bias_b,
    gain_c,
    shift_c,
    qkv_weight,
    proj_weight,
    proj_bias,
):
    rows_a, rows_b, rows_qkv, rows_proj, mod_full, class_full = (
        lax.all_gather(conv_a, "dp", axis=0, tiled=True),
        lax.all_gather(conv_b, "dp", axis=0, tiled=True),
        lax.all_gather(qkv_weight, "dp", axis=0, tiled=True),
        lax.all_gather(proj_weight, "dp", axis=0, tiled=True),
        lax.all_gather(mod_weight, "dp", axis=0, tiled=True),
        lax.all_gather(class_table, "dp", axis=1, tiled=True),
    )
    count, rows, cols, channels = images.shape
    pixels = rows * cols
    groups_n = lax.axis_size("head")
    quarter = channels // groups_n
    heads_local = quarter // DH
    first_dp = lax.axis_index("dp") * groups_n
    class_hot = (labels[:, None] == lax.iota(jnp.int32, class_full.shape[0])[None, :]).astype(
        jnp.bfloat16
    )
    level_hot = (levels[:, None] == lax.iota(jnp.int32, noise_table.shape[0])[None, :]).astype(
        jnp.bfloat16
    )
    embed_pre = jnp.dot(class_hot, class_full, preferred_element_type=jnp.float32) + jnp.dot(
        level_hot, noise_table, preferred_element_type=jnp.float32
    )
    embed = jax.nn.silu(embed_pre).astype(jnp.bfloat16)
    modulation = (
        jnp.einsum("ne,etc->ntc", embed, mod_full, preferred_element_type=jnp.float32)
        + mod_bias.astype(jnp.float32)
    ).astype(jnp.bfloat16)
    mod_pair = modulation.reshape(count, 1, 2, channels)
    (
        conv_one,
        conv_two,
        qkv_full,
        proj_full,
        gain_one,
        shift_one,
        bias_one,
        gain_two,
        shift_two,
        bias_two,
        gain_three,
        shift_three,
        bias_three,
    ) = (
        lax.all_gather(rows_a, "head", axis=2, tiled=True),
        lax.all_gather(rows_b, "head", axis=2, tiled=True),
        lax.all_gather(rows_qkv, "head", axis=2, tiled=True),
        lax.all_gather(rows_proj, "head", axis=1, tiled=True),
        lax.all_gather(gain_a, "head", axis=0, tiled=True),
        lax.all_gather(shift_a, "head", axis=0, tiled=True),
        lax.all_gather(bias_a, "head", axis=0, tiled=True),
        lax.all_gather(gain_b, "head", axis=0, tiled=True),
        lax.all_gather(shift_b, "head", axis=0, tiled=True),
        lax.all_gather(bias_b, "head", axis=0, tiled=True),
        lax.all_gather(gain_c, "head", axis=0, tiled=True),
        lax.all_gather(shift_c, "head", axis=0, tiled=True),
        lax.all_gather(proj_bias, "head", axis=0, tiled=True),
    )
    weights = (
        conv_one,
        conv_two,
        gain_one,
        shift_one,
        bias_one,
        gain_two,
        shift_two,
        bias_two,
        gain_three,
        shift_three,
    )
    live = live_rows(counts, first_dp + lax.axis_index("head"), 1, count)
    total = count * pixels
    width = channels // groups_n
    source = images.astype(jnp.float32)
    resid, attn_in, saved = residual_forward(
        source, mod_pair.astype(jnp.float32), weights, keep_same
    )
    attn_flat = attn_in.reshape(total, channels)
    qkv_flat = qkv_full.reshape(channels, 3 * channels)
    qkv = jnp.dot(attn_flat, qkv_flat, preferred_element_type=jnp.float32).astype(jnp.bfloat16)
    packed = qkv.reshape(1, count, pixels, 3, groups_n, width)
    block = lax.all_to_all(packed, "head", split_axis=4, concat_axis=0, tiled=True)
    groups = block.shape[0]
    items = block.shape[1]
    flat = block.reshape(groups * items, pixels, 3, heads_local, DH)
    mixed, logsum = attend_forward(flat)
    mixed = mixed.reshape(groups, items, pixels, 1, width)
    returned = lax.all_to_all(mixed, "head", split_axis=0, concat_axis=3, tiled=True)
    returned, logsum, kept = (returned, logsum.reshape(groups, items, heads_local, pixels), block)
    mixed_image = returned.reshape(total, channels)
    result = (
        resid.reshape(total, channels)
        + jnp.dot(mixed_image, proj_full, preferred_element_type=jnp.float32)
        + bias_three
    )
    block_out = (result.reshape(images.shape) * live[:, None, None, None]).astype(jnp.bfloat16)
    grad_out = cotangent.astype(jnp.float32) * live[:, None, None, None]
    grad_flat = grad_out.reshape(total, channels)
    grad_low = grad_flat.astype(jnp.bfloat16)
    projw_full = contract_rows(mixed_image, grad_low)
    projb_full = jnp.sum(grad_flat, axis=0)
    grad_mixed = contract_cols(grad_low, proj_full).astype(jnp.bfloat16)
    arrived = lax.all_to_all(
        grad_mixed.reshape(1, count, pixels, groups_n, width),
        "head",
        split_axis=3,
        concat_axis=0,
        tiled=True,
    )
    flat_block = kept.reshape(groups_n * count, pixels, 3, heads_local, DH)
    grad_head = arrived.reshape(groups_n * count, pixels, heads_local, DH)
    stacked = attend_backward(
        flat_block, logsum.reshape(groups_n * count, heads_local, pixels), grad_head
    )
    stacked = stacked.reshape(groups_n, count, pixels, 3, 1, width)
    grad_qkv = lax.all_to_all(stacked, "head", split_axis=0, concat_axis=4, tiled=True).reshape(
        total, 3 * channels
    )
    qkvw_full = contract_rows(attn_flat, grad_qkv).reshape(channels, 3, channels)
    grad_attn = contract_cols(grad_qkv, qkv_flat).reshape(images.shape)
    image_grad, grad_mod_part, conv_terms, vectors = residual_backward(
        grad_attn, grad_out, saved, weights, keep_same
    )
    (
        gaina_full,
        shifta_full,
        biasa_full,
        gainb_full,
        shiftb_full,
        biasb_full,
        gainc_full,
        shiftc_full,
    ) = vectors
    (
        conva_term,
        convb_term,
        qkvw_term,
        projw_term,
        gaina_term,
        shifta_term,
        biasa_term,
        gainb_term,
        shiftb_term,
        biasb_term,
        gainc_term,
        shiftc_term,
        projb_term,
    ) = (
        lax.psum_scatter(
            conv_terms[0].astype(jnp.bfloat16), "head", scatter_dimension=2, tiled=True
        ).astype(jnp.float32),
        lax.psum_scatter(
            conv_terms[1].astype(jnp.bfloat16), "head", scatter_dimension=2, tiled=True
        ).astype(jnp.float32),
        lax.psum_scatter(
            qkvw_full.astype(jnp.bfloat16), "head", scatter_dimension=2, tiled=True
        ).astype(jnp.float32),
        lax.psum_scatter(
            projw_full.astype(jnp.bfloat16), "head", scatter_dimension=1, tiled=True
        ).astype(jnp.float32),
        lax.psum_scatter(
            gaina_full.astype(jnp.bfloat16), "head", scatter_dimension=0, tiled=True
        ).astype(jnp.float32),
        lax.psum_scatter(
            shifta_full.astype(jnp.bfloat16), "head", scatter_dimension=0, tiled=True
        ).astype(jnp.float32),
        lax.psum_scatter(
            biasa_full.astype(jnp.bfloat16), "head", scatter_dimension=0, tiled=True
        ).astype(jnp.float32),
        lax.psum_scatter(
            gainb_full.astype(jnp.bfloat16), "head", scatter_dimension=0, tiled=True
        ).astype(jnp.float32),
        lax.psum_scatter(
            shiftb_full.astype(jnp.bfloat16), "head", scatter_dimension=0, tiled=True
        ).astype(jnp.float32),
        lax.psum_scatter(
            biasb_full.astype(jnp.bfloat16), "head", scatter_dimension=0, tiled=True
        ).astype(jnp.float32),
        lax.psum_scatter(
            gainc_full.astype(jnp.bfloat16), "head", scatter_dimension=0, tiled=True
        ).astype(jnp.float32),
        lax.psum_scatter(
            shiftc_full.astype(jnp.bfloat16), "head", scatter_dimension=0, tiled=True
        ).astype(jnp.float32),
        lax.psum_scatter(
            projb_full.astype(jnp.bfloat16), "head", scatter_dimension=0, tiled=True
        ).astype(jnp.float32),
    )
    grad_mod = grad_mod_part.reshape(count, 2, channels)
    modw_term = jnp.einsum("ne,ntc->etc", embed.astype(jnp.float32), grad_mod, precision=HIGHEST)
    modb_term = jnp.sum(grad_mod, axis=0)
    grad_embed = jnp.einsum(
        "ntc,etc->ne", grad_mod, mod_full.astype(jnp.float32), precision=HIGHEST
    ) * silu_slope(embed_pre)
    class_term = lax.dot_general(
        class_hot.astype(jnp.float32), grad_embed, (((0,), (0,)), ((), ())), precision=HIGHEST
    )
    modw_grad, class_grad, modb_grad = (
        lax.psum_scatter(modw_term, ("dp", "head"), scatter_dimension=0, tiled=True),
        lax.psum_scatter(class_term, ("dp", "head"), scatter_dimension=1, tiled=True),
        lax.psum_scatter(modb_term, ("dp", "head"), scatter_dimension=1, tiled=True),
    )
    conva_grad, convb_grad, qkvw_grad, projw_grad = (
        lax.psum_scatter(conva_term, "dp", scatter_dimension=0, tiled=True),
        lax.psum_scatter(convb_term, "dp", scatter_dimension=0, tiled=True),
        lax.psum_scatter(qkvw_term, "dp", scatter_dimension=0, tiled=True),
        lax.psum_scatter(projw_term, "dp", scatter_dimension=0, tiled=True),
    )
    (
        gaina_grad,
        shifta_grad,
        biasa_grad,
        gainb_grad,
        shiftb_grad,
        biasb_grad,
        gainc_grad,
        shiftc_grad,
        projb_grad,
    ) = lax.psum(
        (
            gaina_term,
            shifta_term,
            biasa_term,
            gainb_term,
            shiftb_term,
            biasb_term,
            gainc_term,
            shiftc_term,
            projb_term,
        ),
        "dp",
    )
    return (
        block_out,
        image_grad,
        class_grad,
        gaina_grad,
        shifta_grad,
        conva_grad,
        biasa_grad,
        modw_grad,
        modb_grad,
        gainb_grad,
        shiftb_grad,
        convb_grad,
        biasb_grad,
        gainc_grad,
        shiftc_grad,
        qkvw_grad,
        projw_grad,
        projb_grad,
    )


MESH = pl.DeviceIdType.MESH
UNITS = 22
PAIRS = UNITS // 2
FAR = 9
VECTORS = 9
RES = 8
SLOTS = 8
PIX = RES * RES
LINE = SLOTS * RES
ALL = RES * LINE
WIDTH = 768
BAND = 256
F32 = jnp.float32
BF16 = jnp.bfloat16
ANY = pl.BlockSpec(memory_space=pl.ANY)
VMEM = pl.BlockSpec(memory_space=pltpu.VMEM)
SMEM = pl.BlockSpec(memory_space=pltpu.SMEM)
DMA = pltpu.SemaphoreType.DMA


def place():
    d, h = lax.axis_index("dp"), lax.axis_index("head")
    return d // 2, lax.rem(d, 2), h // 2, lax.rem(h, 2)


def at_chip(z, y, x, c):
    return (z * 2 + y, x * 2 + c)


def column_peers(n_dp):
    d, h = lax.axis_index("dp"), lax.axis_index("head")
    return [(lax.rem(d + k, n_dp), h) for k in range(1, n_dp)]


def head_peers(n_head):
    d, h = lax.axis_index("dp"), lax.axis_index("head")
    return [(d, lax.rem(h + k, n_head)) for k in range(1, n_head)]


def greet(devices):
    barrier = pltpu.get_barrier_semaphore()
    for device in devices:
        pl.semaphore_signal(barrier, inc=1, device_id=device, device_id_type=MESH)
    pl.semaphore_wait(barrier, len(devices))


def remote(src, dst, send, recv, device):
    return pltpu.make_async_remote_copy(
        src_ref=src, dst_ref=dst, send_sem=send, recv_sem=recv, device_id=device, device_id_type=MESH
    )


def each(count, body):
    def step(n, carry):
        body(n)
        return carry

    lax.fori_loop(0, count, step, 0)


def span(index, size):
    return pl.ds(pl.multiple_of(index * size, size), size)


def row(n):
    return pl.ds(n, 1)


def lines_from(i):
    return pl.ds(i * LINE if isinstance(i, int) else pl.multiple_of(i * LINE, LINE), ALL)


def dot(left, right):
    return jnp.dot(left, right, preferred_element_type=F32)


def dot_nt(left, right):
    return lax.dot_general(left, right, (((1,), (1,)), ((), ())), preferred_element_type=F32)


def dot_tn(left, right):
    return lax.dot_general(left, right, (((0,), (0,)), ((), ())), preferred_element_type=F32)


def in_group(first, second, axis):
    chan = lax.broadcasted_iota(jnp.int32, (first, second), axis)
    group = lax.broadcasted_iota(jnp.int32, (first, second), 1 - axis) * (C // GROUPS)
    inside = jnp.logical_and(chan >= group, chan < group + C // GROUPS)
    return jnp.where(inside, 1.0, 0.0).astype(BF16)


def pieces(values):
    high = values.astype(BF16).astype(F32)
    rest = values - high
    mid = rest.astype(BF16).astype(F32)
    return jnp.concatenate([high, mid, rest - mid], axis=0).astype(BF16)


def group_mean(sums):
    count = sums.shape[0]
    part = dot(pieces(sums), in_group(C, 128, 0))
    part = (part[:count] + part[count : 2 * count] + part[2 * count :]) * (1.0 / (PIX * (C // GROUPS)))
    back = dot(pieces(part), in_group(128, C, 1))
    return back[:count] + back[count : 2 * count] + back[2 * count :]


def sum_rows(values):
    return jnp.sum(values, axis=0, keepdims=True)


def norm_stats(get, mean_ref, inverse_ref, sums_ref):
    def first(n):
        sums_ref[row(n)] = sum_rows(get(n))

    each(SLOTS, first)
    mean_ref[...] = group_mean(sums_ref[...])

    def second(n):
        centred = get(n) - mean_ref[row(n)]
        sums_ref[row(n)] = sum_rows(centred * centred)

    each(SLOTS, second)
    inverse_ref[...] = lax.rsqrt(group_mean(sums_ref[...]) + EPSILON)


def silu(values):
    return values * jax.nn.sigmoid(values)


def shifted(values):
    spot = lax.rem(lax.broadcasted_iota(jnp.int32, values.shape, 0), RES)
    left = jnp.where(spot == 0, 0.0, pltpu.roll(values, 1, 0))
    right = jnp.where(spot == RES - 1, 0.0, pltpu.roll(values, values.shape[0] - 1, 0))
    return left, right


def chunk(n):
    return slice(n * WIDTH, (n + 1) * WIDTH)


CHUNKS = C // WIDTH


def weight_cols(ref, n):
    return ref[:, :, :, chunk(n)].reshape(C, WIDTH)


def weight_rows(ref, n):
    return ref[...].reshape(C, C)[chunk(n)]


def forward_kernel(
    lines,
    weights_a,
    weights_b,
    weights_qkv,
    weights_proj,
    images_hbm,
    cot_hbm,
    counts_ref,
    labels_ref,
    levels_ref,
    class_table,
    noise_table,
    modw_table,
    modb_ref,
    *refs,
):
    vectors, refs = refs[:VECTORS], refs[VECTORS:]
    forward_steps(
        lines,
        vectors,
        weights_a,
        weights_b,
        weights_qkv,
        weights_proj,
        images_hbm,
        cot_hbm,
        counts_ref,
        labels_ref,
        levels_ref,
        class_table,
        noise_table,
        modw_table,
        modb_ref,
        *refs,
    )


def forward_steps(
    lines,
    vectors,
    weights_a,
    weights_b,
    weights_qkv,
    weights_proj,
    images_hbm,
    cot_hbm,
    counts_ref,
    labels_ref,
    levels_ref,
    class_table,
    noise_table,
    modw_table,
    modb_ref,
    whole_out,
    conv_out,
    slopes_out,
    turned_out,
    block_out,
    grad_out,
    low_out,
    right_out,
    vecs_ref,
    mod_ref,
    stats_ref,
    pre_ref,
    all_ids,
    sums_out,
    halves,
    whole_ref,
    vec_ref,
    ids_ref,
    class_ref,
    modw_ref,
    vec_all,
    mod_part,
    mod_got,
    act,
    act_f32,
    sums_ref,
    conv_ref,
    resid_ref,
    slopes,
    turned,
    attn_in,
    qkv,
    right,
    low,
    pair_ref,
    pair_send,
    pair_recv,
    pair_local,
    z_send,
    z_recv,
    p_send,
    x_send,
    x_recv,
    y_send,
    y_recv,
    s_send,
    s_recv,
    vec_send,
    vec_recv,
    ids_send,
    ids_recv,
    mod_send,
    mod_recv,
    unit_sem,
    flush_sem,
    in_sem,
    share_local,
    share_send,
    share_recv,
):
    z, y, x, c = place()
    d, h = lax.axis_index("dp"), lax.axis_index("head")
    n_dp, n_head = lines * 2, 4
    half = lines // 2
    inner = jnp.logical_and(z > 0, z < lines - 1)
    far = at_chip(lax.rem(3 * z + 1, lines), y, x, c)
    rows, cols_own = halves.shape[2:]
    wide = 2 * cols_own
    sibling = at_chip(z, y, x, 1 - c)
    along_x = at_chip(z, y, 1 - x, c)
    along_y = at_chip(z, 1 - y, x, c)
    line = [at_chip(lax.rem(z + k, lines), y, x, c) for k in range(1, lines)]
    column, heads = column_peers(n_dp), head_peers(n_head)
    greet(column + heads)

    def spot(i, cc, zz, yy, xx):
        return whole_ref.at[i, cc, zz, yy, :, span(xx, wide)]

    def parts_of(core):
        return (
            (weights_a.at[pl.ds(4 * core, 4)], pl.ds(0, 4)),
            (weights_b.at[pl.ds(4 * core, 4)], pl.ds(5, 4)),
            (weights_qkv.at[pl.ds(core, 1)], pl.ds(9, 1)),
        )

    last_parts = (
        ((weights_a.at[8], 4), (weights_qkv.at[2], 10)),
        ((weights_b.at[8], 4), (weights_proj, 10)),
    )

    def keep_copy(k):
        source, where = parts_of(c)[k]
        return pltpu.make_async_copy(source, halves.at[c, where], pair_local.at[k])

    def swap_copy(k):
        source, where = parts_of(1 - c)[k]
        return remote(source, halves.at[c, where], pair_send.at[k], pair_recv.at[k], sibling)

    def last_keep(core, k):
        source, where = last_parts[core][k]
        return pltpu.make_async_copy(source, halves.at[c, where], pair_local.at[3 + k])

    def last_swap(core, k):
        source, where = last_parts[core][k]
        return remote(source, halves.at[c, where], pair_send.at[3 + k], pair_recv.at[3 + k], sibling)

    def swap_start():
        for k in range(3):
            swap_copy(k).start()
            keep_copy(k).start()
        for core in range(2):

            @pl.when(c == core)
            def _():
                for k in range(2):
                    last_swap(1 - core, k).start()
                    last_keep(core, k).start()

    def swap_wait(k):
        if k < 3:
            keep_copy(k).wait()
            swap_copy(k).wait()
        else:
            last_keep(0, k - 3).wait()
            last_swap(0, k - 3).wait()

    def images_copy():
        return pltpu.make_async_copy(images_hbm, images_ref, in_sem.at[0])

    def cot_copy():
        return pltpu.make_async_copy(cot_hbm, cot_ref, in_sem.at[1])

    images_ref, cot_ref = attn_in, low

    def vec_copy(k):
        return remote(vec_ref, vec_all.at[h], vec_send.at[k], vec_recv.at[k], heads[k])

    def ids_copy(k):
        return remote(ids_ref, all_ids.at[d], ids_send.at[k], ids_recv.at[k], column[k])

    def mod_copy(k):
        return remote(
            mod_part.at[lax.rem(d + k + 1, n_dp)], mod_got.at[d], mod_send.at[k], mod_recv.at[k], column[k]
        )

    def z_part(i, zz):
        if isinstance(i, int) and i >= FAR:
            return whole_ref.at[i, c, zz]
        return spot(i, c, zz, y, x)

    def z_copy(i, k):
        ref = z_part(i, z)
        return remote(ref, ref, z_send.at[i, k], z_recv.at[i, k], line[k])

    def z_pass(i):
        ref = z_part(i, lax.rem(z + 2, lines))
        return remote(ref, ref, p_send.at[i], z_recv.at[i, lax.rem(2 * z + 2, lines)], far)

    def z_start(i):
        z_copy(i, 1).start()

        @pl.when(z != lines - 1)
        def _():
            z_copy(i, 0).start()

        @pl.when(z != 0)
        def _():
            z_copy(i, 2).start()

    def z_relay(i):
        z_copy(i, 1).wait_recv()

        @pl.when(inner)
        def _():
            z_pass(i).start()

    def z_finish(i):
        z_copy(i, 0).wait_recv()
        z_copy(i, 2).wait_recv()

    def z_drain(i):
        z_copy(i, 1).wait_send()

        @pl.when(z != lines - 1)
        def _():
            z_copy(i, 0).wait_send()

        @pl.when(z != 0)
        def _():
            z_copy(i, 2).wait_send()

        @pl.when(inner)
        def _():
            z_pass(i).wait_send()

    def x_copy(i, part):
        if isinstance(i, int) and i >= FAR:
            ref = spot(i, c, z, y, x) if part == 0 else spot(i, c, z, 1 - y, x).at[pl.ds(rows // 2, rows // 2)]
        elif part == 0:
            ref = spot(i, c, slice(None), y, x)
        else:
            ref = spot(i, c, pl.ds(half, half), 1 - y, x)
        return remote(ref, ref, x_send.at[i, part], x_recv.at[i, part], along_x)

    def y_copy(i, part):
        if isinstance(i, int) and i >= FAR:
            ref = spot(i, c, z, y, x) if part == 0 else spot(i, c, z, y, 1 - x).at[pl.ds(0, rows // 2)]
        elif part == 0:
            ref = spot(i, c, slice(None), y, x)
        else:
            ref = spot(i, c, pl.ds(0, half), y, 1 - x)
        return remote(ref, ref, y_send.at[i, part], y_recv.at[i, part], along_y)

    def s_copy(i, part):
        if isinstance(i, int) and i >= FAR:
            ref = whole_ref.at[i, c, part]
        else:
            yy, xx = ((y, x), (y, 1 - x), (1 - y, x), (1 - y, 1 - x))[part]
            ref = spot(i, c, slice(None), yy, xx)
        return remote(ref, ref, s_send.at[i, part], s_recv.at[i, part], sibling)

    def join(i):
        whole_ref[i, c, z, y, :, span(x, wide)] = jnp.concatenate([halves[0, i], halves[1, i]], axis=-1)

    def begin(i):
        join(i)
        z_start(i)

    def far_begin(i):
        x_copy(i, 0).start()
        y_copy(i, 0).start()

    def far_pass(i):
        x_copy(i, 0).wait_recv()
        y_copy(i, 1).start()
        y_copy(i, 0).wait_recv()
        x_copy(i, 1).start()

    def far_line(i):
        x_copy(i, 1).wait_recv()
        y_copy(i, 1).wait_recv()
        z_start(i)

    def far_finish(i):
        z_finish(i)
        for part in range(lines):
            s_copy(i, part).start()

    def spread_line(i):
        z_finish(i)
        x_copy(i, 0).start()
        y_copy(i, 0).start()
        s_copy(i, 0).start()

    def pass_on(i):
        x_copy(i, 0).wait_recv()
        y_copy(i, 1).start()
        s_copy(i, 1).start()
        y_copy(i, 0).wait_recv()
        x_copy(i, 1).start()
        s_copy(i, 2).start()

    def finish(i):
        x_copy(i, 1).wait_recv()
        y_copy(i, 1).wait_recv()
        s_copy(i, 3).start()

    def arrived(i):
        for part in range(4):
            s_copy(i, part).wait_recv()

    def unit_copy(i):
        return pltpu.make_async_copy(whole_ref.at[i], whole_out.at[i], unit_sem.at[i])

    def fetch(i):
        arrived(i)
        if not isinstance(i, int) or i < FAR:
            unit_copy(i).start()

    def product(total, tap, i, k):
        for n in range(CHUNKS):
            value = dot(act[tap % 3, lines_from(tap // 3)], weight_cols(whole_ref.at[i, k], n))
            total[:, :, :, chunk(n)] += value.reshape(RES, SLOTS, RES, WIDTH)

    def use_pair(total, i, first):
        each(2, lambda k: product(total, i - first + 4 * k, i, k))

    flushed = (
        (conv_ref, conv_out),
        (slopes.at[0], slopes_out.at[0]),
        (slopes.at[1], slopes_out.at[1]),
        (low, block_out),
        (conv_ref, grad_out),
        (attn_in, low_out),
    )

    def share_parts(k):
        if k < 4:
            return turned.at[k], turned_out.at[k, :, span(c, ALL)]
        part = (3, 1 - c, 2)[k - 4]
        return right.at[part], right_out.at[part, span(c, ALL)]

    def share_give(k):
        return remote(*share_parts(k), share_send.at[k], share_recv.at[k], sibling)

    def right_keep(k):
        return pltpu.make_async_copy(right.at[k], right_out.at[k, span(c, ALL)], share_local.at[4 + k])

    def turned_keep(k):
        return pltpu.make_async_copy(*share_parts(k), share_local.at[k])

    def share_if(k, giving, run):
        if k in (1, 4, 6):
            taker = 0 if k == 6 else 1
            pl.when(c == (1 - taker if giving else taker))(run)
        else:
            run()

    def share(k):
        share_if(k, True, lambda: share_give(k).start())

    def share_wait():
        for k in range(7):
            share_if(k, True, lambda k=k: share_give(k).wait_send())
            share_if(k, False, lambda k=k: share_give(k).wait_recv())
        for k in range(4):
            turned_keep(k).wait()
            right_keep(k).wait()

    def flush(k):
        return pltpu.make_async_copy(*flushed[k], flush_sem.at[k])

    def set_act(place_t):
        def by_line(yy):
            value = act_f32[yy].reshape(LINE, C)
            left, right = shifted(value)
            spot_rows = pl.ds(pl.multiple_of((yy + 1) * LINE, LINE), LINE)
            act[0, spot_rows] = left.astype(BF16)
            act[1, spot_rows] = value.astype(BF16)
            act[2, spot_rows] = right.astype(BF16)

        each(RES, by_line)

        def turn(yy):
            value = act_f32[pl.ds(2 * yy, 2)].reshape(2 * LINE, C)
            turned[place_t, :, span(yy, 2 * LINE)] = value.T.astype(BF16)

        each(RES // 2, turn)

    def activate(which, n, value):
        sigma = jax.nn.sigmoid(value)
        act_f32[:, n] = (value * sigma).reshape(RES, RES, C)
        slopes[which, :, n] = (sigma * (1.0 + value * (1.0 - sigma))).reshape(RES, RES, C)

    def norm_a():
        for k in range(n_head - 1):
            vec_copy(k).wait()
        vecs_ref[...] = jnp.concatenate([vec_all[k].astype(F32) for k in range(n_head)], axis=-1)

        images_copy().wait()

        def get(n):
            return images_ref[span(n, PIX)].astype(F32)

        mean, inverse = stats_ref.at[0], stats_ref.at[1]
        norm_stats(get, mean, inverse, sums_ref)

        def to_act(n):
            value = (get(n) - mean[row(n)]) * inverse[row(n)]
            activate(0, n, value * vecs_ref[0:1] + vecs_ref[1:2])
            conv_ref[:, n] = jnp.broadcast_to(vecs_ref[2:3].reshape(1, 1, C), (RES, RES, C))
            resid_ref[:, n] = (get(n) + vecs_ref[5:6]).reshape(RES, RES, C)

        each(SLOTS, to_act)
        set_act(3)
        flush(1).start()
        turned_keep(3).start()
        share(3)

    def embed():
        for k in range(n_dp - 1):
            ids_copy(k).wait()
        ids = all_ids[...].reshape(n_dp * SLOTS, 128)
        table = class_ref.shape[1]
        label_hot = lax.broadcasted_iota(jnp.int32, (n_dp * SLOTS, table), 1) == ids[:, 0:1]
        levels = noise_table.shape[0]
        level_hot = lax.broadcasted_iota(jnp.int32, (n_dp * SLOTS, levels), 1) == ids[:, 1:2]
        pre = dot_nt(jnp.where(label_hot, 1.0, 0.0).astype(BF16), class_ref[...])
        width = class_table.shape[0]
        place_of = lax.broadcasted_iota(jnp.int32, (C, 128), 0) - d * width
        lane = lax.broadcasted_iota(jnp.int32, (C, 128), 1)
        chosen = jnp.logical_and(place_of == lane, lane < width)
        noise = dot(noise_table[...], jnp.where(chosen, 1.0, 0.0).astype(BF16)).astype(BF16)
        pre += dot(jnp.where(level_hot, 1.0, 0.0).astype(BF16), noise)
        pre_ref[...] = pre
        part = dot(silu(pre).astype(BF16), modw_ref[...])
        for k in range(n_dp):
            mine = part[k * SLOTS : (k + 1) * SLOTS]
            mod_part[k] = jnp.concatenate([mine[:, :C], mine[:, C:]], axis=0).astype(BF16)
        mod_got[d] = mod_part[d]
        for k in range(n_dp - 1):
            mod_copy(k).start()

    def norm_b():
        for k in range(n_dp - 1):
            mod_copy(k).wait()
        bias = modb_ref[...].astype(F32)
        total = jnp.concatenate([jnp.broadcast_to(bias[k : k + 1], (SLOTS, C)) for k in range(2)], axis=0)
        for k in range(n_dp):
            total += mod_got[k].astype(F32)
        mod_ref[...] = total.astype(BF16).astype(F32)

        def get(n):
            return conv_ref[:, n].reshape(PIX, C)

        mean, inverse = stats_ref.at[2], stats_ref.at[3]
        norm_stats(get, mean, inverse, sums_ref)

        def to_act(n):
            value = (get(n) - mean[row(n)]) * inverse[row(n)]
            value = value * vecs_ref[3:4] + vecs_ref[4:5]
            value = mod_ref[row(SLOTS + n)] + value * (mod_ref[row(n)] + 1.0)
            activate(1, n, value)

        each(SLOTS, to_act)
        set_act(2)
        flush(0).start()
        flush(2).start()
        turned_keep(2).start()
        share(2)

    def residual(n):
        return resid_ref[:, n].reshape(PIX, C)

    def normed(n):
        return (residual(n) - stats_ref[4, row(n)]) * stats_ref[5, row(n)]

    def transpose_out(source, place_t):
        def turn(k):
            value = source[span(k, 2 * LINE)].astype(F32)
            turned[place_t, :, span(k, 2 * LINE)] = value.T.astype(BF16)

        each(ALL // (2 * LINE), turn)

    def live(n):
        slots = counts_ref[0, d * n_head + h] + counts_ref[1, d * n_head + h]
        return jnp.where(n < slots, 1.0, 0.0)

    def norm_c():
        cot_copy().wait()
        norm_stats(residual, stats_ref.at[4], stats_ref.at[5], sums_ref)
        sums_out[...] = jnp.zeros_like(sums_out)

        def prepare(n):
            attn_in[span(n, PIX)] = (normed(n) * vecs_ref[6:7] + vecs_ref[7:8]).astype(BF16)
            grad = cot_ref[span(n, PIX)].astype(F32) * live(n)
            right[3, span(n, PIX)] = grad.astype(BF16)
            sums_out[8:9] += sum_rows(grad)

        each(SLOTS, prepare)
        transpose_out(attn_in, 0)
        turned_keep(0).start()
        right_keep(3).start()
        share(0)
        share(4)

    def attention():
        unit = tuple(whole_ref.at[9 + t // 2, t % 2] for t in range(4))
        for t in range(4):
            for n in range(CHUNKS):
                if t < 3:
                    value = dot(attn_in[...], weight_cols(unit[t], n))
                else:
                    value = dot_nt(right[3], weight_rows(unit[3], n))
                qkv[t, :, chunk(n)] = value.astype(BF16)
        factor = DH ** (-0.5)
        band = lax.broadcasted_iota(jnp.int32, (PIX, BAND), 1) // DH
        heads_at_once = BAND // DH

        def stack(value):
            zero = jnp.zeros_like(value)
            return jnp.concatenate([jnp.where(band == k, value, zero) for k in range(heads_at_once)], axis=0)

        def pick(value):
            out = value[:PIX]
            for k in range(1, heads_at_once):
                out = jnp.where(band == k, value[k * PIX : (k + 1) * PIX], out)
            return out

        def attend(n):
            for b in range(C // BAND):
                query, key, value, grad = (qkv[t, span(n, PIX), slice(b * BAND, (b + 1) * BAND)] for t in range(4))
                query4, grad4 = stack(query), stack(grad)
                scores = dot_nt(key, query4) * factor
                weight = jnp.exp(scores - jnp.max(scores, axis=0, keepdims=True))
                probs = weight / jnp.sum(weight, axis=0, keepdims=True)
                probs_low = probs.astype(BF16)
                low[span(n, PIX), slice(b * BAND, (b + 1) * BAND)] = pick(dot_tn(probs_low, value)).astype(BF16)
                grad_probs = dot_nt(value, grad4)
                inner_sum = jnp.sum(grad_probs * probs, axis=0, keepdims=True)
                grad_scores = (probs * (grad_probs - inner_sum)).astype(BF16)
                right[0, span(n, PIX), slice(b * BAND, (b + 1) * BAND)] = (pick(dot_tn(grad_scores, key)) * factor).astype(BF16)
                right[1, span(n, PIX), slice(b * BAND, (b + 1) * BAND)] = (dot(grad_scores, query4) * factor).astype(BF16)
                right[2, span(n, PIX), slice(b * BAND, (b + 1) * BAND)] = dot(probs_low, grad4).astype(BF16)

        def attend_two(m):
            attend(2 * m)
            attend(2 * m + 1)

        each(SLOTS // 2, attend_two)
        share(5)
        share(6)
        for k in range(3):
            right_keep(k).start()
        transpose_out(low, 1)
        turned_keep(1).start()
        share(1)
        for n in range(CHUNKS):
            value = dot_nt(right[0], weight_rows(unit[0], n))
            value += dot_nt(right[1], weight_rows(unit[1], n))
            value += dot_nt(right[2], weight_rows(unit[2], n))
            act_f32[:, :, :, chunk(n)] = value.reshape(SLOTS, RES, RES, WIDTH)

        def back(n):
            grad = act_f32[n].reshape(PIX, C)
            pair_ref[row(n)] = sum_rows(grad * normed(n))
            pair_ref[row(SLOTS + n)] = sum_rows(grad)

        each(SLOTS, back)
        sums_out[6:7] = sum_rows(pair_ref[0:SLOTS])
        sums_out[7:8] = sum_rows(pair_ref[SLOTS:])
        pair_ref[...] = group_mean(pair_ref[...] * vecs_ref[6:7])

        def back_second(n):
            inverse = stats_ref[5, row(n)]
            value = act_f32[n].reshape(PIX, C) * (vecs_ref[6:7] * inverse)
            value -= normed(n) * (pair_ref[row(n)] * inverse) + pair_ref[row(SLOTS + n)] * inverse
            value += right[3, span(n, PIX)].astype(F32)
            conv_ref[:, n] = value.reshape(RES, RES, C)
            sums_out[5:6] += sum_rows(value.astype(BF16).astype(F32))

        flush(0).wait()
        each(SLOTS, back_second)
        flush(4).start()

        def lower(yy):
            attn_in[span(yy, LINE)] = conv_ref[yy].reshape(LINE, C).astype(BF16)

        each(RES, lower)
        flush(5).start()
        for n in range(CHUNKS):
            value = dot(low[...], weight_cols(unit[3], n))
            act_f32[:, :, :, chunk(n)] = value.reshape(SLOTS, RES, RES, WIDTH)

        def finish_out(n):
            value = residual(n) + act_f32[n].reshape(PIX, C) + vecs_ref[8:9]
            low[span(n, PIX)] = (value * live(n)).astype(BF16)

        each(SLOTS, finish_out)
        flush(3).start()

    swap_start()
    images_copy().start()
    cot_copy().start()
    one = [ref[...].astype(F32).reshape(1, cols_own) for ref in vectors]
    vec_ref[...] = jnp.concatenate(one + [jnp.zeros((16 - VECTORS, cols_own), F32)], axis=0).astype(BF16)
    lane = lax.broadcasted_iota(jnp.int32, (1, 128), 1)
    for n in range(SLOTS):
        ids_ref[n : n + 1] = jnp.where(lane == 0, labels_ref[n], levels_ref[n])
    for k in range(n_head - 1):
        vec_copy(k).start()
    for k in range(n_dp - 1):
        ids_copy(k).start()
    width = class_table.shape[0]
    class_ref[...] = jnp.zeros_like(class_ref)
    class_ref[0:width, 0 : class_table.shape[1]] = class_table[...]
    modw_ref[...] = jnp.zeros_like(modw_ref)
    table = modw_table[...].astype(F32)
    for k in range(2):
        modw_ref[0:width, k * C : (k + 1) * C] = table[:, k].astype(BF16)
    vec_all[h] = vec_ref[...]
    all_ids[d] = ids_ref[...]
    edge = jnp.zeros((LINE, C), BF16)
    for j in range(3):
        act[j, 0:LINE] = edge
        act[j, ALL + LINE : ALL + 2 * LINE] = edge
    swap_wait(0)
    begin(0)
    for k in range(1, 5):
        swap_wait(k)
    for i in (10, 9):
        join(i)
        far_begin(i)
    begin(1)
    z_relay(0)
    begin(2)
    spread_line(0)
    for i in (10, 9):
        far_pass(i)
    begin(3)
    z_relay(1)
    norm_a()
    spread_line(1)
    pass_on(0)
    begin(4)
    z_relay(2)
    embed()
    spread_line(2)
    pass_on(1)
    finish(0)
    begin(5)
    z_relay(3)
    begin(6)
    z_relay(4)
    far_line(10)
    spread_line(3)
    pass_on(2)
    finish(1)
    fetch(0)

    def body(turn, carry):
        @pl.when(turn < 6)
        def _():
            begin(turn + 3)

        @pl.when(turn == 6)
        def _():
            far_line(9)
            z_relay(10)

        z_relay(turn + 1)
        spread_line(turn)
        pass_on(turn - 1)
        finish(turn - 2)
        fetch(turn - 3)
        use_pair(conv_ref, turn - 4, 0)
        return carry

    lax.fori_loop(4, 8, body, 0)
    spread_line(8)
    pass_on(7)
    finish(6)
    fetch(5)
    product(conv_ref, 8, 4, 0)
    norm_b()
    product(resid_ref, 8, 4, 1)
    pass_on(8)
    finish(7)
    z_relay(9)
    fetch(6)
    far_finish(10)
    use_pair(resid_ref, 5, 5)
    finish(8)
    fetch(7)
    use_pair(resid_ref, 6, 5)
    fetch(8)
    use_pair(resid_ref, 7, 5)
    far_finish(9)
    use_pair(resid_ref, 8, 5)
    norm_c()
    fetch(9)
    fetch(10)
    attention()

    def drain(i):
        z_drain(i)
        for part in range(2):
            x_copy(i, part).wait_send()
            y_copy(i, part).wait_send()
        for part in range(4):
            s_copy(i, part).wait_send()

    each(FAR, drain)
    drain(9)
    drain(10)
    for k in range(1, len(flushed)):
        flush(k).wait()
    each(FAR, lambda i: unit_copy(i).wait())
    share_wait()


def run_forward(weights, images, cotangent, counts, labels, levels, class_table, noise_table, modw, modb, vectors):
    n_dp, n_head = lax.axis_size("dp"), lax.axis_size("head")
    rows, cols = weights[0].shape[1:]
    lines, across, wide = n_dp // 2, n_head // 2, 2 * cols
    board = (RES, SLOTS, RES, C)
    shape = jax.ShapeDtypeStruct
    return pl.pallas_call(
        functools.partial(forward_kernel, lines),
        out_shape=(
            shape((FAR, 2, lines, 2, rows, across * wide), BF16),
            shape(board, F32),
            shape((2,) + board, F32),
            shape((4, C, 2 * ALL), BF16),
            shape((ALL, C), BF16),
            shape(board, F32),
            shape((ALL, C), BF16),
            shape((4, 2 * ALL, C), BF16),
            shape((16, C), F32),
            shape((2 * SLOTS, C), F32),
            shape((6, SLOTS, C), F32),
            shape((n_dp * SLOTS, 128), F32),
            shape((n_dp, SLOTS, 128), jnp.int32),
            shape((16, C), F32),
        ),
        in_specs=[ANY] * 6 + [SMEM] * 3 + [VMEM] * (4 + VECTORS),
        out_specs=(ANY,) * 8 + (VMEM,) * 6,
        scratch_shapes=[
            pltpu.VMEM((2, PAIRS, rows, cols), BF16),
            pltpu.VMEM((PAIRS, 2, lines, 2, rows, across * wide), BF16),
            pltpu.VMEM((16, cols), BF16),
            pltpu.VMEM((SLOTS, 128), jnp.int32),
            pltpu.VMEM((128, 1024), BF16),
            pltpu.VMEM((128, 2 * C), BF16),
            pltpu.VMEM((n_head, 16, cols), BF16),
            pltpu.VMEM((n_dp, 2 * SLOTS, C), BF16),
            pltpu.VMEM((n_dp, 2 * SLOTS, C), BF16),
            pltpu.VMEM((3, ALL + 2 * LINE, C), BF16),
            pltpu.VMEM(board, F32),
            pltpu.VMEM((SLOTS, C), F32),
            pltpu.VMEM(board, F32),
            pltpu.VMEM(board, F32),
            pltpu.VMEM((2,) + board, F32),
            pltpu.VMEM((4, C, ALL), BF16),
            pltpu.VMEM((ALL, C), BF16),
            pltpu.VMEM((4, ALL, C), BF16),
            pltpu.VMEM((4, ALL, C), BF16),
            pltpu.VMEM((ALL, C), BF16),
            pltpu.VMEM((2 * SLOTS, C), F32),
            DMA((5,)),
            DMA((5,)),
            DMA((5,)),
            DMA((PAIRS, lines - 1)),
            DMA((PAIRS, lines - 1)),
            DMA((PAIRS,)),
            DMA((PAIRS, 2)),
            DMA((PAIRS, 2)),
            DMA((PAIRS, 2)),
            DMA((PAIRS, 2)),
            DMA((PAIRS, 4)),
            DMA((PAIRS, 4)),
            DMA((n_head - 1,)),
            DMA((n_head - 1,)),
            DMA((n_dp - 1,)),
            DMA((n_dp - 1,)),
            DMA((n_dp - 1,)),
            DMA((n_dp - 1,)),
            DMA((FAR,)),
            DMA((6,)),
            DMA((2,)),
            DMA((8,)),
            DMA((7,)),
            DMA((7,)),
        ],
        compiler_params=pltpu.CompilerParams(
            collective_id=0, has_side_effects=True, vmem_limit_bytes=62 * 2**20
        ),
        name="gather_forward",
    )(
        *weights,
        images,
        cotangent,
        counts,
        labels,
        levels,
        class_table,
        noise_table,
        modw,
        modb,
        *vectors,
    )


BACK_FAR = (10, 8)
BACK_NEAR = tuple(i for i in range(PAIRS) if i not in BACK_FAR)
AHEAD = 3


def backward_kernel(
    lines,
    whole_ref,
    turned_ref,
    right_ref,
    grad_low_ref,
    grad_resid_ref,
    conv_ref,
    slopes_ref,
    images_hbm,
    stats_ref,
    vecs_ref,
    mod_ref,
    sums_in,
    pre_ref,
    ids_ref,
    modw_table,
    out_a,
    out_b,
    out_qkv,
    out_proj,
    image_ref,
    class_ref,
    modw_out,
    modb_out,
    vec_out,
    mine,
    from_x,
    from_y,
    from_z,
    far_x,
    far_y,
    far_z,
    ends,
    modw_ref,
    lefts,
    rights,
    grads,
    stage,
    stage_mine,
    weights,
    total,
    board,
    slopes,
    image_mine,
    images_ref,
    sums_ref,
    pair_ref,
    coef_ref,
    gm_mine,
    gm_all,
    mw_mine,
    mw_got,
    ge_all,
    vs_mine,
    vs_got,
    vt_mine,
    vt_all,
    x_send,
    x_recv,
    y_send,
    y_recv,
    z_send,
    z_recv,
    p_send,
    p_recv,
    e_send,
    e_recv,
    e_local,
    op_send,
    op_recv,
    op_local,
    load_sem,
    in_sem,
    out_sem,
    gm_send,
    gm_recv,
    mw_send,
    mw_recv,
    ge_send,
    ge_recv,
    vs_send,
    vs_recv,
    vt_send,
    vt_recv,
):
    z, y, x, c = place()
    d, h = lax.axis_index("dp"), lax.axis_index("head")
    n_dp, n_head = lines * 2, 4
    half = lines // 2
    inner = jnp.logical_and(z > 0, z < lines - 1)
    rows, wide = from_z.shape[2], from_z.shape[3]
    cols = wide // 2
    sibling = at_chip(z, y, x, 1 - c)
    along_x = at_chip(z, y, 1 - x, c)
    along_y = at_chip(z, 1 - y, x, c)
    line = [at_chip(lax.rem(z + k, lines), y, x, c) for k in range(1, lines)]
    column, heads = column_peers(n_dp), head_peers(n_head)

    own_rows = pl.ds(LINE, ALL)

    def op_own(k):
        source, place_of = (
            (right_ref.at[2 + c], rights.at[0]),
            (turned_ref.at[c], lefts.at[1]),
            (right_ref.at[c], rights.at[1]),
            (turned_ref.at[0], lefts.at[0]),
            (grad_low_ref, grads.at[1, c, own_rows]),
            (turned_ref.at[2], lefts.at[2]),
            (turned_ref.at[3], lefts.at[3]),
        )[k]
        return pltpu.make_async_copy(source, place_of, op_local.at[k])

    def low_copy():
        return remote(grad_low_ref, grads.at[1, c, own_rows], op_send.at[0], op_recv.at[0], sibling)

    def stage_copy():
        return remote(stage_mine, stage, op_send.at[1], op_recv.at[1], sibling)

    def lanes(xx):
        return span(xx, wide)

    first, second = pl.ds(0, rows // 2), pl.ds(rows // 2, rows // 2)

    def is_far(i):
        return i in BACK_FAR

    def x_copy(i, part):
        if is_far(i):
            into = far_x.at[BACK_FAR.index(i)]
            if part == 0:
                src, dst = mine.at[i, z, 1 - y, second, lanes(1 - x)], into.at[pl.ds(rows, rows // 2)]
            else:
                src, dst = mine.at[i, z, y, :, lanes(1 - x)], into.at[pl.ds(0, rows)]
        elif part == 0:
            src, dst = mine.at[i, pl.ds(half, half), 1 - y, :, lanes(1 - x)], from_x.at[BACK_NEAR.index(i), pl.ds(lines, half)]
        else:
            src, dst = mine.at[i, :, y, :, lanes(1 - x)], from_x.at[BACK_NEAR.index(i), pl.ds(0, lines)]
        return remote(src, dst, x_send.at[i, part], x_recv.at[i, part], along_x)

    def y_copy(i, part):
        if is_far(i):
            into = far_y.at[BACK_FAR.index(i)]
            if part == 0:
                src, dst = mine.at[i, z, 1 - y, first, lanes(1 - x)], into.at[pl.ds(rows, rows // 2)]
            else:
                src, dst = mine.at[i, z, 1 - y, :, lanes(x)], into.at[pl.ds(0, rows)]
        elif part == 0:
            src, dst = mine.at[i, pl.ds(0, half), 1 - y, :, lanes(1 - x)], from_y.at[BACK_NEAR.index(i), pl.ds(lines, half)]
        else:
            src, dst = mine.at[i, :, 1 - y, :, lanes(x)], from_y.at[BACK_NEAR.index(i), pl.ds(0, lines)]
        return remote(src, dst, y_send.at[i, part], y_recv.at[i, part], along_y)

    beyond = lax.rem(z + 2, lines)
    opposite = lines - 1 - z
    near_end = at_chip(1 + z // (lines - 1), y, x, c)

    def z_block(i, zz):
        return mine.at[i, zz] if is_far(i) else mine.at[i, zz, y, :, lanes(x)]

    def z_slot(i, k):
        return far_z.at[BACK_FAR.index(i), k] if is_far(i) else from_z.at[BACK_NEAR.index(i), k]

    def z_copy(i, k):
        return remote(
            z_block(i, lax.rem(z + k + 1, lines)), z_slot(i, k), z_send.at[i, k], z_recv.at[i, k], line[k]
        )

    def z_give(i):
        return remote(z_block(i, opposite), z_slot(i, 3), p_send.at[i], p_recv.at[i], near_end)

    def z_start(i):
        @pl.when(jnp.logical_not(inner))
        def _():
            z_give(i).start()

        @pl.when(z < lines - 1)
        def _():
            z_copy(i, 0).start()

        @pl.when(z > 0)
        def _():
            z_copy(i, 2).start()

        @pl.when(jnp.logical_not(inner))
        def _():
            z_copy(i, 1).start()

    def z_mix(i):
        @pl.when(inner)
        def _():
            z_give(i).wait_recv()
            if is_far(i):
                mine[i, beyond] += far_z[BACK_FAR.index(i), 3]
            else:
                mine[i, beyond, y, :, lanes(x)] += from_z[BACK_NEAR.index(i), 3]
            z_copy(i, 1).start()

    def z_wait(i):
        z_copy(i, 1).wait_recv()

        @pl.when(z > 0)
        def _():
            z_copy(i, 0).wait_recv()

        @pl.when(z < lines - 1)
        def _():
            z_copy(i, 2).wait_recv()

    def z_drain(i):
        z_copy(i, 1).wait_send()

        @pl.when(z < lines - 1)
        def _():
            z_copy(i, 0).wait_send()

        @pl.when(z > 0)
        def _():
            z_copy(i, 2).wait_send()

        @pl.when(jnp.logical_not(inner))
        def _():
            z_give(i).wait_send()

    def target(i, core):
        if isinstance(i, int) and i == 10:
            return out_proj if core == 1 else out_qkv.at[2]
        if isinstance(i, int) and i == 9:
            return out_qkv.at[core]
        if isinstance(i, int) and i == 4:
            return out_b.at[8] if core == 1 else out_a.at[8]
        if isinstance(i, int) and i > 4:
            return out_b.at[4 * core + i - 5]
        return out_a.at[4 * core + i]

    def e_copy(i, core):
        return remote(ends.at[1 - c, i], target(i, core), e_send.at[i], e_recv.at[i], sibling)

    def e_own(i, core):
        return pltpu.make_async_copy(ends.at[c, i], target(i, core), e_local.at[i])

    def finish(i, value):
        for cc in range(2):
            ends[cc, i] = value[:, cc * cols : (cc + 1) * cols]
        if i in (4, 10):
            for core in range(2):

                @pl.when(c == core)
                def _():
                    e_copy(i, core).start()
                    e_own(i, core).start()
        else:
            e_copy(i, c).start()
            e_own(i, c).start()

    def offer(i):
        x_copy(i, 0).start()
        y_copy(i, 0).start()

    def relay(i):
        x_copy(i, 0).wait_recv()
        y_copy(i, 0).wait_recv()
        if is_far(i):
            rest = pl.ds(rows, rows // 2)
            mine[i, z, y, first, lanes(1 - x)] += far_y[BACK_FAR.index(i), rest]
            mine[i, z, 1 - y, second, lanes(x)] += far_x[BACK_FAR.index(i), rest]
        else:
            for j in range(half):
                mine[i, j, y, :, lanes(1 - x)] += from_y[BACK_NEAR.index(i), lines + j]
                mine[i, half + j, 1 - y, :, lanes(x)] += from_x[BACK_NEAR.index(i), lines + j]
        x_copy(i, 1).start()
        y_copy(i, 1).start()

    def collect(i):
        x_copy(i, 1).wait_recv()
        y_copy(i, 1).wait_recv()
        if is_far(i):
            whole_rows = pl.ds(0, rows)
            value = mine[i, z, y, :, lanes(x)].astype(F32)
            value += far_x[BACK_FAR.index(i), whole_rows].astype(F32) + far_y[BACK_FAR.index(i), whole_rows].astype(F32)
            finish(i, value)
            return

        def add(j):
            value = mine[i, j, y, :, lanes(x)].astype(F32)
            value += from_x[BACK_NEAR.index(i), j].astype(F32) + from_y[BACK_NEAR.index(i), j].astype(F32)
            mine[i, j, y, :, lanes(x)] = value.astype(BF16)

        each(lines, add)
        z_start(i)

    def last(i):
        z_wait(i)
        if is_far(i):
            for yy in range(2):
                value = mine[i, z, yy].astype(F32)
                for k in range(lines - 1):
                    value += far_z[BACK_FAR.index(i), k, yy].astype(F32)
                mine[i, z, yy] = value.astype(BF16)
            offer(i)
            return
        value = mine[i, z, y, :, lanes(x)].astype(F32)
        for k in range(lines - 1):
            value += from_z[BACK_NEAR.index(i), k].astype(F32)
        finish(i, value)

    def put(i, n, value):
        mine[i, :, :, :, chunk(n)] = value.astype(BF16).reshape(mine.shape[1:4] + (WIDTH,))

    def plain_unit(i, left, right):
        for n in range(CHUNKS):
            put(i, n, dot(lefts[left], rights[right, :, chunk(n)]))

    def conv_unit(i, left, tap):
        where, side = lines_from(2 - tap // 3), 2 - tap % 3
        for n in range(CHUNKS):
            both = jnp.concatenate([grads[side, core, where, chunk(n)] for core in range(2)], axis=0)
            put(i, n, dot(lefts[left], both))

    def extra_b():
        @pl.when(c == 1)
        def _():
            conv_unit(4, 2, 8)

    def extra_a():
        @pl.when(c == 0)
        def _():
            conv_unit(4, 3, 8)

    def spread_sides(core):
        def by_line(yy):
            value = grads[1, core, pl.ds(pl.multiple_of((yy + 1) * LINE, LINE), LINE)].astype(F32)
            left, right = shifted(value)
            spot_rows = pl.ds(pl.multiple_of((yy + 1) * LINE, LINE), LINE)
            grads[0, core, spot_rows] = left.astype(BF16)
            grads[2, core, spot_rows] = right.astype(BF16)

        each(RES, by_line)

    def load(tap, base):
        ninth = tap // 8
        i = (base // 2 + tap % 4) * (1 - ninth) + 4 * ninth
        k = (tap // 4) % 2 + (base // 10) * ninth
        return pltpu.make_async_copy(whole_ref.at[i, k], weights.at[tap % (AHEAD + 1)], load_sem.at[tap % (AHEAD + 1)])

    def conv_back(tap, base):
        load(tap, base).wait()

        @pl.when(tap < 9 - AHEAD)
        def _():
            load(tap + AHEAD, base).start()

        part = grads[2 - tap % 3, c, lines_from(2 - tap // 3)]
        for n in range(CHUNKS):
            value = dot_nt(part, weight_rows(weights.at[tap % (AHEAD + 1)], n))
            total[:, :, :, chunk(n)] += value.reshape(RES, SLOTS, RES, WIDTH)

    def conv_back_range(first, stop, base):
        def body(tap, carry):
            conv_back(tap, base)
            return carry

        lax.fori_loop(first, stop, body, 0)

    def slope(values):
        sigma = jax.nn.sigmoid(values)
        return sigma * (1.0 + values * (1.0 - sigma))

    for k in (0, 2):
        from_z[:, k] = jnp.zeros_like(from_z[:, k])
        far_z[:, k] = jnp.zeros_like(far_z[:, k])
    greet(column + heads)
    low_copy().start()
    for k in (4, 0, 1, 2, 3, 5):
        op_own(k).start()
    for tap in range(AHEAD):
        load(tap, 10).start()

    def fetch(k):
        source, target = (
            (conv_ref, board),
            (slopes_ref.at[1], slopes),
            (slopes_ref.at[0], slopes),
            (grad_resid_ref, board),
            (images_hbm, images_ref),
        )[k]
        return pltpu.make_async_copy(source, target, in_sem.at[k])

    fetch(0).start()
    fetch(1).start()
    vs_mine[...] = jnp.zeros_like(vs_mine)
    edge = jnp.zeros((LINE, C), BF16)
    for j in range(3):
        for core in range(2):
            grads[j, core, 0:LINE] = edge
            grads[j, core, ALL + LINE : ALL + 2 * LINE] = edge
    total[...] = jnp.zeros_like(total)
    sums_ref[...] = sums_in[...]
    modw_ref[...] = jnp.zeros_like(modw_ref)
    table = modw_table[...].astype(F32)
    for k in range(2):
        modw_ref[0:rows, k * C : (k + 1) * C] = table[:, k].astype(BF16)

    def norm_b_value(n):
        return (board[:, n].reshape(PIX, C) - stats_ref[2, row(n)]) * stats_ref[3, row(n)]

    def norm_a_value(n):
        return (images_ref[span(n, PIX)].astype(F32) - stats_ref[0, row(n)]) * stats_ref[1, row(n)]

    def back_sums(get):
        def body(n):
            grad = (total[:, n] * slopes[:, n]).reshape(PIX, C)
            total[:, n] = grad.reshape(RES, RES, C)
            pair_ref[row(n)] = sum_rows(grad * get(n))
            pair_ref[row(SLOTS + n)] = sum_rows(grad)

        each(SLOTS, body)

    def back_factors(factor, inverse):
        coef_ref[0:SLOTS] = factor * inverse
        means = group_mean(pair_ref[...] * jnp.concatenate([factor, factor], axis=0))
        coef_ref[SLOTS : 2 * SLOTS] = means[:SLOTS] * inverse
        coef_ref[2 * SLOTS :] = means[SLOTS:] * inverse

    def back_value(n, get):
        value = total[:, n].reshape(PIX, C) * coef_ref[row(n)]
        return value - get(n) * coef_ref[row(SLOTS + n)] - coef_ref[row(2 * SLOTS + n)]

    def gm_copy(k):
        return remote(gm_mine, gm_all.at[d], gm_send.at[k], gm_recv.at[k], column[k])

    def mw_copy(k):
        return remote(
            mw_mine.at[lax.rem(h + k + 1, n_head)], mw_got.at[k], mw_send.at[k], mw_recv.at[k], heads[k]
        )

    def ge_copy(k):
        return remote(ge_all.at[h], ge_all.at[h], ge_send.at[k], ge_recv.at[k], heads[k])

    def vs_copy(k):
        return remote(
            vs_mine.at[lax.rem(h + k + 1, n_head)], vs_got.at[k], vs_send.at[k], vs_recv.at[k], heads[k]
        )

    def vt_copy(k):
        return remote(vt_mine, vt_all.at[d], vt_send.at[k], vt_recv.at[k], column[k])

    def image_copy():
        return pltpu.make_async_copy(image_mine, image_ref, out_sem)

    count = n_dp * SLOTS

    def start():
        op_own(0).wait()
        op_own(1).wait()

    def dw(i):
        if i == 10:
            plain_unit(10, 1, 0)
        elif i == 9:
            op_own(2).wait()
            op_own(3).wait()
            plain_unit(9, 0, 1)
        elif i > 4:
            conv_unit(i, 2, 4 * c + i - 5)
        else:
            conv_unit(i, 3, 4 * c + i)

    def sides():
        op_own(4).wait()
        low_copy().wait_recv()
        op_own(5).wait()
        spread_sides(0)
        spread_sides(1)

    def back_b_first():
        for tap in range(AHEAD):
            load(tap, 0).start()
        op_own(6).start()
        fetch(0).wait()
        fetch(1).wait()
        back_sums(norm_b_value)
        alone, with_norm = pair_ref[SLOTS:], pair_ref[:SLOTS]
        scale = mod_ref[0:SLOTS] + 1.0
        gm_mine[...] = jnp.concatenate([vecs_ref[3:4] * with_norm + vecs_ref[4:5] * alone, alone], axis=0).astype(BF16)
        gm_all[d] = gm_mine[...]
        for k in range(n_dp - 1):
            gm_copy(k).start()
        sums_ref[3:4] = sum_rows(with_norm * scale)
        sums_ref[4:5] = sum_rows(alone * scale)
        back_factors(scale * vecs_ref[3:4], stats_ref[3])

    def back_b_second():
        fetch(2).start()
        fetch(4).start()

        def body(n):
            value = back_value(n, norm_b_value).astype(BF16).astype(F32)
            sums_ref[2:3] += sum_rows(value)
            total[:, n] = value.reshape(RES, RES, C)

        each(SLOTS, body)
        fetch(3).start()

    def lower():
        def by_line(yy):
            stage_mine[span(yy, LINE)] = total[yy].reshape(LINE, C).astype(BF16)

        each(RES, by_line)
        stage_copy().start()
        total[...] = jnp.zeros_like(total)

    def take():
        stage_copy().wait_recv()

        def by_line(yy):
            spot_rows = pl.ds(pl.multiple_of((yy + 1) * LINE, LINE), LINE)
            grads[1, c, spot_rows] = stage_mine[span(yy, LINE)]
            grads[1, 1 - c, spot_rows] = stage[span(yy, LINE)]

        each(RES, by_line)
        spread_sides(0)
        spread_sides(1)
        op_own(6).wait()

    def modulation():
        for k in range(n_dp - 1):
            gm_copy(k).wait()
        parts = gm_all[...].astype(F32)
        gm_scale = parts[:, :SLOTS].reshape(count, C)
        gm_offset = parts[:, SLOTS:].reshape(count, C)
        pre = pre_ref[...]
        emb = silu(pre).astype(BF16)
        part_rows = rows // n_head
        for k, value in ((0, gm_scale), (1, gm_offset)):
            low_value = value.astype(BF16)
            grad_w = dot_tn(emb, low_value)
            place_lanes = slice(k * C, (k + 1) * C)
            for hh in range(n_head):
                mw_mine[hh, 0:part_rows, place_lanes] = grad_w[hh * part_rows : (hh + 1) * part_rows]
                mw_mine[hh, part_rows : part_rows + 8, place_lanes] = jnp.broadcast_to(sum_rows(value), (8, C))
        grad_e = dot_nt(gm_scale.astype(BF16), modw_ref[:, :C]) + dot_nt(gm_offset.astype(BF16), modw_ref[:, C:])
        grad_e = grad_e * slope(pre)
        label = ids_ref[...].reshape(count, 128)[:, 0:1].astype(F32)
        lane = lax.broadcasted_iota(jnp.int32, grad_e.shape, 1)
        ge_all[h] = jnp.where(lane < rows, grad_e, label)
        for k in range(n_head - 1):
            mw_copy(k).start()
            ge_copy(k).start()

    def back_a_first():
        fetch(2).wait()
        fetch(4).wait()
        back_sums(norm_a_value)
        sums_ref[0:1] = sum_rows(pair_ref[:SLOTS])
        sums_ref[1:2] = sum_rows(pair_ref[SLOTS:])
        for hh in range(n_head):
            vs_mine[hh] = sums_ref[:, hh * cols : (hh + 1) * cols]
        for k in range(n_head - 1):
            vs_copy(k).start()
        back_factors(jnp.broadcast_to(vecs_ref[0:1], (SLOTS, C)), stats_ref[1])

    def back_a_second():
        fetch(3).wait()

        def body(n):
            image_mine[span(n, PIX)] = back_value(n, norm_a_value) + board[:, n].reshape(PIX, C)

        each(SLOTS, body)
        image_copy().start()

    def vec_first():
        value = vs_mine[h]
        for k in range(n_head - 1):
            vs_copy(k).wait()
            value += vs_got[k]
        vt_mine[...] = value
        vt_all[d] = value
        for k in range(n_dp - 1):
            vt_copy(k).start()

    def mod_out():
        value = mw_mine[h]
        for k in range(n_head - 1):
            mw_copy(k).wait()
            value += mw_got[k]
        part_rows = rows // n_head
        first_lane = (d * n_head + h) * part_rows
        for k in range(2):
            lanes_of = slice(k * C, (k + 1) * C)
            modw_out[:, k] = value[:part_rows, lanes_of]
            turned_row = pltpu.roll(value[part_rows:, lanes_of], lax.rem(C - first_lane, C), 1)
            modb_out[k : k + 1] = turned_row[0:1, :part_rows]

    def class_out():
        for k in range(n_head - 1):
            ge_copy(k).wait()
        table = class_ref.shape[1]
        part = rows // n_head
        value = ge_all[...].reshape(n_head * count, 128)
        label = value[:, rows : rows + 1].astype(jnp.int32)
        hot = lax.broadcasted_iota(jnp.int32, (n_head * count, table), 1) == label
        own = pltpu.roll(value, lax.rem(128 - h * part, 128), 1).astype(BF16)
        value = dot_tn(own, jnp.where(hot, 1.0, 0.0).astype(BF16))
        class_ref[...] = value[:part]

    def vec_second():
        for k in range(n_dp - 1):
            vt_copy(k).wait()
        value = vt_all[0]
        for k in range(1, n_dp):
            value += vt_all[k]
        vec_out[...] = value

    start()
    sides()
    dw(5)
    offer(5)
    dw(7)
    offer(7)
    dw(10)
    z_start(10)
    dw(9)
    offer(9)
    dw(6)
    offer(6)
    conv_back_range(0, 3, 10)
    relay(9)
    dw(8)
    z_start(8)
    relay(7)
    conv_back_range(3, 6, 10)
    relay(6)
    conv_back_range(6, 9, 10)
    relay(5)
    back_b_first()
    back_b_second()
    lower()
    z_mix(10)
    extra_b()
    take()
    dw(2)
    offer(2)
    dw(0)
    offer(0)
    dw(3)
    z_mix(8)
    extra_a()
    collect(6)
    relay(2)
    conv_back_range(0, 3, 0)
    collect(5)
    offer(4)
    relay(0)
    dw(1)
    z_mix(6)
    offer(1)
    offer(3)
    collect(7)
    conv_back_range(3, 6, 0)
    collect(2)
    last(8)
    z_mix(5)
    z_mix(2)
    collect(0)
    collect(9)
    relay(4)
    relay(1)
    conv_back_range(6, 9, 0)
    modulation()
    z_mix(9)
    relay(3)
    relay(8)
    collect(4)
    back_a_first()
    z_mix(4)
    z_mix(7)
    z_mix(0)
    class_out()
    last(5)
    collect(1)
    vec_first()
    last(10)
    z_mix(1)
    back_a_second()
    collect(3)
    vec_second()
    last(9)
    relay(10)
    z_mix(3)
    last(4)
    mod_out()
    last(6)
    last(7)
    collect(8)
    last(0)
    last(2)
    collect(10)
    last(1)
    last(3)

    low_copy().wait_send()
    stage_copy().wait_send()
    image_copy().wait()

    def drain(i):
        for part in range(2):
            x_copy(i, part).wait_send()
            y_copy(i, part).wait_send()
        z_drain(i)
        e_copy(i, 0).wait()
        e_own(i, 0).wait()

    for i in range(PAIRS):
        drain(i)


def run_backward(whole, turned, right, grad_low, grad_resid, conv_out, slopes, images, stats, vecs, mod, sums, pre, ids, modw, classes):
    n_dp, n_head = lax.axis_size("dp"), lax.axis_size("head")
    _, _, lines, _, rows, depth = whole.shape
    cols = depth // n_head
    wide = 2 * cols
    board = (RES, SLOTS, RES, C)
    shape = jax.ShapeDtypeStruct
    return pl.pallas_call(
        functools.partial(backward_kernel, lines),
        out_shape=(
            shape((9, rows, cols), F32),
            shape((9, rows, cols), F32),
            shape((3, rows, cols), F32),
            shape((rows, cols), F32),
            shape((ALL, C), F32),
            shape((rows // n_head, classes), F32),
            shape((rows // n_head, 2, C), F32),
            shape((2, rows // n_head), F32),
            shape((16, cols), F32),
        ),
        in_specs=[ANY] * 8 + [VMEM] * 7,
        out_specs=(ANY,) * 5 + (VMEM,) * 4,
        scratch_shapes=[
            pltpu.VMEM((PAIRS, lines, 2, rows, depth), BF16),
            pltpu.VMEM((len(BACK_NEAR), lines + lines // 2, rows, wide), BF16),
            pltpu.VMEM((len(BACK_NEAR), lines + lines // 2, rows, wide), BF16),
            pltpu.VMEM((len(BACK_NEAR), 4, rows, wide), BF16),
            pltpu.VMEM((len(BACK_FAR), rows + rows // 2, wide), BF16),
            pltpu.VMEM((len(BACK_FAR), rows + rows // 2, wide), BF16),
            pltpu.VMEM((len(BACK_FAR), 4, 2, rows, depth), BF16),
            pltpu.VMEM((2, PAIRS, rows, cols), F32),
            pltpu.VMEM((128, 2 * C), BF16),
            pltpu.VMEM((4, C, 2 * ALL), BF16),
            pltpu.VMEM((2, 2 * ALL, C), BF16),
            pltpu.VMEM((3, 2, ALL + 2 * LINE, C), BF16),
            pltpu.VMEM((ALL, C), BF16),
            pltpu.VMEM((ALL, C), BF16),
            pltpu.VMEM((AHEAD + 1, lines, 2, rows, depth), BF16),
            pltpu.VMEM(board, F32),
            pltpu.VMEM(board, F32),
            pltpu.VMEM(board, F32),
            pltpu.VMEM((ALL, C), F32),
            pltpu.VMEM((ALL, C), BF16),
            pltpu.VMEM((16, C), F32),
            pltpu.VMEM((2 * SLOTS, C), F32),
            pltpu.VMEM((3 * SLOTS, C), F32),
            pltpu.VMEM((2 * SLOTS, C), BF16),
            pltpu.VMEM((n_dp, 2 * SLOTS, C), BF16),
            pltpu.VMEM((n_head, rows // n_head + 8, 2 * C), F32),
            pltpu.VMEM((n_head - 1, rows // n_head + 8, 2 * C), F32),
            pltpu.VMEM((n_head, n_dp * SLOTS, 128), F32),
            pltpu.VMEM((n_head, 16, cols), F32),
            pltpu.VMEM((n_head - 1, 16, cols), F32),
            pltpu.VMEM((16, cols), F32),
            pltpu.VMEM((n_dp, 16, cols), F32),
            DMA((PAIRS, 2)),
            DMA((PAIRS, 2)),
            DMA((PAIRS, 2)),
            DMA((PAIRS, 2)),
            DMA((PAIRS, lines - 1)),
            DMA((PAIRS, lines - 1)),
            DMA((PAIRS,)),
            DMA((PAIRS,)),
            DMA((PAIRS,)),
            DMA((PAIRS,)),
            DMA((PAIRS,)),
            DMA((2,)),
            DMA((2,)),
            DMA((7,)),
            DMA((AHEAD + 1,)),
            DMA((5,)),
            DMA,
            DMA((n_dp - 1,)),
            DMA((n_dp - 1,)),
            DMA((n_head - 1,)),
            DMA((n_head - 1,)),
            DMA((n_head - 1,)),
            DMA((n_head - 1,)),
            DMA((n_head - 1,)),
            DMA((n_head - 1,)),
            DMA((n_dp - 1,)),
            DMA((n_dp - 1,)),
        ],
        compiler_params=pltpu.CompilerParams(
            collective_id=1, has_side_effects=True, vmem_limit_bytes=64 * 2**20 - 2**18
        ),
        name="backward_scatter",
    )(whole, turned, right, grad_low, grad_resid, conv_out, slopes, images, stats, vecs, mod, sums, pre, ids, modw)


def parts_of_array(one):
    length = one.shape[0]
    pieces_of = 4 if length % 64 == 0 else 3 if length == 9 else 1
    size = length // pieces_of
    return [pl.ds(k * size, size) for k in range(pieces_of)]


def results_kernel(count, *refs):
    sources, vec_ref, refs = refs[:count], refs[count], refs[count + 1 :]
    targets, vectors = refs[:count], refs[count : count + VECTORS]
    held, in_sems, out_sems = refs[count + VECTORS : -2], refs[-2], refs[-1]
    every = [(k, part) for k in range(count) for part in parts_of_array(sources[k])]
    arrive, leave = [], []
    for n, (k, part) in enumerate(every):
        arrive.append(pltpu.make_async_copy(sources[k].at[part], held[k].at[part], in_sems.at[n]))
        leave.append(pltpu.make_async_copy(held[k].at[part], targets[k].at[part], out_sems.at[n]))
        arrive[n].start()
    for k, ref in enumerate(vectors):
        ref[...] = vec_ref[k].reshape(ref.shape)
    for n in range(len(every)):
        arrive[n].wait()
        leave[n].start()
    for copy in leave:
        copy.wait()


def run_results(arrays, vec):
    count = len(arrays)
    copies = sum(len(parts_of_array(one)) for one in arrays)
    shape = jax.ShapeDtypeStruct
    return pl.pallas_call(
        functools.partial(results_kernel, count),
        out_shape=tuple(shape(one.shape, one.dtype) for one in arrays)
        + (shape(vec.shape[1:], F32),) * VECTORS,
        in_specs=[ANY] * count + [VMEM],
        out_specs=(ANY,) * count + (VMEM,) * VECTORS,
        scratch_shapes=[pltpu.VMEM(one.shape, one.dtype) for one in arrays] + [DMA((copies,)), DMA((copies,))],
        compiler_params=pltpu.CompilerParams(vmem_limit_bytes=60 * 2**20),
        name="results",
    )(*arrays, vec)


def direct(rows, cols):
    n_dp, n_head = lax.axis_size("dp"), lax.axis_size("head")
    return n_head == 4 and n_dp == 8 and rows % 32 == 0 and cols % 64 == 0


def fast_shards(
    images,
    cotangent,
    counts,
    labels,
    levels,
    noise_table,
    class_table,
    gain_a,
    shift_a,
    conv_a,
    bias_a,
    mod_weight,
    mod_bias,
    gain_b,
    shift_b,
    conv_b,
    bias_b,
    gain_c,
    shift_c,
    qkv_weight,
    proj_weight,
    proj_bias,
):
    weights = (
        jnp.swapaxes(conv_a, 0, 1),
        jnp.swapaxes(conv_b, 0, 1),
        jnp.swapaxes(qkv_weight, 0, 1),
        proj_weight,
    )
    vectors = (gain_a, shift_a, bias_a, gain_b, shift_b, bias_b, gain_c, shift_c, proj_bias)
    flat = images.reshape(ALL, C)
    (
        whole,
        conv_out,
        slopes,
        turned,
        block_out,
        grad_resid,
        grad_low,
        right,
        vecs,
        mod,
        stats,
        pre,
        all_ids,
        sums,
    ) = run_forward(
        weights,
        flat,
        cotangent.reshape(ALL, C),
        counts.T,
        labels,
        levels,
        class_table.T,
        noise_table,
        mod_weight,
        mod_bias,
        vectors,
    )
    *arrays, vec = run_backward(
        whole,
        turned,
        right,
        grad_low,
        grad_resid,
        conv_out,
        slopes,
        flat,
        stats,
        vecs,
        mod,
        sums,
        pre,
        all_ids,
        mod_weight,
        class_table.shape[0],
    )
    block_out, conva, convb, qkvw, projw, image_grad, class_grad, modw_grad, modb_grad, *rest = run_results(
        (block_out, *arrays), vec
    )
    gaina, shifta, biasa, gainb, shiftb, biasb, gainc, shiftc, projb = rest
    return (
        block_out.reshape(images.shape),
        image_grad.reshape(images.shape),
        class_grad.T,
        gaina,
        shifta,
        jnp.swapaxes(conva, 0, 1),
        biasa,
        modw_grad,
        modb_grad,
        gainb,
        shiftb,
        jnp.swapaxes(convb, 0, 1),
        biasb,
        gainc,
        shiftc,
        jnp.swapaxes(qkvw, 0, 1),
        projw,
        projb,
    )


def shards(*args):
    rows, _, cols = args[9].shape
    if direct(rows, cols):
        return fast_shards(*args)
    return plain_shards(*args)


def solution(mesh):
    placed = (
        P(("dp", "head"), None, None, None),
        P(("dp", "head"), None, None, None),
        P(),
        P(("dp", "head")),
        P(("dp", "head")),
        P(),
        P(None, "dp"),
        P("head"),
        P("head"),
        P("dp", None, "head"),
        P("head"),
        P("dp", None, None),
        P(),
        P("head"),
        P("head"),
        P("dp", None, "head"),
        P("head"),
        P("head"),
        P("head"),
        P("dp", None, "head"),
        P("dp", "head"),
        P("head"),
    )
    return jax.shard_map(
        shards,
        mesh=mesh,
        in_specs=placed,
        out_specs=(
            P(("dp", "head"), None, None, None),
            P(("dp", "head"), None, None, None),
            P(None, ("dp", "head")),
            P("head"),
            P("head"),
            P("dp", None, "head"),
            P("head"),
            P(("dp", "head"), None, None),
            P(None, ("dp", "head")),
            P("head"),
            P("head"),
            P("dp", None, "head"),
            P("head"),
            P("head"),
            P("head"),
            P("dp", None, "head"),
            P("dp", "head"),
            P("head"),
        ),
        check_vma=False,
    )
```

```python
import functools

import jax
import jax.numpy as jnp
from jax import lax
from jax.experimental import pallas as pl
from jax.experimental.pallas import tpu as pltpu
from jax.sharding import PartitionSpec as P

C = 768
DH = 64
GROUPS = 32


EPSILON = 1e-05
HIGHEST = lax.Precision.HIGHEST


def norm_forward(values, gain, shift):
    count, chans = (values.shape[0], values.shape[-1])
    span = C // GROUPS
    grouped = values.reshape(count, -1, chans // span, span)
    mean = jnp.mean(grouped, axis=(1, 3), keepdims=True)
    centred = grouped - mean
    inverse = lax.rsqrt(jnp.mean(centred * centred, axis=(1, 3), keepdims=True) + EPSILON)
    normed = (centred * inverse).reshape(values.shape)
    return (normed * gain + shift, normed, inverse)


def norm_backward(grad_out, normed, inverse, gain):
    grad_gain = jnp.sum(grad_out * normed, axis=(0, 1, 2))
    grad_shift = jnp.sum(grad_out, axis=(0, 1, 2))
    count, chans = (grad_out.shape[0], grad_out.shape[-1])
    span = C // GROUPS
    layout = (count, -1, chans // span, span)
    grad_normed = (grad_out * gain).reshape(layout)
    normed_groups = normed.reshape(layout)
    mean_one = jnp.mean(grad_normed, axis=(1, 3), keepdims=True)
    mean_two = jnp.mean(grad_normed * normed_groups, axis=(1, 3), keepdims=True)
    grad_in = inverse * (grad_normed - mean_one - normed_groups * mean_two)
    return (grad_in.reshape(grad_out.shape), grad_gain, grad_shift)


def silu_slope(values):
    sigma = jax.nn.sigmoid(values)
    return sigma * (1.0 + values * (1.0 - sigma))


def patches_of(act):
    count, rows, cols, chans = act.shape
    padded = jnp.pad(act, ((0, 0), (1, 1), (1, 1), (0, 0)))
    taps = [padded[:, i : i + rows, j : j + cols, :] for i in range(3) for j in range(3)]
    return jnp.stack(taps, axis=3).reshape(count * rows * cols, 9, chans)


def contract_rows(left, right):
    return lax.dot_general(
        left, right, (((0,), (0,)), ((), ())), preferred_element_type=jnp.float32
    )


def contract_cols(left, right):
    return lax.dot_general(
        left, right, (((1,), (1,)), ((), ())), preferred_element_type=jnp.float32
    )


def conv_back(grad_low, weight, count, rows, cols):
    chans = weight.shape[0]
    padded = jnp.zeros((count, rows + 2, cols + 2, chans), jnp.float32)
    for tap in range(9):
        i, j = divmod(tap, 3)
        part = contract_cols(grad_low, weight[:, tap, :]).reshape(count, rows, cols, chans)
        padded = padded.at[:, i : i + rows, j : j + cols, :].add(part)
    return padded[:, 1 : rows + 1, 1 : cols + 1, :]


def keep_same(values):
    return values


def live_rows(counts, first, number, count):
    sums = jnp.sum(counts, axis=1)
    chosen = lax.dynamic_slice_in_dim(sums, first, number)
    slots = lax.iota(jnp.int32, count)
    return (slots[None, :] < chosen[:, None]).astype(jnp.float32).reshape(number * count)


def residual_forward(source, mod_pair, weights, spread):
    (
        conv_one,
        conv_two,
        gain_one,
        shift_one,
        bias_one,
        gain_two,
        shift_two,
        bias_two,
        gain_three,
        shift_three,
    ) = weights
    out_a, normed_a, inverse_a = norm_forward(source, gain_one, shift_one)
    wide_a = spread(jax.nn.silu(out_a).astype(jnp.bfloat16))
    conv_out_a = (
        jnp.einsum("ptc,cto->po", patches_of(wide_a), conv_one, preferred_element_type=jnp.float32)
        + bias_one
    ).reshape(source.shape)
    scale = mod_pair[:, :, 0:1, :]
    offset = mod_pair[:, :, 1:2, :]
    out_b, normed_b, inverse_b = norm_forward(conv_out_a, gain_two, shift_two)
    inner_b = offset + out_b * (scale + 1.0)
    wide_b = spread(jax.nn.silu(inner_b).astype(jnp.bfloat16))
    conv_out_b = (
        jnp.einsum("ptc,cto->po", patches_of(wide_b), conv_two, preferred_element_type=jnp.float32)
        + bias_two
    ).reshape(source.shape)
    resid = source + conv_out_b
    out_c, normed_c, inverse_c = norm_forward(resid, gain_three, shift_three)
    attn_in = out_c.astype(jnp.bfloat16)
    saved = (
        out_a,
        normed_a,
        inverse_a,
        wide_a,
        out_b,
        normed_b,
        inverse_b,
        inner_b,
        wide_b,
        normed_c,
        inverse_c,
        scale,
    )
    return (resid, attn_in, saved)


def residual_backward(grad_attn, grad_out, saved, weights, reduce_value):
    conv_one, conv_two, gain_one, gain_two, gain_three = (
        weights[0],
        weights[1],
        weights[2],
        weights[5],
        weights[8],
    )
    (
        out_a,
        normed_a,
        inverse_a,
        wide_a,
        out_b,
        normed_b,
        inverse_b,
        inner_b,
        wide_b,
        normed_c,
        inverse_c,
        scale,
    ) = saved
    count, rows, cols, local = grad_out.shape
    grad_resid_c, gainc_term, shiftc_term = norm_backward(
        grad_attn, normed_c, inverse_c, gain_three
    )
    grad_resid = grad_out + grad_resid_c
    grad_conv_b = grad_resid.reshape(-1, local).astype(jnp.bfloat16)
    biasb_term = jnp.sum(grad_conv_b.astype(jnp.float32), axis=0)
    convb_term = jnp.einsum(
        "ptc,po->cto", patches_of(wide_b), grad_conv_b, preferred_element_type=jnp.float32
    )
    grad_act_b = reduce_value(conv_back(grad_conv_b, conv_two, count, rows, cols))
    grad_inner = grad_act_b * silu_slope(inner_b)
    grad_offset = jnp.sum(grad_inner, axis=(1, 2))
    grad_scale = jnp.sum(grad_inner * out_b, axis=(1, 2))
    grad_mod = jnp.stack([grad_scale, grad_offset], axis=1)[:, None]
    grad_conv_full, gainb_term, shiftb_term = norm_backward(
        grad_inner * (scale + 1.0), normed_b, inverse_b, gain_two
    )
    grad_conv_a = grad_conv_full.reshape(-1, local).astype(jnp.bfloat16)
    biasa_term = jnp.sum(grad_conv_a.astype(jnp.float32), axis=0)
    conva_term = jnp.einsum(
        "ptc,po->cto", patches_of(wide_a), grad_conv_a, preferred_element_type=jnp.float32
    )
    grad_act_a = reduce_value(conv_back(grad_conv_a, conv_one, count, rows, cols))
    grad_source, gaina_term, shifta_term = norm_backward(
        grad_act_a * silu_slope(out_a), normed_a, inverse_a, gain_one
    )
    image_grad = grad_resid + grad_source
    vectors = (
        gaina_term,
        shifta_term,
        biasa_term,
        gainb_term,
        shiftb_term,
        biasb_term,
        gainc_term,
        shiftc_term,
    )
    return (image_grad, grad_mod, (conva_term, convb_term), vectors)


def attend_forward(block):
    query, key, value = (block[:, :, 0], block[:, :, 1], block[:, :, 2])
    batch, pixels, heads_here, depth = query.shape
    scores = jnp.einsum("bqhd,bkhd->bhqk", query, key, preferred_element_type=jnp.float32) * DH ** (
        -0.5
    )
    top = jnp.max(scores, axis=-1, keepdims=True)
    weights = jnp.exp(scores - top)
    sums = jnp.sum(weights, axis=-1, keepdims=True)
    probs = (weights / sums).astype(jnp.bfloat16)
    logsum = (top + jnp.log(sums))[..., 0]
    mixed = jnp.einsum("bhqk,bkhd->bqhd", probs, value, preferred_element_type=jnp.float32).astype(
        jnp.bfloat16
    )
    return (mixed.reshape(batch, pixels, heads_here * depth), logsum)


def attend_backward(block, logsum, grad_head):
    query, key, value = (block[:, :, 0], block[:, :, 1], block[:, :, 2])
    batch, pixels, heads_here, depth = query.shape
    factor = DH ** (-0.5)
    scores = jnp.einsum("bqhd,bkhd->bhqk", query, key, preferred_element_type=jnp.float32) * factor
    probs = jnp.exp(scores - logsum[..., None])
    grad_value = jnp.einsum(
        "bhqk,bqhd->bkhd", probs.astype(jnp.bfloat16), grad_head, preferred_element_type=jnp.float32
    )
    grad_probs = jnp.einsum("bqhd,bkhd->bhqk", grad_head, value, preferred_element_type=jnp.float32)
    inner = jnp.sum(grad_probs * probs, axis=-1, keepdims=True)
    grad_scores = (probs * (grad_probs - inner)).astype(jnp.bfloat16)
    grad_query = (
        jnp.einsum("bhqk,bkhd->bqhd", grad_scores, key, preferred_element_type=jnp.float32) * factor
    )
    grad_key = (
        jnp.einsum("bhqk,bqhd->bkhd", grad_scores, query, preferred_element_type=jnp.float32)
        * factor
    )
    stacked = jnp.stack([grad_query, grad_key, grad_value], axis=2).astype(jnp.bfloat16)
    return stacked.reshape(batch, pixels, 3, heads_here * depth)


def plain_shards(
    images,
    cotangent,
    counts,
    labels,
    levels,
    noise_table,
    class_table,
    gain_a,
    shift_a,
    conv_a,
    bias_a,
    mod_weight,
    mod_bias,
    gain_b,
    shift_b,
    conv_b,
    bias_b,
    gain_c,
    shift_c,
    qkv_weight,
    proj_weight,
    proj_bias,
):
    rows_a, rows_b, rows_qkv, rows_proj, mod_full, class_full = (
        lax.all_gather(conv_a, "dp", axis=0, tiled=True),
        lax.all_gather(conv_b, "dp", axis=0, tiled=True),
        lax.all_gather(qkv_weight, "dp", axis=0, tiled=True),
        lax.all_gather(proj_weight, "dp", axis=0, tiled=True),
        lax.all_gather(mod_weight, "dp", axis=0, tiled=True),
        lax.all_gather(class_table, "dp", axis=1, tiled=True),
    )
    count, rows, cols, channels = images.shape
    pixels = rows * cols
    groups_n = lax.axis_size("head")
    quarter = channels // groups_n
    heads_local = quarter // DH
    first_dp = lax.axis_index("dp") * groups_n
    class_hot = (labels[:, None] == lax.iota(jnp.int32, class_full.shape[0])[None, :]).astype(
        jnp.bfloat16
    )
    level_hot = (levels[:, None] == lax.iota(jnp.int32, noise_table.shape[0])[None, :]).astype(
        jnp.bfloat16
    )
    embed_pre = jnp.dot(class_hot, class_full, preferred_element_type=jnp.float32) + jnp.dot(
        level_hot, noise_table, preferred_element_type=jnp.float32
    )
    embed = jax.nn.silu(embed_pre).astype(jnp.bfloat16)
    modulation = (
        jnp.einsum("ne,etc->ntc", embed, mod_full, preferred_element_type=jnp.float32)
        + mod_bias.astype(jnp.float32)
    ).astype(jnp.bfloat16)
    mod_pair = modulation.reshape(count, 1, 2, channels)
    (
        conv_one,
        conv_two,
        qkv_full,
        proj_full,
        gain_one,
        shift_one,
        bias_one,
        gain_two,
        shift_two,
        bias_two,
        gain_three,
        shift_three,
        bias_three,
    ) = (
        lax.all_gather(rows_a, "head", axis=2, tiled=True),
        lax.all_gather(rows_b, "head", axis=2, tiled=True),
        lax.all_gather(rows_qkv, "head", axis=2, tiled=True),
        lax.all_gather(rows_proj, "head", axis=1, tiled=True),
        lax.all_gather(gain_a, "head", axis=0, tiled=True),
        lax.all_gather(shift_a, "head", axis=0, tiled=True),
        lax.all_gather(bias_a, "head", axis=0, tiled=True),
        lax.all_gather(gain_b, "head", axis=0, tiled=True),
        lax.all_gather(shift_b, "head", axis=0, tiled=True),
        lax.all_gather(bias_b, "head", axis=0, tiled=True),
        lax.all_gather(gain_c, "head", axis=0, tiled=True),
        lax.all_gather(shift_c, "head", axis=0, tiled=True),
        lax.all_gather(proj_bias, "head", axis=0, tiled=True),
    )
    weights = (
        conv_one,
        conv_two,
        gain_one,
        shift_one,
        bias_one,
        gain_two,
        shift_two,
        bias_two,
        gain_three,
        shift_three,
    )
    live = live_rows(counts, first_dp + lax.axis_index("head"), 1, count)
    total = count * pixels
    width = channels // groups_n
    source = images.astype(jnp.float32)
    resid, attn_in, saved = residual_forward(
        source, mod_pair.astype(jnp.float32), weights, keep_same
    )
    attn_flat = attn_in.reshape(total, channels)
    qkv_flat = qkv_full.reshape(channels, 3 * channels)
    qkv = jnp.dot(attn_flat, qkv_flat, preferred_element_type=jnp.float32).astype(jnp.bfloat16)
    packed = qkv.reshape(1, count, pixels, 3, groups_n, width)
    block = lax.all_to_all(packed, "head", split_axis=4, concat_axis=0, tiled=True)
    groups = block.shape[0]
    items = block.shape[1]
    flat = block.reshape(groups * items, pixels, 3, heads_local, DH)
    mixed, logsum = attend_forward(flat)
    mixed = mixed.reshape(groups, items, pixels, 1, width)
    returned = lax.all_to_all(mixed, "head", split_axis=0, concat_axis=3, tiled=True)
    returned, logsum, kept = (returned, logsum.reshape(groups, items, heads_local, pixels), block)
    mixed_image = returned.reshape(total, channels)
    result = (
        resid.reshape(total, channels)
        + jnp.dot(mixed_image, proj_full, preferred_element_type=jnp.float32)
        + bias_three
    )
    block_out = (result.reshape(images.shape) * live[:, None, None, None]).astype(jnp.bfloat16)
    grad_out = cotangent.astype(jnp.float32) * live[:, None, None, None]
    grad_flat = grad_out.reshape(total, channels)
    grad_low = grad_flat.astype(jnp.bfloat16)
    projw_full = contract_rows(mixed_image, grad_low)
    projb_full = jnp.sum(grad_flat, axis=0)
    grad_mixed = contract_cols(grad_low, proj_full).astype(jnp.bfloat16)
    arrived = lax.all_to_all(
        grad_mixed.reshape(1, count, pixels, groups_n, width),
        "head",
        split_axis=3,
        concat_axis=0,
        tiled=True,
    )
    flat_block = kept.reshape(groups_n * count, pixels, 3, heads_local, DH)
    grad_head = arrived.reshape(groups_n * count, pixels, heads_local, DH)
    stacked = attend_backward(
        flat_block, logsum.reshape(groups_n * count, heads_local, pixels), grad_head
    )
    stacked = stacked.reshape(groups_n, count, pixels, 3, 1, width)
    grad_qkv = lax.all_to_all(stacked, "head", split_axis=0, concat_axis=4, tiled=True).reshape(
        total, 3 * channels
    )
    qkvw_full = contract_rows(attn_flat, grad_qkv).reshape(channels, 3, channels)
    grad_attn = contract_cols(grad_qkv, qkv_flat).reshape(images.shape)
    image_grad, grad_mod_part, conv_terms, vectors = residual_backward(
        grad_attn, grad_out, saved, weights, keep_same
    )
    (
        gaina_full,
        shifta_full,
        biasa_full,
        gainb_full,
        shiftb_full,
        biasb_full,
        gainc_full,
        shiftc_full,
    ) = vectors
    (
        conva_term,
        convb_term,
        qkvw_term,
        projw_term,
        gaina_term,
        shifta_term,
        biasa_term,
        gainb_term,
        shiftb_term,
        biasb_term,
        gainc_term,
        shiftc_term,
        projb_term,
    ) = (
        lax.psum_scatter(
            conv_terms[0].astype(jnp.bfloat16), "head", scatter_dimension=2, tiled=True
        ).astype(jnp.float32),
        lax.psum_scatter(
            conv_terms[1].astype(jnp.bfloat16), "head", scatter_dimension=2, tiled=True
        ).astype(jnp.float32),
        lax.psum_scatter(
            qkvw_full.astype(jnp.bfloat16), "head", scatter_dimension=2, tiled=True
        ).astype(jnp.float32),
        lax.psum_scatter(
            projw_full.astype(jnp.bfloat16), "head", scatter_dimension=1, tiled=True
        ).astype(jnp.float32),
        lax.psum_scatter(
            gaina_full.astype(jnp.bfloat16), "head", scatter_dimension=0, tiled=True
        ).astype(jnp.float32),
        lax.psum_scatter(
            shifta_full.astype(jnp.bfloat16), "head", scatter_dimension=0, tiled=True
        ).astype(jnp.float32),
        lax.psum_scatter(
            biasa_full.astype(jnp.bfloat16), "head", scatter_dimension=0, tiled=True
        ).astype(jnp.float32),
        lax.psum_scatter(
            gainb_full.astype(jnp.bfloat16), "head", scatter_dimension=0, tiled=True
        ).astype(jnp.float32),
        lax.psum_scatter(
            shiftb_full.astype(jnp.bfloat16), "head", scatter_dimension=0, tiled=True
        ).astype(jnp.float32),
        lax.psum_scatter(
            biasb_full.astype(jnp.bfloat16), "head", scatter_dimension=0, tiled=True
        ).astype(jnp.float32),
        lax.psum_scatter(
            gainc_full.astype(jnp.bfloat16), "head", scatter_dimension=0, tiled=True
        ).astype(jnp.float32),
        lax.psum_scatter(
            shiftc_full.astype(jnp.bfloat16), "head", scatter_dimension=0, tiled=True
        ).astype(jnp.float32),
        lax.psum_scatter(
            projb_full.astype(jnp.bfloat16), "head", scatter_dimension=0, tiled=True
        ).astype(jnp.float32),
    )
    grad_mod = grad_mod_part.reshape(count, 2, channels)
    modw_term = jnp.einsum("ne,ntc->etc", embed.astype(jnp.float32), grad_mod, precision=HIGHEST)
    modb_term = jnp.sum(grad_mod, axis=0)
    grad_embed = jnp.einsum(
        "ntc,etc->ne", grad_mod, mod_full.astype(jnp.float32), precision=HIGHEST
    ) * silu_slope(embed_pre)
    class_term = lax.dot_general(
        class_hot.astype(jnp.float32), grad_embed, (((0,), (0,)), ((), ())), precision=HIGHEST
    )
    modw_grad, class_grad, modb_grad = (
        lax.psum_scatter(modw_term, ("dp", "head"), scatter_dimension=0, tiled=True),
        lax.psum_scatter(class_term, ("dp", "head"), scatter_dimension=1, tiled=True),
        lax.psum_scatter(modb_term, ("dp", "head"), scatter_dimension=1, tiled=True),
    )
    conva_grad, convb_grad, qkvw_grad, projw_grad = (
        lax.psum_scatter(conva_term, "dp", scatter_dimension=0, tiled=True),
        lax.psum_scatter(convb_term, "dp", scatter_dimension=0, tiled=True),
        lax.psum_scatter(qkvw_term, "dp", scatter_dimension=0, tiled=True),
        lax.psum_scatter(projw_term, "dp", scatter_dimension=0, tiled=True),
    )
    (
        gaina_grad,
        shifta_grad,
        biasa_grad,
        gainb_grad,
        shiftb_grad,
        biasb_grad,
        gainc_grad,
        shiftc_grad,
        projb_grad,
    ) = lax.psum(
        (
            gaina_term,
            shifta_term,
            biasa_term,
            gainb_term,
            shiftb_term,
            biasb_term,
            gainc_term,
            shiftc_term,
            projb_term,
        ),
        "dp",
    )
    return (
        block_out,
        image_grad,
        class_grad,
        gaina_grad,
        shifta_grad,
        conva_grad,
        biasa_grad,
        modw_grad,
        modb_grad,
        gainb_grad,
        shiftb_grad,
        convb_grad,
        biasb_grad,
        gainc_grad,
        shiftc_grad,
        qkvw_grad,
        projw_grad,
        projb_grad,
    )


MESH = pl.DeviceIdType.MESH
UNITS = 22
PAIRS = UNITS // 2
FAR = 9
VECTORS = 9
RES = 8
SLOTS = 8
PIX = RES * RES
LINE = SLOTS * RES
ALL = RES * LINE
WIDTH = 256
BAND = 256
F32 = jnp.float32
BF16 = jnp.bfloat16
ANY = pl.BlockSpec(memory_space=pl.ANY)
VMEM = pl.BlockSpec(memory_space=pltpu.VMEM)
SMEM = pl.BlockSpec(memory_space=pltpu.SMEM)
DMA = pltpu.SemaphoreType.DMA


def place():
    d, h = lax.axis_index("dp"), lax.axis_index("head")
    return d // 2, lax.rem(d, 2), h // 2, lax.rem(h, 2)


def at_chip(z, y, x, c):
    return (z * 2 + y, x * 2 + c)


def column_peers(n_dp):
    d, h = lax.axis_index("dp"), lax.axis_index("head")
    return [(lax.rem(d + k, n_dp), h) for k in range(1, n_dp)]


def head_peers(n_head):
    d, h = lax.axis_index("dp"), lax.axis_index("head")
    return [(d, lax.rem(h + k, n_head)) for k in range(1, n_head)]


def greet(devices):
    barrier = pltpu.get_barrier_semaphore()
    for device in devices:
        pl.semaphore_signal(barrier, inc=1, device_id=device, device_id_type=MESH)
    pl.semaphore_wait(barrier, len(devices))


def remote(src, dst, send, recv, device):
    return pltpu.make_async_remote_copy(
        src_ref=src, dst_ref=dst, send_sem=send, recv_sem=recv, device_id=device, device_id_type=MESH
    )


def each(count, body):
    def step(n, carry):
        body(n)
        return carry

    lax.fori_loop(0, count, step, 0)


def span(index, size):
    return pl.ds(pl.multiple_of(index * size, size), size)


def row(n):
    return pl.ds(n, 1)


def lines_from(i):
    return pl.ds(i * LINE if isinstance(i, int) else pl.multiple_of(i * LINE, LINE), ALL)


def dot(left, right):
    return jnp.dot(left, right, preferred_element_type=F32)


def dot_nt(left, right):
    return lax.dot_general(left, right, (((1,), (1,)), ((), ())), preferred_element_type=F32)


def dot_tn(left, right):
    return lax.dot_general(left, right, (((0,), (0,)), ((), ())), preferred_element_type=F32)


def in_group(first, second, axis):
    chan = lax.broadcasted_iota(jnp.int32, (first, second), axis)
    group = lax.broadcasted_iota(jnp.int32, (first, second), 1 - axis) * (C // GROUPS)
    inside = jnp.logical_and(chan >= group, chan < group + C // GROUPS)
    return jnp.where(inside, 1.0, 0.0).astype(BF16)


def pieces(values):
    high = values.astype(BF16).astype(F32)
    rest = values - high
    mid = rest.astype(BF16).astype(F32)
    return jnp.concatenate([high, mid, rest - mid], axis=0).astype(BF16)


def set_groups(groups):
    groups[0][...] = in_group(C, 128, 0)
    groups[1][...] = in_group(128, C, 1)


def group_mean(sums, groups):
    count = sums.shape[0]
    part = dot(pieces(sums), groups[0][...])
    part = (part[:count] + part[count : 2 * count] + part[2 * count :]) * (1.0 / (PIX * (C // GROUPS)))
    back = dot(pieces(part), groups[1][...])
    return back[:count] + back[count : 2 * count] + back[2 * count :]


def sum_rows(values):
    return jnp.sum(values, axis=0, keepdims=True)


def norm_stats(get, mean_ref, inverse_ref, sums_ref, groups):
    def first(n):
        sums_ref[row(n)] = sum_rows(get(n))

    each(SLOTS, first)
    mean_ref[...] = group_mean(sums_ref[...], groups)

    def second(n):
        centred = get(n) - mean_ref[row(n)]
        sums_ref[row(n)] = sum_rows(centred * centred)

    each(SLOTS, second)
    inverse_ref[...] = lax.rsqrt(group_mean(sums_ref[...], groups) + EPSILON)


def silu(values):
    return values * jax.nn.sigmoid(values)


def shifted(values):
    spot = lax.rem(lax.broadcasted_iota(jnp.int32, values.shape, 0), RES)
    left = jnp.where(spot == 0, 0.0, pltpu.roll(values, 1, 0))
    right = jnp.where(spot == RES - 1, 0.0, pltpu.roll(values, values.shape[0] - 1, 0))
    return left, right


def chunk(n):
    return slice(n * WIDTH, (n + 1) * WIDTH)


CHUNKS = C // WIDTH


def weight_cols(ref, n):
    return ref[:, :, :, chunk(n)].reshape(C, WIDTH)


def weight_rows(ref, n):
    return ref[...].reshape(C, C)[chunk(n)]


def forward_kernel(
    lines,
    weights_a,
    weights_b,
    weights_qkv,
    weights_proj,
    images_hbm,
    cot_hbm,
    counts_ref,
    labels_ref,
    levels_ref,
    class_table,
    noise_table,
    modw_table,
    modb_ref,
    *refs,
):
    vectors, refs = refs[:VECTORS], refs[VECTORS:]
    forward_steps(
        lines,
        vectors,
        weights_a,
        weights_b,
        weights_qkv,
        weights_proj,
        images_hbm,
        cot_hbm,
        counts_ref,
        labels_ref,
        levels_ref,
        class_table,
        noise_table,
        modw_table,
        modb_ref,
        *refs,
    )


def forward_steps(
    lines,
    vectors,
    weights_a,
    weights_b,
    weights_qkv,
    weights_proj,
    images_hbm,
    cot_hbm,
    counts_ref,
    labels_ref,
    levels_ref,
    class_table,
    noise_table,
    modw_table,
    modb_ref,
    whole_out,
    conv_out,
    slopes_out,
    turned_out,
    block_out,
    grad_out,
    low_out,
    right_out,
    vecs_ref,
    mod_ref,
    stats_ref,
    pre_ref,
    all_ids,
    sums_out,
    halves,
    whole_ref,
    vec_ref,
    ids_ref,
    class_ref,
    modw_ref,
    vec_all,
    mod_part,
    mod_got,
    act,
    act_f32,
    sums_ref,
    conv_ref,
    resid_ref,
    slopes,
    turned,
    attn_in,
    qkv,
    right,
    low,
    pair_ref,
    group_sum,
    group_back,
    pair_send,
    pair_recv,
    pair_local,
    z_send,
    z_recv,
    p_send,
    x_send,
    x_recv,
    y_send,
    y_recv,
    s_send,
    s_recv,
    vec_send,
    vec_recv,
    ids_send,
    ids_recv,
    mod_send,
    mod_recv,
    unit_sem,
    flush_sem,
    in_sem,
    share_local,
    share_send,
    share_recv,
):
    z, y, x, c = place()
    d, h = lax.axis_index("dp"), lax.axis_index("head")
    n_dp, n_head = lines * 2, 4
    half = lines // 2
    inner = jnp.logical_and(z > 0, z < lines - 1)
    far = at_chip(lax.rem(3 * z + 1, lines), y, x, c)
    rows, cols_own = halves.shape[2:]
    wide = 2 * cols_own
    sibling = at_chip(z, y, x, 1 - c)
    along_x = at_chip(z, y, 1 - x, c)
    along_y = at_chip(z, 1 - y, x, c)
    line = [at_chip(lax.rem(z + k, lines), y, x, c) for k in range(1, lines)]
    column, heads = column_peers(n_dp), head_peers(n_head)
    greet(column + heads)

    def spot(i, cc, zz, yy, xx):
        return whole_ref.at[i, cc, zz, yy, :, span(xx, wide)]

    def parts_of(core):
        return (
            (weights_a.at[pl.ds(4 * core, 4)], pl.ds(0, 4)),
            (weights_b.at[pl.ds(4 * core, 4)], pl.ds(5, 4)),
            (weights_qkv.at[pl.ds(core, 1)], pl.ds(9, 1)),
        )

    last_parts = (
        ((weights_a.at[8], 4), (weights_qkv.at[2], 10)),
        ((weights_b.at[8], 4), (weights_proj, 10)),
    )

    def keep_copy(k):
        source, where = parts_of(c)[k]
        return pltpu.make_async_copy(source, halves.at[c, where], pair_local.at[k])

    def swap_copy(k):
        source, where = parts_of(1 - c)[k]
        return remote(source, halves.at[c, where], pair_send.at[k], pair_recv.at[k], sibling)

    def last_keep(core, k):
        source, where = last_parts[core][k]
        return pltpu.make_async_copy(source, halves.at[c, where], pair_local.at[3 + k])

    def last_swap(core, k):
        source, where = last_parts[core][k]
        return remote(source, halves.at[c, where], pair_send.at[3 + k], pair_recv.at[3 + k], sibling)

    def swap_start():
        for k in range(3):
            swap_copy(k).start()
            keep_copy(k).start()
        for core in range(2):

            @pl.when(c == core)
            def _():
                for k in range(2):
                    last_swap(1 - core, k).start()
                    last_keep(core, k).start()

    def swap_wait(k):
        if k < 3:
            keep_copy(k).wait()
            swap_copy(k).wait()
        else:
            last_keep(0, k - 3).wait()
            last_swap(0, k - 3).wait()

    def images_copy():
        return pltpu.make_async_copy(images_hbm, images_ref, in_sem.at[0])

    def cot_copy():
        return pltpu.make_async_copy(cot_hbm, cot_ref, in_sem.at[1])

    images_ref, cot_ref = attn_in, low
    groups = (group_sum, group_back)

    def vec_copy(k):
        return remote(vec_ref, vec_all.at[h], vec_send.at[k], vec_recv.at[k], heads[k])

    def ids_copy(k):
        return remote(ids_ref, all_ids.at[d], ids_send.at[k], ids_recv.at[k], column[k])

    def mod_copy(k):
        return remote(
            mod_part.at[lax.rem(d + k + 1, n_dp)], mod_got.at[d], mod_send.at[k], mod_recv.at[k], column[k]
        )

    def z_part(i, zz):
        if isinstance(i, int) and i >= FAR:
            return whole_ref.at[i, c, zz]
        return spot(i, c, zz, y, x)

    def z_copy(i, k):
        ref = z_part(i, z)
        return remote(ref, ref, z_send.at[i, k], z_recv.at[i, k], line[k])

    def z_pass(i):
        ref = z_part(i, lax.rem(z + 2, lines))
        return remote(ref, ref, p_send.at[i], z_recv.at[i, lax.rem(2 * z + 2, lines)], far)

    def z_start(i):
        z_copy(i, 1).start()

        @pl.when(z != lines - 1)
        def _():
            z_copy(i, 0).start()

        @pl.when(z != 0)
        def _():
            z_copy(i, 2).start()

    def z_relay(i):
        z_copy(i, 1).wait_recv()

        @pl.when(inner)
        def _():
            z_pass(i).start()

    def z_finish(i):
        z_copy(i, 0).wait_recv()
        z_copy(i, 2).wait_recv()

    def z_drain(i):
        z_copy(i, 1).wait_send()

        @pl.when(z != lines - 1)
        def _():
            z_copy(i, 0).wait_send()

        @pl.when(z != 0)
        def _():
            z_copy(i, 2).wait_send()

        @pl.when(inner)
        def _():
            z_pass(i).wait_send()

    def x_copy(i, part):
        if isinstance(i, int) and i >= FAR:
            ref = spot(i, c, z, y, x) if part == 0 else spot(i, c, z, 1 - y, x).at[pl.ds(rows // 2, rows // 2)]
        elif part == 0:
            ref = spot(i, c, slice(None), y, x)
        else:
            ref = spot(i, c, pl.ds(half, half), 1 - y, x)
        return remote(ref, ref, x_send.at[i, part], x_recv.at[i, part], along_x)

    def y_copy(i, part):
        if isinstance(i, int) and i >= FAR:
            ref = spot(i, c, z, y, x) if part == 0 else spot(i, c, z, y, 1 - x).at[pl.ds(0, rows // 2)]
        elif part == 0:
            ref = spot(i, c, slice(None), y, x)
        else:
            ref = spot(i, c, pl.ds(0, half), y, 1 - x)
        return remote(ref, ref, y_send.at[i, part], y_recv.at[i, part], along_y)

    def s_copy(i, part):
        if isinstance(i, int) and i >= FAR:
            ref = whole_ref.at[i, c, part]
        else:
            yy, xx = ((y, x), (y, 1 - x), (1 - y, x), (1 - y, 1 - x))[part]
            ref = spot(i, c, slice(None), yy, xx)
        return remote(ref, ref, s_send.at[i, part], s_recv.at[i, part], sibling)

    def join(i):
        whole_ref[i, c, z, y, :, span(x, wide)] = jnp.concatenate([halves[0, i], halves[1, i]], axis=-1)

    def begin(i):
        join(i)
        z_start(i)

    def far_begin(i):
        x_copy(i, 0).start()
        y_copy(i, 0).start()

    def far_pass(i):
        x_copy(i, 0).wait_recv()
        y_copy(i, 1).start()
        y_copy(i, 0).wait_recv()
        x_copy(i, 1).start()

    def far_line(i):
        x_copy(i, 1).wait_recv()
        y_copy(i, 1).wait_recv()
        z_start(i)

    def far_finish(i):
        z_finish(i)
        for part in range(lines):
            s_copy(i, part).start()

    def spread_line(i):
        z_finish(i)
        x_copy(i, 0).start()
        y_copy(i, 0).start()
        s_copy(i, 0).start()

    def pass_on(i):
        x_copy(i, 0).wait_recv()
        y_copy(i, 1).start()
        s_copy(i, 1).start()
        y_copy(i, 0).wait_recv()
        x_copy(i, 1).start()
        s_copy(i, 2).start()

    def finish(i):
        x_copy(i, 1).wait_recv()
        y_copy(i, 1).wait_recv()
        s_copy(i, 3).start()

    def arrived(i):
        for part in range(4):
            s_copy(i, part).wait_recv()

    def unit_copy(i):
        return pltpu.make_async_copy(whole_ref.at[i], whole_out.at[i], unit_sem.at[i])

    def fetch(i):
        arrived(i)
        if not isinstance(i, int) or i < FAR:
            unit_copy(i).start()

    def product(total, tap, i, k):
        for n in range(CHUNKS):
            value = dot(act[tap % 3, lines_from(tap // 3)], weight_cols(whole_ref.at[i, k], n))
            total[:, :, :, chunk(n)] += value.reshape(RES, SLOTS, RES, WIDTH)

    def use_pair(total, i, first):
        each(2, lambda k: product(total, i - first + 4 * k, i, k))

    flushed = (
        (conv_ref, conv_out),
        (slopes.at[0], slopes_out.at[0]),
        (slopes.at[1], slopes_out.at[1]),
        (low, block_out),
        (conv_ref, grad_out),
        (attn_in, low_out),
    )

    def share_parts(k):
        if k < 4:
            return turned.at[k], turned_out.at[k, :, span(c, ALL)]
        part = (3, 1 - c, 2)[k - 4]
        return right.at[part], right_out.at[part, span(c, ALL)]

    def share_give(k):
        return remote(*share_parts(k), share_send.at[k], share_recv.at[k], sibling)

    def right_keep(k):
        return pltpu.make_async_copy(right.at[k], right_out.at[k, span(c, ALL)], share_local.at[4 + k])

    def turned_keep(k):
        return pltpu.make_async_copy(*share_parts(k), share_local.at[k])

    def share_if(k, giving, run):
        if k in (1, 4, 6):
            taker = 0 if k == 6 else 1
            pl.when(c == (1 - taker if giving else taker))(run)
        else:
            run()

    def share(k):
        share_if(k, True, lambda: share_give(k).start())

    def share_wait():
        for k in range(7):
            share_if(k, True, lambda k=k: share_give(k).wait_send())
            share_if(k, False, lambda k=k: share_give(k).wait_recv())
        for k in range(4):
            turned_keep(k).wait()
            right_keep(k).wait()

    def flush(k):
        return pltpu.make_async_copy(*flushed[k], flush_sem.at[k])

    def set_act(place_t):
        def by_line(yy):
            value = act_f32[yy].reshape(LINE, C)
            left, right = shifted(value)
            spot_rows = pl.ds(pl.multiple_of((yy + 1) * LINE, LINE), LINE)
            act[0, spot_rows] = left.astype(BF16)
            act[1, spot_rows] = value.astype(BF16)
            act[2, spot_rows] = right.astype(BF16)

        each(RES, by_line)

        def turn(yy):
            value = act_f32[pl.ds(2 * yy, 2)].reshape(2 * LINE, C)
            turned[place_t, :, span(yy, 2 * LINE)] = value.T.astype(BF16)

        each(RES // 2, turn)

    def activate(which, n, value):
        sigma = jax.nn.sigmoid(value)
        act_f32[:, n] = (value * sigma).reshape(RES, RES, C)
        slopes[which, :, n] = (sigma * (1.0 + value * (1.0 - sigma))).reshape(RES, RES, C)

    def norm_a():
        for k in range(n_head - 1):
            vec_copy(k).wait()
        vecs_ref[...] = jnp.concatenate([vec_all[k].astype(F32) for k in range(n_head)], axis=-1)

        images_copy().wait()

        def get(n):
            return images_ref[span(n, PIX)].astype(F32)

        mean, inverse = stats_ref.at[0], stats_ref.at[1]
        norm_stats(get, mean, inverse, sums_ref, groups)

        def to_act(n):
            value = (get(n) - mean[row(n)]) * inverse[row(n)]
            activate(0, n, value * vecs_ref[0:1] + vecs_ref[1:2])
            conv_ref[:, n] = jnp.broadcast_to(vecs_ref[2:3].reshape(1, 1, C), (RES, RES, C))
            resid_ref[:, n] = (get(n) + vecs_ref[5:6]).reshape(RES, RES, C)

        each(SLOTS, to_act)
        set_act(3)
        flush(1).start()
        turned_keep(3).start()
        share(3)

    def embed():
        for k in range(n_dp - 1):
            ids_copy(k).wait()
        ids = all_ids[...].reshape(n_dp * SLOTS, 128)
        table = class_ref.shape[1]
        label_hot = lax.broadcasted_iota(jnp.int32, (n_dp * SLOTS, table), 1) == ids[:, 0:1]
        levels = noise_table.shape[0]
        level_hot = lax.broadcasted_iota(jnp.int32, (n_dp * SLOTS, levels), 1) == ids[:, 1:2]
        pre = dot_nt(jnp.where(label_hot, 1.0, 0.0).astype(BF16), class_ref[...])
        width = class_table.shape[0]
        place_of = lax.broadcasted_iota(jnp.int32, (C, 128), 0) - d * width
        lane = lax.broadcasted_iota(jnp.int32, (C, 128), 1)
        chosen = jnp.logical_and(place_of == lane, lane < width)
        noise = dot(noise_table[...], jnp.where(chosen, 1.0, 0.0).astype(BF16)).astype(BF16)
        pre += dot(jnp.where(level_hot, 1.0, 0.0).astype(BF16), noise)
        pre_ref[...] = pre
        part = dot(silu(pre).astype(BF16), modw_ref[...])
        for k in range(n_dp):
            mine = part[k * SLOTS : (k + 1) * SLOTS]
            mod_part[k] = jnp.concatenate([mine[:, :C], mine[:, C:]], axis=0).astype(BF16)
        mod_got[d] = mod_part[d]
        for k in range(n_dp - 1):
            mod_copy(k).start()

    def norm_b():
        for k in range(n_dp - 1):
            mod_copy(k).wait()
        bias = modb_ref[...].astype(F32)
        total = jnp.concatenate([jnp.broadcast_to(bias[k : k + 1], (SLOTS, C)) for k in range(2)], axis=0)
        for k in range(n_dp):
            total += mod_got[k].astype(F32)
        mod_ref[...] = total.astype(BF16).astype(F32)

        def get(n):
            return conv_ref[:, n].reshape(PIX, C)

        mean, inverse = stats_ref.at[2], stats_ref.at[3]
        norm_stats(get, mean, inverse, sums_ref, groups)

        def to_act(n):
            value = (get(n) - mean[row(n)]) * inverse[row(n)]
            value = value * vecs_ref[3:4] + vecs_ref[4:5]
            value = mod_ref[row(SLOTS + n)] + value * (mod_ref[row(n)] + 1.0)
            activate(1, n, value)

        each(SLOTS, to_act)
        set_act(2)
        flush(0).start()
        flush(2).start()
        turned_keep(2).start()
        share(2)

    def residual(n):
        return resid_ref[:, n].reshape(PIX, C)

    def normed(n):
        return (residual(n) - stats_ref[4, row(n)]) * stats_ref[5, row(n)]

    def transpose_out(source, place_t):
        def turn(k):
            value = source[span(k, 2 * LINE)].astype(F32)
            turned[place_t, :, span(k, 2 * LINE)] = value.T.astype(BF16)

        each(ALL // (2 * LINE), turn)

    def live(n):
        slots = counts_ref[0, d * n_head + h] + counts_ref[1, d * n_head + h]
        return jnp.where(n < slots, 1.0, 0.0)

    def norm_c():
        cot_copy().wait()
        norm_stats(residual, stats_ref.at[4], stats_ref.at[5], sums_ref, groups)
        sums_out[...] = jnp.zeros_like(sums_out)

        def prepare(n):
            attn_in[span(n, PIX)] = (normed(n) * vecs_ref[6:7] + vecs_ref[7:8]).astype(BF16)
            grad = cot_ref[span(n, PIX)].astype(F32) * live(n)
            right[3, span(n, PIX)] = grad.astype(BF16)
            sums_out[8:9] += sum_rows(grad)

        each(SLOTS, prepare)
        transpose_out(attn_in, 0)
        turned_keep(0).start()
        right_keep(3).start()
        share(0)
        share(4)

    def attention():
        unit = tuple(whole_ref.at[9 + t // 2, t % 2] for t in range(4))
        for t in range(4):
            for n in range(CHUNKS):
                if t < 3:
                    value = dot(attn_in[...], weight_cols(unit[t], n))
                else:
                    value = dot_nt(right[3], weight_rows(unit[3], n))
                qkv[t, :, chunk(n)] = value.astype(BF16)
        factor = DH ** (-0.5)
        band = lax.broadcasted_iota(jnp.int32, (PIX, BAND), 1) // DH
        heads_at_once = BAND // DH

        def stack(value):
            zero = jnp.zeros_like(value)
            return jnp.concatenate([jnp.where(band == k, value, zero) for k in range(heads_at_once)], axis=0)

        def pick(value):
            out = value[:PIX]
            for k in range(1, heads_at_once):
                out = jnp.where(band == k, value[k * PIX : (k + 1) * PIX], out)
            return out

        def attend(n):
            for b in range(C // BAND):
                query, key, value, grad = (qkv[t, span(n, PIX), slice(b * BAND, (b + 1) * BAND)] for t in range(4))
                query4, grad4 = stack(query), stack(grad)
                scores = dot_nt(key, query4) * factor
                weight = jnp.exp(scores - jnp.max(scores, axis=0, keepdims=True))
                probs = weight / jnp.sum(weight, axis=0, keepdims=True)
                probs_low = probs.astype(BF16)
                low[span(n, PIX), slice(b * BAND, (b + 1) * BAND)] = pick(dot_tn(probs_low, value)).astype(BF16)
                grad_probs = dot_nt(value, grad4)
                inner_sum = jnp.sum(grad_probs * probs, axis=0, keepdims=True)
                grad_scores = (probs * (grad_probs - inner_sum)).astype(BF16)
                right[0, span(n, PIX), slice(b * BAND, (b + 1) * BAND)] = (pick(dot_tn(grad_scores, key)) * factor).astype(BF16)
                right[1, span(n, PIX), slice(b * BAND, (b + 1) * BAND)] = (dot(grad_scores, query4) * factor).astype(BF16)
                right[2, span(n, PIX), slice(b * BAND, (b + 1) * BAND)] = dot(probs_low, grad4).astype(BF16)

        def attend_two(m):
            attend(2 * m)
            attend(2 * m + 1)

        each(SLOTS // 2, attend_two)
        share(5)
        share(6)
        for k in range(3):
            right_keep(k).start()
        transpose_out(low, 1)
        turned_keep(1).start()
        share(1)
        for n in range(CHUNKS):
            value = dot_nt(right[0], weight_rows(unit[0], n))
            value += dot_nt(right[1], weight_rows(unit[1], n))
            value += dot_nt(right[2], weight_rows(unit[2], n))
            act_f32[:, :, :, chunk(n)] = value.reshape(SLOTS, RES, RES, WIDTH)

        def back(n):
            grad = act_f32[n].reshape(PIX, C)
            pair_ref[row(n)] = sum_rows(grad * normed(n))
            pair_ref[row(SLOTS + n)] = sum_rows(grad)

        each(SLOTS, back)
        sums_out[6:7] = sum_rows(pair_ref[0:SLOTS])
        sums_out[7:8] = sum_rows(pair_ref[SLOTS:])
        pair_ref[...] = group_mean(pair_ref[...] * vecs_ref[6:7], groups)

        def back_second(n):
            inverse = stats_ref[5, row(n)]
            value = act_f32[n].reshape(PIX, C) * (vecs_ref[6:7] * inverse)
            value -= normed(n) * (pair_ref[row(n)] * inverse) + pair_ref[row(SLOTS + n)] * inverse
            value += right[3, span(n, PIX)].astype(F32)
            conv_ref[:, n] = value.reshape(RES, RES, C)
            sums_out[5:6] += sum_rows(value.astype(BF16).astype(F32))

        flush(0).wait()
        each(SLOTS, back_second)
        flush(4).start()

        def lower(yy):
            attn_in[span(yy, LINE)] = conv_ref[yy].reshape(LINE, C).astype(BF16)

        each(RES, lower)
        flush(5).start()
        for n in range(CHUNKS):
            value = dot(low[...], weight_cols(unit[3], n))
            act_f32[:, :, :, chunk(n)] = value.reshape(SLOTS, RES, RES, WIDTH)

        def finish_out(n):
            value = residual(n) + act_f32[n].reshape(PIX, C) + vecs_ref[8:9]
            low[span(n, PIX)] = (value * live(n)).astype(BF16)

        each(SLOTS, finish_out)
        flush(3).start()

    swap_start()
    images_copy().start()
    set_groups(groups)
    cot_copy().start()
    one = [ref[...].astype(F32).reshape(1, cols_own) for ref in vectors]
    vec_ref[...] = jnp.concatenate(one + [jnp.zeros((16 - VECTORS, cols_own), F32)], axis=0).astype(BF16)
    lane = lax.broadcasted_iota(jnp.int32, (1, 128), 1)
    for n in range(SLOTS):
        ids_ref[n : n + 1] = jnp.where(lane == 0, labels_ref[n], levels_ref[n])
    for k in range(n_head - 1):
        vec_copy(k).start()
    for k in range(n_dp - 1):
        ids_copy(k).start()
    width = class_table.shape[0]
    class_ref[...] = jnp.zeros_like(class_ref)
    class_ref[0:width, 0 : class_table.shape[1]] = class_table[...]
    modw_ref[...] = jnp.zeros_like(modw_ref)
    table = modw_table[...].astype(F32)
    for k in range(2):
        modw_ref[0:width, k * C : (k + 1) * C] = table[:, k].astype(BF16)
    vec_all[h] = vec_ref[...]
    all_ids[d] = ids_ref[...]
    edge = jnp.zeros((LINE, C), BF16)
    for j in range(3):
        act[j, 0:LINE] = edge
        act[j, ALL + LINE : ALL + 2 * LINE] = edge
    swap_wait(0)
    begin(0)
    for k in range(1, 5):
        swap_wait(k)
    for i in (10, 9):
        join(i)
        far_begin(i)
    begin(1)
    z_relay(0)
    begin(2)
    spread_line(0)
    for i in (10, 9):
        far_pass(i)
    begin(3)
    z_relay(1)
    norm_a()
    spread_line(1)
    pass_on(0)
    begin(4)
    z_relay(2)
    embed()
    spread_line(2)
    pass_on(1)
    finish(0)
    begin(5)
    z_relay(3)
    begin(6)
    z_relay(4)
    far_line(10)
    spread_line(3)
    pass_on(2)
    finish(1)
    fetch(0)

    def body(turn, carry):
        @pl.when(turn < 6)
        def _():
            begin(turn + 3)

        @pl.when(turn == 6)
        def _():
            far_line(9)
            z_relay(10)

        z_relay(turn + 1)
        spread_line(turn)
        pass_on(turn - 1)
        finish(turn - 2)
        fetch(turn - 3)
        use_pair(conv_ref, turn - 4, 0)
        return carry

    lax.fori_loop(4, 8, body, 0)
    spread_line(8)
    pass_on(7)
    finish(6)
    fetch(5)
    product(conv_ref, 8, 4, 0)
    norm_b()
    product(resid_ref, 8, 4, 1)
    pass_on(8)
    finish(7)
    z_relay(9)
    fetch(6)
    far_finish(10)
    use_pair(resid_ref, 5, 5)
    finish(8)
    fetch(7)
    use_pair(resid_ref, 6, 5)
    fetch(8)
    use_pair(resid_ref, 7, 5)
    far_finish(9)
    use_pair(resid_ref, 8, 5)
    norm_c()
    fetch(9)
    fetch(10)
    attention()

    def drain(i):
        z_drain(i)
        for part in range(2):
            x_copy(i, part).wait_send()
            y_copy(i, part).wait_send()
        for part in range(4):
            s_copy(i, part).wait_send()

    each(FAR, drain)
    drain(9)
    drain(10)
    for k in range(1, len(flushed)):
        flush(k).wait()
    each(FAR, lambda i: unit_copy(i).wait())
    share_wait()


def run_forward(weights, images, cotangent, counts, labels, levels, class_table, noise_table, modw, modb, vectors):
    n_dp, n_head = lax.axis_size("dp"), lax.axis_size("head")
    rows, cols = weights[0].shape[1:]
    lines, across, wide = n_dp // 2, n_head // 2, 2 * cols
    board = (RES, SLOTS, RES, C)
    shape = jax.ShapeDtypeStruct
    return pl.pallas_call(
        functools.partial(forward_kernel, lines),
        out_shape=(
            shape((FAR, 2, lines, 2, rows, across * wide), BF16),
            shape(board, F32),
            shape((2,) + board, F32),
            shape((4, C, 2 * ALL), BF16),
            shape((ALL, C), BF16),
            shape(board, F32),
            shape((ALL, C), BF16),
            shape((4, 2 * ALL, C), BF16),
            shape((16, C), F32),
            shape((2 * SLOTS, C), F32),
            shape((6, SLOTS, C), F32),
            shape((n_dp * SLOTS, 128), F32),
            shape((n_dp, SLOTS, 128), jnp.int32),
            shape((16, C), F32),
        ),
        in_specs=[ANY] * 6 + [SMEM] * 3 + [VMEM] * (4 + VECTORS),
        out_specs=(ANY,) * 8 + (VMEM,) * 6,
        scratch_shapes=[
            pltpu.VMEM((2, PAIRS, rows, cols), BF16),
            pltpu.VMEM((PAIRS, 2, lines, 2, rows, across * wide), BF16),
            pltpu.VMEM((16, cols), BF16),
            pltpu.VMEM((SLOTS, 128), jnp.int32),
            pltpu.VMEM((128, 1024), BF16),
            pltpu.VMEM((128, 2 * C), BF16),
            pltpu.VMEM((n_head, 16, cols), BF16),
            pltpu.VMEM((n_dp, 2 * SLOTS, C), BF16),
            pltpu.VMEM((n_dp, 2 * SLOTS, C), BF16),
            pltpu.VMEM((3, ALL + 2 * LINE, C), BF16),
            pltpu.VMEM(board, F32),
            pltpu.VMEM((SLOTS, C), F32),
            pltpu.VMEM(board, F32),
            pltpu.VMEM(board, F32),
            pltpu.VMEM((2,) + board, F32),
            pltpu.VMEM((4, C, ALL), BF16),
            pltpu.VMEM((ALL, C), BF16),
            pltpu.VMEM((4, ALL, C), BF16),
            pltpu.VMEM((4, ALL, C), BF16),
            pltpu.VMEM((ALL, C), BF16),
            pltpu.VMEM((2 * SLOTS, C), F32),
            pltpu.VMEM((C, 128), BF16),
            pltpu.VMEM((128, C), BF16),
            DMA((5,)),
            DMA((5,)),
            DMA((5,)),
            DMA((PAIRS, lines - 1)),
            DMA((PAIRS, lines - 1)),
            DMA((PAIRS,)),
            DMA((PAIRS, 2)),
            DMA((PAIRS, 2)),
            DMA((PAIRS, 2)),
            DMA((PAIRS, 2)),
            DMA((PAIRS, 4)),
            DMA((PAIRS, 4)),
            DMA((n_head - 1,)),
            DMA((n_head - 1,)),
            DMA((n_dp - 1,)),
            DMA((n_dp - 1,)),
            DMA((n_dp - 1,)),
            DMA((n_dp - 1,)),
            DMA((FAR,)),
            DMA((6,)),
            DMA((2,)),
            DMA((8,)),
            DMA((7,)),
            DMA((7,)),
        ],
        compiler_params=pltpu.CompilerParams(
            collective_id=0, has_side_effects=True, vmem_limit_bytes=62 * 2**20
        ),
        name="gather_forward",
    )(
        *weights,
        images,
        cotangent,
        counts,
        labels,
        levels,
        class_table,
        noise_table,
        modw,
        modb,
        *vectors,
    )


BACK_FAR = (10, 8)
BACK_NEAR = tuple(i for i in range(PAIRS) if i not in BACK_FAR)


def backward_kernel(
    lines,
    whole_ref,
    turned_ref,
    right_ref,
    grad_low_ref,
    grad_resid_ref,
    conv_ref,
    slopes_ref,
    images_hbm,
    stats_ref,
    vecs_ref,
    mod_ref,
    sums_in,
    pre_ref,
    ids_ref,
    modw_table,
    out_a,
    out_b,
    out_qkv,
    out_proj,
    image_ref,
    class_ref,
    modw_out,
    modb_out,
    vec_out,
    mine,
    from_x,
    from_y,
    from_z,
    far_x,
    far_y,
    far_z,
    ends,
    modw_ref,
    lefts,
    rights,
    grads,
    stage,
    stage_mine,
    weights,
    total,
    board,
    slopes,
    sums_ref,
    pair_ref,
    coef_ref,
    group_sum,
    group_back,
    gm_mine,
    gm_all,
    mw_mine,
    mw_got,
    ge_all,
    vs_mine,
    vs_got,
    vt_mine,
    vt_all,
    x_send,
    x_recv,
    y_send,
    y_recv,
    z_send,
    z_recv,
    p_send,
    p_recv,
    e_send,
    e_recv,
    e_local,
    op_send,
    op_recv,
    op_local,
    load_sem,
    in_sem,
    out_sem,
    gm_send,
    gm_recv,
    mw_send,
    mw_recv,
    ge_send,
    ge_recv,
    vs_send,
    vs_recv,
    vt_send,
    vt_recv,
):
    z, y, x, c = place()
    d, h = lax.axis_index("dp"), lax.axis_index("head")
    n_dp, n_head = lines * 2, 4
    half = lines // 2
    inner = jnp.logical_and(z > 0, z < lines - 1)
    rows, wide = from_z.shape[2], from_z.shape[3]
    cols = wide // 2
    sibling = at_chip(z, y, x, 1 - c)
    along_x = at_chip(z, y, 1 - x, c)
    along_y = at_chip(z, 1 - y, x, c)
    line = [at_chip(lax.rem(z + k, lines), y, x, c) for k in range(1, lines)]
    column, heads = column_peers(n_dp), head_peers(n_head)

    own_rows = pl.ds(LINE, ALL)

    def op_own(k):
        source, place_of = (
            (right_ref.at[2 + c], rights.at[0]),
            (turned_ref.at[c], lefts.at[1]),
            (right_ref.at[c], rights.at[1]),
            (turned_ref.at[0], lefts.at[0]),
            (grad_low_ref, grads.at[1, c, own_rows]),
            (turned_ref.at[2], lefts.at[2]),
            (turned_ref.at[3], lefts.at[3]),
        )[k]
        return pltpu.make_async_copy(source, place_of, op_local.at[k])

    def low_copy():
        return remote(grad_low_ref, grads.at[1, c, own_rows], op_send.at[0], op_recv.at[0], sibling)

    def stage_copy():
        return remote(stage_mine, stage, op_send.at[1], op_recv.at[1], sibling)

    def lanes(xx):
        return span(xx, wide)

    first, second = pl.ds(0, rows // 2), pl.ds(rows // 2, rows // 2)

    def is_far(i):
        return i in BACK_FAR

    def x_copy(i, part):
        if is_far(i):
            into = far_x.at[BACK_FAR.index(i)]
            if part == 0:
                src, dst = mine.at[i, z, 1 - y, second, lanes(1 - x)], into.at[pl.ds(rows, rows // 2)]
            else:
                src, dst = mine.at[i, z, y, :, lanes(1 - x)], into.at[pl.ds(0, rows)]
        elif part == 0:
            src, dst = mine.at[i, pl.ds(half, half), 1 - y, :, lanes(1 - x)], from_x.at[BACK_NEAR.index(i), pl.ds(lines, half)]
        else:
            src, dst = mine.at[i, :, y, :, lanes(1 - x)], from_x.at[BACK_NEAR.index(i), pl.ds(0, lines)]
        return remote(src, dst, x_send.at[i, part], x_recv.at[i, part], along_x)

    def y_copy(i, part):
        if is_far(i):
            into = far_y.at[BACK_FAR.index(i)]
            if part == 0:
                src, dst = mine.at[i, z, 1 - y, first, lanes(1 - x)], into.at[pl.ds(rows, rows // 2)]
            else:
                src, dst = mine.at[i, z, 1 - y, :, lanes(x)], into.at[pl.ds(0, rows)]
        elif part == 0:
            src, dst = mine.at[i, pl.ds(0, half), 1 - y, :, lanes(1 - x)], from_y.at[BACK_NEAR.index(i), pl.ds(lines, half)]
        else:
            src, dst = mine.at[i, :, 1 - y, :, lanes(x)], from_y.at[BACK_NEAR.index(i), pl.ds(0, lines)]
        return remote(src, dst, y_send.at[i, part], y_recv.at[i, part], along_y)

    beyond = lax.rem(z + 2, lines)
    opposite = lines - 1 - z
    near_end = at_chip(1 + z // (lines - 1), y, x, c)

    def z_block(i, zz):
        return mine.at[i, zz] if is_far(i) else mine.at[i, zz, y, :, lanes(x)]

    def z_slot(i, k):
        return far_z.at[BACK_FAR.index(i), k] if is_far(i) else from_z.at[BACK_NEAR.index(i), k]

    def z_copy(i, k):
        return remote(
            z_block(i, lax.rem(z + k + 1, lines)), z_slot(i, k), z_send.at[i, k], z_recv.at[i, k], line[k]
        )

    def z_give(i):
        return remote(z_block(i, opposite), z_slot(i, 3), p_send.at[i], p_recv.at[i], near_end)

    def z_start(i):
        @pl.when(jnp.logical_not(inner))
        def _():
            z_give(i).start()

        @pl.when(z < lines - 1)
        def _():
            z_copy(i, 0).start()

        @pl.when(z > 0)
        def _():
            z_copy(i, 2).start()

        @pl.when(jnp.logical_not(inner))
        def _():
            z_copy(i, 1).start()

    def z_mix(i):
        @pl.when(inner)
        def _():
            z_give(i).wait_recv()
            if is_far(i):
                mine[i, beyond] += far_z[BACK_FAR.index(i), 3]
            else:
                mine[i, beyond, y, :, lanes(x)] += from_z[BACK_NEAR.index(i), 3]
            z_copy(i, 1).start()

    def z_wait(i):
        z_copy(i, 1).wait_recv()

        @pl.when(z > 0)
        def _():
            z_copy(i, 0).wait_recv()

        @pl.when(z < lines - 1)
        def _():
            z_copy(i, 2).wait_recv()

    def z_drain(i):
        z_copy(i, 1).wait_send()

        @pl.when(z < lines - 1)
        def _():
            z_copy(i, 0).wait_send()

        @pl.when(z > 0)
        def _():
            z_copy(i, 2).wait_send()

        @pl.when(jnp.logical_not(inner))
        def _():
            z_give(i).wait_send()

    def target(i, core):
        if isinstance(i, int) and i == 10:
            return out_proj if core == 1 else out_qkv.at[2]
        if isinstance(i, int) and i == 9:
            return out_qkv.at[core]
        if isinstance(i, int) and i == 4:
            return out_b.at[8] if core == 1 else out_a.at[8]
        if isinstance(i, int) and i > 4:
            return out_b.at[4 * core + i - 5]
        return out_a.at[4 * core + i]

    def e_copy(i, core):
        return remote(ends.at[1 - c, i], target(i, core), e_send.at[i], e_recv.at[i], sibling)

    def e_own(i, core):
        return pltpu.make_async_copy(ends.at[c, i], target(i, core), e_local.at[i])

    def finish(i, value):
        for cc in range(2):
            ends[cc, i] = value[:, cc * cols : (cc + 1) * cols]
        if i in (4, 10):
            for core in range(2):

                @pl.when(c == core)
                def _():
                    e_copy(i, core).start()
                    e_own(i, core).start()
        else:
            e_copy(i, c).start()
            e_own(i, c).start()

    def offer(i):
        x_copy(i, 0).start()
        y_copy(i, 0).start()

    def relay(i):
        x_copy(i, 0).wait_recv()
        y_copy(i, 0).wait_recv()
        if is_far(i):
            rest = pl.ds(rows, rows // 2)
            mine[i, z, y, first, lanes(1 - x)] += far_y[BACK_FAR.index(i), rest]
            mine[i, z, 1 - y, second, lanes(x)] += far_x[BACK_FAR.index(i), rest]
        else:
            for j in range(half):
                mine[i, j, y, :, lanes(1 - x)] += from_y[BACK_NEAR.index(i), lines + j]
                mine[i, half + j, 1 - y, :, lanes(x)] += from_x[BACK_NEAR.index(i), lines + j]
        x_copy(i, 1).start()
        y_copy(i, 1).start()

    def collect(i):
        x_copy(i, 1).wait_recv()
        y_copy(i, 1).wait_recv()
        if is_far(i):
            whole_rows = pl.ds(0, rows)
            value = mine[i, z, y, :, lanes(x)].astype(F32)
            value += far_x[BACK_FAR.index(i), whole_rows].astype(F32) + far_y[BACK_FAR.index(i), whole_rows].astype(F32)
            finish(i, value)
            return

        def add(j):
            value = mine[i, j, y, :, lanes(x)].astype(F32)
            value += from_x[BACK_NEAR.index(i), j].astype(F32) + from_y[BACK_NEAR.index(i), j].astype(F32)
            mine[i, j, y, :, lanes(x)] = value.astype(BF16)

        each(lines, add)
        z_start(i)

    def last(i):
        z_wait(i)
        if is_far(i):
            for yy in range(2):
                value = mine[i, z, yy].astype(F32)
                for k in range(lines - 1):
                    value += far_z[BACK_FAR.index(i), k, yy].astype(F32)
                mine[i, z, yy] = value.astype(BF16)
            offer(i)
            return
        value = mine[i, z, y, :, lanes(x)].astype(F32)
        for k in range(lines - 1):
            value += from_z[BACK_NEAR.index(i), k].astype(F32)
        finish(i, value)

    def put(i, n, value):
        mine[i, :, :, :, chunk(n)] = value.astype(BF16).reshape(mine.shape[1:4] + (WIDTH,))

    def plain_unit(i, left, right):
        for n in range(CHUNKS):
            put(i, n, dot(lefts[left], rights[right, :, chunk(n)]))

    def conv_unit(i, left, tap):
        where, side = lines_from(2 - tap // 3), 2 - tap % 3
        for n in range(CHUNKS):
            both = jnp.concatenate([grads[side, core, where, chunk(n)] for core in range(2)], axis=0)
            put(i, n, dot(lefts[left], both))

    def extra_b():
        @pl.when(c == 1)
        def _():
            conv_unit(4, 2, 8)

    def extra_a():
        @pl.when(c == 0)
        def _():
            conv_unit(4, 3, 8)

    def spread_sides(core):
        def by_line(yy):
            value = grads[1, core, pl.ds(pl.multiple_of((yy + 1) * LINE, LINE), LINE)].astype(F32)
            left, right = shifted(value)
            spot_rows = pl.ds(pl.multiple_of((yy + 1) * LINE, LINE), LINE)
            grads[0, core, spot_rows] = left.astype(BF16)
            grads[2, core, spot_rows] = right.astype(BF16)

        each(RES, by_line)

    def load(tap, base):
        ninth = tap // 8
        i = (base // 2 + tap % 4) * (1 - ninth) + 4 * ninth
        k = (tap // 4) % 2 + (base // 10) * ninth
        slot = (tap // 3) % 2 * 3 + tap % 3
        return pltpu.make_async_copy(whole_ref.at[i, k], weights.at[slot], load_sem.at[slot])

    def load_three(group, base):
        for j in range(3):
            load(3 * group + j, base).start()

    def conv_back_range(first_tap, base):
        group = first_tap // 3
        for j in range(3):
            load(first_tap + j, base).wait()
        if group < 2:
            load_three(group + 1, base)
        slot = group % 2 * 3
        part = jnp.concatenate([grads[2 - j, c, lines_from(2 - group)] for j in range(3)], axis=1)
        for n in range(CHUNKS):
            three = jnp.concatenate([weight_rows(weights.at[slot + j], n) for j in range(3)], axis=1)
            value = dot_nt(part, three).reshape(RES, SLOTS, RES, WIDTH)
            if group == 0:
                total[:, :, :, chunk(n)] = value
            else:
                total[:, :, :, chunk(n)] += value

    def slope(values):
        sigma = jax.nn.sigmoid(values)
        return sigma * (1.0 + values * (1.0 - sigma))

    for k in (0, 2):
        from_z[:, k] = jnp.zeros_like(from_z[:, k])
        far_z[:, k] = jnp.zeros_like(far_z[:, k])
    greet(column + heads)
    low_copy().start()
    for k in (4, 0, 1, 2, 3, 5):
        op_own(k).start()
    load_three(0, 10)
    groups = (group_sum, group_back)
    set_groups(groups)

    def fetch(k):
        source, target = (
            (conv_ref, board),
            (slopes_ref.at[1], slopes),
            (slopes_ref.at[0], slopes),
            (grad_resid_ref, board),
            (images_hbm, stage_mine),
        )[k]
        return pltpu.make_async_copy(source, target, in_sem.at[k])

    fetch(0).start()
    fetch(1).start()
    vs_mine[...] = jnp.zeros_like(vs_mine)
    edge = jnp.zeros((LINE, C), BF16)
    for j in range(3):
        for core in range(2):
            grads[j, core, 0:LINE] = edge
            grads[j, core, ALL + LINE : ALL + 2 * LINE] = edge
    sums_ref[...] = sums_in[...]
    modw_ref[...] = jnp.zeros_like(modw_ref)
    table = modw_table[...].astype(F32)
    for k in range(2):
        modw_ref[0:rows, k * C : (k + 1) * C] = table[:, k].astype(BF16)

    def norm_b_value(n):
        return (board[:, n].reshape(PIX, C) - stats_ref[2, row(n)]) * stats_ref[3, row(n)]

    def norm_a_value(n):
        return (stage_mine[span(n, PIX)].astype(F32) - stats_ref[0, row(n)]) * stats_ref[1, row(n)]

    def back_sums(get):
        def body(n):
            grad = (total[:, n] * slopes[:, n]).reshape(PIX, C)
            total[:, n] = grad.reshape(RES, RES, C)
            pair_ref[row(n)] = sum_rows(grad * get(n))
            pair_ref[row(SLOTS + n)] = sum_rows(grad)

        each(SLOTS, body)

    def back_factors(factor, inverse):
        coef_ref[0:SLOTS] = factor * inverse
        means = group_mean(pair_ref[...] * jnp.concatenate([factor, factor], axis=0), groups)
        coef_ref[SLOTS : 2 * SLOTS] = means[:SLOTS] * inverse
        coef_ref[2 * SLOTS :] = means[SLOTS:] * inverse

    def back_value(n, get):
        value = total[:, n].reshape(PIX, C) * coef_ref[row(n)]
        return value - get(n) * coef_ref[row(SLOTS + n)] - coef_ref[row(2 * SLOTS + n)]

    def gm_copy(k):
        return remote(gm_mine, gm_all.at[d], gm_send.at[k], gm_recv.at[k], column[k])

    def mw_copy(k):
        return remote(
            mw_mine.at[lax.rem(h + k + 1, n_head)], mw_got.at[k], mw_send.at[k], mw_recv.at[k], heads[k]
        )

    def ge_copy(k):
        return remote(ge_all.at[h], ge_all.at[h], ge_send.at[k], ge_recv.at[k], heads[k])

    def vs_copy(k):
        return remote(
            vs_mine.at[lax.rem(h + k + 1, n_head)], vs_got.at[k], vs_send.at[k], vs_recv.at[k], heads[k]
        )

    def vt_copy(k):
        return remote(vt_mine, vt_all.at[d], vt_send.at[k], vt_recv.at[k], column[k])

    def image_copy(n):
        return pltpu.make_async_copy(total.at[:, n], image_ref.at[n], out_sem.at[n])

    count = n_dp * SLOTS

    def start():
        op_own(0).wait()
        op_own(1).wait()

    def dw(i):
        if i == 10:
            plain_unit(10, 1, 0)
        elif i == 9:
            op_own(2).wait()
            op_own(3).wait()
            plain_unit(9, 0, 1)
        elif i > 4:
            conv_unit(i, 2, 4 * c + i - 5)
        else:
            conv_unit(i, 3, 4 * c + i)

    def sides():
        op_own(4).wait()
        low_copy().wait_recv()
        op_own(5).wait()
        spread_sides(0)
        spread_sides(1)

    def back_b_first():
        load_three(0, 0)
        op_own(6).start()
        fetch(0).wait()
        fetch(1).wait()
        back_sums(norm_b_value)
        alone, with_norm = pair_ref[SLOTS:], pair_ref[:SLOTS]
        scale = mod_ref[0:SLOTS] + 1.0
        gm_mine[...] = jnp.concatenate([vecs_ref[3:4] * with_norm + vecs_ref[4:5] * alone, alone], axis=0).astype(BF16)
        gm_all[d] = gm_mine[...]
        for k in range(n_dp - 1):
            gm_copy(k).start()
        sums_ref[3:4] = sum_rows(with_norm * scale)
        sums_ref[4:5] = sum_rows(alone * scale)
        back_factors(scale * vecs_ref[3:4], stats_ref[3])

    def back_b_second():
        fetch(2).start()

        def body(n):
            value = back_value(n, norm_b_value).astype(BF16).astype(F32)
            sums_ref[2:3] += sum_rows(value)
            total[:, n] = value.reshape(RES, RES, C)

        each(SLOTS, body)
        fetch(3).start()

    def lower():
        def by_line(yy):
            stage_mine[span(yy, LINE)] = total[yy].reshape(LINE, C).astype(BF16)

        each(RES, by_line)
        stage_copy().start()

    def take():
        stage_copy().wait_recv()

        def by_line(yy):
            spot_rows = pl.ds(pl.multiple_of((yy + 1) * LINE, LINE), LINE)
            grads[1, c, spot_rows] = stage_mine[span(yy, LINE)]
            grads[1, 1 - c, spot_rows] = stage[span(yy, LINE)]

        each(RES, by_line)
        spread_sides(0)
        spread_sides(1)
        stage_copy().wait_send()
        fetch(4).start()
        op_own(6).wait()

    def modulation():
        for k in range(n_dp - 1):
            gm_copy(k).wait()
        parts = gm_all[...].astype(F32)
        gm_scale = parts[:, :SLOTS].reshape(count, C)
        gm_offset = parts[:, SLOTS:].reshape(count, C)
        pre = pre_ref[...]
        emb = silu(pre).astype(BF16)
        part_rows = rows // n_head
        for k, value in ((0, gm_scale), (1, gm_offset)):
            low_value = value.astype(BF16)
            grad_w = dot_tn(emb, low_value)
            place_lanes = slice(k * C, (k + 1) * C)
            for hh in range(n_head):
                mw_mine[hh, 0:part_rows, place_lanes] = grad_w[hh * part_rows : (hh + 1) * part_rows]
                mw_mine[hh, part_rows : part_rows + 8, place_lanes] = jnp.broadcast_to(sum_rows(value), (8, C))
        grad_e = dot_nt(gm_scale.astype(BF16), modw_ref[:, :C]) + dot_nt(gm_offset.astype(BF16), modw_ref[:, C:])
        grad_e = grad_e * slope(pre)
        label = ids_ref[...].reshape(count, 128)[:, 0:1].astype(F32)
        lane = lax.broadcasted_iota(jnp.int32, grad_e.shape, 1)
        ge_all[h] = jnp.where(lane < rows, grad_e, label)
        for k in range(n_head - 1):
            mw_copy(k).start()
            ge_copy(k).start()

    def back_a_first():
        fetch(2).wait()
        fetch(4).wait()
        back_sums(norm_a_value)
        sums_ref[0:1] = sum_rows(pair_ref[:SLOTS])
        sums_ref[1:2] = sum_rows(pair_ref[SLOTS:])
        for hh in range(n_head):
            vs_mine[hh] = sums_ref[:, hh * cols : (hh + 1) * cols]
        for k in range(n_head - 1):
            vs_copy(k).start()
        back_factors(jnp.broadcast_to(vecs_ref[0:1], (SLOTS, C)), stats_ref[1])

    def back_a_second():
        fetch(3).wait()

        def body(n):
            value = back_value(n, norm_a_value).reshape(RES, RES, C)
            total[:, n] = value + board[:, n]
            image_copy(n).start()

        each(SLOTS, body)

    def vec_first():
        value = vs_mine[h]
        for k in range(n_head - 1):
            vs_copy(k).wait()
            value += vs_got[k]
        vt_mine[...] = value
        vt_all[d] = value
        for k in range(n_dp - 1):
            vt_copy(k).start()

    def mod_out():
        value = mw_mine[h]
        for k in range(n_head - 1):
            mw_copy(k).wait()
            value += mw_got[k]
        part_rows = rows // n_head
        first_lane = (d * n_head + h) * part_rows
        for k in range(2):
            lanes_of = slice(k * C, (k + 1) * C)
            modw_out[:, k] = value[:part_rows, lanes_of]
            turned_row = pltpu.roll(value[part_rows:, lanes_of], lax.rem(C - first_lane, C), 1)
            modb_out[k : k + 1] = turned_row[0:1, :part_rows]

    def class_out():
        for k in range(n_head - 1):
            ge_copy(k).wait()
        table = class_ref.shape[1]
        part = rows // n_head
        value = ge_all[...].reshape(n_head * count, 128)
        label = value[:, rows : rows + 1].astype(jnp.int32)
        hot = lax.broadcasted_iota(jnp.int32, (n_head * count, table), 1) == label
        own = pltpu.roll(value, lax.rem(128 - h * part, 128), 1).astype(BF16)
        value = dot_tn(own, jnp.where(hot, 1.0, 0.0).astype(BF16))
        class_ref[...] = value[:part]

    def vec_second():
        for k in range(n_dp - 1):
            vt_copy(k).wait()
        value = vt_all[0]
        for k in range(1, n_dp):
            value += vt_all[k]
        vec_out[...] = value

    start()
    sides()
    dw(5)
    offer(5)
    dw(7)
    offer(7)
    dw(10)
    z_start(10)
    dw(9)
    offer(9)
    dw(6)
    offer(6)
    conv_back_range(0, 10)
    relay(9)
    dw(8)
    z_start(8)
    relay(7)
    conv_back_range(3, 10)
    relay(6)
    conv_back_range(6, 10)
    relay(5)
    back_b_first()
    back_b_second()
    lower()
    z_mix(10)
    extra_b()
    take()
    dw(2)
    offer(2)
    dw(0)
    offer(0)
    dw(3)
    z_mix(8)
    extra_a()
    collect(6)
    relay(2)
    conv_back_range(0, 0)
    collect(5)
    offer(4)
    relay(0)
    dw(1)
    z_mix(6)
    offer(1)
    offer(3)
    collect(7)
    conv_back_range(3, 0)
    collect(2)
    last(8)
    z_mix(5)
    z_mix(2)
    collect(0)
    collect(9)
    relay(4)
    relay(1)
    conv_back_range(6, 0)
    modulation()
    z_mix(9)
    relay(3)
    relay(8)
    collect(4)
    back_a_first()
    z_mix(4)
    z_mix(7)
    z_mix(0)
    class_out()
    last(5)
    collect(1)
    vec_first()
    last(10)
    z_mix(1)
    back_a_second()
    collect(3)
    vec_second()
    last(9)
    relay(10)
    z_mix(3)
    last(4)
    mod_out()
    last(6)
    last(7)
    collect(8)
    last(0)
    last(2)
    collect(10)
    last(1)
    last(3)

    low_copy().wait_send()
    each(SLOTS, lambda n: image_copy(n).wait())

    def drain(i):
        for part in range(2):
            x_copy(i, part).wait_send()
            y_copy(i, part).wait_send()
        z_drain(i)
        e_copy(i, 0).wait()
        e_own(i, 0).wait()

    for i in range(PAIRS):
        drain(i)


def run_backward(whole, turned, right, grad_low, grad_resid, conv_out, slopes, images, stats, vecs, mod, sums, pre, ids, modw, classes):
    n_dp, n_head = lax.axis_size("dp"), lax.axis_size("head")
    _, _, lines, _, rows, depth = whole.shape
    cols = depth // n_head
    wide = 2 * cols
    board = (RES, SLOTS, RES, C)
    shape = jax.ShapeDtypeStruct
    return pl.pallas_call(
        functools.partial(backward_kernel, lines),
        out_shape=(
            shape((9, rows, cols), F32),
            shape((9, rows, cols), F32),
            shape((3, rows, cols), F32),
            shape((rows, cols), F32),
            shape(board, F32),
            shape((rows // n_head, classes), F32),
            shape((rows // n_head, 2, C), F32),
            shape((2, rows // n_head), F32),
            shape((16, cols), F32),
        ),
        in_specs=[ANY] * 8 + [VMEM] * 7,
        out_specs=(ANY,) * 5 + (VMEM,) * 4,
        scratch_shapes=[
            pltpu.VMEM((PAIRS, lines, 2, rows, depth), BF16),
            pltpu.VMEM((len(BACK_NEAR), lines + lines // 2, rows, wide), BF16),
            pltpu.VMEM((len(BACK_NEAR), lines + lines // 2, rows, wide), BF16),
            pltpu.VMEM((len(BACK_NEAR), 4, rows, wide), BF16),
            pltpu.VMEM((len(BACK_FAR), rows + rows // 2, wide), BF16),
            pltpu.VMEM((len(BACK_FAR), rows + rows // 2, wide), BF16),
            pltpu.VMEM((len(BACK_FAR), 4, 2, rows, depth), BF16),
            pltpu.VMEM((2, PAIRS, rows, cols), F32),
            pltpu.VMEM((128, 2 * C), BF16),
            pltpu.VMEM((4, C, 2 * ALL), BF16),
            pltpu.VMEM((2, 2 * ALL, C), BF16),
            pltpu.VMEM((3, 2, ALL + 2 * LINE, C), BF16),
            pltpu.VMEM((ALL, C), BF16),
            pltpu.VMEM((ALL, C), BF16),
            pltpu.VMEM((6, lines, 2, rows, depth), BF16),
            pltpu.VMEM(board, F32),
            pltpu.VMEM(board, F32),
            pltpu.VMEM(board, F32),
            pltpu.VMEM((16, C), F32),
            pltpu.VMEM((2 * SLOTS, C), F32),
            pltpu.VMEM((3 * SLOTS, C), F32),
            pltpu.VMEM((C, 128), BF16),
            pltpu.VMEM((128, C), BF16),
            pltpu.VMEM((2 * SLOTS, C), BF16),
            pltpu.VMEM((n_dp, 2 * SLOTS, C), BF16),
            pltpu.VMEM((n_head, rows // n_head + 8, 2 * C), F32),
            pltpu.VMEM((n_head - 1, rows // n_head + 8, 2 * C), F32),
            pltpu.VMEM((n_head, n_dp * SLOTS, 128), F32),
            pltpu.VMEM((n_head, 16, cols), F32),
            pltpu.VMEM((n_head - 1, 16, cols), F32),
            pltpu.VMEM((16, cols), F32),
            pltpu.VMEM((n_dp, 16, cols), F32),
            DMA((PAIRS, 2)),
            DMA((PAIRS, 2)),
            DMA((PAIRS, 2)),
            DMA((PAIRS, 2)),
            DMA((PAIRS, lines - 1)),
            DMA((PAIRS, lines - 1)),
            DMA((PAIRS,)),
            DMA((PAIRS,)),
            DMA((PAIRS,)),
            DMA((PAIRS,)),
            DMA((PAIRS,)),
            DMA((2,)),
            DMA((2,)),
            DMA((7,)),
            DMA((6,)),
            DMA((5,)),
            DMA((SLOTS,)),
            DMA((n_dp - 1,)),
            DMA((n_dp - 1,)),
            DMA((n_head - 1,)),
            DMA((n_head - 1,)),
            DMA((n_head - 1,)),
            DMA((n_head - 1,)),
            DMA((n_head - 1,)),
            DMA((n_head - 1,)),
            DMA((n_dp - 1,)),
            DMA((n_dp - 1,)),
        ],
        compiler_params=pltpu.CompilerParams(
            collective_id=1, has_side_effects=True, vmem_limit_bytes=64 * 2**20 - 2**18
        ),
        name="backward_scatter",
    )(whole, turned, right, grad_low, grad_resid, conv_out, slopes, images, stats, vecs, mod, sums, pre, ids, modw)


def results_kernel(count, *refs):
    sources, vec_ref, refs = refs[:count], refs[count], refs[count + 1 :]
    targets, vectors, sems = refs[:count], refs[count:-1], refs[-1]
    copies = [
        pltpu.make_async_copy(source, target, sems.at[k])
        for k, (source, target) in enumerate(zip(sources, targets))
    ]
    for copy in copies:
        copy.start()
    for k, ref in enumerate(vectors):
        ref[...] = vec_ref[k].reshape(ref.shape)
    for copy in copies:
        copy.wait()


def run_results(arrays, vec):
    count = len(arrays)
    shape = jax.ShapeDtypeStruct
    return pl.pallas_call(
        functools.partial(results_kernel, count),
        out_shape=tuple(shape(one.shape, one.dtype) for one in arrays)
        + (shape(vec.shape[1:], F32),) * VECTORS,
        in_specs=[VMEM] * (count + 1),
        out_specs=(ANY,) * count + (VMEM,) * VECTORS,
        scratch_shapes=[DMA((count,))],
        compiler_params=pltpu.CompilerParams(vmem_limit_bytes=60 * 2**20),
        name="results",
    )(*arrays, vec)


def direct(rows, cols):
    n_dp, n_head = lax.axis_size("dp"), lax.axis_size("head")
    return n_head == 4 and n_dp == 8 and rows % 32 == 0 and cols % 64 == 0


def fast_shards(
    images,
    cotangent,
    counts,
    labels,
    levels,
    noise_table,
    class_table,
    gain_a,
    shift_a,
    conv_a,
    bias_a,
    mod_weight,
    mod_bias,
    gain_b,
    shift_b,
    conv_b,
    bias_b,
    gain_c,
    shift_c,
    qkv_weight,
    proj_weight,
    proj_bias,
):
    weights = (
        jnp.swapaxes(conv_a, 0, 1),
        jnp.swapaxes(conv_b, 0, 1),
        jnp.swapaxes(qkv_weight, 0, 1),
        proj_weight,
    )
    vectors = (gain_a, shift_a, bias_a, gain_b, shift_b, bias_b, gain_c, shift_c, proj_bias)
    flat = images.reshape(ALL, C)
    (
        whole,
        conv_out,
        slopes,
        turned,
        block_out,
        grad_resid,
        grad_low,
        right,
        vecs,
        mod,
        stats,
        pre,
        all_ids,
        sums,
    ) = run_forward(
        weights,
        flat,
        cotangent.reshape(ALL, C),
        counts.T,
        labels,
        levels,
        class_table.T,
        noise_table,
        mod_weight,
        mod_bias,
        vectors,
    )
    *arrays, vec = run_backward(
        whole,
        turned,
        right,
        grad_low,
        grad_resid,
        conv_out,
        slopes,
        flat,
        stats,
        vecs,
        mod,
        sums,
        pre,
        all_ids,
        mod_weight,
        class_table.shape[0],
    )
    block_out, conva, convb, qkvw, projw, image_grad, class_grad, modw_grad, modb_grad, *rest = run_results(
        (block_out, *arrays), vec
    )
    gaina, shifta, biasa, gainb, shiftb, biasb, gainc, shiftc, projb = rest
    return (
        block_out.reshape(images.shape),
        image_grad.reshape(images.shape),
        class_grad.T,
        gaina,
        shifta,
        jnp.swapaxes(conva, 0, 1),
        biasa,
        modw_grad,
        modb_grad,
        gainb,
        shiftb,
        jnp.swapaxes(convb, 0, 1),
        biasb,
        gainc,
        shiftc,
        jnp.swapaxes(qkvw, 0, 1),
        projw,
        projb,
    )


def shards(*args):
    rows, _, cols = args[9].shape
    if direct(rows, cols):
        return fast_shards(*args)
    return plain_shards(*args)


def solution(mesh):
    placed = (
        P(("dp", "head"), None, None, None),
        P(("dp", "head"), None, None, None),
        P(),
        P(("dp", "head")),
        P(("dp", "head")),
        P(),
        P(None, "dp"),
        P("head"),
        P("head"),
        P("dp", None, "head"),
        P("head"),
        P("dp", None, None),
        P(),
        P("head"),
        P("head"),
        P("dp", None, "head"),
        P("head"),
        P("head"),
        P("head"),
        P("dp", None, "head"),
        P("dp", "head"),
        P("head"),
    )
    return jax.shard_map(
        shards,
        mesh=mesh,
        in_specs=placed,
        out_specs=(
            P(("dp", "head"), None, None, None),
            P(("dp", "head"), None, None, None),
            P(None, ("dp", "head")),
            P("head"),
            P("head"),
            P("dp", None, "head"),
            P("head"),
            P(("dp", "head"), None, None),
            P(None, ("dp", "head")),
            P("head"),
            P("head"),
            P("dp", None, "head"),
            P("head"),
            P("head"),
            P("head"),
            P("dp", None, "head"),
            P("dp", "head"),
            P("head"),
        ),
        check_vma=False,
    )
```

```python
import functools

import jax
import jax.numpy as jnp
from jax import lax
from jax.experimental import pallas as pl
from jax.experimental.pallas import tpu as pltpu
from jax.sharding import PartitionSpec as P

C = 768
DH = 64
GROUPS = 32


EPSILON = 1e-05
HIGHEST = lax.Precision.HIGHEST


def norm_forward(values, gain, shift):
    count, chans = (values.shape[0], values.shape[-1])
    span = C // GROUPS
    grouped = values.reshape(count, -1, chans // span, span)
    mean = jnp.mean(grouped, axis=(1, 3), keepdims=True)
    centred = grouped - mean
    inverse = lax.rsqrt(jnp.mean(centred * centred, axis=(1, 3), keepdims=True) + EPSILON)
    normed = (centred * inverse).reshape(values.shape)
    return (normed * gain + shift, normed, inverse)


def norm_backward(grad_out, normed, inverse, gain):
    grad_gain = jnp.sum(grad_out * normed, axis=(0, 1, 2))
    grad_shift = jnp.sum(grad_out, axis=(0, 1, 2))
    count, chans = (grad_out.shape[0], grad_out.shape[-1])
    span = C // GROUPS
    layout = (count, -1, chans // span, span)
    grad_normed = (grad_out * gain).reshape(layout)
    normed_groups = normed.reshape(layout)
    mean_one = jnp.mean(grad_normed, axis=(1, 3), keepdims=True)
    mean_two = jnp.mean(grad_normed * normed_groups, axis=(1, 3), keepdims=True)
    grad_in = inverse * (grad_normed - mean_one - normed_groups * mean_two)
    return (grad_in.reshape(grad_out.shape), grad_gain, grad_shift)


def silu_slope(values):
    sigma = jax.nn.sigmoid(values)
    return sigma * (1.0 + values * (1.0 - sigma))


def patches_of(act):
    count, rows, cols, chans = act.shape
    padded = jnp.pad(act, ((0, 0), (1, 1), (1, 1), (0, 0)))
    taps = [padded[:, i : i + rows, j : j + cols, :] for i in range(3) for j in range(3)]
    return jnp.stack(taps, axis=3).reshape(count * rows * cols, 9, chans)


def contract_rows(left, right):
    return lax.dot_general(
        left, right, (((0,), (0,)), ((), ())), preferred_element_type=jnp.float32
    )


def contract_cols(left, right):
    return lax.dot_general(
        left, right, (((1,), (1,)), ((), ())), preferred_element_type=jnp.float32
    )


def conv_back(grad_low, weight, count, rows, cols):
    chans = weight.shape[0]
    padded = jnp.zeros((count, rows + 2, cols + 2, chans), jnp.float32)
    for tap in range(9):
        i, j = divmod(tap, 3)
        part = contract_cols(grad_low, weight[:, tap, :]).reshape(count, rows, cols, chans)
        padded = padded.at[:, i : i + rows, j : j + cols, :].add(part)
    return padded[:, 1 : rows + 1, 1 : cols + 1, :]


def keep_same(values):
    return values


def live_rows(counts, first, number, count):
    sums = jnp.sum(counts, axis=1)
    chosen = lax.dynamic_slice_in_dim(sums, first, number)
    slots = lax.iota(jnp.int32, count)
    return (slots[None, :] < chosen[:, None]).astype(jnp.float32).reshape(number * count)


def residual_forward(source, mod_pair, weights, spread):
    (
        conv_one,
        conv_two,
        gain_one,
        shift_one,
        bias_one,
        gain_two,
        shift_two,
        bias_two,
        gain_three,
        shift_three,
    ) = weights
    out_a, normed_a, inverse_a = norm_forward(source, gain_one, shift_one)
    wide_a = spread(jax.nn.silu(out_a).astype(jnp.bfloat16))
    conv_out_a = (
        jnp.einsum("ptc,cto->po", patches_of(wide_a), conv_one, preferred_element_type=jnp.float32)
        + bias_one
    ).reshape(source.shape)
    scale = mod_pair[:, :, 0:1, :]
    offset = mod_pair[:, :, 1:2, :]
    out_b, normed_b, inverse_b = norm_forward(conv_out_a, gain_two, shift_two)
    inner_b = offset + out_b * (scale + 1.0)
    wide_b = spread(jax.nn.silu(inner_b).astype(jnp.bfloat16))
    conv_out_b = (
        jnp.einsum("ptc,cto->po", patches_of(wide_b), conv_two, preferred_element_type=jnp.float32)
        + bias_two
    ).reshape(source.shape)
    resid = source + conv_out_b
    out_c, normed_c, inverse_c = norm_forward(resid, gain_three, shift_three)
    attn_in = out_c.astype(jnp.bfloat16)
    saved = (
        out_a,
        normed_a,
        inverse_a,
        wide_a,
        out_b,
        normed_b,
        inverse_b,
        inner_b,
        wide_b,
        normed_c,
        inverse_c,
        scale,
    )
    return (resid, attn_in, saved)


def residual_backward(grad_attn, grad_out, saved, weights, reduce_value):
    conv_one, conv_two, gain_one, gain_two, gain_three = (
        weights[0],
        weights[1],
        weights[2],
        weights[5],
        weights[8],
    )
    (
        out_a,
        normed_a,
        inverse_a,
        wide_a,
        out_b,
        normed_b,
        inverse_b,
        inner_b,
        wide_b,
        normed_c,
        inverse_c,
        scale,
    ) = saved
    count, rows, cols, local = grad_out.shape
    grad_resid_c, gainc_term, shiftc_term = norm_backward(
        grad_attn, normed_c, inverse_c, gain_three
    )
    grad_resid = grad_out + grad_resid_c
    grad_conv_b = grad_resid.reshape(-1, local).astype(jnp.bfloat16)
    biasb_term = jnp.sum(grad_conv_b.astype(jnp.float32), axis=0)
    convb_term = jnp.einsum(
        "ptc,po->cto", patches_of(wide_b), grad_conv_b, preferred_element_type=jnp.float32
    )
    grad_act_b = reduce_value(conv_back(grad_conv_b, conv_two, count, rows, cols))
    grad_inner = grad_act_b * silu_slope(inner_b)
    grad_offset = jnp.sum(grad_inner, axis=(1, 2))
    grad_scale = jnp.sum(grad_inner * out_b, axis=(1, 2))
    grad_mod = jnp.stack([grad_scale, grad_offset], axis=1)[:, None]
    grad_conv_full, gainb_term, shiftb_term = norm_backward(
        grad_inner * (scale + 1.0), normed_b, inverse_b, gain_two
    )
    grad_conv_a = grad_conv_full.reshape(-1, local).astype(jnp.bfloat16)
    biasa_term = jnp.sum(grad_conv_a.astype(jnp.float32), axis=0)
    conva_term = jnp.einsum(
        "ptc,po->cto", patches_of(wide_a), grad_conv_a, preferred_element_type=jnp.float32
    )
    grad_act_a = reduce_value(conv_back(grad_conv_a, conv_one, count, rows, cols))
    grad_source, gaina_term, shifta_term = norm_backward(
        grad_act_a * silu_slope(out_a), normed_a, inverse_a, gain_one
    )
    image_grad = grad_resid + grad_source
    vectors = (
        gaina_term,
        shifta_term,
        biasa_term,
        gainb_term,
        shiftb_term,
        biasb_term,
        gainc_term,
        shiftc_term,
    )
    return (image_grad, grad_mod, (conva_term, convb_term), vectors)


def attend_forward(block):
    query, key, value = (block[:, :, 0], block[:, :, 1], block[:, :, 2])
    batch, pixels, heads_here, depth = query.shape
    scores = jnp.einsum("bqhd,bkhd->bhqk", query, key, preferred_element_type=jnp.float32) * DH ** (
        -0.5
    )
    top = jnp.max(scores, axis=-1, keepdims=True)
    weights = jnp.exp(scores - top)
    sums = jnp.sum(weights, axis=-1, keepdims=True)
    probs = (weights / sums).astype(jnp.bfloat16)
    logsum = (top + jnp.log(sums))[..., 0]
    mixed = jnp.einsum("bhqk,bkhd->bqhd", probs, value, preferred_element_type=jnp.float32).astype(
        jnp.bfloat16
    )
    return (mixed.reshape(batch, pixels, heads_here * depth), logsum)


def attend_backward(block, logsum, grad_head):
    query, key, value = (block[:, :, 0], block[:, :, 1], block[:, :, 2])
    batch, pixels, heads_here, depth = query.shape
    factor = DH ** (-0.5)
    scores = jnp.einsum("bqhd,bkhd->bhqk", query, key, preferred_element_type=jnp.float32) * factor
    probs = jnp.exp(scores - logsum[..., None])
    grad_value = jnp.einsum(
        "bhqk,bqhd->bkhd", probs.astype(jnp.bfloat16), grad_head, preferred_element_type=jnp.float32
    )
    grad_probs = jnp.einsum("bqhd,bkhd->bhqk", grad_head, value, preferred_element_type=jnp.float32)
    inner = jnp.sum(grad_probs * probs, axis=-1, keepdims=True)
    grad_scores = (probs * (grad_probs - inner)).astype(jnp.bfloat16)
    grad_query = (
        jnp.einsum("bhqk,bkhd->bqhd", grad_scores, key, preferred_element_type=jnp.float32) * factor
    )
    grad_key = (
        jnp.einsum("bhqk,bqhd->bkhd", grad_scores, query, preferred_element_type=jnp.float32)
        * factor
    )
    stacked = jnp.stack([grad_query, grad_key, grad_value], axis=2).astype(jnp.bfloat16)
    return stacked.reshape(batch, pixels, 3, heads_here * depth)


def plain_shards(
    images,
    cotangent,
    counts,
    labels,
    levels,
    noise_table,
    class_table,
    gain_a,
    shift_a,
    conv_a,
    bias_a,
    mod_weight,
    mod_bias,
    gain_b,
    shift_b,
    conv_b,
    bias_b,
    gain_c,
    shift_c,
    qkv_weight,
    proj_weight,
    proj_bias,
):
    rows_a, rows_b, rows_qkv, rows_proj, mod_full, class_full = (
        lax.all_gather(conv_a, "dp", axis=0, tiled=True),
        lax.all_gather(conv_b, "dp", axis=0, tiled=True),
        lax.all_gather(qkv_weight, "dp", axis=0, tiled=True),
        lax.all_gather(proj_weight, "dp", axis=0, tiled=True),
        lax.all_gather(mod_weight, "dp", axis=0, tiled=True),
        lax.all_gather(class_table, "dp", axis=1, tiled=True),
    )
    count, rows, cols, channels = images.shape
    pixels = rows * cols
    groups_n = lax.axis_size("head")
    quarter = channels // groups_n
    heads_local = quarter // DH
    first_dp = lax.axis_index("dp") * groups_n
    class_hot = (labels[:, None] == lax.iota(jnp.int32, class_full.shape[0])[None, :]).astype(
        jnp.bfloat16
    )
    level_hot = (levels[:, None] == lax.iota(jnp.int32, noise_table.shape[0])[None, :]).astype(
        jnp.bfloat16
    )
    embed_pre = jnp.dot(class_hot, class_full, preferred_element_type=jnp.float32) + jnp.dot(
        level_hot, noise_table, preferred_element_type=jnp.float32
    )
    embed = jax.nn.silu(embed_pre).astype(jnp.bfloat16)
    modulation = (
        jnp.einsum("ne,etc->ntc", embed, mod_full, preferred_element_type=jnp.float32)
        + mod_bias.astype(jnp.float32)
    ).astype(jnp.bfloat16)
    mod_pair = modulation.reshape(count, 1, 2, channels)
    (
        conv_one,
        conv_two,
        qkv_full,
        proj_full,
        gain_one,
        shift_one,
        bias_one,
        gain_two,
        shift_two,
        bias_two,
        gain_three,
        shift_three,
        bias_three,
    ) = (
        lax.all_gather(rows_a, "head", axis=2, tiled=True),
        lax.all_gather(rows_b, "head", axis=2, tiled=True),
        lax.all_gather(rows_qkv, "head", axis=2, tiled=True),
        lax.all_gather(rows_proj, "head", axis=1, tiled=True),
        lax.all_gather(gain_a, "head", axis=0, tiled=True),
        lax.all_gather(shift_a, "head", axis=0, tiled=True),
        lax.all_gather(bias_a, "head", axis=0, tiled=True),
        lax.all_gather(gain_b, "head", axis=0, tiled=True),
        lax.all_gather(shift_b, "head", axis=0, tiled=True),
        lax.all_gather(bias_b, "head", axis=0, tiled=True),
        lax.all_gather(gain_c, "head", axis=0, tiled=True),
        lax.all_gather(shift_c, "head", axis=0, tiled=True),
        lax.all_gather(proj_bias, "head", axis=0, tiled=True),
    )
    weights = (
        conv_one,
        conv_two,
        gain_one,
        shift_one,
        bias_one,
        gain_two,
        shift_two,
        bias_two,
        gain_three,
        shift_three,
    )
    live = live_rows(counts, first_dp + lax.axis_index("head"), 1, count)
    total = count * pixels
    width = channels // groups_n
    source = images.astype(jnp.float32)
    resid, attn_in, saved = residual_forward(
        source, mod_pair.astype(jnp.float32), weights, keep_same
    )
    attn_flat = attn_in.reshape(total, channels)
    qkv_flat = qkv_full.reshape(channels, 3 * channels)
    qkv = jnp.dot(attn_flat, qkv_flat, preferred_element_type=jnp.float32).astype(jnp.bfloat16)
    packed = qkv.reshape(1, count, pixels, 3, groups_n, width)
    block = lax.all_to_all(packed, "head", split_axis=4, concat_axis=0, tiled=True)
    groups = block.shape[0]
    items = block.shape[1]
    flat = block.reshape(groups * items, pixels, 3, heads_local, DH)
    mixed, logsum = attend_forward(flat)
    mixed = mixed.reshape(groups, items, pixels, 1, width)
    returned = lax.all_to_all(mixed, "head", split_axis=0, concat_axis=3, tiled=True)
    returned, logsum, kept = (returned, logsum.reshape(groups, items, heads_local, pixels), block)
    mixed_image = returned.reshape(total, channels)
    result = (
        resid.reshape(total, channels)
        + jnp.dot(mixed_image, proj_full, preferred_element_type=jnp.float32)
        + bias_three
    )
    block_out = (result.reshape(images.shape) * live[:, None, None, None]).astype(jnp.bfloat16)
    grad_out = cotangent.astype(jnp.float32) * live[:, None, None, None]
    grad_flat = grad_out.reshape(total, channels)
    grad_low = grad_flat.astype(jnp.bfloat16)
    projw_full = contract_rows(mixed_image, grad_low)
    projb_full = jnp.sum(grad_flat, axis=0)
    grad_mixed = contract_cols(grad_low, proj_full).astype(jnp.bfloat16)
    arrived = lax.all_to_all(
        grad_mixed.reshape(1, count, pixels, groups_n, width),
        "head",
        split_axis=3,
        concat_axis=0,
        tiled=True,
    )
    flat_block = kept.reshape(groups_n * count, pixels, 3, heads_local, DH)
    grad_head = arrived.reshape(groups_n * count, pixels, heads_local, DH)
    stacked = attend_backward(
        flat_block, logsum.reshape(groups_n * count, heads_local, pixels), grad_head
    )
    stacked = stacked.reshape(groups_n, count, pixels, 3, 1, width)
    grad_qkv = lax.all_to_all(stacked, "head", split_axis=0, concat_axis=4, tiled=True).reshape(
        total, 3 * channels
    )
    qkvw_full = contract_rows(attn_flat, grad_qkv).reshape(channels, 3, channels)
    grad_attn = contract_cols(grad_qkv, qkv_flat).reshape(images.shape)
    image_grad, grad_mod_part, conv_terms, vectors = residual_backward(
        grad_attn, grad_out, saved, weights, keep_same
    )
    (
        gaina_full,
        shifta_full,
        biasa_full,
        gainb_full,
        shiftb_full,
        biasb_full,
        gainc_full,
        shiftc_full,
    ) = vectors
    (
        conva_term,
        convb_term,
        qkvw_term,
        projw_term,
        gaina_term,
        shifta_term,
        biasa_term,
        gainb_term,
        shiftb_term,
        biasb_term,
        gainc_term,
        shiftc_term,
        projb_term,
    ) = (
        lax.psum_scatter(
            conv_terms[0].astype(jnp.bfloat16), "head", scatter_dimension=2, tiled=True
        ).astype(jnp.float32),
        lax.psum_scatter(
            conv_terms[1].astype(jnp.bfloat16), "head", scatter_dimension=2, tiled=True
        ).astype(jnp.float32),
        lax.psum_scatter(
            qkvw_full.astype(jnp.bfloat16), "head", scatter_dimension=2, tiled=True
        ).astype(jnp.float32),
        lax.psum_scatter(
            projw_full.astype(jnp.bfloat16), "head", scatter_dimension=1, tiled=True
        ).astype(jnp.float32),
        lax.psum_scatter(
            gaina_full.astype(jnp.bfloat16), "head", scatter_dimension=0, tiled=True
        ).astype(jnp.float32),
        lax.psum_scatter(
            shifta_full.astype(jnp.bfloat16), "head", scatter_dimension=0, tiled=True
        ).astype(jnp.float32),
        lax.psum_scatter(
            biasa_full.astype(jnp.bfloat16), "head", scatter_dimension=0, tiled=True
        ).astype(jnp.float32),
        lax.psum_scatter(
            gainb_full.astype(jnp.bfloat16), "head", scatter_dimension=0, tiled=True
        ).astype(jnp.float32),
        lax.psum_scatter(
            shiftb_full.astype(jnp.bfloat16), "head", scatter_dimension=0, tiled=True
        ).astype(jnp.float32),
        lax.psum_scatter(
            biasb_full.astype(jnp.bfloat16), "head", scatter_dimension=0, tiled=True
        ).astype(jnp.float32),
        lax.psum_scatter(
            gainc_full.astype(jnp.bfloat16), "head", scatter_dimension=0, tiled=True
        ).astype(jnp.float32),
        lax.psum_scatter(
            shiftc_full.astype(jnp.bfloat16), "head", scatter_dimension=0, tiled=True
        ).astype(jnp.float32),
        lax.psum_scatter(
            projb_full.astype(jnp.bfloat16), "head", scatter_dimension=0, tiled=True
        ).astype(jnp.float32),
    )
    grad_mod = grad_mod_part.reshape(count, 2, channels)
    modw_term = jnp.einsum("ne,ntc->etc", embed.astype(jnp.float32), grad_mod, precision=HIGHEST)
    modb_term = jnp.sum(grad_mod, axis=0)
    grad_embed = jnp.einsum(
        "ntc,etc->ne", grad_mod, mod_full.astype(jnp.float32), precision=HIGHEST
    ) * silu_slope(embed_pre)
    class_term = lax.dot_general(
        class_hot.astype(jnp.float32), grad_embed, (((0,), (0,)), ((), ())), precision=HIGHEST
    )
    modw_grad, class_grad, modb_grad = (
        lax.psum_scatter(modw_term, ("dp", "head"), scatter_dimension=0, tiled=True),
        lax.psum_scatter(class_term, ("dp", "head"), scatter_dimension=1, tiled=True),
        lax.psum_scatter(modb_term, ("dp", "head"), scatter_dimension=1, tiled=True),
    )
    conva_grad, convb_grad, qkvw_grad, projw_grad = (
        lax.psum_scatter(conva_term, "dp", scatter_dimension=0, tiled=True),
        lax.psum_scatter(convb_term, "dp", scatter_dimension=0, tiled=True),
        lax.psum_scatter(qkvw_term, "dp", scatter_dimension=0, tiled=True),
        lax.psum_scatter(projw_term, "dp", scatter_dimension=0, tiled=True),
    )
    (
        gaina_grad,
        shifta_grad,
        biasa_grad,
        gainb_grad,
        shiftb_grad,
        biasb_grad,
        gainc_grad,
        shiftc_grad,
        projb_grad,
    ) = lax.psum(
        (
            gaina_term,
            shifta_term,
            biasa_term,
            gainb_term,
            shiftb_term,
            biasb_term,
            gainc_term,
            shiftc_term,
            projb_term,
        ),
        "dp",
    )
    return (
        block_out,
        image_grad,
        class_grad,
        gaina_grad,
        shifta_grad,
        conva_grad,
        biasa_grad,
        modw_grad,
        modb_grad,
        gainb_grad,
        shiftb_grad,
        convb_grad,
        biasb_grad,
        gainc_grad,
        shiftc_grad,
        qkvw_grad,
        projw_grad,
        projb_grad,
    )


MESH = pl.DeviceIdType.MESH
UNITS = 22
PAIRS = UNITS // 2
FAR = 9
VECTORS = 9
RES = 8
SLOTS = 8
PIX = RES * RES
LINE = SLOTS * RES
ALL = RES * LINE
WIDTH = 768
BAND = 256
F32 = jnp.float32
BF16 = jnp.bfloat16
ANY = pl.BlockSpec(memory_space=pl.ANY)
VMEM = pl.BlockSpec(memory_space=pltpu.VMEM)
SMEM = pl.BlockSpec(memory_space=pltpu.SMEM)
DMA = pltpu.SemaphoreType.DMA


def place():
    d, h = lax.axis_index("dp"), lax.axis_index("head")
    return d // 2, lax.rem(d, 2), h // 2, lax.rem(h, 2)


def at_chip(z, y, x, c):
    return (z * 2 + y, x * 2 + c)


def column_peers(n_dp):
    d, h = lax.axis_index("dp"), lax.axis_index("head")
    return [(lax.rem(d + k, n_dp), h) for k in range(1, n_dp)]


def head_peers(n_head):
    d, h = lax.axis_index("dp"), lax.axis_index("head")
    return [(d, lax.rem(h + k, n_head)) for k in range(1, n_head)]


def greet(devices):
    barrier = pltpu.get_barrier_semaphore()
    for device in devices:
        pl.semaphore_signal(barrier, inc=1, device_id=device, device_id_type=MESH)
    pl.semaphore_wait(barrier, len(devices))


def remote(src, dst, send, recv, device):
    return pltpu.make_async_remote_copy(
        src_ref=src, dst_ref=dst, send_sem=send, recv_sem=recv, device_id=device, device_id_type=MESH
    )


def each(count, body):
    def step(n, carry):
        body(n)
        return carry

    lax.fori_loop(0, count, step, 0)


def span(index, size):
    return pl.ds(pl.multiple_of(index * size, size), size)


def row(n):
    return pl.ds(n, 1)


def lines_from(i):
    return pl.ds(i * LINE if isinstance(i, int) else pl.multiple_of(i * LINE, LINE), ALL)


def dot(left, right):
    return jnp.dot(left, right, preferred_element_type=F32)


def dot_nt(left, right):
    return lax.dot_general(left, right, (((1,), (1,)), ((), ())), preferred_element_type=F32)


def dot_tn(left, right):
    return lax.dot_general(left, right, (((0,), (0,)), ((), ())), preferred_element_type=F32)


def in_group(first, second, axis):
    chan = lax.broadcasted_iota(jnp.int32, (first, second), axis)
    group = lax.broadcasted_iota(jnp.int32, (first, second), 1 - axis) * (C // GROUPS)
    inside = jnp.logical_and(chan >= group, chan < group + C // GROUPS)
    return jnp.where(inside, 1.0, 0.0).astype(BF16)


def pieces(values):
    high = values.astype(BF16).astype(F32)
    rest = values - high
    mid = rest.astype(BF16).astype(F32)
    return jnp.concatenate([high, mid, rest - mid], axis=0).astype(BF16)


def group_mean(sums):
    count = sums.shape[0]
    part = dot(pieces(sums), in_group(C, 128, 0))
    part = (part[:count] + part[count : 2 * count] + part[2 * count :]) * (1.0 / (PIX * (C // GROUPS)))
    back = dot(pieces(part), in_group(128, C, 1))
    return back[:count] + back[count : 2 * count] + back[2 * count :]


def sum_rows(values):
    return jnp.sum(values, axis=0, keepdims=True)


def norm_stats(get, mean_ref, inverse_ref, sums_ref):
    def first(n):
        sums_ref[row(n)] = sum_rows(get(n))

    each(SLOTS, first)
    mean_ref[...] = group_mean(sums_ref[...])

    def second(n):
        centred = get(n) - mean_ref[row(n)]
        sums_ref[row(n)] = sum_rows(centred * centred)

    each(SLOTS, second)
    inverse_ref[...] = lax.rsqrt(group_mean(sums_ref[...]) + EPSILON)


def silu(values):
    return values * jax.nn.sigmoid(values)


def shifted(values):
    spot = lax.rem(lax.broadcasted_iota(jnp.int32, values.shape, 0), RES)
    left = jnp.where(spot == 0, 0.0, pltpu.roll(values, 1, 0))
    right = jnp.where(spot == RES - 1, 0.0, pltpu.roll(values, values.shape[0] - 1, 0))
    return left, right


def chunk(n):
    return slice(n * WIDTH, (n + 1) * WIDTH)


CHUNKS = C // WIDTH


def weight_cols(ref, n):
    return ref[:, :, :, chunk(n)].reshape(C, WIDTH)


def weight_rows(ref, n):
    return ref[...].reshape(C, C)[chunk(n)]


def forward_kernel(
    lines,
    weights_a,
    weights_b,
    weights_qkv,
    weights_proj,
    images_hbm,
    cot_hbm,
    counts_ref,
    labels_ref,
    levels_ref,
    class_table,
    noise_table,
    modw_table,
    modb_ref,
    *refs,
):
    vectors, refs = refs[:VECTORS], refs[VECTORS:]
    forward_steps(
        lines,
        vectors,
        weights_a,
        weights_b,
        weights_qkv,
        weights_proj,
        images_hbm,
        cot_hbm,
        counts_ref,
        labels_ref,
        levels_ref,
        class_table,
        noise_table,
        modw_table,
        modb_ref,
        *refs,
    )


def forward_steps(
    lines,
    vectors,
    weights_a,
    weights_b,
    weights_qkv,
    weights_proj,
    images_hbm,
    cot_hbm,
    counts_ref,
    labels_ref,
    levels_ref,
    class_table,
    noise_table,
    modw_table,
    modb_ref,
    whole_out,
    conv_out,
    slopes_out,
    turned_out,
    block_out,
    grad_out,
    low_out,
    right_out,
    vecs_ref,
    mod_ref,
    stats_ref,
    pre_ref,
    all_ids,
    sums_out,
    halves,
    whole_ref,
    vec_ref,
    ids_ref,
    class_ref,
    modw_ref,
    vec_all,
    mod_part,
    mod_got,
    act,
    act_f32,
    sums_ref,
    conv_ref,
    resid_ref,
    slopes,
    turned,
    attn_in,
    qkv,
    right,
    low,
    pair_ref,
    pair_send,
    pair_recv,
    pair_local,
    z_send,
    z_recv,
    p_send,
    x_send,
    x_recv,
    y_send,
    y_recv,
    s_send,
    s_recv,
    vec_send,
    vec_recv,
    ids_send,
    ids_recv,
    mod_send,
    mod_recv,
    unit_sem,
    flush_sem,
    in_sem,
    share_local,
    share_send,
    share_recv,
):
    z, y, x, c = place()
    d, h = lax.axis_index("dp"), lax.axis_index("head")
    n_dp, n_head = lines * 2, 4
    half = lines // 2
    inner = jnp.logical_and(z > 0, z < lines - 1)
    far = at_chip(lax.rem(3 * z + 1, lines), y, x, c)
    rows, cols_own = halves.shape[2:]
    wide = 2 * cols_own
    sibling = at_chip(z, y, x, 1 - c)
    along_x = at_chip(z, y, 1 - x, c)
    along_y = at_chip(z, 1 - y, x, c)
    line = [at_chip(lax.rem(z + k, lines), y, x, c) for k in range(1, lines)]
    column, heads = column_peers(n_dp), head_peers(n_head)
    greet(column + heads)

    def spot(i, cc, zz, yy, xx):
        return whole_ref.at[i, cc, zz, yy, :, span(xx, wide)]

    def parts_of(core):
        return (
            (weights_a.at[pl.ds(4 * core, 4)], pl.ds(0, 4)),
            (weights_b.at[pl.ds(4 * core, 4)], pl.ds(5, 4)),
            (weights_qkv.at[pl.ds(core, 1)], pl.ds(9, 1)),
        )

    last_parts = (
        ((weights_a.at[8], 4), (weights_qkv.at[2], 10)),
        ((weights_b.at[8], 4), (weights_proj, 10)),
    )

    def keep_copy(k):
        source, where = parts_of(c)[k]
        return pltpu.make_async_copy(source, halves.at[c, where], pair_local.at[k])

    def swap_copy(k):
        source, where = parts_of(1 - c)[k]
        return remote(source, halves.at[c, where], pair_send.at[k], pair_recv.at[k], sibling)

    def last_keep(core, k):
        source, where = last_parts[core][k]
        return pltpu.make_async_copy(source, halves.at[c, where], pair_local.at[3 + k])

    def last_swap(core, k):
        source, where = last_parts[core][k]
        return remote(source, halves.at[c, where], pair_send.at[3 + k], pair_recv.at[3 + k], sibling)

    def swap_start():
        for k in range(3):
            swap_copy(k).start()
            keep_copy(k).start()
        for core in range(2):

            @pl.when(c == core)
            def _():
                for k in range(2):
                    last_swap(1 - core, k).start()
                    last_keep(core, k).start()

    def swap_wait(k):
        if k < 3:
            keep_copy(k).wait()
            swap_copy(k).wait()
        else:
            last_keep(0, k - 3).wait()
            last_swap(0, k - 3).wait()

    def images_copy():
        return pltpu.make_async_copy(images_hbm, images_ref, in_sem.at[0])

    def cot_copy():
        return pltpu.make_async_copy(cot_hbm, cot_ref, in_sem.at[1])

    images_ref, cot_ref = attn_in, low

    def vec_copy(k):
        return remote(vec_ref, vec_all.at[h], vec_send.at[k], vec_recv.at[k], heads[k])

    def ids_copy(k):
        return remote(ids_ref, all_ids.at[d], ids_send.at[k], ids_recv.at[k], column[k])

    def mod_copy(k):
        return remote(
            mod_part.at[lax.rem(d + k + 1, n_dp)], mod_got.at[d], mod_send.at[k], mod_recv.at[k], column[k]
        )

    def z_part(i, zz):
        if isinstance(i, int) and i >= FAR:
            return whole_ref.at[i, c, zz]
        return spot(i, c, zz, y, x)

    def z_copy(i, k):
        ref = z_part(i, z)
        return remote(ref, ref, z_send.at[i, k], z_recv.at[i, k], line[k])

    def z_pass(i):
        ref = z_part(i, lax.rem(z + 2, lines))
        return remote(ref, ref, p_send.at[i], z_recv.at[i, lax.rem(2 * z + 2, lines)], far)

    def z_start(i):
        z_copy(i, 1).start()

        @pl.when(z != lines - 1)
        def _():
            z_copy(i, 0).start()

        @pl.when(z != 0)
        def _():
            z_copy(i, 2).start()

    def z_relay(i):
        z_copy(i, 1).wait_recv()

        @pl.when(inner)
        def _():
            z_pass(i).start()

    def z_finish(i):
        z_copy(i, 0).wait_recv()
        z_copy(i, 2).wait_recv()

    def z_drain(i):
        z_copy(i, 1).wait_send()

        @pl.when(z != lines - 1)
        def _():
            z_copy(i, 0).wait_send()

        @pl.when(z != 0)
        def _():
            z_copy(i, 2).wait_send()

        @pl.when(inner)
        def _():
            z_pass(i).wait_send()

    def x_copy(i, part):
        if isinstance(i, int) and i >= FAR:
            ref = spot(i, c, z, y, x) if part == 0 else spot(i, c, z, 1 - y, x).at[pl.ds(rows // 2, rows // 2)]
        elif part == 0:
            ref = spot(i, c, slice(None), y, x)
        else:
            ref = spot(i, c, pl.ds(half, half), 1 - y, x)
        return remote(ref, ref, x_send.at[i, part], x_recv.at[i, part], along_x)

    def y_copy(i, part):
        if isinstance(i, int) and i >= FAR:
            ref = spot(i, c, z, y, x) if part == 0 else spot(i, c, z, y, 1 - x).at[pl.ds(0, rows // 2)]
        elif part == 0:
            ref = spot(i, c, slice(None), y, x)
        else:
            ref = spot(i, c, pl.ds(0, half), y, 1 - x)
        return remote(ref, ref, y_send.at[i, part], y_recv.at[i, part], along_y)

    def s_copy(i, part):
        if isinstance(i, int) and i >= FAR:
            ref = whole_ref.at[i, c, part]
        else:
            yy, xx = ((y, x), (y, 1 - x), (1 - y, x), (1 - y, 1 - x))[part]
            ref = spot(i, c, slice(None), yy, xx)
        return remote(ref, ref, s_send.at[i, part], s_recv.at[i, part], sibling)

    def join(i):
        whole_ref[i, c, z, y, :, span(x, wide)] = jnp.concatenate([halves[0, i], halves[1, i]], axis=-1)

    def begin(i):
        join(i)
        z_start(i)

    def far_begin(i):
        x_copy(i, 0).start()
        y_copy(i, 0).start()

    def far_pass(i):
        x_copy(i, 0).wait_recv()
        y_copy(i, 1).start()
        y_copy(i, 0).wait_recv()
        x_copy(i, 1).start()

    def far_line(i):
        x_copy(i, 1).wait_recv()
        y_copy(i, 1).wait_recv()
        z_start(i)

    def far_finish(i):
        z_finish(i)
        for part in range(lines):
            s_copy(i, part).start()

    def spread_line(i):
        z_finish(i)
        x_copy(i, 0).start()
        y_copy(i, 0).start()
        s_copy(i, 0).start()

    def pass_on(i):
        x_copy(i, 0).wait_recv()
        y_copy(i, 1).start()
        s_copy(i, 1).start()
        y_copy(i, 0).wait_recv()
        x_copy(i, 1).start()
        s_copy(i, 2).start()

    def finish(i):
        x_copy(i, 1).wait_recv()
        y_copy(i, 1).wait_recv()
        s_copy(i, 3).start()

    def arrived(i):
        for part in range(4):
            s_copy(i, part).wait_recv()

    def unit_copy(i):
        return pltpu.make_async_copy(whole_ref.at[i], whole_out.at[i], unit_sem.at[i])

    def fetch(i):
        arrived(i)
        if not isinstance(i, int) or i < FAR:
            unit_copy(i).start()

    def product(total, tap, i, k):
        for n in range(CHUNKS):
            value = dot(act[tap % 3, lines_from(tap // 3)], weight_cols(whole_ref.at[i, k], n))
            total[:, :, :, chunk(n)] += value.reshape(RES, SLOTS, RES, WIDTH)

    def use_pair(total, i, first):
        each(2, lambda k: product(total, i - first + 4 * k, i, k))

    flushed = (
        (conv_ref, conv_out),
        (slopes.at[0], slopes_out.at[0]),
        (slopes.at[1], slopes_out.at[1]),
        (low, block_out),
        (conv_ref, grad_out),
        (attn_in, low_out),
    )

    def share_parts(k):
        if k < 4:
            return turned.at[k], turned_out.at[k, :, span(c, ALL)]
        part = (3, 1 - c, 2)[k - 4]
        return right.at[part], right_out.at[part, span(c, ALL)]

    def share_give(k):
        return remote(*share_parts(k), share_send.at[k], share_recv.at[k], sibling)

    def right_keep(k):
        return pltpu.make_async_copy(right.at[k], right_out.at[k, span(c, ALL)], share_local.at[4 + k])

    def turned_keep(k):
        return pltpu.make_async_copy(*share_parts(k), share_local.at[k])

    def share_if(k, giving, run):
        if k in (1, 4, 6):
            taker = 0 if k == 6 else 1
            pl.when(c == (1 - taker if giving else taker))(run)
        else:
            run()

    def share(k):
        share_if(k, True, lambda: share_give(k).start())

    def share_wait():
        for k in range(7):
            share_if(k, True, lambda k=k: share_give(k).wait_send())
            share_if(k, False, lambda k=k: share_give(k).wait_recv())
        for k in range(4):
            turned_keep(k).wait()
            right_keep(k).wait()

    def flush(k):
        return pltpu.make_async_copy(*flushed[k], flush_sem.at[k])

    def set_act(place_t):
        def by_line(yy):
            value = act_f32[yy].reshape(LINE, C)
            left, right = shifted(value)
            spot_rows = pl.ds(pl.multiple_of((yy + 1) * LINE, LINE), LINE)
            act[0, spot_rows] = left.astype(BF16)
            act[1, spot_rows] = value.astype(BF16)
            act[2, spot_rows] = right.astype(BF16)

        each(RES, by_line)

        def turn(yy):
            value = act_f32[pl.ds(2 * yy, 2)].reshape(2 * LINE, C)
            turned[place_t, :, span(yy, 2 * LINE)] = value.T.astype(BF16)

        each(RES // 2, turn)

    def activate(which, n, value):
        sigma = jax.nn.sigmoid(value)
        act_f32[:, n] = (value * sigma).reshape(RES, RES, C)
        slopes[which, :, n] = (sigma * (1.0 + value * (1.0 - sigma))).reshape(RES, RES, C)

    def norm_a():
        for k in range(n_head - 1):
            vec_copy(k).wait()
        vecs_ref[...] = jnp.concatenate([vec_all[k].astype(F32) for k in range(n_head)], axis=-1)

        images_copy().wait()

        def get(n):
            return images_ref[span(n, PIX)].astype(F32)

        mean, inverse = stats_ref.at[0], stats_ref.at[1]
        norm_stats(get, mean, inverse, sums_ref)

        def to_act(n):
            value = (get(n) - mean[row(n)]) * inverse[row(n)]
            activate(0, n, value * vecs_ref[0:1] + vecs_ref[1:2])
            conv_ref[:, n] = jnp.broadcast_to(vecs_ref[2:3].reshape(1, 1, C), (RES, RES, C))
            resid_ref[:, n] = (get(n) + vecs_ref[5:6]).reshape(RES, RES, C)

        each(SLOTS, to_act)
        set_act(3)
        flush(1).start()
        turned_keep(3).start()
        share(3)

    def embed():
        for k in range(n_dp - 1):
            ids_copy(k).wait()
        ids = all_ids[...].reshape(n_dp * SLOTS, 128)
        table = class_ref.shape[1]
        label_hot = lax.broadcasted_iota(jnp.int32, (n_dp * SLOTS, table), 1) == ids[:, 0:1]
        levels = noise_table.shape[0]
        level_hot = lax.broadcasted_iota(jnp.int32, (n_dp * SLOTS, levels), 1) == ids[:, 1:2]
        pre = dot_nt(jnp.where(label_hot, 1.0, 0.0).astype(BF16), class_ref[...])
        width = class_table.shape[0]
        place_of = lax.broadcasted_iota(jnp.int32, (C, 128), 0) - d * width
        lane = lax.broadcasted_iota(jnp.int32, (C, 128), 1)
        chosen = jnp.logical_and(place_of == lane, lane < width)
        noise = dot(noise_table[...], jnp.where(chosen, 1.0, 0.0).astype(BF16)).astype(BF16)
        pre += dot(jnp.where(level_hot, 1.0, 0.0).astype(BF16), noise)
        pre_ref[...] = pre
        part = dot(silu(pre).astype(BF16), modw_ref[...])
        for k in range(n_dp):
            mine = part[k * SLOTS : (k + 1) * SLOTS]
            mod_part[k] = jnp.concatenate([mine[:, :C], mine[:, C:]], axis=0).astype(BF16)
        mod_got[d] = mod_part[d]
        for k in range(n_dp - 1):
            mod_copy(k).start()

    def conv_value(n):
        return conv_ref[:, n].reshape(PIX, C)

    def norm_b_first():
        for k in range(n_dp - 1):
            mod_copy(k).wait()
        bias = modb_ref[...].astype(F32)
        total = jnp.concatenate([jnp.broadcast_to(bias[k : k + 1], (SLOTS, C)) for k in range(2)], axis=0)
        for k in range(n_dp):
            total += mod_got[k].astype(F32)
        mod_ref[...] = total.astype(BF16).astype(F32)

        norm_stats(conv_value, stats_ref.at[2], stats_ref.at[3], sums_ref)

    def norm_b_second():
        mean, inverse = stats_ref.at[2], stats_ref.at[3]

        def to_act(n):
            value = (conv_value(n) - mean[row(n)]) * inverse[row(n)]
            value = value * vecs_ref[3:4] + vecs_ref[4:5]
            value = mod_ref[row(SLOTS + n)] + value * (mod_ref[row(n)] + 1.0)
            activate(1, n, value)

        each(SLOTS, to_act)
        set_act(2)
        flush(0).start()
        flush(2).start()
        turned_keep(2).start()
        share(2)

    def residual(n):
        return resid_ref[:, n].reshape(PIX, C)

    def normed(n):
        return (residual(n) - stats_ref[4, row(n)]) * stats_ref[5, row(n)]

    def transpose_out(source, place_t):
        def turn(k):
            value = source[span(k, 2 * LINE)].astype(F32)
            turned[place_t, :, span(k, 2 * LINE)] = value.T.astype(BF16)

        each(ALL // (2 * LINE), turn)

    def live(n):
        slots = counts_ref[0, d * n_head + h] + counts_ref[1, d * n_head + h]
        return jnp.where(n < slots, 1.0, 0.0)

    def norm_c():
        cot_copy().wait()
        norm_stats(residual, stats_ref.at[4], stats_ref.at[5], sums_ref)
        sums_out[...] = jnp.zeros_like(sums_out)

        def prepare(n):
            attn_in[span(n, PIX)] = (normed(n) * vecs_ref[6:7] + vecs_ref[7:8]).astype(BF16)
            grad = cot_ref[span(n, PIX)].astype(F32) * live(n)
            right[3, span(n, PIX)] = grad.astype(BF16)
            sums_out[8:9] += sum_rows(grad)

        each(SLOTS, prepare)
        transpose_out(attn_in, 0)
        turned_keep(0).start()
        right_keep(3).start()
        share(0)
        share(4)

    def attention():
        unit = tuple(whole_ref.at[9 + t // 2, t % 2] for t in range(4))
        for t in range(4):
            for n in range(CHUNKS):
                if t < 3:
                    value = dot(attn_in[...], weight_cols(unit[t], n))
                else:
                    value = dot_nt(right[3], weight_rows(unit[3], n))
                qkv[t, :, chunk(n)] = value.astype(BF16)
        factor = DH ** (-0.5)
        band = lax.broadcasted_iota(jnp.int32, (PIX, BAND), 1) // DH
        heads_at_once = BAND // DH

        def stack(value):
            zero = jnp.zeros_like(value)
            return jnp.concatenate([jnp.where(band == k, value, zero) for k in range(heads_at_once)], axis=0)

        def pick(value):
            out = value[:PIX]
            for k in range(1, heads_at_once):
                out = jnp.where(band == k, value[k * PIX : (k + 1) * PIX], out)
            return out

        def attend(n):
            for b in range(C // BAND):
                query, key, value, grad = (qkv[t, span(n, PIX), slice(b * BAND, (b + 1) * BAND)] for t in range(4))
                query4, grad4 = stack(query), stack(grad)
                scores = dot_nt(key, query4) * factor
                weight = jnp.exp(scores - jnp.max(scores, axis=0, keepdims=True))
                probs = weight / jnp.sum(weight, axis=0, keepdims=True)
                probs_low = probs.astype(BF16)
                low[span(n, PIX), slice(b * BAND, (b + 1) * BAND)] = pick(dot_tn(probs_low, value)).astype(BF16)
                grad_probs = dot_nt(value, grad4)
                inner_sum = jnp.sum(grad_probs * probs, axis=0, keepdims=True)
                grad_scores = (probs * (grad_probs - inner_sum)).astype(BF16)
                right[0, span(n, PIX), slice(b * BAND, (b + 1) * BAND)] = (pick(dot_tn(grad_scores, key)) * factor).astype(BF16)
                right[1, span(n, PIX), slice(b * BAND, (b + 1) * BAND)] = (dot(grad_scores, query4) * factor).astype(BF16)
                right[2, span(n, PIX), slice(b * BAND, (b + 1) * BAND)] = dot(probs_low, grad4).astype(BF16)

        def attend_two(m):
            attend(2 * m)
            attend(2 * m + 1)

        each(SLOTS // 2, attend_two)
        share(5)
        share(6)
        for k in range(3):
            right_keep(k).start()
        transpose_out(low, 1)
        turned_keep(1).start()
        share(1)
        for n in range(CHUNKS):
            value = dot_nt(right[0], weight_rows(unit[0], n))
            value += dot_nt(right[1], weight_rows(unit[1], n))
            value += dot_nt(right[2], weight_rows(unit[2], n))
            act_f32[:, :, :, chunk(n)] = value.reshape(SLOTS, RES, RES, WIDTH)

        def back(n):
            grad = act_f32[n].reshape(PIX, C)
            pair_ref[row(n)] = sum_rows(grad * normed(n))
            pair_ref[row(SLOTS + n)] = sum_rows(grad)

        each(SLOTS, back)
        sums_out[6:7] = sum_rows(pair_ref[0:SLOTS])
        sums_out[7:8] = sum_rows(pair_ref[SLOTS:])
        pair_ref[...] = group_mean(pair_ref[...] * vecs_ref[6:7])

        def back_second(n):
            inverse = stats_ref[5, row(n)]
            value = act_f32[n].reshape(PIX, C) * (vecs_ref[6:7] * inverse)
            value -= normed(n) * (pair_ref[row(n)] * inverse) + pair_ref[row(SLOTS + n)] * inverse
            value += right[3, span(n, PIX)].astype(F32)
            conv_ref[:, n] = value.reshape(RES, RES, C)
            sums_out[5:6] += sum_rows(value.astype(BF16).astype(F32))

        flush(0).wait()
        each(SLOTS, back_second)
        flush(4).start()

        def lower(yy):
            attn_in[span(yy, LINE)] = conv_ref[yy].reshape(LINE, C).astype(BF16)

        each(RES, lower)
        flush(5).start()
        for n in range(CHUNKS):
            value = dot(low[...], weight_cols(unit[3], n))
            act_f32[:, :, :, chunk(n)] = value.reshape(SLOTS, RES, RES, WIDTH)

        def finish_out(n):
            value = residual(n) + act_f32[n].reshape(PIX, C) + vecs_ref[8:9]
            low[span(n, PIX)] = (value * live(n)).astype(BF16)

        each(SLOTS, finish_out)
        flush(3).start()

    swap_start()
    images_copy().start()
    cot_copy().start()
    one = [ref[...].astype(F32).reshape(1, cols_own) for ref in vectors]
    vec_ref[...] = jnp.concatenate(one + [jnp.zeros((16 - VECTORS, cols_own), F32)], axis=0).astype(BF16)
    lane = lax.broadcasted_iota(jnp.int32, (1, 128), 1)
    for n in range(SLOTS):
        ids_ref[n : n + 1] = jnp.where(lane == 0, labels_ref[n], levels_ref[n])
    for k in range(n_head - 1):
        vec_copy(k).start()
    for k in range(n_dp - 1):
        ids_copy(k).start()
    width = class_table.shape[0]
    class_ref[...] = jnp.zeros_like(class_ref)
    class_ref[0:width, 0 : class_table.shape[1]] = class_table[...]
    modw_ref[...] = jnp.zeros_like(modw_ref)
    table = modw_table[...].astype(F32)
    for k in range(2):
        modw_ref[0:width, k * C : (k + 1) * C] = table[:, k].astype(BF16)
    vec_all[h] = vec_ref[...]
    all_ids[d] = ids_ref[...]
    edge = jnp.zeros((LINE, C), BF16)
    for j in range(3):
        act[j, 0:LINE] = edge
        act[j, ALL + LINE : ALL + 2 * LINE] = edge
    swap_wait(0)
    begin(0)
    for k in range(1, 5):
        swap_wait(k)
    for i in (10, 9):
        join(i)
        far_begin(i)
    begin(1)
    z_relay(0)
    begin(2)
    spread_line(0)
    for i in (10, 9):
        far_pass(i)
    begin(3)
    z_relay(1)
    norm_a()
    spread_line(1)
    pass_on(0)
    begin(4)
    z_relay(2)
    embed()
    spread_line(2)
    pass_on(1)
    finish(0)
    begin(5)
    z_relay(3)
    begin(6)
    z_relay(4)
    far_line(10)
    spread_line(3)
    pass_on(2)
    finish(1)
    fetch(0)

    def body(turn, carry):
        @pl.when(turn < 6)
        def _():
            begin(turn + 3)

        @pl.when(turn == 6)
        def _():
            far_line(9)
            z_relay(10)

        z_relay(turn + 1)
        spread_line(turn)
        pass_on(turn - 1)
        finish(turn - 2)
        fetch(turn - 3)
        use_pair(conv_ref, turn - 4, 0)
        return carry

    lax.fori_loop(4, 8, body, 0)
    spread_line(8)
    pass_on(7)
    finish(6)
    fetch(5)
    product(conv_ref, 8, 4, 0)
    norm_b_first()
    pass_on(8)
    finish(7)
    z_relay(9)
    norm_b_second()
    product(resid_ref, 8, 4, 1)
    fetch(6)
    far_finish(10)
    use_pair(resid_ref, 5, 5)
    finish(8)
    fetch(7)
    use_pair(resid_ref, 6, 5)
    fetch(8)
    use_pair(resid_ref, 7, 5)
    far_finish(9)
    use_pair(resid_ref, 8, 5)
    norm_c()
    fetch(9)
    fetch(10)
    attention()

    def drain(i):
        z_drain(i)
        for part in range(2):
            x_copy(i, part).wait_send()
            y_copy(i, part).wait_send()
        for part in range(4):
            s_copy(i, part).wait_send()

    each(FAR, drain)
    drain(9)
    drain(10)
    for k in range(1, len(flushed)):
        flush(k).wait()
    each(FAR, lambda i: unit_copy(i).wait())
    share_wait()


def run_forward(weights, images, cotangent, counts, labels, levels, class_table, noise_table, modw, modb, vectors):
    n_dp, n_head = lax.axis_size("dp"), lax.axis_size("head")
    rows, cols = weights[0].shape[1:]
    lines, across, wide = n_dp // 2, n_head // 2, 2 * cols
    board = (RES, SLOTS, RES, C)
    shape = jax.ShapeDtypeStruct
    return pl.pallas_call(
        functools.partial(forward_kernel, lines),
        out_shape=(
            shape((FAR, 2, lines, 2, rows, across * wide), BF16),
            shape(board, F32),
            shape((2,) + board, F32),
            shape((4, C, 2 * ALL), BF16),
            shape((ALL, C), BF16),
            shape(board, F32),
            shape((ALL, C), BF16),
            shape((4, 2 * ALL, C), BF16),
            shape((16, C), F32),
            shape((2 * SLOTS, C), F32),
            shape((6, SLOTS, C), F32),
            shape((n_dp * SLOTS, 128), F32),
            shape((n_dp, SLOTS, 128), jnp.int32),
            shape((16, C), F32),
        ),
        in_specs=[ANY] * 6 + [SMEM] * 3 + [VMEM] * (4 + VECTORS),
        out_specs=(ANY,) * 8 + (VMEM,) * 6,
        scratch_shapes=[
            pltpu.VMEM((2, PAIRS, rows, cols), BF16),
            pltpu.VMEM((PAIRS, 2, lines, 2, rows, across * wide), BF16),
            pltpu.VMEM((16, cols), BF16),
            pltpu.VMEM((SLOTS, 128), jnp.int32),
            pltpu.VMEM((128, 1024), BF16),
            pltpu.VMEM((128, 2 * C), BF16),
            pltpu.VMEM((n_head, 16, cols), BF16),
            pltpu.VMEM((n_dp, 2 * SLOTS, C), BF16),
            pltpu.VMEM((n_dp, 2 * SLOTS, C), BF16),
            pltpu.VMEM((3, ALL + 2 * LINE, C), BF16),
            pltpu.VMEM(board, F32),
            pltpu.VMEM((SLOTS, C), F32),
            pltpu.VMEM(board, F32),
            pltpu.VMEM(board, F32),
            pltpu.VMEM((2,) + board, F32),
            pltpu.VMEM((4, C, ALL), BF16),
            pltpu.VMEM((ALL, C), BF16),
            pltpu.VMEM((4, ALL, C), BF16),
            pltpu.VMEM((4, ALL, C), BF16),
            pltpu.VMEM((ALL, C), BF16),
            pltpu.VMEM((2 * SLOTS, C), F32),
            DMA((5,)),
            DMA((5,)),
            DMA((5,)),
            DMA((PAIRS, lines - 1)),
            DMA((PAIRS, lines - 1)),
            DMA((PAIRS,)),
            DMA((PAIRS, 2)),
            DMA((PAIRS, 2)),
            DMA((PAIRS, 2)),
            DMA((PAIRS, 2)),
            DMA((PAIRS, 4)),
            DMA((PAIRS, 4)),
            DMA((n_head - 1,)),
            DMA((n_head - 1,)),
            DMA((n_dp - 1,)),
            DMA((n_dp - 1,)),
            DMA((n_dp - 1,)),
            DMA((n_dp - 1,)),
            DMA((FAR,)),
            DMA((6,)),
            DMA((2,)),
            DMA((8,)),
            DMA((7,)),
            DMA((7,)),
        ],
        compiler_params=pltpu.CompilerParams(
            collective_id=0, has_side_effects=True, vmem_limit_bytes=62 * 2**20
        ),
        name="gather_forward",
    )(
        *weights,
        images,
        cotangent,
        counts,
        labels,
        levels,
        class_table,
        noise_table,
        modw,
        modb,
        *vectors,
    )


BACK_FAR = (10, 8)
BACK_NEAR = tuple(i for i in range(PAIRS) if i not in BACK_FAR)
AHEAD = 3


def backward_kernel(
    lines,
    whole_ref,
    turned_ref,
    right_ref,
    grad_low_ref,
    grad_resid_ref,
    conv_ref,
    slopes_ref,
    images_hbm,
    stats_ref,
    vecs_ref,
    mod_ref,
    sums_in,
    pre_ref,
    ids_ref,
    modw_table,
    out_a,
    out_b,
    out_qkv,
    out_proj,
    image_ref,
    class_ref,
    modw_out,
    modb_out,
    vec_out,
    mine,
    from_x,
    from_y,
    from_z,
    far_x,
    far_y,
    far_z,
    ends,
    modw_ref,
    lefts,
    rights,
    grads,
    stage,
    stage_mine,
    weights,
    total,
    board,
    slopes,
    image_mine,
    images_ref,
    sums_ref,
    pair_ref,
    coef_ref,
    gm_mine,
    gm_all,
    mw_mine,
    mw_got,
    ge_all,
    vs_mine,
    vs_got,
    vt_mine,
    vt_all,
    x_send,
    x_recv,
    y_send,
    y_recv,
    z_send,
    z_recv,
    p_send,
    p_recv,
    e_send,
    e_recv,
    e_local,
    op_send,
    op_recv,
    op_local,
    load_sem,
    in_sem,
    out_sem,
    gm_send,
    gm_recv,
    mw_send,
    mw_recv,
    ge_send,
    ge_recv,
    vs_send,
    vs_recv,
    vt_send,
    vt_recv,
):
    z, y, x, c = place()
    d, h = lax.axis_index("dp"), lax.axis_index("head")
    n_dp, n_head = lines * 2, 4
    half = lines // 2
    inner = jnp.logical_and(z > 0, z < lines - 1)
    rows, wide = from_z.shape[2], from_z.shape[3]
    cols = wide // 2
    sibling = at_chip(z, y, x, 1 - c)
    along_x = at_chip(z, y, 1 - x, c)
    along_y = at_chip(z, 1 - y, x, c)
    line = [at_chip(lax.rem(z + k, lines), y, x, c) for k in range(1, lines)]
    column, heads = column_peers(n_dp), head_peers(n_head)

    own_rows = pl.ds(LINE, ALL)

    def op_own(k):
        source, place_of = (
            (right_ref.at[2 + c], rights.at[0]),
            (turned_ref.at[c], lefts.at[1]),
            (right_ref.at[c], rights.at[1]),
            (turned_ref.at[0], lefts.at[0]),
            (grad_low_ref, grads.at[1, c, own_rows]),
            (turned_ref.at[2], lefts.at[2]),
            (turned_ref.at[3], lefts.at[3]),
        )[k]
        return pltpu.make_async_copy(source, place_of, op_local.at[k])

    def low_copy():
        return remote(grad_low_ref, grads.at[1, c, own_rows], op_send.at[0], op_recv.at[0], sibling)

    def stage_copy():
        return remote(stage_mine, stage, op_send.at[1], op_recv.at[1], sibling)

    def lanes(xx):
        return span(xx, wide)

    first, second = pl.ds(0, rows // 2), pl.ds(rows // 2, rows // 2)

    def is_far(i):
        return i in BACK_FAR

    def x_copy(i, part):
        if is_far(i):
            into = far_x.at[BACK_FAR.index(i)]
            if part == 0:
                src, dst = mine.at[i, z, 1 - y, second, lanes(1 - x)], into.at[pl.ds(rows, rows // 2)]
            else:
                src, dst = mine.at[i, z, y, :, lanes(1 - x)], into.at[pl.ds(0, rows)]
        elif part == 0:
            src, dst = mine.at[i, pl.ds(half, half), 1 - y, :, lanes(1 - x)], from_x.at[BACK_NEAR.index(i), pl.ds(lines, half)]
        else:
            src, dst = mine.at[i, :, y, :, lanes(1 - x)], from_x.at[BACK_NEAR.index(i), pl.ds(0, lines)]
        return remote(src, dst, x_send.at[i, part], x_recv.at[i, part], along_x)

    def y_copy(i, part):
        if is_far(i):
            into = far_y.at[BACK_FAR.index(i)]
            if part == 0:
                src, dst = mine.at[i, z, 1 - y, first, lanes(1 - x)], into.at[pl.ds(rows, rows // 2)]
            else:
                src, dst = mine.at[i, z, 1 - y, :, lanes(x)], into.at[pl.ds(0, rows)]
        elif part == 0:
            src, dst = mine.at[i, pl.ds(0, half), 1 - y, :, lanes(1 - x)], from_y.at[BACK_NEAR.index(i), pl.ds(lines, half)]
        else:
            src, dst = mine.at[i, :, 1 - y, :, lanes(x)], from_y.at[BACK_NEAR.index(i), pl.ds(0, lines)]
        return remote(src, dst, y_send.at[i, part], y_recv.at[i, part], along_y)

    beyond = lax.rem(z + 2, lines)
    opposite = lines - 1 - z
    near_end = at_chip(1 + z // (lines - 1), y, x, c)

    def z_block(i, zz):
        return mine.at[i, zz] if is_far(i) else mine.at[i, zz, y, :, lanes(x)]

    def z_slot(i, k):
        return far_z.at[BACK_FAR.index(i), k] if is_far(i) else from_z.at[BACK_NEAR.index(i), k]

    def z_copy(i, k):
        return remote(
            z_block(i, lax.rem(z + k + 1, lines)), z_slot(i, k), z_send.at[i, k], z_recv.at[i, k], line[k]
        )

    def z_give(i):
        return remote(z_block(i, opposite), z_slot(i, 3), p_send.at[i], p_recv.at[i], near_end)

    def z_start(i):
        @pl.when(jnp.logical_not(inner))
        def _():
            z_give(i).start()

        @pl.when(z < lines - 1)
        def _():
            z_copy(i, 0).start()

        @pl.when(z > 0)
        def _():
            z_copy(i, 2).start()

        @pl.when(jnp.logical_not(inner))
        def _():
            z_copy(i, 1).start()

    def z_mix(i):
        @pl.when(inner)
        def _():
            z_give(i).wait_recv()
            if is_far(i):
                mine[i, beyond] += far_z[BACK_FAR.index(i), 3]
            else:
                mine[i, beyond, y, :, lanes(x)] += from_z[BACK_NEAR.index(i), 3]
            z_copy(i, 1).start()

    def z_wait(i):
        z_copy(i, 1).wait_recv()

        @pl.when(z > 0)
        def _():
            z_copy(i, 0).wait_recv()

        @pl.when(z < lines - 1)
        def _():
            z_copy(i, 2).wait_recv()

    def z_drain(i):
        z_copy(i, 1).wait_send()

        @pl.when(z < lines - 1)
        def _():
            z_copy(i, 0).wait_send()

        @pl.when(z > 0)
        def _():
            z_copy(i, 2).wait_send()

        @pl.when(jnp.logical_not(inner))
        def _():
            z_give(i).wait_send()

    def target(i, core):
        if isinstance(i, int) and i == 10:
            return out_proj if core == 1 else out_qkv.at[2]
        if isinstance(i, int) and i == 9:
            return out_qkv.at[core]
        if isinstance(i, int) and i == 4:
            return out_b.at[8] if core == 1 else out_a.at[8]
        if isinstance(i, int) and i > 4:
            return out_b.at[4 * core + i - 5]
        return out_a.at[4 * core + i]

    def e_copy(i, core):
        return remote(ends.at[1 - c, i], target(i, core), e_send.at[i], e_recv.at[i], sibling)

    def e_own(i, core):
        return pltpu.make_async_copy(ends.at[c, i], target(i, core), e_local.at[i])

    def finish(i, value):
        for cc in range(2):
            ends[cc, i] = value[:, cc * cols : (cc + 1) * cols]
        if i in (4, 10):
            for core in range(2):

                @pl.when(c == core)
                def _():
                    e_copy(i, core).start()
                    e_own(i, core).start()
        else:
            e_copy(i, c).start()
            e_own(i, c).start()

    def offer(i):
        x_copy(i, 0).start()
        y_copy(i, 0).start()

    def relay(i):
        x_copy(i, 0).wait_recv()
        y_copy(i, 0).wait_recv()
        if is_far(i):
            rest = pl.ds(rows, rows // 2)
            mine[i, z, y, first, lanes(1 - x)] += far_y[BACK_FAR.index(i), rest]
            mine[i, z, 1 - y, second, lanes(x)] += far_x[BACK_FAR.index(i), rest]
        else:
            for j in range(half):
                mine[i, j, y, :, lanes(1 - x)] += from_y[BACK_NEAR.index(i), lines + j]
                mine[i, half + j, 1 - y, :, lanes(x)] += from_x[BACK_NEAR.index(i), lines + j]
        x_copy(i, 1).start()
        y_copy(i, 1).start()

    def collect(i):
        x_copy(i, 1).wait_recv()
        y_copy(i, 1).wait_recv()
        if is_far(i):
            whole_rows = pl.ds(0, rows)
            value = mine[i, z, y, :, lanes(x)].astype(F32)
            value += far_x[BACK_FAR.index(i), whole_rows].astype(F32) + far_y[BACK_FAR.index(i), whole_rows].astype(F32)
            finish(i, value)
            return

        def add(j):
            value = mine[i, j, y, :, lanes(x)].astype(F32)
            value += from_x[BACK_NEAR.index(i), j].astype(F32) + from_y[BACK_NEAR.index(i), j].astype(F32)
            mine[i, j, y, :, lanes(x)] = value.astype(BF16)

        each(lines, add)
        z_start(i)

    def last(i):
        z_wait(i)
        if is_far(i):
            for yy in range(2):
                value = mine[i, z, yy].astype(F32)
                for k in range(lines - 1):
                    value += far_z[BACK_FAR.index(i), k, yy].astype(F32)
                mine[i, z, yy] = value.astype(BF16)
            offer(i)
            return
        value = mine[i, z, y, :, lanes(x)].astype(F32)
        for k in range(lines - 1):
            value += from_z[BACK_NEAR.index(i), k].astype(F32)
        finish(i, value)

    def put(i, n, value):
        mine[i, :, :, :, chunk(n)] = value.astype(BF16).reshape(mine.shape[1:4] + (WIDTH,))

    def plain_unit(i, left, right):
        for n in range(CHUNKS):
            put(i, n, dot(lefts[left], rights[right, :, chunk(n)]))

    def conv_unit(i, left, tap):
        where, side = lines_from(2 - tap // 3), 2 - tap % 3
        for n in range(CHUNKS):
            both = jnp.concatenate([grads[side, core, where, chunk(n)] for core in range(2)], axis=0)
            put(i, n, dot(lefts[left], both))

    def extra_b():
        @pl.when(c == 1)
        def _():
            conv_unit(4, 2, 8)

    def extra_a():
        @pl.when(c == 0)
        def _():
            conv_unit(4, 3, 8)

    def spread_sides(core):
        def by_line(yy):
            value = grads[1, core, pl.ds(pl.multiple_of((yy + 1) * LINE, LINE), LINE)].astype(F32)
            left, right = shifted(value)
            spot_rows = pl.ds(pl.multiple_of((yy + 1) * LINE, LINE), LINE)
            grads[0, core, spot_rows] = left.astype(BF16)
            grads[2, core, spot_rows] = right.astype(BF16)

        each(RES, by_line)

    def load(tap, base):
        ninth = tap // 8
        i = (base // 2 + tap % 4) * (1 - ninth) + 4 * ninth
        k = (tap // 4) % 2 + (base // 10) * ninth
        return pltpu.make_async_copy(whole_ref.at[i, k], weights.at[tap % (AHEAD + 1)], load_sem.at[tap % (AHEAD + 1)])

    def conv_back(tap, base):
        load(tap, base).wait()

        @pl.when(tap < 9 - AHEAD)
        def _():
            load(tap + AHEAD, base).start()

        part = grads[2 - tap % 3, c, lines_from(2 - tap // 3)]
        for n in range(CHUNKS):
            value = dot_nt(part, weight_rows(weights.at[tap % (AHEAD + 1)], n))
            total[:, :, :, chunk(n)] += value.reshape(RES, SLOTS, RES, WIDTH)

    def conv_back_range(first, stop, base):
        def body(tap, carry):
            conv_back(tap, base)
            return carry

        lax.fori_loop(first, stop, body, 0)

    def slope(values):
        sigma = jax.nn.sigmoid(values)
        return sigma * (1.0 + values * (1.0 - sigma))

    for k in (0, 2):
        from_z[:, k] = jnp.zeros_like(from_z[:, k])
        far_z[:, k] = jnp.zeros_like(far_z[:, k])
    greet(column + heads)
    low_copy().start()
    for k in (4, 0, 1, 2, 3, 5):
        op_own(k).start()
    for tap in range(AHEAD):
        load(tap, 10).start()

    def fetch(k):
        source, target = (
            (conv_ref, board),
            (slopes_ref.at[1], slopes),
            (slopes_ref.at[0], slopes),
            (grad_resid_ref, board),
            (images_hbm, images_ref),
        )[k]
        return pltpu.make_async_copy(source, target, in_sem.at[k])

    fetch(0).start()
    fetch(1).start()
    vs_mine[...] = jnp.zeros_like(vs_mine)
    edge = jnp.zeros((LINE, C), BF16)
    for j in range(3):
        for core in range(2):
            grads[j, core, 0:LINE] = edge
            grads[j, core, ALL + LINE : ALL + 2 * LINE] = edge
    total[...] = jnp.zeros_like(total)
    sums_ref[...] = sums_in[...]
    modw_ref[...] = jnp.zeros_like(modw_ref)
    table = modw_table[...].astype(F32)
    for k in range(2):
        modw_ref[0:rows, k * C : (k + 1) * C] = table[:, k].astype(BF16)

    def norm_b_value(n):
        return (board[:, n].reshape(PIX, C) - stats_ref[2, row(n)]) * stats_ref[3, row(n)]

    def norm_a_value(n):
        return (images_ref[span(n, PIX)].astype(F32) - stats_ref[0, row(n)]) * stats_ref[1, row(n)]

    def back_sums(get):
        def body(n):
            grad = (total[:, n] * slopes[:, n]).reshape(PIX, C)
            total[:, n] = grad.reshape(RES, RES, C)
            pair_ref[row(n)] = sum_rows(grad * get(n))
            pair_ref[row(SLOTS + n)] = sum_rows(grad)

        each(SLOTS, body)

    def back_factors(factor, inverse):
        coef_ref[0:SLOTS] = factor * inverse
        means = group_mean(pair_ref[...] * jnp.concatenate([factor, factor], axis=0))
        coef_ref[SLOTS : 2 * SLOTS] = means[:SLOTS] * inverse
        coef_ref[2 * SLOTS :] = means[SLOTS:] * inverse

    def back_value(n, get):
        value = total[:, n].reshape(PIX, C) * coef_ref[row(n)]
        return value - get(n) * coef_ref[row(SLOTS + n)] - coef_ref[row(2 * SLOTS + n)]

    def gm_copy(k):
        return remote(gm_mine, gm_all.at[d], gm_send.at[k], gm_recv.at[k], column[k])

    def mw_copy(k):
        return remote(
            mw_mine.at[lax.rem(h + k + 1, n_head)], mw_got.at[k], mw_send.at[k], mw_recv.at[k], heads[k]
        )

    def ge_copy(k):
        return remote(ge_all.at[h], ge_all.at[h], ge_send.at[k], ge_recv.at[k], heads[k])

    def vs_copy(k):
        return remote(
            vs_mine.at[lax.rem(h + k + 1, n_head)], vs_got.at[k], vs_send.at[k], vs_recv.at[k], heads[k]
        )

    def vt_copy(k):
        return remote(vt_mine, vt_all.at[d], vt_send.at[k], vt_recv.at[k], column[k])

    def image_copy():
        return pltpu.make_async_copy(image_mine, image_ref, out_sem)

    count = n_dp * SLOTS

    def start():
        op_own(0).wait()
        op_own(1).wait()

    def dw(i):
        if i == 10:
            plain_unit(10, 1, 0)
        elif i == 9:
            op_own(2).wait()
            op_own(3).wait()
            plain_unit(9, 0, 1)
        elif i > 4:
            conv_unit(i, 2, 4 * c + i - 5)
        else:
            conv_unit(i, 3, 4 * c + i)

    def sides():
        op_own(4).wait()
        low_copy().wait_recv()
        op_own(5).wait()
        spread_sides(0)
        spread_sides(1)

    def back_b_first():
        for tap in range(AHEAD):
            load(tap, 0).start()
        op_own(6).start()
        fetch(0).wait()
        fetch(1).wait()
        back_sums(norm_b_value)
        alone, with_norm = pair_ref[SLOTS:], pair_ref[:SLOTS]
        scale = mod_ref[0:SLOTS] + 1.0
        gm_mine[...] = jnp.concatenate([vecs_ref[3:4] * with_norm + vecs_ref[4:5] * alone, alone], axis=0).astype(BF16)
        gm_all[d] = gm_mine[...]
        for k in range(n_dp - 1):
            gm_copy(k).start()
        sums_ref[3:4] = sum_rows(with_norm * scale)
        sums_ref[4:5] = sum_rows(alone * scale)
        back_factors(scale * vecs_ref[3:4], stats_ref[3])

    def back_b_second():
        fetch(2).start()
        fetch(4).start()

        def body(n):
            value = back_value(n, norm_b_value).astype(BF16).astype(F32)
            sums_ref[2:3] += sum_rows(value)
            total[:, n] = value.reshape(RES, RES, C)

        each(SLOTS, body)
        fetch(3).start()

    def lower():
        def by_line(yy):
            stage_mine[span(yy, LINE)] = total[yy].reshape(LINE, C).astype(BF16)

        each(RES, by_line)
        stage_copy().start()
        total[...] = jnp.zeros_like(total)

    def take():
        stage_copy().wait_recv()

        def by_line(yy):
            spot_rows = pl.ds(pl.multiple_of((yy + 1) * LINE, LINE), LINE)
            grads[1, c, spot_rows] = stage_mine[span(yy, LINE)]
            grads[1, 1 - c, spot_rows] = stage[span(yy, LINE)]

        each(RES, by_line)
        spread_sides(0)
        spread_sides(1)
        op_own(6).wait()

    def modulation():
        for k in range(n_dp - 1):
            gm_copy(k).wait()
        parts = gm_all[...].astype(F32)
        gm_scale = parts[:, :SLOTS].reshape(count, C)
        gm_offset = parts[:, SLOTS:].reshape(count, C)
        pre = pre_ref[...]
        emb = silu(pre).astype(BF16)
        part_rows = rows // n_head
        for k, value in ((0, gm_scale), (1, gm_offset)):
            low_value = value.astype(BF16)
            grad_w = dot_tn(emb, low_value)
            place_lanes = slice(k * C, (k + 1) * C)
            for hh in range(n_head):
                mw_mine[hh, 0:part_rows, place_lanes] = grad_w[hh * part_rows : (hh + 1) * part_rows]
                mw_mine[hh, part_rows : part_rows + 8, place_lanes] = jnp.broadcast_to(sum_rows(value), (8, C))
        grad_e = dot_nt(gm_scale.astype(BF16), modw_ref[:, :C]) + dot_nt(gm_offset.astype(BF16), modw_ref[:, C:])
        grad_e = grad_e * slope(pre)
        label = ids_ref[...].reshape(count, 128)[:, 0:1].astype(F32)
        lane = lax.broadcasted_iota(jnp.int32, grad_e.shape, 1)
        ge_all[h] = jnp.where(lane < rows, grad_e, label)
        for k in range(n_head - 1):
            mw_copy(k).start()
            ge_copy(k).start()

    def back_a_first():
        fetch(2).wait()
        fetch(4).wait()
        back_sums(norm_a_value)
        sums_ref[0:1] = sum_rows(pair_ref[:SLOTS])
        sums_ref[1:2] = sum_rows(pair_ref[SLOTS:])
        for hh in range(n_head):
            vs_mine[hh] = sums_ref[:, hh * cols : (hh + 1) * cols]
        for k in range(n_head - 1):
            vs_copy(k).start()
        back_factors(jnp.broadcast_to(vecs_ref[0:1], (SLOTS, C)), stats_ref[1])

    def back_a_second():
        fetch(3).wait()

        def body(n):
            image_mine[span(n, PIX)] = back_value(n, norm_a_value) + board[:, n].reshape(PIX, C)

        each(SLOTS, body)
        image_copy().start()

    def vec_first():
        value = vs_mine[h]
        for k in range(n_head - 1):
            vs_copy(k).wait()
            value += vs_got[k]
        vt_mine[...] = value
        vt_all[d] = value
        for k in range(n_dp - 1):
            vt_copy(k).start()

    def mod_out():
        value = mw_mine[h]
        for k in range(n_head - 1):
            mw_copy(k).wait()
            value += mw_got[k]
        part_rows = rows // n_head
        first_lane = (d * n_head + h) * part_rows
        for k in range(2):
            lanes_of = slice(k * C, (k + 1) * C)
            modw_out[:, k] = value[:part_rows, lanes_of]
            turned_row = pltpu.roll(value[part_rows:, lanes_of], lax.rem(C - first_lane, C), 1)
            modb_out[k : k + 1] = turned_row[0:1, :part_rows]

    def class_out():
        for k in range(n_head - 1):
            ge_copy(k).wait()
        table = class_ref.shape[1]
        part = rows // n_head
        value = ge_all[...].reshape(n_head * count, 128)
        label = value[:, rows : rows + 1].astype(jnp.int32)
        hot = lax.broadcasted_iota(jnp.int32, (n_head * count, table), 1) == label
        own = pltpu.roll(value, lax.rem(128 - h * part, 128), 1).astype(BF16)
        value = dot_tn(own, jnp.where(hot, 1.0, 0.0).astype(BF16))
        class_ref[...] = value[:part]

    def vec_second():
        for k in range(n_dp - 1):
            vt_copy(k).wait()
        value = vt_all[0]
        for k in range(1, n_dp):
            value += vt_all[k]
        vec_out[...] = value

    start()
    sides()
    dw(5)
    offer(5)
    dw(7)
    offer(7)
    dw(10)
    z_start(10)
    dw(9)
    offer(9)
    dw(6)
    offer(6)
    conv_back_range(0, 3, 10)
    relay(9)
    dw(8)
    z_start(8)
    relay(7)
    conv_back_range(3, 6, 10)
    relay(6)
    conv_back_range(6, 9, 10)
    relay(5)
    back_b_first()
    back_b_second()
    lower()
    z_mix(10)
    extra_b()
    take()
    dw(2)
    offer(2)
    dw(0)
    offer(0)
    dw(3)
    z_mix(8)
    extra_a()
    collect(6)
    relay(2)
    conv_back_range(0, 3, 0)
    collect(5)
    offer(4)
    relay(0)
    dw(1)
    z_mix(6)
    offer(1)
    offer(3)
    collect(7)
    conv_back_range(3, 6, 0)
    collect(2)
    last(8)
    z_mix(5)
    z_mix(2)
    collect(0)
    collect(9)
    relay(4)
    relay(1)
    conv_back_range(6, 9, 0)
    modulation()
    z_mix(9)
    relay(3)
    relay(8)
    collect(4)
    back_a_first()
    z_mix(4)
    z_mix(7)
    z_mix(0)
    class_out()
    last(5)
    collect(1)
    vec_first()
    last(10)
    z_mix(1)
    back_a_second()
    collect(3)
    vec_second()
    last(9)
    relay(10)
    z_mix(3)
    last(4)
    mod_out()
    last(6)
    last(7)
    collect(8)
    last(0)
    last(2)
    collect(10)
    last(1)
    last(3)

    low_copy().wait_send()
    stage_copy().wait_send()
    image_copy().wait()

    def drain(i):
        for part in range(2):
            x_copy(i, part).wait_send()
            y_copy(i, part).wait_send()
        z_drain(i)
        e_copy(i, 0).wait()
        e_own(i, 0).wait()

    for i in range(PAIRS):
        drain(i)


def run_backward(whole, turned, right, grad_low, grad_resid, conv_out, slopes, images, stats, vecs, mod, sums, pre, ids, modw, classes):
    n_dp, n_head = lax.axis_size("dp"), lax.axis_size("head")
    _, _, lines, _, rows, depth = whole.shape
    cols = depth // n_head
    wide = 2 * cols
    board = (RES, SLOTS, RES, C)
    shape = jax.ShapeDtypeStruct
    return pl.pallas_call(
        functools.partial(backward_kernel, lines),
        out_shape=(
            shape((9, rows, cols), F32),
            shape((9, rows, cols), F32),
            shape((3, rows, cols), F32),
            shape((rows, cols), F32),
            shape((ALL, C), F32),
            shape((rows // n_head, classes), F32),
            shape((rows // n_head, 2, C), F32),
            shape((2, rows // n_head), F32),
            shape((16, cols), F32),
        ),
        in_specs=[ANY] * 8 + [VMEM] * 7,
        out_specs=(ANY,) * 5 + (VMEM,) * 4,
        scratch_shapes=[
            pltpu.VMEM((PAIRS, lines, 2, rows, depth), BF16),
            pltpu.VMEM((len(BACK_NEAR), lines + lines // 2, rows, wide), BF16),
            pltpu.VMEM((len(BACK_NEAR), lines + lines // 2, rows, wide), BF16),
            pltpu.VMEM((len(BACK_NEAR), 4, rows, wide), BF16),
            pltpu.VMEM((len(BACK_FAR), rows + rows // 2, wide), BF16),
            pltpu.VMEM((len(BACK_FAR), rows + rows // 2, wide), BF16),
            pltpu.VMEM((len(BACK_FAR), 4, 2, rows, depth), BF16),
            pltpu.VMEM((2, PAIRS, rows, cols), F32),
            pltpu.VMEM((128, 2 * C), BF16),
            pltpu.VMEM((4, C, 2 * ALL), BF16),
            pltpu.VMEM((2, 2 * ALL, C), BF16),
            pltpu.VMEM((3, 2, ALL + 2 * LINE, C), BF16),
            pltpu.VMEM((ALL, C), BF16),
            pltpu.VMEM((ALL, C), BF16),
            pltpu.VMEM((AHEAD + 1, lines, 2, rows, depth), BF16),
            pltpu.VMEM(board, F32),
            pltpu.VMEM(board, F32),
            pltpu.VMEM(board, F32),
            pltpu.VMEM((ALL, C), F32),
            pltpu.VMEM((ALL, C), BF16),
            pltpu.VMEM((16, C), F32),
            pltpu.VMEM((2 * SLOTS, C), F32),
            pltpu.VMEM((3 * SLOTS, C), F32),
            pltpu.VMEM((2 * SLOTS, C), BF16),
            pltpu.VMEM((n_dp, 2 * SLOTS, C), BF16),
            pltpu.VMEM((n_head, rows // n_head + 8, 2 * C), F32),
            pltpu.VMEM((n_head - 1, rows // n_head + 8, 2 * C), F32),
            pltpu.VMEM((n_head, n_dp * SLOTS, 128), F32),
            pltpu.VMEM((n_head, 16, cols), F32),
            pltpu.VMEM((n_head - 1, 16, cols), F32),
            pltpu.VMEM((16, cols), F32),
            pltpu.VMEM((n_dp, 16, cols), F32),
            DMA((PAIRS, 2)),
            DMA((PAIRS, 2)),
            DMA((PAIRS, 2)),
            DMA((PAIRS, 2)),
            DMA((PAIRS, lines - 1)),
            DMA((PAIRS, lines - 1)),
            DMA((PAIRS,)),
            DMA((PAIRS,)),
            DMA((PAIRS,)),
            DMA((PAIRS,)),
            DMA((PAIRS,)),
            DMA((2,)),
            DMA((2,)),
            DMA((7,)),
            DMA((AHEAD + 1,)),
            DMA((5,)),
            DMA,
            DMA((n_dp - 1,)),
            DMA((n_dp - 1,)),
            DMA((n_head - 1,)),
            DMA((n_head - 1,)),
            DMA((n_head - 1,)),
            DMA((n_head - 1,)),
            DMA((n_head - 1,)),
            DMA((n_head - 1,)),
            DMA((n_dp - 1,)),
            DMA((n_dp - 1,)),
        ],
        compiler_params=pltpu.CompilerParams(
            collective_id=1, has_side_effects=True, vmem_limit_bytes=64 * 2**20 - 2**18
        ),
        name="backward_scatter",
    )(whole, turned, right, grad_low, grad_resid, conv_out, slopes, images, stats, vecs, mod, sums, pre, ids, modw)


def results_kernel(count, *refs):
    sources, vec_ref, refs = refs[:count], refs[count], refs[count + 1 :]
    targets, vectors, sems = refs[:count], refs[count:-1], refs[-1]
    copies = [
        pltpu.make_async_copy(source, target, sems.at[k])
        for k, (source, target) in enumerate(zip(sources, targets))
    ]
    for copy in copies:
        copy.start()
    for k, ref in enumerate(vectors):
        ref[...] = vec_ref[k].reshape(ref.shape)
    for copy in copies:
        copy.wait()


def run_results(arrays, vec):
    count = len(arrays)
    shape = jax.ShapeDtypeStruct
    return pl.pallas_call(
        functools.partial(results_kernel, count),
        out_shape=tuple(shape(one.shape, one.dtype) for one in arrays)
        + (shape(vec.shape[1:], F32),) * VECTORS,
        in_specs=[VMEM] * (count + 1),
        out_specs=(ANY,) * count + (VMEM,) * VECTORS,
        scratch_shapes=[DMA((count,))],
        compiler_params=pltpu.CompilerParams(vmem_limit_bytes=60 * 2**20),
        name="results",
    )(*arrays, vec)


def direct(rows, cols):
    n_dp, n_head = lax.axis_size("dp"), lax.axis_size("head")
    return n_head == 4 and n_dp == 8 and rows % 32 == 0 and cols % 64 == 0


def fast_shards(
    images,
    cotangent,
    counts,
    labels,
    levels,
    noise_table,
    class_table,
    gain_a,
    shift_a,
    conv_a,
    bias_a,
    mod_weight,
    mod_bias,
    gain_b,
    shift_b,
    conv_b,
    bias_b,
    gain_c,
    shift_c,
    qkv_weight,
    proj_weight,
    proj_bias,
):
    weights = (
        jnp.swapaxes(conv_a, 0, 1),
        jnp.swapaxes(conv_b, 0, 1),
        jnp.swapaxes(qkv_weight, 0, 1),
        proj_weight,
    )
    vectors = (gain_a, shift_a, bias_a, gain_b, shift_b, bias_b, gain_c, shift_c, proj_bias)
    flat = images.reshape(ALL, C)
    (
        whole,
        conv_out,
        slopes,
        turned,
        block_out,
        grad_resid,
        grad_low,
        right,
        vecs,
        mod,
        stats,
        pre,
        all_ids,
        sums,
    ) = run_forward(
        weights,
        flat,
        cotangent.reshape(ALL, C),
        counts.T,
        labels,
        levels,
        class_table.T,
        noise_table,
        mod_weight,
        mod_bias,
        vectors,
    )
    *arrays, vec = run_backward(
        whole,
        turned,
        right,
        grad_low,
        grad_resid,
        conv_out,
        slopes,
        flat,
        stats,
        vecs,
        mod,
        sums,
        pre,
        all_ids,
        mod_weight,
        class_table.shape[0],
    )
    block_out, conva, convb, qkvw, projw, image_grad, class_grad, modw_grad, modb_grad, *rest = run_results(
        (block_out, *arrays), vec
    )
    gaina, shifta, biasa, gainb, shiftb, biasb, gainc, shiftc, projb = rest
    return (
        block_out.reshape(images.shape),
        image_grad.reshape(images.shape),
        class_grad.T,
        gaina,
        shifta,
        jnp.swapaxes(conva, 0, 1),
        biasa,
        modw_grad,
        modb_grad,
        gainb,
        shiftb,
        jnp.swapaxes(convb, 0, 1),
        biasb,
        gainc,
        shiftc,
        jnp.swapaxes(qkvw, 0, 1),
        projw,
        projb,
    )


def shards(*args):
    rows, _, cols = args[9].shape
    if direct(rows, cols):
        return fast_shards(*args)
    return plain_shards(*args)


def solution(mesh):
    placed = (
        P(("dp", "head"), None, None, None),
        P(("dp", "head"), None, None, None),
        P(),
        P(("dp", "head")),
        P(("dp", "head")),
        P(),
        P(None, "dp"),
        P("head"),
        P("head"),
        P("dp", None, "head"),
        P("head"),
        P("dp", None, None),
        P(),
        P("head"),
        P("head"),
        P("dp", None, "head"),
        P("head"),
        P("head"),
        P("head"),
        P("dp", None, "head"),
        P("dp", "head"),
        P("head"),
    )
    return jax.shard_map(
        shards,
        mesh=mesh,
        in_specs=placed,
        out_specs=(
            P(("dp", "head"), None, None, None),
            P(("dp", "head"), None, None, None),
            P(None, ("dp", "head")),
            P("head"),
            P("head"),
            P("dp", None, "head"),
            P("head"),
            P(("dp", "head"), None, None),
            P(None, ("dp", "head")),
            P("head"),
            P("head"),
            P("dp", None, "head"),
            P("head"),
            P("head"),
            P("head"),
            P("dp", None, "head"),
            P("dp", "head"),
            P("head"),
        ),
        check_vma=False,
    )
```

```python
import functools

import jax
import jax.numpy as jnp
from jax import lax
from jax.experimental import pallas as pl
from jax.experimental.pallas import tpu as pltpu
from jax.sharding import PartitionSpec as P

C = 768
DH = 64
GROUPS = 32


EPSILON = 1e-05
HIGHEST = lax.Precision.HIGHEST


def norm_forward(values, gain, shift):
    count, chans = (values.shape[0], values.shape[-1])
    span = C // GROUPS
    grouped = values.reshape(count, -1, chans // span, span)
    mean = jnp.mean(grouped, axis=(1, 3), keepdims=True)
    centred = grouped - mean
    inverse = lax.rsqrt(jnp.mean(centred * centred, axis=(1, 3), keepdims=True) + EPSILON)
    normed = (centred * inverse).reshape(values.shape)
    return (normed * gain + shift, normed, inverse)


def norm_backward(grad_out, normed, inverse, gain):
    grad_gain = jnp.sum(grad_out * normed, axis=(0, 1, 2))
    grad_shift = jnp.sum(grad_out, axis=(0, 1, 2))
    count, chans = (grad_out.shape[0], grad_out.shape[-1])
    span = C // GROUPS
    layout = (count, -1, chans // span, span)
    grad_normed = (grad_out * gain).reshape(layout)
    normed_groups = normed.reshape(layout)
    mean_one = jnp.mean(grad_normed, axis=(1, 3), keepdims=True)
    mean_two = jnp.mean(grad_normed * normed_groups, axis=(1, 3), keepdims=True)
    grad_in = inverse * (grad_normed - mean_one - normed_groups * mean_two)
    return (grad_in.reshape(grad_out.shape), grad_gain, grad_shift)


def silu_slope(values):
    sigma = jax.nn.sigmoid(values)
    return sigma * (1.0 + values * (1.0 - sigma))


def patches_of(act):
    count, rows, cols, chans = act.shape
    padded = jnp.pad(act, ((0, 0), (1, 1), (1, 1), (0, 0)))
    taps = [padded[:, i : i + rows, j : j + cols, :] for i in range(3) for j in range(3)]
    return jnp.stack(taps, axis=3).reshape(count * rows * cols, 9, chans)


def contract_rows(left, right):
    return lax.dot_general(
        left, right, (((0,), (0,)), ((), ())), preferred_element_type=jnp.float32
    )


def contract_cols(left, right):
    return lax.dot_general(
        left, right, (((1,), (1,)), ((), ())), preferred_element_type=jnp.float32
    )


def conv_back(grad_low, weight, count, rows, cols):
    chans = weight.shape[0]
    padded = jnp.zeros((count, rows + 2, cols + 2, chans), jnp.float32)
    for tap in range(9):
        i, j = divmod(tap, 3)
        part = contract_cols(grad_low, weight[:, tap, :]).reshape(count, rows, cols, chans)
        padded = padded.at[:, i : i + rows, j : j + cols, :].add(part)
    return padded[:, 1 : rows + 1, 1 : cols + 1, :]


def keep_same(values):
    return values


def live_rows(counts, first, number, count):
    sums = jnp.sum(counts, axis=1)
    chosen = lax.dynamic_slice_in_dim(sums, first, number)
    slots = lax.iota(jnp.int32, count)
    return (slots[None, :] < chosen[:, None]).astype(jnp.float32).reshape(number * count)


def residual_forward(source, mod_pair, weights, spread):
    (
        conv_one,
        conv_two,
        gain_one,
        shift_one,
        bias_one,
        gain_two,
        shift_two,
        bias_two,
        gain_three,
        shift_three,
    ) = weights
    out_a, normed_a, inverse_a = norm_forward(source, gain_one, shift_one)
    wide_a = spread(jax.nn.silu(out_a).astype(jnp.bfloat16))
    conv_out_a = (
        jnp.einsum("ptc,cto->po", patches_of(wide_a), conv_one, preferred_element_type=jnp.float32)
        + bias_one
    ).reshape(source.shape)
    scale = mod_pair[:, :, 0:1, :]
    offset = mod_pair[:, :, 1:2, :]
    out_b, normed_b, inverse_b = norm_forward(conv_out_a, gain_two, shift_two)
    inner_b = offset + out_b * (scale + 1.0)
    wide_b = spread(jax.nn.silu(inner_b).astype(jnp.bfloat16))
    conv_out_b = (
        jnp.einsum("ptc,cto->po", patches_of(wide_b), conv_two, preferred_element_type=jnp.float32)
        + bias_two
    ).reshape(source.shape)
    resid = source + conv_out_b
    out_c, normed_c, inverse_c = norm_forward(resid, gain_three, shift_three)
    attn_in = out_c.astype(jnp.bfloat16)
    saved = (
        out_a,
        normed_a,
        inverse_a,
        wide_a,
        out_b,
        normed_b,
        inverse_b,
        inner_b,
        wide_b,
        normed_c,
        inverse_c,
        scale,
    )
    return (resid, attn_in, saved)


def residual_backward(grad_attn, grad_out, saved, weights, reduce_value):
    conv_one, conv_two, gain_one, gain_two, gain_three = (
        weights[0],
        weights[1],
        weights[2],
        weights[5],
        weights[8],
    )
    (
        out_a,
        normed_a,
        inverse_a,
        wide_a,
        out_b,
        normed_b,
        inverse_b,
        inner_b,
        wide_b,
        normed_c,
        inverse_c,
        scale,
    ) = saved
    count, rows, cols, local = grad_out.shape
    grad_resid_c, gainc_term, shiftc_term = norm_backward(
        grad_attn, normed_c, inverse_c, gain_three
    )
    grad_resid = grad_out + grad_resid_c
    grad_conv_b = grad_resid.reshape(-1, local).astype(jnp.bfloat16)
    biasb_term = jnp.sum(grad_conv_b.astype(jnp.float32), axis=0)
    convb_term = jnp.einsum(
        "ptc,po->cto", patches_of(wide_b), grad_conv_b, preferred_element_type=jnp.float32
    )
    grad_act_b = reduce_value(conv_back(grad_conv_b, conv_two, count, rows, cols))
    grad_inner = grad_act_b * silu_slope(inner_b)
    grad_offset = jnp.sum(grad_inner, axis=(1, 2))
    grad_scale = jnp.sum(grad_inner * out_b, axis=(1, 2))
    grad_mod = jnp.stack([grad_scale, grad_offset], axis=1)[:, None]
    grad_conv_full, gainb_term, shiftb_term = norm_backward(
        grad_inner * (scale + 1.0), normed_b, inverse_b, gain_two
    )
    grad_conv_a = grad_conv_full.reshape(-1, local).astype(jnp.bfloat16)
    biasa_term = jnp.sum(grad_conv_a.astype(jnp.float32), axis=0)
    conva_term = jnp.einsum(
        "ptc,po->cto", patches_of(wide_a), grad_conv_a, preferred_element_type=jnp.float32
    )
    grad_act_a = reduce_value(conv_back(grad_conv_a, conv_one, count, rows, cols))
    grad_source, gaina_term, shifta_term = norm_backward(
        grad_act_a * silu_slope(out_a), normed_a, inverse_a, gain_one
    )
    image_grad = grad_resid + grad_source
    vectors = (
        gaina_term,
        shifta_term,
        biasa_term,
        gainb_term,
        shiftb_term,
        biasb_term,
        gainc_term,
        shiftc_term,
    )
    return (image_grad, grad_mod, (conva_term, convb_term), vectors)


def attend_forward(block):
    query, key, value = (block[:, :, 0], block[:, :, 1], block[:, :, 2])
    batch, pixels, heads_here, depth = query.shape
    scores = jnp.einsum("bqhd,bkhd->bhqk", query, key, preferred_element_type=jnp.float32) * DH ** (
        -0.5
    )
    top = jnp.max(scores, axis=-1, keepdims=True)
    weights = jnp.exp(scores - top)
    sums = jnp.sum(weights, axis=-1, keepdims=True)
    probs = (weights / sums).astype(jnp.bfloat16)
    logsum = (top + jnp.log(sums))[..., 0]
    mixed = jnp.einsum("bhqk,bkhd->bqhd", probs, value, preferred_element_type=jnp.float32).astype(
        jnp.bfloat16
    )
    return (mixed.reshape(batch, pixels, heads_here * depth), logsum)


def attend_backward(block, logsum, grad_head):
    query, key, value = (block[:, :, 0], block[:, :, 1], block[:, :, 2])
    batch, pixels, heads_here, depth = query.shape
    factor = DH ** (-0.5)
    scores = jnp.einsum("bqhd,bkhd->bhqk", query, key, preferred_element_type=jnp.float32) * factor
    probs = jnp.exp(scores - logsum[..., None])
    grad_value = jnp.einsum(
        "bhqk,bqhd->bkhd", probs.astype(jnp.bfloat16), grad_head, preferred_element_type=jnp.float32
    )
    grad_probs = jnp.einsum("bqhd,bkhd->bhqk", grad_head, value, preferred_element_type=jnp.float32)
    inner = jnp.sum(grad_probs * probs, axis=-1, keepdims=True)
    grad_scores = (probs * (grad_probs - inner)).astype(jnp.bfloat16)
    grad_query = (
        jnp.einsum("bhqk,bkhd->bqhd", grad_scores, key, preferred_element_type=jnp.float32) * factor
    )
    grad_key = (
        jnp.einsum("bhqk,bqhd->bkhd", grad_scores, query, preferred_element_type=jnp.float32)
        * factor
    )
    stacked = jnp.stack([grad_query, grad_key, grad_value], axis=2).astype(jnp.bfloat16)
    return stacked.reshape(batch, pixels, 3, heads_here * depth)


def plain_shards(
    images,
    cotangent,
    counts,
    labels,
    levels,
    noise_table,
    class_table,
    gain_a,
    shift_a,
    conv_a,
    bias_a,
    mod_weight,
    mod_bias,
    gain_b,
    shift_b,
    conv_b,
    bias_b,
    gain_c,
    shift_c,
    qkv_weight,
    proj_weight,
    proj_bias,
):
    rows_a, rows_b, rows_qkv, rows_proj, mod_full, class_full = (
        lax.all_gather(conv_a, "dp", axis=0, tiled=True),
        lax.all_gather(conv_b, "dp", axis=0, tiled=True),
        lax.all_gather(qkv_weight, "dp", axis=0, tiled=True),
        lax.all_gather(proj_weight, "dp", axis=0, tiled=True),
        lax.all_gather(mod_weight, "dp", axis=0, tiled=True),
        lax.all_gather(class_table, "dp", axis=1, tiled=True),
    )
    count, rows, cols, channels = images.shape
    pixels = rows * cols
    groups_n = lax.axis_size("head")
    quarter = channels // groups_n
    heads_local = quarter // DH
    first_dp = lax.axis_index("dp") * groups_n
    class_hot = (labels[:, None] == lax.iota(jnp.int32, class_full.shape[0])[None, :]).astype(
        jnp.bfloat16
    )
    level_hot = (levels[:, None] == lax.iota(jnp.int32, noise_table.shape[0])[None, :]).astype(
        jnp.bfloat16
    )
    embed_pre = jnp.dot(class_hot, class_full, preferred_element_type=jnp.float32) + jnp.dot(
        level_hot, noise_table, preferred_element_type=jnp.float32
    )
    embed = jax.nn.silu(embed_pre).astype(jnp.bfloat16)
    modulation = (
        jnp.einsum("ne,etc->ntc", embed, mod_full, preferred_element_type=jnp.float32)
        + mod_bias.astype(jnp.float32)
    ).astype(jnp.bfloat16)
    mod_pair = modulation.reshape(count, 1, 2, channels)
    (
        conv_one,
        conv_two,
        qkv_full,
        proj_full,
        gain_one,
        shift_one,
        bias_one,
        gain_two,
        shift_two,
        bias_two,
        gain_three,
        shift_three,
        bias_three,
    ) = (
        lax.all_gather(rows_a, "head", axis=2, tiled=True),
        lax.all_gather(rows_b, "head", axis=2, tiled=True),
        lax.all_gather(rows_qkv, "head", axis=2, tiled=True),
        lax.all_gather(rows_proj, "head", axis=1, tiled=True),
        lax.all_gather(gain_a, "head", axis=0, tiled=True),
        lax.all_gather(shift_a, "head", axis=0, tiled=True),
        lax.all_gather(bias_a, "head", axis=0, tiled=True),
        lax.all_gather(gain_b, "head", axis=0, tiled=True),
        lax.all_gather(shift_b, "head", axis=0, tiled=True),
        lax.all_gather(bias_b, "head", axis=0, tiled=True),
        lax.all_gather(gain_c, "head", axis=0, tiled=True),
        lax.all_gather(shift_c, "head", axis=0, tiled=True),
        lax.all_gather(proj_bias, "head", axis=0, tiled=True),
    )
    weights = (
        conv_one,
        conv_two,
        gain_one,
        shift_one,
        bias_one,
        gain_two,
        shift_two,
        bias_two,
        gain_three,
        shift_three,
    )
    live = live_rows(counts, first_dp + lax.axis_index("head"), 1, count)
    total = count * pixels
    width = channels // groups_n
    source = images.astype(jnp.float32)
    resid, attn_in, saved = residual_forward(
        source, mod_pair.astype(jnp.float32), weights, keep_same
    )
    attn_flat = attn_in.reshape(total, channels)
    qkv_flat = qkv_full.reshape(channels, 3 * channels)
    qkv = jnp.dot(attn_flat, qkv_flat, preferred_element_type=jnp.float32).astype(jnp.bfloat16)
    packed = qkv.reshape(1, count, pixels, 3, groups_n, width)
    block = lax.all_to_all(packed, "head", split_axis=4, concat_axis=0, tiled=True)
    groups = block.shape[0]
    items = block.shape[1]
    flat = block.reshape(groups * items, pixels, 3, heads_local, DH)
    mixed, logsum = attend_forward(flat)
    mixed = mixed.reshape(groups, items, pixels, 1, width)
    returned = lax.all_to_all(mixed, "head", split_axis=0, concat_axis=3, tiled=True)
    returned, logsum, kept = (returned, logsum.reshape(groups, items, heads_local, pixels), block)
    mixed_image = returned.reshape(total, channels)
    result = (
        resid.reshape(total, channels)
        + jnp.dot(mixed_image, proj_full, preferred_element_type=jnp.float32)
        + bias_three
    )
    block_out = (result.reshape(images.shape) * live[:, None, None, None]).astype(jnp.bfloat16)
    grad_out = cotangent.astype(jnp.float32) * live[:, None, None, None]
    grad_flat = grad_out.reshape(total, channels)
    grad_low = grad_flat.astype(jnp.bfloat16)
    projw_full = contract_rows(mixed_image, grad_low)
    projb_full = jnp.sum(grad_flat, axis=0)
    grad_mixed = contract_cols(grad_low, proj_full).astype(jnp.bfloat16)
    arrived = lax.all_to_all(
        grad_mixed.reshape(1, count, pixels, groups_n, width),
        "head",
        split_axis=3,
        concat_axis=0,
        tiled=True,
    )
    flat_block = kept.reshape(groups_n * count, pixels, 3, heads_local, DH)
    grad_head = arrived.reshape(groups_n * count, pixels, heads_local, DH)
    stacked = attend_backward(
        flat_block, logsum.reshape(groups_n * count, heads_local, pixels), grad_head
    )
    stacked = stacked.reshape(groups_n, count, pixels, 3, 1, width)
    grad_qkv = lax.all_to_all(stacked, "head", split_axis=0, concat_axis=4, tiled=True).reshape(
        total, 3 * channels
    )
    qkvw_full = contract_rows(attn_flat, grad_qkv).reshape(channels, 3, channels)
    grad_attn = contract_cols(grad_qkv, qkv_flat).reshape(images.shape)
    image_grad, grad_mod_part, conv_terms, vectors = residual_backward(
        grad_attn, grad_out, saved, weights, keep_same
    )
    (
        gaina_full,
        shifta_full,
        biasa_full,
        gainb_full,
        shiftb_full,
        biasb_full,
        gainc_full,
        shiftc_full,
    ) = vectors
    (
        conva_term,
        convb_term,
        qkvw_term,
        projw_term,
        gaina_term,
        shifta_term,
        biasa_term,
        gainb_term,
        shiftb_term,
        biasb_term,
        gainc_term,
        shiftc_term,
        projb_term,
    ) = (
        lax.psum_scatter(
            conv_terms[0].astype(jnp.bfloat16), "head", scatter_dimension=2, tiled=True
        ).astype(jnp.float32),
        lax.psum_scatter(
            conv_terms[1].astype(jnp.bfloat16), "head", scatter_dimension=2, tiled=True
        ).astype(jnp.float32),
        lax.psum_scatter(
            qkvw_full.astype(jnp.bfloat16), "head", scatter_dimension=2, tiled=True
        ).astype(jnp.float32),
        lax.psum_scatter(
            projw_full.astype(jnp.bfloat16), "head", scatter_dimension=1, tiled=True
        ).astype(jnp.float32),
        lax.psum_scatter(
            gaina_full.astype(jnp.bfloat16), "head", scatter_dimension=0, tiled=True
        ).astype(jnp.float32),
        lax.psum_scatter(
            shifta_full.astype(jnp.bfloat16), "head", scatter_dimension=0, tiled=True
        ).astype(jnp.float32),
        lax.psum_scatter(
            biasa_full.astype(jnp.bfloat16), "head", scatter_dimension=0, tiled=True
        ).astype(jnp.float32),
        lax.psum_scatter(
            gainb_full.astype(jnp.bfloat16), "head", scatter_dimension=0, tiled=True
        ).astype(jnp.float32),
        lax.psum_scatter(
            shiftb_full.astype(jnp.bfloat16), "head", scatter_dimension=0, tiled=True
        ).astype(jnp.float32),
        lax.psum_scatter(
            biasb_full.astype(jnp.bfloat16), "head", scatter_dimension=0, tiled=True
        ).astype(jnp.float32),
        lax.psum_scatter(
            gainc_full.astype(jnp.bfloat16), "head", scatter_dimension=0, tiled=True
        ).astype(jnp.float32),
        lax.psum_scatter(
            shiftc_full.astype(jnp.bfloat16), "head", scatter_dimension=0, tiled=True
        ).astype(jnp.float32),
        lax.psum_scatter(
            projb_full.astype(jnp.bfloat16), "head", scatter_dimension=0, tiled=True
        ).astype(jnp.float32),
    )
    grad_mod = grad_mod_part.reshape(count, 2, channels)
    modw_term = jnp.einsum("ne,ntc->etc", embed.astype(jnp.float32), grad_mod, precision=HIGHEST)
    modb_term = jnp.sum(grad_mod, axis=0)
    grad_embed = jnp.einsum(
        "ntc,etc->ne", grad_mod, mod_full.astype(jnp.float32), precision=HIGHEST
    ) * silu_slope(embed_pre)
    class_term = lax.dot_general(
        class_hot.astype(jnp.float32), grad_embed, (((0,), (0,)), ((), ())), precision=HIGHEST
    )
    modw_grad, class_grad, modb_grad = (
        lax.psum_scatter(modw_term, ("dp", "head"), scatter_dimension=0, tiled=True),
        lax.psum_scatter(class_term, ("dp", "head"), scatter_dimension=1, tiled=True),
        lax.psum_scatter(modb_term, ("dp", "head"), scatter_dimension=1, tiled=True),
    )
    conva_grad, convb_grad, qkvw_grad, projw_grad = (
        lax.psum_scatter(conva_term, "dp", scatter_dimension=0, tiled=True),
        lax.psum_scatter(convb_term, "dp", scatter_dimension=0, tiled=True),
        lax.psum_scatter(qkvw_term, "dp", scatter_dimension=0, tiled=True),
        lax.psum_scatter(projw_term, "dp", scatter_dimension=0, tiled=True),
    )
    (
        gaina_grad,
        shifta_grad,
        biasa_grad,
        gainb_grad,
        shiftb_grad,
        biasb_grad,
        gainc_grad,
        shiftc_grad,
        projb_grad,
    ) = lax.psum(
        (
            gaina_term,
            shifta_term,
            biasa_term,
            gainb_term,
            shiftb_term,
            biasb_term,
            gainc_term,
            shiftc_term,
            projb_term,
        ),
        "dp",
    )
    return (
        block_out,
        image_grad,
        class_grad,
        gaina_grad,
        shifta_grad,
        conva_grad,
        biasa_grad,
        modw_grad,
        modb_grad,
        gainb_grad,
        shiftb_grad,
        convb_grad,
        biasb_grad,
        gainc_grad,
        shiftc_grad,
        qkvw_grad,
        projw_grad,
        projb_grad,
    )


MESH = pl.DeviceIdType.MESH
UNITS = 22
PAIRS = UNITS // 2
FAR = 9
VECTORS = 9
RES = 8
SLOTS = 8
PIX = RES * RES
LINE = SLOTS * RES
ALL = RES * LINE
WIDTH = 768
BAND = 256
F32 = jnp.float32
BF16 = jnp.bfloat16
ANY = pl.BlockSpec(memory_space=pl.ANY)
VMEM = pl.BlockSpec(memory_space=pltpu.VMEM)
SMEM = pl.BlockSpec(memory_space=pltpu.SMEM)
DMA = pltpu.SemaphoreType.DMA


def place():
    d, h = lax.axis_index("dp"), lax.axis_index("head")
    return d // 2, lax.rem(d, 2), h // 2, lax.rem(h, 2)


def at_chip(z, y, x, c):
    return (z * 2 + y, x * 2 + c)


def column_peers(n_dp):
    d, h = lax.axis_index("dp"), lax.axis_index("head")
    return [(lax.rem(d + k, n_dp), h) for k in range(1, n_dp)]


def head_peers(n_head):
    d, h = lax.axis_index("dp"), lax.axis_index("head")
    return [(d, lax.rem(h + k, n_head)) for k in range(1, n_head)]


def greet(devices):
    barrier = pltpu.get_barrier_semaphore()
    for device in devices:
        pl.semaphore_signal(barrier, inc=1, device_id=device, device_id_type=MESH)
    pl.semaphore_wait(barrier, len(devices))


def remote(src, dst, send, recv, device):
    return pltpu.make_async_remote_copy(
        src_ref=src, dst_ref=dst, send_sem=send, recv_sem=recv, device_id=device, device_id_type=MESH
    )


def each(count, body):
    def step(n, carry):
        body(n)
        return carry

    lax.fori_loop(0, count, step, 0)


def span(index, size):
    return pl.ds(pl.multiple_of(index * size, size), size)


def row(n):
    return pl.ds(n, 1)


def lines_from(i):
    return pl.ds(i * LINE if isinstance(i, int) else pl.multiple_of(i * LINE, LINE), ALL)


def dot(left, right):
    return jnp.dot(left, right, preferred_element_type=F32)


def dot_nt(left, right):
    return lax.dot_general(left, right, (((1,), (1,)), ((), ())), preferred_element_type=F32)


def dot_tn(left, right):
    return lax.dot_general(left, right, (((0,), (0,)), ((), ())), preferred_element_type=F32)


def in_group(first, second, axis):
    chan = lax.broadcasted_iota(jnp.int32, (first, second), axis)
    group = lax.broadcasted_iota(jnp.int32, (first, second), 1 - axis) * (C // GROUPS)
    inside = jnp.logical_and(chan >= group, chan < group + C // GROUPS)
    return jnp.where(inside, 1.0, 0.0).astype(BF16)


def pieces(values):
    high = values.astype(BF16).astype(F32)
    rest = values - high
    mid = rest.astype(BF16).astype(F32)
    return jnp.concatenate([high, mid, rest - mid], axis=0).astype(BF16)


def group_mean(sums):
    count = sums.shape[0]
    part = dot(pieces(sums), in_group(C, 128, 0))
    part = (part[:count] + part[count : 2 * count] + part[2 * count :]) * (1.0 / (PIX * (C // GROUPS)))
    back = dot(pieces(part), in_group(128, C, 1))
    return back[:count] + back[count : 2 * count] + back[2 * count :]


def sum_rows(values):
    return jnp.sum(values, axis=0, keepdims=True)


def norm_stats(get, mean_ref, inverse_ref, sums_ref):
    def first(n):
        sums_ref[row(n)] = sum_rows(get(n))

    each(SLOTS, first)
    mean_ref[...] = group_mean(sums_ref[...])

    def second(n):
        centred = get(n) - mean_ref[row(n)]
        sums_ref[row(n)] = sum_rows(centred * centred)

    each(SLOTS, second)
    inverse_ref[...] = lax.rsqrt(group_mean(sums_ref[...]) + EPSILON)


def silu(values):
    return values * jax.nn.sigmoid(values)


def shifted(values):
    spot = lax.rem(lax.broadcasted_iota(jnp.int32, values.shape, 0), RES)
    left = jnp.where(spot == 0, 0.0, pltpu.roll(values, 1, 0))
    right = jnp.where(spot == RES - 1, 0.0, pltpu.roll(values, values.shape[0] - 1, 0))
    return left, right


def chunk(n):
    return slice(n * WIDTH, (n + 1) * WIDTH)


CHUNKS = C // WIDTH


def weight_cols(ref, n):
    return ref[:, :, :, chunk(n)].reshape(C, WIDTH)


def weight_rows(ref, n):
    return ref[...].reshape(C, C)[chunk(n)]


def forward_kernel(
    lines,
    weights_a,
    weights_b,
    weights_qkv,
    weights_proj,
    images_hbm,
    cot_hbm,
    counts_ref,
    labels_ref,
    levels_ref,
    class_table,
    noise_table,
    modw_table,
    modb_ref,
    *refs,
):
    vectors, refs = refs[:VECTORS], refs[VECTORS:]
    forward_steps(
        lines,
        vectors,
        weights_a,
        weights_b,
        weights_qkv,
        weights_proj,
        images_hbm,
        cot_hbm,
        counts_ref,
        labels_ref,
        levels_ref,
        class_table,
        noise_table,
        modw_table,
        modb_ref,
        *refs,
    )


def forward_steps(
    lines,
    vectors,
    weights_a,
    weights_b,
    weights_qkv,
    weights_proj,
    images_hbm,
    cot_hbm,
    counts_ref,
    labels_ref,
    levels_ref,
    class_table,
    noise_table,
    modw_table,
    modb_ref,
    whole_out,
    conv_out,
    slopes_out,
    turned_out,
    block_out,
    grad_out,
    low_out,
    right_out,
    vecs_ref,
    mod_ref,
    stats_ref,
    pre_ref,
    all_ids,
    sums_out,
    halves,
    whole_ref,
    vec_ref,
    ids_ref,
    class_ref,
    modw_ref,
    vec_all,
    mod_part,
    mod_got,
    act,
    act_f32,
    sums_ref,
    conv_ref,
    resid_ref,
    slopes,
    turned,
    attn_in,
    qkv,
    right,
    low,
    pair_ref,
    pair_send,
    pair_recv,
    pair_local,
    z_send,
    z_recv,
    p_send,
    x_send,
    x_recv,
    y_send,
    y_recv,
    s_send,
    s_recv,
    vec_send,
    vec_recv,
    ids_send,
    ids_recv,
    mod_send,
    mod_recv,
    unit_sem,
    flush_sem,
    in_sem,
    share_local,
    share_send,
    share_recv,
):
    z, y, x, c = place()
    d, h = lax.axis_index("dp"), lax.axis_index("head")
    n_dp, n_head = lines * 2, 4
    half = lines // 2
    inner = jnp.logical_and(z > 0, z < lines - 1)
    far = at_chip(lax.rem(3 * z + 1, lines), y, x, c)
    rows, cols_own = halves.shape[2:]
    wide = 2 * cols_own
    sibling = at_chip(z, y, x, 1 - c)
    along_x = at_chip(z, y, 1 - x, c)
    along_y = at_chip(z, 1 - y, x, c)
    line = [at_chip(lax.rem(z + k, lines), y, x, c) for k in range(1, lines)]
    column, heads = column_peers(n_dp), head_peers(n_head)
    greet(column + heads)

    def spot(i, cc, zz, yy, xx):
        return whole_ref.at[i, cc, zz, yy, :, span(xx, wide)]

    def parts_of(core):
        return (
            (weights_a.at[pl.ds(4 * core, 4)], pl.ds(0, 4)),
            (weights_b.at[pl.ds(4 * core, 4)], pl.ds(5, 4)),
            (weights_qkv.at[pl.ds(core, 1)], pl.ds(9, 1)),
        )

    last_parts = (
        ((weights_a.at[8], 4), (weights_qkv.at[2], 10)),
        ((weights_b.at[8], 4), (weights_proj, 10)),
    )

    def keep_copy(k):
        source, where = parts_of(c)[k]
        return pltpu.make_async_copy(source, halves.at[c, where], pair_local.at[k])

    def swap_copy(k):
        source, where = parts_of(1 - c)[k]
        return remote(source, halves.at[c, where], pair_send.at[k], pair_recv.at[k], sibling)

    def last_keep(core, k):
        source, where = last_parts[core][k]
        return pltpu.make_async_copy(source, halves.at[c, where], pair_local.at[3 + k])

    def last_swap(core, k):
        source, where = last_parts[core][k]
        return remote(source, halves.at[c, where], pair_send.at[3 + k], pair_recv.at[3 + k], sibling)

    def swap_start():
        for k in range(3):
            swap_copy(k).start()
            keep_copy(k).start()
        for core in range(2):

            @pl.when(c == core)
            def _():
                for k in range(2):
                    last_swap(1 - core, k).start()
                    last_keep(core, k).start()

    def swap_wait(k):
        if k < 3:
            keep_copy(k).wait()
            swap_copy(k).wait()
        else:
            last_keep(0, k - 3).wait()
            last_swap(0, k - 3).wait()

    def images_copy():
        return pltpu.make_async_copy(images_hbm, images_ref, in_sem.at[0])

    def cot_copy():
        return pltpu.make_async_copy(cot_hbm, cot_ref, in_sem.at[1])

    images_ref, cot_ref = attn_in, low

    def vec_copy(k):
        return remote(vec_ref, vec_all.at[h], vec_send.at[k], vec_recv.at[k], heads[k])

    def ids_copy(k):
        return remote(ids_ref, all_ids.at[d], ids_send.at[k], ids_recv.at[k], column[k])

    def mod_copy(k):
        return remote(
            mod_part.at[lax.rem(d + k + 1, n_dp)], mod_got.at[d], mod_send.at[k], mod_recv.at[k], column[k]
        )

    def z_part(i, zz):
        if isinstance(i, int) and i >= FAR:
            return whole_ref.at[i, c, zz]
        return spot(i, c, zz, y, x)

    def z_copy(i, k):
        ref = z_part(i, z)
        return remote(ref, ref, z_send.at[i, k], z_recv.at[i, k], line[k])

    def z_pass(i):
        ref = z_part(i, lax.rem(z + 2, lines))
        return remote(ref, ref, p_send.at[i], z_recv.at[i, lax.rem(2 * z + 2, lines)], far)

    def z_start(i):
        z_copy(i, 1).start()

        @pl.when(z != lines - 1)
        def _():
            z_copy(i, 0).start()

        @pl.when(z != 0)
        def _():
            z_copy(i, 2).start()

    def z_relay(i):
        z_copy(i, 1).wait_recv()

        @pl.when(inner)
        def _():
            z_pass(i).start()

    def z_finish(i):
        z_copy(i, 0).wait_recv()
        z_copy(i, 2).wait_recv()

    def z_drain(i):
        z_copy(i, 1).wait_send()

        @pl.when(z != lines - 1)
        def _():
            z_copy(i, 0).wait_send()

        @pl.when(z != 0)
        def _():
            z_copy(i, 2).wait_send()

        @pl.when(inner)
        def _():
            z_pass(i).wait_send()

    def x_copy(i, part):
        if isinstance(i, int) and i >= FAR:
            ref = spot(i, c, z, y, x) if part == 0 else spot(i, c, z, 1 - y, x).at[pl.ds(rows // 2, rows // 2)]
        elif part == 0:
            ref = spot(i, c, slice(None), y, x)
        else:
            ref = spot(i, c, pl.ds(half, half), 1 - y, x)
        return remote(ref, ref, x_send.at[i, part], x_recv.at[i, part], along_x)

    def y_copy(i, part):
        if isinstance(i, int) and i >= FAR:
            ref = spot(i, c, z, y, x) if part == 0 else spot(i, c, z, y, 1 - x).at[pl.ds(0, rows // 2)]
        elif part == 0:
            ref = spot(i, c, slice(None), y, x)
        else:
            ref = spot(i, c, pl.ds(0, half), y, 1 - x)
        return remote(ref, ref, y_send.at[i, part], y_recv.at[i, part], along_y)

    def s_copy(i, part):
        if isinstance(i, int) and i >= FAR:
            ref = whole_ref.at[i, c, part]
        else:
            yy, xx = ((y, x), (y, 1 - x), (1 - y, x), (1 - y, 1 - x))[part]
            ref = spot(i, c, slice(None), yy, xx)
        return remote(ref, ref, s_send.at[i, part], s_recv.at[i, part], sibling)

    def join(i):
        whole_ref[i, c, z, y, :, span(x, wide)] = jnp.concatenate([halves[0, i], halves[1, i]], axis=-1)

    def begin(i):
        join(i)
        z_start(i)

    def far_begin(i):
        x_copy(i, 0).start()
        y_copy(i, 0).start()

    def far_pass(i):
        x_copy(i, 0).wait_recv()
        y_copy(i, 1).start()
        y_copy(i, 0).wait_recv()
        x_copy(i, 1).start()

    def far_line(i):
        x_copy(i, 1).wait_recv()
        y_copy(i, 1).wait_recv()
        z_start(i)

    def far_finish(i):
        z_finish(i)
        for part in range(lines):
            s_copy(i, part).start()

    def spread_line(i):
        z_finish(i)
        x_copy(i, 0).start()
        y_copy(i, 0).start()
        s_copy(i, 0).start()

    def pass_on(i):
        x_copy(i, 0).wait_recv()
        y_copy(i, 1).start()
        s_copy(i, 1).start()
        y_copy(i, 0).wait_recv()
        x_copy(i, 1).start()
        s_copy(i, 2).start()

    def finish(i):
        x_copy(i, 1).wait_recv()
        y_copy(i, 1).wait_recv()
        s_copy(i, 3).start()

    def arrived(i):
        for part in range(4):
            s_copy(i, part).wait_recv()

    def unit_copy(i):
        return pltpu.make_async_copy(whole_ref.at[i], whole_out.at[i], unit_sem.at[i])

    def fetch(i):
        arrived(i)
        if not isinstance(i, int) or i < FAR:
            unit_copy(i).start()

    def product(total, tap, i, k):
        for n in range(CHUNKS):
            value = dot(act[tap % 3, lines_from(tap // 3)], weight_cols(whole_ref.at[i, k], n))
            total[:, :, :, chunk(n)] += value.reshape(RES, SLOTS, RES, WIDTH)

    def use_pair(total, i, first):
        each(2, lambda k: product(total, i - first + 4 * k, i, k))

    flushed = (
        (conv_ref, conv_out),
        (slopes.at[0], slopes_out.at[0]),
        (slopes.at[1], slopes_out.at[1]),
        (low, block_out),
        (conv_ref, grad_out),
        (attn_in, low_out),
    )

    def share_parts(k):
        if k < 4:
            return turned.at[k], turned_out.at[k, :, span(c, ALL)]
        part = (3, 1 - c, 2)[k - 4]
        return right.at[part], right_out.at[part, span(c, ALL)]

    def share_give(k):
        return remote(*share_parts(k), share_send.at[k], share_recv.at[k], sibling)

    def right_keep(k):
        return pltpu.make_async_copy(right.at[k], right_out.at[k, span(c, ALL)], share_local.at[4 + k])

    def turned_keep(k):
        return pltpu.make_async_copy(*share_parts(k), share_local.at[k])

    def share_if(k, giving, run):
        if k in (1, 4, 6):
            taker = 0 if k == 6 else 1
            pl.when(c == (1 - taker if giving else taker))(run)
        else:
            run()

    def share(k):
        share_if(k, True, lambda: share_give(k).start())

    def share_wait():
        for k in range(7):
            share_if(k, True, lambda k=k: share_give(k).wait_send())
            share_if(k, False, lambda k=k: share_give(k).wait_recv())
        for k in range(4):
            turned_keep(k).wait()
            right_keep(k).wait()

    def flush(k):
        return pltpu.make_async_copy(*flushed[k], flush_sem.at[k])

    def set_act(place_t):
        def by_line(yy):
            value = act_f32[yy].reshape(LINE, C)
            left, right = shifted(value)
            spot_rows = pl.ds(pl.multiple_of((yy + 1) * LINE, LINE), LINE)
            act[0, spot_rows] = left.astype(BF16)
            act[1, spot_rows] = value.astype(BF16)
            act[2, spot_rows] = right.astype(BF16)

        each(RES, by_line)

        def turn(yy):
            value = act_f32[pl.ds(2 * yy, 2)].reshape(2 * LINE, C)
            turned[place_t, :, span(yy, 2 * LINE)] = value.T.astype(BF16)

        each(RES // 2, turn)

    def activate(which, n, value):
        sigma = jax.nn.sigmoid(value)
        act_f32[:, n] = (value * sigma).reshape(RES, RES, C)
        slopes[which, :, n] = (sigma * (1.0 + value * (1.0 - sigma))).reshape(RES, RES, C)

    def norm_a():
        for k in range(n_head - 1):
            vec_copy(k).wait()
        vecs_ref[...] = jnp.concatenate([vec_all[k].astype(F32) for k in range(n_head)], axis=-1)

        images_copy().wait()

        def get(n):
            return images_ref[span(n, PIX)].astype(F32)

        mean, inverse = stats_ref.at[0], stats_ref.at[1]
        norm_stats(get, mean, inverse, sums_ref)

        def to_act(n):
            value = (get(n) - mean[row(n)]) * inverse[row(n)]
            activate(0, n, value * vecs_ref[0:1] + vecs_ref[1:2])
            conv_ref[:, n] = jnp.broadcast_to(vecs_ref[2:3].reshape(1, 1, C), (RES, RES, C))
            resid_ref[:, n] = (get(n) + vecs_ref[5:6]).reshape(RES, RES, C)

        each(SLOTS, to_act)
        set_act(3)
        flush(1).start()
        turned_keep(3).start()
        share(3)

    def embed():
        for k in range(n_dp - 1):
            ids_copy(k).wait()
        ids = all_ids[...].reshape(n_dp * SLOTS, 128)
        table = class_ref.shape[1]
        label_hot = lax.broadcasted_iota(jnp.int32, (n_dp * SLOTS, table), 1) == ids[:, 0:1]
        levels = noise_table.shape[0]
        level_hot = lax.broadcasted_iota(jnp.int32, (n_dp * SLOTS, levels), 1) == ids[:, 1:2]
        pre = dot_nt(jnp.where(label_hot, 1.0, 0.0).astype(BF16), class_ref[...])
        width = class_table.shape[0]
        place_of = lax.broadcasted_iota(jnp.int32, (C, 128), 0) - d * width
        lane = lax.broadcasted_iota(jnp.int32, (C, 128), 1)
        chosen = jnp.logical_and(place_of == lane, lane < width)
        noise = dot(noise_table[...], jnp.where(chosen, 1.0, 0.0).astype(BF16)).astype(BF16)
        pre += dot(jnp.where(level_hot, 1.0, 0.0).astype(BF16), noise)
        pre_ref[...] = pre
        part = dot(silu(pre).astype(BF16), modw_ref[...])
        for k in range(n_dp):
            mine = part[k * SLOTS : (k + 1) * SLOTS]
            mod_part[k] = jnp.concatenate([mine[:, :C], mine[:, C:]], axis=0).astype(BF16)
        mod_got[d] = mod_part[d]
        for k in range(n_dp - 1):
            mod_copy(k).start()

    def conv_value(n):
        return conv_ref[:, n].reshape(PIX, C)

    def norm_b_first():
        for k in range(n_dp - 1):
            mod_copy(k).wait()
        bias = modb_ref[...].astype(F32)
        total = jnp.concatenate([jnp.broadcast_to(bias[k : k + 1], (SLOTS, C)) for k in range(2)], axis=0)
        for k in range(n_dp):
            total += mod_got[k].astype(F32)
        mod_ref[...] = total.astype(BF16).astype(F32)

        norm_stats(conv_value, stats_ref.at[2], stats_ref.at[3], sums_ref)

    def norm_b_second():
        mean, inverse = stats_ref.at[2], stats_ref.at[3]

        def to_act(n):
            value = (conv_value(n) - mean[row(n)]) * inverse[row(n)]
            value = value * vecs_ref[3:4] + vecs_ref[4:5]
            value = mod_ref[row(SLOTS + n)] + value * (mod_ref[row(n)] + 1.0)
            activate(1, n, value)

        each(SLOTS, to_act)
        set_act(2)
        flush(0).start()
        flush(2).start()
        turned_keep(2).start()
        share(2)

    def residual(n):
        return resid_ref[:, n].reshape(PIX, C)

    def normed(n):
        return (residual(n) - stats_ref[4, row(n)]) * stats_ref[5, row(n)]

    def transpose_out(source, place_t):
        def turn(k):
            value = source[span(k, 2 * LINE)].astype(F32)
            turned[place_t, :, span(k, 2 * LINE)] = value.T.astype(BF16)

        each(ALL // (2 * LINE), turn)

    def live(n):
        slots = counts_ref[0, d * n_head + h] + counts_ref[1, d * n_head + h]
        return jnp.where(n < slots, 1.0, 0.0)

    def norm_c():
        cot_copy().wait()
        norm_stats(residual, stats_ref.at[4], stats_ref.at[5], sums_ref)
        sums_out[...] = jnp.zeros_like(sums_out)

        def prepare(n):
            attn_in[span(n, PIX)] = (normed(n) * vecs_ref[6:7] + vecs_ref[7:8]).astype(BF16)
            grad = cot_ref[span(n, PIX)].astype(F32) * live(n)
            right[3, span(n, PIX)] = grad.astype(BF16)
            sums_out[8:9] += sum_rows(grad)

        each(SLOTS, prepare)
        transpose_out(attn_in, 0)
        turned_keep(0).start()
        right_keep(3).start()
        share(0)
        share(4)

    def attention():
        unit = tuple(whole_ref.at[9 + t // 2, t % 2] for t in range(4))
        for t in range(4):
            for n in range(CHUNKS):
                if t < 3:
                    value = dot(attn_in[...], weight_cols(unit[t], n))
                else:
                    value = dot_nt(right[3], weight_rows(unit[3], n))
                qkv[t, :, chunk(n)] = value.astype(BF16)
        factor = DH ** (-0.5)
        band = lax.broadcasted_iota(jnp.int32, (PIX, BAND), 1) // DH
        heads_at_once = BAND // DH

        def stack(value):
            zero = jnp.zeros_like(value)
            return jnp.concatenate([jnp.where(band == k, value, zero) for k in range(heads_at_once)], axis=0)

        def pick(value):
            out = value[:PIX]
            for k in range(1, heads_at_once):
                out = jnp.where(band == k, value[k * PIX : (k + 1) * PIX], out)
            return out

        def attend(n):
            for b in range(C // BAND):
                query, key, value, grad = (qkv[t, span(n, PIX), slice(b * BAND, (b + 1) * BAND)] for t in range(4))
                query4, grad4 = stack(query), stack(grad)
                scores = dot_nt(key, query4) * factor
                weight = jnp.exp(scores - jnp.max(scores, axis=0, keepdims=True))
                probs = weight / jnp.sum(weight, axis=0, keepdims=True)
                probs_low = probs.astype(BF16)
                low[span(n, PIX), slice(b * BAND, (b + 1) * BAND)] = pick(dot_tn(probs_low, value)).astype(BF16)
                grad_probs = dot_nt(value, grad4)
                inner_sum = jnp.sum(grad_probs * probs, axis=0, keepdims=True)
                grad_scores = (probs * (grad_probs - inner_sum)).astype(BF16)
                right[0, span(n, PIX), slice(b * BAND, (b + 1) * BAND)] = (pick(dot_tn(grad_scores, key)) * factor).astype(BF16)
                right[1, span(n, PIX), slice(b * BAND, (b + 1) * BAND)] = (dot(grad_scores, query4) * factor).astype(BF16)
                right[2, span(n, PIX), slice(b * BAND, (b + 1) * BAND)] = dot(probs_low, grad4).astype(BF16)

        def attend_two(m):
            attend(2 * m)
            attend(2 * m + 1)

        each(SLOTS // 2, attend_two)
        share(5)
        share(6)
        for k in range(3):
            right_keep(k).start()
        transpose_out(low, 1)
        turned_keep(1).start()
        share(1)
        for n in range(CHUNKS):
            value = dot_nt(right[0], weight_rows(unit[0], n))
            value += dot_nt(right[1], weight_rows(unit[1], n))
            value += dot_nt(right[2], weight_rows(unit[2], n))
            act_f32[:, :, :, chunk(n)] = value.reshape(SLOTS, RES, RES, WIDTH)

        def back(n):
            grad = act_f32[n].reshape(PIX, C)
            pair_ref[row(n)] = sum_rows(grad * normed(n))
            pair_ref[row(SLOTS + n)] = sum_rows(grad)

        each(SLOTS, back)
        sums_out[6:7] = sum_rows(pair_ref[0:SLOTS])
        sums_out[7:8] = sum_rows(pair_ref[SLOTS:])
        pair_ref[...] = group_mean(pair_ref[...] * vecs_ref[6:7])

        def back_second(n):
            inverse = stats_ref[5, row(n)]
            value = act_f32[n].reshape(PIX, C) * (vecs_ref[6:7] * inverse)
            value -= normed(n) * (pair_ref[row(n)] * inverse) + pair_ref[row(SLOTS + n)] * inverse
            value += right[3, span(n, PIX)].astype(F32)
            conv_ref[:, n] = value.reshape(RES, RES, C)
            sums_out[5:6] += sum_rows(value.astype(BF16).astype(F32))

        flush(0).wait()
        each(SLOTS, back_second)
        flush(4).start()

        def lower(yy):
            attn_in[span(yy, LINE)] = conv_ref[yy].reshape(LINE, C).astype(BF16)

        each(RES, lower)
        flush(5).start()
        for n in range(CHUNKS):
            value = dot(low[...], weight_cols(unit[3], n))
            act_f32[:, :, :, chunk(n)] = value.reshape(SLOTS, RES, RES, WIDTH)

        def finish_out(n):
            value = residual(n) + act_f32[n].reshape(PIX, C) + vecs_ref[8:9]
            low[span(n, PIX)] = (value * live(n)).astype(BF16)

        each(SLOTS, finish_out)
        flush(3).start()

    swap_start()
    images_copy().start()
    cot_copy().start()
    one = [ref[...].astype(F32).reshape(1, cols_own) for ref in vectors]
    vec_ref[...] = jnp.concatenate(one + [jnp.zeros((16 - VECTORS, cols_own), F32)], axis=0).astype(BF16)
    lane = lax.broadcasted_iota(jnp.int32, (1, 128), 1)
    for n in range(SLOTS):
        ids_ref[n : n + 1] = jnp.where(lane == 0, labels_ref[n], levels_ref[n])
    for k in range(n_head - 1):
        vec_copy(k).start()
    for k in range(n_dp - 1):
        ids_copy(k).start()
    width = class_table.shape[0]
    class_ref[...] = jnp.zeros_like(class_ref)
    class_ref[0:width, 0 : class_table.shape[1]] = class_table[...]
    modw_ref[...] = jnp.zeros_like(modw_ref)
    table = modw_table[...].astype(F32)
    for k in range(2):
        modw_ref[0:width, k * C : (k + 1) * C] = table[:, k].astype(BF16)
    vec_all[h] = vec_ref[...]
    all_ids[d] = ids_ref[...]
    edge = jnp.zeros((LINE, C), BF16)
    for j in range(3):
        act[j, 0:LINE] = edge
        act[j, ALL + LINE : ALL + 2 * LINE] = edge
    swap_wait(0)
    begin(0)
    for k in range(1, 5):
        swap_wait(k)
    for i in (10, 9):
        join(i)
        far_begin(i)
    begin(1)
    z_relay(0)
    begin(2)
    spread_line(0)
    for i in (10, 9):
        far_pass(i)
    begin(3)
    z_relay(1)
    norm_a()
    spread_line(1)
    pass_on(0)
    begin(4)
    z_relay(2)
    embed()
    spread_line(2)
    pass_on(1)
    finish(0)
    begin(5)
    z_relay(3)
    begin(6)
    z_relay(4)
    far_line(10)
    spread_line(3)
    pass_on(2)
    finish(1)
    fetch(0)

    def body(turn, carry):
        @pl.when(turn < 6)
        def _():
            begin(turn + 3)

        @pl.when(turn == 6)
        def _():
            far_line(9)
            z_relay(10)

        z_relay(turn + 1)
        spread_line(turn)
        pass_on(turn - 1)
        finish(turn - 2)
        fetch(turn - 3)
        use_pair(conv_ref, turn - 4, 0)
        return carry

    lax.fori_loop(4, 8, body, 0)
    spread_line(8)
    pass_on(7)
    finish(6)
    fetch(5)
    product(conv_ref, 8, 4, 0)
    norm_b_first()
    pass_on(8)
    finish(7)
    norm_b_second()
    product(resid_ref, 8, 4, 1)
    z_relay(9)
    fetch(6)
    far_finish(10)
    use_pair(resid_ref, 5, 5)
    finish(8)
    fetch(7)
    use_pair(resid_ref, 6, 5)
    fetch(8)
    use_pair(resid_ref, 7, 5)
    use_pair(resid_ref, 8, 5)
    far_finish(9)
    norm_c()
    fetch(9)
    fetch(10)
    attention()

    def drain(i):
        z_drain(i)
        for part in range(2):
            x_copy(i, part).wait_send()
            y_copy(i, part).wait_send()
        for part in range(4):
            s_copy(i, part).wait_send()

    each(FAR, drain)
    drain(9)
    drain(10)
    for k in range(1, len(flushed)):
        flush(k).wait()
    each(FAR, lambda i: unit_copy(i).wait())
    share_wait()


def run_forward(weights, images, cotangent, counts, labels, levels, class_table, noise_table, modw, modb, vectors):
    n_dp, n_head = lax.axis_size("dp"), lax.axis_size("head")
    rows, cols = weights[0].shape[1:]
    lines, across, wide = n_dp // 2, n_head // 2, 2 * cols
    board = (RES, SLOTS, RES, C)
    shape = jax.ShapeDtypeStruct
    return pl.pallas_call(
        functools.partial(forward_kernel, lines),
        out_shape=(
            shape((FAR, 2, lines, 2, rows, across * wide), BF16),
            shape(board, F32),
            shape((2,) + board, F32),
            shape((4, C, 2 * ALL), BF16),
            shape((ALL, C), BF16),
            shape(board, F32),
            shape((ALL, C), BF16),
            shape((4, 2 * ALL, C), BF16),
            shape((16, C), F32),
            shape((2 * SLOTS, C), F32),
            shape((6, SLOTS, C), F32),
            shape((n_dp * SLOTS, 128), F32),
            shape((n_dp, SLOTS, 128), jnp.int32),
            shape((16, C), F32),
        ),
        in_specs=[ANY] * 6 + [SMEM] * 3 + [VMEM] * (4 + VECTORS),
        out_specs=(ANY,) * 8 + (VMEM,) * 6,
        scratch_shapes=[
            pltpu.VMEM((2, PAIRS, rows, cols), BF16),
            pltpu.VMEM((PAIRS, 2, lines, 2, rows, across * wide), BF16),
            pltpu.VMEM((16, cols), BF16),
            pltpu.VMEM((SLOTS, 128), jnp.int32),
            pltpu.VMEM((128, 1024), BF16),
            pltpu.VMEM((128, 2 * C), BF16),
            pltpu.VMEM((n_head, 16, cols), BF16),
            pltpu.VMEM((n_dp, 2 * SLOTS, C), BF16),
            pltpu.VMEM((n_dp, 2 * SLOTS, C), BF16),
            pltpu.VMEM((3, ALL + 2 * LINE, C), BF16),
            pltpu.VMEM(board, F32),
            pltpu.VMEM((SLOTS, C), F32),
            pltpu.VMEM(board, F32),
            pltpu.VMEM(board, F32),
            pltpu.VMEM((2,) + board, F32),
            pltpu.VMEM((4, C, ALL), BF16),
            pltpu.VMEM((ALL, C), BF16),
            pltpu.VMEM((4, ALL, C), BF16),
            pltpu.VMEM((4, ALL, C), BF16),
            pltpu.VMEM((ALL, C), BF16),
            pltpu.VMEM((2 * SLOTS, C), F32),
            DMA((5,)),
            DMA((5,)),
            DMA((5,)),
            DMA((PAIRS, lines - 1)),
            DMA((PAIRS, lines - 1)),
            DMA((PAIRS,)),
            DMA((PAIRS, 2)),
            DMA((PAIRS, 2)),
            DMA((PAIRS, 2)),
            DMA((PAIRS, 2)),
            DMA((PAIRS, 4)),
            DMA((PAIRS, 4)),
            DMA((n_head - 1,)),
            DMA((n_head - 1,)),
            DMA((n_dp - 1,)),
            DMA((n_dp - 1,)),
            DMA((n_dp - 1,)),
            DMA((n_dp - 1,)),
            DMA((FAR,)),
            DMA((6,)),
            DMA((2,)),
            DMA((8,)),
            DMA((7,)),
            DMA((7,)),
        ],
        compiler_params=pltpu.CompilerParams(
            collective_id=0, has_side_effects=True, vmem_limit_bytes=62 * 2**20
        ),
        name="gather_forward",
    )(
        *weights,
        images,
        cotangent,
        counts,
        labels,
        levels,
        class_table,
        noise_table,
        modw,
        modb,
        *vectors,
    )


BACK_FAR = (10, 8)
BACK_NEAR = tuple(i for i in range(PAIRS) if i not in BACK_FAR)
AHEAD = 3


def backward_kernel(
    lines,
    whole_ref,
    turned_ref,
    right_ref,
    grad_low_ref,
    grad_resid_ref,
    conv_ref,
    slopes_ref,
    images_hbm,
    stats_ref,
    vecs_ref,
    mod_ref,
    sums_in,
    pre_ref,
    ids_ref,
    modw_table,
    out_a,
    out_b,
    out_qkv,
    out_proj,
    image_ref,
    class_ref,
    modw_out,
    modb_out,
    vec_out,
    mine,
    from_x,
    from_y,
    from_z,
    far_x,
    far_y,
    far_z,
    ends,
    modw_ref,
    lefts,
    rights,
    grads,
    stage,
    stage_mine,
    weights,
    total,
    board,
    slopes,
    image_mine,
    images_ref,
    sums_ref,
    pair_ref,
    coef_ref,
    gm_mine,
    gm_all,
    mw_mine,
    mw_got,
    ge_all,
    vs_mine,
    vs_got,
    vt_mine,
    vt_all,
    x_send,
    x_recv,
    y_send,
    y_recv,
    z_send,
    z_recv,
    p_send,
    p_recv,
    e_send,
    e_recv,
    e_local,
    op_send,
    op_recv,
    op_local,
    load_sem,
    in_sem,
    out_sem,
    gm_send,
    gm_recv,
    mw_send,
    mw_recv,
    ge_send,
    ge_recv,
    vs_send,
    vs_recv,
    vt_send,
    vt_recv,
):
    z, y, x, c = place()
    d, h = lax.axis_index("dp"), lax.axis_index("head")
    n_dp, n_head = lines * 2, 4
    half = lines // 2
    inner = jnp.logical_and(z > 0, z < lines - 1)
    rows, wide = from_z.shape[2], from_z.shape[3]
    cols = wide // 2
    sibling = at_chip(z, y, x, 1 - c)
    along_x = at_chip(z, y, 1 - x, c)
    along_y = at_chip(z, 1 - y, x, c)
    line = [at_chip(lax.rem(z + k, lines), y, x, c) for k in range(1, lines)]
    column, heads = column_peers(n_dp), head_peers(n_head)

    own_rows = pl.ds(LINE, ALL)

    def op_own(k):
        source, place_of = (
            (right_ref.at[2 + c], rights.at[0]),
            (turned_ref.at[c], lefts.at[1]),
            (right_ref.at[c], rights.at[1]),
            (turned_ref.at[0], lefts.at[0]),
            (grad_low_ref, grads.at[1, c, own_rows]),
            (turned_ref.at[2], lefts.at[2]),
            (turned_ref.at[3], lefts.at[3]),
        )[k]
        return pltpu.make_async_copy(source, place_of, op_local.at[k])

    def low_copy():
        return remote(grad_low_ref, grads.at[1, c, own_rows], op_send.at[0], op_recv.at[0], sibling)

    def stage_copy():
        return remote(stage_mine, stage, op_send.at[1], op_recv.at[1], sibling)

    def lanes(xx):
        return span(xx, wide)

    first, second = pl.ds(0, rows // 2), pl.ds(rows // 2, rows // 2)

    def is_far(i):
        return i in BACK_FAR

    def x_copy(i, part):
        if is_far(i):
            into = far_x.at[BACK_FAR.index(i)]
            if part == 0:
                src, dst = mine.at[i, z, 1 - y, second, lanes(1 - x)], into.at[pl.ds(rows, rows // 2)]
            else:
                src, dst = mine.at[i, z, y, :, lanes(1 - x)], into.at[pl.ds(0, rows)]
        elif part == 0:
            src, dst = mine.at[i, pl.ds(half, half), 1 - y, :, lanes(1 - x)], from_x.at[BACK_NEAR.index(i), pl.ds(lines, half)]
        else:
            src, dst = mine.at[i, :, y, :, lanes(1 - x)], from_x.at[BACK_NEAR.index(i), pl.ds(0, lines)]
        return remote(src, dst, x_send.at[i, part], x_recv.at[i, part], along_x)

    def y_copy(i, part):
        if is_far(i):
            into = far_y.at[BACK_FAR.index(i)]
            if part == 0:
                src, dst = mine.at[i, z, 1 - y, first, lanes(1 - x)], into.at[pl.ds(rows, rows // 2)]
            else:
                src, dst = mine.at[i, z, 1 - y, :, lanes(x)], into.at[pl.ds(0, rows)]
        elif part == 0:
            src, dst = mine.at[i, pl.ds(0, half), 1 - y, :, lanes(1 - x)], from_y.at[BACK_NEAR.index(i), pl.ds(lines, half)]
        else:
            src, dst = mine.at[i, :, 1 - y, :, lanes(x)], from_y.at[BACK_NEAR.index(i), pl.ds(0, lines)]
        return remote(src, dst, y_send.at[i, part], y_recv.at[i, part], along_y)

    beyond = lax.rem(z + 2, lines)
    opposite = lines - 1 - z
    near_end = at_chip(1 + z // (lines - 1), y, x, c)

    def z_block(i, zz):
        return mine.at[i, zz] if is_far(i) else mine.at[i, zz, y, :, lanes(x)]

    def z_slot(i, k):
        return far_z.at[BACK_FAR.index(i), k] if is_far(i) else from_z.at[BACK_NEAR.index(i), k]

    def z_copy(i, k):
        return remote(
            z_block(i, lax.rem(z + k + 1, lines)), z_slot(i, k), z_send.at[i, k], z_recv.at[i, k], line[k]
        )

    def z_give(i):
        return remote(z_block(i, opposite), z_slot(i, 3), p_send.at[i], p_recv.at[i], near_end)

    def z_start(i):
        @pl.when(jnp.logical_not(inner))
        def _():
            z_give(i).start()

        @pl.when(z < lines - 1)
        def _():
            z_copy(i, 0).start()

        @pl.when(z > 0)
        def _():
            z_copy(i, 2).start()

        @pl.when(jnp.logical_not(inner))
        def _():
            z_copy(i, 1).start()

    def z_mix(i):
        @pl.when(inner)
        def _():
            z_give(i).wait_recv()
            if is_far(i):
                mine[i, beyond] += far_z[BACK_FAR.index(i), 3]
            else:
                mine[i, beyond, y, :, lanes(x)] += from_z[BACK_NEAR.index(i), 3]
            z_copy(i, 1).start()

    def z_wait(i):
        z_copy(i, 1).wait_recv()

        @pl.when(z > 0)
        def _():
            z_copy(i, 0).wait_recv()

        @pl.when(z < lines - 1)
        def _():
            z_copy(i, 2).wait_recv()

    def z_drain(i):
        z_copy(i, 1).wait_send()

        @pl.when(z < lines - 1)
        def _():
            z_copy(i, 0).wait_send()

        @pl.when(z > 0)
        def _():
            z_copy(i, 2).wait_send()

        @pl.when(jnp.logical_not(inner))
        def _():
            z_give(i).wait_send()

    def target(i, core):
        if isinstance(i, int) and i == 10:
            return out_proj if core == 1 else out_qkv.at[2]
        if isinstance(i, int) and i == 9:
            return out_qkv.at[core]
        if isinstance(i, int) and i == 4:
            return out_b.at[8] if core == 1 else out_a.at[8]
        if isinstance(i, int) and i > 4:
            return out_b.at[4 * core + i - 5]
        return out_a.at[4 * core + i]

    def e_copy(i, core):
        return remote(ends.at[1 - c, i], target(i, core), e_send.at[i], e_recv.at[i], sibling)

    def e_own(i, core):
        return pltpu.make_async_copy(ends.at[c, i], target(i, core), e_local.at[i])

    def finish(i, value):
        for cc in range(2):
            ends[cc, i] = value[:, cc * cols : (cc + 1) * cols]
        if i in (4, 10):
            for core in range(2):

                @pl.when(c == core)
                def _():
                    e_copy(i, core).start()
                    e_own(i, core).start()
        else:
            e_copy(i, c).start()
            e_own(i, c).start()

    def offer(i):
        x_copy(i, 0).start()
        y_copy(i, 0).start()

    def relay(i):
        x_copy(i, 0).wait_recv()
        y_copy(i, 0).wait_recv()
        if is_far(i):
            rest = pl.ds(rows, rows // 2)
            mine[i, z, y, first, lanes(1 - x)] += far_y[BACK_FAR.index(i), rest]
            mine[i, z, 1 - y, second, lanes(x)] += far_x[BACK_FAR.index(i), rest]
        else:
            for j in range(half):
                mine[i, j, y, :, lanes(1 - x)] += from_y[BACK_NEAR.index(i), lines + j]
                mine[i, half + j, 1 - y, :, lanes(x)] += from_x[BACK_NEAR.index(i), lines + j]
        x_copy(i, 1).start()
        y_copy(i, 1).start()

    def collect(i):
        x_copy(i, 1).wait_recv()
        y_copy(i, 1).wait_recv()
        if is_far(i):
            whole_rows = pl.ds(0, rows)
            value = mine[i, z, y, :, lanes(x)].astype(F32)
            value += far_x[BACK_FAR.index(i), whole_rows].astype(F32) + far_y[BACK_FAR.index(i), whole_rows].astype(F32)
            finish(i, value)
            return

        def add(j):
            value = mine[i, j, y, :, lanes(x)].astype(F32)
            value += from_x[BACK_NEAR.index(i), j].astype(F32) + from_y[BACK_NEAR.index(i), j].astype(F32)
            mine[i, j, y, :, lanes(x)] = value.astype(BF16)

        each(lines, add)
        z_start(i)

    def last(i):
        z_wait(i)
        if is_far(i):
            for yy in range(2):
                value = mine[i, z, yy].astype(F32)
                for k in range(lines - 1):
                    value += far_z[BACK_FAR.index(i), k, yy].astype(F32)
                mine[i, z, yy] = value.astype(BF16)
            offer(i)
            return
        value = mine[i, z, y, :, lanes(x)].astype(F32)
        for k in range(lines - 1):
            value += from_z[BACK_NEAR.index(i), k].astype(F32)
        finish(i, value)

    def put(i, n, value):
        mine[i, :, :, :, chunk(n)] = value.astype(BF16).reshape(mine.shape[1:4] + (WIDTH,))

    def plain_unit(i, left, right):
        for n in range(CHUNKS):
            put(i, n, dot(lefts[left], rights[right, :, chunk(n)]))

    def conv_unit(i, left, tap):
        where, side = lines_from(2 - tap // 3), 2 - tap % 3
        for n in range(CHUNKS):
            both = jnp.concatenate([grads[side, core, where, chunk(n)] for core in range(2)], axis=0)
            put(i, n, dot(lefts[left], both))

    def extra_b():
        @pl.when(c == 1)
        def _():
            conv_unit(4, 2, 8)

    def extra_a():
        @pl.when(c == 0)
        def _():
            conv_unit(4, 3, 8)

    def spread_sides(core):
        def by_line(yy):
            value = grads[1, core, pl.ds(pl.multiple_of((yy + 1) * LINE, LINE), LINE)].astype(F32)
            left, right = shifted(value)
            spot_rows = pl.ds(pl.multiple_of((yy + 1) * LINE, LINE), LINE)
            grads[0, core, spot_rows] = left.astype(BF16)
            grads[2, core, spot_rows] = right.astype(BF16)

        each(RES, by_line)

    def load(tap, base):
        ninth = tap // 8
        i = (base // 2 + tap % 4) * (1 - ninth) + 4 * ninth
        k = (tap // 4) % 2 + (base // 10) * ninth
        return pltpu.make_async_copy(whole_ref.at[i, k], weights.at[tap % (AHEAD + 1)], load_sem.at[tap % (AHEAD + 1)])

    def conv_back(tap, base):
        load(tap, base).wait()

        @pl.when(tap < 9 - AHEAD)
        def _():
            load(tap + AHEAD, base).start()

        part = grads[2 - tap % 3, c, lines_from(2 - tap // 3)]
        for n in range(CHUNKS):
            value = dot_nt(part, weight_rows(weights.at[tap % (AHEAD + 1)], n))
            total[:, :, :, chunk(n)] += value.reshape(RES, SLOTS, RES, WIDTH)

    def conv_back_range(first, stop, base):
        def body(tap, carry):
            conv_back(tap, base)
            return carry

        lax.fori_loop(first, stop, body, 0)

    def slope(values):
        sigma = jax.nn.sigmoid(values)
        return sigma * (1.0 + values * (1.0 - sigma))

    for k in (0, 2):
        from_z[:, k] = jnp.zeros_like(from_z[:, k])
        far_z[:, k] = jnp.zeros_like(far_z[:, k])
    greet(column + heads)
    low_copy().start()
    for k in (4, 0, 1, 2, 3, 5):
        op_own(k).start()
    for tap in range(AHEAD):
        load(tap, 10).start()

    def fetch(k):
        source, target = (
            (conv_ref, board),
            (slopes_ref.at[1], slopes),
            (slopes_ref.at[0], slopes),
            (grad_resid_ref, board),
            (images_hbm, images_ref),
        )[k]
        return pltpu.make_async_copy(source, target, in_sem.at[k])

    fetch(0).start()
    fetch(1).start()
    vs_mine[...] = jnp.zeros_like(vs_mine)
    edge = jnp.zeros((LINE, C), BF16)
    for j in range(3):
        for core in range(2):
            grads[j, core, 0:LINE] = edge
            grads[j, core, ALL + LINE : ALL + 2 * LINE] = edge
    total[...] = jnp.zeros_like(total)
    sums_ref[...] = sums_in[...]
    modw_ref[...] = jnp.zeros_like(modw_ref)
    table = modw_table[...].astype(F32)
    for k in range(2):
        modw_ref[0:rows, k * C : (k + 1) * C] = table[:, k].astype(BF16)

    def norm_b_value(n):
        return (board[:, n].reshape(PIX, C) - stats_ref[2, row(n)]) * stats_ref[3, row(n)]

    def norm_a_value(n):
        return (images_ref[span(n, PIX)].astype(F32) - stats_ref[0, row(n)]) * stats_ref[1, row(n)]

    def back_sums(get):
        def body(n):
            grad = (total[:, n] * slopes[:, n]).reshape(PIX, C)
            total[:, n] = grad.reshape(RES, RES, C)
            pair_ref[row(n)] = sum_rows(grad * get(n))
            pair_ref[row(SLOTS + n)] = sum_rows(grad)

        each(SLOTS, body)

    def back_factors(factor, inverse):
        coef_ref[0:SLOTS] = factor * inverse
        means = group_mean(pair_ref[...] * jnp.concatenate([factor, factor], axis=0))
        coef_ref[SLOTS : 2 * SLOTS] = means[:SLOTS] * inverse
        coef_ref[2 * SLOTS :] = means[SLOTS:] * inverse

    def back_value(n, get):
        value = total[:, n].reshape(PIX, C) * coef_ref[row(n)]
        return value - get(n) * coef_ref[row(SLOTS + n)] - coef_ref[row(2 * SLOTS + n)]

    def gm_copy(k):
        return remote(gm_mine, gm_all.at[d], gm_send.at[k], gm_recv.at[k], column[k])

    def mw_copy(k):
        return remote(
            mw_mine.at[lax.rem(h + k + 1, n_head)], mw_got.at[k], mw_send.at[k], mw_recv.at[k], heads[k]
        )

    def ge_copy(k):
        return remote(ge_all.at[h], ge_all.at[h], ge_send.at[k], ge_recv.at[k], heads[k])

    def vs_copy(k):
        return remote(
            vs_mine.at[lax.rem(h + k + 1, n_head)], vs_got.at[k], vs_send.at[k], vs_recv.at[k], heads[k]
        )

    def vt_copy(k):
        return remote(vt_mine, vt_all.at[d], vt_send.at[k], vt_recv.at[k], column[k])

    def image_copy():
        return pltpu.make_async_copy(image_mine, image_ref, out_sem)

    count = n_dp * SLOTS

    def start():
        op_own(0).wait()
        op_own(1).wait()

    def dw(i):
        if i == 10:
            plain_unit(10, 1, 0)
        elif i == 9:
            op_own(2).wait()
            op_own(3).wait()
            plain_unit(9, 0, 1)
        elif i > 4:
            conv_unit(i, 2, 4 * c + i - 5)
        else:
            conv_unit(i, 3, 4 * c + i)

    def sides():
        op_own(4).wait()
        low_copy().wait_recv()
        op_own(5).wait()
        spread_sides(0)
        spread_sides(1)

    def back_b_first():
        for tap in range(AHEAD):
            load(tap, 0).start()
        op_own(6).start()
        fetch(0).wait()
        fetch(1).wait()
        back_sums(norm_b_value)
        alone, with_norm = pair_ref[SLOTS:], pair_ref[:SLOTS]
        scale = mod_ref[0:SLOTS] + 1.0
        gm_mine[...] = jnp.concatenate([vecs_ref[3:4] * with_norm + vecs_ref[4:5] * alone, alone], axis=0).astype(BF16)
        gm_all[d] = gm_mine[...]
        for k in range(n_dp - 1):
            gm_copy(k).start()
        sums_ref[3:4] = sum_rows(with_norm * scale)
        sums_ref[4:5] = sum_rows(alone * scale)
        back_factors(scale * vecs_ref[3:4], stats_ref[3])

    def back_b_second():
        fetch(2).start()
        fetch(4).start()

        def body(n):
            value = back_value(n, norm_b_value).astype(BF16).astype(F32)
            sums_ref[2:3] += sum_rows(value)
            total[:, n] = value.reshape(RES, RES, C)

        each(SLOTS, body)
        fetch(3).start()

    def lower():
        def by_line(yy):
            stage_mine[span(yy, LINE)] = total[yy].reshape(LINE, C).astype(BF16)

        each(RES, by_line)
        stage_copy().start()
        total[...] = jnp.zeros_like(total)

    def take():
        stage_copy().wait_recv()

        def by_line(yy):
            spot_rows = pl.ds(pl.multiple_of((yy + 1) * LINE, LINE), LINE)
            grads[1, c, spot_rows] = stage_mine[span(yy, LINE)]
            grads[1, 1 - c, spot_rows] = stage[span(yy, LINE)]

        each(RES, by_line)
        spread_sides(0)
        spread_sides(1)
        op_own(6).wait()

    def modulation():
        for k in range(n_dp - 1):
            gm_copy(k).wait()
        parts = gm_all[...].astype(F32)
        gm_scale = parts[:, :SLOTS].reshape(count, C)
        gm_offset = parts[:, SLOTS:].reshape(count, C)
        pre = pre_ref[...]
        emb = silu(pre).astype(BF16)
        part_rows = rows // n_head
        for k, value in ((0, gm_scale), (1, gm_offset)):
            low_value = value.astype(BF16)
            grad_w = dot_tn(emb, low_value)
            place_lanes = slice(k * C, (k + 1) * C)
            for hh in range(n_head):
                mw_mine[hh, 0:part_rows, place_lanes] = grad_w[hh * part_rows : (hh + 1) * part_rows]
                mw_mine[hh, part_rows : part_rows + 8, place_lanes] = jnp.broadcast_to(sum_rows(value), (8, C))
        grad_e = dot_nt(gm_scale.astype(BF16), modw_ref[:, :C]) + dot_nt(gm_offset.astype(BF16), modw_ref[:, C:])
        grad_e = grad_e * slope(pre)
        label = ids_ref[...].reshape(count, 128)[:, 0:1].astype(F32)
        lane = lax.broadcasted_iota(jnp.int32, grad_e.shape, 1)
        ge_all[h] = jnp.where(lane < rows, grad_e, label)
        for k in range(n_head - 1):
            mw_copy(k).start()
            ge_copy(k).start()

    def back_a_first():
        fetch(2).wait()
        fetch(4).wait()
        back_sums(norm_a_value)
        sums_ref[0:1] = sum_rows(pair_ref[:SLOTS])
        sums_ref[1:2] = sum_rows(pair_ref[SLOTS:])
        for hh in range(n_head):
            vs_mine[hh] = sums_ref[:, hh * cols : (hh + 1) * cols]
        for k in range(n_head - 1):
            vs_copy(k).start()
        back_factors(jnp.broadcast_to(vecs_ref[0:1], (SLOTS, C)), stats_ref[1])

    def back_a_second():
        fetch(3).wait()

        def body(n):
            image_mine[span(n, PIX)] = back_value(n, norm_a_value) + board[:, n].reshape(PIX, C)

        each(SLOTS, body)
        image_copy().start()

    def vec_first():
        value = vs_mine[h]
        for k in range(n_head - 1):
            vs_copy(k).wait()
            value += vs_got[k]
        vt_mine[...] = value
        vt_all[d] = value
        for k in range(n_dp - 1):
            vt_copy(k).start()

    def mod_out():
        value = mw_mine[h]
        for k in range(n_head - 1):
            mw_copy(k).wait()
            value += mw_got[k]
        part_rows = rows // n_head
        first_lane = (d * n_head + h) * part_rows
        for k in range(2):
            lanes_of = slice(k * C, (k + 1) * C)
            modw_out[:, k] = value[:part_rows, lanes_of]
            turned_row = pltpu.roll(value[part_rows:, lanes_of], lax.rem(C - first_lane, C), 1)
            modb_out[k : k + 1] = turned_row[0:1, :part_rows]

    def class_out():
        for k in range(n_head - 1):
            ge_copy(k).wait()
        table = class_ref.shape[1]
        part = rows // n_head
        value = ge_all[...].reshape(n_head * count, 128)
        label = value[:, rows : rows + 1].astype(jnp.int32)
        hot = lax.broadcasted_iota(jnp.int32, (n_head * count, table), 1) == label
        own = pltpu.roll(value, lax.rem(128 - h * part, 128), 1).astype(BF16)
        value = dot_tn(own, jnp.where(hot, 1.0, 0.0).astype(BF16))
        class_ref[...] = value[:part]

    def vec_second():
        for k in range(n_dp - 1):
            vt_copy(k).wait()
        value = vt_all[0]
        for k in range(1, n_dp):
            value += vt_all[k]
        vec_out[...] = value

    start()
    sides()
    dw(7)
    offer(7)
    dw(10)
    z_start(10)
    dw(5)
    offer(5)
    extra_b()
    dw(6)
    offer(6)
    dw(9)
    offer(9)
    relay(7)
    dw(8)
    conv_back_range(0, 3, 10)
    relay(5)
    relay(6)
    z_start(8)
    conv_back_range(3, 6, 10)
    conv_back_range(6, 9, 10)
    back_b_first()
    relay(9)
    back_b_second()
    lower()
    take()
    dw(0)
    extra_a()
    z_mix(10)
    offer(4)
    collect(6)
    offer(0)
    conv_back_range(0, 3, 0)
    relay(4)
    collect(5)
    dw(3)
    relay(0)
    collect(7)
    z_mix(8)
    z_mix(6)
    offer(3)
    collect(9)
    dw(1)
    offer(1)
    dw(2)
    conv_back_range(3, 6, 0)
    offer(2)
    z_mix(5)
    collect(0)
    conv_back_range(6, 9, 0)
    collect(4)
    z_mix(0)
    relay(1)
    modulation()
    z_mix(9)
    last(5)
    relay(2)
    last(10)
    mod_out()
    z_mix(4)
    collect(1)
    back_a_first()
    relay(3)
    z_mix(7)
    collect(2)
    last(8)
    last(9)
    z_mix(1)
    back_a_second()
    z_mix(2)
    last(6)
    collect(3)
    relay(8)
    class_out()
    vec_first()
    last(4)
    relay(10)
    z_mix(3)
    vec_second()
    last(7)
    last(0)
    last(2)
    collect(10)
    collect(8)
    last(1)
    last(3)

    low_copy().wait_send()
    stage_copy().wait_send()
    image_copy().wait()

    def drain(i):
        for part in range(2):
            x_copy(i, part).wait_send()
            y_copy(i, part).wait_send()
        z_drain(i)
        e_copy(i, 0).wait()
        e_own(i, 0).wait()

    for i in range(PAIRS):
        drain(i)


def run_backward(whole, turned, right, grad_low, grad_resid, conv_out, slopes, images, stats, vecs, mod, sums, pre, ids, modw, classes):
    n_dp, n_head = lax.axis_size("dp"), lax.axis_size("head")
    _, _, lines, _, rows, depth = whole.shape
    cols = depth // n_head
    wide = 2 * cols
    board = (RES, SLOTS, RES, C)
    shape = jax.ShapeDtypeStruct
    return pl.pallas_call(
        functools.partial(backward_kernel, lines),
        out_shape=(
            shape((9, rows, cols), F32),
            shape((9, rows, cols), F32),
            shape((3, rows, cols), F32),
            shape((rows, cols), F32),
            shape((ALL, C), F32),
            shape((rows // n_head, classes), F32),
            shape((rows // n_head, 2, C), F32),
            shape((2, rows // n_head), F32),
            shape((16, cols), F32),
        ),
        in_specs=[ANY] * 8 + [VMEM] * 7,
        out_specs=(ANY,) * 5 + (VMEM,) * 4,
        scratch_shapes=[
            pltpu.VMEM((PAIRS, lines, 2, rows, depth), BF16),
            pltpu.VMEM((len(BACK_NEAR), lines + lines // 2, rows, wide), BF16),
            pltpu.VMEM((len(BACK_NEAR), lines + lines // 2, rows, wide), BF16),
            pltpu.VMEM((len(BACK_NEAR), 4, rows, wide), BF16),
            pltpu.VMEM((len(BACK_FAR), rows + rows // 2, wide), BF16),
            pltpu.VMEM((len(BACK_FAR), rows + rows // 2, wide), BF16),
            pltpu.VMEM((len(BACK_FAR), 4, 2, rows, depth), BF16),
            pltpu.VMEM((2, PAIRS, rows, cols), F32),
            pltpu.VMEM((128, 2 * C), BF16),
            pltpu.VMEM((4, C, 2 * ALL), BF16),
            pltpu.VMEM((2, 2 * ALL, C), BF16),
            pltpu.VMEM((3, 2, ALL + 2 * LINE, C), BF16),
            pltpu.VMEM((ALL, C), BF16),
            pltpu.VMEM((ALL, C), BF16),
            pltpu.VMEM((AHEAD + 1, lines, 2, rows, depth), BF16),
            pltpu.VMEM(board, F32),
            pltpu.VMEM(board, F32),
            pltpu.VMEM(board, F32),
            pltpu.VMEM((ALL, C), F32),
            pltpu.VMEM((ALL, C), BF16),
            pltpu.VMEM((16, C), F32),
            pltpu.VMEM((2 * SLOTS, C), F32),
            pltpu.VMEM((3 * SLOTS, C), F32),
            pltpu.VMEM((2 * SLOTS, C), BF16),
            pltpu.VMEM((n_dp, 2 * SLOTS, C), BF16),
            pltpu.VMEM((n_head, rows // n_head + 8, 2 * C), F32),
            pltpu.VMEM((n_head - 1, rows // n_head + 8, 2 * C), F32),
            pltpu.VMEM((n_head, n_dp * SLOTS, 128), F32),
            pltpu.VMEM((n_head, 16, cols), F32),
            pltpu.VMEM((n_head - 1, 16, cols), F32),
            pltpu.VMEM((16, cols), F32),
            pltpu.VMEM((n_dp, 16, cols), F32),
            DMA((PAIRS, 2)),
            DMA((PAIRS, 2)),
            DMA((PAIRS, 2)),
            DMA((PAIRS, 2)),
            DMA((PAIRS, lines - 1)),
            DMA((PAIRS, lines - 1)),
            DMA((PAIRS,)),
            DMA((PAIRS,)),
            DMA((PAIRS,)),
            DMA((PAIRS,)),
            DMA((PAIRS,)),
            DMA((2,)),
            DMA((2,)),
            DMA((7,)),
            DMA((AHEAD + 1,)),
            DMA((5,)),
            DMA,
            DMA((n_dp - 1,)),
            DMA((n_dp - 1,)),
            DMA((n_head - 1,)),
            DMA((n_head - 1,)),
            DMA((n_head - 1,)),
            DMA((n_head - 1,)),
            DMA((n_head - 1,)),
            DMA((n_head - 1,)),
            DMA((n_dp - 1,)),
            DMA((n_dp - 1,)),
        ],
        compiler_params=pltpu.CompilerParams(
            collective_id=1, has_side_effects=True, vmem_limit_bytes=64 * 2**20 - 2**18
        ),
        name="backward_scatter",
    )(whole, turned, right, grad_low, grad_resid, conv_out, slopes, images, stats, vecs, mod, sums, pre, ids, modw)


def results_kernel(count, *refs):
    sources, vec_ref, refs = refs[:count], refs[count], refs[count + 1 :]
    targets, vectors, sems = refs[:count], refs[count:-1], refs[-1]
    copies = [
        pltpu.make_async_copy(source, target, sems.at[k])
        for k, (source, target) in enumerate(zip(sources, targets))
    ]
    for copy in copies:
        copy.start()
    for k, ref in enumerate(vectors):
        ref[...] = vec_ref[k].reshape(ref.shape)
    for copy in copies:
        copy.wait()


def run_results(arrays, vec):
    count = len(arrays)
    shape = jax.ShapeDtypeStruct
    return pl.pallas_call(
        functools.partial(results_kernel, count),
        out_shape=tuple(shape(one.shape, one.dtype) for one in arrays)
        + (shape(vec.shape[1:], F32),) * VECTORS,
        in_specs=[VMEM] * (count + 1),
        out_specs=(ANY,) * count + (VMEM,) * VECTORS,
        scratch_shapes=[DMA((count,))],
        compiler_params=pltpu.CompilerParams(vmem_limit_bytes=60 * 2**20),
        name="results",
    )(*arrays, vec)


def direct(rows, cols):
    n_dp, n_head = lax.axis_size("dp"), lax.axis_size("head")
    return n_head == 4 and n_dp == 8 and rows % 32 == 0 and cols % 64 == 0


def fast_shards(
    images,
    cotangent,
    counts,
    labels,
    levels,
    noise_table,
    class_table,
    gain_a,
    shift_a,
    conv_a,
    bias_a,
    mod_weight,
    mod_bias,
    gain_b,
    shift_b,
    conv_b,
    bias_b,
    gain_c,
    shift_c,
    qkv_weight,
    proj_weight,
    proj_bias,
):
    weights = (
        jnp.swapaxes(conv_a, 0, 1),
        jnp.swapaxes(conv_b, 0, 1),
        jnp.swapaxes(qkv_weight, 0, 1),
        proj_weight,
    )
    vectors = (gain_a, shift_a, bias_a, gain_b, shift_b, bias_b, gain_c, shift_c, proj_bias)
    flat = images.reshape(ALL, C)
    (
        whole,
        conv_out,
        slopes,
        turned,
        block_out,
        grad_resid,
        grad_low,
        right,
        vecs,
        mod,
        stats,
        pre,
        all_ids,
        sums,
    ) = run_forward(
        weights,
        flat,
        cotangent.reshape(ALL, C),
        counts.T,
        labels,
        levels,
        class_table.T,
        noise_table,
        mod_weight,
        mod_bias,
        vectors,
    )
    *arrays, vec = run_backward(
        whole,
        turned,
        right,
        grad_low,
        grad_resid,
        conv_out,
        slopes,
        flat,
        stats,
        vecs,
        mod,
        sums,
        pre,
        all_ids,
        mod_weight,
        class_table.shape[0],
    )
    block_out, conva, convb, qkvw, projw, image_grad, class_grad, modw_grad, modb_grad, *rest = run_results(
        (block_out, *arrays), vec
    )
    gaina, shifta, biasa, gainb, shiftb, biasb, gainc, shiftc, projb = rest
    return (
        block_out.reshape(images.shape),
        image_grad.reshape(images.shape),
        class_grad.T,
        gaina,
        shifta,
        jnp.swapaxes(conva, 0, 1),
        biasa,
        modw_grad,
        modb_grad,
        gainb,
        shiftb,
        jnp.swapaxes(convb, 0, 1),
        biasb,
        gainc,
        shiftc,
        jnp.swapaxes(qkvw, 0, 1),
        projw,
        projb,
    )


def shards(*args):
    rows, _, cols = args[9].shape
    if direct(rows, cols):
        return fast_shards(*args)
    return plain_shards(*args)


def solution(mesh):
    placed = (
        P(("dp", "head"), None, None, None),
        P(("dp", "head"), None, None, None),
        P(),
        P(("dp", "head")),
        P(("dp", "head")),
        P(),
        P(None, "dp"),
        P("head"),
        P("head"),
        P("dp", None, "head"),
        P("head"),
        P("dp", None, None),
        P(),
        P("head"),
        P("head"),
        P("dp", None, "head"),
        P("head"),
        P("head"),
        P("head"),
        P("dp", None, "head"),
        P("dp", "head"),
        P("head"),
    )
    return jax.shard_map(
        shards,
        mesh=mesh,
        in_specs=placed,
        out_specs=(
            P(("dp", "head"), None, None, None),
            P(("dp", "head"), None, None, None),
            P(None, ("dp", "head")),
            P("head"),
            P("head"),
            P("dp", None, "head"),
            P("head"),
            P(("dp", "head"), None, None),
            P(None, ("dp", "head")),
            P("head"),
            P("head"),
            P("dp", None, "head"),
            P("head"),
            P("head"),
            P("head"),
            P("dp", None, "head"),
            P("dp", "head"),
            P("head"),
        ),
        check_vma=False,
    )
```
